32 devices in a mesh: gx: 8 (over y, x, core), gy: 4 (over z).
Axes of the slice: x: 2, y: 2, z: 4, core: 2. Of those that a mesh axis runs over, the one named last changes fastest.
Arguments:
- traces: bfloat16 [3, 48, 32, 16, 128], P(None, None, 'gx', 'gy'), may hold values from -6 to 6
- dirichlet: int32 [3, 32, 16, 128], P(None, 'gx', 'gy'), may hold values 0 or 1
- visc_class: int32 [32, 16, 128], P('gx', 'gy'), may hold values from 0 to 3
- viscosity: float32 [4], replicated, may hold values from 0.25 to 4
- coarse_diag: float32 [32, 16, 128], P('gx', 'gy'), may hold values from 2 to 16
- solve_map: bfloat16 [256, 288], replicated, may hold values from -0.375 to 0.375
- flux_map: bfloat16 [288, 256], replicated, may hold values from -0.375 to 0.375
Outputs:
- corrected: bfloat16 [3, 48, 32, 16, 128], P(None, None, 'gx', 'gy')
The draws below stay inside these ranges and needn't reach their ends.
All inputs are finite; a program needn't handle non-finite values. No bound on the sum of `dirichlet` on one device may be relied on, other than what follows from the above.
Results may differ from the reference program's by a relative error of at most 0.005.
Values may be sent and summed in bfloat16 or wider, within the bound.
No kernel may reach another device: no remote copies, remote signals or barrier semaphores. Data moves between devices by JAX's collectives and lax.ppermute only.
A program may use at most 64 MiB of HBM per device.

```python
import math
import jax
import jax.numpy as jnp
from jax import lax

FU = 48
NI = 256
NCLS = 4
NX = 32
NY = 16
NZ = 128


def with_ends(entries, key, low, high):
    longest = entries.shape.index(max(entries.shape))
    spots = []
    for shift in (0, 1):
        where = [jax.random.randint(jax.random.fold_in(key, axis), (), 0, length) for axis, length in enumerate(entries.shape)]
        where[longest] = (where[longest] + shift) % entries.shape[longest]
        spots.append(tuple(where))
    return entries.at[spots[0]].set(low).at[spots[1]].set(high)


def block_scale(key, shape, shards, smallest, high):
    def one(position, blocks):
        heights = jax.random.uniform(jax.random.fold_in(jax.random.fold_in(key, 6), position), (blocks,), jnp.float32, smallest / len(shards), high / len(shards))
        return jnp.repeat(jnp.exp(heights), shape[position] // blocks).reshape((-1,) + (1,) * (len(shape) - position - 1))

    level = one(*shards[0])
    for cut in shards[1:]:
        level = level * one(*cut)
    return level


def centred(rng, dims, width, reach, pieces=(), kind=jnp.bfloat16):
    level = block_scale(rng, dims, pieces, -0.22, 0.18) if pieces else 1.0
    values = jax.random.normal(rng, dims, jnp.float32) * width * level
    return jnp.minimum(jnp.maximum(values, -reach), reach).astype(kind)


def setup_inputs(seed: int = 0) -> dict:
    arg_keys = jax.random.split(jax.random.key(seed), 8)
    return {
        "traces": centred(arg_keys[0], (3, FU, NX, NY, NZ), 1.0, 6.0, ((2, 8), (3, 4))),
        "dirichlet": with_ends((jax.random.randint(arg_keys[1], (3, NX, NY, NZ), 0, 8) < 1).astype(jnp.int32), jax.random.fold_in(arg_keys[1], 1), 0, 1),
        "visc_class": with_ends(jax.random.randint(arg_keys[2], (NX, NY, NZ), 0, NCLS), jax.random.fold_in(arg_keys[2], 1), 0, NCLS - 1).astype(jnp.int32),
        "viscosity": jnp.clip(jnp.exp(jax.random.uniform(arg_keys[3], (NCLS,), jnp.float32, math.log(0.25), math.log(4.0))), 0.25, 4.0),
        "coarse_diag": jnp.clip(jnp.exp(math.log(16.0) - 2.0794415 * jax.random.uniform(arg_keys[4], (NX, NY, NZ), jnp.float32) ** block_scale(arg_keys[4], (NX, NY, NZ), ((0, 8), (1, 4)), -0.2, 0.2)), 2.0, 16.0),
        "solve_map": centred(arg_keys[5], (NI, 6 * FU), (6 * FU) ** -0.5, 0.375),
        "flux_map": centred(arg_keys[6], (6 * FU, NI), NI ** -0.5, 0.375),
    }


penalty = 0.5

def corner_table():
    gll_points = [-1.0, -math.sqrt(0.2), math.sqrt(0.2), 1.0]
    table_rows = []
    for node_s in range(4):
        for node_t in range(4):
            table_row = []
            for high_s in range(2):
                for high_t in range(2):
                    table_row.append((1.0 + (2 * high_s - 1) * gll_points[node_s]) * (1.0 + (2 * high_t - 1) * gll_points[node_t]) / 4.0)
            table_rows.append(table_row)
    return jnp.asarray(table_rows, dtype=jnp.float32)

def landing(face_slot, high_s, high_t):
    direction = face_slot // 2
    outward = face_slot % 2
    if direction == 0:
        return (outward, high_s, high_t)
    if direction == 1:
        return (high_s, outward, high_t)
    return (high_s, high_t, outward)

def cell_viscosity(visc_class, viscosity):
    result = jnp.zeros(visc_class.shape, jnp.float32)
    for level in range(viscosity.shape[0]):
        result = result + jnp.where(visc_class == level, viscosity[level], jnp.float32(0.0))
    return result

def forward_last(piece, axis):
    zero_part = jnp.zeros_like(lax.slice_in_dim(piece, 0, 1, axis=axis))
    return jnp.concatenate([zero_part, lax.slice_in_dim(piece, 0, piece.shape[axis] - 1, axis=axis)], axis=axis)

def backward_last(piece, axis):
    zero_part = jnp.zeros_like(lax.slice_in_dim(piece, 0, 1, axis=axis))
    return jnp.concatenate([lax.slice_in_dim(piece, 1, piece.shape[axis], axis=axis), zero_part], axis=axis)

def reference(traces, dirichlet, visc_class, viscosity, coarse_diag, solve_map, flux_map):
    weights = corner_table()
    faces = traces.shape[1]
    keep_mask = (1 - dirichlet).astype(jnp.bfloat16)
    lifted = traces * keep_mask[:, None]
    visc_all = cell_viscosity(visc_class, viscosity)

    def plane_contrib(index):
        has_next = index + 1 < NX
        next_index = jnp.minimum(index + 1, NX - 1).astype(jnp.int32)
        here = lax.dynamic_index_in_dim(lifted, index, 2, keepdims=False)
        keep_here = lax.dynamic_index_in_dim(keep_mask, index, 1, keepdims=False)
        x_next = jnp.where(has_next, lax.dynamic_index_in_dim(lifted, next_index, 2, keepdims=False)[0], jnp.zeros((), jnp.bfloat16))
        keep_xnext = jnp.where(has_next, lax.dynamic_index_in_dim(keep_mask, next_index, 1, keepdims=False)[0], jnp.zeros((), jnp.bfloat16))
        y_high = backward_last(here[1], 1)
        z_high = backward_last(here[2], 2)
        keep_yhigh = backward_last(keep_here[1], 0)
        keep_zhigh = backward_last(keep_here[2], 1)
        element_traces = jnp.concatenate([here[0], x_next, here[1], y_high, here[2], z_high], axis=0)
        flat_traces = element_traces.reshape(6 * faces, NY * NZ)
        interior = jnp.dot(solve_map, flat_traces, preferred_element_type=jnp.float32).astype(jnp.bfloat16)
        flux_term = jnp.dot(flux_map, interior, preferred_element_type=jnp.float32) + penalty * flat_traces.astype(jnp.float32)
        face_keep = jnp.stack([keep_here[0], keep_xnext, keep_here[1], keep_yhigh, keep_here[2], keep_zhigh]).astype(jnp.float32)
        visc_here = lax.dynamic_index_in_dim(visc_all, index, 0, keepdims=False)
        scaled = (visc_here[None] * face_keep).reshape(6, 1, NY * NZ)
        return (flux_term.reshape(6, faces, NY * NZ) * scaled).reshape(6, faces, NY, NZ)

    def plane_terms(index):
        contrib = plane_contrib(index)
        res_y = contrib[2] + forward_last(contrib[3], 1)
        res_z = contrib[4] + forward_last(contrib[5], 2)
        split_parts = contrib.reshape(6, 3, faces // 3, NY, NZ)
        corners = jnp.einsum('fmnyz,nc->fcmyz', split_parts, weights, precision=lax.Precision.HIGHEST)
        here_sum = jnp.zeros((3, NY, NZ), jnp.float32)
        next_sum = jnp.zeros((3, NY, NZ), jnp.float32)
        for face_slot in range(6):
            for high_s in range(2):
                for high_t in range(2):
                    step_x, step_y, step_z = landing(face_slot, high_s, high_t)
                    corner_part = corners[face_slot, 2 * high_s + high_t]
                    if step_y:
                        corner_part = forward_last(corner_part, 1)
                    if step_z:
                        corner_part = forward_last(corner_part, 2)
                    if step_x:
                        next_sum = next_sum + corner_part
                    else:
                        here_sum = here_sum + corner_part
        return (jnp.stack([contrib[0], res_y, res_z]), contrib[1], here_sum, next_sum)
    own_planes, high_planes, here_sums, next_sums = lax.map(plane_terms, jnp.arange(NX, dtype=jnp.int32))
    residual_x = own_planes[:, 0] + forward_last(high_planes, 0)
    residual_planes = jnp.concatenate([residual_x[:, None], own_planes[:, 1:]], axis=1)
    vertex_planes = forward_last(next_sums, 0) + here_sums
    coarse_fix = jnp.moveaxis(vertex_planes, 0, 1) / coarse_diag[None]

    def plane_output(index):
        has_next = index + 1 < NX
        next_index = jnp.minimum(index + 1, NX - 1).astype(jnp.int32)
        fix_here = lax.dynamic_index_in_dim(coarse_fix, index, 1, keepdims=False)
        fix_next = jnp.where(has_next, lax.dynamic_index_in_dim(coarse_fix, next_index, 1, keepdims=False), jnp.float32(0.0))
        paired = jnp.pad(jnp.stack([fix_here, fix_next]), ((0, 0), (0, 0), (0, 1), (0, 1)))
        residual_here = lax.dynamic_index_in_dim(residual_planes, index, 0, keepdims=False)
        keep_here = lax.dynamic_index_in_dim(keep_mask, index, 1, keepdims=False)
        results = []
        for direction in range(3):
            picks = []
            for high_s in range(2):
                for high_t in range(2):
                    step_x, step_y, step_z = landing(2 * direction, high_s, high_t)
                    picks.append(paired[step_x][:, step_y:step_y + NY, step_z:step_z + NZ])
            lifted_fix = jnp.einsum('nc,cmyz->mnyz', weights, jnp.stack(picks), precision=lax.Precision.HIGHEST).reshape(faces, NY, NZ)
            results.append(residual_here[direction] + keep_here[direction].astype(jnp.float32) * lifted_fix)
        return jnp.stack(results).astype(jnp.bfloat16)
    planes_out = lax.map(plane_output, jnp.arange(NX, dtype=jnp.int32))
    return jnp.transpose(planes_out, (1, 2, 0, 3, 4))
```

```python
import functools
import math

import jax
import jax.numpy as jnp
import ml_dtypes
import numpy as np
from jax import lax
from jax.experimental import pallas as pl
from jax.experimental.pallas import tpu as pltpu
from jax.sharding import PartitionSpec as P

penalty = 0.5
BF = jnp.bfloat16
F32 = jnp.float32


def from_behind(value, axis, steps):
    count = lax.axis_size(axis)
    leading, last = (max(0, -steps), min(count, count - steps))
    return lax.ppermute(value, axis, [(source, source + steps) for source in range(leading, last)])


def corner_table():
    gll_points = [-1.0, -math.sqrt(0.2), math.sqrt(0.2), 1.0]
    table = np.zeros((16, 4), np.float64)
    for s in range(4):
        for t in range(4):
            for p in range(2):
                for q in range(2):
                    table[4 * s + t, 2 * p + q] = (
                        (1 + (2 * p - 1) * gll_points[s]) * (1 + (2 * q - 1) * gll_points[t]) / 4
                    )
    return table


def landing(face_slot, high_s, high_t):
    direction, outward = divmod(face_slot, 2)
    if direction == 0:
        return (outward, high_s, high_t)
    if direction == 1:
        return (high_s, outward, high_t)
    return (high_s, high_t, outward)


def gather_table():
    weights = corner_table()
    table = np.zeros((32, 288), np.float64)
    for slot in range(6):
        for s in range(2):
            for t in range(2):
                p, q, r = landing(slot, s, t)
                for c in range(3):
                    cols = slot * 48 + 16 * c + np.arange(16)
                    table[16 * r + 8 * p + 4 * q + c, cols] += weights[:, 2 * s + t]
    return table.astype(ml_dtypes.bfloat16)


def spread_table(wx, wy, rows):
    weights = corner_table()
    planes = (wx + 1) * rows
    depth = -(-2 * planes // 128) * 128
    table = np.zeros((3, 48, wx, wy, depth), np.float64)
    for d in range(3):
        for x in range(wx):
            for y in range(wy):
                for s in range(2):
                    for t in range(2):
                        p, q, r = landing(2 * d, s, t)
                        for c in range(3):
                            k = r * planes + (x + p) * rows + 4 * (y + q) + c
                            table[d, 16 * c : 16 * c + 16, x, y, k] += weights[:, 2 * s + t]
    return table.reshape(-1, depth).astype(ml_dtypes.bfloat16)


def lanes(shape):
    return lax.broadcasted_iota(jnp.int32, shape, len(shape) - 1)


def z_next(value):
    last = value.shape[-1] - 1
    return jnp.where(lanes(value.shape) < last, pltpu.roll(value, last, value.ndim - 1), 0.0)


def z_prev(value):
    return jnp.where(lanes(value.shape) > 0, pltpu.roll(value, 1, value.ndim - 1), 0.0)


def hex_batch(slots, scales, s_map, f_map, gather):
    element = jnp.concatenate(
        [jnp.concatenate([slots[h][s] for h in range(len(slots))], axis=1) for s in range(6)], axis=0
    )
    interior = jnp.dot(s_map, element, preferred_element_type=F32).astype(BF)
    flux = jnp.dot(f_map, interior, preferred_element_type=F32) + penalty * element.astype(F32)
    scale = jnp.concatenate(
        [
            jnp.concatenate([jnp.broadcast_to(row[s], (48, row[s].shape[1])) for row in scales], axis=1)
            for s in range(6)
        ],
        axis=0,
    )
    contrib = flux * scale
    corners = jnp.dot(gather, contrib.astype(BF), preferred_element_type=F32)
    return contrib, corners


def hex_parts(l_ref, kp_ref, wy, x, y, x_high=None, y_high=None):
    here = x * wy + y
    row = lambda i, col: kp_ref[i, pl.ds(col, 1), :]
    if x_high is None:
        x_high = (l_ref[0, here + wy], row(0, here + wy))
    if y_high is None:
        y_high = (l_ref[1, here + 1], row(1, here + 1))
    slots = [l_ref[0, here], x_high[0], l_ref[1, here], y_high[0], l_ref[2, here], l_ref[3, here]]
    visc = row(4, here)
    keeps = [row(0, here), x_high[1], row(1, here), y_high[1], row(2, here), row(3, here)]
    return slots, [visc * keep for keep in keeps]


def add_corners(vs_ref, corners, x, y):
    for p in range(2):
        part = corners[8 * p : 8 * p + 8] + z_prev(corners[16 + 8 * p : 24 + 8 * p])
        vs_ref[x + p, pl.ds(4 * y, 8), :] += part


def store_contrib(c_ref, contrib, order, z):
    for at, h in enumerate(order):
        for s in range(6):
            c_ref[s, at] = contrib[48 * s : 48 * s + 48, z * h : z * h + z]


def first_kernel(
    wx, wy, visc_ref, t_ref, dir_ref, cls_ref, diag_ref, st_ref, f_ref, g_ref,
    l_ref, kp_ref, s_ref, c_ref, vs_ref, pkg_ref, nat, vert,
):
    z = t_ref.shape[2]
    cells = wx * wy
    s_ref[...] = st_ref[...].T
    classes = cls_ref[...]
    visc = jnp.zeros(classes.shape, F32)
    for level in range(visc_ref.shape[0]):
        visc = visc + jnp.where(classes == level, visc_ref[level], F32(0.0))
    kp_ref[4] = visc
    for d in range(3):
        keep = (1 - dir_ref[d]).astype(F32)
        kp_ref[d] = keep
        masked = t_ref[d].astype(F32).reshape(48, cells, z) * keep[None]
        nat[...] = masked.reshape(48 * cells, z)
        for col in range(cells):
            part = nat[pl.ds(col, 48, stride=cells), :]
            l_ref[d, col] = part.astype(BF)
            if d == 2:
                l_ref[3, col] = z_next(part).astype(BF)
    kp_ref[3] = z_next(kp_ref[2])
    vs_ref[...] = jnp.zeros_like(vs_ref)
    unknown = (jnp.zeros((48, z), BF), jnp.ones((1, z), F32))
    parts = [
        hex_parts(l_ref, kp_ref, wy, x, 0, x_high=unknown if x == wx - 1 else None) for x in range(wx)
    ]
    contrib, corners = hex_batch(
        [p[0] for p in parts], [p[1] for p in parts], s_ref[...], f_ref[...], g_ref[...]
    )
    store_contrib(c_ref, contrib, range(wx - 1), z)
    vert[...] = jnp.zeros_like(vert)
    only_high = jnp.concatenate(
        [jnp.zeros((48, z), F32), contrib[48:96, z * (wx - 1) :], jnp.zeros((192, z), F32)], axis=0
    )
    unkept = jnp.dot(g_ref[...], only_high.astype(BF), preferred_element_type=F32)
    for r in range(2):
        vert[pl.ds(4 * (wx + 1) + wx + 4 * r, 4), :] = unkept[16 * r + 8 : 16 * r + 12]
    for x in range(wx):
        own = corners[:, z * x : z * x + z]
        if x < wx - 1:
            add_corners(vs_ref, own, x, 0)
        else:
            own = own - unkept
        low = own[0:16] + z_prev(own[16:32])
        for p in range(2):
            vert[pl.ds(4 * (x + p), 4), :] += low[8 * p : 8 * p + 4]
    for x in range(wx):
        diag = diag_ref[pl.ds(x * wy, 1), :]
        high = diag.astype(BF).astype(F32)
        vert[pl.ds(4 * x + 3, 1), :] = high
        vert[pl.ds(4 * (wx + 1) + x, 1), :] = diag - high
    for x in range(wx):
        pkg_ref[pl.ds(48 * x, 48), :] = l_ref[1, x * wy]
    base = 48 * wx
    pkg_ref[pl.ds(base, 48), :] = l_ref[0, 0]
    corner = (wx - 1) * wy
    misc = [kp_ref[1, pl.ds(x * wy, 1), :] for x in range(wx)]
    misc += [kp_ref[0, pl.ds(0, 1), :], cls_ref[pl.ds(corner, 1), :].astype(F32)]
    misc += [kp_ref[0, pl.ds(corner, 1), :], kp_ref[1, pl.ds(corner + 1, 1), :]]
    misc += [kp_ref[2, pl.ds(corner, 1), :], kp_ref[3, pl.ds(corner, 1), :]]
    misc += [jnp.zeros((16 - len(misc), z), F32)]
    pkg_ref[pl.ds(base + 48, 16), :] = jnp.concatenate(misc, axis=0).astype(BF)
    pkg_ref[pl.ds(base + 64, 32), :] = vert[...].astype(BF)


def middle_kernel(wx, wy, l_ref, kp_ref, s_ref, f_ref, g_ref, c_ref, vs_ref):
    z = l_ref.shape[3]
    vs_ref[...] = jnp.zeros_like(vs_ref)
    where = [(x, y) for x in range(wx - 1) for y in range(1, wy - 1)]
    parts = [hex_parts(l_ref, kp_ref, wy, x, y) for x, y in where]
    contrib, corners = hex_batch(
        [p[0] for p in parts], [p[1] for p in parts], s_ref[...], f_ref[...], g_ref[...]
    )
    store_contrib(c_ref, contrib, range(len(where)), z)
    for h, (x, y) in enumerate(where):
        add_corners(vs_ref, corners[:, z * h : z * h + z], x, y)


def after_y_kernel(
    wx, wy, l_ref, kp_ref, s_ref, f_ref, g_ref, yd_ref, diag_ref, vsa_ref, vsb_ref,
    c_ref, vs_ref, pkg_ref, vert,
):
    z = l_ref.shape[3]
    base = 48 * wx
    misc = yd_ref[pl.ds(base + 48, 16), :].astype(F32)
    rim = yd_ref[pl.ds(base + 64, 32), :].astype(F32)
    vs_ref[...] = jnp.zeros_like(vs_ref)
    slots, scales = hex_parts(
        l_ref, kp_ref, wy, 0, wy - 1, y_high=(yd_ref[pl.ds(0, 48), :], misc[0:1])
    )
    contrib, corners = hex_batch([slots], [scales], s_ref[...], f_ref[...], g_ref[...])
    store_contrib(c_ref, contrib, range(1), z)
    add_corners(vs_ref, corners, 0, wy - 1)
    vert[...] = jnp.zeros_like(vert)
    edge = 4 * (wy + 1)
    vert[pl.ds(0, edge), :] = (
        vsa_ref[0, pl.ds(0, edge), :] + vsb_ref[0, pl.ds(0, edge), :] + vs_ref[0, pl.ds(0, edge), :]
    )
    vert[pl.ds(4 * wy, 3), :] += rim[0:3]
    vert[pl.ds(edge + 5, 3), :] = vs_ref[0, pl.ds(4 * wy, 3), :]
    for y in range(wy):
        diag = diag_ref[pl.ds(y, 1), :]
        high = diag.astype(BF).astype(F32)
        vert[pl.ds(4 * y + 3, 1), :] = high
        vert[pl.ds(edge + y, 1), :] = diag - high
    vert[pl.ds(4 * wy + 3, 1), :] = rim[3:4]
    vert[pl.ds(edge + wy, 1), :] = rim[4 * (wx + 1) : 4 * (wx + 1) + 1]
    for y in range(wy):
        pkg_ref[pl.ds(48 * y, 48), :] = l_ref[0, y]
    base = 48 * wy
    pkg_ref[pl.ds(base, 48), :] = yd_ref[pl.ds(48 * wx, 48), :]
    rows = [kp_ref[0, pl.ds(0, wy), :], misc[wx : wx + 1], jnp.zeros((15 - wy, z), F32)]
    pkg_ref[pl.ds(base + 48, 16), :] = jnp.concatenate(rows, axis=0).astype(BF)
    pkg_ref[pl.ds(base + 64, 32), :] = vert[...].astype(BF)


def last_row_kernel(wx, wy, l_ref, kp_ref, s_ref, f_ref, g_ref, yd_ref, c_ref, vs_ref):
    z = l_ref.shape[3]
    misc = yd_ref[pl.ds(48 * wx + 48, 16), :].astype(F32)
    vs_ref[...] = jnp.zeros_like(vs_ref)
    parts = [
        hex_parts(
            l_ref, kp_ref, wy, x, wy - 1, y_high=(yd_ref[pl.ds(48 * x, 48), :], misc[x : x + 1])
        )
        for x in range(1, wx - 1)
    ]
    contrib, corners = hex_batch(
        [p[0] for p in parts], [p[1] for p in parts], s_ref[...], f_ref[...], g_ref[...]
    )
    store_contrib(c_ref, contrib, range(wx - 2), z)
    for h, x in enumerate(range(1, wx - 1)):
        add_corners(vs_ref, corners[:, z * h : z * h + z], x, wy - 1)


def after_x_kernel(
    wx, wy, visc_ref, l_ref, kp_ref, s_ref, f_ref, g_ref, yd_ref, xd_ref,
    c_ref, vs_ref, vx_ref, pkg_ref, vert,
):
    z = l_ref.shape[3]
    misc_y = yd_ref[pl.ds(48 * wx + 48, 16), :].astype(F32)
    rim_y = yd_ref[pl.ds(48 * wx + 64, 32), :].astype(F32)
    misc_x = xd_ref[pl.ds(48 * wy + 48, 16), :].astype(F32)
    vs_ref[...] = jnp.zeros_like(vs_ref)
    vx_ref[...] = jnp.zeros_like(vx_ref)
    slots, scales = [], []
    for y in range(wy):
        y_high = None
        if y == wy - 1:
            y_high = (yd_ref[pl.ds(48 * (wx - 1), 48), :], misc_y[wx - 1 : wx])
        part = hex_parts(
            l_ref, kp_ref, wy, wx - 1, y,
            x_high=(xd_ref[pl.ds(48 * y, 48), :], misc_x[y : y + 1]), y_high=y_high,
        )
        slots.append(part[0])
        scales.append(part[1])
    nothing = jnp.zeros((48, z), BF)
    slots.append([nothing, xd_ref[pl.ds(48 * wy, 48), :]] + [nothing] * 4)
    level = misc_y[wx + 1 : wx + 2]
    visc = jnp.zeros((1, z), F32)
    for k in range(visc_ref.shape[0]):
        visc = visc + jnp.where(level == F32(k), visc_ref[k], F32(0.0))
    keeps = [
        misc_y[wx + 2 : wx + 3], misc_x[wy : wy + 1], misc_y[wx - 1 : wx],
        misc_y[wx + 3 : wx + 4], misc_y[wx + 4 : wx + 5], misc_y[wx + 5 : wx + 6],
    ]
    scales.append([visc * keep for keep in keeps])
    contrib, corners = hex_batch(slots, scales, s_ref[...], f_ref[...], g_ref[...])
    store_contrib(c_ref, contrib, range(wy), z)
    for y in range(wy):
        add_corners(vs_ref, corners[:, z * y : z * y + z], wx - 1, y)
    beyond = corners[:, z * wy : z * wy + z]
    spare = 4 * (wx + 1) + wx
    unkept = [rim_y[spare + 4 * r : spare + 4 * r + 4] * misc_x[wy : wy + 1] for r in range(2)]
    beyond = beyond[0:16] + z_prev(beyond[16:32])
    beyond = [beyond[0:4], beyond[8:12] + unkept[0] + z_prev(unkept[1])]
    for p in range(2):
        vx_ref[wx - 1 + p, pl.ds(4 * wy, 4), :] = beyond[p]
    vert[...] = jnp.zeros_like(vert)
    edge = 4 * (wy + 1)
    vert[pl.ds(0, edge), :] = vs_ref[wx, pl.ds(0, edge), :]
    vert[pl.ds(edge + 5, 3), :] = vert[pl.ds(4 * wy, 3), :]
    vert[pl.ds(4 * wy, 3), :] += beyond[1][0:3] + rim_y[4 * wx : 4 * wx + 3]
    for y in range(wy):
        pkg_ref[pl.ds(48 * y, 48), :] = c_ref[1, y].astype(BF)
    pkg_ref[pl.ds(48 * wy, 32), :] = vert[...].astype(BF)


def up_y_kernel(
    wx, wy, cc_ref, cc2_ref, cd_ref, vsc_ref, vsc2_ref, vsd_ref, xd_ref, xu_ref, pkg_ref, vert
):
    top = [cc_ref.at[3, 0]] + [cc2_ref.at[3, x] for x in range(wx - 2)] + [cd_ref.at[3, wy - 1]]
    for x in range(wx):
        pkg_ref[pl.ds(48 * x, 48), :] = top[x][...].astype(BF)
    edge = 4 * (wy + 1)
    from_high = xd_ref[pl.ds(48 * wy + 64, 32), :].astype(F32)
    from_low = xu_ref[pl.ds(48 * wy, 32), :].astype(F32)
    vert[...] = jnp.zeros_like(vert)
    for i in range(wx + 1):
        rows = pl.ds(4 * wy, 3)
        total = vsc_ref[i, rows, :] + vsc2_ref[i, rows, :] + vsd_ref[i, rows, :]
        if i == 0:
            total = total + from_low[edge + 5 : edge + 8]
        if i == wx:
            total = total + from_high[edge + 5 : edge + 8]
        vert[pl.ds(4 * i, 3), :] = total
    pkg_ref[pl.ds(48 * wx, 32), :] = vert[...].astype(BF)


def assemble_kernel(
    wx, wy, diag_ref, ca_ref, cb_ref, cc_ref, cc2_ref, cd_ref, vsa_ref, vsb_ref, vsc_ref, vsc2_ref,
    vsd_ref, vsx_ref, yd_ref, xd_ref, xu_ref, r_ref, vs_ref, inv_ref, dg,
):
    cells = wx * wy

    def contrib(slot, x, y):
        if x == wx - 1:
            return cd_ref[slot, y]
        if y == 0:
            return ca_ref[slot, x]
        if y < wy - 1:
            return cb_ref[slot, x * (wy - 2) + y - 1]
        if x == 0:
            return cc_ref[slot, 0]
        return cc2_ref[slot, x - 1]

    for x in range(wx):
        for y in range(wy):
            col = pl.ds(x * wy + y, 48, stride=cells)
            if x:
                behind = contrib(1, x - 1, y)
            else:
                behind = xu_ref[pl.ds(48 * y, 48), :].astype(F32)
            r_ref[0, col, :] = contrib(0, x, y) + behind
            if y:
                r_ref[1, col, :] = contrib(2, x, y) + contrib(3, x, y - 1)
            else:
                r_ref[1, col, :] = contrib(2, x, y)
            r_ref[2, col, :] = contrib(4, x, y) + z_prev(contrib(5, x, y))
    edge = 4 * (wy + 1)
    rim_y = yd_ref[pl.ds(48 * wx + 64, 32), :].astype(F32)
    rim_x = xd_ref[pl.ds(48 * wy + 64, 32), :].astype(F32)
    rim_low = xu_ref[pl.ds(48 * wy, 32), :].astype(F32)
    vs_ref[...] = (
        vsa_ref[...] + vsb_ref[...] + vsc_ref[...] + vsc2_ref[...] + vsd_ref[...] + vsx_ref[...]
    )
    dg[...] = jnp.zeros_like(dg)
    for x in range(wx):
        for y in range(wy):
            row = diag_ref[pl.ds(x * wy + y, 1), :]
            dg[x, pl.ds(4 * y, 4), :] = jnp.broadcast_to(row, (4, row.shape[1]))
        vs_ref[x, pl.ds(4 * wy, 3), :] += rim_y[4 * x : 4 * x + 3]
        row = rim_y[4 * x + 3 : 4 * x + 4] + rim_y[4 * (wx + 1) + x : 4 * (wx + 1) + x + 1]
        dg[x, pl.ds(4 * wy, 4), :] = jnp.broadcast_to(row, (4, row.shape[1]))
    for y in range(wy + 1):
        vs_ref[wx, pl.ds(4 * y, 3), :] += rim_x[4 * y : 4 * y + 3]
        vs_ref[0, pl.ds(4 * y, 3), :] += rim_low[4 * y : 4 * y + 3]
        row = rim_x[4 * y + 3 : 4 * y + 4] + rim_x[edge + y : edge + y + 1]
        dg[wx, pl.ds(4 * y, 4), :] = jnp.broadcast_to(row, (4, row.shape[1]))
    vs_ref[wx, pl.ds(4 * wy, 3), :] += rim_y[4 * wx : 4 * wx + 3]
    present = dg[...] > 0.0
    inv_ref[...] = jnp.where(present, 1.0 / jnp.where(present, dg[...], 1.0), 0.0)


def final_kernel(wx, wy, kp_ref, r_ref, vs_ref, inv_ref, yu_ref, p_ref, out_ref, fix, first):
    cells, z = wx * wy, vs_ref.shape[2]
    rows = vs_ref.shape[1]
    planes = (wx + 1) * rows
    rim = yu_ref[pl.ds(48 * wx, 32), :].astype(F32)
    fix[...] = jnp.zeros_like(fix)
    first[...] = vs_ref[...]
    for i in range(wx + 1):
        first[i, pl.ds(0, 3), :] += rim[4 * i : 4 * i + 3]
    value = (first[...] * inv_ref[...]).reshape(planes, z)
    fix[pl.ds(0, planes), :] = value
    fix[pl.ds(planes, planes), :] = z_next(value)
    rhs = fix[...].astype(BF)
    for x in range(wx):
        col = pl.ds(x * wy, 48, stride=cells)
        r_ref[1, col, :] += yu_ref[pl.ds(48 * x, 48), :].astype(F32)
    for d in range(3):
        lift = jnp.dot(p_ref[pl.ds(48 * cells * d, 48 * cells), :], rhs, preferred_element_type=F32)
        lift = lift.reshape(48, cells, z) * kp_ref[d][None]
        out_ref[d] = (r_ref[d] + lift.reshape(48 * cells, z)).astype(BF)


def call(body, outs, scratch, flops):
    return pl.pallas_call(
        body,
        out_shape=outs,
        scratch_shapes=scratch,
        cost_estimate=pl.CostEstimate(flops=flops, bytes_accessed=1000000, transcendentals=0),
        compiler_params=pltpu.CompilerParams(vmem_limit_bytes=16 * 1024 * 1024),
    )


def local(traces, dirichlet, visc_class, viscosity, coarse_diag, solve_map, flux_map):
    wx, wy, z = traces.shape[2:]
    cells = wx * wy
    rows = -(-4 * (wy + 1) // 8) * 8
    gather = jnp.asarray(gather_table())
    spread = jnp.asarray(spread_table(wx, wy, rows))
    per_hex = 4 * 288 * 256 * z
    sums = pltpu.VMEM((wx + 1, rows, z), F32)
    vert = pltpu.VMEM((32, z), F32)
    contribs = lambda hexes: pltpu.VMEM((6, hexes, 48, z), F32)
    partial = functools.partial
    natural = traces.reshape(3, 48 * cells, z)
    diag = coarse_diag.reshape(cells, z)

    lifted, flags, s_map, c_a, vs_a, send = pl.pallas_call(
        partial(first_kernel, wx, wy),
        in_specs=[pl.BlockSpec(memory_space=pltpu.SMEM)] + [pl.BlockSpec(memory_space=pltpu.VMEM)] * 7,
        out_shape=(
            pltpu.VMEM((4, cells, 48, z), BF), pltpu.VMEM((5, cells, z), F32),
            pltpu.VMEM(solve_map.shape, BF), contribs(wx - 1), sums, pltpu.VMEM((48 * wx + 96, z), BF),
        ),
        scratch_shapes=[pltpu.VMEM((48 * cells, z), F32), vert],
        cost_estimate=pl.CostEstimate(flops=wx * per_hex, bytes_accessed=1000000, transcendentals=0),
        compiler_params=pltpu.CompilerParams(vmem_limit_bytes=16 * 1024 * 1024),
    )(
        viscosity, natural, dirichlet.reshape(3, cells, z), visc_class.reshape(cells, z), diag,
        solve_map.T, flux_map, gather,
    )
    yd = from_behind(send, "gy", -1)
    maps = (lifted, flags, s_map, flux_map, gather)
    hexes = (wx - 1) * (wy - 2)
    c_b, vs_b = call(partial(middle_kernel, wx, wy), (contribs(hexes), sums), [], hexes * per_hex)(*maps)
    c_c, vs_c, send = call(
        partial(after_y_kernel, wx, wy),
        (contribs(1), sums, pltpu.VMEM((48 * wy + 96, z), BF)), [vert], per_hex,
    )(*maps, yd, diag, vs_a, vs_b)
    xd = from_behind(send, "gx", -1)
    c_c2, vs_c2 = call(
        partial(last_row_kernel, wx, wy), (contribs(wx - 2), sums), [], (wx - 2) * per_hex
    )(*maps, yd)
    c_d, vs_d, vs_x, send = pl.pallas_call(
        partial(after_x_kernel, wx, wy),
        in_specs=[pl.BlockSpec(memory_space=pltpu.SMEM)] + [pl.BlockSpec(memory_space=pltpu.VMEM)] * 7,
        out_shape=(contribs(wy), sums, sums, pltpu.VMEM((48 * wy + 32, z), BF)),
        scratch_shapes=[vert],
        cost_estimate=pl.CostEstimate(flops=(wy + 1) * per_hex, bytes_accessed=1000000, transcendentals=0),
        compiler_params=pltpu.CompilerParams(vmem_limit_bytes=16 * 1024 * 1024),
    )(viscosity, *maps, yd, xd)
    xu = from_behind(send, "gx", 1)
    send = call(partial(up_y_kernel, wx, wy), pltpu.VMEM((48 * wx + 32, z), BF), [vert], 1000)(
        c_c, c_c2, c_d, vs_c, vs_c2, vs_d, xd, xu
    )
    yu = from_behind(send, "gy", 1)
    residual, vs, inverse = call(
        partial(assemble_kernel, wx, wy),
        (pltpu.VMEM((3, 48 * cells, z), F32), sums, sums), [sums], 1000000,
    )(diag, c_a, c_b, c_c, c_c2, c_d, vs_a, vs_b, vs_c, vs_c2, vs_d, vs_x, yd, xd, xu)
    out = call(
        partial(final_kernel, wx, wy),
        jax.ShapeDtypeStruct((3, 48 * cells, z), BF),
        [pltpu.VMEM((spread.shape[1], z), F32), sums], 2 * spread.size * z,
    )(flags, residual, vs, inverse, yu, spread)
    return out.reshape(traces.shape)


def solution(mesh):
    in_specs = (
        P(None, None, "gx", "gy", None),
        P(None, "gx", "gy", None),
        P("gx", "gy", None),
        P(),
        P("gx", "gy", None),
        P(),
        P(),
    )
    out_specs = P(None, None, "gx", "gy", None)
    return jax.shard_map(local, mesh=mesh, in_specs=in_specs, out_specs=out_specs, check_vma=False)
```

```python
import functools
import math

import jax
import jax.numpy as jnp
import ml_dtypes
import numpy as np
from jax import lax
from jax.experimental import pallas as pl
from jax.experimental.pallas import tpu as pltpu
from jax.sharding import PartitionSpec as P

penalty = 0.5
BF = jnp.bfloat16
F32 = jnp.float32
lift = 1.3264
gain = 1.3280711361297461


def from_behind(value, axis, steps):
    count = lax.axis_size(axis)
    leading, last = (max(0, -steps), min(count, count - steps))
    return lax.ppermute(value, axis, [(source, source + steps) for source in range(leading, last)])


def corner_table():
    gll_points = [-1.0, -math.sqrt(0.2), math.sqrt(0.2), 1.0]
    table = np.zeros((16, 4), np.float64)
    for s in range(4):
        for t in range(4):
            for p in range(2):
                for q in range(2):
                    table[4 * s + t, 2 * p + q] = (
                        (1 + (2 * p - 1) * gll_points[s]) * (1 + (2 * q - 1) * gll_points[t]) / 4
                    )
    return table


def landing(face_slot, high_s, high_t):
    direction, outward = divmod(face_slot, 2)
    if direction == 0:
        return (outward, high_s, high_t)
    if direction == 1:
        return (high_s, outward, high_t)
    return (high_s, high_t, outward)


def gather_table():
    weights = lift * corner_table()
    table = np.zeros((32, 288), np.float64)
    for slot in range(6):
        for s in range(2):
            for t in range(2):
                p, q, r = landing(slot, s, t)
                for c in range(3):
                    cols = slot * 48 + 16 * c + np.arange(16)
                    table[16 * r + 8 * p + 4 * q + c, cols] += weights[:, 2 * s + t]
    return table.astype(ml_dtypes.bfloat16)


def slot_table():
    return np.concatenate(np.split(gather_table(), 6, axis=1), axis=0)


def spread_table(wx, wy, rows):
    weights = lift * corner_table()
    planes = (wx + 1) * rows
    depth = -(-2 * planes // 128) * 128
    table = np.zeros((3, 48, wx, wy, depth), np.float64)
    for d in range(3):
        for x in range(wx):
            for y in range(wy):
                for s in range(2):
                    for t in range(2):
                        p, q, r = landing(2 * d, s, t)
                        for c in range(3):
                            k = r * planes + (x + p) * rows + 4 * (y + q) + c
                            table[d, 16 * c : 16 * c + 16, x, y, k] += weights[:, 2 * s + t]
    return table.reshape(-1, depth).astype(ml_dtypes.bfloat16)


def lanes(shape):
    return lax.broadcasted_iota(jnp.int32, shape, len(shape) - 1)


def z_next(value):
    last = value.shape[-1] - 1
    return jnp.where(lanes(value.shape) < last, pltpu.roll(value, last, value.ndim - 1), 0.0)


def z_prev(value):
    return jnp.where(lanes(value.shape) > 0, pltpu.roll(value, 1, value.ndim - 1), 0.0)


def dot(left, right):
    return jnp.dot(left, right, preferred_element_type=F32)


def wide(parts):
    return jnp.concatenate(parts, axis=1)


def tall(parts):
    return jnp.concatenate(parts, axis=0)


def hex_batch(slots, scales, s_map, f_map):
    z = slots[0][0].shape[1]
    element = tall([wide([hexa[s] for hexa in slots]) for s in range(6)])
    interior = dot(s_map, element).astype(BF)
    flux = dot(f_map, interior) + penalty * element.astype(F32)
    return [
        [flux[48 * s : 48 * s + 48, z * h : z * h + z] * scales[h][s] for s in range(6)]
        for h in range(len(slots))
    ]


def corner_batch(blocks, left_out, gather):
    z = blocks[0][0].shape[1]
    nothing = jnp.zeros((48, z), BF)
    right = tall(
        [
            wide([nothing if s in left_out[h] else blocks[h][s].astype(BF) for h in range(len(blocks))])
            for s in range(6)
        ]
    )
    return [dot(gather, right)[:, z * h : z * h + z] for h in range(len(blocks))]


def slot_corners(traces, parts_ref, slot):
    z = traces[0].shape[1]
    rows = dot(parts_ref[pl.ds(32 * slot, 32), :], wide([trace.astype(BF) for trace in traces]))
    return [rows[:, z * h : z * h + z] for h in range(len(traces))]


def settle(rows, p):
    return rows[8 * p : 8 * p + 8] + z_prev(rows[16 + 8 * p : 24 + 8 * p])


def scaled_corners(delta, scales):
    terms = [delta[32 * s : 32 * s + 32] * scales[s] for s in range(6) if scales[s] is not None]
    return sum(terms[1:], terms[0])


def level_visc(code, visc_ref):
    visc = jnp.zeros(code.shape, F32)
    for level in range(visc_ref.shape[0]):
        visc = visc + jnp.where(code == F32(level + 1), visc_ref[level], F32(0.0))
    return visc


def merge(even, odd):
    odd = tall(odd)
    return tall(even) + pltpu.roll(odd, odd.shape[0] - 4, 0)


def first_kernel(
    wx, wy, visc_ref, t_hbm, dir_hbm, cls_hbm, diag_hbm, st_hbm, f_hbm, g_hbm, parts_hbm,
    l_ref, kp_ref, diag_ref, s_ref, st_ref, f_ref, g_ref, parts_ref, c_ref, v_ref, v1_ref, v3_ref,
    down_ref, up_ref, t_ref, dir_ref, cls_ref, nat, sems,
):
    cells = wx * wy
    pairs = [
        (t_hbm, t_ref), (dir_hbm, dir_ref), (cls_hbm, cls_ref), (diag_hbm, diag_ref),
        (st_hbm, st_ref), (f_hbm, f_ref), (g_hbm, g_ref), (parts_hbm, parts_ref),
    ]
    copies = [pltpu.make_async_copy(a, b, sems.at[i]) for i, (a, b) in enumerate(pairs)]
    for copy in copies:
        copy.start()
    copies[4].wait()
    s_ref[...] = st_ref[...].T
    for i in (1, 2, 3, 0):
        copies[i].wait()
    z = t_ref.shape[2]
    code = cls_ref[...].astype(F32) + 1.0
    kp_ref[4] = level_visc(code, visc_ref)
    kp_ref[5] = code
    for d in range(3):
        keep = (1 - dir_ref[d]).astype(F32)
        kp_ref[d] = keep
        masked = t_ref[d].astype(F32).reshape(48, cells, z) * keep[None]
        nat[...] = masked.reshape(48 * cells, z)
        for col in range(cells):
            part = nat[pl.ds(col, 48, stride=cells), :]
            l_ref[d, col] = part.astype(BF)
            if d == 2:
                l_ref[3, col] = z_next(part).astype(BF)
    kp_ref[3] = z_next(kp_ref[2])
    for i in (5, 6, 7):
        copies[i].wait()
    row = lambda i, col: kp_ref[i, pl.ds(col, 1), :]
    where = [(x, 0) for x in range(wx)] + [(x, wy - 1) for x in range(wx)]
    blocks, left_out = known_hexes(wx, wy, where, l_ref, kp_ref, s_ref, f_ref, c_ref)
    corners = corner_batch(blocks, left_out, g_ref[...])
    lone = slot_corners([blocks[wx - 1][1], blocks[2 * wx - 1][1]], parts_ref, 1)
    for h in range(2):
        v1_ref[h, 0:8] = lone[h][8:16]
        v1_ref[h, 8:16] = lone[h][24:32]
    for x, rows in enumerate(slot_corners([blocks[wx + x][3] for x in range(wx)], parts_ref, 3)):
        v3_ref[x] = rows
    sums = [line_sums(corners[:wx]), line_sums(corners[wx:])]
    for side in range(2):
        for i in range(wx + 1):
            v_ref[side, i] = sums[side][i]
    corner = (wx - 1) * wy
    top = wy - 1
    for x in range(wx):
        down_ref[pl.ds(48 * x, 48), :] = l_ref[1, x * wy]
        up_ref[pl.ds(48 * x, 48), :] = blocks[wx + x][3].astype(BF)
    down_ref[pl.ds(48 * wx, 48), :] = l_ref[0, 0]
    up_ref[pl.ds(48 * wx, 48), :] = l_ref[0, top]
    place = lax.broadcasted_iota(jnp.int32, (8, z), 0)
    rim = []
    for i in range(wx):
        diag = diag_ref[pl.ds(i * wy, 1), :]
        high = diag.astype(BF).astype(F32)
        rim.append(jnp.where(place == 4, high, jnp.where(place == 5, diag - high, sums[0][i])))
    rim += [sums[0][wx], v1_ref[0]]
    rim += [row(1, x * wy) for x in range(wx)] + [row(0, 0), row(5, corner), row(0, corner), row(2, corner)]
    put_tail(down_ref, 48 * wx + 48, rim)
    rim = [sums[1][i] for i in range(wx + 1)] + [v1_ref[1]]
    for kind in (5, 0, 2):
        rim += [row(kind, x * wy + top) for x in range(wx)]
    put_tail(up_ref, 48 * wx + 48, rim)


def tail_rows(count):
    return -(-count // 16) * 16


def put_tail(ref, start, rows):
    count = sum(part.shape[0] for part in rows)
    full = tail_rows(count)
    if full > count:
        rows = rows + [jnp.zeros((full - count, rows[0].shape[1]), F32)]
    ref[pl.ds(start, full), :] = tall(rows).astype(BF)


def tail_misc(ref, wx):
    start = 48 * wx + 48
    return ref[pl.ds(start, ref.shape[0] - start), :].astype(F32)[8 * (wx + 1) + 16 :]


def line_sums(corners):
    width = len(corners)
    low = [settle(rows, 0) for rows in corners]
    high = [settle(rows, 1) for rows in corners]
    return [low[0]] + [low[x] + high[x - 1] for x in range(1, width)] + [high[-1]]


def known_hexes(wx, wy, where, l_ref, kp_ref, s_ref, f_ref, c_ref):
    z = l_ref.shape[3]
    nothing = jnp.zeros((48, z), BF)
    row = lambda i, col: kp_ref[i, pl.ds(col, 1), :]
    slots, scales, left_out = [], [], []
    for x, y in where:
        here = x * wy + y
        visc = row(4, here)
        last_x, last_y = x == wx - 1, y == wy - 1
        slots.append(
            [
                l_ref[0, here], nothing if last_x else l_ref[0, here + wy],
                l_ref[1, here], nothing if last_y else l_ref[1, here + 1],
                l_ref[2, here], l_ref[3, here],
            ]
        )
        scales.append(
            [
                visc * row(0, here), visc if last_x else visc * row(0, here + wy),
                visc * row(1, here), visc if last_y else visc * row(1, here + 1),
                visc * row(2, here), visc * row(3, here),
            ]
        )
        left_out.append(([1] if last_x else []) + ([3] if last_y else []))
    blocks = hex_batch(slots, scales, s_ref[...], f_ref[...])
    for h in range(len(where)):
        for s in range(6):
            c_ref[s, h] = blocks[h][s]
    return blocks, left_out


def middle_kernel(
    wx, wy, l_ref, kp_ref, s_ref, st_ref, f_ref, g_ref, parts_ref,
    c_ref, v_ref, v1_ref, mx_ref, my_ref, own_ref,
):
    z = l_ref.shape[3]
    for slot, ref in ((1, mx_ref), (3, my_ref)):
        flux = lax.dot_general(
            f_ref[...], st_ref[pl.ds(48 * slot, 48), :], (((1,), (1,)), ((), ())),
            preferred_element_type=F32,
        )
        ref[pl.ds(0, 288), :] = flux.astype(BF)
        eye = lax.broadcasted_iota(jnp.int32, (48, 48), 0) == lax.broadcasted_iota(jnp.int32, (48, 48), 1)
        for s in range(6):
            block = flux[48 * s : 48 * s + 48]
            if s == slot:
                block = block + jnp.where(eye, F32(penalty), F32(0.0))
            ref[pl.ds(288 + 32 * s, 32), :] = dot(parts_ref[pl.ds(32 * s, 32), :], block.astype(BF)).astype(BF)
    own_ref[...] = dot(tall([my_ref[pl.ds(144, 48), :], my_ref[pl.ds(288, 192), :]]), wide([l_ref[1, x * wy] for x in range(wx)]))
    where = [(x, y) for y in range(1, wy - 1) for x in range(wx)]
    blocks, left_out = known_hexes(wx, wy, where, l_ref, kp_ref, s_ref, f_ref, c_ref)
    corners = corner_batch(blocks, left_out, g_ref[...])
    lone = slot_corners([blocks[wx * y + wx - 1][1] for y in range(wy - 2)], parts_ref, 1)
    for y in range(wy - 2):
        v1_ref[y, 0:8] = lone[y][8:16]
        v1_ref[y, 8:16] = lone[y][24:32]
        for i, rows in enumerate(line_sums(corners[wx * y : wx * y + wx])):
            v_ref[y, i] = rows


def after_y(wx, wy, xs, visc_ref, l_ref, kp_ref, parts_ref, my_ref, own_ref, v3_ref, down_ref, up_ref):
    z = l_ref.shape[3]
    misc_d = tail_misc(down_ref, wx)
    misc_u = tail_misc(up_ref, wx)
    row = lambda i, col: kp_ref[i, pl.ds(col, 1), :]
    delta = dot(my_ref[...], wide([down_ref[pl.ds(48 * x, 48), :] for x in xs]))
    arrived = [up_ref[pl.ds(48 * x, 48), :].astype(F32) for x in xs]
    arrived_corners = slot_corners(arrived, parts_ref, 3)
    results = []
    for n, x in enumerate(xs):
        here = x * wy + wy - 1
        last = x == wx - 1
        part = delta[:, z * n : z * n + z]
        visc = row(4, here)
        scales = [
            visc * row(0, here), visc if last else visc * row(0, here + wy), visc * row(1, here),
            visc * misc_d[x : x + 1], visc * row(2, here), visc * row(3, here),
        ]
        flux = [part[48 * s : 48 * s + 48] * scales[s] for s in range(6)]
        used = [None if (s == 1 and last) else scales[s] for s in range(6)]
        top = scaled_corners(part[288:480], used) + v3_ref[x] * misc_d[x : x + 1]
        top_one = part[320:352] * visc
        here = x * wy
        visc = level_visc(misc_u[x : x + 1], visc_ref)
        flag = row(1, here)
        own = own_ref[:, pl.ds(z * x, z)]
        keep_z = misc_u[2 * wx + x : 2 * wx + x + 1]
        scales = [
            visc * misc_u[wx + x : wx + x + 1], None if last else visc * misc_u[wx + x + 1 : wx + x + 2],
            None, visc * flag, visc * keep_z, visc * z_next(keep_z),
        ]
        low = scaled_corners(own[48:240], scales) + arrived_corners[n] * flag
        low_one = own[80:112] * visc
        face = (arrived[n] + visc * (own[0:48] + penalty * l_ref[1, here].astype(F32))) * flag
        results.append((flux, top, top_one, low, low_one, face))
    return results


def turn_kernel(
    wx, wy, visc_ref, l_ref, kp_ref, diag_ref, parts_ref, my_ref, own_ref, c1_ref, c2_ref, va_ref, vb_ref,
    v1a_ref, v1b_ref, v3_ref, yd_ref, yu_ref,
    c3_ref, vt_ref, vl_ref, v1_ref, face_ref, down_ref, up_ref,
):
    z = l_ref.shape[3]
    xs = (0, wx - 1)
    results = after_y(wx, wy, xs, visc_ref, l_ref, kp_ref, parts_ref, my_ref, own_ref, v3_ref, yd_ref, yu_ref)
    row = lambda i, col: kp_ref[i, pl.ds(col, 1), :]
    tail = 48 * wx + 48
    rim_d = yd_ref[pl.ds(tail, yd_ref.shape[0] - tail), :].astype(F32)
    rim_u = yu_ref[pl.ds(tail, yu_ref.shape[0] - tail), :].astype(F32)
    ones = 8 * (wx + 1)
    base = ones + 16
    for n, (flux, top, top_one, low, low_one, face) in enumerate(results):
        for s in range(6):
            c3_ref[n, s] = flux[s]
        face_ref[n] = face
        for p in range(2):
            vt_ref[n, p] = settle(top, p)
            vl_ref[n, p] = settle(low, p)
    flux, top, top_one, low, low_one, face = results[1]
    mine = rim_u[ones : ones + 16] + tall([low_one[8:16], low_one[24:32]])
    v1_ref[0] = mine
    v1_ref[1] = v1a_ref[0]
    for y in range(wy - 2):
        v1_ref[2 + y] = v1b_ref[y]
    v1_ref[wy] = v1a_ref[1] + tall([top_one[8:16], top_one[24:32]])
    v1_ref[wy + 1] = rim_d[ones : ones + 16]

    def plane(i, n, p):
        lines = [rim_u[8 * i : 8 * i + 8] + vl_ref[n, p], va_ref[0, i]]
        lines += [vb_ref[y, i] for y in range(wy - 2)]
        lines += [va_ref[1, i] + vt_ref[n, p], rim_d[8 * i : 8 * i + 8]]
        return merge(lines[1::2], lines[0::2])

    down_ref[pl.ds(0, 48), :] = yu_ref[pl.ds(48 * wx, 48), :]
    for y in range(wy):
        down_ref[pl.ds(48 + 48 * y, 48), :] = l_ref[0, y]
    down_ref[pl.ds(48 * (wy + 1), 48), :] = yd_ref[pl.ds(48 * wx, 48), :]
    diag = [jnp.broadcast_to(diag_ref[pl.ds(y, 1), :], (4, z)) for y in range(wy)]
    high = [part.astype(BF).astype(F32) for part in diag]
    low_bits = [a - b for a, b in zip(diag, high)]
    high += [jnp.broadcast_to(rim_d[4:5], (4, z)), jnp.zeros((4, z), F32)]
    low_bits += [jnp.broadcast_to(rim_d[5:6], (4, z)), jnp.zeros((4, z), F32)]
    rim = [plane(0, 0, 0)] + high + low_bits
    rim += [rim_u[base + wx : base + wx + 1], kp_ref[0, 0:wy], rim_d[base + wx : base + wx + 1]]
    put_tail(down_ref, 48 * (wy + 2), rim)
    corner = (wx - 1) * wy
    up_ref[pl.ds(0, 48), :] = c1_ref[1, wx - 1].astype(BF)
    for y in range(1, wy - 1):
        up_ref[pl.ds(48 * y, 48), :] = c2_ref[1, wx * (y - 1) + wx - 1].astype(BF)
    up_ref[pl.ds(48 * (wy - 1), 48), :] = (c1_ref[1, 2 * wx - 1] + flux[1]).astype(BF)
    last = pl.ds(corner, wy)
    rim = [plane(wx, 1, 1), mine, rim_d[ones : ones + 16]]
    rim += [rim_u[base + wx - 1 : base + wx], kp_ref[5, last], rim_d[base + wx + 1 : base + wx + 2]]
    rim += [rim_u[base + 3 * wx - 1 : base + 3 * wx], kp_ref[2, last], rim_d[base + wx + 3 : base + wx + 4]]
    rim += [kp_ref[1, last], rim_d[base + wx - 1 : base + wx]]
    put_tail(up_ref, 48 * wy, rim)


def assemble_kernel(
    wx, wy, visc_ref, l_ref, kp_ref, diag_ref, parts_ref, mx_ref, my_ref, own_ref, c1_ref, c2_ref, c3_ref,
    va_ref, vb_ref, v3_ref, vt_ref, vl_ref, face_ref, yd_ref, yu_ref,
    r_ref, v_ref, inv_ref, ownx_ref, mid,
):
    z = l_ref.shape[3]
    cells = wx * wy
    xs = tuple(range(1, wx - 1))
    results = after_y(wx, wy, xs, visc_ref, l_ref, kp_ref, parts_ref, my_ref, own_ref, v3_ref, yd_ref, yu_ref)
    for n, part in enumerate(results):
        for s in range(6):
            mid[n, s] = part[0][s]
    traces = [yu_ref[pl.ds(48 * wx, 48), :]] + [l_ref[0, y] for y in range(wy)] + [yd_ref[pl.ds(48 * wx, 48), :]]
    ownx_ref[...] = dot(tall([mx_ref[pl.ds(48, 48), :], mx_ref[pl.ds(288, 192), :]]), wide(traces))

    def contrib(slot, x, y):
        if 0 < y < wy - 1:
            return c2_ref[slot, wx * (y - 1) + x]
        if y == 0:
            return c1_ref[slot, x]
        extra = mid[x - 1, slot] if 0 < x < wx - 1 else c3_ref[0 if x == 0 else 1, slot]
        return c1_ref[slot, wx + x] + extra

    for x in range(wx):
        for y in range(wy):
            col = pl.ds(x * wy + y, 48, stride=cells)
            if x:
                r_ref[0, col, :] = contrib(0, x, y) + contrib(1, x - 1, y)
            else:
                r_ref[0, col, :] = contrib(0, x, y)
            if y:
                behind = contrib(3, x, y - 1)
            elif 0 < x < wx - 1:
                behind = results[x - 1][5]
            else:
                behind = face_ref[0 if x == 0 else 1]
            r_ref[1, col, :] = contrib(2, x, y) + behind
            r_ref[2, col, :] = contrib(4, x, y) + z_prev(contrib(5, x, y))
    tail = 48 * wx + 48
    rim_d = yd_ref[pl.ds(tail, yd_ref.shape[0] - tail), :].astype(F32)
    rim_u = yu_ref[pl.ds(tail, yu_ref.shape[0] - tail), :].astype(F32)

    def brought(which, i):
        held = vt_ref if which == 1 else vl_ref
        terms = []
        for x, p in ((i, 0), (i - 1, 1)):
            if x in (0, wx - 1):
                terms.append(held[0 if x == 0 else 1, p])
            elif 0 < x < wx - 1:
                terms.append(settle(results[x - 1][which], p))
        return sum(terms[1:], terms[0])

    for i in range(wx + 1):
        lines = [rim_u[8 * i : 8 * i + 8] + brought(3, i), va_ref[0, i]]
        lines += [vb_ref[y, i] for y in range(wy - 2)]
        lines += [va_ref[1, i] + brought(1, i), rim_d[8 * i : 8 * i + 8]]
        v_ref[i] = merge(lines[1::2], lines[0::2])
        if i < wx:
            parts = [jnp.broadcast_to(diag_ref[pl.ds(i * wy + y, 1), :], (4, z)) for y in range(wy)]
            edge = rim_d[8 * i + 4 : 8 * i + 5] + rim_d[8 * i + 5 : 8 * i + 6]
            parts += [jnp.broadcast_to(edge, (4, z)), jnp.zeros((4, z), F32)]
            inv_ref[i] = reciprocal(tall(parts))


def reciprocal(diag):
    present = diag > 0.0
    return jnp.where(present, (1.0 / (gain * gain)) / jnp.where(present, diag, 1.0), 0.0)


def final_kernel(
    wx, wy, visc_ref, l_ref, kp_ref, parts_ref, mx_ref, ownx_ref, r_ref, v_ref, inv_ref, v1_ref,
    yd_ref, yu_ref, xd_ref, xu_ref, p_ref, out_ref, fix,
):
    cells, z = wx * wy, l_ref.shape[3]
    rows = v_ref.shape[1]
    planes = (wx + 1) * rows
    row = lambda i, col: kp_ref[i, pl.ds(col, 1), :]
    delta = dot(mx_ref[...], wide([xd_ref[pl.ds(48 * j, 48), :] for j in range(wy + 2)]))
    rim_x = xd_ref[pl.ds(48 * (wy + 2), xd_ref.shape[0] - 48 * (wy + 2)), :].astype(F32)
    rim_l = xu_ref[pl.ds(48 * wy, xu_ref.shape[0] - 48 * wy), :].astype(F32)
    misc_d = tail_misc(yd_ref, wx)
    misc_u = tail_misc(yu_ref, wx)
    flags_high = rim_x[3 * rows : 3 * rows + wy + 2]
    corner = (wx - 1) * wy
    arrived = [xu_ref[pl.ds(48 * y, 48), :].astype(F32) for y in range(wy)]
    arrived_corners = slot_corners(arrived, parts_ref, 1)
    codes = rim_l[rows + 32 : rows + 32 + wy + 2]
    keep_z = rim_l[rows + 32 + wy + 2 : rows + 32 + 2 * (wy + 2)]
    keep_y = rim_l[rows + 32 + 2 * (wy + 2) : rows + 32 + 3 * (wy + 2) - 1]
    low_visc = level_visc(codes, visc_ref)
    low_keep_z = z_next(keep_z)
    lines = [[], [], []]
    high_flux = []
    for j in range(-1, wy + 1):
        n = j + 1
        part = delta[:, z * n : z * n + z]
        flag = flags_high[n : n + 1]
        if j < 0:
            visc = level_visc(misc_u[wx - 1 : wx], visc_ref)
            kz = misc_u[3 * wx - 1 : 3 * wx]
            keeps = [misc_u[2 * wx - 1 : 2 * wx], flag, None, row(1, corner), kz, z_next(kz)]
        elif j < wy:
            here = corner + j
            visc = row(4, here)
            high_y = row(1, here + 1) if j < wy - 1 else misc_d[wx - 1 : wx]
            keeps = [row(0, here), flag, row(1, here), high_y, row(2, here), row(3, here)]
        else:
            visc = level_visc(misc_d[wx + 1 : wx + 2], visc_ref)
            kz = misc_d[wx + 3 : wx + 4]
            keeps = [misc_d[wx + 2 : wx + 3], flag, misc_d[wx - 1 : wx], None, kz, z_next(kz)]
        scales = [None if keep is None else visc * keep for keep in keeps]
        corners = scaled_corners(part[288:480], scales)
        one = v1_ref[n] * flag
        lines[0].append(settle(corners, 0))
        lines[1].append(settle(corners, 1) + one[0:8] + z_prev(one[8:16]))
        high_flux.append([None if k is None else part[48 * s : 48 * s + 48] * k for s, k in enumerate(scales)])
        own = ownx_ref[:, pl.ds(z * n, z)]
        visc = low_visc[n : n + 1]
        flag = misc_u[wx : wx + 1] if j < 0 else misc_d[wx : wx + 1] if j == wy else row(0, j)
        scales = [
            None, visc * flag, None if j < 0 else visc * keep_y[j : j + 1],
            None if j == wy else visc * keep_y[j + 1 : j + 2], visc * keep_z[n : n + 1], visc * low_keep_z[n : n + 1],
        ]
        corners = settle(scaled_corners(own[48:240], scales), 1)
        if 0 <= j < wy:
            lines[2].append(corners + settle(arrived_corners[j] * flag, 1))
            face = (arrived[j] + visc * (own[0:48] + penalty * l_ref[0, j].astype(F32))) * flag
            r_ref[0, pl.ds(j, 48, stride=cells), :] += face
        else:
            at = rows + (0 if j < 0 else 16)
            one = rim_l[at : at + 16] * flag
            lines[2].append(corners + one[0:8] + z_prev(one[8:16]))
    low, before, first = [merge(part[1::2], part[0::2]) for part in lines]
    top = v_ref[wx] + before + rim_x[0:rows]
    values = [(v_ref[0] + first + rim_l[0:rows]) * inv_ref[0]]
    values += [v_ref[i] * inv_ref[i] for i in range(1, wx - 1)]
    values += [(v_ref[wx - 1] + low) * inv_ref[wx - 1]]
    values += [top * reciprocal(rim_x[rows : 2 * rows] + rim_x[2 * rows : 3 * rows])]
    value = tall(values)
    fix[...] = jnp.zeros_like(fix)
    fix[pl.ds(0, planes), :] = value
    fix[pl.ds(planes, planes), :] = z_next(value)
    rhs = fix[...].astype(BF)
    for j in range(wy):
        col = pl.ds(corner + j, 48, stride=cells)
        flux = high_flux[j + 1]
        r_ref[0, col, :] += flux[0]
        r_ref[1, col, :] += flux[2] + high_flux[j][3]
        r_ref[2, col, :] += flux[4] + z_prev(flux[5])
    for d in range(3):
        spread = dot(p_ref[pl.ds(48 * cells * d, 48 * cells), :], rhs)
        spread = spread.reshape(48, cells, z) * kp_ref[d][None]
        out_ref[d] = (r_ref[d] + spread.reshape(48 * cells, z)).astype(BF)


def call(body, args, outs, scratch, flops, scalars=0, hbm=False):
    space = pltpu.HBM if hbm else pltpu.VMEM
    specs = [pl.BlockSpec(memory_space=pltpu.SMEM)] * scalars
    specs += [pl.BlockSpec(memory_space=space)] * (len(args) - scalars)
    return pl.pallas_call(
        body,
        in_specs=specs,
        out_shape=outs,
        scratch_shapes=scratch,
        cost_estimate=pl.CostEstimate(flops=flops, bytes_accessed=1000000, transcendentals=0),
        compiler_params=pltpu.CompilerParams(vmem_limit_bytes=16 * 1024 * 1024),
    )(*args)


def local(traces, dirichlet, visc_class, viscosity, coarse_diag, solve_map, flux_map):
    wx, wy, z = traces.shape[2:]
    cells = wx * wy
    rows = 8 * (wy // 2 + 1)
    per_hex = 4 * 288 * 256 * z
    gather = jnp.asarray(gather_table())
    parts = jnp.asarray(slot_table())
    spread = jnp.asarray(spread_table(wx, wy, rows))
    vm = pltpu.VMEM
    bind = lambda body: functools.partial(body, wx, wy)
    base = 48 * wx + 48

    (lifted, flags, diag, s_map, s_turned, f_map, gather, parts, c1, va, v1a, v3, down, up) = call(
        bind(first_kernel),
        (
            viscosity, traces.reshape(3, 48 * cells, z), dirichlet.reshape(3, cells, z),
            visc_class.reshape(cells, z), coarse_diag.reshape(cells, z), solve_map.T, flux_map, gather, parts,
        ),
        (
            vm((4, cells, 48, z), BF), vm((6, cells, z), F32), vm((cells, z), F32), vm(solve_map.shape, BF),
            vm(solve_map.shape[::-1], BF), vm(flux_map.shape, BF), vm(gather.shape, BF), vm(parts.shape, BF),
            vm((6, 2 * wx, 48, z), F32), vm((2, wx + 1, 8, z), F32), vm((2, 16, z), F32), vm((wx, 32, z), F32),
            vm((base + tail_rows(8 * (wx + 1) + 16 + wx + 4), z), BF),
            vm((base + tail_rows(8 * (wx + 1) + 16 + 3 * wx), z), BF),
        ),
        [
            vm((3, 48 * cells, z), BF), vm((3, cells, z), jnp.int32), vm((cells, z), jnp.int32),
            vm((48 * cells, z), F32), pltpu.SemaphoreType.DMA((8,)),
        ],
        2 * wx * per_hex, 1, True,
    )
    yd = from_behind(down, "gy", -1)
    yu = from_behind(up, "gy", 1)
    inner = wx * (wy - 2)
    c2, vb, v1b, mx, my, own = call(
        bind(middle_kernel),
        (lifted, flags, s_map, s_turned, f_map, gather, parts),
        (
            vm((6, inner, 48, z), F32), vm((wy - 2, wx + 1, 8, z), F32), vm((wy - 2, 16, z), F32),
            vm((480, 48), BF), vm((480, 48), BF), vm((240, wx * z), F32),
        ),
        [], inner * per_hex,
    )
    c3, vt, vl, v1, face, down, up = call(
        bind(turn_kernel),
        (
            viscosity, lifted, flags, diag, parts, my, own, c1, c2, va, vb, v1a, v1b, v3, yd, yu,
        ),
        (
            vm((2, 6, 48, z), F32), vm((2, 2, 8, z), F32), vm((2, 2, 8, z), F32), vm((wy + 2, 16, z), F32),
            vm((2, 48, z), F32), vm((48 * (wy + 2) + tail_rows(3 * rows + wy + 2), z), BF),
            vm((48 * wy + tail_rows(rows + 32 + 3 * (wy + 2) - 1), z), BF),
        ),
        [], 2 * per_hex, 1,
    )
    xd = from_behind(down, "gx", -1)
    xu = from_behind(up, "gx", 1)
    residual, vs, inverse, ownx = call(
        bind(assemble_kernel),
        (
            viscosity, lifted, flags, diag, parts, mx, my, own, c1, c2, c3, va, vb, v3, vt, vl, face, yd, yu,
        ),
        (
            vm((3, 48 * cells, z), F32), vm((wx + 1, rows, z), F32), vm((wx, rows, z), F32),
            vm((240, (wy + 2) * z), F32),
        ),
        [vm((wx - 2, 6, 48, z), F32)], 4 * per_hex, 1,
    )
    out = call(
        bind(final_kernel),
        (
            viscosity, lifted, flags, parts, mx, ownx, residual, vs, inverse, v1, yd, yu, xd, xu, spread,
        ),
        jax.ShapeDtypeStruct((3, 48 * cells, z), BF),
        [vm((spread.shape[1], z), F32)], 2 * spread.size * z, 1,
    )
    return out.reshape(traces.shape)


def solution(mesh):
    in_specs = (
        P(None, None, "gx", "gy", None),
        P(None, "gx", "gy", None),
        P("gx", "gy", None),
        P(),
        P("gx", "gy", None),
        P(),
        P(),
    )
    out_specs = P(None, None, "gx", "gy", None)
    return jax.shard_map(local, mesh=mesh, in_specs=in_specs, out_specs=out_specs, check_vma=False)
```

```python
import functools
import math

import jax
import jax.numpy as jnp
import ml_dtypes
import numpy as np
from jax import lax
from jax.experimental import pallas as pl
from jax.experimental.pallas import tpu as pltpu
from jax.sharding import PartitionSpec as P

penalty = 0.5
BF = jnp.bfloat16
F32 = jnp.float32
lift = 1.3264
gain = 1.3280711361297461


def from_behind(value, axis, steps):
    count = lax.axis_size(axis)
    leading, last = (max(0, -steps), min(count, count - steps))
    return lax.ppermute(value, axis, [(source, source + steps) for source in range(leading, last)])


def corner_table():
    gll_points = [-1.0, -math.sqrt(0.2), math.sqrt(0.2), 1.0]
    table = np.zeros((16, 4), np.float64)
    for s in range(4):
        for t in range(4):
            for p in range(2):
                for q in range(2):
                    table[4 * s + t, 2 * p + q] = (
                        (1 + (2 * p - 1) * gll_points[s]) * (1 + (2 * q - 1) * gll_points[t]) / 4
                    )
    return table


def landing(face_slot, high_s, high_t):
    direction, outward = divmod(face_slot, 2)
    if direction == 0:
        return (outward, high_s, high_t)
    if direction == 1:
        return (high_s, outward, high_t)
    return (high_s, high_t, outward)


def gather_table():
    weights = lift * corner_table()
    table = np.zeros((32, 288), np.float64)
    for slot in range(6):
        for s in range(2):
            for t in range(2):
                p, q, r = landing(slot, s, t)
                for c in range(3):
                    cols = slot * 48 + 16 * c + np.arange(16)
                    table[16 * r + 8 * p + 4 * q + c, cols] += weights[:, 2 * s + t]
    return table.astype(ml_dtypes.bfloat16)


def slot_table():
    return np.concatenate(np.split(gather_table(), 6, axis=1), axis=0)


def spread_table(wx, wy, rows):
    weights = lift * corner_table()
    planes = (wx + 1) * rows
    depth = -(-2 * planes // 128) * 128
    table = np.zeros((3, 48, wx, wy, depth), np.float64)
    for d in range(3):
        for x in range(wx):
            for y in range(wy):
                for s in range(2):
                    for t in range(2):
                        p, q, r = landing(2 * d, s, t)
                        for c in range(3):
                            k = r * planes + (x + p) * rows + 4 * (y + q) + c
                            table[d, 16 * c : 16 * c + 16, x, y, k] += weights[:, 2 * s + t]
    return table.reshape(-1, depth).astype(ml_dtypes.bfloat16)


def lanes(shape):
    return lax.broadcasted_iota(jnp.int32, shape, len(shape) - 1)


def z_next(value):
    last = value.shape[-1] - 1
    return jnp.where(lanes(value.shape) < last, pltpu.roll(value, last, value.ndim - 1), 0.0)


def z_prev(value):
    return jnp.where(lanes(value.shape) > 0, pltpu.roll(value, 1, value.ndim - 1), 0.0)


def dot(left, right):
    return jnp.dot(left, right, preferred_element_type=F32)


def wide(parts):
    return jnp.concatenate(parts, axis=1)


def tall(parts):
    return jnp.concatenate(parts, axis=0)


def hex_batch(slots, scales, s_map, f_map):
    z = slots[0][0].shape[1]
    element = tall([wide([hexa[s] for hexa in slots]) for s in range(6)])
    interior = dot(s_map, element).astype(BF)
    flux = dot(f_map, interior) + penalty * element.astype(F32)
    return [
        [flux[48 * s : 48 * s + 48, z * h : z * h + z] * scales[h][s] for s in range(6)]
        for h in range(len(slots))
    ]


def corner_batch(blocks, left_out, gather):
    z = blocks[0][0].shape[1]
    nothing = jnp.zeros((48, z), BF)
    right = tall(
        [
            wide([nothing if s in left_out[h] else blocks[h][s].astype(BF) for h in range(len(blocks))])
            for s in range(6)
        ]
    )
    return [dot(gather, right)[:, z * h : z * h + z] for h in range(len(blocks))]


def slot_corners(traces, parts_ref, slot):
    z = traces[0].shape[1]
    rows = dot(parts_ref[pl.ds(32 * slot, 32), :], wide([trace.astype(BF) for trace in traces]))
    return [rows[:, z * h : z * h + z] for h in range(len(traces))]


def settle(rows, p):
    return rows[8 * p : 8 * p + 8] + z_prev(rows[16 + 8 * p : 24 + 8 * p])


def scaled_corners(delta, scales):
    terms = [delta[32 * s : 32 * s + 32] * scales[s] for s in range(6) if scales[s] is not None]
    return sum(terms[1:], terms[0])


def level_visc(code, visc_ref):
    visc = jnp.zeros(code.shape, F32)
    for level in range(visc_ref.shape[0]):
        visc = visc + jnp.where(code == F32(level + 1), visc_ref[pl.ds(level, 1), :], F32(0.0))
    return visc


def merge(even, odd):
    odd = tall(odd)
    return tall(even) + pltpu.roll(odd, odd.shape[0] - 4, 0)


def first_kernel(
    wx, wy, visc_hbm, t_hbm, dir_hbm, cls_hbm, diag_hbm, st_hbm, f_hbm, g_hbm, parts_hbm,
    l_ref, kp_ref, visc_ref, diag_ref, s_ref, st_ref, f_ref, g_ref, parts_ref, c_ref, v_ref, v1_ref, v3_ref,
    down_ref, up_ref, t_ref, dir_ref, cls_ref, nat, levels, sems,
):
    cells = wx * wy
    pairs = [
        (t_hbm, t_ref), (dir_hbm, dir_ref), (cls_hbm, cls_ref), (diag_hbm, diag_ref),
        (st_hbm, st_ref), (f_hbm, f_ref), (g_hbm, g_ref), (parts_hbm, parts_ref),
        (visc_hbm, levels),
    ]
    copies = [pltpu.make_async_copy(a, b, sems.at[i]) for i, (a, b) in enumerate(pairs)]
    for copy in copies:
        copy.start()
    copies[4].wait()
    s_ref[...] = st_ref[...].T
    for i in (8, 1, 2, 3, 0):
        copies[i].wait()
    z = t_ref.shape[2]
    for level in range(visc_ref.shape[0]):
        visc_ref[pl.ds(level, 1), :] = jnp.full((1, z), levels[level], F32)
    code = cls_ref[...].astype(F32) + 1.0
    kp_ref[4] = level_visc(code, visc_ref)
    kp_ref[5] = code
    for d in range(3):
        keep = (1 - dir_ref[d]).astype(F32)
        kp_ref[d] = keep
        masked = t_ref[d].astype(F32).reshape(48, cells, z) * keep[None]
        nat[...] = masked.reshape(48 * cells, z)
        for col in range(cells):
            part = nat[pl.ds(col, 48, stride=cells), :]
            l_ref[d, col] = part.astype(BF)
            if d == 2:
                l_ref[3, col] = z_next(part).astype(BF)
    kp_ref[3] = z_next(kp_ref[2])
    for i in (5, 6, 7):
        copies[i].wait()
    row = lambda i, col: kp_ref[i, pl.ds(col, 1), :]
    where = [(x, 0) for x in range(wx)] + [(x, wy - 1) for x in range(wx)]
    blocks, left_out = known_hexes(wx, wy, where, l_ref, kp_ref, s_ref, f_ref, c_ref)
    corners = corner_batch(blocks, left_out, g_ref[...])
    lone = slot_corners([blocks[wx - 1][1], blocks[2 * wx - 1][1]], parts_ref, 1)
    for h in range(2):
        v1_ref[h, 0:8] = lone[h][8:16]
        v1_ref[h, 8:16] = lone[h][24:32]
    for x, rows in enumerate(slot_corners([blocks[wx + x][3] for x in range(wx)], parts_ref, 3)):
        v3_ref[x] = rows
    sums = [line_sums(corners[:wx]), line_sums(corners[wx:])]
    for side in range(2):
        for i in range(wx + 1):
            v_ref[side, i] = sums[side][i]
    corner = (wx - 1) * wy
    top = wy - 1
    for x in range(wx):
        down_ref[pl.ds(48 * x, 48), :] = l_ref[1, x * wy]
        up_ref[pl.ds(48 * x, 48), :] = blocks[wx + x][3].astype(BF)
    down_ref[pl.ds(48 * wx, 48), :] = l_ref[0, 0]
    up_ref[pl.ds(48 * wx, 48), :] = l_ref[0, top]
    place = lax.broadcasted_iota(jnp.int32, (8, z), 0)
    rim = []
    for i in range(wx):
        diag = diag_ref[pl.ds(i * wy, 1), :]
        high = diag.astype(BF).astype(F32)
        rim.append(jnp.where(place == 4, high, jnp.where(place == 5, diag - high, sums[0][i])))
    rim += [sums[0][wx], v1_ref[0]]
    rim += [row(1, x * wy) for x in range(wx)] + [row(0, 0), row(5, corner), row(0, corner), row(2, corner)]
    put_tail(down_ref, 48 * wx + 48, rim)
    rim = [sums[1][i] for i in range(wx + 1)] + [v1_ref[1]]
    for kind in (5, 0, 2):
        rim += [row(kind, x * wy + top) for x in range(wx)]
    put_tail(up_ref, 48 * wx + 48, rim)


def tail_rows(count):
    return -(-count // 16) * 16


def put_tail(ref, start, rows):
    count = sum(part.shape[0] for part in rows)
    full = tail_rows(count)
    if full > count:
        rows = rows + [jnp.zeros((full - count, rows[0].shape[1]), F32)]
    ref[pl.ds(start, full), :] = tall(rows).astype(BF)


def tail_misc(ref, wx):
    start = 48 * wx + 48
    return ref[pl.ds(start, ref.shape[0] - start), :].astype(F32)[8 * (wx + 1) + 16 :]


def line_sums(corners):
    width = len(corners)
    low = [settle(rows, 0) for rows in corners]
    high = [settle(rows, 1) for rows in corners]
    return [low[0]] + [low[x] + high[x - 1] for x in range(1, width)] + [high[-1]]


def known_hexes(wx, wy, where, l_ref, kp_ref, s_ref, f_ref, c_ref):
    z = l_ref.shape[3]
    nothing = jnp.zeros((48, z), BF)
    row = lambda i, col: kp_ref[i, pl.ds(col, 1), :]
    slots, scales, left_out = [], [], []
    for x, y in where:
        here = x * wy + y
        visc = row(4, here)
        last_x, last_y = x == wx - 1, y == wy - 1
        slots.append(
            [
                l_ref[0, here], nothing if last_x else l_ref[0, here + wy],
                l_ref[1, here], nothing if last_y else l_ref[1, here + 1],
                l_ref[2, here], l_ref[3, here],
            ]
        )
        scales.append(
            [
                visc * row(0, here), visc if last_x else visc * row(0, here + wy),
                visc * row(1, here), visc if last_y else visc * row(1, here + 1),
                visc * row(2, here), visc * row(3, here),
            ]
        )
        left_out.append(([1] if last_x else []) + ([3] if last_y else []))
    blocks = hex_batch(slots, scales, s_ref[...], f_ref[...])
    for h in range(len(where)):
        for s in range(6):
            c_ref[s, h] = blocks[h][s]
    return blocks, left_out


def middle_kernel(
    wx, wy, l_ref, kp_ref, s_ref, st_ref, f_ref, g_ref, parts_ref,
    c_ref, v_ref, v1_ref, mx_ref, my_ref, own_ref,
):
    z = l_ref.shape[3]
    for slot, ref in ((1, mx_ref), (3, my_ref)):
        flux = lax.dot_general(
            f_ref[...], st_ref[pl.ds(48 * slot, 48), :], (((1,), (1,)), ((), ())),
            preferred_element_type=F32,
        )
        ref[pl.ds(0, 288), :] = flux.astype(BF)
        eye = lax.broadcasted_iota(jnp.int32, (48, 48), 0) == lax.broadcasted_iota(jnp.int32, (48, 48), 1)
        for s in range(6):
            block = flux[48 * s : 48 * s + 48]
            if s == slot:
                block = block + jnp.where(eye, F32(penalty), F32(0.0))
            ref[pl.ds(288 + 32 * s, 32), :] = dot(parts_ref[pl.ds(32 * s, 32), :], block.astype(BF)).astype(BF)
    own_ref[...] = dot(tall([my_ref[pl.ds(144, 48), :], my_ref[pl.ds(288, 192), :]]), wide([l_ref[1, x * wy] for x in range(wx)]))
    where = [(x, y) for y in range(1, wy - 1) for x in range(wx)]
    blocks, left_out = known_hexes(wx, wy, where, l_ref, kp_ref, s_ref, f_ref, c_ref)
    corners = corner_batch(blocks, left_out, g_ref[...])
    lone = slot_corners([blocks[wx * y + wx - 1][1] for y in range(wy - 2)], parts_ref, 1)
    for y in range(wy - 2):
        v1_ref[y, 0:8] = lone[y][8:16]
        v1_ref[y, 8:16] = lone[y][24:32]
        for i, rows in enumerate(line_sums(corners[wx * y : wx * y + wx])):
            v_ref[y, i] = rows


def after_y(wx, wy, xs, visc_ref, l_ref, kp_ref, parts_ref, my_ref, own_ref, v3_ref, down_ref, up_ref):
    z = l_ref.shape[3]
    misc_d = tail_misc(down_ref, wx)
    misc_u = tail_misc(up_ref, wx)
    row = lambda i, col: kp_ref[i, pl.ds(col, 1), :]
    delta = dot(my_ref[...], wide([down_ref[pl.ds(48 * x, 48), :] for x in xs]))
    arrived = [up_ref[pl.ds(48 * x, 48), :].astype(F32) for x in xs]
    arrived_corners = slot_corners(arrived, parts_ref, 3)
    results = []
    for n, x in enumerate(xs):
        here = x * wy + wy - 1
        last = x == wx - 1
        part = delta[:, z * n : z * n + z]
        visc = row(4, here)
        scales = [
            visc * row(0, here), visc if last else visc * row(0, here + wy), visc * row(1, here),
            visc * misc_d[x : x + 1], visc * row(2, here), visc * row(3, here),
        ]
        flux = [part[48 * s : 48 * s + 48] * scales[s] for s in range(6)]
        used = [None if (s == 1 and last) else scales[s] for s in range(6)]
        top = scaled_corners(part[288:480], used) + v3_ref[x] * misc_d[x : x + 1]
        top_one = part[320:352] * visc
        here = x * wy
        visc = level_visc(misc_u[x : x + 1], visc_ref)
        flag = row(1, here)
        own = own_ref[:, pl.ds(z * x, z)]
        keep_z = misc_u[2 * wx + x : 2 * wx + x + 1]
        scales = [
            visc * misc_u[wx + x : wx + x + 1], None if last else visc * misc_u[wx + x + 1 : wx + x + 2],
            None, visc * flag, visc * keep_z, visc * z_next(keep_z),
        ]
        low = scaled_corners(own[48:240], scales) + arrived_corners[n] * flag
        low_one = own[80:112] * visc
        face = (arrived[n] + visc * (own[0:48] + penalty * l_ref[1, here].astype(F32))) * flag
        results.append((flux, top, top_one, low, low_one, face))
    return results


def turn_kernel(
    wx, wy, visc_ref, l_ref, kp_ref, diag_ref, parts_ref, my_ref, own_ref, c1_ref, c2_ref, va_ref, vb_ref,
    v1a_ref, v1b_ref, v3_ref, yd_ref, yu_ref,
    c3_ref, vt_ref, vl_ref, v1_ref, face_ref, down_ref, up_ref,
):
    z = l_ref.shape[3]
    xs = (0, wx - 1)
    results = after_y(wx, wy, xs, visc_ref, l_ref, kp_ref, parts_ref, my_ref, own_ref, v3_ref, yd_ref, yu_ref)
    row = lambda i, col: kp_ref[i, pl.ds(col, 1), :]
    tail = 48 * wx + 48
    rim_d = yd_ref[pl.ds(tail, yd_ref.shape[0] - tail), :].astype(F32)
    rim_u = yu_ref[pl.ds(tail, yu_ref.shape[0] - tail), :].astype(F32)
    ones = 8 * (wx + 1)
    base = ones + 16
    for n, (flux, top, top_one, low, low_one, face) in enumerate(results):
        for s in range(6):
            c3_ref[n, s] = flux[s]
        face_ref[n] = face
        for p in range(2):
            vt_ref[n, p] = settle(top, p)
            vl_ref[n, p] = settle(low, p)
    flux, top, top_one, low, low_one, face = results[1]
    mine = rim_u[ones : ones + 16] + tall([low_one[8:16], low_one[24:32]])
    v1_ref[0] = mine
    v1_ref[1] = v1a_ref[0]
    for y in range(wy - 2):
        v1_ref[2 + y] = v1b_ref[y]
    v1_ref[wy] = v1a_ref[1] + tall([top_one[8:16], top_one[24:32]])
    v1_ref[wy + 1] = rim_d[ones : ones + 16]

    def plane(i, n, p):
        lines = [rim_u[8 * i : 8 * i + 8] + vl_ref[n, p], va_ref[0, i]]
        lines += [vb_ref[y, i] for y in range(wy - 2)]
        lines += [va_ref[1, i] + vt_ref[n, p], rim_d[8 * i : 8 * i + 8]]
        return merge(lines[1::2], lines[0::2])

    down_ref[pl.ds(0, 48), :] = yu_ref[pl.ds(48 * wx, 48), :]
    for y in range(wy):
        down_ref[pl.ds(48 + 48 * y, 48), :] = l_ref[0, y]
    down_ref[pl.ds(48 * (wy + 1), 48), :] = yd_ref[pl.ds(48 * wx, 48), :]
    diag = [jnp.broadcast_to(diag_ref[pl.ds(y, 1), :], (4, z)) for y in range(wy)]
    high = [part.astype(BF).astype(F32) for part in diag]
    low_bits = [a - b for a, b in zip(diag, high)]
    high += [jnp.broadcast_to(rim_d[4:5], (4, z)), jnp.zeros((4, z), F32)]
    low_bits += [jnp.broadcast_to(rim_d[5:6], (4, z)), jnp.zeros((4, z), F32)]
    rim = [plane(0, 0, 0)] + high + low_bits
    rim += [rim_u[base + wx : base + wx + 1], kp_ref[0, 0:wy], rim_d[base + wx : base + wx + 1]]
    put_tail(down_ref, 48 * (wy + 2), rim)
    corner = (wx - 1) * wy
    up_ref[pl.ds(0, 48), :] = c1_ref[1, wx - 1].astype(BF)
    for y in range(1, wy - 1):
        up_ref[pl.ds(48 * y, 48), :] = c2_ref[1, wx * (y - 1) + wx - 1].astype(BF)
    up_ref[pl.ds(48 * (wy - 1), 48), :] = (c1_ref[1, 2 * wx - 1] + flux[1]).astype(BF)
    last = pl.ds(corner, wy)
    rim = [plane(wx, 1, 1), mine, rim_d[ones : ones + 16]]
    rim += [rim_u[base + wx - 1 : base + wx], kp_ref[5, last], rim_d[base + wx + 1 : base + wx + 2]]
    rim += [rim_u[base + 3 * wx - 1 : base + 3 * wx], kp_ref[2, last], rim_d[base + wx + 3 : base + wx + 4]]
    rim += [kp_ref[1, last], rim_d[base + wx - 1 : base + wx]]
    put_tail(up_ref, 48 * wy, rim)


def assemble_kernel(
    wx, wy, visc_ref, l_ref, kp_ref, diag_ref, parts_ref, mx_ref, my_ref, own_ref, c1_ref, c2_ref, c3_ref,
    va_ref, vb_ref, v3_ref, vt_ref, vl_ref, face_ref, yd_ref, yu_ref,
    r_ref, v_ref, inv_ref, ownx_ref, mid,
):
    z = l_ref.shape[3]
    cells = wx * wy
    xs = tuple(range(1, wx - 1))
    results = after_y(wx, wy, xs, visc_ref, l_ref, kp_ref, parts_ref, my_ref, own_ref, v3_ref, yd_ref, yu_ref)
    for n, part in enumerate(results):
        for s in range(6):
            mid[n, s] = part[0][s]
    traces = [yu_ref[pl.ds(48 * wx, 48), :]] + [l_ref[0, y] for y in range(wy)] + [yd_ref[pl.ds(48 * wx, 48), :]]
    ownx_ref[...] = dot(tall([mx_ref[pl.ds(48, 48), :], mx_ref[pl.ds(288, 192), :]]), wide(traces))

    def contrib(slot, x, y):
        if 0 < y < wy - 1:
            return c2_ref[slot, wx * (y - 1) + x]
        if y == 0:
            return c1_ref[slot, x]
        extra = mid[x - 1, slot] if 0 < x < wx - 1 else c3_ref[0 if x == 0 else 1, slot]
        return c1_ref[slot, wx + x] + extra

    for x in range(wx):
        for y in range(wy):
            col = pl.ds(x * wy + y, 48, stride=cells)
            if x:
                r_ref[0, col, :] = contrib(0, x, y) + contrib(1, x - 1, y)
            else:
                r_ref[0, col, :] = contrib(0, x, y)
            if y:
                behind = contrib(3, x, y - 1)
            elif 0 < x < wx - 1:
                behind = results[x - 1][5]
            else:
                behind = face_ref[0 if x == 0 else 1]
            r_ref[1, col, :] = contrib(2, x, y) + behind
            r_ref[2, col, :] = contrib(4, x, y) + z_prev(contrib(5, x, y))
    tail = 48 * wx + 48
    rim_d = yd_ref[pl.ds(tail, yd_ref.shape[0] - tail), :].astype(F32)
    rim_u = yu_ref[pl.ds(tail, yu_ref.shape[0] - tail), :].astype(F32)

    def brought(which, i):
        held = vt_ref if which == 1 else vl_ref
        terms = []
        for x, p in ((i, 0), (i - 1, 1)):
            if x in (0, wx - 1):
                terms.append(held[0 if x == 0 else 1, p])
            elif 0 < x < wx - 1:
                terms.append(settle(results[x - 1][which], p))
        return sum(terms[1:], terms[0])

    for i in range(wx + 1):
        lines = [rim_u[8 * i : 8 * i + 8] + brought(3, i), va_ref[0, i]]
        lines += [vb_ref[y, i] for y in range(wy - 2)]
        lines += [va_ref[1, i] + brought(1, i), rim_d[8 * i : 8 * i + 8]]
        v_ref[i] = merge(lines[1::2], lines[0::2])
        if i < wx:
            parts = [jnp.broadcast_to(diag_ref[pl.ds(i * wy + y, 1), :], (4, z)) for y in range(wy)]
            edge = rim_d[8 * i + 4 : 8 * i + 5] + rim_d[8 * i + 5 : 8 * i + 6]
            parts += [jnp.broadcast_to(edge, (4, z)), jnp.zeros((4, z), F32)]
            inv_ref[i] = reciprocal(tall(parts))


def reciprocal(diag):
    present = diag > 0.0
    return jnp.where(present, (1.0 / (gain * gain)) / jnp.where(present, diag, 1.0), 0.0)


def final_kernel(
    wx, wy, visc_ref, l_ref, kp_ref, parts_ref, mx_ref, ownx_ref, r_ref, v_ref, inv_ref, v1_ref,
    yd_ref, yu_ref, xd_ref, xu_ref, p_ref, out_ref, fix,
):
    cells, z = wx * wy, l_ref.shape[3]
    rows = v_ref.shape[1]
    planes = (wx + 1) * rows
    row = lambda i, col: kp_ref[i, pl.ds(col, 1), :]
    delta = dot(mx_ref[...], wide([xd_ref[pl.ds(48 * j, 48), :] for j in range(wy + 2)]))
    rim_x = xd_ref[pl.ds(48 * (wy + 2), xd_ref.shape[0] - 48 * (wy + 2)), :].astype(F32)
    rim_l = xu_ref[pl.ds(48 * wy, xu_ref.shape[0] - 48 * wy), :].astype(F32)
    misc_d = tail_misc(yd_ref, wx)
    misc_u = tail_misc(yu_ref, wx)
    flags_high = rim_x[3 * rows : 3 * rows + wy + 2]
    corner = (wx - 1) * wy
    arrived = [xu_ref[pl.ds(48 * y, 48), :].astype(F32) for y in range(wy)]
    arrived_corners = slot_corners(arrived, parts_ref, 1)
    codes = rim_l[rows + 32 : rows + 32 + wy + 2]
    keep_z = rim_l[rows + 32 + wy + 2 : rows + 32 + 2 * (wy + 2)]
    keep_y = rim_l[rows + 32 + 2 * (wy + 2) : rows + 32 + 3 * (wy + 2) - 1]
    low_visc = level_visc(codes, visc_ref)
    low_keep_z = z_next(keep_z)
    lines = [[], [], []]
    high_flux = []
    for j in range(-1, wy + 1):
        n = j + 1
        part = delta[:, z * n : z * n + z]
        flag = flags_high[n : n + 1]
        if j < 0:
            visc = level_visc(misc_u[wx - 1 : wx], visc_ref)
            kz = misc_u[3 * wx - 1 : 3 * wx]
            keeps = [misc_u[2 * wx - 1 : 2 * wx], flag, None, row(1, corner), kz, z_next(kz)]
        elif j < wy:
            here = corner + j
            visc = row(4, here)
            high_y = row(1, here + 1) if j < wy - 1 else misc_d[wx - 1 : wx]
            keeps = [row(0, here), flag, row(1, here), high_y, row(2, here), row(3, here)]
        else:
            visc = level_visc(misc_d[wx + 1 : wx + 2], visc_ref)
            kz = misc_d[wx + 3 : wx + 4]
            keeps = [misc_d[wx + 2 : wx + 3], flag, misc_d[wx - 1 : wx], None, kz, z_next(kz)]
        scales = [None if keep is None else visc * keep for keep in keeps]
        corners = scaled_corners(part[288:480], scales)
        one = v1_ref[n] * flag
        lines[0].append(settle(corners, 0))
        lines[1].append(settle(corners, 1) + one[0:8] + z_prev(one[8:16]))
        high_flux.append([None if k is None else part[48 * s : 48 * s + 48] * k for s, k in enumerate(scales)])
        own = ownx_ref[:, pl.ds(z * n, z)]
        visc = low_visc[n : n + 1]
        flag = misc_u[wx : wx + 1] if j < 0 else misc_d[wx : wx + 1] if j == wy else row(0, j)
        scales = [
            None, visc * flag, None if j < 0 else visc * keep_y[j : j + 1],
            None if j == wy else visc * keep_y[j + 1 : j + 2], visc * keep_z[n : n + 1], visc * low_keep_z[n : n + 1],
        ]
        corners = settle(scaled_corners(own[48:240], scales), 1)
        if 0 <= j < wy:
            lines[2].append(corners + settle(arrived_corners[j] * flag, 1))
            face = (arrived[j] + visc * (own[0:48] + penalty * l_ref[0, j].astype(F32))) * flag
            r_ref[0, pl.ds(j, 48, stride=cells), :] += face
        else:
            at = rows + (0 if j < 0 else 16)
            one = rim_l[at : at + 16] * flag
            lines[2].append(corners + one[0:8] + z_prev(one[8:16]))
    low, before, first = [merge(part[1::2], part[0::2]) for part in lines]
    top = v_ref[wx] + before + rim_x[0:rows]
    values = [(v_ref[0] + first + rim_l[0:rows]) * inv_ref[0]]
    values += [v_ref[i] * inv_ref[i] for i in range(1, wx - 1)]
    values += [(v_ref[wx - 1] + low) * inv_ref[wx - 1]]
    values += [top * reciprocal(rim_x[rows : 2 * rows] + rim_x[2 * rows : 3 * rows])]
    value = tall(values)
    fix[...] = jnp.zeros_like(fix)
    fix[pl.ds(0, planes), :] = value
    fix[pl.ds(planes, planes), :] = z_next(value)
    rhs = fix[...].astype(BF)
    for j in range(wy):
        col = pl.ds(corner + j, 48, stride=cells)
        flux = high_flux[j + 1]
        r_ref[0, col, :] += flux[0]
        r_ref[1, col, :] += flux[2] + high_flux[j][3]
        r_ref[2, col, :] += flux[4] + z_prev(flux[5])
    for d in range(3):
        spread = dot(p_ref[pl.ds(48 * cells * d, 48 * cells), :], rhs)
        spread = spread.reshape(48, cells, z) * kp_ref[d][None]
        out_ref[d] = (r_ref[d] + spread.reshape(48 * cells, z)).astype(BF)


def call(body, args, outs, scratch, flops, hbm=False):
    if hbm:
        args = tuple(pltpu.with_memory_space_constraint(a, pltpu.HBM) for a in args)
    return pl.pallas_call(
        body,
        in_specs=[pl.BlockSpec(memory_space=pltpu.HBM if hbm else pltpu.VMEM)] * len(args),
        out_shape=outs,
        scratch_shapes=scratch,
        cost_estimate=pl.CostEstimate(flops=flops, bytes_accessed=1000000, transcendentals=0),
        compiler_params=pltpu.CompilerParams(vmem_limit_bytes=16 * 1024 * 1024),
    )(*args)


def local(traces, dirichlet, visc_class, viscosity, coarse_diag, solve_map, flux_map):
    wx, wy, z = traces.shape[2:]
    cells = wx * wy
    rows = 8 * (wy // 2 + 1)
    per_hex = 4 * 288 * 256 * z
    gather = jnp.asarray(gather_table())
    parts = jnp.asarray(slot_table())
    spread = jnp.asarray(spread_table(wx, wy, rows))
    vm = pltpu.VMEM
    bind = lambda body: functools.partial(body, wx, wy)
    base = 48 * wx + 48

    (lifted, flags, visc, diag, s_map, s_turned, f_map, gather, parts, c1, va, v1a, v3, down, up) = call(
        bind(first_kernel),
        (
            viscosity, traces.reshape(3, 48 * cells, z), dirichlet.reshape(3, cells, z),
            visc_class.reshape(cells, z), coarse_diag.reshape(cells, z), solve_map.T, flux_map, gather, parts,
        ),
        (
            vm((4, cells, 48, z), BF), vm((6, cells, z), F32), vm((viscosity.shape[0], z), F32), vm((cells, z), F32),
            vm(solve_map.shape, BF),
            vm(solve_map.shape[::-1], BF), vm(flux_map.shape, BF), vm(gather.shape, BF), vm(parts.shape, BF),
            vm((6, 2 * wx, 48, z), F32), vm((2, wx + 1, 8, z), F32), vm((2, 16, z), F32), vm((wx, 32, z), F32),
            vm((base + tail_rows(8 * (wx + 1) + 16 + wx + 4), z), BF),
            vm((base + tail_rows(8 * (wx + 1) + 16 + 3 * wx), z), BF),
        ),
        [
            vm((3, 48 * cells, z), BF), vm((3, cells, z), jnp.int32), vm((cells, z), jnp.int32),
            vm((48 * cells, z), F32), pltpu.SMEM(viscosity.shape, F32), pltpu.SemaphoreType.DMA((9,)),
        ],
        2 * wx * per_hex, True,
    )
    yd = from_behind(down, "gy", -1)
    yu = from_behind(up, "gy", 1)
    inner = wx * (wy - 2)
    c2, vb, v1b, mx, my, own = call(
        bind(middle_kernel),
        (lifted, flags, s_map, s_turned, f_map, gather, parts),
        (
            vm((6, inner, 48, z), F32), vm((wy - 2, wx + 1, 8, z), F32), vm((wy - 2, 16, z), F32),
            vm((480, 48), BF), vm((480, 48), BF), vm((240, wx * z), F32),
        ),
        [], inner * per_hex,
    )
    c3, vt, vl, v1, face, down, up = call(
        bind(turn_kernel),
        (
            visc, lifted, flags, diag, parts, my, own, c1, c2, va, vb, v1a, v1b, v3, yd, yu,
        ),
        (
            vm((2, 6, 48, z), F32), vm((2, 2, 8, z), F32), vm((2, 2, 8, z), F32), vm((wy + 2, 16, z), F32),
            vm((2, 48, z), F32), vm((48 * (wy + 2) + tail_rows(3 * rows + wy + 2), z), BF),
            vm((48 * wy + tail_rows(rows + 32 + 3 * (wy + 2) - 1), z), BF),
        ),
        [], 2 * per_hex,
    )
    xd = from_behind(down, "gx", -1)
    xu = from_behind(up, "gx", 1)
    residual, vs, inverse, ownx = call(
        bind(assemble_kernel),
        (
            visc, lifted, flags, diag, parts, mx, my, own, c1, c2, c3, va, vb, v3, vt, vl, face, yd, yu,
        ),
        (
            vm((3, 48 * cells, z), F32), vm((wx + 1, rows, z), F32), vm((wx, rows, z), F32),
            vm((240, (wy + 2) * z), F32),
        ),
        [vm((wx - 2, 6, 48, z), F32)], 4 * per_hex,
    )
    out = call(
        bind(final_kernel),
        (
            visc, lifted, flags, parts, mx, ownx, residual, vs, inverse, v1, yd, yu, xd, xu, spread,
        ),
        jax.ShapeDtypeStruct((3, 48 * cells, z), BF),
        [vm((spread.shape[1], z), F32)], 2 * spread.size * z,
    )
    return out.reshape(traces.shape)


def solution(mesh):
    in_specs = (
        P(None, None, "gx", "gy", None),
        P(None, "gx", "gy", None),
        P("gx", "gy", None),
        P(),
        P("gx", "gy", None),
        P(),
        P(),
    )
    out_specs = P(None, None, "gx", "gy", None)
    return jax.shard_map(local, mesh=mesh, in_specs=in_specs, out_specs=out_specs, check_vma=False)
```

```python
import functools
import math

import jax
import jax.numpy as jnp
import ml_dtypes
import numpy as np
from jax import lax
from jax.experimental import pallas as pl
from jax.experimental.pallas import tpu as pltpu
from jax.sharding import PartitionSpec as P

penalty = 0.5
BF = jnp.bfloat16
F32 = jnp.float32
lift = 1.3264
gain = 1.3280711361297461


def swap(value, axis, first):
    count = lax.axis_size(axis)
    pairs = [(low, low + 1) for low in range(first, count - 1, 2)]
    return lax.ppermute(value, axis, pairs + [(high, low) for low, high in pairs])


def even(axis):
    return lax.rem(lax.axis_index(axis), 2) == 0


def choose(condition, yes_ref, no_ref, out_ref):
    out_ref[...] = jnp.where(condition, yes_ref[...], no_ref[...])


def corner_table():
    gll_points = [-1.0, -math.sqrt(0.2), math.sqrt(0.2), 1.0]
    table = np.zeros((16, 4), np.float64)
    for s in range(4):
        for t in range(4):
            for p in range(2):
                for q in range(2):
                    table[4 * s + t, 2 * p + q] = (
                        (1 + (2 * p - 1) * gll_points[s]) * (1 + (2 * q - 1) * gll_points[t]) / 4
                    )
    return table


def landing(face_slot, high_s, high_t):
    direction, outward = divmod(face_slot, 2)
    if direction == 0:
        return (outward, high_s, high_t)
    if direction == 1:
        return (high_s, outward, high_t)
    return (high_s, high_t, outward)


def gather_table():
    weights = lift * corner_table()
    table = np.zeros((32, 288), np.float64)
    for slot in range(6):
        for s in range(2):
            for t in range(2):
                p, q, r = landing(slot, s, t)
                for c in range(3):
                    cols = slot * 48 + 16 * c + np.arange(16)
                    table[16 * r + 8 * p + 4 * q + c, cols] += weights[:, 2 * s + t]
    return table.astype(ml_dtypes.bfloat16)


def slot_table():
    return np.concatenate(np.split(gather_table(), 6, axis=1), axis=0)


def spread_table(wx, wy, rows):
    weights = lift * corner_table()
    planes = (wx + 1) * rows
    depth = -(-2 * planes // 128) * 128
    table = np.zeros((3, 48, wx, wy, depth), np.float64)
    for d in range(3):
        for x in range(wx):
            for y in range(wy):
                for s in range(2):
                    for t in range(2):
                        p, q, r = landing(2 * d, s, t)
                        for c in range(3):
                            k = r * planes + (x + p) * rows + 4 * (y + q) + c
                            table[d, 16 * c : 16 * c + 16, x, y, k] += weights[:, 2 * s + t]
    return table.reshape(-1, depth).astype(ml_dtypes.bfloat16)


def lanes(shape):
    return lax.broadcasted_iota(jnp.int32, shape, len(shape) - 1)


def z_next(value):
    last = value.shape[-1] - 1
    return jnp.where(lanes(value.shape) < last, pltpu.roll(value, last, value.ndim - 1), 0.0)


def z_prev(value):
    return jnp.where(lanes(value.shape) > 0, pltpu.roll(value, 1, value.ndim - 1), 0.0)


def dot(left, right):
    return jnp.dot(left, right, preferred_element_type=F32)


def wide(parts):
    return jnp.concatenate(parts, axis=1)


def tall(parts):
    return jnp.concatenate(parts, axis=0)


def hex_batch(slots, scales, s_map, f_map):
    z = slots[0][0].shape[1]
    element = tall([wide([hexa[s] for hexa in slots]) for s in range(6)])
    interior = dot(s_map, element).astype(BF)
    flux = dot(f_map, interior) + penalty * element.astype(F32)
    return [
        [flux[48 * s : 48 * s + 48, z * h : z * h + z] * scales[h][s] for s in range(6)]
        for h in range(len(slots))
    ]


def corner_batch(blocks, left_out, gather):
    z = blocks[0][0].shape[1]
    nothing = jnp.zeros((48, z), BF)
    right = tall(
        [
            wide([nothing if s in left_out[h] else blocks[h][s].astype(BF) for h in range(len(blocks))])
            for s in range(6)
        ]
    )
    return [dot(gather, right)[:, z * h : z * h + z] for h in range(len(blocks))]


def slot_corners(traces, parts_ref, slot):
    z = traces[0].shape[1]
    rows = dot(parts_ref[pl.ds(32 * slot, 32), :], wide([trace.astype(BF) for trace in traces]))
    return [rows[:, z * h : z * h + z] for h in range(len(traces))]


def settle(rows, p):
    return rows[8 * p : 8 * p + 8] + z_prev(rows[16 + 8 * p : 24 + 8 * p])


def scaled_corners(delta, scales):
    terms = [delta[32 * s : 32 * s + 32] * scales[s] for s in range(6) if scales[s] is not None]
    return sum(terms[1:], terms[0])


def level_visc(code, visc_ref):
    visc = jnp.zeros(code.shape, F32)
    for level in range(visc_ref.shape[0]):
        visc = visc + jnp.where(code == F32(level + 1), visc_ref[pl.ds(level, 1), :], F32(0.0))
    return visc


def merge(even, odd):
    odd = tall(odd)
    return tall(even) + pltpu.roll(odd, odd.shape[0] - 4, 0)


def first_kernel(
    wx, wy, visc_hbm, t_hbm, dir_hbm, cls_hbm, diag_hbm, st_hbm, f_hbm, g_hbm, parts_hbm,
    l_ref, kp_ref, visc_ref, diag_ref, s_ref, st_ref, f_ref, g_ref, parts_ref, c_ref, v_ref, v1_ref, v3_ref,
    inner_ref, outer_ref, down_ref, up_ref, t_ref, dir_ref, cls_ref, nat, levels, sems,
):
    cells = wx * wy
    pairs = [
        (t_hbm, t_ref), (dir_hbm, dir_ref), (cls_hbm, cls_ref), (diag_hbm, diag_ref),
        (st_hbm, st_ref), (f_hbm, f_ref), (g_hbm, g_ref), (parts_hbm, parts_ref),
        (visc_hbm, levels),
    ]
    copies = [pltpu.make_async_copy(a, b, sems.at[i]) for i, (a, b) in enumerate(pairs)]
    for copy in copies:
        copy.start()
    copies[4].wait()
    s_ref[...] = st_ref[...].T
    for i in (8, 1, 2, 3, 0):
        copies[i].wait()
    z = t_ref.shape[2]
    for level in range(visc_ref.shape[0]):
        visc_ref[pl.ds(level, 1), :] = jnp.full((1, z), levels[level], F32)
    code = cls_ref[...].astype(F32) + 1.0
    kp_ref[4] = level_visc(code, visc_ref)
    kp_ref[5] = code
    for d in range(3):
        keep = (1 - dir_ref[d]).astype(F32)
        kp_ref[d] = keep
        masked = t_ref[d].astype(F32).reshape(48, cells, z) * keep[None]
        nat[...] = masked.reshape(48 * cells, z)
        for col in range(cells):
            part = nat[pl.ds(col, 48, stride=cells), :]
            l_ref[d, col] = part.astype(BF)
            if d == 2:
                l_ref[3, col] = z_next(part).astype(BF)
    kp_ref[3] = z_next(kp_ref[2])
    for i in (5, 6, 7):
        copies[i].wait()
    row = lambda i, col: kp_ref[i, pl.ds(col, 1), :]
    where = [(x, 0) for x in range(wx)] + [(x, wy - 1) for x in range(wx)]
    blocks, left_out = known_hexes(wx, wy, where, l_ref, kp_ref, s_ref, f_ref, c_ref)
    corners = corner_batch(blocks, left_out, g_ref[...])
    lone = slot_corners([blocks[wx - 1][1], blocks[2 * wx - 1][1]], parts_ref, 1)
    for h in range(2):
        v1_ref[h, 0:8] = lone[h][8:16]
        v1_ref[h, 8:16] = lone[h][24:32]
    for x, rows in enumerate(slot_corners([blocks[wx + x][3] for x in range(wx)], parts_ref, 3)):
        v3_ref[x] = rows
    sums = [line_sums(corners[:wx]), line_sums(corners[wx:])]
    for side in range(2):
        for i in range(wx + 1):
            v_ref[side, i] = sums[side][i]
    corner = (wx - 1) * wy
    top = wy - 1
    for x in range(wx):
        down_ref[pl.ds(48 * x, 48), :] = l_ref[1, x * wy]
        up_ref[pl.ds(48 * x, 48), :] = blocks[wx + x][3].astype(BF)
    down_ref[pl.ds(48 * wx, 48), :] = l_ref[0, 0]
    up_ref[pl.ds(48 * wx, 48), :] = l_ref[0, top]
    place = lax.broadcasted_iota(jnp.int32, (8, z), 0)
    rim = []
    for i in range(wx):
        diag = diag_ref[pl.ds(i * wy, 1), :]
        high = diag.astype(BF).astype(F32)
        rim.append(jnp.where(place == 4, high, jnp.where(place == 5, diag - high, sums[0][i])))
    rim += [sums[0][wx], v1_ref[0]]
    rim += [row(1, x * wy) for x in range(wx)] + [row(0, 0), row(5, corner), row(0, corner), row(2, corner)]
    put_tail(down_ref, 48 * wx + 48, rim)
    rim = [sums[1][i] for i in range(wx + 1)] + [v1_ref[1]]
    for kind in (5, 0, 2):
        rim += [row(kind, x * wy + top) for x in range(wx)]
    put_tail(up_ref, 48 * wx + 48, rim)
    choose(even("gy"), up_ref, down_ref, inner_ref)
    choose(even("gy"), down_ref, up_ref, outer_ref)


def tail_rows(count):
    return -(-count // 16) * 16


def put_tail(ref, start, rows):
    count = sum(part.shape[0] for part in rows)
    full = ref.shape[0] - start
    if full > count:
        rows = rows + [jnp.zeros((full - count, rows[0].shape[1]), F32)]
    ref[pl.ds(start, full), :] = tall(rows).astype(BF)


def tail_misc(ref, wx):
    start = 48 * wx + 48
    return ref[pl.ds(start, ref.shape[0] - start), :].astype(F32)[8 * (wx + 1) + 16 :]


def line_sums(corners):
    width = len(corners)
    low = [settle(rows, 0) for rows in corners]
    high = [settle(rows, 1) for rows in corners]
    return [low[0]] + [low[x] + high[x - 1] for x in range(1, width)] + [high[-1]]


def known_hexes(wx, wy, where, l_ref, kp_ref, s_ref, f_ref, c_ref):
    z = l_ref.shape[3]
    nothing = jnp.zeros((48, z), BF)
    row = lambda i, col: kp_ref[i, pl.ds(col, 1), :]
    slots, scales, left_out = [], [], []
    for x, y in where:
        here = x * wy + y
        visc = row(4, here)
        last_x, last_y = x == wx - 1, y == wy - 1
        slots.append(
            [
                l_ref[0, here], nothing if last_x else l_ref[0, here + wy],
                l_ref[1, here], nothing if last_y else l_ref[1, here + 1],
                l_ref[2, here], l_ref[3, here],
            ]
        )
        scales.append(
            [
                visc * row(0, here), visc if last_x else visc * row(0, here + wy),
                visc * row(1, here), visc if last_y else visc * row(1, here + 1),
                visc * row(2, here), visc * row(3, here),
            ]
        )
        left_out.append(([1] if last_x else []) + ([3] if last_y else []))
    blocks = hex_batch(slots, scales, s_ref[...], f_ref[...])
    for h in range(len(where)):
        for s in range(6):
            c_ref[s, h] = blocks[h][s]
    return blocks, left_out


def middle_kernel(
    wx, wy, l_ref, kp_ref, s_ref, st_ref, f_ref, g_ref, parts_ref,
    c_ref, v_ref, v1_ref, mx_ref, my_ref, own_ref,
):
    z = l_ref.shape[3]
    for slot, ref in ((1, mx_ref), (3, my_ref)):
        flux = lax.dot_general(
            f_ref[...], st_ref[pl.ds(48 * slot, 48), :], (((1,), (1,)), ((), ())),
            preferred_element_type=F32,
        )
        ref[pl.ds(0, 288), :] = flux.astype(BF)
        eye = lax.broadcasted_iota(jnp.int32, (48, 48), 0) == lax.broadcasted_iota(jnp.int32, (48, 48), 1)
        for s in range(6):
            block = flux[48 * s : 48 * s + 48]
            if s == slot:
                block = block + jnp.where(eye, F32(penalty), F32(0.0))
            ref[pl.ds(288 + 32 * s, 32), :] = dot(parts_ref[pl.ds(32 * s, 32), :], block.astype(BF)).astype(BF)
    own_ref[...] = dot(tall([my_ref[pl.ds(144, 48), :], my_ref[pl.ds(288, 192), :]]), wide([l_ref[1, x * wy] for x in range(wx)]))
    where = [(x, y) for y in range(1, wy - 1) for x in range(wx)]
    blocks, left_out = known_hexes(wx, wy, where, l_ref, kp_ref, s_ref, f_ref, c_ref)
    corners = corner_batch(blocks, left_out, g_ref[...])
    lone = slot_corners([blocks[wx * y + wx - 1][1] for y in range(wy - 2)], parts_ref, 1)
    for y in range(wy - 2):
        v1_ref[y, 0:8] = lone[y][8:16]
        v1_ref[y, 8:16] = lone[y][24:32]
        for i, rows in enumerate(line_sums(corners[wx * y : wx * y + wx])):
            v_ref[y, i] = rows


def after_y(wx, wy, xs, visc_ref, l_ref, kp_ref, parts_ref, my_ref, own_ref, v3_ref, down_ref, up_ref):
    z = l_ref.shape[3]
    misc_d = tail_misc(down_ref, wx)
    misc_u = tail_misc(up_ref, wx)
    row = lambda i, col: kp_ref[i, pl.ds(col, 1), :]
    delta = dot(my_ref[...], wide([down_ref[pl.ds(48 * x, 48), :] for x in xs]))
    arrived = [up_ref[pl.ds(48 * x, 48), :].astype(F32) for x in xs]
    arrived_corners = slot_corners(arrived, parts_ref, 3)
    results = []
    for n, x in enumerate(xs):
        here = x * wy + wy - 1
        last = x == wx - 1
        part = delta[:, z * n : z * n + z]
        visc = row(4, here)
        scales = [
            visc * row(0, here), visc if last else visc * row(0, here + wy), visc * row(1, here),
            visc * misc_d[x : x + 1], visc * row(2, here), visc * row(3, here),
        ]
        flux = [part[48 * s : 48 * s + 48] * scales[s] for s in range(6)]
        used = [None if (s == 1 and last) else scales[s] for s in range(6)]
        top = scaled_corners(part[288:480], used) + v3_ref[x] * misc_d[x : x + 1]
        top_one = part[320:352] * visc
        here = x * wy
        visc = level_visc(misc_u[x : x + 1], visc_ref)
        flag = row(1, here)
        own = own_ref[:, pl.ds(z * x, z)]
        keep_z = misc_u[2 * wx + x : 2 * wx + x + 1]
        scales = [
            visc * misc_u[wx + x : wx + x + 1], None if last else visc * misc_u[wx + x + 1 : wx + x + 2],
            None, visc * flag, visc * keep_z, visc * z_next(keep_z),
        ]
        low = scaled_corners(own[48:240], scales) + arrived_corners[n] * flag
        low_one = own[80:112] * visc
        face = (arrived[n] + visc * (own[0:48] + penalty * l_ref[1, here].astype(F32))) * flag
        results.append((flux, top, top_one, low, low_one, face))
    return results


def turn_kernel(
    wx, wy, visc_ref, l_ref, kp_ref, diag_ref, parts_ref, my_ref, own_ref, c1_ref, c2_ref, va_ref, vb_ref,
    v1a_ref, v1b_ref, v3_ref, inner_in, outer_in,
    c3_ref, vt_ref, vl_ref, v1_ref, face_ref, yd_ref, yu_ref, inner_ref, outer_ref, down_ref, up_ref,
):
    z = l_ref.shape[3]
    choose(even("gy"), inner_in, outer_in, yd_ref)
    choose(even("gy"), outer_in, inner_in, yu_ref)
    xs = (0, wx - 1)
    results = after_y(wx, wy, xs, visc_ref, l_ref, kp_ref, parts_ref, my_ref, own_ref, v3_ref, yd_ref, yu_ref)
    row = lambda i, col: kp_ref[i, pl.ds(col, 1), :]
    tail = 48 * wx + 48
    rim_d = yd_ref[pl.ds(tail, yd_ref.shape[0] - tail), :].astype(F32)
    rim_u = yu_ref[pl.ds(tail, yu_ref.shape[0] - tail), :].astype(F32)
    ones = 8 * (wx + 1)
    base = ones + 16
    for n, (flux, top, top_one, low, low_one, face) in enumerate(results):
        for s in range(6):
            c3_ref[n, s] = flux[s]
        face_ref[n] = face
        for p in range(2):
            vt_ref[n, p] = settle(top, p)
            vl_ref[n, p] = settle(low, p)
    flux, top, top_one, low, low_one, face = results[1]
    mine = rim_u[ones : ones + 16] + tall([low_one[8:16], low_one[24:32]])
    v1_ref[0] = mine
    v1_ref[1] = v1a_ref[0]
    for y in range(wy - 2):
        v1_ref[2 + y] = v1b_ref[y]
    v1_ref[wy] = v1a_ref[1] + tall([top_one[8:16], top_one[24:32]])
    v1_ref[wy + 1] = rim_d[ones : ones + 16]

    def plane(i, n, p):
        lines = [rim_u[8 * i : 8 * i + 8] + vl_ref[n, p], va_ref[0, i]]
        lines += [vb_ref[y, i] for y in range(wy - 2)]
        lines += [va_ref[1, i] + vt_ref[n, p], rim_d[8 * i : 8 * i + 8]]
        return merge(lines[1::2], lines[0::2])

    down_ref[pl.ds(0, 48), :] = yu_ref[pl.ds(48 * wx, 48), :]
    for y in range(wy):
        down_ref[pl.ds(48 + 48 * y, 48), :] = l_ref[0, y]
    down_ref[pl.ds(48 * (wy + 1), 48), :] = yd_ref[pl.ds(48 * wx, 48), :]
    diag = [jnp.broadcast_to(diag_ref[pl.ds(y, 1), :], (4, z)) for y in range(wy)]
    high = [part.astype(BF).astype(F32) for part in diag]
    low_bits = [a - b for a, b in zip(diag, high)]
    high += [jnp.broadcast_to(rim_d[4:5], (4, z)), jnp.zeros((4, z), F32)]
    low_bits += [jnp.broadcast_to(rim_d[5:6], (4, z)), jnp.zeros((4, z), F32)]
    rim = [plane(0, 0, 0)] + high + low_bits
    rim += [rim_u[base + wx : base + wx + 1], kp_ref[0, 0:wy], rim_d[base + wx : base + wx + 1]]
    put_tail(down_ref, 48 * (wy + 2), rim)
    corner = (wx - 1) * wy
    up_ref[pl.ds(0, 48), :] = c1_ref[1, wx - 1].astype(BF)
    for y in range(1, wy - 1):
        up_ref[pl.ds(48 * y, 48), :] = c2_ref[1, wx * (y - 1) + wx - 1].astype(BF)
    up_ref[pl.ds(48 * (wy - 1), 48), :] = (c1_ref[1, 2 * wx - 1] + flux[1]).astype(BF)
    last = pl.ds(corner, wy)
    rim = [plane(wx, 1, 1), mine, rim_d[ones : ones + 16]]
    rim += [rim_u[base + wx - 1 : base + wx], kp_ref[5, last], rim_d[base + wx + 1 : base + wx + 2]]
    rim += [rim_u[base + 3 * wx - 1 : base + 3 * wx], kp_ref[2, last], rim_d[base + wx + 3 : base + wx + 4]]
    rim += [kp_ref[1, last], rim_d[base + wx - 1 : base + wx]]
    put_tail(up_ref, 48 * wy, rim)
    choose(even("gx"), up_ref, down_ref, inner_ref)
    choose(even("gx"), down_ref, up_ref, outer_ref)


def assemble_kernel(
    wx, wy, visc_ref, l_ref, kp_ref, diag_ref, parts_ref, mx_ref, my_ref, own_ref, c1_ref, c2_ref, c3_ref,
    va_ref, vb_ref, v3_ref, vt_ref, vl_ref, face_ref, yd_ref, yu_ref,
    r_ref, v_ref, inv_ref, ownx_ref, mid,
):
    z = l_ref.shape[3]
    cells = wx * wy
    xs = tuple(range(1, wx - 1))
    results = after_y(wx, wy, xs, visc_ref, l_ref, kp_ref, parts_ref, my_ref, own_ref, v3_ref, yd_ref, yu_ref)
    for n, part in enumerate(results):
        for s in range(6):
            mid[n, s] = part[0][s]
    traces = [yu_ref[pl.ds(48 * wx, 48), :]] + [l_ref[0, y] for y in range(wy)] + [yd_ref[pl.ds(48 * wx, 48), :]]
    ownx_ref[...] = dot(tall([mx_ref[pl.ds(48, 48), :], mx_ref[pl.ds(288, 192), :]]), wide(traces))

    def contrib(slot, x, y):
        if 0 < y < wy - 1:
            return c2_ref[slot, wx * (y - 1) + x]
        if y == 0:
            return c1_ref[slot, x]
        extra = mid[x - 1, slot] if 0 < x < wx - 1 else c3_ref[0 if x == 0 else 1, slot]
        return c1_ref[slot, wx + x] + extra

    for x in range(wx):
        for y in range(wy):
            col = pl.ds(x * wy + y, 48, stride=cells)
            if x:
                r_ref[0, col, :] = contrib(0, x, y) + contrib(1, x - 1, y)
            else:
                r_ref[0, col, :] = contrib(0, x, y)
            if y:
                behind = contrib(3, x, y - 1)
            elif 0 < x < wx - 1:
                behind = results[x - 1][5]
            else:
                behind = face_ref[0 if x == 0 else 1]
            r_ref[1, col, :] = contrib(2, x, y) + behind
            r_ref[2, col, :] = contrib(4, x, y) + z_prev(contrib(5, x, y))
    tail = 48 * wx + 48
    rim_d = yd_ref[pl.ds(tail, yd_ref.shape[0] - tail), :].astype(F32)
    rim_u = yu_ref[pl.ds(tail, yu_ref.shape[0] - tail), :].astype(F32)

    def brought(which, i):
        held = vt_ref if which == 1 else vl_ref
        terms = []
        for x, p in ((i, 0), (i - 1, 1)):
            if x in (0, wx - 1):
                terms.append(held[0 if x == 0 else 1, p])
            elif 0 < x < wx - 1:
                terms.append(settle(results[x - 1][which], p))
        return sum(terms[1:], terms[0])

    for i in range(wx + 1):
        lines = [rim_u[8 * i : 8 * i + 8] + brought(3, i), va_ref[0, i]]
        lines += [vb_ref[y, i] for y in range(wy - 2)]
        lines += [va_ref[1, i] + brought(1, i), rim_d[8 * i : 8 * i + 8]]
        v_ref[i] = merge(lines[1::2], lines[0::2])
        if i < wx:
            parts = [jnp.broadcast_to(diag_ref[pl.ds(i * wy + y, 1), :], (4, z)) for y in range(wy)]
            edge = rim_d[8 * i + 4 : 8 * i + 5] + rim_d[8 * i + 5 : 8 * i + 6]
            parts += [jnp.broadcast_to(edge, (4, z)), jnp.zeros((4, z), F32)]
            inv_ref[i] = reciprocal(tall(parts))


def reciprocal(diag):
    present = diag > 0.0
    return jnp.where(present, (1.0 / (gain * gain)) / jnp.where(present, diag, 1.0), 0.0)


def final_kernel(
    wx, wy, visc_ref, l_ref, kp_ref, parts_ref, mx_ref, ownx_ref, r_ref, v_ref, inv_ref, v1_ref,
    yd_ref, yu_ref, inner_in, outer_in, p_ref, out_ref, fix, xd_ref, xu_ref,
):
    choose(even("gx"), inner_in, outer_in, xd_ref)
    choose(even("gx"), outer_in, inner_in, xu_ref)
    cells, z = wx * wy, l_ref.shape[3]
    rows = v_ref.shape[1]
    planes = (wx + 1) * rows
    row = lambda i, col: kp_ref[i, pl.ds(col, 1), :]
    delta = dot(mx_ref[...], wide([xd_ref[pl.ds(48 * j, 48), :] for j in range(wy + 2)]))
    rim_x = xd_ref[pl.ds(48 * (wy + 2), xd_ref.shape[0] - 48 * (wy + 2)), :].astype(F32)
    rim_l = xu_ref[pl.ds(48 * wy, xu_ref.shape[0] - 48 * wy), :].astype(F32)
    misc_d = tail_misc(yd_ref, wx)
    misc_u = tail_misc(yu_ref, wx)
    flags_high = rim_x[3 * rows : 3 * rows + wy + 2]
    corner = (wx - 1) * wy
    arrived = [xu_ref[pl.ds(48 * y, 48), :].astype(F32) for y in range(wy)]
    arrived_corners = slot_corners(arrived, parts_ref, 1)
    codes = rim_l[rows + 32 : rows + 32 + wy + 2]
    keep_z = rim_l[rows + 32 + wy + 2 : rows + 32 + 2 * (wy + 2)]
    keep_y = rim_l[rows + 32 + 2 * (wy + 2) : rows + 32 + 3 * (wy + 2) - 1]
    low_visc = level_visc(codes, visc_ref)
    low_keep_z = z_next(keep_z)
    lines = [[], [], []]
    high_flux = []
    for j in range(-1, wy + 1):
        n = j + 1
        part = delta[:, z * n : z * n + z]
        flag = flags_high[n : n + 1]
        if j < 0:
            visc = level_visc(misc_u[wx - 1 : wx], visc_ref)
            kz = misc_u[3 * wx - 1 : 3 * wx]
            keeps = [misc_u[2 * wx - 1 : 2 * wx], flag, None, row(1, corner), kz, z_next(kz)]
        elif j < wy:
            here = corner + j
            visc = row(4, here)
            high_y = row(1, here + 1) if j < wy - 1 else misc_d[wx - 1 : wx]
            keeps = [row(0, here), flag, row(1, here), high_y, row(2, here), row(3, here)]
        else:
            visc = level_visc(misc_d[wx + 1 : wx + 2], visc_ref)
            kz = misc_d[wx + 3 : wx + 4]
            keeps = [misc_d[wx + 2 : wx + 3], flag, misc_d[wx - 1 : wx], None, kz, z_next(kz)]
        scales = [None if keep is None else visc * keep for keep in keeps]
        corners = scaled_corners(part[288:480], scales)
        one = v1_ref[n] * flag
        lines[0].append(settle(corners, 0))
        lines[1].append(settle(corners, 1) + one[0:8] + z_prev(one[8:16]))
        high_flux.append([None if k is None else part[48 * s : 48 * s + 48] * k for s, k in enumerate(scales)])
        own = ownx_ref[:, pl.ds(z * n, z)]
        visc = low_visc[n : n + 1]
        flag = misc_u[wx : wx + 1] if j < 0 else misc_d[wx : wx + 1] if j == wy else row(0, j)
        scales = [
            None, visc * flag, None if j < 0 else visc * keep_y[j : j + 1],
            None if j == wy else visc * keep_y[j + 1 : j + 2], visc * keep_z[n : n + 1], visc * low_keep_z[n : n + 1],
        ]
        corners = settle(scaled_corners(own[48:240], scales), 1)
        if 0 <= j < wy:
            lines[2].append(corners + settle(arrived_corners[j] * flag, 1))
            face = (arrived[j] + visc * (own[0:48] + penalty * l_ref[0, j].astype(F32))) * flag
            r_ref[0, pl.ds(j, 48, stride=cells), :] += face
        else:
            at = rows + (0 if j < 0 else 16)
            one = rim_l[at : at + 16] * flag
            lines[2].append(corners + one[0:8] + z_prev(one[8:16]))
    low, before, first = [merge(part[1::2], part[0::2]) for part in lines]
    top = v_ref[wx] + before + rim_x[0:rows]
    values = [(v_ref[0] + first + rim_l[0:rows]) * inv_ref[0]]
    values += [v_ref[i] * inv_ref[i] for i in range(1, wx - 1)]
    values += [(v_ref[wx - 1] + low) * inv_ref[wx - 1]]
    values += [top * reciprocal(rim_x[rows : 2 * rows] + rim_x[2 * rows : 3 * rows])]
    value = tall(values)
    fix[...] = jnp.zeros_like(fix)
    fix[pl.ds(0, planes), :] = value
    fix[pl.ds(planes, planes), :] = z_next(value)
    rhs = fix[...].astype(BF)
    for j in range(wy):
        col = pl.ds(corner + j, 48, stride=cells)
        flux = high_flux[j + 1]
        r_ref[0, col, :] += flux[0]
        r_ref[1, col, :] += flux[2] + high_flux[j][3]
        r_ref[2, col, :] += flux[4] + z_prev(flux[5])
    for d in range(3):
        spread = dot(p_ref[pl.ds(48 * cells * d, 48 * cells), :], rhs)
        spread = spread.reshape(48, cells, z) * kp_ref[d][None]
        out_ref[d] = (r_ref[d] + spread.reshape(48 * cells, z)).astype(BF)


def call(body, args, outs, scratch, flops, hbm=False):
    if hbm:
        args = tuple(pltpu.with_memory_space_constraint(a, pltpu.HBM) for a in args)
    return pl.pallas_call(
        body,
        in_specs=[pl.BlockSpec(memory_space=pltpu.HBM if hbm else pltpu.VMEM)] * len(args),
        out_shape=outs,
        scratch_shapes=scratch,
        cost_estimate=pl.CostEstimate(flops=flops, bytes_accessed=1000000, transcendentals=0),
        compiler_params=pltpu.CompilerParams(vmem_limit_bytes=16 * 1024 * 1024),
    )(*args)


def local(traces, dirichlet, visc_class, viscosity, coarse_diag, solve_map, flux_map):
    wx, wy, z = traces.shape[2:]
    cells = wx * wy
    rows = 8 * (wy // 2 + 1)
    per_hex = 4 * 288 * 256 * z
    gather = jnp.asarray(gather_table())
    parts = jnp.asarray(slot_table())
    spread = jnp.asarray(spread_table(wx, wy, rows))
    vm = pltpu.VMEM
    bind = lambda body: functools.partial(body, wx, wy)
    y_message = vm((48 * wx + 48 + tail_rows(8 * (wx + 1) + 16 + 3 * wx), z), BF)
    x_message = vm((48 * (wy + 2) + tail_rows(3 * rows + wy + 2), z), BF)

    (lifted, flags, visc, diag, s_map, s_turned, f_map, gather, parts, c1, va, v1a, v3, inner, outer) = call(
        bind(first_kernel),
        (
            viscosity, traces.reshape(3, 48 * cells, z), dirichlet.reshape(3, cells, z),
            visc_class.reshape(cells, z), coarse_diag.reshape(cells, z), solve_map.T, flux_map, gather, parts,
        ),
        (
            vm((4, cells, 48, z), BF), vm((6, cells, z), F32), vm((viscosity.shape[0], z), F32), vm((cells, z), F32),
            vm(solve_map.shape, BF),
            vm(solve_map.shape[::-1], BF), vm(flux_map.shape, BF), vm(gather.shape, BF), vm(parts.shape, BF),
            vm((6, 2 * wx, 48, z), F32), vm((2, wx + 1, 8, z), F32), vm((2, 16, z), F32), vm((wx, 32, z), F32),
            y_message, y_message,
        ),
        [
            y_message, y_message,
            vm((3, 48 * cells, z), BF), vm((3, cells, z), jnp.int32), vm((cells, z), jnp.int32),
            vm((48 * cells, z), F32), pltpu.SMEM(viscosity.shape, F32), pltpu.SemaphoreType.DMA((9,)),
        ],
        2 * wx * per_hex, True,
    )
    outer = swap(outer, "gy", 1)
    inner = swap(inner, "gy", 0)
    between = wx * (wy - 2)
    c2, vb, v1b, mx, my, own = call(
        bind(middle_kernel),
        (lifted, flags, s_map, s_turned, f_map, gather, parts),
        (
            vm((6, between, 48, z), F32), vm((wy - 2, wx + 1, 8, z), F32), vm((wy - 2, 16, z), F32),
            vm((480, 48), BF), vm((480, 48), BF), vm((240, wx * z), F32),
        ),
        [], between * per_hex,
    )
    c3, vt, vl, v1, face, yd, yu, inner, outer = call(
        bind(turn_kernel),
        (
            visc, lifted, flags, diag, parts, my, own, c1, c2, va, vb, v1a, v1b, v3, inner, outer,
        ),
        (
            vm((2, 6, 48, z), F32), vm((2, 2, 8, z), F32), vm((2, 2, 8, z), F32), vm((wy + 2, 16, z), F32),
            vm((2, 48, z), F32), y_message, y_message, x_message, x_message,
        ),
        [x_message, x_message], 2 * per_hex,
    )
    outer = swap(outer, "gx", 1)
    inner = swap(inner, "gx", 0)
    residual, vs, inverse, ownx = call(
        bind(assemble_kernel),
        (
            visc, lifted, flags, diag, parts, mx, my, own, c1, c2, c3, va, vb, v3, vt, vl, face, yd, yu,
        ),
        (
            vm((3, 48 * cells, z), F32), vm((wx + 1, rows, z), F32), vm((wx, rows, z), F32),
            vm((240, (wy + 2) * z), F32),
        ),
        [vm((wx - 2, 6, 48, z), F32)], 4 * per_hex,
    )
    out = call(
        bind(final_kernel),
        (
            visc, lifted, flags, parts, mx, ownx, residual, vs, inverse, v1, yd, yu, inner, outer, spread,
        ),
        jax.ShapeDtypeStruct((3, 48 * cells, z), BF),
        [vm((spread.shape[1], z), F32), x_message, x_message], 2 * spread.size * z,
    )
    return out.reshape(traces.shape)


def solution(mesh):
    in_specs = (
        P(None, None, "gx", "gy", None),
        P(None, "gx", "gy", None),
        P("gx", "gy", None),
        P(),
        P("gx", "gy", None),
        P(),
        P(),
    )
    out_specs = P(None, None, "gx", "gy", None)
    return jax.shard_map(local, mesh=mesh, in_specs=in_specs, out_specs=out_specs, check_vma=False)
```

```python
import functools
import math

import jax
import jax.numpy as jnp
import ml_dtypes
import numpy as np
from jax import lax
from jax.experimental import pallas as pl
from jax.experimental.pallas import tpu as pltpu
from jax.sharding import PartitionSpec as P

penalty = 0.5
BF = jnp.bfloat16
F32 = jnp.float32
lift = 1.3264
gain = 1.3280711361297461


def swap(value, axis, first):
    count = lax.axis_size(axis)
    pairs = [(low, low + 1) for low in range(first, count - 1, 2)]
    return lax.ppermute(value, axis, pairs + [(high, low) for low, high in pairs])


def even(axis):
    return lax.rem(lax.axis_index(axis), 2) == 0


def choose(condition, yes_ref, no_ref, out_ref):
    size = min(yes_ref.shape[0], no_ref.shape[0], out_ref.shape[0])
    rows = pl.ds(0, size)
    out_ref[rows, :] = jnp.where(condition, yes_ref[rows, :], no_ref[rows, :])
    if out_ref.shape[0] > size:
        rest = pl.ds(size, out_ref.shape[0] - size)
        out_ref[rest, :] = jnp.zeros((out_ref.shape[0] - size, out_ref.shape[1]), out_ref.dtype)


def corner_table():
    gll_points = [-1.0, -math.sqrt(0.2), math.sqrt(0.2), 1.0]
    table = np.zeros((16, 4), np.float64)
    for s in range(4):
        for t in range(4):
            for p in range(2):
                for q in range(2):
                    table[4 * s + t, 2 * p + q] = (
                        (1 + (2 * p - 1) * gll_points[s]) * (1 + (2 * q - 1) * gll_points[t]) / 4
                    )
    return table


def landing(face_slot, high_s, high_t):
    direction, outward = divmod(face_slot, 2)
    if direction == 0:
        return (outward, high_s, high_t)
    if direction == 1:
        return (high_s, outward, high_t)
    return (high_s, high_t, outward)


def gather_table():
    weights = lift * corner_table()
    table = np.zeros((32, 288), np.float64)
    for slot in range(6):
        for s in range(2):
            for t in range(2):
                p, q, r = landing(slot, s, t)
                for c in range(3):
                    cols = slot * 48 + 16 * c + np.arange(16)
                    table[16 * r + 8 * p + 4 * q + c, cols] += weights[:, 2 * s + t]
    return table.astype(ml_dtypes.bfloat16)


def slot_table():
    return np.concatenate(np.split(gather_table(), 6, axis=1), axis=0)


def spread_table(wx, wy, rows):
    weights = lift * corner_table()
    planes = (wx + 1) * rows
    depth = -(-2 * planes // 128) * 128
    table = np.zeros((3, 48, wx, wy, depth), np.float64)
    for d in range(3):
        for x in range(wx):
            for y in range(wy):
                for s in range(2):
                    for t in range(2):
                        p, q, r = landing(2 * d, s, t)
                        for c in range(3):
                            k = r * planes + (x + p) * rows + 4 * (y + q) + c
                            table[d, 16 * c : 16 * c + 16, x, y, k] += weights[:, 2 * s + t]
    return table.reshape(-1, depth).astype(ml_dtypes.bfloat16)


def lanes(shape):
    return lax.broadcasted_iota(jnp.int32, shape, len(shape) - 1)


def z_next(value):
    last = value.shape[-1] - 1
    return jnp.where(lanes(value.shape) < last, pltpu.roll(value, last, value.ndim - 1), 0.0)


def z_prev(value):
    return jnp.where(lanes(value.shape) > 0, pltpu.roll(value, 1, value.ndim - 1), 0.0)


def dot(left, right):
    return jnp.dot(left, right, preferred_element_type=F32)


def wide(parts):
    return jnp.concatenate(parts, axis=1)


def tall(parts):
    return jnp.concatenate(parts, axis=0)


def hex_batch(slots, scales, s_map, f_map):
    z = slots[0][0].shape[1]
    element = tall([wide([hexa[s] for hexa in slots]) for s in range(6)])
    interior = dot(s_map, element).astype(BF)
    flux = dot(f_map, interior) + penalty * element.astype(F32)
    return [
        [flux[48 * s : 48 * s + 48, z * h : z * h + z] * scales[h][s] for s in range(6)]
        for h in range(len(slots))
    ]


def corner_batch(blocks, left_out, gather):
    z = blocks[0][0].shape[1]
    nothing = jnp.zeros((48, z), BF)
    right = tall(
        [
            wide([nothing if s in left_out[h] else blocks[h][s].astype(BF) for h in range(len(blocks))])
            for s in range(6)
        ]
    )
    return [dot(gather, right)[:, z * h : z * h + z] for h in range(len(blocks))]


def slot_corners(traces, parts_ref, slot):
    z = traces[0].shape[1]
    rows = dot(parts_ref[pl.ds(32 * slot, 32), :], wide([trace.astype(BF) for trace in traces]))
    return [rows[:, z * h : z * h + z] for h in range(len(traces))]


def settle(rows, p):
    return rows[8 * p : 8 * p + 8] + z_prev(rows[16 + 8 * p : 24 + 8 * p])


def scaled_corners(delta, scales):
    terms = [delta[32 * s : 32 * s + 32] * scales[s] for s in range(6) if scales[s] is not None]
    return sum(terms[1:], terms[0])


def level_visc(code, visc_ref):
    visc = jnp.zeros(code.shape, F32)
    for level in range(visc_ref.shape[0]):
        visc = visc + jnp.where(code == F32(level + 1), visc_ref[pl.ds(level, 1), :], F32(0.0))
    return visc


def merge(even, odd):
    odd = tall(odd)
    return tall(even) + pltpu.roll(odd, odd.shape[0] - 4, 0)


def first_kernel(
    wx, wy, visc_hbm, t_hbm, dir_hbm, cls_hbm, diag_hbm, st_hbm, f_hbm, g_hbm, parts_hbm,
    l_ref, kp_ref, visc_ref, diag_ref, s_ref, st_ref, f_ref, g_ref, parts_ref, c_ref, v_ref, v1_ref, v3_ref,
    inner_ref, outer_ref, down_ref, up_ref, t_ref, dir_ref, cls_ref, nat, levels, sems,
):
    cells = wx * wy
    pairs = [
        (t_hbm, t_ref), (dir_hbm, dir_ref), (cls_hbm, cls_ref), (diag_hbm, diag_ref),
        (st_hbm, st_ref), (f_hbm, f_ref), (g_hbm, g_ref), (parts_hbm, parts_ref),
        (visc_hbm, levels),
    ]
    copies = [pltpu.make_async_copy(a, b, sems.at[i]) for i, (a, b) in enumerate(pairs)]
    for copy in copies:
        copy.start()
    copies[4].wait()
    s_ref[...] = st_ref[...].T
    for i in (8, 1, 2, 3, 0):
        copies[i].wait()
    z = t_ref.shape[2]
    for level in range(visc_ref.shape[0]):
        visc_ref[pl.ds(level, 1), :] = jnp.full((1, z), levels[level], F32)
    code = cls_ref[...].astype(F32) + 1.0
    kp_ref[4] = level_visc(code, visc_ref)
    kp_ref[5] = code
    for d in range(3):
        keep = (1 - dir_ref[d]).astype(F32)
        kp_ref[d] = keep
        masked = t_ref[d].astype(F32).reshape(48, cells, z) * keep[None]
        nat[...] = masked.reshape(48 * cells, z)
        for col in range(cells):
            part = nat[pl.ds(col, 48, stride=cells), :]
            l_ref[d, col] = part.astype(BF)
            if d == 2:
                l_ref[3, col] = z_next(part).astype(BF)
    kp_ref[3] = z_next(kp_ref[2])
    for i in (5, 6, 7):
        copies[i].wait()
    row = lambda i, col: kp_ref[i, pl.ds(col, 1), :]
    where = [(x, 0) for x in range(wx)] + [(x, wy - 1) for x in range(wx)]
    blocks, left_out = known_hexes(wx, wy, where, l_ref, kp_ref, s_ref, f_ref, c_ref)
    corners = corner_batch(blocks, left_out, g_ref[...])
    lone = slot_corners([blocks[wx - 1][1], blocks[2 * wx - 1][1]], parts_ref, 1)
    for h in range(2):
        v1_ref[h, 0:8] = lone[h][8:16]
        v1_ref[h, 8:16] = lone[h][24:32]
    for x, rows in enumerate(slot_corners([blocks[wx + x][3] for x in range(wx)], parts_ref, 3)):
        v3_ref[x] = rows
    sums = [line_sums(corners[:wx]), line_sums(corners[wx:])]
    for side in range(2):
        for i in range(wx + 1):
            v_ref[side, i] = sums[side][i]
    corner = (wx - 1) * wy
    top = wy - 1
    for x in range(wx):
        down_ref[pl.ds(48 * x, 48), :] = l_ref[1, x * wy]
        up_ref[pl.ds(48 * x, 48), :] = blocks[wx + x][3].astype(BF)
    down_ref[pl.ds(48 * wx, 48), :] = l_ref[0, 0]
    up_ref[pl.ds(48 * wx, 48), :] = l_ref[0, top]
    place = lax.broadcasted_iota(jnp.int32, (8, z), 0)
    rim = []
    for i in range(wx):
        diag = diag_ref[pl.ds(i * wy, 1), :]
        high = diag.astype(BF).astype(F32)
        rim.append(jnp.where(place == 4, high, jnp.where(place == 5, diag - high, sums[0][i])))
    rim += [sums[0][wx], v1_ref[0]]
    rim += [row(1, x * wy) for x in range(wx)] + [row(0, 0), row(5, corner), row(0, corner), row(2, corner)]
    put_tail(down_ref, 48 * wx + 48, rim)
    rim = [sums[1][i] for i in range(wx + 1)] + [v1_ref[1]]
    for kind in (5, 0, 2):
        rim += [row(kind, x * wy + top) for x in range(wx)]
    put_tail(up_ref, 48 * wx + 48, rim)
    choose(even("gy"), up_ref, down_ref, inner_ref)
    choose(even("gy"), down_ref, up_ref, outer_ref)


def tail_rows(count):
    return -(-count // 16) * 16


def put_tail(ref, start, rows):
    count = sum(part.shape[0] for part in rows)
    full = ref.shape[0] - start
    if full > count:
        rows = rows + [jnp.zeros((full - count, rows[0].shape[1]), F32)]
    ref[pl.ds(start, full), :] = tall(rows).astype(BF)


def tail_misc(ref, wx):
    start = 48 * wx + 48
    return ref[pl.ds(start, ref.shape[0] - start), :].astype(F32)[8 * (wx + 1) + 16 :]


def line_sums(corners):
    width = len(corners)
    low = [settle(rows, 0) for rows in corners]
    high = [settle(rows, 1) for rows in corners]
    return [low[0]] + [low[x] + high[x - 1] for x in range(1, width)] + [high[-1]]


def known_hexes(wx, wy, where, l_ref, kp_ref, s_ref, f_ref, c_ref):
    z = l_ref.shape[3]
    nothing = jnp.zeros((48, z), BF)
    row = lambda i, col: kp_ref[i, pl.ds(col, 1), :]
    slots, scales, left_out = [], [], []
    for x, y in where:
        here = x * wy + y
        visc = row(4, here)
        last_x, last_y = x == wx - 1, y == wy - 1
        slots.append(
            [
                l_ref[0, here], nothing if last_x else l_ref[0, here + wy],
                l_ref[1, here], nothing if last_y else l_ref[1, here + 1],
                l_ref[2, here], l_ref[3, here],
            ]
        )
        scales.append(
            [
                visc * row(0, here), visc if last_x else visc * row(0, here + wy),
                visc * row(1, here), visc if last_y else visc * row(1, here + 1),
                visc * row(2, here), visc * row(3, here),
            ]
        )
        left_out.append(([1] if last_x else []) + ([3] if last_y else []))
    blocks = hex_batch(slots, scales, s_ref[...], f_ref[...])
    for h in range(len(where)):
        for s in range(6):
            c_ref[s, h] = blocks[h][s]
    return blocks, left_out


def middle_kernel(
    wx, wy, l_ref, kp_ref, s_ref, st_ref, f_ref, g_ref, parts_ref,
    c_ref, v_ref, v1_ref, mx_ref, my_ref, own_ref,
):
    z = l_ref.shape[3]
    for slot, ref in ((1, mx_ref), (3, my_ref)):
        flux = lax.dot_general(
            f_ref[...], st_ref[pl.ds(48 * slot, 48), :], (((1,), (1,)), ((), ())),
            preferred_element_type=F32,
        )
        ref[pl.ds(0, 288), :] = flux.astype(BF)
        eye = lax.broadcasted_iota(jnp.int32, (48, 48), 0) == lax.broadcasted_iota(jnp.int32, (48, 48), 1)
        for s in range(6):
            block = flux[48 * s : 48 * s + 48]
            if s == slot:
                block = block + jnp.where(eye, F32(penalty), F32(0.0))
            ref[pl.ds(288 + 32 * s, 32), :] = dot(parts_ref[pl.ds(32 * s, 32), :], block.astype(BF)).astype(BF)
    own_ref[...] = dot(tall([my_ref[pl.ds(144, 48), :], my_ref[pl.ds(288, 192), :]]), wide([l_ref[1, x * wy] for x in range(wx)]))
    where = [(x, y) for y in range(1, wy - 1) for x in range(wx)]
    blocks, left_out = known_hexes(wx, wy, where, l_ref, kp_ref, s_ref, f_ref, c_ref)
    corners = corner_batch(blocks, left_out, g_ref[...])
    lone = slot_corners([blocks[wx * y + wx - 1][1] for y in range(wy - 2)], parts_ref, 1)
    for y in range(wy - 2):
        v1_ref[y, 0:8] = lone[y][8:16]
        v1_ref[y, 8:16] = lone[y][24:32]
        for i, rows in enumerate(line_sums(corners[wx * y : wx * y + wx])):
            v_ref[y, i] = rows


def after_y(wx, wy, xs, visc_ref, l_ref, kp_ref, parts_ref, my_ref, own_ref, v3_ref, down_ref, up_ref):
    z = l_ref.shape[3]
    misc_d = tail_misc(down_ref, wx)
    misc_u = tail_misc(up_ref, wx)
    row = lambda i, col: kp_ref[i, pl.ds(col, 1), :]
    delta = dot(my_ref[...], wide([down_ref[pl.ds(48 * x, 48), :] for x in xs]))
    arrived = [up_ref[pl.ds(48 * x, 48), :].astype(F32) for x in xs]
    arrived_corners = slot_corners(arrived, parts_ref, 3)
    results = []
    for n, x in enumerate(xs):
        here = x * wy + wy - 1
        last = x == wx - 1
        part = delta[:, z * n : z * n + z]
        visc = row(4, here)
        scales = [
            visc * row(0, here), visc if last else visc * row(0, here + wy), visc * row(1, here),
            visc * misc_d[x : x + 1], visc * row(2, here), visc * row(3, here),
        ]
        flux = [part[48 * s : 48 * s + 48] * scales[s] for s in range(6)]
        used = [None if (s == 1 and last) else scales[s] for s in range(6)]
        top = scaled_corners(part[288:480], used) + v3_ref[x] * misc_d[x : x + 1]
        top_one = part[320:352] * visc
        here = x * wy
        visc = level_visc(misc_u[x : x + 1], visc_ref)
        flag = row(1, here)
        own = own_ref[:, pl.ds(z * x, z)]
        keep_z = misc_u[2 * wx + x : 2 * wx + x + 1]
        scales = [
            visc * misc_u[wx + x : wx + x + 1], None if last else visc * misc_u[wx + x + 1 : wx + x + 2],
            None, visc * flag, visc * keep_z, visc * z_next(keep_z),
        ]
        low = scaled_corners(own[48:240], scales) + arrived_corners[n] * flag
        low_one = own[80:112] * visc
        face = (arrived[n] + visc * (own[0:48] + penalty * l_ref[1, here].astype(F32))) * flag
        results.append((flux, top, top_one, low, low_one, face))
    return results


def turn_kernel(
    wx, wy, visc_ref, l_ref, kp_ref, diag_ref, parts_ref, my_ref, own_ref, c1_ref, c2_ref, va_ref, vb_ref,
    v1a_ref, v1b_ref, v3_ref, inner_in, outer_in,
    c3_ref, vt_ref, vl_ref, v1_ref, face_ref, yd_ref, yu_ref, inner_ref, outer_ref, down_ref, up_ref,
):
    z = l_ref.shape[3]
    choose(even("gy"), inner_in, outer_in, yd_ref)
    choose(even("gy"), outer_in, inner_in, yu_ref)
    xs = (0, wx - 1)
    results = after_y(wx, wy, xs, visc_ref, l_ref, kp_ref, parts_ref, my_ref, own_ref, v3_ref, yd_ref, yu_ref)
    row = lambda i, col: kp_ref[i, pl.ds(col, 1), :]
    tail = 48 * wx + 48
    rim_d = yd_ref[pl.ds(tail, yd_ref.shape[0] - tail), :].astype(F32)
    rim_u = yu_ref[pl.ds(tail, yu_ref.shape[0] - tail), :].astype(F32)
    ones = 8 * (wx + 1)
    base = ones + 16
    for n, (flux, top, top_one, low, low_one, face) in enumerate(results):
        for s in range(6):
            c3_ref[n, s] = flux[s]
        face_ref[n] = face
        for p in range(2):
            vt_ref[n, p] = settle(top, p)
            vl_ref[n, p] = settle(low, p)
    flux, top, top_one, low, low_one, face = results[1]
    mine = rim_u[ones : ones + 16] + tall([low_one[8:16], low_one[24:32]])
    v1_ref[0] = mine
    v1_ref[1] = v1a_ref[0]
    for y in range(wy - 2):
        v1_ref[2 + y] = v1b_ref[y]
    v1_ref[wy] = v1a_ref[1] + tall([top_one[8:16], top_one[24:32]])
    v1_ref[wy + 1] = rim_d[ones : ones + 16]

    def plane(i, n, p):
        lines = [rim_u[8 * i : 8 * i + 8] + vl_ref[n, p], va_ref[0, i]]
        lines += [vb_ref[y, i] for y in range(wy - 2)]
        lines += [va_ref[1, i] + vt_ref[n, p], rim_d[8 * i : 8 * i + 8]]
        return merge(lines[1::2], lines[0::2])

    down_ref[pl.ds(0, 48), :] = yu_ref[pl.ds(48 * wx, 48), :]
    for y in range(wy):
        down_ref[pl.ds(48 + 48 * y, 48), :] = l_ref[0, y]
    down_ref[pl.ds(48 * (wy + 1), 48), :] = yd_ref[pl.ds(48 * wx, 48), :]
    diag = [jnp.broadcast_to(diag_ref[pl.ds(y, 1), :], (4, z)) for y in range(wy)]
    high = [part.astype(BF).astype(F32) for part in diag]
    low_bits = [a - b for a, b in zip(diag, high)]
    high += [jnp.broadcast_to(rim_d[4:5], (4, z)), jnp.zeros((4, z), F32)]
    low_bits += [jnp.broadcast_to(rim_d[5:6], (4, z)), jnp.zeros((4, z), F32)]
    rim = [plane(0, 0, 0)] + high + low_bits
    rim += [rim_u[base + wx : base + wx + 1], kp_ref[0, 0:wy], rim_d[base + wx : base + wx + 1]]
    put_tail(down_ref, 48 * (wy + 2), rim)
    corner = (wx - 1) * wy
    up_ref[pl.ds(0, 48), :] = c1_ref[1, wx - 1].astype(BF)
    for y in range(1, wy - 1):
        up_ref[pl.ds(48 * y, 48), :] = c2_ref[1, wx * (y - 1) + wx - 1].astype(BF)
    up_ref[pl.ds(48 * (wy - 1), 48), :] = (c1_ref[1, 2 * wx - 1] + flux[1]).astype(BF)
    last = pl.ds(corner, wy)
    rim = [plane(wx, 1, 1), mine, rim_d[ones : ones + 16]]
    rim += [rim_u[base + wx - 1 : base + wx], kp_ref[5, last], rim_d[base + wx + 1 : base + wx + 2]]
    rim += [rim_u[base + 3 * wx - 1 : base + 3 * wx], kp_ref[2, last], rim_d[base + wx + 3 : base + wx + 4]]
    rim += [kp_ref[1, last], rim_d[base + wx - 1 : base + wx]]
    put_tail(up_ref, 48 * wy, rim)
    choose(even("gx"), up_ref, down_ref, inner_ref)
    choose(even("gx"), down_ref, up_ref, outer_ref)


def assemble_kernel(
    wx, wy, visc_ref, l_ref, kp_ref, diag_ref, parts_ref, mx_ref, my_ref, own_ref, c1_ref, c2_ref, c3_ref,
    va_ref, vb_ref, v3_ref, vt_ref, vl_ref, face_ref, yd_ref, yu_ref,
    r_ref, v_ref, inv_ref, ownx_ref, mid,
):
    z = l_ref.shape[3]
    cells = wx * wy
    xs = tuple(range(1, wx - 1))
    results = after_y(wx, wy, xs, visc_ref, l_ref, kp_ref, parts_ref, my_ref, own_ref, v3_ref, yd_ref, yu_ref)
    for n, part in enumerate(results):
        for s in range(6):
            mid[n, s] = part[0][s]
    traces = [yu_ref[pl.ds(48 * wx, 48), :]] + [l_ref[0, y] for y in range(wy)] + [yd_ref[pl.ds(48 * wx, 48), :]]
    ownx_ref[...] = dot(tall([mx_ref[pl.ds(48, 48), :], mx_ref[pl.ds(288, 192), :]]), wide(traces))

    def contrib(slot, x, y):
        if 0 < y < wy - 1:
            return c2_ref[slot, wx * (y - 1) + x]
        if y == 0:
            return c1_ref[slot, x]
        extra = mid[x - 1, slot] if 0 < x < wx - 1 else c3_ref[0 if x == 0 else 1, slot]
        return c1_ref[slot, wx + x] + extra

    for x in range(wx):
        for y in range(wy):
            col = pl.ds(x * wy + y, 48, stride=cells)
            if x:
                r_ref[0, col, :] = contrib(0, x, y) + contrib(1, x - 1, y)
            else:
                r_ref[0, col, :] = contrib(0, x, y)
            if y:
                behind = contrib(3, x, y - 1)
            elif 0 < x < wx - 1:
                behind = results[x - 1][5]
            else:
                behind = face_ref[0 if x == 0 else 1]
            r_ref[1, col, :] = contrib(2, x, y) + behind
            r_ref[2, col, :] = contrib(4, x, y) + z_prev(contrib(5, x, y))
    tail = 48 * wx + 48
    rim_d = yd_ref[pl.ds(tail, yd_ref.shape[0] - tail), :].astype(F32)
    rim_u = yu_ref[pl.ds(tail, yu_ref.shape[0] - tail), :].astype(F32)

    def brought(which, i):
        held = vt_ref if which == 1 else vl_ref
        terms = []
        for x, p in ((i, 0), (i - 1, 1)):
            if x in (0, wx - 1):
                terms.append(held[0 if x == 0 else 1, p])
            elif 0 < x < wx - 1:
                terms.append(settle(results[x - 1][which], p))
        return sum(terms[1:], terms[0])

    for i in range(wx + 1):
        lines = [rim_u[8 * i : 8 * i + 8] + brought(3, i), va_ref[0, i]]
        lines += [vb_ref[y, i] for y in range(wy - 2)]
        lines += [va_ref[1, i] + brought(1, i), rim_d[8 * i : 8 * i + 8]]
        v_ref[i] = merge(lines[1::2], lines[0::2])
        if i < wx:
            parts = [jnp.broadcast_to(diag_ref[pl.ds(i * wy + y, 1), :], (4, z)) for y in range(wy)]
            edge = rim_d[8 * i + 4 : 8 * i + 5] + rim_d[8 * i + 5 : 8 * i + 6]
            parts += [jnp.broadcast_to(edge, (4, z)), jnp.zeros((4, z), F32)]
            inv_ref[i] = reciprocal(tall(parts))


def reciprocal(diag):
    present = diag > 0.0
    return jnp.where(present, (1.0 / (gain * gain)) / jnp.where(present, diag, 1.0), 0.0)


def final_kernel(
    wx, wy, visc_ref, l_ref, kp_ref, parts_ref, mx_ref, ownx_ref, r_ref, v_ref, inv_ref, v1_ref,
    yd_ref, yu_ref, inner_in, outer_in, p_ref, out_ref, fix, xd_ref, xu_ref,
):
    choose(even("gx"), inner_in, outer_in, xd_ref)
    choose(even("gx"), outer_in, inner_in, xu_ref)
    cells, z = wx * wy, l_ref.shape[3]
    rows = v_ref.shape[1]
    planes = (wx + 1) * rows
    row = lambda i, col: kp_ref[i, pl.ds(col, 1), :]
    delta = dot(mx_ref[...], wide([xd_ref[pl.ds(48 * j, 48), :] for j in range(wy + 2)]))
    rim_x = xd_ref[pl.ds(48 * (wy + 2), xd_ref.shape[0] - 48 * (wy + 2)), :].astype(F32)
    rim_l = xu_ref[pl.ds(48 * wy, xu_ref.shape[0] - 48 * wy), :].astype(F32)
    misc_d = tail_misc(yd_ref, wx)
    misc_u = tail_misc(yu_ref, wx)
    flags_high = rim_x[3 * rows : 3 * rows + wy + 2]
    corner = (wx - 1) * wy
    arrived = [xu_ref[pl.ds(48 * y, 48), :].astype(F32) for y in range(wy)]
    arrived_corners = slot_corners(arrived, parts_ref, 1)
    codes = rim_l[rows + 32 : rows + 32 + wy + 2]
    keep_z = rim_l[rows + 32 + wy + 2 : rows + 32 + 2 * (wy + 2)]
    keep_y = rim_l[rows + 32 + 2 * (wy + 2) : rows + 32 + 3 * (wy + 2) - 1]
    low_visc = level_visc(codes, visc_ref)
    low_keep_z = z_next(keep_z)
    lines = [[], [], []]
    high_flux = []
    for j in range(-1, wy + 1):
        n = j + 1
        part = delta[:, z * n : z * n + z]
        flag = flags_high[n : n + 1]
        if j < 0:
            visc = level_visc(misc_u[wx - 1 : wx], visc_ref)
            kz = misc_u[3 * wx - 1 : 3 * wx]
            keeps = [misc_u[2 * wx - 1 : 2 * wx], flag, None, row(1, corner), kz, z_next(kz)]
        elif j < wy:
            here = corner + j
            visc = row(4, here)
            high_y = row(1, here + 1) if j < wy - 1 else misc_d[wx - 1 : wx]
            keeps = [row(0, here), flag, row(1, here), high_y, row(2, here), row(3, here)]
        else:
            visc = level_visc(misc_d[wx + 1 : wx + 2], visc_ref)
            kz = misc_d[wx + 3 : wx + 4]
            keeps = [misc_d[wx + 2 : wx + 3], flag, misc_d[wx - 1 : wx], None, kz, z_next(kz)]
        scales = [None if keep is None else visc * keep for keep in keeps]
        corners = scaled_corners(part[288:480], scales)
        one = v1_ref[n] * flag
        lines[0].append(settle(corners, 0))
        lines[1].append(settle(corners, 1) + one[0:8] + z_prev(one[8:16]))
        high_flux.append([None if k is None else part[48 * s : 48 * s + 48] * k for s, k in enumerate(scales)])
        own = ownx_ref[:, pl.ds(z * n, z)]
        visc = low_visc[n : n + 1]
        flag = misc_u[wx : wx + 1] if j < 0 else misc_d[wx : wx + 1] if j == wy else row(0, j)
        scales = [
            None, visc * flag, None if j < 0 else visc * keep_y[j : j + 1],
            None if j == wy else visc * keep_y[j + 1 : j + 2], visc * keep_z[n : n + 1], visc * low_keep_z[n : n + 1],
        ]
        corners = settle(scaled_corners(own[48:240], scales), 1)
        if 0 <= j < wy:
            lines[2].append(corners + settle(arrived_corners[j] * flag, 1))
            face = (arrived[j] + visc * (own[0:48] + penalty * l_ref[0, j].astype(F32))) * flag
            r_ref[0, pl.ds(j, 48, stride=cells), :] += face
        else:
            at = rows + (0 if j < 0 else 16)
            one = rim_l[at : at + 16] * flag
            lines[2].append(corners + one[0:8] + z_prev(one[8:16]))
    low, before, first = [merge(part[1::2], part[0::2]) for part in lines]
    top = v_ref[wx] + before + rim_x[0:rows]
    values = [(v_ref[0] + first + rim_l[0:rows]) * inv_ref[0]]
    values += [v_ref[i] * inv_ref[i] for i in range(1, wx - 1)]
    values += [(v_ref[wx - 1] + low) * inv_ref[wx - 1]]
    values += [top * reciprocal(rim_x[rows : 2 * rows] + rim_x[2 * rows : 3 * rows])]
    value = tall(values)
    fix[...] = jnp.zeros_like(fix)
    fix[pl.ds(0, planes), :] = value
    fix[pl.ds(planes, planes), :] = z_next(value)
    rhs = fix[...].astype(BF)
    for j in range(wy):
        col = pl.ds(corner + j, 48, stride=cells)
        flux = high_flux[j + 1]
        r_ref[0, col, :] += flux[0]
        r_ref[1, col, :] += flux[2] + high_flux[j][3]
        r_ref[2, col, :] += flux[4] + z_prev(flux[5])
    for d in range(3):
        spread = dot(p_ref[pl.ds(48 * cells * d, 48 * cells), :], rhs)
        spread = spread.reshape(48, cells, z) * kp_ref[d][None]
        out_ref[d] = (r_ref[d] + spread.reshape(48 * cells, z)).astype(BF)


def call(body, args, outs, scratch, flops, hbm=False):
    if hbm:
        args = tuple(pltpu.with_memory_space_constraint(a, pltpu.HBM) for a in args)
    return pl.pallas_call(
        body,
        in_specs=[pl.BlockSpec(memory_space=pltpu.HBM if hbm else pltpu.VMEM)] * len(args),
        out_shape=outs,
        scratch_shapes=scratch,
        cost_estimate=pl.CostEstimate(flops=flops, bytes_accessed=1000000, transcendentals=0),
        compiler_params=pltpu.CompilerParams(vmem_limit_bytes=16 * 1024 * 1024),
    )(*args)


def local(traces, dirichlet, visc_class, viscosity, coarse_diag, solve_map, flux_map):
    wx, wy, z = traces.shape[2:]
    cells = wx * wy
    rows = 8 * (wy // 2 + 1)
    per_hex = 4 * 288 * 256 * z
    gather = jnp.asarray(gather_table())
    parts = jnp.asarray(slot_table())
    spread = jnp.asarray(spread_table(wx, wy, rows))
    vm = pltpu.VMEM
    bind = lambda body: functools.partial(body, wx, wy)
    y_message = vm((48 * wx + 48 + tail_rows(8 * (wx + 1) + 16 + 3 * wx), z), BF)
    y_outer = vm((y_message.shape[0] + 16, z), BF)
    x_message = vm((48 * (wy + 2) + tail_rows(3 * rows + wy + 2), z), BF)
    x_outer = vm((x_message.shape[0] + 16, z), BF)

    (lifted, flags, visc, diag, s_map, s_turned, f_map, gather, parts, c1, va, v1a, v3, inner, outer) = call(
        bind(first_kernel),
        (
            viscosity, traces.reshape(3, 48 * cells, z), dirichlet.reshape(3, cells, z),
            visc_class.reshape(cells, z), coarse_diag.reshape(cells, z), solve_map.T, flux_map, gather, parts,
        ),
        (
            vm((4, cells, 48, z), BF), vm((6, cells, z), F32), vm((viscosity.shape[0], z), F32), vm((cells, z), F32),
            vm(solve_map.shape, BF),
            vm(solve_map.shape[::-1], BF), vm(flux_map.shape, BF), vm(gather.shape, BF), vm(parts.shape, BF),
            vm((6, 2 * wx, 48, z), F32), vm((2, wx + 1, 8, z), F32), vm((2, 16, z), F32), vm((wx, 32, z), F32),
            y_message, y_outer,
        ),
        [
            y_message, y_message,
            vm((3, 48 * cells, z), BF), vm((3, cells, z), jnp.int32), vm((cells, z), jnp.int32),
            vm((48 * cells, z), F32), pltpu.SMEM(viscosity.shape, F32), pltpu.SemaphoreType.DMA((9,)),
        ],
        2 * wx * per_hex, True,
    )
    inner = swap(inner, "gy", 0)
    outer = swap(outer, "gy", 1)
    between = wx * (wy - 2)
    c2, vb, v1b, mx, my, own = call(
        bind(middle_kernel),
        (lifted, flags, s_map, s_turned, f_map, gather, parts),
        (
            vm((6, between, 48, z), F32), vm((wy - 2, wx + 1, 8, z), F32), vm((wy - 2, 16, z), F32),
            vm((480, 48), BF), vm((480, 48), BF), vm((240, wx * z), F32),
        ),
        [], between * per_hex,
    )
    c3, vt, vl, v1, face, yd, yu, inner, outer = call(
        bind(turn_kernel),
        (
            visc, lifted, flags, diag, parts, my, own, c1, c2, va, vb, v1a, v1b, v3, inner, outer,
        ),
        (
            vm((2, 6, 48, z), F32), vm((2, 2, 8, z), F32), vm((2, 2, 8, z), F32), vm((wy + 2, 16, z), F32),
            vm((2, 48, z), F32), y_message, y_message, x_message, x_outer,
        ),
        [x_message, x_message], 2 * per_hex,
    )
    inner = swap(inner, "gx", 0)
    outer = swap(outer, "gx", 1)
    residual, vs, inverse, ownx = call(
        bind(assemble_kernel),
        (
            visc, lifted, flags, diag, parts, mx, my, own, c1, c2, c3, va, vb, v3, vt, vl, face, yd, yu,
        ),
        (
            vm((3, 48 * cells, z), F32), vm((wx + 1, rows, z), F32), vm((wx, rows, z), F32),
            vm((240, (wy + 2) * z), F32),
        ),
        [vm((wx - 2, 6, 48, z), F32)], 4 * per_hex,
    )
    out = call(
        bind(final_kernel),
        (
            visc, lifted, flags, parts, mx, ownx, residual, vs, inverse, v1, yd, yu, inner, outer, spread,
        ),
        jax.ShapeDtypeStruct((3, 48 * cells, z), BF),
        [vm((spread.shape[1], z), F32), x_message, x_message], 2 * spread.size * z,
    )
    return out.reshape(traces.shape)


def solution(mesh):
    in_specs = (
        P(None, None, "gx", "gy", None),
        P(None, "gx", "gy", None),
        P("gx", "gy", None),
        P(),
        P("gx", "gy", None),
        P(),
        P(),
    )
    out_specs = P(None, None, "gx", "gy", None)
    return jax.shard_map(local, mesh=mesh, in_specs=in_specs, out_specs=out_specs, check_vma=False)
```

```python
import functools
import math

import jax
import jax.numpy as jnp
import ml_dtypes
import numpy as np
from jax import lax
from jax.experimental import pallas as pl
from jax.experimental.pallas import tpu as pltpu
from jax.sharding import PartitionSpec as P

penalty = 0.5
BF = jnp.bfloat16
F32 = jnp.float32
lift = 1.3264
gain = 1.3280711361297461


def swap(value, axis, first):
    count = lax.axis_size(axis)
    pairs = [(low, low + 1) for low in range(first, count - 1, 2)]
    moved = [device for pair in pairs for device in pair]
    alone = [(device, device) for device in range(count) if device not in moved]
    return lax.ppermute(value, axis, pairs + [(high, low) for low, high in pairs] + alone)


def even(axis):
    return lax.rem(lax.axis_index(axis), 2) == 0


def arrive(axis, inner_ref, outer_ref, down_ref, up_ref):
    here, last = lax.axis_index(axis), lax.axis_size(axis) - 1
    choose(even(axis), inner_ref, outer_ref, down_ref, here < last)
    choose(even(axis), outer_ref, inner_ref, up_ref, here > 0)


def depart(axis, down_ref, up_ref, inner_ref, outer_ref):
    choose(even(axis), up_ref, down_ref, inner_ref)
    choose(even(axis), down_ref, up_ref, outer_ref)


def choose(condition, yes_ref, no_ref, out_ref, present=None):
    size = min(yes_ref.shape[0], no_ref.shape[0], out_ref.shape[0])
    rows = pl.ds(0, size)
    value = jnp.where(condition, yes_ref[rows, :], no_ref[rows, :])
    out_ref[rows, :] = value if present is None else jnp.where(present, value, jnp.zeros_like(value))
    if out_ref.shape[0] > size:
        rest = pl.ds(size, out_ref.shape[0] - size)
        out_ref[rest, :] = jnp.zeros((out_ref.shape[0] - size, out_ref.shape[1]), out_ref.dtype)


def corner_table():
    gll_points = [-1.0, -math.sqrt(0.2), math.sqrt(0.2), 1.0]
    table = np.zeros((16, 4), np.float64)
    for s in range(4):
        for t in range(4):
            for p in range(2):
                for q in range(2):
                    table[4 * s + t, 2 * p + q] = (
                        (1 + (2 * p - 1) * gll_points[s]) * (1 + (2 * q - 1) * gll_points[t]) / 4
                    )
    return table


def landing(face_slot, high_s, high_t):
    direction, outward = divmod(face_slot, 2)
    if direction == 0:
        return (outward, high_s, high_t)
    if direction == 1:
        return (high_s, outward, high_t)
    return (high_s, high_t, outward)


def gather_table():
    weights = lift * corner_table()
    table = np.zeros((32, 288), np.float64)
    for slot in range(6):
        for s in range(2):
            for t in range(2):
                p, q, r = landing(slot, s, t)
                for c in range(3):
                    cols = slot * 48 + 16 * c + np.arange(16)
                    table[16 * r + 8 * p + 4 * q + c, cols] += weights[:, 2 * s + t]
    return table.astype(ml_dtypes.bfloat16)


def slot_table():
    return np.concatenate(np.split(gather_table(), 6, axis=1), axis=0)


def spread_table(wx, wy, rows):
    weights = lift * corner_table()
    planes = (wx + 1) * rows
    depth = -(-2 * planes // 128) * 128
    table = np.zeros((3, 48, wx, wy, depth), np.float64)
    for d in range(3):
        for x in range(wx):
            for y in range(wy):
                for s in range(2):
                    for t in range(2):
                        p, q, r = landing(2 * d, s, t)
                        for c in range(3):
                            k = r * planes + (x + p) * rows + 4 * (y + q) + c
                            table[d, 16 * c : 16 * c + 16, x, y, k] += weights[:, 2 * s + t]
    return table.reshape(-1, depth).astype(ml_dtypes.bfloat16)


def lanes(shape):
    return lax.broadcasted_iota(jnp.int32, shape, len(shape) - 1)


def z_next(value):
    last = value.shape[-1] - 1
    return jnp.where(lanes(value.shape) < last, pltpu.roll(value, last, value.ndim - 1), 0.0)


def z_prev(value):
    return jnp.where(lanes(value.shape) > 0, pltpu.roll(value, 1, value.ndim - 1), 0.0)


def dot(left, right):
    return jnp.dot(left, right, preferred_element_type=F32)


def wide(parts):
    return jnp.concatenate(parts, axis=1)


def tall(parts):
    return jnp.concatenate(parts, axis=0)


def hex_batch(slots, scales, s_map, f_map):
    z = slots[0][0].shape[1]
    element = tall([wide([hexa[s] for hexa in slots]) for s in range(6)])
    interior = dot(s_map, element).astype(BF)
    flux = dot(f_map, interior) + penalty * element.astype(F32)
    return [
        [flux[48 * s : 48 * s + 48, z * h : z * h + z] * scales[h][s] for s in range(6)]
        for h in range(len(slots))
    ]


def corner_batch(blocks, left_out, gather):
    z = blocks[0][0].shape[1]
    nothing = jnp.zeros((48, z), BF)
    right = tall(
        [
            wide([nothing if s in left_out[h] else blocks[h][s].astype(BF) for h in range(len(blocks))])
            for s in range(6)
        ]
    )
    return [dot(gather, right)[:, z * h : z * h + z] for h in range(len(blocks))]


def slot_corners(traces, parts_ref, slot):
    z = traces[0].shape[1]
    rows = dot(parts_ref[pl.ds(32 * slot, 32), :], wide([trace.astype(BF) for trace in traces]))
    return [rows[:, z * h : z * h + z] for h in range(len(traces))]


def settle(rows, p):
    return rows[8 * p : 8 * p + 8] + z_prev(rows[16 + 8 * p : 24 + 8 * p])


def scaled_corners(delta, scales):
    terms = [delta[32 * s : 32 * s + 32] * scales[s] for s in range(6) if scales[s] is not None]
    return sum(terms[1:], terms[0])


def level_visc(code, visc_ref):
    visc = jnp.zeros(code.shape, F32)
    for level in range(visc_ref.shape[0]):
        visc = visc + jnp.where(code == F32(level + 1), visc_ref[pl.ds(level, 1), :], F32(0.0))
    return visc


def merge(even, odd):
    odd = tall(odd)
    return tall(even) + pltpu.roll(odd, odd.shape[0] - 4, 0)


def first_kernel(
    wx, wy, visc_hbm, t_hbm, dir_hbm, cls_hbm, diag_hbm, st_hbm, f_hbm, g_hbm, parts_hbm,
    l_ref, kp_ref, visc_ref, diag_ref, s_ref, st_ref, f_ref, g_ref, parts_ref, c_ref, v_ref, v1_ref, v3_ref,
    inner_ref, outer_ref, down_ref, up_ref, t_ref, dir_ref, cls_ref, nat, levels, sems,
):
    cells = wx * wy
    pairs = [
        (t_hbm, t_ref), (dir_hbm, dir_ref), (cls_hbm, cls_ref), (diag_hbm, diag_ref),
        (st_hbm, st_ref), (f_hbm, f_ref), (g_hbm, g_ref), (parts_hbm, parts_ref),
        (visc_hbm, levels),
    ]
    copies = [pltpu.make_async_copy(a, b, sems.at[i]) for i, (a, b) in enumerate(pairs)]
    for copy in copies:
        copy.start()
    copies[4].wait()
    s_ref[...] = st_ref[...].T
    for i in (8, 1, 2, 3, 0):
        copies[i].wait()
    z = t_ref.shape[2]
    for level in range(visc_ref.shape[0]):
        visc_ref[pl.ds(level, 1), :] = jnp.full((1, z), levels[level], F32)
    code = cls_ref[...].astype(F32) + 1.0
    kp_ref[4] = level_visc(code, visc_ref)
    kp_ref[5] = code
    for d in range(3):
        keep = (1 - dir_ref[d]).astype(F32)
        kp_ref[d] = keep
        masked = t_ref[d].astype(F32).reshape(48, cells, z) * keep[None]
        nat[...] = masked.reshape(48 * cells, z)
        for col in range(cells):
            part = nat[pl.ds(col, 48, stride=cells), :]
            l_ref[d, col] = part.astype(BF)
            if d == 2:
                l_ref[3, col] = z_next(part).astype(BF)
    kp_ref[3] = z_next(kp_ref[2])
    for i in (5, 6, 7):
        copies[i].wait()
    row = lambda i, col: kp_ref[i, pl.ds(col, 1), :]
    where = [(x, 0) for x in range(wx)] + [(x, wy - 1) for x in range(wx)]
    blocks, left_out = known_hexes(wx, wy, where, l_ref, kp_ref, s_ref, f_ref, c_ref)
    corners = corner_batch(blocks, left_out, g_ref[...])
    lone = slot_corners([blocks[wx - 1][1], blocks[2 * wx - 1][1]], parts_ref, 1)
    for h in range(2):
        v1_ref[h, 0:8] = lone[h][8:16]
        v1_ref[h, 8:16] = lone[h][24:32]
    for x, rows in enumerate(slot_corners([blocks[wx + x][3] for x in range(wx)], parts_ref, 3)):
        v3_ref[x] = rows
    sums = [line_sums(corners[:wx]), line_sums(corners[wx:])]
    for side in range(2):
        for i in range(wx + 1):
            v_ref[side, i] = sums[side][i]
    corner = (wx - 1) * wy
    top = wy - 1
    for x in range(wx):
        down_ref[pl.ds(48 * x, 48), :] = l_ref[1, x * wy]
        up_ref[pl.ds(48 * x, 48), :] = blocks[wx + x][3].astype(BF)
    down_ref[pl.ds(48 * wx, 48), :] = l_ref[0, 0]
    up_ref[pl.ds(48 * wx, 48), :] = l_ref[0, top]
    place = lax.broadcasted_iota(jnp.int32, (8, z), 0)
    rim = []
    for i in range(wx):
        diag = diag_ref[pl.ds(i * wy, 1), :]
        high = diag.astype(BF).astype(F32)
        rim.append(jnp.where(place == 4, high, jnp.where(place == 5, diag - high, sums[0][i])))
    rim += [sums[0][wx], v1_ref[0]]
    rim += [row(1, x * wy) for x in range(wx)] + [row(0, 0), row(5, corner), row(0, corner), row(2, corner)]
    put_tail(down_ref, 48 * wx + 48, rim)
    rim = [sums[1][i] for i in range(wx + 1)] + [v1_ref[1]]
    for kind in (5, 0, 2):
        rim += [row(kind, x * wy + top) for x in range(wx)]
    put_tail(up_ref, 48 * wx + 48, rim)
    depart("gy", down_ref, up_ref, inner_ref, outer_ref)


def tail_rows(count):
    return -(-count // 16) * 16


def put_tail(ref, start, rows):
    count = sum(part.shape[0] for part in rows)
    full = ref.shape[0] - start
    if full > count:
        rows = rows + [jnp.zeros((full - count, rows[0].shape[1]), F32)]
    ref[pl.ds(start, full), :] = tall(rows).astype(BF)


def tail_misc(ref, wx):
    start = 48 * wx + 48
    return ref[pl.ds(start, ref.shape[0] - start), :].astype(F32)[8 * (wx + 1) + 16 :]


def line_sums(corners):
    width = len(corners)
    low = [settle(rows, 0) for rows in corners]
    high = [settle(rows, 1) for rows in corners]
    return [low[0]] + [low[x] + high[x - 1] for x in range(1, width)] + [high[-1]]


def known_hexes(wx, wy, where, l_ref, kp_ref, s_ref, f_ref, c_ref):
    z = l_ref.shape[3]
    nothing = jnp.zeros((48, z), BF)
    row = lambda i, col: kp_ref[i, pl.ds(col, 1), :]
    slots, scales, left_out = [], [], []
    for x, y in where:
        here = x * wy + y
        visc = row(4, here)
        last_x, last_y = x == wx - 1, y == wy - 1
        slots.append(
            [
                l_ref[0, here], nothing if last_x else l_ref[0, here + wy],
                l_ref[1, here], nothing if last_y else l_ref[1, here + 1],
                l_ref[2, here], l_ref[3, here],
            ]
        )
        scales.append(
            [
                visc * row(0, here), visc if last_x else visc * row(0, here + wy),
                visc * row(1, here), visc if last_y else visc * row(1, here + 1),
                visc * row(2, here), visc * row(3, here),
            ]
        )
        left_out.append(([1] if last_x else []) + ([3] if last_y else []))
    blocks = hex_batch(slots, scales, s_ref[...], f_ref[...])
    for h in range(len(where)):
        for s in range(6):
            c_ref[s, h] = blocks[h][s]
    return blocks, left_out


def middle_kernel(
    wx, wy, l_ref, kp_ref, s_ref, st_ref, f_ref, g_ref, parts_ref,
    c_ref, v_ref, v1_ref, mx_ref, my_ref, own_ref,
):
    z = l_ref.shape[3]
    for slot, ref in ((1, mx_ref), (3, my_ref)):
        flux = lax.dot_general(
            f_ref[...], st_ref[pl.ds(48 * slot, 48), :], (((1,), (1,)), ((), ())),
            preferred_element_type=F32,
        )
        ref[pl.ds(0, 288), :] = flux.astype(BF)
        eye = lax.broadcasted_iota(jnp.int32, (48, 48), 0) == lax.broadcasted_iota(jnp.int32, (48, 48), 1)
        for s in range(6):
            block = flux[48 * s : 48 * s + 48]
            if s == slot:
                block = block + jnp.where(eye, F32(penalty), F32(0.0))
            ref[pl.ds(288 + 32 * s, 32), :] = dot(parts_ref[pl.ds(32 * s, 32), :], block.astype(BF)).astype(BF)
    own_ref[...] = dot(tall([my_ref[pl.ds(144, 48), :], my_ref[pl.ds(288, 192), :]]), wide([l_ref[1, x * wy] for x in range(wx)]))
    where = [(x, y) for y in range(1, wy - 1) for x in range(wx)]
    blocks, left_out = known_hexes(wx, wy, where, l_ref, kp_ref, s_ref, f_ref, c_ref)
    corners = corner_batch(blocks, left_out, g_ref[...])
    lone = slot_corners([blocks[wx * y + wx - 1][1] for y in range(wy - 2)], parts_ref, 1)
    for y in range(wy - 2):
        v1_ref[y, 0:8] = lone[y][8:16]
        v1_ref[y, 8:16] = lone[y][24:32]
        for i, rows in enumerate(line_sums(corners[wx * y : wx * y + wx])):
            v_ref[y, i] = rows


def after_y(wx, wy, xs, visc_ref, l_ref, kp_ref, parts_ref, my_ref, own_ref, v3_ref, down_ref, up_ref):
    z = l_ref.shape[3]
    misc_d = tail_misc(down_ref, wx)
    misc_u = tail_misc(up_ref, wx)
    row = lambda i, col: kp_ref[i, pl.ds(col, 1), :]
    delta = dot(my_ref[...], wide([down_ref[pl.ds(48 * x, 48), :] for x in xs]))
    arrived = [up_ref[pl.ds(48 * x, 48), :].astype(F32) for x in xs]
    arrived_corners = slot_corners(arrived, parts_ref, 3)
    results = []
    for n, x in enumerate(xs):
        here = x * wy + wy - 1
        last = x == wx - 1
        part = delta[:, z * n : z * n + z]
        visc = row(4, here)
        scales = [
            visc * row(0, here), visc if last else visc * row(0, here + wy), visc * row(1, here),
            visc * misc_d[x : x + 1], visc * row(2, here), visc * row(3, here),
        ]
        flux = [part[48 * s : 48 * s + 48] * scales[s] for s in range(6)]
        used = [None if (s == 1 and last) else scales[s] for s in range(6)]
        top = scaled_corners(part[288:480], used) + v3_ref[x] * misc_d[x : x + 1]
        top_one = part[320:352] * visc
        here = x * wy
        visc = level_visc(misc_u[x : x + 1], visc_ref)
        flag = row(1, here)
        own = own_ref[:, pl.ds(z * x, z)]
        keep_z = misc_u[2 * wx + x : 2 * wx + x + 1]
        scales = [
            visc * misc_u[wx + x : wx + x + 1], None if last else visc * misc_u[wx + x + 1 : wx + x + 2],
            None, visc * flag, visc * keep_z, visc * z_next(keep_z),
        ]
        low = scaled_corners(own[48:240], scales) + arrived_corners[n] * flag
        low_one = own[80:112] * visc
        face = (arrived[n] + visc * (own[0:48] + penalty * l_ref[1, here].astype(F32))) * flag
        results.append((flux, top, top_one, low, low_one, face))
    return results


def turn_kernel(
    wx, wy, visc_ref, l_ref, kp_ref, diag_ref, parts_ref, my_ref, own_ref, c1_ref, c2_ref, va_ref, vb_ref,
    v1a_ref, v1b_ref, v3_ref, inner_in, outer_in,
    c3_ref, vt_ref, vl_ref, v1_ref, face_ref, yd_ref, yu_ref, inner_ref, outer_ref, down_ref, up_ref,
):
    z = l_ref.shape[3]
    arrive("gy", inner_in, outer_in, yd_ref, yu_ref)
    xs = (0, wx - 1)
    results = after_y(wx, wy, xs, visc_ref, l_ref, kp_ref, parts_ref, my_ref, own_ref, v3_ref, yd_ref, yu_ref)
    row = lambda i, col: kp_ref[i, pl.ds(col, 1), :]
    tail = 48 * wx + 48
    rim_d = yd_ref[pl.ds(tail, yd_ref.shape[0] - tail), :].astype(F32)
    rim_u = yu_ref[pl.ds(tail, yu_ref.shape[0] - tail), :].astype(F32)
    ones = 8 * (wx + 1)
    base = ones + 16
    for n, (flux, top, top_one, low, low_one, face) in enumerate(results):
        for s in range(6):
            c3_ref[n, s] = flux[s]
        face_ref[n] = face
        for p in range(2):
            vt_ref[n, p] = settle(top, p)
            vl_ref[n, p] = settle(low, p)
    flux, top, top_one, low, low_one, face = results[1]
    mine = rim_u[ones : ones + 16] + tall([low_one[8:16], low_one[24:32]])
    v1_ref[0] = mine
    v1_ref[1] = v1a_ref[0]
    for y in range(wy - 2):
        v1_ref[2 + y] = v1b_ref[y]
    v1_ref[wy] = v1a_ref[1] + tall([top_one[8:16], top_one[24:32]])
    v1_ref[wy + 1] = rim_d[ones : ones + 16]

    def plane(i, n, p):
        lines = [rim_u[8 * i : 8 * i + 8] + vl_ref[n, p], va_ref[0, i]]
        lines += [vb_ref[y, i] for y in range(wy - 2)]
        lines += [va_ref[1, i] + vt_ref[n, p], rim_d[8 * i : 8 * i + 8]]
        return merge(lines[1::2], lines[0::2])

    down_ref[pl.ds(0, 48), :] = yu_ref[pl.ds(48 * wx, 48), :]
    for y in range(wy):
        down_ref[pl.ds(48 + 48 * y, 48), :] = l_ref[0, y]
    down_ref[pl.ds(48 * (wy + 1), 48), :] = yd_ref[pl.ds(48 * wx, 48), :]
    diag = [jnp.broadcast_to(diag_ref[pl.ds(y, 1), :], (4, z)) for y in range(wy)]
    high = [part.astype(BF).astype(F32) for part in diag]
    low_bits = [a - b for a, b in zip(diag, high)]
    high += [jnp.broadcast_to(rim_d[4:5], (4, z)), jnp.zeros((4, z), F32)]
    low_bits += [jnp.broadcast_to(rim_d[5:6], (4, z)), jnp.zeros((4, z), F32)]
    rim = [plane(0, 0, 0)] + high + low_bits
    rim += [rim_u[base + wx : base + wx + 1], kp_ref[0, 0:wy], rim_d[base + wx : base + wx + 1]]
    put_tail(down_ref, 48 * (wy + 2), rim)
    corner = (wx - 1) * wy
    up_ref[pl.ds(0, 48), :] = c1_ref[1, wx - 1].astype(BF)
    for y in range(1, wy - 1):
        up_ref[pl.ds(48 * y, 48), :] = c2_ref[1, wx * (y - 1) + wx - 1].astype(BF)
    up_ref[pl.ds(48 * (wy - 1), 48), :] = (c1_ref[1, 2 * wx - 1] + flux[1]).astype(BF)
    last = pl.ds(corner, wy)
    rim = [plane(wx, 1, 1), mine, rim_d[ones : ones + 16]]
    rim += [rim_u[base + wx - 1 : base + wx], kp_ref[5, last], rim_d[base + wx + 1 : base + wx + 2]]
    rim += [rim_u[base + 3 * wx - 1 : base + 3 * wx], kp_ref[2, last], rim_d[base + wx + 3 : base + wx + 4]]
    rim += [kp_ref[1, last], rim_d[base + wx - 1 : base + wx]]
    put_tail(up_ref, 48 * wy, rim)
    depart("gx", down_ref, up_ref, inner_ref, outer_ref)


def assemble_kernel(
    wx, wy, visc_ref, l_ref, kp_ref, diag_ref, parts_ref, mx_ref, my_ref, own_ref, c1_ref, c2_ref, c3_ref,
    va_ref, vb_ref, v3_ref, vt_ref, vl_ref, face_ref, yd_ref, yu_ref,
    r_ref, v_ref, inv_ref, ownx_ref, mid,
):
    z = l_ref.shape[3]
    cells = wx * wy
    xs = tuple(range(1, wx - 1))
    results = after_y(wx, wy, xs, visc_ref, l_ref, kp_ref, parts_ref, my_ref, own_ref, v3_ref, yd_ref, yu_ref)
    for n, part in enumerate(results):
        for s in range(6):
            mid[n, s] = part[0][s]
    traces = [yu_ref[pl.ds(48 * wx, 48), :]] + [l_ref[0, y] for y in range(wy)] + [yd_ref[pl.ds(48 * wx, 48), :]]
    ownx_ref[...] = dot(tall([mx_ref[pl.ds(48, 48), :], mx_ref[pl.ds(288, 192), :]]), wide(traces))

    def contrib(slot, x, y):
        if 0 < y < wy - 1:
            return c2_ref[slot, wx * (y - 1) + x]
        if y == 0:
            return c1_ref[slot, x]
        extra = mid[x - 1, slot] if 0 < x < wx - 1 else c3_ref[0 if x == 0 else 1, slot]
        return c1_ref[slot, wx + x] + extra

    for x in range(wx):
        for y in range(wy):
            col = pl.ds(x * wy + y, 48, stride=cells)
            if x:
                r_ref[0, col, :] = contrib(0, x, y) + contrib(1, x - 1, y)
            else:
                r_ref[0, col, :] = contrib(0, x, y)
            if y:
                behind = contrib(3, x, y - 1)
            elif 0 < x < wx - 1:
                behind = results[x - 1][5]
            else:
                behind = face_ref[0 if x == 0 else 1]
            r_ref[1, col, :] = contrib(2, x, y) + behind
            r_ref[2, col, :] = contrib(4, x, y) + z_prev(contrib(5, x, y))
    tail = 48 * wx + 48
    rim_d = yd_ref[pl.ds(tail, yd_ref.shape[0] - tail), :].astype(F32)
    rim_u = yu_ref[pl.ds(tail, yu_ref.shape[0] - tail), :].astype(F32)

    def brought(which, i):
        held = vt_ref if which == 1 else vl_ref
        terms = []
        for x, p in ((i, 0), (i - 1, 1)):
            if x in (0, wx - 1):
                terms.append(held[0 if x == 0 else 1, p])
            elif 0 < x < wx - 1:
                terms.append(settle(results[x - 1][which], p))
        return sum(terms[1:], terms[0])

    for i in range(wx + 1):
        lines = [rim_u[8 * i : 8 * i + 8] + brought(3, i), va_ref[0, i]]
        lines += [vb_ref[y, i] for y in range(wy - 2)]
        lines += [va_ref[1, i] + brought(1, i), rim_d[8 * i : 8 * i + 8]]
        v_ref[i] = merge(lines[1::2], lines[0::2])
        if i < wx:
            parts = [jnp.broadcast_to(diag_ref[pl.ds(i * wy + y, 1), :], (4, z)) for y in range(wy)]
            edge = rim_d[8 * i + 4 : 8 * i + 5] + rim_d[8 * i + 5 : 8 * i + 6]
            parts += [jnp.broadcast_to(edge, (4, z)), jnp.zeros((4, z), F32)]
            inv_ref[i] = reciprocal(tall(parts))


def reciprocal(diag):
    present = diag > 0.0
    return jnp.where(present, (1.0 / (gain * gain)) / jnp.where(present, diag, 1.0), 0.0)


def final_kernel(
    wx, wy, visc_ref, l_ref, kp_ref, parts_ref, mx_ref, ownx_ref, r_ref, v_ref, inv_ref, v1_ref,
    yd_ref, yu_ref, inner_in, outer_in, p_ref, out_ref, fix, xd_ref, xu_ref,
):
    arrive("gx", inner_in, outer_in, xd_ref, xu_ref)
    cells, z = wx * wy, l_ref.shape[3]
    rows = v_ref.shape[1]
    planes = (wx + 1) * rows
    row = lambda i, col: kp_ref[i, pl.ds(col, 1), :]
    delta = dot(mx_ref[...], wide([xd_ref[pl.ds(48 * j, 48), :] for j in range(wy + 2)]))
    rim_x = xd_ref[pl.ds(48 * (wy + 2), xd_ref.shape[0] - 48 * (wy + 2)), :].astype(F32)
    rim_l = xu_ref[pl.ds(48 * wy, xu_ref.shape[0] - 48 * wy), :].astype(F32)
    misc_d = tail_misc(yd_ref, wx)
    misc_u = tail_misc(yu_ref, wx)
    flags_high = rim_x[3 * rows : 3 * rows + wy + 2]
    corner = (wx - 1) * wy
    arrived = [xu_ref[pl.ds(48 * y, 48), :].astype(F32) for y in range(wy)]
    arrived_corners = slot_corners(arrived, parts_ref, 1)
    codes = rim_l[rows + 32 : rows + 32 + wy + 2]
    keep_z = rim_l[rows + 32 + wy + 2 : rows + 32 + 2 * (wy + 2)]
    keep_y = rim_l[rows + 32 + 2 * (wy + 2) : rows + 32 + 3 * (wy + 2) - 1]
    low_visc = level_visc(codes, visc_ref)
    low_keep_z = z_next(keep_z)
    lines = [[], [], []]
    high_flux = []
    for j in range(-1, wy + 1):
        n = j + 1
        part = delta[:, z * n : z * n + z]
        flag = flags_high[n : n + 1]
        if j < 0:
            visc = level_visc(misc_u[wx - 1 : wx], visc_ref)
            kz = misc_u[3 * wx - 1 : 3 * wx]
            keeps = [misc_u[2 * wx - 1 : 2 * wx], flag, None, row(1, corner), kz, z_next(kz)]
        elif j < wy:
            here = corner + j
            visc = row(4, here)
            high_y = row(1, here + 1) if j < wy - 1 else misc_d[wx - 1 : wx]
            keeps = [row(0, here), flag, row(1, here), high_y, row(2, here), row(3, here)]
        else:
            visc = level_visc(misc_d[wx + 1 : wx + 2], visc_ref)
            kz = misc_d[wx + 3 : wx + 4]
            keeps = [misc_d[wx + 2 : wx + 3], flag, misc_d[wx - 1 : wx], None, kz, z_next(kz)]
        scales = [None if keep is None else visc * keep for keep in keeps]
        corners = scaled_corners(part[288:480], scales)
        one = v1_ref[n] * flag
        lines[0].append(settle(corners, 0))
        lines[1].append(settle(corners, 1) + one[0:8] + z_prev(one[8:16]))
        high_flux.append([None if k is None else part[48 * s : 48 * s + 48] * k for s, k in enumerate(scales)])
        own = ownx_ref[:, pl.ds(z * n, z)]
        visc = low_visc[n : n + 1]
        flag = misc_u[wx : wx + 1] if j < 0 else misc_d[wx : wx + 1] if j == wy else row(0, j)
        scales = [
            None, visc * flag, None if j < 0 else visc * keep_y[j : j + 1],
            None if j == wy else visc * keep_y[j + 1 : j + 2], visc * keep_z[n : n + 1], visc * low_keep_z[n : n + 1],
        ]
        corners = settle(scaled_corners(own[48:240], scales), 1)
        if 0 <= j < wy:
            lines[2].append(corners + settle(arrived_corners[j] * flag, 1))
            face = (arrived[j] + visc * (own[0:48] + penalty * l_ref[0, j].astype(F32))) * flag
            r_ref[0, pl.ds(j, 48, stride=cells), :] += face
        else:
            at = rows + (0 if j < 0 else 16)
            one = rim_l[at : at + 16] * flag
            lines[2].append(corners + one[0:8] + z_prev(one[8:16]))
    low, before, first = [merge(part[1::2], part[0::2]) for part in lines]
    top = v_ref[wx] + before + rim_x[0:rows]
    values = [(v_ref[0] + first + rim_l[0:rows]) * inv_ref[0]]
    values += [v_ref[i] * inv_ref[i] for i in range(1, wx - 1)]
    values += [(v_ref[wx - 1] + low) * inv_ref[wx - 1]]
    values += [top * reciprocal(rim_x[rows : 2 * rows] + rim_x[2 * rows : 3 * rows])]
    value = tall(values)
    fix[...] = jnp.zeros_like(fix)
    fix[pl.ds(0, planes), :] = value
    fix[pl.ds(planes, planes), :] = z_next(value)
    rhs = fix[...].astype(BF)
    for j in range(wy):
        col = pl.ds(corner + j, 48, stride=cells)
        flux = high_flux[j + 1]
        r_ref[0, col, :] += flux[0]
        r_ref[1, col, :] += flux[2] + high_flux[j][3]
        r_ref[2, col, :] += flux[4] + z_prev(flux[5])
    for d in range(3):
        spread = dot(p_ref[pl.ds(48 * cells * d, 48 * cells), :], rhs)
        spread = spread.reshape(48, cells, z) * kp_ref[d][None]
        out_ref[d] = (r_ref[d] + spread.reshape(48 * cells, z)).astype(BF)


def call(body, args, outs, scratch, flops, hbm=False):
    if hbm:
        args = tuple(pltpu.with_memory_space_constraint(a, pltpu.HBM) for a in args)
    return pl.pallas_call(
        body,
        in_specs=[pl.BlockSpec(memory_space=pltpu.HBM if hbm else pltpu.VMEM)] * len(args),
        out_shape=outs,
        scratch_shapes=scratch,
        cost_estimate=pl.CostEstimate(flops=flops, bytes_accessed=1000000, transcendentals=0),
        compiler_params=pltpu.CompilerParams(vmem_limit_bytes=16 * 1024 * 1024),
    )(*args)


def local(traces, dirichlet, visc_class, viscosity, coarse_diag, solve_map, flux_map):
    wx, wy, z = traces.shape[2:]
    cells = wx * wy
    rows = 8 * (wy // 2 + 1)
    per_hex = 4 * 288 * 256 * z
    gather = jnp.asarray(gather_table())
    parts = jnp.asarray(slot_table())
    spread = jnp.asarray(spread_table(wx, wy, rows))
    vm = pltpu.VMEM
    bind = lambda body: functools.partial(body, wx, wy)
    y_message = vm((48 * wx + 48 + tail_rows(8 * (wx + 1) + 16 + 3 * wx), z), BF)
    y_outer = vm((y_message.shape[0] + 16, z), BF)
    x_message = vm((48 * (wy + 2) + tail_rows(3 * rows + wy + 2), z), BF)
    x_outer = vm((x_message.shape[0] + 16, z), BF)

    (lifted, flags, visc, diag, s_map, s_turned, f_map, gather, parts, c1, va, v1a, v3, inner, outer) = call(
        bind(first_kernel),
        (
            viscosity, traces.reshape(3, 48 * cells, z), dirichlet.reshape(3, cells, z),
            visc_class.reshape(cells, z), coarse_diag.reshape(cells, z), solve_map.T, flux_map, gather, parts,
        ),
        (
            vm((4, cells, 48, z), BF), vm((6, cells, z), F32), vm((viscosity.shape[0], z), F32), vm((cells, z), F32),
            vm(solve_map.shape, BF),
            vm(solve_map.shape[::-1], BF), vm(flux_map.shape, BF), vm(gather.shape, BF), vm(parts.shape, BF),
            vm((6, 2 * wx, 48, z), F32), vm((2, wx + 1, 8, z), F32), vm((2, 16, z), F32), vm((wx, 32, z), F32),
            y_message, y_outer,
        ),
        [
            y_message, y_message,
            vm((3, 48 * cells, z), BF), vm((3, cells, z), jnp.int32), vm((cells, z), jnp.int32),
            vm((48 * cells, z), F32), pltpu.SMEM(viscosity.shape, F32), pltpu.SemaphoreType.DMA((9,)),
        ],
        2 * wx * per_hex, True,
    )
    inner = swap(inner, "gy", 0)
    outer = swap(outer, "gy", 1)
    between = wx * (wy - 2)
    c2, vb, v1b, mx, my, own = call(
        bind(middle_kernel),
        (lifted, flags, s_map, s_turned, f_map, gather, parts),
        (
            vm((6, between, 48, z), F32), vm((wy - 2, wx + 1, 8, z), F32), vm((wy - 2, 16, z), F32),
            vm((480, 48), BF), vm((480, 48), BF), vm((240, wx * z), F32),
        ),
        [], between * per_hex,
    )
    c3, vt, vl, v1, face, yd, yu, inner, outer = call(
        bind(turn_kernel),
        (
            visc, lifted, flags, diag, parts, my, own, c1, c2, va, vb, v1a, v1b, v3, inner, outer,
        ),
        (
            vm((2, 6, 48, z), F32), vm((2, 2, 8, z), F32), vm((2, 2, 8, z), F32), vm((wy + 2, 16, z), F32),
            vm((2, 48, z), F32), y_message, y_message, x_message, x_outer,
        ),
        [x_message, x_message], 2 * per_hex,
    )
    inner = swap(inner, "gx", 0)
    outer = swap(outer, "gx", 1)
    residual, vs, inverse, ownx = call(
        bind(assemble_kernel),
        (
            visc, lifted, flags, diag, parts, mx, my, own, c1, c2, c3, va, vb, v3, vt, vl, face, yd, yu,
        ),
        (
            vm((3, 48 * cells, z), F32), vm((wx + 1, rows, z), F32), vm((wx, rows, z), F32),
            vm((240, (wy + 2) * z), F32),
        ),
        [vm((wx - 2, 6, 48, z), F32)], 4 * per_hex,
    )
    out = call(
        bind(final_kernel),
        (
            visc, lifted, flags, parts, mx, ownx, residual, vs, inverse, v1, yd, yu, inner, outer, spread,
        ),
        jax.ShapeDtypeStruct((3, 48 * cells, z), BF),
        [vm((spread.shape[1], z), F32), x_message, x_message], 2 * spread.size * z,
    )
    return out.reshape(traces.shape)


def solution(mesh):
    in_specs = (
        P(None, None, "gx", "gy", None),
        P(None, "gx", "gy", None),
        P("gx", "gy", None),
        P(),
        P("gx", "gy", None),
        P(),
        P(),
    )
    out_specs = P(None, None, "gx", "gy", None)
    return jax.shard_map(local, mesh=mesh, in_specs=in_specs, out_specs=out_specs, check_vma=False)
```

```python
import functools
import math

import jax
import jax.numpy as jnp
import ml_dtypes
import numpy as np
from jax import lax
from jax.experimental import pallas as pl
from jax.experimental.pallas import tpu as pltpu
from jax.sharding import PartitionSpec as P

penalty = 0.5
BF = jnp.bfloat16
F32 = jnp.float32
lift = 1.3264
gain = 1.3280711361297461


def swap(value, axis, first, ring=False):
    count = lax.axis_size(axis)
    pairs = [(low, low + 1) for low in range(first, count - 1, 2)]
    if ring and first and count % 2 == 0:
        pairs.append((count - 1, 0))
    return lax.ppermute(value, axis, pairs + [(high, low) for low, high in pairs])


def even(axis):
    return lax.rem(lax.axis_index(axis), 2) == 0


def arrive(axis, inner_ref, outer_ref, down_ref, up_ref):
    here, last = lax.axis_index(axis), lax.axis_size(axis) - 1
    choose(even(axis), inner_ref, outer_ref, down_ref, here < last)
    choose(even(axis), outer_ref, inner_ref, up_ref, here > 0)


def depart(axis, down_ref, up_ref, inner_ref, outer_ref):
    choose(even(axis), up_ref, down_ref, inner_ref)
    choose(even(axis), down_ref, up_ref, outer_ref)


def choose(condition, yes_ref, no_ref, out_ref, present=None):
    size = min(yes_ref.shape[0], no_ref.shape[0], out_ref.shape[0])
    rows = pl.ds(0, size)
    value = jnp.where(condition, yes_ref[rows, :], no_ref[rows, :])
    out_ref[rows, :] = value if present is None else jnp.where(present, value, jnp.zeros_like(value))
    if out_ref.shape[0] > size:
        rest = pl.ds(size, out_ref.shape[0] - size)
        out_ref[rest, :] = jnp.zeros((out_ref.shape[0] - size, out_ref.shape[1]), out_ref.dtype)


def corner_table():
    gll_points = [-1.0, -math.sqrt(0.2), math.sqrt(0.2), 1.0]
    table = np.zeros((16, 4), np.float64)
    for s in range(4):
        for t in range(4):
            for p in range(2):
                for q in range(2):
                    table[4 * s + t, 2 * p + q] = (
                        (1 + (2 * p - 1) * gll_points[s]) * (1 + (2 * q - 1) * gll_points[t]) / 4
                    )
    return table


def landing(face_slot, high_s, high_t):
    direction, outward = divmod(face_slot, 2)
    if direction == 0:
        return (outward, high_s, high_t)
    if direction == 1:
        return (high_s, outward, high_t)
    return (high_s, high_t, outward)


def gather_table():
    weights = lift * corner_table()
    table = np.zeros((32, 288), np.float64)
    for slot in range(6):
        for s in range(2):
            for t in range(2):
                p, q, r = landing(slot, s, t)
                for c in range(3):
                    cols = slot * 48 + 16 * c + np.arange(16)
                    table[16 * r + 8 * p + 4 * q + c, cols] += weights[:, 2 * s + t]
    return table.astype(ml_dtypes.bfloat16)


def slot_table():
    return np.concatenate(np.split(gather_table(), 6, axis=1), axis=0)


def spread_table(wx, wy, rows):
    weights = lift * corner_table()
    planes = (wx + 1) * rows
    depth = -(-2 * planes // 128) * 128
    table = np.zeros((3, 48, wx, wy, depth), np.float64)
    for d in range(3):
        for x in range(wx):
            for y in range(wy):
                for s in range(2):
                    for t in range(2):
                        p, q, r = landing(2 * d, s, t)
                        for c in range(3):
                            k = r * planes + (x + p) * rows + 4 * (y + q) + c
                            table[d, 16 * c : 16 * c + 16, x, y, k] += weights[:, 2 * s + t]
    return table.reshape(-1, depth).astype(ml_dtypes.bfloat16)


def lanes(shape):
    return lax.broadcasted_iota(jnp.int32, shape, len(shape) - 1)


def z_next(value):
    last = value.shape[-1] - 1
    return jnp.where(lanes(value.shape) < last, pltpu.roll(value, last, value.ndim - 1), 0.0)


def z_prev(value):
    return jnp.where(lanes(value.shape) > 0, pltpu.roll(value, 1, value.ndim - 1), 0.0)


def dot(left, right):
    return jnp.dot(left, right, preferred_element_type=F32)


def wide(parts):
    return jnp.concatenate(parts, axis=1)


def tall(parts):
    return jnp.concatenate(parts, axis=0)


def hex_batch(slots, scales, s_map, f_map):
    z = slots[0][0].shape[1]
    element = tall([wide([hexa[s] for hexa in slots]) for s in range(6)])
    interior = dot(s_map, element).astype(BF)
    flux = dot(f_map, interior) + penalty * element.astype(F32)
    return [
        [flux[48 * s : 48 * s + 48, z * h : z * h + z] * scales[h][s] for s in range(6)]
        for h in range(len(slots))
    ]


def corner_batch(blocks, left_out, gather):
    z = blocks[0][0].shape[1]
    nothing = jnp.zeros((48, z), BF)
    right = tall(
        [
            wide([nothing if s in left_out[h] else blocks[h][s].astype(BF) for h in range(len(blocks))])
            for s in range(6)
        ]
    )
    return [dot(gather, right)[:, z * h : z * h + z] for h in range(len(blocks))]


def slot_corners(traces, parts_ref, slot):
    z = traces[0].shape[1]
    rows = dot(parts_ref[pl.ds(32 * slot, 32), :], wide([trace.astype(BF) for trace in traces]))
    return [rows[:, z * h : z * h + z] for h in range(len(traces))]


def settle(rows, p):
    return rows[8 * p : 8 * p + 8] + z_prev(rows[16 + 8 * p : 24 + 8 * p])


def scaled_corners(delta, scales):
    terms = [delta[32 * s : 32 * s + 32] * scales[s] for s in range(6) if scales[s] is not None]
    return sum(terms[1:], terms[0])


def level_visc(code, visc_ref):
    visc = jnp.zeros(code.shape, F32)
    for level in range(visc_ref.shape[0]):
        visc = visc + jnp.where(code == F32(level + 1), visc_ref[pl.ds(level, 1), :], F32(0.0))
    return visc


def merge(even, odd):
    odd = tall(odd)
    return tall(even) + pltpu.roll(odd, odd.shape[0] - 4, 0)


def first_kernel(
    wx, wy, visc_hbm, t_hbm, dir_hbm, cls_hbm, diag_hbm, st_hbm, f_hbm, g_hbm, parts_hbm,
    l_ref, kp_ref, visc_ref, diag_ref, s_ref, st_ref, f_ref, g_ref, parts_ref, c_ref, v_ref, v1_ref, v3_ref,
    inner_ref, outer_ref, down_ref, up_ref, t_ref, dir_ref, cls_ref, nat, levels, sems,
):
    cells = wx * wy
    pairs = [
        (t_hbm, t_ref), (dir_hbm, dir_ref), (cls_hbm, cls_ref), (diag_hbm, diag_ref),
        (st_hbm, st_ref), (f_hbm, f_ref), (g_hbm, g_ref), (parts_hbm, parts_ref),
        (visc_hbm, levels),
    ]
    copies = [pltpu.make_async_copy(a, b, sems.at[i]) for i, (a, b) in enumerate(pairs)]
    for copy in copies:
        copy.start()
    copies[4].wait()
    s_ref[...] = st_ref[...].T
    for i in (8, 1, 2, 3, 0):
        copies[i].wait()
    z = t_ref.shape[2]
    for level in range(visc_ref.shape[0]):
        visc_ref[pl.ds(level, 1), :] = jnp.full((1, z), levels[level], F32)
    code = cls_ref[...].astype(F32) + 1.0
    kp_ref[4] = level_visc(code, visc_ref)
    kp_ref[5] = code
    for d in range(3):
        keep = (1 - dir_ref[d]).astype(F32)
        kp_ref[d] = keep
        masked = t_ref[d].astype(F32).reshape(48, cells, z) * keep[None]
        nat[...] = masked.reshape(48 * cells, z)
        for col in range(cells):
            part = nat[pl.ds(col, 48, stride=cells), :]
            l_ref[d, col] = part.astype(BF)
            if d == 2:
                l_ref[3, col] = z_next(part).astype(BF)
    kp_ref[3] = z_next(kp_ref[2])
    for i in (5, 6, 7):
        copies[i].wait()
    row = lambda i, col: kp_ref[i, pl.ds(col, 1), :]
    where = [(x, 0) for x in range(wx)] + [(x, wy - 1) for x in range(wx)]
    blocks, left_out = known_hexes(wx, wy, where, l_ref, kp_ref, s_ref, f_ref, c_ref)
    corners = corner_batch(blocks, left_out, g_ref[...])
    lone = slot_corners([blocks[wx - 1][1], blocks[2 * wx - 1][1]], parts_ref, 1)
    for h in range(2):
        v1_ref[h, 0:8] = lone[h][8:16]
        v1_ref[h, 8:16] = lone[h][24:32]
    for x, rows in enumerate(slot_corners([blocks[wx + x][3] for x in range(wx)], parts_ref, 3)):
        v3_ref[x] = rows
    sums = [line_sums(corners[:wx]), line_sums(corners[wx:])]
    for side in range(2):
        for i in range(wx + 1):
            v_ref[side, i] = sums[side][i]
    corner = (wx - 1) * wy
    top = wy - 1
    for x in range(wx):
        down_ref[pl.ds(48 * x, 48), :] = l_ref[1, x * wy]
        up_ref[pl.ds(48 * x, 48), :] = blocks[wx + x][3].astype(BF)
    down_ref[pl.ds(48 * wx, 48), :] = l_ref[0, 0]
    up_ref[pl.ds(48 * wx, 48), :] = l_ref[0, top]
    place = lax.broadcasted_iota(jnp.int32, (8, z), 0)
    rim = []
    for i in range(wx):
        diag = diag_ref[pl.ds(i * wy, 1), :]
        high = diag.astype(BF).astype(F32)
        rim.append(jnp.where(place == 4, high, jnp.where(place == 5, diag - high, sums[0][i])))
    rim += [sums[0][wx], v1_ref[0]]
    rim += [row(1, x * wy) for x in range(wx)] + [row(0, 0), row(5, corner), row(0, corner), row(2, corner)]
    put_tail(down_ref, 48 * wx + 48, rim)
    rim = [sums[1][i] for i in range(wx + 1)] + [v1_ref[1]]
    for kind in (5, 0, 2):
        rim += [row(kind, x * wy + top) for x in range(wx)]
    put_tail(up_ref, 48 * wx + 48, rim)
    depart("gy", down_ref, up_ref, inner_ref, outer_ref)


def tail_rows(count):
    return -(-count // 16) * 16


def put_tail(ref, start, rows):
    count = sum(part.shape[0] for part in rows)
    full = ref.shape[0] - start
    if full > count:
        rows = rows + [jnp.zeros((full - count, rows[0].shape[1]), F32)]
    ref[pl.ds(start, full), :] = tall(rows).astype(BF)


def tail_misc(ref, wx):
    start = 48 * wx + 48
    return ref[pl.ds(start, ref.shape[0] - start), :].astype(F32)[8 * (wx + 1) + 16 :]


def line_sums(corners):
    width = len(corners)
    low = [settle(rows, 0) for rows in corners]
    high = [settle(rows, 1) for rows in corners]
    return [low[0]] + [low[x] + high[x - 1] for x in range(1, width)] + [high[-1]]


def known_hexes(wx, wy, where, l_ref, kp_ref, s_ref, f_ref, c_ref):
    z = l_ref.shape[3]
    nothing = jnp.zeros((48, z), BF)
    row = lambda i, col: kp_ref[i, pl.ds(col, 1), :]
    slots, scales, left_out = [], [], []
    for x, y in where:
        here = x * wy + y
        visc = row(4, here)
        last_x, last_y = x == wx - 1, y == wy - 1
        slots.append(
            [
                l_ref[0, here], nothing if last_x else l_ref[0, here + wy],
                l_ref[1, here], nothing if last_y else l_ref[1, here + 1],
                l_ref[2, here], l_ref[3, here],
            ]
        )
        scales.append(
            [
                visc * row(0, here), visc if last_x else visc * row(0, here + wy),
                visc * row(1, here), visc if last_y else visc * row(1, here + 1),
                visc * row(2, here), visc * row(3, here),
            ]
        )
        left_out.append(([1] if last_x else []) + ([3] if last_y else []))
    blocks = hex_batch(slots, scales, s_ref[...], f_ref[...])
    for h in range(len(where)):
        for s in range(6):
            c_ref[s, h] = blocks[h][s]
    return blocks, left_out


def middle_kernel(
    wx, wy, l_ref, kp_ref, s_ref, st_ref, f_ref, g_ref, parts_ref,
    c_ref, v_ref, v1_ref, mx_ref, my_ref, own_ref,
):
    z = l_ref.shape[3]
    for slot, ref in ((1, mx_ref), (3, my_ref)):
        flux = lax.dot_general(
            f_ref[...], st_ref[pl.ds(48 * slot, 48), :], (((1,), (1,)), ((), ())),
            preferred_element_type=F32,
        )
        ref[pl.ds(0, 288), :] = flux.astype(BF)
        eye = lax.broadcasted_iota(jnp.int32, (48, 48), 0) == lax.broadcasted_iota(jnp.int32, (48, 48), 1)
        for s in range(6):
            block = flux[48 * s : 48 * s + 48]
            if s == slot:
                block = block + jnp.where(eye, F32(penalty), F32(0.0))
            ref[pl.ds(288 + 32 * s, 32), :] = dot(parts_ref[pl.ds(32 * s, 32), :], block.astype(BF)).astype(BF)
    own_ref[...] = dot(tall([my_ref[pl.ds(144, 48), :], my_ref[pl.ds(288, 192), :]]), wide([l_ref[1, x * wy] for x in range(wx)]))
    where = [(x, y) for y in range(1, wy - 1) for x in range(wx)]
    blocks, left_out = known_hexes(wx, wy, where, l_ref, kp_ref, s_ref, f_ref, c_ref)
    corners = corner_batch(blocks, left_out, g_ref[...])
    lone = slot_corners([blocks[wx * y + wx - 1][1] for y in range(wy - 2)], parts_ref, 1)
    for y in range(wy - 2):
        v1_ref[y, 0:8] = lone[y][8:16]
        v1_ref[y, 8:16] = lone[y][24:32]
        for i, rows in enumerate(line_sums(corners[wx * y : wx * y + wx])):
            v_ref[y, i] = rows


def after_y(wx, wy, xs, visc_ref, l_ref, kp_ref, parts_ref, my_ref, own_ref, v3_ref, down_ref, up_ref):
    z = l_ref.shape[3]
    misc_d = tail_misc(down_ref, wx)
    misc_u = tail_misc(up_ref, wx)
    row = lambda i, col: kp_ref[i, pl.ds(col, 1), :]
    delta = dot(my_ref[...], wide([down_ref[pl.ds(48 * x, 48), :] for x in xs]))
    arrived = [up_ref[pl.ds(48 * x, 48), :].astype(F32) for x in xs]
    arrived_corners = slot_corners(arrived, parts_ref, 3)
    results = []
    for n, x in enumerate(xs):
        here = x * wy + wy - 1
        last = x == wx - 1
        part = delta[:, z * n : z * n + z]
        visc = row(4, here)
        scales = [
            visc * row(0, here), visc if last else visc * row(0, here + wy), visc * row(1, here),
            visc * misc_d[x : x + 1], visc * row(2, here), visc * row(3, here),
        ]
        flux = [part[48 * s : 48 * s + 48] * scales[s] for s in range(6)]
        used = [None if (s == 1 and last) else scales[s] for s in range(6)]
        top = scaled_corners(part[288:480], used) + v3_ref[x] * misc_d[x : x + 1]
        top_one = part[320:352] * visc
        here = x * wy
        visc = level_visc(misc_u[x : x + 1], visc_ref)
        flag = row(1, here)
        own = own_ref[:, pl.ds(z * x, z)]
        keep_z = misc_u[2 * wx + x : 2 * wx + x + 1]
        scales = [
            visc * misc_u[wx + x : wx + x + 1], None if last else visc * misc_u[wx + x + 1 : wx + x + 2],
            None, visc * flag, visc * keep_z, visc * z_next(keep_z),
        ]
        low = scaled_corners(own[48:240], scales) + arrived_corners[n] * flag
        low_one = own[80:112] * visc
        face = (arrived[n] + visc * (own[0:48] + penalty * l_ref[1, here].astype(F32))) * flag
        results.append((flux, top, top_one, low, low_one, face))
    return results


def turn_kernel(
    wx, wy, visc_ref, l_ref, kp_ref, diag_ref, parts_ref, my_ref, own_ref, c1_ref, c2_ref, va_ref, vb_ref,
    v1a_ref, v1b_ref, v3_ref, inner_in, outer_in,
    c3_ref, vt_ref, vl_ref, v1_ref, face_ref, yd_ref, yu_ref, inner_ref, outer_ref, down_ref, up_ref,
):
    z = l_ref.shape[3]
    arrive("gy", inner_in, outer_in, yd_ref, yu_ref)
    xs = (0, wx - 1)
    results = after_y(wx, wy, xs, visc_ref, l_ref, kp_ref, parts_ref, my_ref, own_ref, v3_ref, yd_ref, yu_ref)
    row = lambda i, col: kp_ref[i, pl.ds(col, 1), :]
    tail = 48 * wx + 48
    rim_d = yd_ref[pl.ds(tail, yd_ref.shape[0] - tail), :].astype(F32)
    rim_u = yu_ref[pl.ds(tail, yu_ref.shape[0] - tail), :].astype(F32)
    ones = 8 * (wx + 1)
    base = ones + 16
    for n, (flux, top, top_one, low, low_one, face) in enumerate(results):
        for s in range(6):
            c3_ref[n, s] = flux[s]
        face_ref[n] = face
        for p in range(2):
            vt_ref[n, p] = settle(top, p)
            vl_ref[n, p] = settle(low, p)
    flux, top, top_one, low, low_one, face = results[1]
    mine = rim_u[ones : ones + 16] + tall([low_one[8:16], low_one[24:32]])
    v1_ref[0] = mine
    v1_ref[1] = v1a_ref[0]
    for y in range(wy - 2):
        v1_ref[2 + y] = v1b_ref[y]
    v1_ref[wy] = v1a_ref[1] + tall([top_one[8:16], top_one[24:32]])
    v1_ref[wy + 1] = rim_d[ones : ones + 16]

    def plane(i, n, p):
        lines = [rim_u[8 * i : 8 * i + 8] + vl_ref[n, p], va_ref[0, i]]
        lines += [vb_ref[y, i] for y in range(wy - 2)]
        lines += [va_ref[1, i] + vt_ref[n, p], rim_d[8 * i : 8 * i + 8]]
        return merge(lines[1::2], lines[0::2])

    down_ref[pl.ds(0, 48), :] = yu_ref[pl.ds(48 * wx, 48), :]
    for y in range(wy):
        down_ref[pl.ds(48 + 48 * y, 48), :] = l_ref[0, y]
    down_ref[pl.ds(48 * (wy + 1), 48), :] = yd_ref[pl.ds(48 * wx, 48), :]
    diag = [jnp.broadcast_to(diag_ref[pl.ds(y, 1), :], (4, z)) for y in range(wy)]
    high = [part.astype(BF).astype(F32) for part in diag]
    low_bits = [a - b for a, b in zip(diag, high)]
    high += [jnp.broadcast_to(rim_d[4:5], (4, z)), jnp.zeros((4, z), F32)]
    low_bits += [jnp.broadcast_to(rim_d[5:6], (4, z)), jnp.zeros((4, z), F32)]
    rim = [plane(0, 0, 0)] + high + low_bits
    rim += [rim_u[base + wx : base + wx + 1], kp_ref[0, 0:wy], rim_d[base + wx : base + wx + 1]]
    put_tail(down_ref, 48 * (wy + 2), rim)
    corner = (wx - 1) * wy
    up_ref[pl.ds(0, 48), :] = c1_ref[1, wx - 1].astype(BF)
    for y in range(1, wy - 1):
        up_ref[pl.ds(48 * y, 48), :] = c2_ref[1, wx * (y - 1) + wx - 1].astype(BF)
    up_ref[pl.ds(48 * (wy - 1), 48), :] = (c1_ref[1, 2 * wx - 1] + flux[1]).astype(BF)
    last = pl.ds(corner, wy)
    rim = [plane(wx, 1, 1), mine, rim_d[ones : ones + 16]]
    rim += [rim_u[base + wx - 1 : base + wx], kp_ref[5, last], rim_d[base + wx + 1 : base + wx + 2]]
    rim += [rim_u[base + 3 * wx - 1 : base + 3 * wx], kp_ref[2, last], rim_d[base + wx + 3 : base + wx + 4]]
    rim += [kp_ref[1, last], rim_d[base + wx - 1 : base + wx]]
    put_tail(up_ref, 48 * wy, rim)
    depart("gx", down_ref, up_ref, inner_ref, outer_ref)


def assemble_kernel(
    wx, wy, visc_ref, l_ref, kp_ref, diag_ref, parts_ref, mx_ref, my_ref, own_ref, c1_ref, c2_ref, c3_ref,
    va_ref, vb_ref, v3_ref, vt_ref, vl_ref, face_ref, yd_ref, yu_ref,
    r_ref, v_ref, inv_ref, ownx_ref, mid,
):
    z = l_ref.shape[3]
    cells = wx * wy
    xs = tuple(range(1, wx - 1))
    results = after_y(wx, wy, xs, visc_ref, l_ref, kp_ref, parts_ref, my_ref, own_ref, v3_ref, yd_ref, yu_ref)
    for n, part in enumerate(results):
        for s in range(6):
            mid[n, s] = part[0][s]
    traces = [yu_ref[pl.ds(48 * wx, 48), :]] + [l_ref[0, y] for y in range(wy)] + [yd_ref[pl.ds(48 * wx, 48), :]]
    ownx_ref[...] = dot(tall([mx_ref[pl.ds(48, 48), :], mx_ref[pl.ds(288, 192), :]]), wide(traces))

    def contrib(slot, x, y):
        if 0 < y < wy - 1:
            return c2_ref[slot, wx * (y - 1) + x]
        if y == 0:
            return c1_ref[slot, x]
        extra = mid[x - 1, slot] if 0 < x < wx - 1 else c3_ref[0 if x == 0 else 1, slot]
        return c1_ref[slot, wx + x] + extra

    for x in range(wx):
        for y in range(wy):
            col = pl.ds(x * wy + y, 48, stride=cells)
            if x:
                r_ref[0, col, :] = contrib(0, x, y) + contrib(1, x - 1, y)
            else:
                r_ref[0, col, :] = contrib(0, x, y)
            if y:
                behind = contrib(3, x, y - 1)
            elif 0 < x < wx - 1:
                behind = results[x - 1][5]
            else:
                behind = face_ref[0 if x == 0 else 1]
            r_ref[1, col, :] = contrib(2, x, y) + behind
            r_ref[2, col, :] = contrib(4, x, y) + z_prev(contrib(5, x, y))
    tail = 48 * wx + 48
    rim_d = yd_ref[pl.ds(tail, yd_ref.shape[0] - tail), :].astype(F32)
    rim_u = yu_ref[pl.ds(tail, yu_ref.shape[0] - tail), :].astype(F32)

    def brought(which, i):
        held = vt_ref if which == 1 else vl_ref
        terms = []
        for x, p in ((i, 0), (i - 1, 1)):
            if x in (0, wx - 1):
                terms.append(held[0 if x == 0 else 1, p])
            elif 0 < x < wx - 1:
                terms.append(settle(results[x - 1][which], p))
        return sum(terms[1:], terms[0])

    for i in range(wx + 1):
        lines = [rim_u[8 * i : 8 * i + 8] + brought(3, i), va_ref[0, i]]
        lines += [vb_ref[y, i] for y in range(wy - 2)]
        lines += [va_ref[1, i] + brought(1, i), rim_d[8 * i : 8 * i + 8]]
        v_ref[i] = merge(lines[1::2], lines[0::2])
        if i < wx:
            parts = [jnp.broadcast_to(diag_ref[pl.ds(i * wy + y, 1), :], (4, z)) for y in range(wy)]
            edge = rim_d[8 * i + 4 : 8 * i + 5] + rim_d[8 * i + 5 : 8 * i + 6]
            parts += [jnp.broadcast_to(edge, (4, z)), jnp.zeros((4, z), F32)]
            inv_ref[i] = reciprocal(tall(parts))


def reciprocal(diag):
    present = diag > 0.0
    return jnp.where(present, (1.0 / (gain * gain)) / jnp.where(present, diag, 1.0), 0.0)


def final_kernel(
    wx, wy, visc_ref, l_ref, kp_ref, parts_ref, mx_ref, ownx_ref, r_ref, v_ref, inv_ref, v1_ref,
    yd_ref, yu_ref, inner_in, outer_in, p_ref, out_ref, fix, xd_ref, xu_ref,
):
    arrive("gx", inner_in, outer_in, xd_ref, xu_ref)
    cells, z = wx * wy, l_ref.shape[3]
    rows = v_ref.shape[1]
    planes = (wx + 1) * rows
    row = lambda i, col: kp_ref[i, pl.ds(col, 1), :]
    delta = dot(mx_ref[...], wide([xd_ref[pl.ds(48 * j, 48), :] for j in range(wy + 2)]))
    rim_x = xd_ref[pl.ds(48 * (wy + 2), xd_ref.shape[0] - 48 * (wy + 2)), :].astype(F32)
    rim_l = xu_ref[pl.ds(48 * wy, xu_ref.shape[0] - 48 * wy), :].astype(F32)
    misc_d = tail_misc(yd_ref, wx)
    misc_u = tail_misc(yu_ref, wx)
    flags_high = rim_x[3 * rows : 3 * rows + wy + 2]
    corner = (wx - 1) * wy
    arrived = [xu_ref[pl.ds(48 * y, 48), :].astype(F32) for y in range(wy)]
    arrived_corners = slot_corners(arrived, parts_ref, 1)
    codes = rim_l[rows + 32 : rows + 32 + wy + 2]
    keep_z = rim_l[rows + 32 + wy + 2 : rows + 32 + 2 * (wy + 2)]
    keep_y = rim_l[rows + 32 + 2 * (wy + 2) : rows + 32 + 3 * (wy + 2) - 1]
    low_visc = level_visc(codes, visc_ref)
    low_keep_z = z_next(keep_z)
    lines = [[], [], []]
    high_flux = []
    for j in range(-1, wy + 1):
        n = j + 1
        part = delta[:, z * n : z * n + z]
        flag = flags_high[n : n + 1]
        if j < 0:
            visc = level_visc(misc_u[wx - 1 : wx], visc_ref)
            kz = misc_u[3 * wx - 1 : 3 * wx]
            keeps = [misc_u[2 * wx - 1 : 2 * wx], flag, None, row(1, corner), kz, z_next(kz)]
        elif j < wy:
            here = corner + j
            visc = row(4, here)
            high_y = row(1, here + 1) if j < wy - 1 else misc_d[wx - 1 : wx]
            keeps = [row(0, here), flag, row(1, here), high_y, row(2, here), row(3, here)]
        else:
            visc = level_visc(misc_d[wx + 1 : wx + 2], visc_ref)
            kz = misc_d[wx + 3 : wx + 4]
            keeps = [misc_d[wx + 2 : wx + 3], flag, misc_d[wx - 1 : wx], None, kz, z_next(kz)]
        scales = [None if keep is None else visc * keep for keep in keeps]
        corners = scaled_corners(part[288:480], scales)
        one = v1_ref[n] * flag
        lines[0].append(settle(corners, 0))
        lines[1].append(settle(corners, 1) + one[0:8] + z_prev(one[8:16]))
        high_flux.append([None if k is None else part[48 * s : 48 * s + 48] * k for s, k in enumerate(scales)])
        own = ownx_ref[:, pl.ds(z * n, z)]
        visc = low_visc[n : n + 1]
        flag = misc_u[wx : wx + 1] if j < 0 else misc_d[wx : wx + 1] if j == wy else row(0, j)
        scales = [
            None, visc * flag, None if j < 0 else visc * keep_y[j : j + 1],
            None if j == wy else visc * keep_y[j + 1 : j + 2], visc * keep_z[n : n + 1], visc * low_keep_z[n : n + 1],
        ]
        corners = settle(scaled_corners(own[48:240], scales), 1)
        if 0 <= j < wy:
            lines[2].append(corners + settle(arrived_corners[j] * flag, 1))
            face = (arrived[j] + visc * (own[0:48] + penalty * l_ref[0, j].astype(F32))) * flag
            r_ref[0, pl.ds(j, 48, stride=cells), :] += face
        else:
            at = rows + (0 if j < 0 else 16)
            one = rim_l[at : at + 16] * flag
            lines[2].append(corners + one[0:8] + z_prev(one[8:16]))
    low, before, first = [merge(part[1::2], part[0::2]) for part in lines]
    top = v_ref[wx] + before + rim_x[0:rows]
    values = [(v_ref[0] + first + rim_l[0:rows]) * inv_ref[0]]
    values += [v_ref[i] * inv_ref[i] for i in range(1, wx - 1)]
    values += [(v_ref[wx - 1] + low) * inv_ref[wx - 1]]
    values += [top * reciprocal(rim_x[rows : 2 * rows] + rim_x[2 * rows : 3 * rows])]
    value = tall(values)
    fix[...] = jnp.zeros_like(fix)
    fix[pl.ds(0, planes), :] = value
    fix[pl.ds(planes, planes), :] = z_next(value)
    rhs = fix[...].astype(BF)
    for j in range(wy):
        col = pl.ds(corner + j, 48, stride=cells)
        flux = high_flux[j + 1]
        r_ref[0, col, :] += flux[0]
        r_ref[1, col, :] += flux[2] + high_flux[j][3]
        r_ref[2, col, :] += flux[4] + z_prev(flux[5])
    for d in range(3):
        spread = dot(p_ref[pl.ds(48 * cells * d, 48 * cells), :], rhs)
        spread = spread.reshape(48, cells, z) * kp_ref[d][None]
        out_ref[d] = (r_ref[d] + spread.reshape(48 * cells, z)).astype(BF)


def call(body, args, outs, scratch, flops, hbm=False):
    if hbm:
        args = tuple(pltpu.with_memory_space_constraint(a, pltpu.HBM) for a in args)
    return pl.pallas_call(
        body,
        in_specs=[pl.BlockSpec(memory_space=pltpu.HBM if hbm else pltpu.VMEM)] * len(args),
        out_shape=outs,
        scratch_shapes=scratch,
        cost_estimate=pl.CostEstimate(flops=flops, bytes_accessed=1000000, transcendentals=0),
        compiler_params=pltpu.CompilerParams(vmem_limit_bytes=16 * 1024 * 1024),
    )(*args)


def local(traces, dirichlet, visc_class, viscosity, coarse_diag, solve_map, flux_map):
    wx, wy, z = traces.shape[2:]
    cells = wx * wy
    rows = 8 * (wy // 2 + 1)
    per_hex = 4 * 288 * 256 * z
    gather = jnp.asarray(gather_table())
    parts = jnp.asarray(slot_table())
    spread = jnp.asarray(spread_table(wx, wy, rows))
    vm = pltpu.VMEM
    bind = lambda body: functools.partial(body, wx, wy)
    y_message = vm((48 * wx + 48 + tail_rows(8 * (wx + 1) + 16 + 3 * wx), z), BF)
    y_outer = vm((y_message.shape[0] + 16, z), BF)
    x_message = vm((48 * (wy + 2) + tail_rows(3 * rows + wy + 2), z), BF)
    x_outer = vm((x_message.shape[0] + 16, z), BF)

    (lifted, flags, visc, diag, s_map, s_turned, f_map, gather, parts, c1, va, v1a, v3, inner, outer) = call(
        bind(first_kernel),
        (
            viscosity, traces.reshape(3, 48 * cells, z), dirichlet.reshape(3, cells, z),
            visc_class.reshape(cells, z), coarse_diag.reshape(cells, z), solve_map.T, flux_map, gather, parts,
        ),
        (
            vm((4, cells, 48, z), BF), vm((6, cells, z), F32), vm((viscosity.shape[0], z), F32), vm((cells, z), F32),
            vm(solve_map.shape, BF),
            vm(solve_map.shape[::-1], BF), vm(flux_map.shape, BF), vm(gather.shape, BF), vm(parts.shape, BF),
            vm((6, 2 * wx, 48, z), F32), vm((2, wx + 1, 8, z), F32), vm((2, 16, z), F32), vm((wx, 32, z), F32),
            y_message, y_outer,
        ),
        [
            y_message, y_message,
            vm((3, 48 * cells, z), BF), vm((3, cells, z), jnp.int32), vm((cells, z), jnp.int32),
            vm((48 * cells, z), F32), pltpu.SMEM(viscosity.shape, F32), pltpu.SemaphoreType.DMA((9,)),
        ],
        2 * wx * per_hex, True,
    )
    inner = swap(inner, "gy", 0)
    outer = swap(outer, "gy", 1)
    between = wx * (wy - 2)
    c2, vb, v1b, mx, my, own = call(
        bind(middle_kernel),
        (lifted, flags, s_map, s_turned, f_map, gather, parts),
        (
            vm((6, between, 48, z), F32), vm((wy - 2, wx + 1, 8, z), F32), vm((wy - 2, 16, z), F32),
            vm((480, 48), BF), vm((480, 48), BF), vm((240, wx * z), F32),
        ),
        [], between * per_hex,
    )
    c3, vt, vl, v1, face, yd, yu, inner, outer = call(
        bind(turn_kernel),
        (
            visc, lifted, flags, diag, parts, my, own, c1, c2, va, vb, v1a, v1b, v3, inner, outer,
        ),
        (
            vm((2, 6, 48, z), F32), vm((2, 2, 8, z), F32), vm((2, 2, 8, z), F32), vm((wy + 2, 16, z), F32),
            vm((2, 48, z), F32), y_message, y_message, x_message, x_outer,
        ),
        [x_message, x_message], 2 * per_hex,
    )
    inner = swap(inner, "gx", 0)
    outer = swap(outer, "gx", 1, True)
    residual, vs, inverse, ownx = call(
        bind(assemble_kernel),
        (
            visc, lifted, flags, diag, parts, mx, my, own, c1, c2, c3, va, vb, v3, vt, vl, face, yd, yu,
        ),
        (
            vm((3, 48 * cells, z), F32), vm((wx + 1, rows, z), F32), vm((wx, rows, z), F32),
            vm((240, (wy + 2) * z), F32),
        ),
        [vm((wx - 2, 6, 48, z), F32)], 4 * per_hex,
    )
    out = call(
        bind(final_kernel),
        (
            visc, lifted, flags, parts, mx, ownx, residual, vs, inverse, v1, yd, yu, inner, outer, spread,
        ),
        jax.ShapeDtypeStruct((3, 48 * cells, z), BF),
        [vm((spread.shape[1], z), F32), x_message, x_message], 2 * spread.size * z,
    )
    return out.reshape(traces.shape)


def solution(mesh):
    in_specs = (
        P(None, None, "gx", "gy", None),
        P(None, "gx", "gy", None),
        P("gx", "gy", None),
        P(),
        P("gx", "gy", None),
        P(),
        P(),
    )
    out_specs = P(None, None, "gx", "gy", None)
    return jax.shard_map(local, mesh=mesh, in_specs=in_specs, out_specs=out_specs, check_vma=False)
```

```python
import functools
import math

import jax
import jax.numpy as jnp
import ml_dtypes
import numpy as np
from jax import lax
from jax.experimental import pallas as pl
from jax.experimental.pallas import tpu as pltpu
from jax.sharding import PartitionSpec as P

penalty = 0.5
BF = jnp.bfloat16
F32 = jnp.float32
lift = 1.3264
gain = 1.3280711361297461


def swap(value, axis, other, first):
    count, width = lax.axis_size(axis), lax.axis_size(other)
    place = (lambda i, j: i * width + j) if (axis, other) == ("gx", "gy") else (lambda i, j: j * count + i)
    lows = list(range(first, count - 1, 2))
    pairs = [(place(low, j), place(low + 1, j)) for low in lows for j in range(width)]
    alone = [i for i in range(count) if i not in lows and i - 1 not in lows]
    pairs += [(place(i, j), place(i, j + 1)) for i in alone for j in range(0, width - 1, 2)]
    return lax.ppermute(value, ("gx", "gy"), pairs + [(high, low) for low, high in pairs])


def even(axis):
    return lax.rem(lax.axis_index(axis), 2) == 0


def arrive(axis, inner_ref, outer_ref, down_ref, up_ref):
    here, last = lax.axis_index(axis), lax.axis_size(axis) - 1
    choose(even(axis), inner_ref, outer_ref, down_ref, here < last)
    choose(even(axis), outer_ref, inner_ref, up_ref, here > 0)


def depart(axis, down_ref, up_ref, inner_ref, outer_ref):
    choose(even(axis), up_ref, down_ref, inner_ref)
    choose(even(axis), down_ref, up_ref, outer_ref)


def choose(condition, yes_ref, no_ref, out_ref, present=None):
    size = min(yes_ref.shape[0], no_ref.shape[0], out_ref.shape[0])
    rows = pl.ds(0, size)
    value = jnp.where(condition, yes_ref[rows, :], no_ref[rows, :])
    out_ref[rows, :] = value if present is None else jnp.where(present, value, jnp.zeros_like(value))
    if out_ref.shape[0] > size:
        rest = pl.ds(size, out_ref.shape[0] - size)
        out_ref[rest, :] = jnp.zeros((out_ref.shape[0] - size, out_ref.shape[1]), out_ref.dtype)


def corner_table():
    gll_points = [-1.0, -math.sqrt(0.2), math.sqrt(0.2), 1.0]
    table = np.zeros((16, 4), np.float64)
    for s in range(4):
        for t in range(4):
            for p in range(2):
                for q in range(2):
                    table[4 * s + t, 2 * p + q] = (
                        (1 + (2 * p - 1) * gll_points[s]) * (1 + (2 * q - 1) * gll_points[t]) / 4
                    )
    return table


def landing(face_slot, high_s, high_t):
    direction, outward = divmod(face_slot, 2)
    if direction == 0:
        return (outward, high_s, high_t)
    if direction == 1:
        return (high_s, outward, high_t)
    return (high_s, high_t, outward)


def gather_table():
    weights = lift * corner_table()
    table = np.zeros((32, 288), np.float64)
    for slot in range(6):
        for s in range(2):
            for t in range(2):
                p, q, r = landing(slot, s, t)
                for c in range(3):
                    cols = slot * 48 + 16 * c + np.arange(16)
                    table[16 * r + 8 * p + 4 * q + c, cols] += weights[:, 2 * s + t]
    return table.astype(ml_dtypes.bfloat16)


def slot_table():
    return np.concatenate(np.split(gather_table(), 6, axis=1), axis=0)


def spread_table(wx, wy, rows):
    weights = lift * corner_table()
    planes = (wx + 1) * rows
    depth = -(-2 * planes // 128) * 128
    table = np.zeros((3, 48, wx, wy, depth), np.float64)
    for d in range(3):
        for x in range(wx):
            for y in range(wy):
                for s in range(2):
                    for t in range(2):
                        p, q, r = landing(2 * d, s, t)
                        for c in range(3):
                            k = r * planes + (x + p) * rows + 4 * (y + q) + c
                            table[d, 16 * c : 16 * c + 16, x, y, k] += weights[:, 2 * s + t]
    return table.reshape(-1, depth).astype(ml_dtypes.bfloat16)


def lanes(shape):
    return lax.broadcasted_iota(jnp.int32, shape, len(shape) - 1)


def z_next(value):
    last = value.shape[-1] - 1
    return jnp.where(lanes(value.shape) < last, pltpu.roll(value, last, value.ndim - 1), 0.0)


def z_prev(value):
    return jnp.where(lanes(value.shape) > 0, pltpu.roll(value, 1, value.ndim - 1), 0.0)


def dot(left, right):
    return jnp.dot(left, right, preferred_element_type=F32)


def wide(parts):
    return jnp.concatenate(parts, axis=1)


def tall(parts):
    return jnp.concatenate(parts, axis=0)


def hex_batch(slots, scales, s_map, f_map):
    z = slots[0][0].shape[1]
    element = tall([wide([hexa[s] for hexa in slots]) for s in range(6)])
    interior = dot(s_map, element).astype(BF)
    flux = dot(f_map, interior) + penalty * element.astype(F32)
    return [
        [flux[48 * s : 48 * s + 48, z * h : z * h + z] * scales[h][s] for s in range(6)]
        for h in range(len(slots))
    ]


def corner_batch(blocks, left_out, gather):
    z = blocks[0][0].shape[1]
    nothing = jnp.zeros((48, z), BF)
    right = tall(
        [
            wide([nothing if s in left_out[h] else blocks[h][s].astype(BF) for h in range(len(blocks))])
            for s in range(6)
        ]
    )
    return [dot(gather, right)[:, z * h : z * h + z] for h in range(len(blocks))]


def slot_corners(traces, parts_ref, slot):
    z = traces[0].shape[1]
    rows = dot(parts_ref[pl.ds(32 * slot, 32), :], wide([trace.astype(BF) for trace in traces]))
    return [rows[:, z * h : z * h + z] for h in range(len(traces))]


def settle(rows, p):
    return rows[8 * p : 8 * p + 8] + z_prev(rows[16 + 8 * p : 24 + 8 * p])


def scaled_corners(delta, scales):
    terms = [delta[32 * s : 32 * s + 32] * scales[s] for s in range(6) if scales[s] is not None]
    return sum(terms[1:], terms[0])


def level_visc(code, visc_ref):
    visc = jnp.zeros(code.shape, F32)
    for level in range(visc_ref.shape[0]):
        visc = visc + jnp.where(code == F32(level + 1), visc_ref[pl.ds(level, 1), :], F32(0.0))
    return visc


def merge(even, odd):
    odd = tall(odd)
    return tall(even) + pltpu.roll(odd, odd.shape[0] - 4, 0)


def first_kernel(
    wx, wy, visc_hbm, t_hbm, dir_hbm, cls_hbm, diag_hbm, st_hbm, f_hbm, g_hbm, parts_hbm,
    l_ref, kp_ref, visc_ref, diag_ref, s_ref, st_ref, f_ref, g_ref, parts_ref, c_ref, v_ref, v1_ref, v3_ref,
    inner_ref, outer_ref, down_ref, up_ref, t_ref, dir_ref, cls_ref, nat, levels, sems,
):
    cells = wx * wy
    pairs = [
        (t_hbm, t_ref), (dir_hbm, dir_ref), (cls_hbm, cls_ref), (diag_hbm, diag_ref),
        (st_hbm, st_ref), (f_hbm, f_ref), (g_hbm, g_ref), (parts_hbm, parts_ref),
        (visc_hbm, levels),
    ]
    copies = [pltpu.make_async_copy(a, b, sems.at[i]) for i, (a, b) in enumerate(pairs)]
    for copy in copies:
        copy.start()
    copies[4].wait()
    s_ref[...] = st_ref[...].T
    for i in (8, 1, 2, 3, 0):
        copies[i].wait()
    z = t_ref.shape[2]
    for level in range(visc_ref.shape[0]):
        visc_ref[pl.ds(level, 1), :] = jnp.full((1, z), levels[level], F32)
    code = cls_ref[...].astype(F32) + 1.0
    kp_ref[4] = level_visc(code, visc_ref)
    kp_ref[5] = code
    for d in range(3):
        keep = (1 - dir_ref[d]).astype(F32)
        kp_ref[d] = keep
        masked = t_ref[d].astype(F32).reshape(48, cells, z) * keep[None]
        nat[...] = masked.reshape(48 * cells, z)
        for col in range(cells):
            part = nat[pl.ds(col, 48, stride=cells), :]
            l_ref[d, col] = part.astype(BF)
            if d == 2:
                l_ref[3, col] = z_next(part).astype(BF)
    kp_ref[3] = z_next(kp_ref[2])
    for i in (5, 6, 7):
        copies[i].wait()
    row = lambda i, col: kp_ref[i, pl.ds(col, 1), :]
    where = [(x, 0) for x in range(wx)] + [(x, wy - 1) for x in range(wx)]
    blocks, left_out = known_hexes(wx, wy, where, l_ref, kp_ref, s_ref, f_ref, c_ref)
    corners = corner_batch(blocks, left_out, g_ref[...])
    lone = slot_corners([blocks[wx - 1][1], blocks[2 * wx - 1][1]], parts_ref, 1)
    for h in range(2):
        v1_ref[h, 0:8] = lone[h][8:16]
        v1_ref[h, 8:16] = lone[h][24:32]
    for x, rows in enumerate(slot_corners([blocks[wx + x][3] for x in range(wx)], parts_ref, 3)):
        v3_ref[x] = rows
    sums = [line_sums(corners[:wx]), line_sums(corners[wx:])]
    for side in range(2):
        for i in range(wx + 1):
            v_ref[side, i] = sums[side][i]
    corner = (wx - 1) * wy
    top = wy - 1
    for x in range(wx):
        down_ref[pl.ds(48 * x, 48), :] = l_ref[1, x * wy]
        up_ref[pl.ds(48 * x, 48), :] = blocks[wx + x][3].astype(BF)
    down_ref[pl.ds(48 * wx, 48), :] = l_ref[0, 0]
    up_ref[pl.ds(48 * wx, 48), :] = l_ref[0, top]
    place = lax.broadcasted_iota(jnp.int32, (8, z), 0)
    rim = []
    for i in range(wx):
        diag = diag_ref[pl.ds(i * wy, 1), :]
        high = diag.astype(BF).astype(F32)
        rim.append(jnp.where(place == 4, high, jnp.where(place == 5, diag - high, sums[0][i])))
    rim += [sums[0][wx], v1_ref[0]]
    rim += [row(1, x * wy) for x in range(wx)] + [row(0, 0), row(5, corner), row(0, corner), row(2, corner)]
    put_tail(down_ref, 48 * wx + 48, rim)
    rim = [sums[1][i] for i in range(wx + 1)] + [v1_ref[1]]
    for kind in (5, 0, 2):
        rim += [row(kind, x * wy + top) for x in range(wx)]
    put_tail(up_ref, 48 * wx + 48, rim)
    depart("gy", down_ref, up_ref, inner_ref, outer_ref)


def tail_rows(count):
    return -(-count // 16) * 16


def put_tail(ref, start, rows):
    count = sum(part.shape[0] for part in rows)
    full = ref.shape[0] - start
    if full > count:
        rows = rows + [jnp.zeros((full - count, rows[0].shape[1]), F32)]
    ref[pl.ds(start, full), :] = tall(rows).astype(BF)


def tail_misc(ref, wx):
    start = 48 * wx + 48
    return ref[pl.ds(start, ref.shape[0] - start), :].astype(F32)[8 * (wx + 1) + 16 :]


def line_sums(corners):
    width = len(corners)
    low = [settle(rows, 0) for rows in corners]
    high = [settle(rows, 1) for rows in corners]
    return [low[0]] + [low[x] + high[x - 1] for x in range(1, width)] + [high[-1]]


def known_hexes(wx, wy, where, l_ref, kp_ref, s_ref, f_ref, c_ref):
    z = l_ref.shape[3]
    nothing = jnp.zeros((48, z), BF)
    row = lambda i, col: kp_ref[i, pl.ds(col, 1), :]
    slots, scales, left_out = [], [], []
    for x, y in where:
        here = x * wy + y
        visc = row(4, here)
        last_x, last_y = x == wx - 1, y == wy - 1
        slots.append(
            [
                l_ref[0, here], nothing if last_x else l_ref[0, here + wy],
                l_ref[1, here], nothing if last_y else l_ref[1, here + 1],
                l_ref[2, here], l_ref[3, here],
            ]
        )
        scales.append(
            [
                visc * row(0, here), visc if last_x else visc * row(0, here + wy),
                visc * row(1, here), visc if last_y else visc * row(1, here + 1),
                visc * row(2, here), visc * row(3, here),
            ]
        )
        left_out.append(([1] if last_x else []) + ([3] if last_y else []))
    blocks = hex_batch(slots, scales, s_ref[...], f_ref[...])
    for h in range(len(where)):
        for s in range(6):
            c_ref[s, h] = blocks[h][s]
    return blocks, left_out


def middle_kernel(
    wx, wy, l_ref, kp_ref, s_ref, st_ref, f_ref, g_ref, parts_ref,
    c_ref, v_ref, v1_ref, mx_ref, my_ref, own_ref,
):
    z = l_ref.shape[3]
    for slot, ref in ((1, mx_ref), (3, my_ref)):
        flux = lax.dot_general(
            f_ref[...], st_ref[pl.ds(48 * slot, 48), :], (((1,), (1,)), ((), ())),
            preferred_element_type=F32,
        )
        ref[pl.ds(0, 288), :] = flux.astype(BF)
        eye = lax.broadcasted_iota(jnp.int32, (48, 48), 0) == lax.broadcasted_iota(jnp.int32, (48, 48), 1)
        for s in range(6):
            block = flux[48 * s : 48 * s + 48]
            if s == slot:
                block = block + jnp.where(eye, F32(penalty), F32(0.0))
            ref[pl.ds(288 + 32 * s, 32), :] = dot(parts_ref[pl.ds(32 * s, 32), :], block.astype(BF)).astype(BF)
    own_ref[...] = dot(tall([my_ref[pl.ds(144, 48), :], my_ref[pl.ds(288, 192), :]]), wide([l_ref[1, x * wy] for x in range(wx)]))
    where = [(x, y) for y in range(1, wy - 1) for x in range(wx)]
    blocks, left_out = known_hexes(wx, wy, where, l_ref, kp_ref, s_ref, f_ref, c_ref)
    corners = corner_batch(blocks, left_out, g_ref[...])
    lone = slot_corners([blocks[wx * y + wx - 1][1] for y in range(wy - 2)], parts_ref, 1)
    for y in range(wy - 2):
        v1_ref[y, 0:8] = lone[y][8:16]
        v1_ref[y, 8:16] = lone[y][24:32]
        for i, rows in enumerate(line_sums(corners[wx * y : wx * y + wx])):
            v_ref[y, i] = rows


def after_y(wx, wy, xs, visc_ref, l_ref, kp_ref, parts_ref, my_ref, own_ref, v3_ref, down_ref, up_ref):
    z = l_ref.shape[3]
    misc_d = tail_misc(down_ref, wx)
    misc_u = tail_misc(up_ref, wx)
    row = lambda i, col: kp_ref[i, pl.ds(col, 1), :]
    delta = dot(my_ref[...], wide([down_ref[pl.ds(48 * x, 48), :] for x in xs]))
    arrived = [up_ref[pl.ds(48 * x, 48), :].astype(F32) for x in xs]
    arrived_corners = slot_corners(arrived, parts_ref, 3)
    results = []
    for n, x in enumerate(xs):
        here = x * wy + wy - 1
        last = x == wx - 1
        part = delta[:, z * n : z * n + z]
        visc = row(4, here)
        scales = [
            visc * row(0, here), visc if last else visc * row(0, here + wy), visc * row(1, here),
            visc * misc_d[x : x + 1], visc * row(2, here), visc * row(3, here),
        ]
        flux = [part[48 * s : 48 * s + 48] * scales[s] for s in range(6)]
        used = [None if (s == 1 and last) else scales[s] for s in range(6)]
        top = scaled_corners(part[288:480], used) + v3_ref[x] * misc_d[x : x + 1]
        top_one = part[320:352] * visc
        here = x * wy
        visc = level_visc(misc_u[x : x + 1], visc_ref)
        flag = row(1, here)
        own = own_ref[:, pl.ds(z * x, z)]
        keep_z = misc_u[2 * wx + x : 2 * wx + x + 1]
        scales = [
            visc * misc_u[wx + x : wx + x + 1], None if last else visc * misc_u[wx + x + 1 : wx + x + 2],
            None, visc * flag, visc * keep_z, visc * z_next(keep_z),
        ]
        low = scaled_corners(own[48:240], scales) + arrived_corners[n] * flag
        low_one = own[80:112] * visc
        face = (arrived[n] + visc * (own[0:48] + penalty * l_ref[1, here].astype(F32))) * flag
        results.append((flux, top, top_one, low, low_one, face))
    return results


def turn_kernel(
    wx, wy, visc_ref, l_ref, kp_ref, diag_ref, parts_ref, my_ref, own_ref, c1_ref, c2_ref, va_ref, vb_ref,
    v1a_ref, v1b_ref, v3_ref, inner_in, outer_in,
    c3_ref, vt_ref, vl_ref, v1_ref, face_ref, yd_ref, yu_ref, inner_ref, outer_ref, down_ref, up_ref,
):
    z = l_ref.shape[3]
    arrive("gy", inner_in, outer_in, yd_ref, yu_ref)
    xs = (0, wx - 1)
    results = after_y(wx, wy, xs, visc_ref, l_ref, kp_ref, parts_ref, my_ref, own_ref, v3_ref, yd_ref, yu_ref)
    row = lambda i, col: kp_ref[i, pl.ds(col, 1), :]
    tail = 48 * wx + 48
    rim_d = yd_ref[pl.ds(tail, yd_ref.shape[0] - tail), :].astype(F32)
    rim_u = yu_ref[pl.ds(tail, yu_ref.shape[0] - tail), :].astype(F32)
    ones = 8 * (wx + 1)
    base = ones + 16
    for n, (flux, top, top_one, low, low_one, face) in enumerate(results):
        for s in range(6):
            c3_ref[n, s] = flux[s]
        face_ref[n] = face
        for p in range(2):
            vt_ref[n, p] = settle(top, p)
            vl_ref[n, p] = settle(low, p)
    flux, top, top_one, low, low_one, face = results[1]
    mine = rim_u[ones : ones + 16] + tall([low_one[8:16], low_one[24:32]])
    v1_ref[0] = mine
    v1_ref[1] = v1a_ref[0]
    for y in range(wy - 2):
        v1_ref[2 + y] = v1b_ref[y]
    v1_ref[wy] = v1a_ref[1] + tall([top_one[8:16], top_one[24:32]])
    v1_ref[wy + 1] = rim_d[ones : ones + 16]

    def plane(i, n, p):
        lines = [rim_u[8 * i : 8 * i + 8] + vl_ref[n, p], va_ref[0, i]]
        lines += [vb_ref[y, i] for y in range(wy - 2)]
        lines += [va_ref[1, i] + vt_ref[n, p], rim_d[8 * i : 8 * i + 8]]
        return merge(lines[1::2], lines[0::2])

    down_ref[pl.ds(0, 48), :] = yu_ref[pl.ds(48 * wx, 48), :]
    for y in range(wy):
        down_ref[pl.ds(48 + 48 * y, 48), :] = l_ref[0, y]
    down_ref[pl.ds(48 * (wy + 1), 48), :] = yd_ref[pl.ds(48 * wx, 48), :]
    diag = [jnp.broadcast_to(diag_ref[pl.ds(y, 1), :], (4, z)) for y in range(wy)]
    high = [part.astype(BF).astype(F32) for part in diag]
    low_bits = [a - b for a, b in zip(diag, high)]
    high += [jnp.broadcast_to(rim_d[4:5], (4, z)), jnp.zeros((4, z), F32)]
    low_bits += [jnp.broadcast_to(rim_d[5:6], (4, z)), jnp.zeros((4, z), F32)]
    rim = [plane(0, 0, 0)] + high + low_bits
    rim += [rim_u[base + wx : base + wx + 1], kp_ref[0, 0:wy], rim_d[base + wx : base + wx + 1]]
    put_tail(down_ref, 48 * (wy + 2), rim)
    corner = (wx - 1) * wy
    up_ref[pl.ds(0, 48), :] = c1_ref[1, wx - 1].astype(BF)
    for y in range(1, wy - 1):
        up_ref[pl.ds(48 * y, 48), :] = c2_ref[1, wx * (y - 1) + wx - 1].astype(BF)
    up_ref[pl.ds(48 * (wy - 1), 48), :] = (c1_ref[1, 2 * wx - 1] + flux[1]).astype(BF)
    last = pl.ds(corner, wy)
    rim = [plane(wx, 1, 1), mine, rim_d[ones : ones + 16]]
    rim += [rim_u[base + wx - 1 : base + wx], kp_ref[5, last], rim_d[base + wx + 1 : base + wx + 2]]
    rim += [rim_u[base + 3 * wx - 1 : base + 3 * wx], kp_ref[2, last], rim_d[base + wx + 3 : base + wx + 4]]
    rim += [kp_ref[1, last], rim_d[base + wx - 1 : base + wx]]
    put_tail(up_ref, 48 * wy, rim)
    depart("gx", down_ref, up_ref, inner_ref, outer_ref)


def assemble_kernel(
    wx, wy, visc_ref, l_ref, kp_ref, diag_ref, parts_ref, mx_ref, my_ref, own_ref, c1_ref, c2_ref, c3_ref,
    va_ref, vb_ref, v3_ref, vt_ref, vl_ref, face_ref, yd_ref, yu_ref,
    r_ref, v_ref, inv_ref, ownx_ref, mid,
):
    z = l_ref.shape[3]
    cells = wx * wy
    xs = tuple(range(1, wx - 1))
    results = after_y(wx, wy, xs, visc_ref, l_ref, kp_ref, parts_ref, my_ref, own_ref, v3_ref, yd_ref, yu_ref)
    for n, part in enumerate(results):
        for s in range(6):
            mid[n, s] = part[0][s]
    traces = [yu_ref[pl.ds(48 * wx, 48), :]] + [l_ref[0, y] for y in range(wy)] + [yd_ref[pl.ds(48 * wx, 48), :]]
    ownx_ref[...] = dot(tall([mx_ref[pl.ds(48, 48), :], mx_ref[pl.ds(288, 192), :]]), wide(traces))

    def contrib(slot, x, y):
        if 0 < y < wy - 1:
            return c2_ref[slot, wx * (y - 1) + x]
        if y == 0:
            return c1_ref[slot, x]
        extra = mid[x - 1, slot] if 0 < x < wx - 1 else c3_ref[0 if x == 0 else 1, slot]
        return c1_ref[slot, wx + x] + extra

    for x in range(wx):
        for y in range(wy):
            col = pl.ds(x * wy + y, 48, stride=cells)
            if x:
                r_ref[0, col, :] = contrib(0, x, y) + contrib(1, x - 1, y)
            else:
                r_ref[0, col, :] = contrib(0, x, y)
            if y:
                behind = contrib(3, x, y - 1)
            elif 0 < x < wx - 1:
                behind = results[x - 1][5]
            else:
                behind = face_ref[0 if x == 0 else 1]
            r_ref[1, col, :] = contrib(2, x, y) + behind
            r_ref[2, col, :] = contrib(4, x, y) + z_prev(contrib(5, x, y))
    tail = 48 * wx + 48
    rim_d = yd_ref[pl.ds(tail, yd_ref.shape[0] - tail), :].astype(F32)
    rim_u = yu_ref[pl.ds(tail, yu_ref.shape[0] - tail), :].astype(F32)

    def brought(which, i):
        held = vt_ref if which == 1 else vl_ref
        terms = []
        for x, p in ((i, 0), (i - 1, 1)):
            if x in (0, wx - 1):
                terms.append(held[0 if x == 0 else 1, p])
            elif 0 < x < wx - 1:
                terms.append(settle(results[x - 1][which], p))
        return sum(terms[1:], terms[0])

    for i in range(wx + 1):
        lines = [rim_u[8 * i : 8 * i + 8] + brought(3, i), va_ref[0, i]]
        lines += [vb_ref[y, i] for y in range(wy - 2)]
        lines += [va_ref[1, i] + brought(1, i), rim_d[8 * i : 8 * i + 8]]
        v_ref[i] = merge(lines[1::2], lines[0::2])
        if i < wx:
            parts = [jnp.broadcast_to(diag_ref[pl.ds(i * wy + y, 1), :], (4, z)) for y in range(wy)]
            edge = rim_d[8 * i + 4 : 8 * i + 5] + rim_d[8 * i + 5 : 8 * i + 6]
            parts += [jnp.broadcast_to(edge, (4, z)), jnp.zeros((4, z), F32)]
            inv_ref[i] = reciprocal(tall(parts))


def reciprocal(diag):
    present = diag > 0.0
    return jnp.where(present, (1.0 / (gain * gain)) / jnp.where(present, diag, 1.0), 0.0)


def final_kernel(
    wx, wy, visc_ref, l_ref, kp_ref, parts_ref, mx_ref, ownx_ref, r_ref, v_ref, inv_ref, v1_ref,
    yd_ref, yu_ref, inner_in, outer_in, p_ref, out_ref, fix, xd_ref, xu_ref,
):
    arrive("gx", inner_in, outer_in, xd_ref, xu_ref)
    cells, z = wx * wy, l_ref.shape[3]
    rows = v_ref.shape[1]
    planes = (wx + 1) * rows
    row = lambda i, col: kp_ref[i, pl.ds(col, 1), :]
    delta = dot(mx_ref[...], wide([xd_ref[pl.ds(48 * j, 48), :] for j in range(wy + 2)]))
    rim_x = xd_ref[pl.ds(48 * (wy + 2), xd_ref.shape[0] - 48 * (wy + 2)), :].astype(F32)
    rim_l = xu_ref[pl.ds(48 * wy, xu_ref.shape[0] - 48 * wy), :].astype(F32)
    misc_d = tail_misc(yd_ref, wx)
    misc_u = tail_misc(yu_ref, wx)
    flags_high = rim_x[3 * rows : 3 * rows + wy + 2]
    corner = (wx - 1) * wy
    arrived = [xu_ref[pl.ds(48 * y, 48), :].astype(F32) for y in range(wy)]
    arrived_corners = slot_corners(arrived, parts_ref, 1)
    codes = rim_l[rows + 32 : rows + 32 + wy + 2]
    keep_z = rim_l[rows + 32 + wy + 2 : rows + 32 + 2 * (wy + 2)]
    keep_y = rim_l[rows + 32 + 2 * (wy + 2) : rows + 32 + 3 * (wy + 2) - 1]
    low_visc = level_visc(codes, visc_ref)
    low_keep_z = z_next(keep_z)
    lines = [[], [], []]
    high_flux = []
    for j in range(-1, wy + 1):
        n = j + 1
        part = delta[:, z * n : z * n + z]
        flag = flags_high[n : n + 1]
        if j < 0:
            visc = level_visc(misc_u[wx - 1 : wx], visc_ref)
            kz = misc_u[3 * wx - 1 : 3 * wx]
            keeps = [misc_u[2 * wx - 1 : 2 * wx], flag, None, row(1, corner), kz, z_next(kz)]
        elif j < wy:
            here = corner + j
            visc = row(4, here)
            high_y = row(1, here + 1) if j < wy - 1 else misc_d[wx - 1 : wx]
            keeps = [row(0, here), flag, row(1, here), high_y, row(2, here), row(3, here)]
        else:
            visc = level_visc(misc_d[wx + 1 : wx + 2], visc_ref)
            kz = misc_d[wx + 3 : wx + 4]
            keeps = [misc_d[wx + 2 : wx + 3], flag, misc_d[wx - 1 : wx], None, kz, z_next(kz)]
        scales = [None if keep is None else visc * keep for keep in keeps]
        corners = scaled_corners(part[288:480], scales)
        one = v1_ref[n] * flag
        lines[0].append(settle(corners, 0))
        lines[1].append(settle(corners, 1) + one[0:8] + z_prev(one[8:16]))
        high_flux.append([None if k is None else part[48 * s : 48 * s + 48] * k for s, k in enumerate(scales)])
        own = ownx_ref[:, pl.ds(z * n, z)]
        visc = low_visc[n : n + 1]
        flag = misc_u[wx : wx + 1] if j < 0 else misc_d[wx : wx + 1] if j == wy else row(0, j)
        scales = [
            None, visc * flag, None if j < 0 else visc * keep_y[j : j + 1],
            None if j == wy else visc * keep_y[j + 1 : j + 2], visc * keep_z[n : n + 1], visc * low_keep_z[n : n + 1],
        ]
        corners = settle(scaled_corners(own[48:240], scales), 1)
        if 0 <= j < wy:
            lines[2].append(corners + settle(arrived_corners[j] * flag, 1))
            face = (arrived[j] + visc * (own[0:48] + penalty * l_ref[0, j].astype(F32))) * flag
            r_ref[0, pl.ds(j, 48, stride=cells), :] += face
        else:
            at = rows + (0 if j < 0 else 16)
            one = rim_l[at : at + 16] * flag
            lines[2].append(corners + one[0:8] + z_prev(one[8:16]))
    low, before, first = [merge(part[1::2], part[0::2]) for part in lines]
    top = v_ref[wx] + before + rim_x[0:rows]
    values = [(v_ref[0] + first + rim_l[0:rows]) * inv_ref[0]]
    values += [v_ref[i] * inv_ref[i] for i in range(1, wx - 1)]
    values += [(v_ref[wx - 1] + low) * inv_ref[wx - 1]]
    values += [top * reciprocal(rim_x[rows : 2 * rows] + rim_x[2 * rows : 3 * rows])]
    value = tall(values)
    fix[...] = jnp.zeros_like(fix)
    fix[pl.ds(0, planes), :] = value
    fix[pl.ds(planes, planes), :] = z_next(value)
    rhs = fix[...].astype(BF)
    for j in range(wy):
        col = pl.ds(corner + j, 48, stride=cells)
        flux = high_flux[j + 1]
        r_ref[0, col, :] += flux[0]
        r_ref[1, col, :] += flux[2] + high_flux[j][3]
        r_ref[2, col, :] += flux[4] + z_prev(flux[5])
    for d in range(3):
        spread = dot(p_ref[pl.ds(48 * cells * d, 48 * cells), :], rhs)
        spread = spread.reshape(48, cells, z) * kp_ref[d][None]
        out_ref[d] = (r_ref[d] + spread.reshape(48 * cells, z)).astype(BF)


def call(body, args, outs, scratch, flops, hbm=False):
    if hbm:
        args = tuple(pltpu.with_memory_space_constraint(a, pltpu.HBM) for a in args)
    return pl.pallas_call(
        body,
        in_specs=[pl.BlockSpec(memory_space=pltpu.HBM if hbm else pltpu.VMEM)] * len(args),
        out_shape=outs,
        scratch_shapes=scratch,
        cost_estimate=pl.CostEstimate(flops=flops, bytes_accessed=1000000, transcendentals=0),
        compiler_params=pltpu.CompilerParams(vmem_limit_bytes=16 * 1024 * 1024),
    )(*args)


def local(traces, dirichlet, visc_class, viscosity, coarse_diag, solve_map, flux_map):
    wx, wy, z = traces.shape[2:]
    cells = wx * wy
    rows = 8 * (wy // 2 + 1)
    per_hex = 4 * 288 * 256 * z
    gather = jnp.asarray(gather_table())
    parts = jnp.asarray(slot_table())
    spread = jnp.asarray(spread_table(wx, wy, rows))
    vm = pltpu.VMEM
    bind = lambda body: functools.partial(body, wx, wy)
    y_message = vm((48 * wx + 48 + tail_rows(8 * (wx + 1) + 16 + 3 * wx), z), BF)
    y_outer = vm((y_message.shape[0] + 16, z), BF)
    x_message = vm((48 * (wy + 2) + tail_rows(3 * rows + wy + 2), z), BF)
    x_outer = vm((x_message.shape[0] + 16, z), BF)

    (lifted, flags, visc, diag, s_map, s_turned, f_map, gather, parts, c1, va, v1a, v3, inner, outer) = call(
        bind(first_kernel),
        (
            viscosity, traces.reshape(3, 48 * cells, z), dirichlet.reshape(3, cells, z),
            visc_class.reshape(cells, z), coarse_diag.reshape(cells, z), solve_map.T, flux_map, gather, parts,
        ),
        (
            vm((4, cells, 48, z), BF), vm((6, cells, z), F32), vm((viscosity.shape[0], z), F32), vm((cells, z), F32),
            vm(solve_map.shape, BF),
            vm(solve_map.shape[::-1], BF), vm(flux_map.shape, BF), vm(gather.shape, BF), vm(parts.shape, BF),
            vm((6, 2 * wx, 48, z), F32), vm((2, wx + 1, 8, z), F32), vm((2, 16, z), F32), vm((wx, 32, z), F32),
            y_message, y_outer,
        ),
        [
            y_message, y_message,
            vm((3, 48 * cells, z), BF), vm((3, cells, z), jnp.int32), vm((cells, z), jnp.int32),
            vm((48 * cells, z), F32), pltpu.SMEM(viscosity.shape, F32), pltpu.SemaphoreType.DMA((9,)),
        ],
        2 * wx * per_hex, True,
    )
    inner = swap(inner, "gy", "gx", 0)
    outer = swap(outer, "gy", "gx", 1)
    between = wx * (wy - 2)
    c2, vb, v1b, mx, my, own = call(
        bind(middle_kernel),
        (lifted, flags, s_map, s_turned, f_map, gather, parts),
        (
            vm((6, between, 48, z), F32), vm((wy - 2, wx + 1, 8, z), F32), vm((wy - 2, 16, z), F32),
            vm((480, 48), BF), vm((480, 48), BF), vm((240, wx * z), F32),
        ),
        [], between * per_hex,
    )
    c3, vt, vl, v1, face, yd, yu, inner, outer = call(
        bind(turn_kernel),
        (
            visc, lifted, flags, diag, parts, my, own, c1, c2, va, vb, v1a, v1b, v3, inner, outer,
        ),
        (
            vm((2, 6, 48, z), F32), vm((2, 2, 8, z), F32), vm((2, 2, 8, z), F32), vm((wy + 2, 16, z), F32),
            vm((2, 48, z), F32), y_message, y_message, x_message, x_outer,
        ),
        [x_message, x_message], 2 * per_hex,
    )
    inner = swap(inner, "gx", "gy", 0)
    outer = swap(outer, "gx", "gy", 1)
    residual, vs, inverse, ownx = call(
        bind(assemble_kernel),
        (
            visc, lifted, flags, diag, parts, mx, my, own, c1, c2, c3, va, vb, v3, vt, vl, face, yd, yu,
        ),
        (
            vm((3, 48 * cells, z), F32), vm((wx + 1, rows, z), F32), vm((wx, rows, z), F32),
            vm((240, (wy + 2) * z), F32),
        ),
        [vm((wx - 2, 6, 48, z), F32)], 4 * per_hex,
    )
    out = call(
        bind(final_kernel),
        (
            visc, lifted, flags, parts, mx, ownx, residual, vs, inverse, v1, yd, yu, inner, outer, spread,
        ),
        jax.ShapeDtypeStruct((3, 48 * cells, z), BF),
        [vm((spread.shape[1], z), F32), x_message, x_message], 2 * spread.size * z,
    )
    return out.reshape(traces.shape)


def solution(mesh):
    in_specs = (
        P(None, None, "gx", "gy", None),
        P(None, "gx", "gy", None),
        P("gx", "gy", None),
        P(),
        P("gx", "gy", None),
        P(),
        P(),
    )
    out_specs = P(None, None, "gx", "gy", None)
    return jax.shard_map(local, mesh=mesh, in_specs=in_specs, out_specs=out_specs, check_vma=False)
```

```python
import functools
import math

import jax
import jax.numpy as jnp
import ml_dtypes
import numpy as np
from jax import lax
from jax.experimental import pallas as pl
from jax.experimental.pallas import tpu as pltpu
from jax.sharding import PartitionSpec as P

penalty = 0.5
BF = jnp.bfloat16
F32 = jnp.float32
lift = 1.3264
gain = 1.3280711361297461


def swap(value, axis, other, first):
    count, width = lax.axis_size(axis), lax.axis_size(other)
    place = (lambda i, j: i * width + j) if (axis, other) == ("gx", "gy") else (lambda i, j: j * count + i)
    lows = list(range(first, count - 1, 2))
    pairs = [(place(low, j), place(low + 1, j)) for low in lows for j in range(width)]
    alone = [i for i in range(count) if i not in lows and i - 1 not in lows]
    pairs += [(place(i, j), place(i, j + 1)) for i in alone for j in range(0, width - 1, 2)]
    return lax.ppermute(value, ("gx", "gy"), pairs + [(high, low) for low, high in pairs])


def even(axis):
    return lax.rem(lax.axis_index(axis), 2) == 0


def arrive(axis, inner_ref, outer_ref, down_ref, up_ref):
    here, last = lax.axis_index(axis), lax.axis_size(axis) - 1
    choose(even(axis), inner_ref, outer_ref, down_ref, here < last)
    choose(even(axis), outer_ref, inner_ref, up_ref, here > 0)


def depart(axis, down_ref, up_ref, inner_ref, outer_ref):
    choose(even(axis), up_ref, down_ref, inner_ref)
    choose(even(axis), down_ref, up_ref, outer_ref)


def choose(condition, yes_ref, no_ref, out_ref, present=None):
    size = min(yes_ref.shape[0], no_ref.shape[0], out_ref.shape[0])
    rows = pl.ds(0, size)
    value = jnp.where(condition, yes_ref[rows, :], no_ref[rows, :])
    out_ref[rows, :] = value if present is None else jnp.where(present, value, jnp.zeros_like(value))
    if out_ref.shape[0] > size:
        rest = pl.ds(size, out_ref.shape[0] - size)
        out_ref[rest, :] = jnp.zeros((out_ref.shape[0] - size, out_ref.shape[1]), out_ref.dtype)


def corner_table():
    gll_points = [-1.0, -math.sqrt(0.2), math.sqrt(0.2), 1.0]
    table = np.zeros((16, 4), np.float64)
    for s in range(4):
        for t in range(4):
            for p in range(2):
                for q in range(2):
                    table[4 * s + t, 2 * p + q] = (
                        (1 + (2 * p - 1) * gll_points[s]) * (1 + (2 * q - 1) * gll_points[t]) / 4
                    )
    return table


def landing(face_slot, high_s, high_t):
    direction, outward = divmod(face_slot, 2)
    if direction == 0:
        return (outward, high_s, high_t)
    if direction == 1:
        return (high_s, outward, high_t)
    return (high_s, high_t, outward)


def gather_table():
    weights = lift * corner_table()
    table = np.zeros((32, 288), np.float64)
    for slot in range(6):
        for s in range(2):
            for t in range(2):
                p, q, r = landing(slot, s, t)
                for c in range(3):
                    cols = slot * 48 + 16 * c + np.arange(16)
                    table[16 * r + 8 * p + 4 * q + c, cols] += weights[:, 2 * s + t]
    return table.astype(ml_dtypes.bfloat16)


def slot_table():
    return np.concatenate(np.split(gather_table(), 6, axis=1), axis=0)


def spread_table(wy, rows):
    weights = lift * corner_table()
    table = np.zeros((3, 48, 2, wy, 6 * rows), np.float64)
    for d in range(3):
        for x in range(2):
            for y in range(wy):
                for s in range(2):
                    for t in range(2):
                        p, q, r = landing(2 * d, s, t)
                        for c in range(3):
                            k = (3 * r + x + p) * rows + 4 * (y + q) + c
                            table[d, 16 * c : 16 * c + 16, x, y, k] += weights[:, 2 * s + t]
    return table.reshape(-1, 6 * rows).astype(ml_dtypes.bfloat16)


def lanes(shape):
    return lax.broadcasted_iota(jnp.int32, shape, len(shape) - 1)


def z_next(value):
    last = value.shape[-1] - 1
    return jnp.where(lanes(value.shape) < last, pltpu.roll(value, last, value.ndim - 1), 0.0)


def z_prev(value):
    return jnp.where(lanes(value.shape) > 0, pltpu.roll(value, 1, value.ndim - 1), 0.0)


def dot(left, right):
    return jnp.dot(left, right, preferred_element_type=F32)


def wide(parts):
    return jnp.concatenate(parts, axis=1)


def tall(parts):
    return jnp.concatenate(parts, axis=0)


def hex_batch(slots, scales, s_map, f_map):
    z = slots[0][0].shape[1]
    element = tall([wide([hexa[s] for hexa in slots]) for s in range(6)])
    interior = dot(s_map, element).astype(BF)
    flux = dot(f_map, interior) + penalty * element.astype(F32)
    return [
        [flux[48 * s : 48 * s + 48, z * h : z * h + z] * scales[h][s] for s in range(6)]
        for h in range(len(slots))
    ]


def corner_batch(blocks, left_out, gather):
    z = blocks[0][0].shape[1]
    nothing = jnp.zeros((48, z), BF)
    right = tall(
        [
            wide([nothing if s in left_out[h] else blocks[h][s].astype(BF) for h in range(len(blocks))])
            for s in range(6)
        ]
    )
    return [dot(gather, right)[:, z * h : z * h + z] for h in range(len(blocks))]


def slot_corners(traces, parts_ref, slot):
    z = traces[0].shape[1]
    rows = dot(parts_ref[pl.ds(32 * slot, 32), :], wide([trace.astype(BF) for trace in traces]))
    return [rows[:, z * h : z * h + z] for h in range(len(traces))]


def settle(rows, p):
    return rows[8 * p : 8 * p + 8] + z_prev(rows[16 + 8 * p : 24 + 8 * p])


def scaled_corners(delta, scales):
    terms = [delta[32 * s : 32 * s + 32] * scales[s] for s in range(6) if scales[s] is not None]
    return sum(terms[1:], terms[0])


def level_visc(code, visc_ref):
    visc = jnp.zeros(code.shape, F32)
    for level in range(visc_ref.shape[0]):
        visc = visc + jnp.where(code == F32(level + 1), visc_ref[pl.ds(level, 1), :], F32(0.0))
    return visc


def merge(even, odd):
    odd = tall(odd)
    return tall(even) + pltpu.roll(odd, odd.shape[0] - 4, 0)


def first_kernel(
    wx, wy, visc_hbm, t_hbm, dir_hbm, cls_hbm, diag_hbm, st_hbm, f_hbm, g_hbm, parts_hbm,
    l_ref, kp_ref, visc_ref, diag_ref, s_ref, st_ref, f_ref, g_ref, parts_ref, c_ref, v_ref, v1_ref, v3_ref,
    inner_ref, outer_ref, down_ref, up_ref, t_ref, dir_ref, cls_ref, nat, levels, sems,
):
    cells = wx * wy
    pairs = [
        (t_hbm, t_ref), (dir_hbm, dir_ref), (cls_hbm, cls_ref), (diag_hbm, diag_ref),
        (st_hbm, st_ref), (f_hbm, f_ref), (g_hbm, g_ref), (parts_hbm, parts_ref),
        (visc_hbm, levels),
    ]
    copies = [pltpu.make_async_copy(a, b, sems.at[i]) for i, (a, b) in enumerate(pairs)]
    for copy in copies:
        copy.start()
    copies[4].wait()
    s_ref[...] = st_ref[...].T
    for i in (8, 1, 2, 3, 0):
        copies[i].wait()
    z = t_ref.shape[2]
    for level in range(visc_ref.shape[0]):
        visc_ref[pl.ds(level, 1), :] = jnp.full((1, z), levels[level], F32)
    code = cls_ref[...].astype(F32) + 1.0
    kp_ref[4] = level_visc(code, visc_ref)
    kp_ref[5] = code
    for d in range(3):
        keep = (1 - dir_ref[d]).astype(F32)
        kp_ref[d] = keep
        masked = t_ref[d].astype(F32).reshape(48, cells, z) * keep[None]
        nat[...] = masked.reshape(48 * cells, z)
        for col in range(cells):
            part = nat[pl.ds(col, 48, stride=cells), :]
            l_ref[d, col] = part.astype(BF)
            if d == 2:
                l_ref[3, col] = z_next(part).astype(BF)
    kp_ref[3] = z_next(kp_ref[2])
    for i in (5, 6, 7):
        copies[i].wait()
    row = lambda i, col: kp_ref[i, pl.ds(col, 1), :]
    where = [(x, 0) for x in range(wx)] + [(x, wy - 1) for x in range(wx)]
    blocks, left_out = known_hexes(wx, wy, where, l_ref, kp_ref, s_ref, f_ref, c_ref)
    corners = corner_batch(blocks, left_out, g_ref[...])
    lone = slot_corners([blocks[wx - 1][1], blocks[2 * wx - 1][1]], parts_ref, 1)
    for h in range(2):
        v1_ref[h, 0:8] = lone[h][8:16]
        v1_ref[h, 8:16] = lone[h][24:32]
    for x, rows in enumerate(slot_corners([blocks[wx + x][3] for x in range(wx)], parts_ref, 3)):
        v3_ref[x] = rows
    sums = [line_sums(corners[:wx]), line_sums(corners[wx:])]
    for side in range(2):
        for i in range(wx + 1):
            v_ref[side, i] = sums[side][i]
    corner = (wx - 1) * wy
    top = wy - 1
    for x in range(wx):
        down_ref[pl.ds(48 * x, 48), :] = l_ref[1, x * wy]
        up_ref[pl.ds(48 * x, 48), :] = blocks[wx + x][3].astype(BF)
    down_ref[pl.ds(48 * wx, 48), :] = l_ref[0, 0]
    up_ref[pl.ds(48 * wx, 48), :] = l_ref[0, top]
    flags = [row(1, x * wy) for x in range(wx)] + [row(0, 0), row(5, corner), row(0, corner), row(2, corner)]
    diag = tall([diag_ref[pl.ds(x * wy, 1), :] for x in range(wx)])
    high = diag.astype(BF).astype(F32)
    rim = pack(sums[0], 0) + pack([v1_ref[0, 0:8], v1_ref[0, 8:16]], 0) + flags + [high, diag - high]
    put_tail(down_ref, 48 * wx + 48, rim)
    flags = [row(kind, x * wy + top) for kind in (5, 0, 2) for x in range(wx)]
    rim = pack(sums[1], 1) + pack([v1_ref[1, 0:8], v1_ref[1, 8:16]], 1) + flags
    put_tail(up_ref, 48 * wx + 48, rim)
    depart("gy", down_ref, up_ref, inner_ref, outer_ref)


def tail_rows(count):
    return -(-count // 16) * 16


def put_tail(ref, start, rows):
    count = sum(part.shape[0] for part in rows)
    full = ref.shape[0] - start
    if full > count:
        rows = rows + [jnp.zeros((full - count, rows[0].shape[1]), F32)]
    ref[pl.ds(start, full), :] = tall(rows).astype(BF)


def pack(parts, half):
    place = lax.broadcasted_iota(jnp.int32, parts[0].shape, 0)
    parts = parts + [jnp.zeros_like(parts[0])] * (len(parts) % 2)
    packed = []
    for low, high in zip(parts[0::2], parts[1::2]):
        if half:
            low = pltpu.roll(low, 4, 0)
        else:
            high = pltpu.roll(high, 4, 0)
        packed.append(jnp.where(place < 4, low, high))
    return packed


def unpack(packed, count, half):
    parts = []
    for n in range(count):
        part = packed[8 * (n // 2) : 8 * (n // 2) + 8]
        parts.append(part if n % 2 == half else pltpu.roll(part, 4, 0))
    return parts


def read_tail(ref, wx, half):
    start = 48 * wx + 48
    rows = ref[pl.ds(start, ref.shape[0] - start), :].astype(F32)
    size = 8 * ((wx + 2) // 2)
    return unpack(rows, wx + 1, half), unpack(rows[size : size + 8], 2, half), rows[size + 8 :]


def line_sums(corners):
    width = len(corners)
    low = [settle(rows, 0) for rows in corners]
    high = [settle(rows, 1) for rows in corners]
    return [low[0]] + [low[x] + high[x - 1] for x in range(1, width)] + [high[-1]]


def known_hexes(wx, wy, where, l_ref, kp_ref, s_ref, f_ref, c_ref):
    z = l_ref.shape[3]
    nothing = jnp.zeros((48, z), BF)
    row = lambda i, col: kp_ref[i, pl.ds(col, 1), :]
    slots, scales, left_out = [], [], []
    for x, y in where:
        here = x * wy + y
        visc = row(4, here)
        last_x, last_y = x == wx - 1, y == wy - 1
        slots.append(
            [
                l_ref[0, here], nothing if last_x else l_ref[0, here + wy],
                l_ref[1, here], nothing if last_y else l_ref[1, here + 1],
                l_ref[2, here], l_ref[3, here],
            ]
        )
        scales.append(
            [
                visc * row(0, here), visc if last_x else visc * row(0, here + wy),
                visc * row(1, here), visc if last_y else visc * row(1, here + 1),
                visc * row(2, here), visc * row(3, here),
            ]
        )
        left_out.append(([1] if last_x else []) + ([3] if last_y else []))
    blocks = hex_batch(slots, scales, s_ref[...], f_ref[...])
    for h in range(len(where)):
        for s in range(6):
            c_ref[s, h] = blocks[h][s]
    return blocks, left_out


def middle_kernel(
    wx, wy, l_ref, kp_ref, s_ref, st_ref, f_ref, g_ref, parts_ref,
    c_ref, v_ref, v1_ref, mx_ref, my_ref, own_ref,
):
    z = l_ref.shape[3]
    for slot, ref in ((1, mx_ref), (3, my_ref)):
        flux = lax.dot_general(
            f_ref[...], st_ref[pl.ds(48 * slot, 48), :], (((1,), (1,)), ((), ())),
            preferred_element_type=F32,
        )
        ref[pl.ds(0, 288), :] = flux.astype(BF)
        eye = lax.broadcasted_iota(jnp.int32, (48, 48), 0) == lax.broadcasted_iota(jnp.int32, (48, 48), 1)
        for s in range(6):
            block = flux[48 * s : 48 * s + 48]
            if s == slot:
                block = block + jnp.where(eye, F32(penalty), F32(0.0))
            ref[pl.ds(288 + 32 * s, 32), :] = dot(parts_ref[pl.ds(32 * s, 32), :], block.astype(BF)).astype(BF)
    own_ref[...] = dot(tall([my_ref[pl.ds(144, 48), :], my_ref[pl.ds(288, 192), :]]), wide([l_ref[1, x * wy] for x in range(wx)]))
    where = [(x, y) for y in range(1, wy - 1) for x in range(wx)]
    blocks, left_out = known_hexes(wx, wy, where, l_ref, kp_ref, s_ref, f_ref, c_ref)
    corners = corner_batch(blocks, left_out, g_ref[...])
    lone = slot_corners([blocks[wx * y + wx - 1][1] for y in range(wy - 2)], parts_ref, 1)
    for y in range(wy - 2):
        v1_ref[y, 0:8] = lone[y][8:16]
        v1_ref[y, 8:16] = lone[y][24:32]
        for i, rows in enumerate(line_sums(corners[wx * y : wx * y + wx])):
            v_ref[y, i] = rows


def after_y(wx, wy, xs, visc_ref, l_ref, kp_ref, parts_ref, my_ref, own_ref, v3_ref, down_ref, up_ref):
    z = l_ref.shape[3]
    misc_d = read_tail(down_ref, wx, 0)[2]
    misc_u = read_tail(up_ref, wx, 1)[2]
    row = lambda i, col: kp_ref[i, pl.ds(col, 1), :]
    delta = dot(my_ref[...], wide([down_ref[pl.ds(48 * x, 48), :] for x in xs]))
    arrived = [up_ref[pl.ds(48 * x, 48), :].astype(F32) for x in xs]
    arrived_corners = slot_corners(arrived, parts_ref, 3)
    results = []
    for n, x in enumerate(xs):
        here = x * wy + wy - 1
        last = x == wx - 1
        part = delta[:, z * n : z * n + z]
        visc = row(4, here)
        scales = [
            visc * row(0, here), visc if last else visc * row(0, here + wy), visc * row(1, here),
            visc * misc_d[x : x + 1], visc * row(2, here), visc * row(3, here),
        ]
        flux = [part[48 * s : 48 * s + 48] * scales[s] for s in range(6)]
        used = [None if (s == 1 and last) else scales[s] for s in range(6)]
        top = scaled_corners(part[288:480], used) + v3_ref[x] * misc_d[x : x + 1]
        top_one = part[320:352] * visc
        here = x * wy
        visc = level_visc(misc_u[x : x + 1], visc_ref)
        flag = row(1, here)
        own = own_ref[:, pl.ds(z * x, z)]
        keep_z = misc_u[2 * wx + x : 2 * wx + x + 1]
        scales = [
            visc * misc_u[wx + x : wx + x + 1], None if last else visc * misc_u[wx + x + 1 : wx + x + 2],
            None, visc * flag, visc * keep_z, visc * z_next(keep_z),
        ]
        low = scaled_corners(own[48:240], scales) + arrived_corners[n] * flag
        low_one = own[80:112] * visc
        face = (arrived[n] + visc * (own[0:48] + penalty * l_ref[1, here].astype(F32))) * flag
        results.append((flux, top, top_one, low, low_one, face))
    return results


def turn_kernel(
    wx, wy, visc_ref, l_ref, kp_ref, diag_ref, parts_ref, my_ref, own_ref, c1_ref, c2_ref, va_ref, vb_ref,
    v1a_ref, v1b_ref, v3_ref, inner_in, outer_in,
    c3_ref, vt_ref, vl_ref, v1_ref, face_ref, yd_ref, yu_ref, inner_ref, outer_ref, down_ref, up_ref,
):
    z = l_ref.shape[3]
    arrive("gy", inner_in, outer_in, yd_ref, yu_ref)
    xs = (0, wx - 1)
    results = after_y(wx, wy, xs, visc_ref, l_ref, kp_ref, parts_ref, my_ref, own_ref, v3_ref, yd_ref, yu_ref)
    row = lambda i, col: kp_ref[i, pl.ds(col, 1), :]
    sums_d, one_d, misc_d = read_tail(yd_ref, wx, 0)
    sums_u, one_u, misc_u = read_tail(yu_ref, wx, 1)
    edge_high, edge_low = misc_d[wx + 4 : 2 * wx + 4], misc_d[2 * wx + 4 : 3 * wx + 4]
    for n, (flux, top, top_one, low, low_one, face) in enumerate(results):
        for s in range(6):
            c3_ref[n, s] = flux[s]
        face_ref[n] = face
        for p in range(2):
            vt_ref[n, p] = settle(top, p)
            vl_ref[n, p] = settle(low, p)
    flux, top, top_one, low, low_one, face = results[1]
    mine = tall([one_u[0] + low_one[8:16], one_u[1] + low_one[24:32]])
    v1_ref[0] = mine
    v1_ref[1] = v1a_ref[0]
    for y in range(wy - 2):
        v1_ref[2 + y] = v1b_ref[y]
    v1_ref[wy] = v1a_ref[1] + tall([top_one[8:16], top_one[24:32]])
    v1_ref[wy + 1] = tall(one_d)

    def plane(i, n, p):
        lines = [sums_u[i] + vl_ref[n, p], va_ref[0, i]]
        lines += [vb_ref[y, i] for y in range(wy - 2)]
        lines += [va_ref[1, i] + vt_ref[n, p], sums_d[i]]
        return merge(lines[1::2], lines[0::2])

    down_ref[pl.ds(0, 48), :] = yu_ref[pl.ds(48 * wx, 48), :]
    for y in range(wy):
        down_ref[pl.ds(48 + 48 * y, 48), :] = l_ref[0, y]
    down_ref[pl.ds(48 * (wy + 1), 48), :] = yd_ref[pl.ds(48 * wx, 48), :]
    diag = diag_ref[pl.ds(0, wy), :]
    high = diag.astype(BF).astype(F32)
    rim = [plane(0, 0, 0), high, edge_high[0:1], diag - high, edge_low[0:1]]
    rim += [misc_u[wx : wx + 1], kp_ref[0, 0:wy], misc_d[wx : wx + 1]]
    put_tail(down_ref, 48 * (wy + 2), rim)
    corner = (wx - 1) * wy
    up_ref[pl.ds(0, 48), :] = c1_ref[1, wx - 1].astype(BF)
    for y in range(1, wy - 1):
        up_ref[pl.ds(48 * y, 48), :] = c2_ref[1, wx * (y - 1) + wx - 1].astype(BF)
    up_ref[pl.ds(48 * (wy - 1), 48), :] = (c1_ref[1, 2 * wx - 1] + flux[1]).astype(BF)
    last = pl.ds(corner, wy)
    rim = [plane(wx, 1, 1), mine, *one_d]
    rim += [misc_u[wx - 1 : wx], kp_ref[5, last], misc_d[wx + 1 : wx + 2]]
    rim += [misc_u[3 * wx - 1 : 3 * wx], kp_ref[2, last], misc_d[wx + 3 : wx + 4]]
    rim += [kp_ref[1, last], misc_d[wx - 1 : wx]]
    put_tail(up_ref, 48 * wy, rim)
    depart("gx", down_ref, up_ref, inner_ref, outer_ref)


def assemble_kernel(
    wx, wy, visc_ref, l_ref, kp_ref, diag_ref, parts_ref, mx_ref, my_ref, own_ref, c1_ref, c2_ref, c3_ref,
    va_ref, vb_ref, v3_ref, vt_ref, vl_ref, face_ref, yd_ref, yu_ref,
    r_ref, v_ref, inv_ref, ownx_ref, mid,
):
    z = l_ref.shape[3]
    cells = wx * wy
    xs = tuple(range(1, wx - 1))
    results = after_y(wx, wy, xs, visc_ref, l_ref, kp_ref, parts_ref, my_ref, own_ref, v3_ref, yd_ref, yu_ref)
    for n, part in enumerate(results):
        for s in range(6):
            mid[n, s] = part[0][s]
    traces = [yu_ref[pl.ds(48 * wx, 48), :]] + [l_ref[0, y] for y in range(wy)] + [yd_ref[pl.ds(48 * wx, 48), :]]
    ownx_ref[...] = dot(tall([mx_ref[pl.ds(48, 48), :], mx_ref[pl.ds(288, 192), :]]), wide(traces))

    def contrib(slot, x, y):
        if 0 < y < wy - 1:
            return c2_ref[slot, wx * (y - 1) + x]
        if y == 0:
            return c1_ref[slot, x]
        extra = mid[x - 1, slot] if 0 < x < wx - 1 else c3_ref[0 if x == 0 else 1, slot]
        return c1_ref[slot, wx + x] + extra

    for x in range(wx):
        for y in range(wy):
            col = pl.ds(x * wy + y, 48, stride=cells)
            if x:
                r_ref[0, col, :] = contrib(0, x, y) + contrib(1, x - 1, y)
            else:
                r_ref[0, col, :] = contrib(0, x, y)
            if y:
                behind = contrib(3, x, y - 1)
            elif 0 < x < wx - 1:
                behind = results[x - 1][5]
            else:
                behind = face_ref[0 if x == 0 else 1]
            r_ref[1, col, :] = contrib(2, x, y) + behind
            r_ref[2, col, :] = contrib(4, x, y) + z_prev(contrib(5, x, y))
    sums_d, one_d, misc_d = read_tail(yd_ref, wx, 0)
    sums_u, one_u, misc_u = read_tail(yu_ref, wx, 1)
    edge_diag = misc_d[wx + 4 : 2 * wx + 4] + misc_d[2 * wx + 4 : 3 * wx + 4]

    def brought(which, i):
        held = vt_ref if which == 1 else vl_ref
        terms = []
        for x, p in ((i, 0), (i - 1, 1)):
            if x in (0, wx - 1):
                terms.append(held[0 if x == 0 else 1, p])
            elif 0 < x < wx - 1:
                terms.append(settle(results[x - 1][which], p))
        return sum(terms[1:], terms[0])

    for i in range(wx + 1):
        lines = [sums_u[i] + brought(3, i), va_ref[0, i]]
        lines += [vb_ref[y, i] for y in range(wy - 2)]
        lines += [va_ref[1, i] + brought(1, i), sums_d[i]]
        v_ref[i] = merge(lines[1::2], lines[0::2])
        if i < wx:
            parts = [jnp.broadcast_to(diag_ref[pl.ds(i * wy + y, 1), :], (4, z)) for y in range(wy)]
            parts += [jnp.broadcast_to(edge_diag[i : i + 1], (4, z)), jnp.zeros((4, z), F32)]
            inv_ref[i] = reciprocal(tall(parts))


def reciprocal(diag):
    present = diag > 0.0
    return jnp.where(present, (1.0 / (gain * gain)) / jnp.where(present, diag, 1.0), 0.0)


def final_kernel(
    wx, wy, visc_ref, l_ref, kp_ref, parts_ref, mx_ref, ownx_ref, r_ref, v_ref, inv_ref, v1_ref,
    yd_ref, yu_ref, inner_in, outer_in, p_ref, out_hbm, held, xd_ref, xu_ref, sems,
):
    arrive("gx", inner_in, outer_in, xd_ref, xu_ref)
    cells, z = wx * wy, l_ref.shape[3]
    rows = v_ref.shape[1]
    row = lambda i, col: kp_ref[i, pl.ds(col, 1), :]
    delta = dot(mx_ref[...], wide([xd_ref[pl.ds(48 * j, 48), :] for j in range(wy + 2)]))
    rim_x = xd_ref[pl.ds(48 * (wy + 2), xd_ref.shape[0] - 48 * (wy + 2)), :].astype(F32)
    rim_l = xu_ref[pl.ds(48 * wy, xu_ref.shape[0] - 48 * wy), :].astype(F32)
    misc_d = read_tail(yd_ref, wx, 0)[2]
    misc_u = read_tail(yu_ref, wx, 1)[2]
    flags_high = rim_x[rows + 2 * (wy + 1) : rows + 3 * wy + 4]
    corner = (wx - 1) * wy
    arrived = [xu_ref[pl.ds(48 * y, 48), :].astype(F32) for y in range(wy)]
    arrived_corners = slot_corners(arrived, parts_ref, 1)
    codes = rim_l[rows + 32 : rows + 32 + wy + 2]
    keep_z = rim_l[rows + 32 + wy + 2 : rows + 32 + 2 * (wy + 2)]
    keep_y = rim_l[rows + 32 + 2 * (wy + 2) : rows + 32 + 3 * (wy + 2) - 1]
    low_visc = level_visc(codes, visc_ref)
    low_keep_z = z_next(keep_z)
    lines = [[], [], []]
    high_flux = []
    for j in range(-1, wy + 1):
        n = j + 1
        part = delta[:, z * n : z * n + z]
        flag = flags_high[n : n + 1]
        if j < 0:
            visc = level_visc(misc_u[wx - 1 : wx], visc_ref)
            kz = misc_u[3 * wx - 1 : 3 * wx]
            keeps = [misc_u[2 * wx - 1 : 2 * wx], flag, None, row(1, corner), kz, z_next(kz)]
        elif j < wy:
            here = corner + j
            visc = row(4, here)
            high_y = row(1, here + 1) if j < wy - 1 else misc_d[wx - 1 : wx]
            keeps = [row(0, here), flag, row(1, here), high_y, row(2, here), row(3, here)]
        else:
            visc = level_visc(misc_d[wx + 1 : wx + 2], visc_ref)
            kz = misc_d[wx + 3 : wx + 4]
            keeps = [misc_d[wx + 2 : wx + 3], flag, misc_d[wx - 1 : wx], None, kz, z_next(kz)]
        scales = [None if keep is None else visc * keep for keep in keeps]
        corners = scaled_corners(part[288:480], scales)
        one = v1_ref[n] * flag
        lines[0].append(settle(corners, 0))
        lines[1].append(settle(corners, 1) + one[0:8] + z_prev(one[8:16]))
        high_flux.append([None if k is None else part[48 * s : 48 * s + 48] * k for s, k in enumerate(scales)])
        own = ownx_ref[:, pl.ds(z * n, z)]
        visc = low_visc[n : n + 1]
        flag = misc_u[wx : wx + 1] if j < 0 else misc_d[wx : wx + 1] if j == wy else row(0, j)
        scales = [
            None, visc * flag, None if j < 0 else visc * keep_y[j : j + 1],
            None if j == wy else visc * keep_y[j + 1 : j + 2], visc * keep_z[n : n + 1], visc * low_keep_z[n : n + 1],
        ]
        corners = settle(scaled_corners(own[48:240], scales), 1)
        if 0 <= j < wy:
            lines[2].append(corners + settle(arrived_corners[j] * flag, 1))
            face = (arrived[j] + visc * (own[0:48] + penalty * l_ref[0, j].astype(F32))) * flag
            r_ref[0, pl.ds(j, 48, stride=cells), :] += face
        else:
            at = rows + (0 if j < 0 else 16)
            one = rim_l[at : at + 16] * flag
            lines[2].append(corners + one[0:8] + z_prev(one[8:16]))
    low, before, first = [merge(part[1::2], part[0::2]) for part in lines]
    top = v_ref[wx] + before + rim_x[0:rows]
    values = [(v_ref[0] + first + rim_l[0:rows]) * inv_ref[0]]
    values += [v_ref[i] * inv_ref[i] for i in range(1, wx - 1)]
    values += [(v_ref[wx - 1] + low) * inv_ref[wx - 1]]
    diag = rim_x[rows : rows + wy + 1] + rim_x[rows + wy + 1 : rows + 2 * (wy + 1)]
    parts = [jnp.broadcast_to(diag[j : j + 1], (4, z)) for j in range(wy + 1)]
    values += [top * reciprocal(tall(parts + [jnp.zeros((rows - 4 * (wy + 1), z), F32)]))]
    low = [tall(values[x : x + 3]) for x in range(0, wx, 2)]
    rhs = tall([wide(low), wide([z_next(part) for part in low])]).astype(BF)
    for j in range(wy):
        col = pl.ds(corner + j, 48, stride=cells)
        flux = high_flux[j + 1]
        r_ref[0, col, :] += flux[0]
        r_ref[1, col, :] += flux[2] + high_flux[j][3]
        r_ref[2, col, :] += flux[4] + z_prev(flux[5])
    size = 96 * wy
    copies = []
    for d in range(3):
        spread = dot(p_ref[pl.ds(size * d, size), :], rhs)
        spread = jnp.concatenate(
            [spread[:, z * g : z * g + z].reshape(48, 2 * wy, z) for g in range(wx // 2)], axis=1
        )
        total = r_ref[d].reshape(48, cells, z) + spread * kp_ref[d][None]
        held[d] = total.reshape(48 * cells, z).astype(BF)
        copies.append(pltpu.make_async_copy(held.at[d], out_hbm.at[d], sems.at[d]))
        copies[d].start()
    for copy in copies:
        copy.wait()


def call(body, args, outs, scratch, flops, hbm=False, out_hbm=False):
    if hbm:
        args = tuple(pltpu.with_memory_space_constraint(a, pltpu.HBM) for a in args)
    keywords = dict(out_specs=pl.BlockSpec(memory_space=pltpu.HBM)) if out_hbm else {}
    return pl.pallas_call(
        body,
        **keywords,
        in_specs=[pl.BlockSpec(memory_space=pltpu.HBM if hbm else pltpu.VMEM)] * len(args),
        out_shape=outs,
        scratch_shapes=scratch,
        cost_estimate=pl.CostEstimate(flops=flops, bytes_accessed=1000000, transcendentals=0),
        compiler_params=pltpu.CompilerParams(vmem_limit_bytes=16 * 1024 * 1024),
    )(*args)


def local(traces, dirichlet, visc_class, viscosity, coarse_diag, solve_map, flux_map):
    wx, wy, z = traces.shape[2:]
    cells = wx * wy
    rows = 8 * (wy // 2 + 1)
    per_hex = 4 * 288 * 256 * z
    gather = jnp.asarray(gather_table())
    parts = jnp.asarray(slot_table())
    spread = jnp.asarray(spread_table(wy, rows))
    vm = pltpu.VMEM
    bind = lambda body: functools.partial(body, wx, wy)
    y_message = vm((48 * wx + 48 + tail_rows(8 * ((wx + 2) // 2) + 8 + 3 * wx + 4), z), BF)
    y_outer = vm((y_message.shape[0] + 16, z), BF)
    x_message = vm((48 * (wy + 2) + tail_rows(rows + 3 * wy + 4), z), BF)
    x_outer = vm((x_message.shape[0] + 16, z), BF)

    (lifted, flags, visc, diag, s_map, s_turned, f_map, gather, parts, c1, va, v1a, v3, inner, outer) = call(
        bind(first_kernel),
        (
            viscosity, traces.reshape(3, 48 * cells, z), dirichlet.reshape(3, cells, z),
            visc_class.reshape(cells, z), coarse_diag.reshape(cells, z), solve_map.T, flux_map, gather, parts,
        ),
        (
            vm((4, cells, 48, z), BF), vm((6, cells, z), F32), vm((viscosity.shape[0], z), F32), vm((cells, z), F32),
            vm(solve_map.shape, BF),
            vm(solve_map.shape[::-1], BF), vm(flux_map.shape, BF), vm(gather.shape, BF), vm(parts.shape, BF),
            vm((6, 2 * wx, 48, z), F32), vm((2, wx + 1, 8, z), F32), vm((2, 16, z), F32), vm((wx, 32, z), F32),
            y_message, y_outer,
        ),
        [
            y_message, y_message,
            vm((3, 48 * cells, z), BF), vm((3, cells, z), jnp.int32), vm((cells, z), jnp.int32),
            vm((48 * cells, z), F32), pltpu.SMEM(viscosity.shape, F32), pltpu.SemaphoreType.DMA((9,)),
        ],
        2 * wx * per_hex, True,
    )
    inner = swap(inner, "gy", "gx", 0)
    outer = swap(outer, "gy", "gx", 1)
    between = wx * (wy - 2)
    c2, vb, v1b, mx, my, own = call(
        bind(middle_kernel),
        (lifted, flags, s_map, s_turned, f_map, gather, parts),
        (
            vm((6, between, 48, z), F32), vm((wy - 2, wx + 1, 8, z), F32), vm((wy - 2, 16, z), F32),
            vm((480, 48), BF), vm((480, 48), BF), vm((240, wx * z), F32),
        ),
        [], between * per_hex,
    )
    c3, vt, vl, v1, face, yd, yu, inner, outer = call(
        bind(turn_kernel),
        (
            visc, lifted, flags, diag, parts, my, own, c1, c2, va, vb, v1a, v1b, v3, inner, outer,
        ),
        (
            vm((2, 6, 48, z), F32), vm((2, 2, 8, z), F32), vm((2, 2, 8, z), F32), vm((wy + 2, 16, z), F32),
            vm((2, 48, z), F32), y_message, y_message, x_message, x_outer,
        ),
        [x_message, x_message], 2 * per_hex,
    )
    inner = swap(inner, "gx", "gy", 0)
    outer = swap(outer, "gx", "gy", 1)
    residual, vs, inverse, ownx = call(
        bind(assemble_kernel),
        (
            visc, lifted, flags, diag, parts, mx, my, own, c1, c2, c3, va, vb, v3, vt, vl, face, yd, yu,
        ),
        (
            vm((3, 48 * cells, z), F32), vm((wx + 1, rows, z), F32), vm((wx, rows, z), F32),
            vm((240, (wy + 2) * z), F32),
        ),
        [vm((wx - 2, 6, 48, z), F32)], 4 * per_hex,
    )
    out = call(
        bind(final_kernel),
        (
            visc, lifted, flags, parts, mx, ownx, residual, vs, inverse, v1, yd, yu, inner, outer, spread,
        ),
        jax.ShapeDtypeStruct((3, 48 * cells, z), BF),
        [vm((3, 48 * cells, z), BF), x_message, x_message, pltpu.SemaphoreType.DMA((3,))], 4 * spread.size * z,
        out_hbm=True,
    )
    return out.reshape(traces.shape)


def solution(mesh):
    in_specs = (
        P(None, None, "gx", "gy", None),
        P(None, "gx", "gy", None),
        P("gx", "gy", None),
        P(),
        P("gx", "gy", None),
        P(),
        P(),
    )
    out_specs = P(None, None, "gx", "gy", None)
    return jax.shard_map(local, mesh=mesh, in_specs=in_specs, out_specs=out_specs, check_vma=False)
```

```python
import functools
import math

import jax
import jax.numpy as jnp
import ml_dtypes
import numpy as np
from jax import lax
from jax.experimental import pallas as pl
from jax.experimental.pallas import tpu as pltpu
from jax.sharding import PartitionSpec as P

penalty = 0.5
BF = jnp.bfloat16
F32 = jnp.float32
lift = 1.3264
gain = 1.3280711361297461


def swap(value, axis, other, first):
    count, width = lax.axis_size(axis), lax.axis_size(other)
    place = (lambda i, j: i * width + j) if (axis, other) == ("gx", "gy") else (lambda i, j: j * count + i)
    lows = list(range(first, count - 1, 2))
    pairs = [(place(low, j), place(low + 1, j)) for low in lows for j in range(width)]
    alone = [i for i in range(count) if i not in lows and i - 1 not in lows]
    pairs += [(place(i, j), place(i, j + 1)) for i in alone for j in range(0, width - 1, 2)]
    return lax.ppermute(value, ("gx", "gy"), pairs + [(high, low) for low, high in pairs])


def even(axis):
    return lax.rem(lax.axis_index(axis), 2) == 0


def arrive(axis, inner_ref, outer_ref, down_ref, up_ref):
    here, last = lax.axis_index(axis), lax.axis_size(axis) - 1
    choose(even(axis), inner_ref, outer_ref, down_ref, here < last)
    choose(even(axis), outer_ref, inner_ref, up_ref, here > 0)


def depart(axis, down_ref, up_ref, inner_ref, outer_ref):
    choose(even(axis), up_ref, down_ref, inner_ref)
    choose(even(axis), down_ref, up_ref, outer_ref)


def choose(condition, yes_ref, no_ref, out_ref, present=None):
    size = min(yes_ref.shape[0], no_ref.shape[0], out_ref.shape[0])
    rows = pl.ds(0, size)
    value = jnp.where(condition, yes_ref[rows, :], no_ref[rows, :])
    out_ref[rows, :] = value if present is None else jnp.where(present, value, jnp.zeros_like(value))
    if out_ref.shape[0] > size:
        rest = pl.ds(size, out_ref.shape[0] - size)
        out_ref[rest, :] = jnp.zeros((out_ref.shape[0] - size, out_ref.shape[1]), out_ref.dtype)


def corner_table():
    gll_points = [-1.0, -math.sqrt(0.2), math.sqrt(0.2), 1.0]
    table = np.zeros((16, 4), np.float64)
    for s in range(4):
        for t in range(4):
            for p in range(2):
                for q in range(2):
                    table[4 * s + t, 2 * p + q] = (
                        (1 + (2 * p - 1) * gll_points[s]) * (1 + (2 * q - 1) * gll_points[t]) / 4
                    )
    return table


def landing(face_slot, high_s, high_t):
    direction, outward = divmod(face_slot, 2)
    if direction == 0:
        return (outward, high_s, high_t)
    if direction == 1:
        return (high_s, outward, high_t)
    return (high_s, high_t, outward)


def gather_table():
    weights = lift * corner_table()
    table = np.zeros((32, 288), np.float64)
    for slot in range(6):
        for s in range(2):
            for t in range(2):
                p, q, r = landing(slot, s, t)
                for c in range(3):
                    cols = slot * 48 + 16 * c + np.arange(16)
                    table[16 * r + 8 * p + 4 * q + c, cols] += weights[:, 2 * s + t]
    return table.astype(ml_dtypes.bfloat16)


def slot_table():
    slots = np.split(gather_table(), 6, axis=1)
    rows = [
        np.r_[0:8, 16:24], np.r_[8:16, 24:32], np.arange(32), np.arange(32), np.arange(16), np.arange(16, 32),
    ]
    return np.concatenate([slot[kept] for slot, kept in zip(slots, rows)], axis=0)


slot_rows = (0, 16, 32, 64, 96, 112, 128)


def spread_table(wy, rows):
    weights = lift * corner_table()
    table = np.zeros((3, 48, 2, wy, 6 * rows), np.float64)
    for d in range(3):
        for x in range(2):
            for y in range(wy):
                for s in range(2):
                    for t in range(2):
                        p, q, r = landing(2 * d, s, t)
                        for c in range(3):
                            k = (3 * r + x + p) * rows + 4 * (y + q) + c
                            table[d, 16 * c : 16 * c + 16, x, y, k] += weights[:, 2 * s + t]
    return table.reshape(-1, 6 * rows).astype(ml_dtypes.bfloat16)


def lanes(shape):
    return lax.broadcasted_iota(jnp.int32, shape, len(shape) - 1)


def z_next(value):
    last = value.shape[-1] - 1
    return jnp.where(lanes(value.shape) < last, pltpu.roll(value, last, value.ndim - 1), 0.0)


def z_prev(value):
    return jnp.where(lanes(value.shape) > 0, pltpu.roll(value, 1, value.ndim - 1), 0.0)


def dot(left, right):
    return jnp.dot(left, right, preferred_element_type=F32)


def wide(parts):
    return jnp.concatenate(parts, axis=1)


def tall(parts):
    return jnp.concatenate(parts, axis=0)


def hex_batch(slots, scales, s_map, f_map):
    z = slots[0][0].shape[1]
    element = tall([wide([hexa[s] for hexa in slots]) for s in range(6)])
    interior = dot(s_map, element).astype(BF)
    flux = dot(f_map, interior) + penalty * element.astype(F32)
    return [
        [flux[48 * s : 48 * s + 48, z * h : z * h + z] * scales[h][s] for s in range(6)]
        for h in range(len(slots))
    ]


def corner_batch(blocks, left_out, gather):
    z = blocks[0][0].shape[1]
    nothing = jnp.zeros((48, z), BF)
    right = tall(
        [
            wide([nothing if s in left_out[h] else blocks[h][s].astype(BF) for h in range(len(blocks))])
            for s in range(6)
        ]
    )
    return [dot(gather, right)[:, z * h : z * h + z] for h in range(len(blocks))]


def slot_corners(traces, parts_ref, slot):
    z = traces[0].shape[1]
    first, size = slot_rows[slot], slot_rows[slot + 1] - slot_rows[slot]
    rows = dot(parts_ref[pl.ds(first, size), :], wide([trace.astype(BF) for trace in traces]))
    return [rows[:, z * h : z * h + z] for h in range(len(traces))]


def settle(rows, p):
    return rows[8 * p : 8 * p + 8] + z_prev(rows[16 + 8 * p : 24 + 8 * p])


def scaled_corners(delta, scales, offsets=(0, 1)):
    shape = (8, delta.shape[1])
    blank = jnp.zeros((1, shape[1]), F32)
    y_scale = jnp.where(
        lax.broadcasted_iota(jnp.int32, shape, 0) < 4,
        blank if scales[2] is None else scales[2], blank if scales[3] is None else scales[3],
    )
    results = []
    for p in offsets:
        parts = []
        for r in range(2):
            at = 32 + 16 * r + 8 * p
            part = delta[at : at + 8] * y_scale + delta[at + 32 : at + 40] * scales[4 + r]
            if scales[p] is not None:
                part = part + delta[16 * p + 8 * r : 16 * p + 8 * r + 8] * scales[p]
            parts.append(part)
        results.append(parts[0] + z_prev(parts[1]))
    return results


def level_visc(code, visc_ref):
    visc = jnp.zeros(code.shape, F32)
    for level in range(visc_ref.shape[0]):
        visc = visc + jnp.where(code == F32(level + 1), visc_ref[pl.ds(level, 1), :], F32(0.0))
    return visc


def merge(even, odd):
    odd = tall(odd)
    return tall(even) + pltpu.roll(odd, odd.shape[0] - 4, 0)


def first_kernel(
    wx, wy, visc_hbm, t_hbm, dir_hbm, cls_hbm, diag_hbm, st_hbm, f_hbm, g_hbm, parts_hbm,
    l_ref, nat, kp_ref, visc_ref, diag_ref, s_ref, st_ref, f_ref, g_ref, parts_ref, c_ref, v_ref, v1_ref, v3_ref,
    inner_ref, outer_ref, down_ref, up_ref, t_ref, dir_ref, cls_ref, levels, sems,
):
    cells = wx * wy
    pairs = [
        (st_hbm, st_ref), (dir_hbm, dir_ref), (t_hbm.at[0], t_ref.at[0]), (t_hbm.at[1], t_ref.at[1]),
        (t_hbm.at[2], t_ref.at[2]), (cls_hbm, cls_ref), (visc_hbm, levels), (f_hbm, f_ref), (g_hbm, g_ref),
        (parts_hbm, parts_ref), (diag_hbm, diag_ref),
    ]
    copies = [pltpu.make_async_copy(a, b, sems.at[i]) for i, (a, b) in enumerate(pairs)]
    for copy in copies:
        copy.start()
    copies[0].wait()
    s_ref[...] = st_ref[...].T
    copies[1].wait()
    z = t_ref.shape[2]
    for d in range(3):
        keep = (1 - dir_ref[d]).astype(F32)
        kp_ref[d] = keep
        copies[2 + d].wait()
        masked = t_ref[d].astype(F32).reshape(48, cells, z) * keep[None]
        nat[d] = masked.reshape(48 * cells, z)
        lay_out(wx, wy, d, nat, l_ref, True)
    kp_ref[3] = z_next(kp_ref[2])
    for copy in copies[5:]:
        copy.wait()
    for level in range(visc_ref.shape[0]):
        visc_ref[pl.ds(level, 1), :] = jnp.full((1, z), levels[level], F32)
    code = cls_ref[...].astype(F32) + 1.0
    kp_ref[4] = level_visc(code, visc_ref)
    kp_ref[5] = code
    row = lambda i, col: kp_ref[i, pl.ds(col, 1), :]
    blocks, corners = [], []
    for y in (0, wy - 1):
        some, left_out = known_hexes(
            wx, wy, [(x, y) for x in range(wx)], (l_ref, None), kp_ref, s_ref, f_ref, c_ref, len(blocks)
        )
        corners += corner_batch(some, left_out, g_ref[...])
        blocks += some
    lone = slot_corners([blocks[wx - 1][1], blocks[2 * wx - 1][1]], parts_ref, 1)
    for h in range(2):
        v1_ref[h] = lone[h]
    for x, rows in enumerate(slot_corners([blocks[wx + x][3] for x in range(wx)], parts_ref, 3)):
        v3_ref[x] = rows
    sums = [line_sums(corners[:wx]), line_sums(corners[wx:])]
    for side in range(2):
        for i in range(wx + 1):
            v_ref[side, i] = sums[side][i]
    corner = (wx - 1) * wy
    top = wy - 1
    for x in range(wx):
        down_ref[pl.ds(48 * x, 48), :] = l_ref[1, x * wy]
        up_ref[pl.ds(48 * x, 48), :] = blocks[wx + x][3].astype(BF)
    down_ref[pl.ds(48 * wx, 48), :] = l_ref[0, 0]
    up_ref[pl.ds(48 * wx, 48), :] = l_ref[0, top]
    flags = [row(1, x * wy) for x in range(wx)] + [row(0, 0), row(5, corner), row(0, corner), row(2, corner)]
    diag = tall([diag_ref[pl.ds(x * wy, 1), :] for x in range(wx)])
    high = diag.astype(BF).astype(F32)
    rim = pack(sums[0], 0) + pack([v1_ref[0, 0:8], v1_ref[0, 8:16]], 0) + flags + [high, diag - high]
    put_tail(down_ref, 48 * wx + 48, rim)
    flags = [row(kind, x * wy + top) for kind in (5, 0, 2) for x in range(wx)]
    rim = pack(sums[1], 1) + pack([v1_ref[1, 0:8], v1_ref[1, 8:16]], 1) + flags
    put_tail(up_ref, 48 * wx + 48, rim)
    depart("gy", down_ref, up_ref, inner_ref, outer_ref)


def tail_rows(count):
    return -(-count // 16) * 16


def put_tail(ref, start, rows):
    count = sum(part.shape[0] for part in rows)
    full = ref.shape[0] - start
    if full > count:
        rows = rows + [jnp.zeros((full - count, rows[0].shape[1]), F32)]
    ref[pl.ds(start, full), :] = tall(rows).astype(BF)


def pack(parts, half):
    place = lax.broadcasted_iota(jnp.int32, parts[0].shape, 0)
    parts = parts + [jnp.zeros_like(parts[0])] * (len(parts) % 2)
    packed = []
    for low, high in zip(parts[0::2], parts[1::2]):
        if half:
            low = pltpu.roll(low, 4, 0)
        else:
            high = pltpu.roll(high, 4, 0)
        packed.append(jnp.where(place < 4, low, high))
    return packed


def unpack(packed, count, half):
    parts = []
    for n in range(count):
        part = packed[8 * (n // 2) : 8 * (n // 2) + 8]
        parts.append(part if n % 2 == half else pltpu.roll(part, 4, 0))
    return parts


def read_tail(ref, wx, half):
    start = 48 * wx + 48
    rows = ref[pl.ds(start, ref.shape[0] - start), :].astype(F32)
    size = 8 * ((wx + 2) // 2)
    return unpack(rows, wx + 1, half), unpack(rows[size : size + 8], 2, half), rows[size + 8 :]


def line_sums(corners):
    width = len(corners)
    low = [settle(rows, 0) for rows in corners]
    high = [settle(rows, 1) for rows in corners]
    return [low[0]] + [low[x] + high[x - 1] for x in range(1, width)] + [high[-1]]


def early(wx, wy, d, x, y):
    return y in (0, wy - 1) or (d == 0 and x == 0) or (d == 1 and y == 1)


def lay_out(wx, wy, d, nat, l_ref, first):
    for x in range(wx):
        for y in range(wy):
            if early(wx, wy, d, x, y) == first:
                col = x * wy + y
                part = nat[d, pl.ds(col, 48, stride=wx * wy), :]
                l_ref[d, col] = part.astype(BF)
                if d == 2:
                    l_ref[3, col] = z_next(part).astype(BF)


def known_hexes(wx, wy, where, l_refs, kp_ref, s_ref, f_ref, c_ref, start):
    z = l_refs[0].shape[3]
    nothing = jnp.zeros((48, z), BF)
    row = lambda i, col: kp_ref[i, pl.ds(col, 1), :]
    trace = lambda d, x, y: l_refs[0 if early(wx, wy, min(d, 2), x, y) else 1][d, x * wy + y]
    slots, scales, left_out = [], [], []
    for x, y in where:
        here = x * wy + y
        visc = row(4, here)
        last_x, last_y = x == wx - 1, y == wy - 1
        slots.append(
            [
                trace(0, x, y), nothing if last_x else trace(0, x + 1, y),
                trace(1, x, y), nothing if last_y else trace(1, x, y + 1),
                trace(2, x, y), trace(3, x, y),
            ]
        )
        scales.append(
            [
                visc * row(0, here), visc if last_x else visc * row(0, here + wy),
                visc * row(1, here), visc if last_y else visc * row(1, here + 1),
                visc * row(2, here), visc * row(3, here),
            ]
        )
        left_out.append(([1] if last_x else []) + ([3] if last_y else []))
    blocks = hex_batch(slots, scales, s_ref[...], f_ref[...])
    for h in range(len(where)):
        for s in range(6):
            c_ref[s, start + h] = blocks[h][s]
    return blocks, left_out


def middle_kernel(
    wx, wy, l_ref, nat, kp_ref, s_ref, st_ref, f_ref, g_ref, parts_ref,
    c_ref, v_ref, v1_ref, mx_ref, my_ref, own_ref, rest_ref,
):
    z = l_ref.shape[3]
    for slot, ref in ((1, mx_ref), (3, my_ref)):
        flux = lax.dot_general(
            f_ref[...], st_ref[pl.ds(48 * slot, 48), :], (((1,), (1,)), ((), ())),
            preferred_element_type=F32,
        )
        ref[pl.ds(0, 288), :] = flux.astype(BF)
        eye = lax.broadcasted_iota(jnp.int32, (48, 48), 0) == lax.broadcasted_iota(jnp.int32, (48, 48), 1)
        rows = []
        for s in range(6):
            block = flux[48 * s : 48 * s + 48]
            if s == slot:
                block = block + jnp.where(eye, F32(penalty), F32(0.0))
            first, size = slot_rows[s], slot_rows[s + 1] - slot_rows[s]
            rows.append(dot(parts_ref[pl.ds(first, size), :], block.astype(BF)))
        rows[2:4] = [rows[2] + rows[3]]
        ref[pl.ds(288, 96), :] = tall(rows).astype(BF)
    for d in range(3):
        lay_out(wx, wy, d, nat, rest_ref, False)
    own_ref[...] = dot(tall([my_ref[pl.ds(144, 48), :], my_ref[pl.ds(288, 96), :]]), wide([l_ref[1, x * wy] for x in range(wx)]))
    where = [(x, y) for y in range(1, wy - 1) for x in range(wx)]
    blocks, left_out = known_hexes(wx, wy, where, (l_ref, rest_ref), kp_ref, s_ref, f_ref, c_ref, 0)
    corners = corner_batch(blocks, left_out, g_ref[...])
    lone = slot_corners([blocks[wx * y + wx - 1][1] for y in range(wy - 2)], parts_ref, 1)
    for y in range(wy - 2):
        v1_ref[y] = lone[y]
        for i, rows in enumerate(line_sums(corners[wx * y : wx * y + wx])):
            v_ref[y, i] = rows


def after_y(wx, wy, xs, visc_ref, l_ref, kp_ref, parts_ref, my_ref, own_ref, v3_ref, down_ref, up_ref):
    z = l_ref.shape[3]
    misc_d = read_tail(down_ref, wx, 0)[2]
    misc_u = read_tail(up_ref, wx, 1)[2]
    row = lambda i, col: kp_ref[i, pl.ds(col, 1), :]
    delta = dot(my_ref[...], wide([down_ref[pl.ds(48 * x, 48), :] for x in xs]))
    arrived = [up_ref[pl.ds(48 * x, 48), :].astype(F32) for x in xs]
    arrived_corners = slot_corners(arrived, parts_ref, 3)
    results = []
    for n, x in enumerate(xs):
        here = x * wy + wy - 1
        last = x == wx - 1
        part = delta[:, z * n : z * n + z]
        visc = row(4, here)
        scales = [
            visc * row(0, here), visc if last else visc * row(0, here + wy), visc * row(1, here),
            visc * misc_d[x : x + 1], visc * row(2, here), visc * row(3, here),
        ]
        flux = [part[48 * s : 48 * s + 48] * scales[s] for s in range(6)]
        used = [None if (s == 1 and last) else scales[s] for s in range(6)]
        known = v3_ref[x] * misc_d[x : x + 1]
        top = [rows + settle(known, p) for p, rows in enumerate(scaled_corners(part[288:384], used))]
        top_one = part[304:320] * visc
        here = x * wy
        visc = level_visc(misc_u[x : x + 1], visc_ref)
        flag = row(1, here)
        own = own_ref[:, pl.ds(z * x, z)]
        keep_z = misc_u[2 * wx + x : 2 * wx + x + 1]
        scales = [
            visc * misc_u[wx + x : wx + x + 1], None if last else visc * misc_u[wx + x + 1 : wx + x + 2],
            None, visc * flag, visc * keep_z, visc * z_next(keep_z),
        ]
        known = arrived_corners[n] * flag
        low = [rows + settle(known, p) for p, rows in enumerate(scaled_corners(own[48:144], scales))]
        low_one = own[64:80] * visc
        face = (arrived[n] + visc * (own[0:48] + penalty * l_ref[1, here].astype(F32))) * flag
        results.append((flux, top, top_one, low, low_one, face))
    return results


def turn_kernel(
    wx, wy, visc_ref, l_ref, kp_ref, diag_ref, parts_ref, my_ref, own_ref, c1_ref, c2_ref, va_ref, vb_ref,
    v1a_ref, v1b_ref, v3_ref, inner_in, outer_in,
    c3_ref, vt_ref, vl_ref, v1_ref, face_ref, yd_ref, yu_ref, inner_ref, outer_ref, down_ref, up_ref,
):
    z = l_ref.shape[3]
    arrive("gy", inner_in, outer_in, yd_ref, yu_ref)
    xs = (0, wx - 1)
    results = after_y(wx, wy, xs, visc_ref, l_ref, kp_ref, parts_ref, my_ref, own_ref, v3_ref, yd_ref, yu_ref)
    row = lambda i, col: kp_ref[i, pl.ds(col, 1), :]
    sums_d, one_d, misc_d = read_tail(yd_ref, wx, 0)
    sums_u, one_u, misc_u = read_tail(yu_ref, wx, 1)
    edge_high, edge_low = misc_d[wx + 4 : 2 * wx + 4], misc_d[2 * wx + 4 : 3 * wx + 4]
    for n, (flux, top, top_one, low, low_one, face) in enumerate(results):
        for s in range(6):
            c3_ref[n, s] = flux[s]
        face_ref[n] = face
        for p in range(2):
            vt_ref[n, p] = top[p]
            vl_ref[n, p] = low[p]
    flux, top, top_one, low, low_one, face = results[1]
    mine = tall(one_u) + low_one
    v1_ref[0] = mine
    v1_ref[1] = v1a_ref[0]
    for y in range(wy - 2):
        v1_ref[2 + y] = v1b_ref[y]
    v1_ref[wy] = v1a_ref[1] + top_one
    v1_ref[wy + 1] = tall(one_d)

    def plane(i, n, p):
        lines = [sums_u[i] + vl_ref[n, p], va_ref[0, i]]
        lines += [vb_ref[y, i] for y in range(wy - 2)]
        lines += [va_ref[1, i] + vt_ref[n, p], sums_d[i]]
        return merge(lines[1::2], lines[0::2])

    down_ref[pl.ds(0, 48), :] = yu_ref[pl.ds(48 * wx, 48), :]
    for y in range(wy):
        down_ref[pl.ds(48 + 48 * y, 48), :] = l_ref[0, y]
    down_ref[pl.ds(48 * (wy + 1), 48), :] = yd_ref[pl.ds(48 * wx, 48), :]
    diag = diag_ref[pl.ds(0, wy), :]
    high = diag.astype(BF).astype(F32)
    rim = [plane(0, 0, 0), high, edge_high[0:1], diag - high, edge_low[0:1]]
    rim += [misc_u[wx : wx + 1], kp_ref[0, 0:wy], misc_d[wx : wx + 1]]
    put_tail(down_ref, 48 * (wy + 2), rim)
    corner = (wx - 1) * wy
    up_ref[pl.ds(0, 48), :] = c1_ref[1, wx - 1].astype(BF)
    for y in range(1, wy - 1):
        up_ref[pl.ds(48 * y, 48), :] = c2_ref[1, wx * (y - 1) + wx - 1].astype(BF)
    up_ref[pl.ds(48 * (wy - 1), 48), :] = (c1_ref[1, 2 * wx - 1] + flux[1]).astype(BF)
    last = pl.ds(corner, wy)
    rim = [plane(wx, 1, 1), mine, *one_d]
    rim += [misc_u[wx - 1 : wx], kp_ref[5, last], misc_d[wx + 1 : wx + 2]]
    rim += [misc_u[3 * wx - 1 : 3 * wx], kp_ref[2, last], misc_d[wx + 3 : wx + 4]]
    rim += [kp_ref[1, last], misc_d[wx - 1 : wx]]
    put_tail(up_ref, 48 * wy, rim)
    depart("gx", down_ref, up_ref, inner_ref, outer_ref)


def assemble_kernel(
    wx, wy, visc_ref, l_ref, kp_ref, diag_ref, parts_ref, mx_ref, my_ref, own_ref, c1_ref, c2_ref, c3_ref,
    va_ref, vb_ref, v3_ref, vt_ref, vl_ref, face_ref, yd_ref, yu_ref,
    r_ref, v_ref, inv_ref, ownx_ref, mid,
):
    z = l_ref.shape[3]
    cells = wx * wy
    xs = tuple(range(1, wx - 1))
    results = after_y(wx, wy, xs, visc_ref, l_ref, kp_ref, parts_ref, my_ref, own_ref, v3_ref, yd_ref, yu_ref)
    for n, part in enumerate(results):
        for s in range(6):
            mid[n, s] = part[0][s]
    traces = [yu_ref[pl.ds(48 * wx, 48), :]] + [l_ref[0, y] for y in range(wy)] + [yd_ref[pl.ds(48 * wx, 48), :]]
    ownx_ref[...] = dot(tall([mx_ref[pl.ds(48, 48), :], mx_ref[pl.ds(288, 96), :]]), wide(traces))

    def contrib(slot, x, y):
        if 0 < y < wy - 1:
            return c2_ref[slot, wx * (y - 1) + x]
        if y == 0:
            return c1_ref[slot, x]
        extra = mid[x - 1, slot] if 0 < x < wx - 1 else c3_ref[0 if x == 0 else 1, slot]
        return c1_ref[slot, wx + x] + extra

    for x in range(wx):
        for y in range(wy):
            col = pl.ds(x * wy + y, 48, stride=cells)
            if x:
                r_ref[0, col, :] = contrib(0, x, y) + contrib(1, x - 1, y)
            else:
                r_ref[0, col, :] = contrib(0, x, y)
            if y:
                behind = contrib(3, x, y - 1)
            elif 0 < x < wx - 1:
                behind = results[x - 1][5]
            else:
                behind = face_ref[0 if x == 0 else 1]
            r_ref[1, col, :] = contrib(2, x, y) + behind
            r_ref[2, col, :] = contrib(4, x, y) + z_prev(contrib(5, x, y))
    sums_d, one_d, misc_d = read_tail(yd_ref, wx, 0)
    sums_u, one_u, misc_u = read_tail(yu_ref, wx, 1)
    edge_diag = misc_d[wx + 4 : 2 * wx + 4] + misc_d[2 * wx + 4 : 3 * wx + 4]

    def brought(which, i):
        held = vt_ref if which == 1 else vl_ref
        terms = []
        for x, p in ((i, 0), (i - 1, 1)):
            if x in (0, wx - 1):
                terms.append(held[0 if x == 0 else 1, p])
            elif 0 < x < wx - 1:
                terms.append(results[x - 1][which][p])
        return sum(terms[1:], terms[0])

    for i in range(wx + 1):
        lines = [sums_u[i] + brought(3, i), va_ref[0, i]]
        lines += [vb_ref[y, i] for y in range(wy - 2)]
        lines += [va_ref[1, i] + brought(1, i), sums_d[i]]
        v_ref[i] = merge(lines[1::2], lines[0::2])
        if i < wx:
            parts = [jnp.broadcast_to(diag_ref[pl.ds(i * wy + y, 1), :], (4, z)) for y in range(wy)]
            parts += [jnp.broadcast_to(edge_diag[i : i + 1], (4, z)), jnp.zeros((4, z), F32)]
            inv_ref[i] = reciprocal(tall(parts))


def reciprocal(diag):
    present = diag > 0.0
    return jnp.where(present, (1.0 / (gain * gain)) / jnp.where(present, diag, 1.0), 0.0)


def final_kernel(
    wx, wy, visc_ref, l_ref, kp_ref, parts_ref, mx_ref, ownx_ref, r_ref, v_ref, inv_ref, v1_ref,
    yd_ref, yu_ref, inner_in, outer_in, p_ref, out_hbm, held, xd_ref, xu_ref, sems,
):
    arrive("gx", inner_in, outer_in, xd_ref, xu_ref)
    cells, z = wx * wy, l_ref.shape[3]
    rows = v_ref.shape[1]
    row = lambda i, col: kp_ref[i, pl.ds(col, 1), :]
    traces = [xd_ref[pl.ds(48 * j, 48), :] for j in range(wy + 2)]
    delta = dot(mx_ref[pl.ds(288, 96), :], wide(traces))
    rim_x = xd_ref[pl.ds(48 * (wy + 2), xd_ref.shape[0] - 48 * (wy + 2)), :].astype(F32)
    rim_l = xu_ref[pl.ds(48 * wy, xu_ref.shape[0] - 48 * wy), :].astype(F32)
    misc_d = read_tail(yd_ref, wx, 0)[2]
    misc_u = read_tail(yu_ref, wx, 1)[2]
    flags_high = rim_x[rows + 2 * (wy + 1) : rows + 3 * wy + 4]
    corner = (wx - 1) * wy
    arrived = [xu_ref[pl.ds(48 * y, 48), :].astype(F32) for y in range(wy)]
    arrived_corners = slot_corners(arrived, parts_ref, 1)
    codes = rim_l[rows + 32 : rows + 32 + wy + 2]
    keep_z = rim_l[rows + 32 + wy + 2 : rows + 32 + 2 * (wy + 2)]
    keep_y = rim_l[rows + 32 + 2 * (wy + 2) : rows + 32 + 3 * (wy + 2) - 1]
    low_visc = level_visc(codes, visc_ref)
    low_keep_z = z_next(keep_z)
    lines = [[], [], []]
    high_scales = []
    for j in range(-1, wy + 1):
        n = j + 1
        part = delta[:, z * n : z * n + z]
        flag = flags_high[n : n + 1]
        if j < 0:
            visc = level_visc(misc_u[wx - 1 : wx], visc_ref)
            kz = misc_u[3 * wx - 1 : 3 * wx]
            keeps = [misc_u[2 * wx - 1 : 2 * wx], flag, None, row(1, corner), kz, z_next(kz)]
        elif j < wy:
            here = corner + j
            visc = row(4, here)
            high_y = row(1, here + 1) if j < wy - 1 else misc_d[wx - 1 : wx]
            keeps = [row(0, here), flag, row(1, here), high_y, row(2, here), row(3, here)]
        else:
            visc = level_visc(misc_d[wx + 1 : wx + 2], visc_ref)
            kz = misc_d[wx + 3 : wx + 4]
            keeps = [misc_d[wx + 2 : wx + 3], flag, misc_d[wx - 1 : wx], None, kz, z_next(kz)]
        scales = [None if keep is None else visc * keep for keep in keeps]
        corners = scaled_corners(part, scales)
        one = v1_ref[n] * flag
        lines[0].append(corners[0])
        lines[1].append(corners[1] + one[0:8] + z_prev(one[8:16]))
        high_scales.append(scales)
        own = ownx_ref[:, pl.ds(z * n, z)]
        visc = low_visc[n : n + 1]
        flag = misc_u[wx : wx + 1] if j < 0 else misc_d[wx : wx + 1] if j == wy else row(0, j)
        scales = [
            None, visc * flag, None if j < 0 else visc * keep_y[j : j + 1],
            None if j == wy else visc * keep_y[j + 1 : j + 2], visc * keep_z[n : n + 1], visc * low_keep_z[n : n + 1],
        ]
        corners = scaled_corners(own[48:144], scales, (1,))[0]
        if 0 <= j < wy:
            one = arrived_corners[j] * flag
            lines[2].append(corners + one[0:8] + z_prev(one[8:16]))
            face = (arrived[j] + visc * (own[0:48] + penalty * l_ref[0, j].astype(F32))) * flag
            r_ref[0, pl.ds(j, 48, stride=cells), :] += face
        else:
            at = rows + (0 if j < 0 else 16)
            one = rim_l[at : at + 16] * flag
            lines[2].append(corners + one[0:8] + z_prev(one[8:16]))
    low, before, first = [merge(part[1::2], part[0::2]) for part in lines]
    top = v_ref[wx] + before + rim_x[0:rows]
    values = [(v_ref[0] + first + rim_l[0:rows]) * inv_ref[0]]
    values += [v_ref[i] * inv_ref[i] for i in range(1, wx - 1)]
    values += [(v_ref[wx - 1] + low) * inv_ref[wx - 1]]
    diag = rim_x[rows : rows + wy + 1] + rim_x[rows + wy + 1 : rows + 2 * (wy + 1)]
    parts = [jnp.broadcast_to(diag[j : j + 1], (4, z)) for j in range(wy + 1)]
    values += [top * reciprocal(tall(parts + [jnp.zeros((rows - 4 * (wy + 1), z), F32)]))]
    low = [tall(values[x : x + 3]) for x in range(0, wx, 2)]
    rhs = tall([wide(low), wide([z_next(part) for part in low])]).astype(BF)
    delta = dot(mx_ref[pl.ds(0, 288), :], wide(traces[1 : wy + 1]))
    behind = dot(mx_ref[pl.ds(144, 48), :], traces[0]) * high_scales[0][3]
    for j in range(wy):
        col = pl.ds(corner + j, 48, stride=cells)
        part = delta[:, z * j : z * j + z]
        flux = [part[48 * s : 48 * s + 48] * high_scales[j + 1][s] for s in range(6)]
        r_ref[0, col, :] += flux[0]
        r_ref[1, col, :] += flux[2] + behind
        r_ref[2, col, :] += flux[4] + z_prev(flux[5])
        behind = flux[3]
    size = 96 * wy
    copies = []
    for d in range(3):
        spread = dot(p_ref[pl.ds(size * d, size), :], rhs)
        spread = jnp.concatenate(
            [spread[:, z * g : z * g + z].reshape(48, 2 * wy, z) for g in range(wx // 2)], axis=1
        )
        total = r_ref[d].reshape(48, cells, z) + spread * kp_ref[d][None]
        held[d] = total.reshape(48 * cells, z).astype(BF)
        copies.append(pltpu.make_async_copy(held.at[d], out_hbm.at[d], sems.at[d]))
        copies[d].start()
    for copy in copies:
        copy.wait()


def call(body, args, outs, scratch, flops, hbm=False, out_hbm=False):
    if hbm:
        args = tuple(pltpu.with_memory_space_constraint(a, pltpu.HBM) for a in args)
    keywords = dict(out_specs=pl.BlockSpec(memory_space=pltpu.HBM)) if out_hbm else {}
    return pl.pallas_call(
        body,
        **keywords,
        in_specs=[pl.BlockSpec(memory_space=pltpu.HBM if hbm else pltpu.VMEM)] * len(args),
        out_shape=outs,
        scratch_shapes=scratch,
        cost_estimate=pl.CostEstimate(flops=flops, bytes_accessed=1000000, transcendentals=0),
        compiler_params=pltpu.CompilerParams(vmem_limit_bytes=16 * 1024 * 1024),
    )(*args)


def local(traces, dirichlet, visc_class, viscosity, coarse_diag, solve_map, flux_map):
    wx, wy, z = traces.shape[2:]
    cells = wx * wy
    rows = 8 * (wy // 2 + 1)
    per_hex = 4 * 288 * 256 * z
    gather = jnp.asarray(gather_table())
    parts = jnp.asarray(slot_table())
    spread = jnp.asarray(spread_table(wy, rows))
    vm = pltpu.VMEM
    bind = lambda body: functools.partial(body, wx, wy)
    y_message = vm((48 * wx + 48 + tail_rows(8 * ((wx + 2) // 2) + 8 + 3 * wx + 4), z), BF)
    y_outer = vm((y_message.shape[0] + 16, z), BF)
    x_message = vm((48 * (wy + 2) + tail_rows(rows + 3 * wy + 4), z), BF)
    x_outer = vm((x_message.shape[0] + 16, z), BF)

    (lifted, nat, flags, visc, diag, s_map, s_turned, f_map, gather, parts, c1, va, v1a, v3, inner, outer) = call(
        bind(first_kernel),
        (
            viscosity, traces.reshape(3, 48 * cells, z), dirichlet.reshape(3, cells, z),
            visc_class.reshape(cells, z), coarse_diag.reshape(cells, z), solve_map.T, flux_map, gather, parts,
        ),
        (
            vm((4, cells, 48, z), BF), vm((3, 48 * cells, z), F32), vm((6, cells, z), F32), vm((viscosity.shape[0], z), F32), vm((cells, z), F32),
            vm(solve_map.shape, BF),
            vm(solve_map.shape[::-1], BF), vm(flux_map.shape, BF), vm(gather.shape, BF), vm(parts.shape, BF),
            vm((6, 2 * wx, 48, z), F32), vm((2, wx + 1, 8, z), F32), vm((2, 16, z), F32), vm((wx, 32, z), F32),
            y_message, y_outer,
        ),
        [
            y_message, y_message,
            vm((3, 48 * cells, z), BF), vm((3, cells, z), jnp.int32), vm((cells, z), jnp.int32),
            pltpu.SMEM(viscosity.shape, F32), pltpu.SemaphoreType.DMA((11,)),
        ],
        2 * wx * per_hex, True,
    )
    inner = swap(inner, "gy", "gx", 0)
    outer = swap(outer, "gy", "gx", 1)
    between = wx * (wy - 2)
    c2, vb, v1b, mx, my, own = call(
        bind(middle_kernel),
        (lifted, nat, flags, s_map, s_turned, f_map, gather, parts),
        (
            vm((6, between, 48, z), F32), vm((wy - 2, wx + 1, 8, z), F32), vm((wy - 2, 16, z), F32),
            vm((384, 48), BF), vm((384, 48), BF), vm((144, wx * z), F32),
        ),
        [vm((4, cells, 48, z), BF)], between * per_hex,
    )
    c3, vt, vl, v1, face, yd, yu, inner, outer = call(
        bind(turn_kernel),
        (
            visc, lifted, flags, diag, parts, my, own, c1, c2, va, vb, v1a, v1b, v3, inner, outer,
        ),
        (
            vm((2, 6, 48, z), F32), vm((2, 2, 8, z), F32), vm((2, 2, 8, z), F32), vm((wy + 2, 16, z), F32),
            vm((2, 48, z), F32), y_message, y_message, x_message, x_outer,
        ),
        [x_message, x_message], 2 * per_hex,
    )
    inner = swap(inner, "gx", "gy", 0)
    outer = swap(outer, "gx", "gy", 1)
    residual, vs, inverse, ownx = call(
        bind(assemble_kernel),
        (
            visc, lifted, flags, diag, parts, mx, my, own, c1, c2, c3, va, vb, v3, vt, vl, face, yd, yu,
        ),
        (
            vm((3, 48 * cells, z), F32), vm((wx + 1, rows, z), F32), vm((wx, rows, z), F32),
            vm((144, (wy + 2) * z), F32),
        ),
        [vm((wx - 2, 6, 48, z), F32)], 4 * per_hex,
    )
    out = call(
        bind(final_kernel),
        (
            visc, lifted, flags, parts, mx, ownx, residual, vs, inverse, v1, yd, yu, inner, outer, spread,
        ),
        jax.ShapeDtypeStruct((3, 48 * cells, z), BF),
        [vm((3, 48 * cells, z), BF), x_message, x_message, pltpu.SemaphoreType.DMA((3,))], 4 * spread.size * z,
        out_hbm=True,
    )
    return out.reshape(traces.shape)


def solution(mesh):
    in_specs = (
        P(None, None, "gx", "gy", None),
        P(None, "gx", "gy", None),
        P("gx", "gy", None),
        P(),
        P("gx", "gy", None),
        P(),
        P(),
    )
    out_specs = P(None, None, "gx", "gy", None)
    return jax.shard_map(local, mesh=mesh, in_specs=in_specs, out_specs=out_specs, check_vma=False)
```

```python
import functools
import math

import jax
import jax.numpy as jnp
import ml_dtypes
import numpy as np
from jax import lax
from jax.experimental import pallas as pl
from jax.experimental.pallas import tpu as pltpu
from jax.sharding import PartitionSpec as P

penalty = 0.5
BF = jnp.bfloat16
F32 = jnp.float32
lift = 1.3264
gain = 1.3280711361297461


def swap(value, axis, other, first):
    count, width = lax.axis_size(axis), lax.axis_size(other)
    place = (lambda i, j: i * width + j) if (axis, other) == ("gx", "gy") else (lambda i, j: j * count + i)
    lows = list(range(first, count - 1, 2))
    pairs = [(place(low, j), place(low + 1, j)) for low in lows for j in range(width)]
    alone = [i for i in range(count) if i not in lows and i - 1 not in lows]
    pairs += [(place(i, j), place(i, j + 1)) for i in alone for j in range(0, width - 1, 2)]
    return lax.ppermute(value, ("gx", "gy"), pairs + [(high, low) for low, high in pairs])


def even(axis):
    return lax.rem(lax.axis_index(axis), 2) == 0


def arrive(axis, inner_ref, outer_ref, down_ref, up_ref):
    here, last = lax.axis_index(axis), lax.axis_size(axis) - 1
    choose(even(axis), inner_ref, outer_ref, down_ref, here < last)
    choose(even(axis), outer_ref, inner_ref, up_ref, here > 0)


def depart(axis, down_ref, up_ref, inner_ref, outer_ref):
    choose(even(axis), up_ref, down_ref, inner_ref)
    choose(even(axis), down_ref, up_ref, outer_ref)


def choose(condition, yes_ref, no_ref, out_ref, present=None):
    size = min(yes_ref.shape[0], no_ref.shape[0], out_ref.shape[0])
    rows = pl.ds(0, size)
    value = jnp.where(condition, yes_ref[rows, :], no_ref[rows, :])
    out_ref[rows, :] = value if present is None else jnp.where(present, value, jnp.zeros_like(value))
    if out_ref.shape[0] > size:
        rest = pl.ds(size, out_ref.shape[0] - size)
        out_ref[rest, :] = jnp.zeros((out_ref.shape[0] - size, out_ref.shape[1]), out_ref.dtype)


def corner_table():
    gll_points = [-1.0, -math.sqrt(0.2), math.sqrt(0.2), 1.0]
    table = np.zeros((16, 4), np.float64)
    for s in range(4):
        for t in range(4):
            for p in range(2):
                for q in range(2):
                    table[4 * s + t, 2 * p + q] = (
                        (1 + (2 * p - 1) * gll_points[s]) * (1 + (2 * q - 1) * gll_points[t]) / 4
                    )
    return table


def landing(face_slot, high_s, high_t):
    direction, outward = divmod(face_slot, 2)
    if direction == 0:
        return (outward, high_s, high_t)
    if direction == 1:
        return (high_s, outward, high_t)
    return (high_s, high_t, outward)


def gather_table():
    weights = lift * corner_table()
    table = np.zeros((32, 288), np.float64)
    for slot in range(6):
        for s in range(2):
            for t in range(2):
                p, q, r = landing(slot, s, t)
                for c in range(3):
                    cols = slot * 48 + 16 * c + np.arange(16)
                    table[16 * r + 8 * p + 4 * q + c, cols] += weights[:, 2 * s + t]
    return table.astype(ml_dtypes.bfloat16)


def slot_table():
    slots = np.split(gather_table(), 6, axis=1)
    rows = [
        np.r_[0:8, 16:24], np.r_[8:16, 24:32], np.arange(32), np.arange(32), np.arange(16), np.arange(16, 32),
    ]
    return np.concatenate([slot[kept] for slot, kept in zip(slots, rows)], axis=0)


slot_rows = (0, 16, 32, 64, 96, 112, 128)


def spread_table(wy, rows):
    weights = lift * corner_table()
    table = np.zeros((3, 48, 2, wy, 6 * rows), np.float64)
    for d in range(3):
        for x in range(2):
            for y in range(wy):
                for s in range(2):
                    for t in range(2):
                        p, q, r = landing(2 * d, s, t)
                        for c in range(3):
                            k = (3 * r + x + p) * rows + 4 * (y + q) + c
                            table[d, 16 * c : 16 * c + 16, x, y, k] += weights[:, 2 * s + t]
    return table.reshape(-1, 6 * rows).astype(ml_dtypes.bfloat16)


def lanes(shape):
    return lax.broadcasted_iota(jnp.int32, shape, len(shape) - 1)


def z_next(value):
    last = value.shape[-1] - 1
    return jnp.where(lanes(value.shape) < last, pltpu.roll(value, last, value.ndim - 1), 0.0)


def z_prev(value):
    return jnp.where(lanes(value.shape) > 0, pltpu.roll(value, 1, value.ndim - 1), 0.0)


def dot(left, right):
    return jnp.dot(left, right, preferred_element_type=F32)


def wide(parts):
    return jnp.concatenate(parts, axis=1)


def tall(parts):
    return jnp.concatenate(parts, axis=0)


def hex_batch(slots, scales, m_ref):
    z = slots[0][0].shape[1]
    element = tall([wide([hexa[s] for hexa in slots]) for s in range(6)])
    rows = dot(m_ref[...], element)
    columns = [rows[:, z * h : z * h + z] for h in range(len(slots))]
    blocks = [[part[48 * s : 48 * s + 48] * scales[h][s] for s in range(6)] for h, part in enumerate(columns)]
    return blocks, [part[288:] for part in columns]


def vertex_part(flux, parts_ref):
    rows = []
    for s in range(6):
        first, size = slot_rows[s], slot_rows[s + 1] - slot_rows[s]
        rows.append(dot(parts_ref[pl.ds(first, size), :], flux[48 * s : 48 * s + 48].astype(BF)))
    rows[2:4] = [rows[2] + rows[3]]
    return tall(rows)


def product(f_ref, st_ref, slots):
    turned = st_ref[...] if slots is None else st_ref[pl.ds(48 * slots, 48), :]
    flux = lax.dot_general(f_ref[...], turned, (((1,), (1,)), ((), ())), preferred_element_type=F32)
    shift = 0 if slots is None else 48 * slots
    rows = lax.broadcasted_iota(jnp.int32, flux.shape, 0)
    columns = lax.broadcasted_iota(jnp.int32, flux.shape, 1)
    return flux, flux + jnp.where(rows == columns + shift, F32(penalty), F32(0.0))


def slot_corners(traces, parts_ref, slot):
    z = traces[0].shape[1]
    first, size = slot_rows[slot], slot_rows[slot + 1] - slot_rows[slot]
    rows = dot(parts_ref[pl.ds(first, size), :], wide([trace.astype(BF) for trace in traces]))
    return [rows[:, z * h : z * h + z] for h in range(len(traces))]


def settle(rows, p):
    return rows[8 * p : 8 * p + 8] + z_prev(rows[16 + 8 * p : 24 + 8 * p])


def scaled_corners(delta, scales, offsets=(0, 1)):
    shape = (8, delta.shape[1])
    blank = jnp.zeros((1, shape[1]), F32)
    y_scale = jnp.where(
        lax.broadcasted_iota(jnp.int32, shape, 0) < 4,
        blank if scales[2] is None else scales[2], blank if scales[3] is None else scales[3],
    )
    results = []
    for p in offsets:
        parts = []
        for r in range(2):
            at = 32 + 16 * r + 8 * p
            part = delta[at : at + 8] * y_scale + delta[at + 32 : at + 40] * scales[4 + r]
            if scales[p] is not None:
                part = part + delta[16 * p + 8 * r : 16 * p + 8 * r + 8] * scales[p]
            parts.append(part)
        results.append(parts[0] + z_prev(parts[1]))
    return results


def level_visc(code, visc_ref):
    visc = jnp.zeros(code.shape, F32)
    for level in range(visc_ref.shape[0]):
        visc = visc + jnp.where(code == F32(level + 1), visc_ref[pl.ds(level, 1), :], F32(0.0))
    return visc


def merge(even, odd):
    odd = tall(odd)
    return tall(even) + pltpu.roll(odd, odd.shape[0] - 4, 0)


def first_kernel(
    wx, wy, visc_hbm, t_hbm, dir_hbm, cls_hbm, diag_hbm, st_hbm, f_hbm, parts_hbm,
    l_ref, nat, kp_ref, visc_ref, diag_ref, m_ref, st_ref, f_ref, parts_ref, c_ref, v_ref, v1_ref, v3_ref,
    inner_ref, outer_ref, down_ref, up_ref, t_ref, dir_ref, cls_ref, levels, sems,
):
    cells = wx * wy
    pairs = [
        (st_hbm, st_ref), (f_hbm, f_ref), (parts_hbm, parts_ref), (dir_hbm, dir_ref), (t_hbm.at[0], t_ref.at[0]),
        (t_hbm.at[1], t_ref.at[1]), (t_hbm.at[2], t_ref.at[2]), (cls_hbm, cls_ref), (visc_hbm, levels),
        (diag_hbm, diag_ref),
    ]
    copies = [pltpu.make_async_copy(a, b, sems.at[i]) for i, (a, b) in enumerate(pairs)]
    for copy in copies:
        copy.start()
    for copy in copies[:3]:
        copy.wait()
    flux = product(f_ref, st_ref, None)[1].astype(BF)
    m_ref[pl.ds(0, 288), :] = flux
    m_ref[pl.ds(288, 96), :] = vertex_part(flux, parts_ref).astype(BF)
    copies[3].wait()
    z = t_ref.shape[2]
    for d in range(3):
        keep = (1 - dir_ref[d]).astype(F32)
        kp_ref[d] = keep
        copies[4 + d].wait()
        masked = t_ref[d].astype(F32).reshape(48, cells, z) * keep[None]
        nat[d] = masked.reshape(48 * cells, z)
        lay_out(wx, wy, d, nat, l_ref, True)
    kp_ref[3] = z_next(kp_ref[2])
    for copy in copies[7:]:
        copy.wait()
    for level in range(visc_ref.shape[0]):
        visc_ref[pl.ds(level, 1), :] = jnp.full((1, z), levels[level], F32)
    code = cls_ref[...].astype(F32) + 1.0
    kp_ref[4] = level_visc(code, visc_ref)
    kp_ref[5] = code
    row = lambda i, col: kp_ref[i, pl.ds(col, 1), :]
    blocks, corners = [], []
    for side, y in enumerate((0, wy - 1)):
        some, some_corners, alone = known_hexes(
            wx, wy, [(x, y) for x in range(wx)], (l_ref, None), kp_ref, m_ref, c_ref, len(blocks)
        )
        blocks += some
        corners += some_corners
        v1_ref[side] = alone[wx - 1][16:32]
    place = lax.broadcasted_iota(jnp.int32, (32, z), 0)
    for x in range(wx):
        v3_ref[x] = jnp.where(lax.rem(place, 8) < 4, 0.0, alone[x][32:64])
    sums = [line_sums(corners[:wx]), line_sums(corners[wx:])]
    for side in range(2):
        for i in range(wx + 1):
            v_ref[side, i] = sums[side][i]
    corner = (wx - 1) * wy
    top = wy - 1
    for x in range(wx):
        down_ref[pl.ds(48 * x, 48), :] = l_ref[1, x * wy]
        up_ref[pl.ds(48 * x, 48), :] = blocks[wx + x][3].astype(BF)
    down_ref[pl.ds(48 * wx, 48), :] = l_ref[0, 0]
    up_ref[pl.ds(48 * wx, 48), :] = l_ref[0, top]
    flags = [row(1, x * wy) for x in range(wx)] + [row(0, 0), row(5, corner), row(0, corner), row(2, corner)]
    diag = tall([diag_ref[pl.ds(x * wy, 1), :] for x in range(wx)])
    high = diag.astype(BF).astype(F32)
    rim = pack(sums[0], 0) + pack([v1_ref[0, 0:8], v1_ref[0, 8:16]], 0) + flags + [high, diag - high]
    put_tail(down_ref, 48 * wx + 48, rim)
    flags = [row(kind, x * wy + top) for kind in (5, 0, 2) for x in range(wx)]
    rim = pack(sums[1], 1) + pack([v1_ref[1, 0:8], v1_ref[1, 8:16]], 1) + flags
    put_tail(up_ref, 48 * wx + 48, rim)
    depart("gy", down_ref, up_ref, inner_ref, outer_ref)


def tail_rows(count):
    return -(-count // 16) * 16


def put_tail(ref, start, rows):
    count = sum(part.shape[0] for part in rows)
    full = ref.shape[0] - start
    if full > count:
        rows = rows + [jnp.zeros((full - count, rows[0].shape[1]), F32)]
    ref[pl.ds(start, full), :] = tall(rows).astype(BF)


def pack(parts, half):
    place = lax.broadcasted_iota(jnp.int32, parts[0].shape, 0)
    parts = parts + [jnp.zeros_like(parts[0])] * (len(parts) % 2)
    packed = []
    for low, high in zip(parts[0::2], parts[1::2]):
        if half:
            low = pltpu.roll(low, 4, 0)
        else:
            high = pltpu.roll(high, 4, 0)
        packed.append(jnp.where(place < 4, low, high))
    return packed


def unpack(packed, count, half):
    parts = []
    for n in range(count):
        part = packed[8 * (n // 2) : 8 * (n // 2) + 8]
        parts.append(part if n % 2 == half else pltpu.roll(part, 4, 0))
    return parts


def read_tail(ref, wx, half):
    start = 48 * wx + 48
    rows = ref[pl.ds(start, ref.shape[0] - start), :].astype(F32)
    size = 8 * ((wx + 2) // 2)
    return unpack(rows, wx + 1, half), unpack(rows[size : size + 8], 2, half), rows[size + 8 :]


def line_sums(corners):
    low, high = [part[0] for part in corners], [part[1] for part in corners]
    return [low[0]] + [low[x] + high[x - 1] for x in range(1, len(low))] + [high[-1]]


def early(wx, wy, d, x, y):
    return y in (0, wy - 1) or (d == 0 and x == 0) or (d == 1 and y == 1)


def lay_out(wx, wy, d, nat, l_ref, first):
    for x in range(wx):
        for y in range(wy):
            if early(wx, wy, d, x, y) == first:
                col = x * wy + y
                part = nat[d, pl.ds(col, 48, stride=wx * wy), :]
                l_ref[d, col] = part.astype(BF)
                if d == 2:
                    l_ref[3, col] = z_next(part).astype(BF)


def known_hexes(wx, wy, where, l_refs, kp_ref, m_ref, c_ref, start):
    z = l_refs[0].shape[3]
    nothing = jnp.zeros((48, z), BF)
    row = lambda i, col: kp_ref[i, pl.ds(col, 1), :]
    trace = lambda d, x, y: l_refs[0 if early(wx, wy, min(d, 2), x, y) else 1][d, x * wy + y]
    slots, scales, left_out = [], [], []
    for x, y in where:
        here = x * wy + y
        visc = row(4, here)
        last_x, last_y = x == wx - 1, y == wy - 1
        slots.append(
            [
                trace(0, x, y), nothing if last_x else trace(0, x + 1, y),
                trace(1, x, y), nothing if last_y else trace(1, x, y + 1),
                trace(2, x, y), trace(3, x, y),
            ]
        )
        scales.append(
            [
                visc * row(0, here), visc if last_x else visc * row(0, here + wy),
                visc * row(1, here), visc if last_y else visc * row(1, here + 1),
                visc * row(2, here), visc * row(3, here),
            ]
        )
        left_out.append(([1] if last_x else []) + ([3] if last_y else []))
    blocks, vertex = hex_batch(slots, scales, m_ref)
    corners, alone = [], []
    for h, (x, y) in enumerate(where):
        for s in range(6):
            c_ref[s, start + h] = blocks[h][s]
        used = [None if s in left_out[h] else scales[h][s] for s in range(6)]
        corners.append(scaled_corners(vertex[h], used))
        alone.append(vertex[h] * row(4, x * wy + y))
    return blocks, corners, alone


def middle_kernel(
    wx, wy, l_ref, nat, kp_ref, m_ref, st_ref, f_ref, parts_ref,
    c_ref, v_ref, v1_ref, mx_ref, my_ref, own_ref, rest_ref,
):
    z = l_ref.shape[3]
    for slot, ref in ((1, mx_ref), (3, my_ref)):
        bare, flux = product(f_ref, st_ref, slot)
        ref[pl.ds(0, 288), :] = bare.astype(BF)
        ref[pl.ds(288, 96), :] = vertex_part(flux, parts_ref).astype(BF)
    for d in range(3):
        lay_out(wx, wy, d, nat, rest_ref, False)
    own_ref[...] = dot(tall([my_ref[pl.ds(144, 48), :], my_ref[pl.ds(288, 96), :]]), wide([l_ref[1, x * wy] for x in range(wx)]))
    where = [(x, y) for y in range(1, wy - 1) for x in range(wx)]
    blocks, corners, alone = known_hexes(wx, wy, where, (l_ref, rest_ref), kp_ref, m_ref, c_ref, 0)
    for y in range(wy - 2):
        v1_ref[y] = alone[wx * y + wx - 1][16:32]
        for i, rows in enumerate(line_sums(corners[wx * y : wx * y + wx])):
            v_ref[y, i] = rows


def after_y(wx, wy, xs, visc_ref, l_ref, kp_ref, parts_ref, my_ref, own_ref, v3_ref, down_ref, up_ref):
    z = l_ref.shape[3]
    misc_d = read_tail(down_ref, wx, 0)[2]
    misc_u = read_tail(up_ref, wx, 1)[2]
    row = lambda i, col: kp_ref[i, pl.ds(col, 1), :]
    delta = dot(my_ref[...], wide([down_ref[pl.ds(48 * x, 48), :] for x in xs]))
    arrived = [up_ref[pl.ds(48 * x, 48), :].astype(F32) for x in xs]
    arrived_corners = slot_corners(arrived, parts_ref, 3)
    results = []
    for n, x in enumerate(xs):
        here = x * wy + wy - 1
        last = x == wx - 1
        part = delta[:, z * n : z * n + z]
        visc = row(4, here)
        scales = [
            visc * row(0, here), visc if last else visc * row(0, here + wy), visc * row(1, here),
            visc * misc_d[x : x + 1], visc * row(2, here), visc * row(3, here),
        ]
        flux = [part[48 * s : 48 * s + 48] * scales[s] for s in range(6)]
        used = [None if (s == 1 and last) else scales[s] for s in range(6)]
        known = v3_ref[x] * misc_d[x : x + 1]
        top = [rows + settle(known, p) for p, rows in enumerate(scaled_corners(part[288:384], used))]
        top_one = part[304:320] * visc
        here = x * wy
        visc = level_visc(misc_u[x : x + 1], visc_ref)
        flag = row(1, here)
        own = own_ref[:, pl.ds(z * x, z)]
        keep_z = misc_u[2 * wx + x : 2 * wx + x + 1]
        scales = [
            visc * misc_u[wx + x : wx + x + 1], None if last else visc * misc_u[wx + x + 1 : wx + x + 2],
            None, visc * flag, visc * keep_z, visc * z_next(keep_z),
        ]
        known = arrived_corners[n] * flag
        low = [rows + settle(known, p) for p, rows in enumerate(scaled_corners(own[48:144], scales))]
        low_one = own[64:80] * visc
        face = (arrived[n] + visc * (own[0:48] + penalty * l_ref[1, here].astype(F32))) * flag
        results.append((flux, top, top_one, low, low_one, face))
    return results


def turn_kernel(
    wx, wy, visc_ref, l_ref, kp_ref, diag_ref, parts_ref, my_ref, own_ref, c1_ref, c2_ref, va_ref, vb_ref,
    v1a_ref, v1b_ref, v3_ref, inner_in, outer_in,
    c3_ref, vt_ref, vl_ref, v1_ref, face_ref, yd_ref, yu_ref, inner_ref, outer_ref, down_ref, up_ref,
):
    z = l_ref.shape[3]
    arrive("gy", inner_in, outer_in, yd_ref, yu_ref)
    xs = (0, wx - 1)
    results = after_y(wx, wy, xs, visc_ref, l_ref, kp_ref, parts_ref, my_ref, own_ref, v3_ref, yd_ref, yu_ref)
    row = lambda i, col: kp_ref[i, pl.ds(col, 1), :]
    sums_d, one_d, misc_d = read_tail(yd_ref, wx, 0)
    sums_u, one_u, misc_u = read_tail(yu_ref, wx, 1)
    edge_high, edge_low = misc_d[wx + 4 : 2 * wx + 4], misc_d[2 * wx + 4 : 3 * wx + 4]
    for n, (flux, top, top_one, low, low_one, face) in enumerate(results):
        for s in range(6):
            c3_ref[n, s] = flux[s]
        face_ref[n] = face
        for p in range(2):
            vt_ref[n, p] = top[p]
            vl_ref[n, p] = low[p]
    flux, top, top_one, low, low_one, face = results[1]
    mine = tall(one_u) + low_one
    v1_ref[0] = mine
    v1_ref[1] = v1a_ref[0]
    for y in range(wy - 2):
        v1_ref[2 + y] = v1b_ref[y]
    v1_ref[wy] = v1a_ref[1] + top_one
    v1_ref[wy + 1] = tall(one_d)

    def plane(i, n, p):
        lines = [sums_u[i] + vl_ref[n, p], va_ref[0, i]]
        lines += [vb_ref[y, i] for y in range(wy - 2)]
        lines += [va_ref[1, i] + vt_ref[n, p], sums_d[i]]
        return merge(lines[1::2], lines[0::2])

    down_ref[pl.ds(0, 48), :] = yu_ref[pl.ds(48 * wx, 48), :]
    for y in range(wy):
        down_ref[pl.ds(48 + 48 * y, 48), :] = l_ref[0, y]
    down_ref[pl.ds(48 * (wy + 1), 48), :] = yd_ref[pl.ds(48 * wx, 48), :]
    diag = diag_ref[pl.ds(0, wy), :]
    high = diag.astype(BF).astype(F32)
    rim = [plane(0, 0, 0), high, edge_high[0:1], diag - high, edge_low[0:1]]
    rim += [misc_u[wx : wx + 1], kp_ref[0, 0:wy], misc_d[wx : wx + 1]]
    put_tail(down_ref, 48 * (wy + 2), rim)
    corner = (wx - 1) * wy
    up_ref[pl.ds(0, 48), :] = c1_ref[1, wx - 1].astype(BF)
    for y in range(1, wy - 1):
        up_ref[pl.ds(48 * y, 48), :] = c2_ref[1, wx * (y - 1) + wx - 1].astype(BF)
    up_ref[pl.ds(48 * (wy - 1), 48), :] = (c1_ref[1, 2 * wx - 1] + flux[1]).astype(BF)
    last = pl.ds(corner, wy)
    rim = [plane(wx, 1, 1), mine, *one_d]
    rim += [misc_u[wx - 1 : wx], kp_ref[5, last], misc_d[wx + 1 : wx + 2]]
    rim += [misc_u[3 * wx - 1 : 3 * wx], kp_ref[2, last], misc_d[wx + 3 : wx + 4]]
    rim += [kp_ref[1, last], misc_d[wx - 1 : wx]]
    put_tail(up_ref, 48 * wy, rim)
    depart("gx", down_ref, up_ref, inner_ref, outer_ref)


def assemble_kernel(
    wx, wy, visc_ref, l_ref, kp_ref, diag_ref, parts_ref, mx_ref, my_ref, own_ref, c1_ref, c2_ref, c3_ref,
    va_ref, vb_ref, v3_ref, vt_ref, vl_ref, face_ref, yd_ref, yu_ref,
    r_ref, v_ref, inv_ref, ownx_ref, mid,
):
    z = l_ref.shape[3]
    cells = wx * wy
    xs = tuple(range(1, wx - 1))
    results = after_y(wx, wy, xs, visc_ref, l_ref, kp_ref, parts_ref, my_ref, own_ref, v3_ref, yd_ref, yu_ref)
    for n, part in enumerate(results):
        for s in range(6):
            mid[n, s] = part[0][s]
    traces = [yu_ref[pl.ds(48 * wx, 48), :]] + [l_ref[0, y] for y in range(wy)] + [yd_ref[pl.ds(48 * wx, 48), :]]
    ownx_ref[...] = dot(tall([mx_ref[pl.ds(48, 48), :], mx_ref[pl.ds(288, 96), :]]), wide(traces))

    def contrib(slot, x, y):
        if 0 < y < wy - 1:
            return c2_ref[slot, wx * (y - 1) + x]
        if y == 0:
            return c1_ref[slot, x]
        extra = mid[x - 1, slot] if 0 < x < wx - 1 else c3_ref[0 if x == 0 else 1, slot]
        return c1_ref[slot, wx + x] + extra

    for x in range(wx):
        for y in range(wy):
            col = pl.ds(x * wy + y, 48, stride=cells)
            if x:
                r_ref[0, col, :] = contrib(0, x, y) + contrib(1, x - 1, y)
            else:
                r_ref[0, col, :] = contrib(0, x, y)
            if y:
                behind = contrib(3, x, y - 1)
            elif 0 < x < wx - 1:
                behind = results[x - 1][5]
            else:
                behind = face_ref[0 if x == 0 else 1]
            r_ref[1, col, :] = contrib(2, x, y) + behind
            r_ref[2, col, :] = contrib(4, x, y) + z_prev(contrib(5, x, y))
    sums_d, one_d, misc_d = read_tail(yd_ref, wx, 0)
    sums_u, one_u, misc_u = read_tail(yu_ref, wx, 1)
    edge_diag = misc_d[wx + 4 : 2 * wx + 4] + misc_d[2 * wx + 4 : 3 * wx + 4]

    def brought(which, i):
        held = vt_ref if which == 1 else vl_ref
        terms = []
        for x, p in ((i, 0), (i - 1, 1)):
            if x in (0, wx - 1):
                terms.append(held[0 if x == 0 else 1, p])
            elif 0 < x < wx - 1:
                terms.append(results[x - 1][which][p])
        return sum(terms[1:], terms[0])

    for i in range(wx + 1):
        lines = [sums_u[i] + brought(3, i), va_ref[0, i]]
        lines += [vb_ref[y, i] for y in range(wy - 2)]
        lines += [va_ref[1, i] + brought(1, i), sums_d[i]]
        v_ref[i] = merge(lines[1::2], lines[0::2])
        if i < wx:
            parts = [jnp.broadcast_to(diag_ref[pl.ds(i * wy + y, 1), :], (4, z)) for y in range(wy)]
            parts += [jnp.broadcast_to(edge_diag[i : i + 1], (4, z)), jnp.zeros((4, z), F32)]
            inv_ref[i] = reciprocal(tall(parts))


def reciprocal(diag):
    present = diag > 0.0
    return jnp.where(present, (1.0 / (gain * gain)) / jnp.where(present, diag, 1.0), 0.0)


def final_kernel(
    wx, wy, visc_ref, l_ref, kp_ref, parts_ref, mx_ref, ownx_ref, r_ref, v_ref, inv_ref, v1_ref,
    yd_ref, yu_ref, inner_in, outer_in, p_ref, out_hbm, held, xd_ref, xu_ref, sems,
):
    arrive("gx", inner_in, outer_in, xd_ref, xu_ref)
    cells, z = wx * wy, l_ref.shape[3]
    rows = v_ref.shape[1]
    row = lambda i, col: kp_ref[i, pl.ds(col, 1), :]
    traces = [xd_ref[pl.ds(48 * j, 48), :] for j in range(wy + 2)]
    delta = dot(mx_ref[pl.ds(288, 96), :], wide(traces))
    rim_x = xd_ref[pl.ds(48 * (wy + 2), xd_ref.shape[0] - 48 * (wy + 2)), :].astype(F32)
    rim_l = xu_ref[pl.ds(48 * wy, xu_ref.shape[0] - 48 * wy), :].astype(F32)
    misc_d = read_tail(yd_ref, wx, 0)[2]
    misc_u = read_tail(yu_ref, wx, 1)[2]
    flags_high = rim_x[rows + 2 * (wy + 1) : rows + 3 * wy + 4]
    corner = (wx - 1) * wy
    arrived = [xu_ref[pl.ds(48 * y, 48), :].astype(F32) for y in range(wy)]
    arrived_corners = slot_corners(arrived, parts_ref, 1)
    codes = rim_l[rows + 32 : rows + 32 + wy + 2]
    keep_z = rim_l[rows + 32 + wy + 2 : rows + 32 + 2 * (wy + 2)]
    keep_y = rim_l[rows + 32 + 2 * (wy + 2) : rows + 32 + 3 * (wy + 2) - 1]
    low_visc = level_visc(codes, visc_ref)
    low_keep_z = z_next(keep_z)
    lines = [[], [], []]
    high_scales = []
    for j in range(-1, wy + 1):
        n = j + 1
        part = delta[:, z * n : z * n + z]
        flag = flags_high[n : n + 1]
        if j < 0:
            visc = level_visc(misc_u[wx - 1 : wx], visc_ref)
            kz = misc_u[3 * wx - 1 : 3 * wx]
            keeps = [misc_u[2 * wx - 1 : 2 * wx], flag, None, row(1, corner), kz, z_next(kz)]
        elif j < wy:
            here = corner + j
            visc = row(4, here)
            high_y = row(1, here + 1) if j < wy - 1 else misc_d[wx - 1 : wx]
            keeps = [row(0, here), flag, row(1, here), high_y, row(2, here), row(3, here)]
        else:
            visc = level_visc(misc_d[wx + 1 : wx + 2], visc_ref)
            kz = misc_d[wx + 3 : wx + 4]
            keeps = [misc_d[wx + 2 : wx + 3], flag, misc_d[wx - 1 : wx], None, kz, z_next(kz)]
        scales = [None if keep is None else visc * keep for keep in keeps]
        corners = scaled_corners(part, scales)
        one = v1_ref[n] * flag
        lines[0].append(corners[0])
        lines[1].append(corners[1] + one[0:8] + z_prev(one[8:16]))
        high_scales.append(scales)
        own = ownx_ref[:, pl.ds(z * n, z)]
        visc = low_visc[n : n + 1]
        flag = misc_u[wx : wx + 1] if j < 0 else misc_d[wx : wx + 1] if j == wy else row(0, j)
        scales = [
            None, visc * flag, None if j < 0 else visc * keep_y[j : j + 1],
            None if j == wy else visc * keep_y[j + 1 : j + 2], visc * keep_z[n : n + 1], visc * low_keep_z[n : n + 1],
        ]
        corners = scaled_corners(own[48:144], scales, (1,))[0]
        if 0 <= j < wy:
            one = arrived_corners[j] * flag
            lines[2].append(corners + one[0:8] + z_prev(one[8:16]))
            face = (arrived[j] + visc * (own[0:48] + penalty * l_ref[0, j].astype(F32))) * flag
            r_ref[0, pl.ds(j, 48, stride=cells), :] += face
        else:
            at = rows + (0 if j < 0 else 16)
            one = rim_l[at : at + 16] * flag
            lines[2].append(corners + one[0:8] + z_prev(one[8:16]))
    low, before, first = [merge(part[1::2], part[0::2]) for part in lines]
    top = v_ref[wx] + before + rim_x[0:rows]
    values = [(v_ref[0] + first + rim_l[0:rows]) * inv_ref[0]]
    values += [v_ref[i] * inv_ref[i] for i in range(1, wx - 1)]
    values += [(v_ref[wx - 1] + low) * inv_ref[wx - 1]]
    diag = rim_x[rows : rows + wy + 1] + rim_x[rows + wy + 1 : rows + 2 * (wy + 1)]
    parts = [jnp.broadcast_to(diag[j : j + 1], (4, z)) for j in range(wy + 1)]
    values += [top * reciprocal(tall(parts + [jnp.zeros((rows - 4 * (wy + 1), z), F32)]))]
    low = [tall(values[x : x + 3]) for x in range(0, wx, 2)]
    rhs = tall([wide(low), wide([z_next(part) for part in low])]).astype(BF)
    delta = dot(mx_ref[pl.ds(0, 288), :], wide(traces[1 : wy + 1]))
    behind = dot(mx_ref[pl.ds(144, 48), :], traces[0]) * high_scales[0][3]
    for j in range(wy):
        col = pl.ds(corner + j, 48, stride=cells)
        part = delta[:, z * j : z * j + z]
        flux = [part[48 * s : 48 * s + 48] * high_scales[j + 1][s] for s in range(6)]
        r_ref[0, col, :] += flux[0]
        r_ref[1, col, :] += flux[2] + behind
        r_ref[2, col, :] += flux[4] + z_prev(flux[5])
        behind = flux[3]
    size = 96 * wy
    copies = []
    for d in range(3):
        spread = dot(p_ref[pl.ds(size * d, size), :], rhs)
        spread = jnp.concatenate(
            [spread[:, z * g : z * g + z].reshape(48, 2 * wy, z) for g in range(wx // 2)], axis=1
        )
        total = r_ref[d].reshape(48, cells, z) + spread * kp_ref[d][None]
        held[d] = total.reshape(48 * cells, z).astype(BF)
        copies.append(pltpu.make_async_copy(held.at[d], out_hbm.at[d], sems.at[d]))
        copies[d].start()
    for copy in copies:
        copy.wait()


def call(body, args, outs, scratch, flops, hbm=False, out_hbm=False):
    if hbm:
        args = tuple(pltpu.with_memory_space_constraint(a, pltpu.HBM) for a in args)
    keywords = dict(out_specs=pl.BlockSpec(memory_space=pltpu.HBM)) if out_hbm else {}
    return pl.pallas_call(
        body,
        **keywords,
        in_specs=[pl.BlockSpec(memory_space=pltpu.HBM if hbm else pltpu.VMEM)] * len(args),
        out_shape=outs,
        scratch_shapes=scratch,
        cost_estimate=pl.CostEstimate(flops=flops, bytes_accessed=1000000, transcendentals=0),
        compiler_params=pltpu.CompilerParams(vmem_limit_bytes=16 * 1024 * 1024),
    )(*args)


def local(traces, dirichlet, visc_class, viscosity, coarse_diag, solve_map, flux_map):
    wx, wy, z = traces.shape[2:]
    cells = wx * wy
    rows = 8 * (wy // 2 + 1)
    per_hex = 2 * 384 * 288 * z
    parts = jnp.asarray(slot_table())
    spread = jnp.asarray(spread_table(wy, rows))
    vm = pltpu.VMEM
    bind = lambda body: functools.partial(body, wx, wy)
    y_message = vm((48 * wx + 48 + tail_rows(8 * ((wx + 2) // 2) + 8 + 3 * wx + 4), z), BF)
    y_outer = vm((y_message.shape[0] + 16, z), BF)
    x_message = vm((48 * (wy + 2) + tail_rows(rows + 3 * wy + 4), z), BF)
    x_outer = vm((x_message.shape[0] + 16, z), BF)

    (lifted, nat, flags, visc, diag, m, s_turned, f_map, parts, c1, va, v1a, v3, inner, outer) = call(
        bind(first_kernel),
        (
            viscosity, traces.reshape(3, 48 * cells, z), dirichlet.reshape(3, cells, z),
            visc_class.reshape(cells, z), coarse_diag.reshape(cells, z), solve_map.T, flux_map, parts,
        ),
        (
            vm((4, cells, 48, z), BF), vm((3, 48 * cells, z), F32), vm((6, cells, z), F32), vm((viscosity.shape[0], z), F32), vm((cells, z), F32),
            vm((384, 288), BF), vm(solve_map.shape[::-1], BF), vm(flux_map.shape, BF), vm(parts.shape, BF),
            vm((6, 2 * wx, 48, z), F32), vm((2, wx + 1, 8, z), F32), vm((2, 16, z), F32), vm((wx, 32, z), F32),
            y_message, y_outer,
        ),
        [
            y_message, y_message,
            vm((3, 48 * cells, z), BF), vm((3, cells, z), jnp.int32), vm((cells, z), jnp.int32),
            pltpu.SMEM(viscosity.shape, F32), pltpu.SemaphoreType.DMA((10,)),
        ],
        2 * wx * per_hex, True,
    )
    inner = swap(inner, "gy", "gx", 0)
    outer = swap(outer, "gy", "gx", 1)
    between = wx * (wy - 2)
    c2, vb, v1b, mx, my, own = call(
        bind(middle_kernel),
        (lifted, nat, flags, m, s_turned, f_map, parts),
        (
            vm((6, between, 48, z), F32), vm((wy - 2, wx + 1, 8, z), F32), vm((wy - 2, 16, z), F32),
            vm((384, 48), BF), vm((384, 48), BF), vm((144, wx * z), F32),
        ),
        [vm((4, cells, 48, z), BF)], between * per_hex,
    )
    c3, vt, vl, v1, face, yd, yu, inner, outer = call(
        bind(turn_kernel),
        (
            visc, lifted, flags, diag, parts, my, own, c1, c2, va, vb, v1a, v1b, v3, inner, outer,
        ),
        (
            vm((2, 6, 48, z), F32), vm((2, 2, 8, z), F32), vm((2, 2, 8, z), F32), vm((wy + 2, 16, z), F32),
            vm((2, 48, z), F32), y_message, y_message, x_message, x_outer,
        ),
        [x_message, x_message], 2 * per_hex,
    )
    inner = swap(inner, "gx", "gy", 0)
    outer = swap(outer, "gx", "gy", 1)
    residual, vs, inverse, ownx = call(
        bind(assemble_kernel),
        (
            visc, lifted, flags, diag, parts, mx, my, own, c1, c2, c3, va, vb, v3, vt, vl, face, yd, yu,
        ),
        (
            vm((3, 48 * cells, z), F32), vm((wx + 1, rows, z), F32), vm((wx, rows, z), F32),
            vm((144, (wy + 2) * z), F32),
        ),
        [vm((wx - 2, 6, 48, z), F32)], 4 * per_hex,
    )
    out = call(
        bind(final_kernel),
        (
            visc, lifted, flags, parts, mx, ownx, residual, vs, inverse, v1, yd, yu, inner, outer, spread,
        ),
        jax.ShapeDtypeStruct((3, 48 * cells, z), BF),
        [vm((3, 48 * cells, z), BF), x_message, x_message, pltpu.SemaphoreType.DMA((3,))], 4 * spread.size * z,
        out_hbm=True,
    )
    return out.reshape(traces.shape)


def solution(mesh):
    in_specs = (
        P(None, None, "gx", "gy", None),
        P(None, "gx", "gy", None),
        P("gx", "gy", None),
        P(),
        P("gx", "gy", None),
        P(),
        P(),
    )
    out_specs = P(None, None, "gx", "gy", None)
    return jax.shard_map(local, mesh=mesh, in_specs=in_specs, out_specs=out_specs, check_vma=False)
```

```python
import functools
import math

import jax
import jax.numpy as jnp
import ml_dtypes
import numpy as np
from jax import lax
from jax.experimental import pallas as pl
from jax.experimental.pallas import tpu as pltpu
from jax.sharding import PartitionSpec as P

penalty = 0.5
BF = jnp.bfloat16
F32 = jnp.float32
lift = 1.3264
gain = 1.3280711361297461


def swap(value, axis, other, first):
    count, width = lax.axis_size(axis), lax.axis_size(other)
    place = (lambda i, j: i * width + j) if (axis, other) == ("gx", "gy") else (lambda i, j: j * count + i)
    lows = list(range(first, count - 1, 2))
    pairs = [(place(low, j), place(low + 1, j)) for low in lows for j in range(width)]
    alone = [i for i in range(count) if i not in lows and i - 1 not in lows]
    pairs += [(place(i, j), place(i, j + 1)) for i in alone for j in range(0, width - 1, 2)]
    return lax.ppermute(value, ("gx", "gy"), pairs + [(high, low) for low, high in pairs])


def even(axis):
    return lax.rem(lax.axis_index(axis), 2) == 0


def arrive(axis, inner_ref, outer_ref, down_ref, up_ref):
    here, last = lax.axis_index(axis), lax.axis_size(axis) - 1
    choose(even(axis), inner_ref, outer_ref, down_ref, here < last)
    choose(even(axis), outer_ref, inner_ref, up_ref, here > 0)


def depart(axis, down_ref, up_ref, inner_ref, outer_ref):
    choose(even(axis), up_ref, down_ref, inner_ref)
    choose(even(axis), down_ref, up_ref, outer_ref)


def choose(condition, yes_ref, no_ref, out_ref, present=None):
    size = min(yes_ref.shape[0], no_ref.shape[0], out_ref.shape[0])
    rows = pl.ds(0, size)
    value = jnp.where(condition, yes_ref[rows, :], no_ref[rows, :])
    out_ref[rows, :] = value if present is None else jnp.where(present, value, jnp.zeros_like(value))
    if out_ref.shape[0] > size:
        rest = pl.ds(size, out_ref.shape[0] - size)
        out_ref[rest, :] = jnp.zeros((out_ref.shape[0] - size, out_ref.shape[1]), out_ref.dtype)


def corner_table():
    gll_points = [-1.0, -math.sqrt(0.2), math.sqrt(0.2), 1.0]
    table = np.zeros((16, 4), np.float64)
    for s in range(4):
        for t in range(4):
            for p in range(2):
                for q in range(2):
                    table[4 * s + t, 2 * p + q] = (
                        (1 + (2 * p - 1) * gll_points[s]) * (1 + (2 * q - 1) * gll_points[t]) / 4
                    )
    return table


def landing(face_slot, high_s, high_t):
    direction, outward = divmod(face_slot, 2)
    if direction == 0:
        return (outward, high_s, high_t)
    if direction == 1:
        return (high_s, outward, high_t)
    return (high_s, high_t, outward)


def gather_table():
    weights = lift * corner_table()
    table = np.zeros((32, 288), np.float64)
    for slot in range(6):
        for s in range(2):
            for t in range(2):
                p, q, r = landing(slot, s, t)
                for c in range(3):
                    cols = slot * 48 + 16 * c + np.arange(16)
                    table[16 * r + 8 * p + 4 * q + c, cols] += weights[:, 2 * s + t]
    return table.astype(ml_dtypes.bfloat16)


def slot_table():
    slots = np.split(gather_table(), 6, axis=1)
    rows = [
        np.r_[0:8, 16:24], np.r_[8:16, 24:32], np.arange(32), np.arange(32), np.arange(16), np.arange(16, 32),
    ]
    return np.concatenate([slot[kept] for slot, kept in zip(slots, rows)], axis=0)


slot_rows = (0, 16, 32, 64, 96, 112, 128)


def penalty_table():
    slots = np.split(slot_table().astype(np.float64), slot_rows[1:6], axis=0)
    table = np.zeros((144, 288), np.float64)
    for s, first in enumerate((0, 16, 32, 32, 64, 80)):
        table[first : first + len(slots[s]), 48 * s : 48 * s + 48] += penalty * slots[s]
    table[96:, 144:192] = penalty * np.eye(48)
    return table.astype(ml_dtypes.bfloat16)


def spread_table(wy, rows):
    weights = lift * corner_table()
    table = np.zeros((3, 48, 2, wy, 6 * rows), np.float64)
    for d in range(3):
        for x in range(2):
            for y in range(wy):
                for s in range(2):
                    for t in range(2):
                        p, q, r = landing(2 * d, s, t)
                        for c in range(3):
                            k = (3 * r + x + p) * rows + 4 * (y + q) + c
                            table[d, 16 * c : 16 * c + 16, x, y, k] += weights[:, 2 * s + t]
    return table.reshape(-1, 6 * rows).astype(ml_dtypes.bfloat16)


def lanes(shape):
    return lax.broadcasted_iota(jnp.int32, shape, len(shape) - 1)


def z_next(value):
    last = value.shape[-1] - 1
    return jnp.where(lanes(value.shape) < last, pltpu.roll(value, last, value.ndim - 1), 0.0)


def z_prev(value):
    return jnp.where(lanes(value.shape) > 0, pltpu.roll(value, 1, value.ndim - 1), 0.0)


def dot(left, right):
    return jnp.dot(left, right, preferred_element_type=F32)


def wide(parts):
    return jnp.concatenate(parts, axis=1)


def tall(parts):
    return jnp.concatenate(parts, axis=0)


def columns(rows, count):
    z = rows.shape[1] // count
    return [rows[:, z * h : z * h + z] for h in range(count)]


def elements(slots):
    return tall([wide([hexa[s] for hexa in slots]) for s in range(6)])


def vertex_part(flux, parts_ref):
    rows = []
    for s in range(6):
        first, size = slot_rows[s], slot_rows[s + 1] - slot_rows[s]
        rows.append(dot(parts_ref[pl.ds(first, size), :], flux[48 * s : 48 * s + 48].astype(BF)))
    rows[2:4] = [rows[2] + rows[3]]
    return tall(rows)


def turned_dot(left, right):
    return lax.dot_general(left, right, (((1,), (1,)), ((), ())), preferred_element_type=F32)


def product(f_ref, st_ref, slot):
    first = 0 if slot is None else 48 * slot
    flux = turned_dot(f_ref[...], st_ref[...] if slot is None else st_ref[pl.ds(first, 48), :])
    rows = lax.broadcasted_iota(jnp.int32, flux.shape, 0)
    return flux, flux + jnp.where(rows == lax.broadcasted_iota(jnp.int32, flux.shape, 1) + first, F32(penalty), F32(0.0))


def slot_corners(traces, parts_ref, slot):
    z = traces[0].shape[1]
    first, size = slot_rows[slot], slot_rows[slot + 1] - slot_rows[slot]
    rows = dot(parts_ref[pl.ds(first, size), :], wide([trace.astype(BF) for trace in traces]))
    return [rows[:, z * h : z * h + z] for h in range(len(traces))]


def settle(rows, p):
    return rows[8 * p : 8 * p + 8] + z_prev(rows[16 + 8 * p : 24 + 8 * p])


def scaled_corners(delta, scales, offsets=(0, 1)):
    shape = (8, delta.shape[1])
    blank = jnp.zeros((1, shape[1]), F32)
    y_scale = jnp.where(
        lax.broadcasted_iota(jnp.int32, shape, 0) < 4,
        blank if scales[2] is None else scales[2], blank if scales[3] is None else scales[3],
    )
    results = []
    for p in offsets:
        parts = []
        for r in range(2):
            at = 32 + 16 * r + 8 * p
            part = delta[at : at + 8] * y_scale + delta[at + 32 : at + 40] * scales[4 + r]
            if scales[p] is not None:
                part = part + delta[16 * p + 8 * r : 16 * p + 8 * r + 8] * scales[p]
            parts.append(part)
        results.append(parts[0] + z_prev(parts[1]))
    return results


def level_visc(code, visc_ref):
    visc = jnp.zeros(code.shape, F32)
    for level in range(visc_ref.shape[0]):
        visc = visc + jnp.where(code == F32(level + 1), visc_ref[pl.ds(level, 1), :], F32(0.0))
    return visc


def merge(even, odd):
    odd = tall(odd)
    return tall(even) + pltpu.roll(odd, odd.shape[0] - 4, 0)


def first_kernel(
    wx, wy, visc_hbm, t_hbm, dir_hbm, cls_hbm, diag_hbm, st_hbm, f_hbm, parts_hbm, own_hbm,
    l_ref, nat, kp_ref, visc_ref, diag_ref, st_ref, f_ref, parts_ref, v_ref, v1_ref, v3_ref,
    inner_ref, outer_ref, down_ref, up_ref, own_ref, t_ref, dir_ref, cls_ref, levels, sems,
):
    cells = wx * wy
    pairs = [
        (f_hbm, f_ref), (parts_hbm, parts_ref), (st_hbm, st_ref), (own_hbm, own_ref), (dir_hbm, dir_ref), (t_hbm.at[0], t_ref.at[0]),
        (t_hbm.at[1], t_ref.at[1]), (t_hbm.at[2], t_ref.at[2]), (cls_hbm, cls_ref), (visc_hbm, levels),
        (diag_hbm, diag_ref),
    ]
    copies = [pltpu.make_async_copy(a, b, sems.at[i]) for i, (a, b) in enumerate(pairs)]
    for copy in copies:
        copy.start()
    copies[0].wait()
    copies[1].wait()
    left = tall([vertex_part(f_ref[...], parts_ref).astype(BF), f_ref[pl.ds(144, 48), :]])
    copies[2].wait()
    copies[3].wait()
    short = (turned_dot(left, st_ref[...]) + own_ref[...].astype(F32)).astype(BF)
    copies[4].wait()
    z = t_ref.shape[2]
    for d in range(3):
        keep = (1 - dir_ref[d]).astype(F32)
        kp_ref[d] = keep
        copies[5 + d].wait()
        masked = t_ref[d].astype(F32).reshape(48, cells, z) * keep[None]
        nat[d] = masked.reshape(48 * cells, z)
        lay_out(wx, wy, d, nat, l_ref, True)
    kp_ref[3] = z_next(kp_ref[2])
    for copy in copies[8:]:
        copy.wait()
    for level in range(visc_ref.shape[0]):
        visc_ref[pl.ds(level, 1), :] = jnp.full((1, z), levels[level], F32)
    code = cls_ref[...].astype(F32) + 1.0
    kp_ref[4] = level_visc(code, visc_ref)
    kp_ref[5] = code
    row = lambda i, col: kp_ref[i, pl.ds(col, 1), :]
    corners = []
    for side, y in enumerate((0, wy - 1)):
        where = [(x, y) for x in range(wx)]
        slots, scales, left_out = known_hexes(wx, wy, where, (l_ref, None), kp_ref)
        rows = columns(dot(short if side else short[0:96], elements(slots)), wx)
        corners += known_corners(rows, scales, left_out)
        v1_ref[side] = rows[wx - 1][16:32] * row(4, (wx - 1) * wy + y)
    place = lax.broadcasted_iota(jnp.int32, (32, z), 0)
    lone = [part * row(4, x * wy + wy - 1) for x, part in enumerate(rows)]
    for x in range(wx):
        v3_ref[x] = jnp.where(lax.rem(place, 8) < 4, 0.0, lone[x][32:64])
    sums = [line_sums(corners[:wx]), line_sums(corners[wx:])]
    for side in range(2):
        for i in range(wx + 1):
            v_ref[side, i] = sums[side][i]
    corner = (wx - 1) * wy
    top = wy - 1
    for x in range(wx):
        down_ref[pl.ds(48 * x, 48), :] = l_ref[1, x * wy]
        up_ref[pl.ds(48 * x, 48), :] = lone[x][96:144].astype(BF)
    down_ref[pl.ds(48 * wx, 48), :] = l_ref[0, 0]
    up_ref[pl.ds(48 * wx, 48), :] = l_ref[0, top]
    flags = [row(1, x * wy) for x in range(wx)] + [row(0, 0), row(5, corner), row(0, corner), row(2, corner)]
    diag = tall([diag_ref[pl.ds(x * wy, 1), :] for x in range(wx)])
    high = diag.astype(BF).astype(F32)
    rim = pack(sums[0], 0) + pack([v1_ref[0, 0:8], v1_ref[0, 8:16]], 0) + flags + [high, diag - high]
    put_tail(down_ref, 48 * wx + 48, rim)
    flags = [row(kind, x * wy + top) for kind in (5, 0, 2) for x in range(wx)]
    rim = pack(sums[1], 1) + pack([v1_ref[1, 0:8], v1_ref[1, 8:16]], 1) + flags
    put_tail(up_ref, 48 * wx + 48, rim)
    depart("gy", down_ref, up_ref, inner_ref, outer_ref)


def tail_rows(count):
    return -(-count // 16) * 16


def put_tail(ref, start, rows):
    count = sum(part.shape[0] for part in rows)
    full = ref.shape[0] - start
    if full > count:
        rows = rows + [jnp.zeros((full - count, rows[0].shape[1]), F32)]
    ref[pl.ds(start, full), :] = tall(rows).astype(BF)


def pack(parts, half):
    place = lax.broadcasted_iota(jnp.int32, parts[0].shape, 0)
    parts = parts + [jnp.zeros_like(parts[0])] * (len(parts) % 2)
    packed = []
    for low, high in zip(parts[0::2], parts[1::2]):
        if half:
            low = pltpu.roll(low, 4, 0)
        else:
            high = pltpu.roll(high, 4, 0)
        packed.append(jnp.where(place < 4, low, high))
    return packed


def unpack(packed, count, half):
    parts = []
    for n in range(count):
        part = packed[8 * (n // 2) : 8 * (n // 2) + 8]
        parts.append(part if n % 2 == half else pltpu.roll(part, 4, 0))
    return parts


def read_tail(ref, wx, half):
    start = 48 * wx + 48
    rows = ref[pl.ds(start, ref.shape[0] - start), :].astype(F32)
    size = 8 * ((wx + 2) // 2)
    return unpack(rows, wx + 1, half), unpack(rows[size : size + 8], 2, half), rows[size + 8 :]


def line_sums(corners):
    low, high = [part[0] for part in corners], [part[1] for part in corners]
    return [low[0]] + [low[x] + high[x - 1] for x in range(1, len(low))] + [high[-1]]


def early(wx, wy, d, x, y):
    return y in (0, wy - 1) or (d == 0 and x == 0) or (d == 1 and y == 1)


def lay_out(wx, wy, d, nat, l_ref, first):
    for x in range(wx):
        for y in range(wy):
            if early(wx, wy, d, x, y) == first:
                col = x * wy + y
                part = nat[d, pl.ds(col, 48, stride=wx * wy), :]
                l_ref[d, col] = part.astype(BF)
                if d == 2:
                    l_ref[3, col] = z_next(part).astype(BF)


def known_hexes(wx, wy, where, l_refs, kp_ref):
    z = l_refs[0].shape[3]
    nothing = jnp.zeros((48, z), BF)
    row = lambda i, col: kp_ref[i, pl.ds(col, 1), :]
    trace = lambda d, x, y: l_refs[0 if early(wx, wy, min(d, 2), x, y) else 1][d, x * wy + y]
    slots, scales, left_out = [], [], []
    for x, y in where:
        here = x * wy + y
        visc = row(4, here)
        last_x, last_y = x == wx - 1, y == wy - 1
        slots.append(
            [
                trace(0, x, y), nothing if last_x else trace(0, x + 1, y),
                trace(1, x, y), nothing if last_y else trace(1, x, y + 1),
                trace(2, x, y), trace(3, x, y),
            ]
        )
        scales.append(
            [
                visc * row(0, here), visc if last_x else visc * row(0, here + wy),
                visc * row(1, here), visc if last_y else visc * row(1, here + 1),
                visc * row(2, here), visc * row(3, here),
            ]
        )
        left_out.append(([1] if last_x else []) + ([3] if last_y else []))
    return slots, scales, left_out


def known_corners(vertex, scales, left_out):
    return [
        scaled_corners(part, [None if s in out else scale[s] for s in range(6)])
        for part, scale, out in zip(vertex, scales, left_out)
    ]


def middle_kernel(
    wx, wy, l_ref, nat, kp_ref, st_ref, f_ref, parts_ref,
    c_ref, v_ref, v1_ref, mx_ref, my_ref, own_ref, rest_ref, m_ref, lost_ref,
):
    for slot, ref in ((1, mx_ref), (3, my_ref)):
        bare, flux = product(f_ref, st_ref, slot)
        ref[pl.ds(0, 288), :] = bare.astype(BF)
        ref[pl.ds(288, 96), :] = vertex_part(flux, parts_ref).astype(BF)
    flux = product(f_ref, st_ref, None)[1]
    m_ref[pl.ds(0, 288), :] = flux.astype(BF)
    m_ref[pl.ds(288, 96), :] = vertex_part(flux, parts_ref).astype(BF)
    lost_ref[...] = (flux - flux.astype(BF).astype(F32))[:, 0:256].astype(BF)
    for d in range(3):
        lay_out(wx, wy, d, nat, rest_ref, False)
    own_ref[...] = dot(
        tall([my_ref[pl.ds(144, 48), :], my_ref[pl.ds(288, 96), :]]), wide([l_ref[1, x * wy] for x in range(wx)])
    )
    for y in range(wy):
        inside = 0 < y < wy - 1
        where = [(x, y) for x in range(wx)]
        slots, scales, left_out = known_hexes(wx, wy, where, (l_ref, rest_ref), kp_ref)
        element = elements(slots)
        rows = dot(m_ref[...] if inside else m_ref[pl.ds(0, 288), :], element)
        lost = columns(dot(lost_ref[...], element[0:256]), wx)
        rows = columns(rows, wx)
        for x in range(wx):
            for s in range(6):
                part = slice(48 * s, 48 * s + 48)
                c_ref[s, x * wy + y] = (rows[x][part] + lost[x][part]) * scales[x][s]
        if inside:
            corners = known_corners([part[288:] for part in rows], scales, left_out)
            v1_ref[y - 1] = rows[wx - 1][304:320] * kp_ref[4, pl.ds((wx - 1) * wy + y, 1), :]
            for i, part in enumerate(line_sums(corners)):
                v_ref[y - 1, i] = part


def after_y(wx, wy, xs, visc_ref, l_ref, kp_ref, parts_ref, my_ref, own_ref, v3_ref, down_ref, up_ref):
    z = l_ref.shape[3]
    misc_d = read_tail(down_ref, wx, 0)[2]
    misc_u = read_tail(up_ref, wx, 1)[2]
    row = lambda i, col: kp_ref[i, pl.ds(col, 1), :]
    delta = dot(my_ref[...], wide([down_ref[pl.ds(48 * x, 48), :] for x in xs]))
    arrived = [up_ref[pl.ds(48 * x, 48), :].astype(F32) for x in xs]
    arrived_corners = slot_corners(arrived, parts_ref, 3)
    results = []
    for n, x in enumerate(xs):
        here = x * wy + wy - 1
        last = x == wx - 1
        part = delta[:, z * n : z * n + z]
        visc = row(4, here)
        scales = [
            visc * row(0, here), visc if last else visc * row(0, here + wy), visc * row(1, here),
            visc * misc_d[x : x + 1], visc * row(2, here), visc * row(3, here),
        ]
        flux = [part[48 * s : 48 * s + 48] * scales[s] for s in range(6)]
        used = [None if (s == 1 and last) else scales[s] for s in range(6)]
        known = v3_ref[x] * misc_d[x : x + 1]
        top = [rows + settle(known, p) for p, rows in enumerate(scaled_corners(part[288:384], used))]
        top_one = part[304:320] * visc
        here = x * wy
        visc = level_visc(misc_u[x : x + 1], visc_ref)
        flag = row(1, here)
        own = own_ref[:, pl.ds(z * x, z)]
        keep_z = misc_u[2 * wx + x : 2 * wx + x + 1]
        scales = [
            visc * misc_u[wx + x : wx + x + 1], None if last else visc * misc_u[wx + x + 1 : wx + x + 2],
            None, visc * flag, visc * keep_z, visc * z_next(keep_z),
        ]
        known = arrived_corners[n] * flag
        low = [rows + settle(known, p) for p, rows in enumerate(scaled_corners(own[48:144], scales))]
        low_one = own[64:80] * visc
        face = (arrived[n] + visc * (own[0:48] + penalty * l_ref[1, here].astype(F32))) * flag
        results.append((flux, top, top_one, low, low_one, face))
    return results


def turn_kernel(
    wx, wy, visc_ref, l_ref, kp_ref, diag_ref, parts_ref, my_ref, own_ref, c_ref, va_ref, vb_ref,
    v1a_ref, v1b_ref, v3_ref, inner_in, outer_in,
    c3_ref, vt_ref, vl_ref, v1_ref, face_ref, yd_ref, yu_ref, inner_ref, outer_ref, down_ref, up_ref,
):
    z = l_ref.shape[3]
    arrive("gy", inner_in, outer_in, yd_ref, yu_ref)
    xs = (0, wx - 1)
    results = after_y(wx, wy, xs, visc_ref, l_ref, kp_ref, parts_ref, my_ref, own_ref, v3_ref, yd_ref, yu_ref)
    row = lambda i, col: kp_ref[i, pl.ds(col, 1), :]
    sums_d, one_d, misc_d = read_tail(yd_ref, wx, 0)
    sums_u, one_u, misc_u = read_tail(yu_ref, wx, 1)
    edge_high, edge_low = misc_d[wx + 4 : 2 * wx + 4], misc_d[2 * wx + 4 : 3 * wx + 4]
    for n, (flux, top, top_one, low, low_one, face) in enumerate(results):
        for s in range(6):
            c3_ref[n, s] = flux[s]
        face_ref[n] = face
        for p in range(2):
            vt_ref[n, p] = top[p]
            vl_ref[n, p] = low[p]
    flux, top, top_one, low, low_one, face = results[1]
    mine = tall(one_u) + low_one
    v1_ref[0] = mine
    v1_ref[1] = v1a_ref[0]
    for y in range(wy - 2):
        v1_ref[2 + y] = v1b_ref[y]
    v1_ref[wy] = v1a_ref[1] + top_one
    v1_ref[wy + 1] = tall(one_d)

    def plane(i, n, p):
        lines = [sums_u[i] + vl_ref[n, p], va_ref[0, i]]
        lines += [vb_ref[y, i] for y in range(wy - 2)]
        lines += [va_ref[1, i] + vt_ref[n, p], sums_d[i]]
        return merge(lines[1::2], lines[0::2])

    down_ref[pl.ds(0, 48), :] = yu_ref[pl.ds(48 * wx, 48), :]
    for y in range(wy):
        down_ref[pl.ds(48 + 48 * y, 48), :] = l_ref[0, y]
    down_ref[pl.ds(48 * (wy + 1), 48), :] = yd_ref[pl.ds(48 * wx, 48), :]
    diag = diag_ref[pl.ds(0, wy), :]
    high = diag.astype(BF).astype(F32)
    rim = [plane(0, 0, 0), high, edge_high[0:1], diag - high, edge_low[0:1]]
    rim += [misc_u[wx : wx + 1], kp_ref[0, 0:wy], misc_d[wx : wx + 1]]
    put_tail(down_ref, 48 * (wy + 2), rim)
    corner = (wx - 1) * wy
    for y in range(wy):
        part = c_ref[1, corner + y]
        up_ref[pl.ds(48 * y, 48), :] = (part + flux[1] if y == wy - 1 else part).astype(BF)
    last = pl.ds(corner, wy)
    rim = [plane(wx, 1, 1), mine, *one_d]
    rim += [misc_u[wx - 1 : wx], kp_ref[5, last], misc_d[wx + 1 : wx + 2]]
    rim += [misc_u[3 * wx - 1 : 3 * wx], kp_ref[2, last], misc_d[wx + 3 : wx + 4]]
    rim += [kp_ref[1, last], misc_d[wx - 1 : wx]]
    put_tail(up_ref, 48 * wy, rim)
    depart("gx", down_ref, up_ref, inner_ref, outer_ref)


def assemble_kernel(
    wx, wy, visc_ref, l_ref, kp_ref, diag_ref, parts_ref, mx_ref, my_ref, own_ref, c_ref, c3_ref,
    va_ref, vb_ref, v3_ref, vt_ref, vl_ref, face_ref, yd_ref, yu_ref,
    r_ref, v_ref, inv_ref, ownx_ref, mid,
):
    z = l_ref.shape[3]
    cells = wx * wy
    xs = tuple(range(1, wx - 1))
    results = after_y(wx, wy, xs, visc_ref, l_ref, kp_ref, parts_ref, my_ref, own_ref, v3_ref, yd_ref, yu_ref)
    for n, part in enumerate(results):
        for s in range(6):
            mid[n, s] = part[0][s]
    traces = [yu_ref[pl.ds(48 * wx, 48), :]] + [l_ref[0, y] for y in range(wy)] + [yd_ref[pl.ds(48 * wx, 48), :]]
    ownx_ref[...] = dot(tall([mx_ref[pl.ds(48, 48), :], mx_ref[pl.ds(288, 96), :]]), wide(traces))

    def contrib(slot, x, y):
        here = c_ref[slot, x * wy + y]
        if y < wy - 1:
            return here
        return here + (mid[x - 1, slot] if 0 < x < wx - 1 else c3_ref[0 if x == 0 else 1, slot])

    for x in range(wx):
        for y in range(wy):
            col = pl.ds(x * wy + y, 48, stride=cells)
            if x:
                r_ref[0, col, :] = contrib(0, x, y) + contrib(1, x - 1, y)
            else:
                r_ref[0, col, :] = contrib(0, x, y)
            if y:
                behind = contrib(3, x, y - 1)
            elif 0 < x < wx - 1:
                behind = results[x - 1][5]
            else:
                behind = face_ref[0 if x == 0 else 1]
            r_ref[1, col, :] = contrib(2, x, y) + behind
            r_ref[2, col, :] = contrib(4, x, y) + z_prev(contrib(5, x, y))
    sums_d, one_d, misc_d = read_tail(yd_ref, wx, 0)
    sums_u, one_u, misc_u = read_tail(yu_ref, wx, 1)
    edge_diag = misc_d[wx + 4 : 2 * wx + 4] + misc_d[2 * wx + 4 : 3 * wx + 4]

    def brought(which, i):
        held = vt_ref if which == 1 else vl_ref
        terms = []
        for x, p in ((i, 0), (i - 1, 1)):
            if x in (0, wx - 1):
                terms.append(held[0 if x == 0 else 1, p])
            elif 0 < x < wx - 1:
                terms.append(results[x - 1][which][p])
        return sum(terms[1:], terms[0])

    for i in range(wx + 1):
        lines = [sums_u[i] + brought(3, i), va_ref[0, i]]
        lines += [vb_ref[y, i] for y in range(wy - 2)]
        lines += [va_ref[1, i] + brought(1, i), sums_d[i]]
        v_ref[i] = merge(lines[1::2], lines[0::2])
        if i < wx:
            parts = [jnp.broadcast_to(diag_ref[pl.ds(i * wy + y, 1), :], (4, z)) for y in range(wy)]
            parts += [jnp.broadcast_to(edge_diag[i : i + 1], (4, z)), jnp.zeros((4, z), F32)]
            inv_ref[i] = reciprocal(tall(parts))


def reciprocal(diag):
    present = diag > 0.0
    return jnp.where(present, (1.0 / (gain * gain)) / jnp.where(present, diag, 1.0), 0.0)


def final_kernel(
    wx, wy, visc_ref, l_ref, kp_ref, parts_ref, mx_ref, ownx_ref, r_ref, v_ref, inv_ref, v1_ref,
    yd_ref, yu_ref, inner_in, outer_in, p_ref, out_hbm, held, xd_ref, xu_ref, sems,
):
    arrive("gx", inner_in, outer_in, xd_ref, xu_ref)
    cells, z = wx * wy, l_ref.shape[3]
    rows = v_ref.shape[1]
    row = lambda i, col: kp_ref[i, pl.ds(col, 1), :]
    traces = [xd_ref[pl.ds(48 * j, 48), :] for j in range(wy + 2)]
    delta = dot(mx_ref[pl.ds(288, 96), :], wide(traces))
    rim_x = xd_ref[pl.ds(48 * (wy + 2), xd_ref.shape[0] - 48 * (wy + 2)), :].astype(F32)
    rim_l = xu_ref[pl.ds(48 * wy, xu_ref.shape[0] - 48 * wy), :].astype(F32)
    misc_d = read_tail(yd_ref, wx, 0)[2]
    misc_u = read_tail(yu_ref, wx, 1)[2]
    flags_high = rim_x[rows + 2 * (wy + 1) : rows + 3 * wy + 4]
    corner = (wx - 1) * wy
    arrived = [xu_ref[pl.ds(48 * y, 48), :].astype(F32) for y in range(wy)]
    arrived_corners = slot_corners(arrived, parts_ref, 1)
    codes = rim_l[rows + 32 : rows + 32 + wy + 2]
    keep_z = rim_l[rows + 32 + wy + 2 : rows + 32 + 2 * (wy + 2)]
    keep_y = rim_l[rows + 32 + 2 * (wy + 2) : rows + 32 + 3 * (wy + 2) - 1]
    low_visc = level_visc(codes, visc_ref)
    low_keep_z = z_next(keep_z)
    lines = [[], [], []]
    high_scales = []
    for j in range(-1, wy + 1):
        n = j + 1
        part = delta[:, z * n : z * n + z]
        flag = flags_high[n : n + 1]
        if j < 0:
            visc = level_visc(misc_u[wx - 1 : wx], visc_ref)
            kz = misc_u[3 * wx - 1 : 3 * wx]
            keeps = [misc_u[2 * wx - 1 : 2 * wx], flag, None, row(1, corner), kz, z_next(kz)]
        elif j < wy:
            here = corner + j
            visc = row(4, here)
            high_y = row(1, here + 1) if j < wy - 1 else misc_d[wx - 1 : wx]
            keeps = [row(0, here), flag, row(1, here), high_y, row(2, here), row(3, here)]
        else:
            visc = level_visc(misc_d[wx + 1 : wx + 2], visc_ref)
            kz = misc_d[wx + 3 : wx + 4]
            keeps = [misc_d[wx + 2 : wx + 3], flag, misc_d[wx - 1 : wx], None, kz, z_next(kz)]
        scales = [None if keep is None else visc * keep for keep in keeps]
        corners = scaled_corners(part, scales)
        one = v1_ref[n] * flag
        lines[0].append(corners[0])
        lines[1].append(corners[1] + one[0:8] + z_prev(one[8:16]))
        high_scales.append(scales)
        own = ownx_ref[:, pl.ds(z * n, z)]
        visc = low_visc[n : n + 1]
        flag = misc_u[wx : wx + 1] if j < 0 else misc_d[wx : wx + 1] if j == wy else row(0, j)
        scales = [
            None, visc * flag, None if j < 0 else visc * keep_y[j : j + 1],
            None if j == wy else visc * keep_y[j + 1 : j + 2], visc * keep_z[n : n + 1], visc * low_keep_z[n : n + 1],
        ]
        corners = scaled_corners(own[48:144], scales, (1,))[0]
        if 0 <= j < wy:
            one = arrived_corners[j] * flag
            lines[2].append(corners + one[0:8] + z_prev(one[8:16]))
            face = (arrived[j] + visc * (own[0:48] + penalty * l_ref[0, j].astype(F32))) * flag
            r_ref[0, pl.ds(j, 48, stride=cells), :] += face
        else:
            at = rows + (0 if j < 0 else 16)
            one = rim_l[at : at + 16] * flag
            lines[2].append(corners + one[0:8] + z_prev(one[8:16]))
    low, before, first = [merge(part[1::2], part[0::2]) for part in lines]
    top = v_ref[wx] + before + rim_x[0:rows]
    values = [(v_ref[0] + first + rim_l[0:rows]) * inv_ref[0]]
    values += [v_ref[i] * inv_ref[i] for i in range(1, wx - 1)]
    values += [(v_ref[wx - 1] + low) * inv_ref[wx - 1]]
    diag = rim_x[rows : rows + wy + 1] + rim_x[rows + wy + 1 : rows + 2 * (wy + 1)]
    parts = [jnp.broadcast_to(diag[j : j + 1], (4, z)) for j in range(wy + 1)]
    values += [top * reciprocal(tall(parts + [jnp.zeros((rows - 4 * (wy + 1), z), F32)]))]
    low = [tall(values[x : x + 3]) for x in range(0, wx, 2)]
    rhs = tall([wide(low), wide([z_next(part) for part in low])]).astype(BF)
    delta = dot(mx_ref[pl.ds(0, 288), :], wide(traces[1 : wy + 1]))
    behind = dot(mx_ref[pl.ds(144, 48), :], traces[0]) * high_scales[0][3]
    for j in range(wy):
        col = pl.ds(corner + j, 48, stride=cells)
        part = delta[:, z * j : z * j + z]
        flux = [part[48 * s : 48 * s + 48] * high_scales[j + 1][s] for s in range(6)]
        r_ref[0, col, :] += flux[0]
        r_ref[1, col, :] += flux[2] + behind
        r_ref[2, col, :] += flux[4] + z_prev(flux[5])
        behind = flux[3]
    size = 96 * wy
    copies = []
    for d in range(3):
        spread = dot(p_ref[pl.ds(size * d, size), :], rhs)
        spread = jnp.concatenate(
            [spread[:, z * g : z * g + z].reshape(48, 2 * wy, z) for g in range(wx // 2)], axis=1
        )
        total = r_ref[d].reshape(48, cells, z) + spread * kp_ref[d][None]
        held[d] = total.reshape(48 * cells, z).astype(BF)
        copies.append(pltpu.make_async_copy(held.at[d], out_hbm.at[d], sems.at[d]))
        copies[d].start()
    for copy in copies:
        copy.wait()


def call(body, args, outs, scratch, flops, hbm=False, out_hbm=False):
    if hbm:
        args = tuple(pltpu.with_memory_space_constraint(a, pltpu.HBM) for a in args)
    keywords = dict(out_specs=pl.BlockSpec(memory_space=pltpu.HBM)) if out_hbm else {}
    return pl.pallas_call(
        body,
        **keywords,
        in_specs=[pl.BlockSpec(memory_space=pltpu.HBM if hbm else pltpu.VMEM)] * len(args),
        out_shape=outs,
        scratch_shapes=scratch,
        cost_estimate=pl.CostEstimate(flops=flops, bytes_accessed=1000000, transcendentals=0),
        compiler_params=pltpu.CompilerParams(vmem_limit_bytes=16 * 1024 * 1024),
    )(*args)


def local(traces, dirichlet, visc_class, viscosity, coarse_diag, solve_map, flux_map):
    wx, wy, z = traces.shape[2:]
    cells = wx * wy
    rows = 8 * (wy // 2 + 1)
    per_hex = 2 * 384 * 288 * z
    parts = jnp.asarray(slot_table())
    own_rows = jnp.asarray(penalty_table())
    spread = jnp.asarray(spread_table(wy, rows))
    vm = pltpu.VMEM
    bind = lambda body: functools.partial(body, wx, wy)
    y_message = vm((48 * wx + 48 + tail_rows(8 * ((wx + 2) // 2) + 8 + 3 * wx + 4), z), BF)
    y_outer = vm((y_message.shape[0] + 16, z), BF)
    x_message = vm((48 * (wy + 2) + tail_rows(rows + 3 * wy + 4), z), BF)
    x_outer = vm((x_message.shape[0] + 16, z), BF)

    (lifted, nat, flags, visc, diag, s_turned, f_map, parts, va, v1a, v3, inner, outer) = call(
        bind(first_kernel),
        (
            viscosity, traces.reshape(3, 48 * cells, z), dirichlet.reshape(3, cells, z),
            visc_class.reshape(cells, z), coarse_diag.reshape(cells, z), solve_map.T, flux_map, parts, own_rows,
        ),
        (
            vm((4, cells, 48, z), BF), vm((3, 48 * cells, z), F32), vm((6, cells, z), F32), vm((viscosity.shape[0], z), F32), vm((cells, z), F32),
            vm(solve_map.shape[::-1], BF), vm(flux_map.shape, BF), vm(parts.shape, BF),
            vm((2, wx + 1, 8, z), F32), vm((2, 16, z), F32), vm((wx, 32, z), F32),
            y_message, y_outer,
        ),
        [
            y_message, y_message, vm(own_rows.shape, BF),
            vm((3, 48 * cells, z), BF), vm((3, cells, z), jnp.int32), vm((cells, z), jnp.int32),
            pltpu.SMEM(viscosity.shape, F32), pltpu.SemaphoreType.DMA((11,)),
        ],
        wx * per_hex, True,
    )
    inner = swap(inner, "gy", "gx", 0)
    outer = swap(outer, "gy", "gx", 1)
    c, vb, v1b, mx, my, own = call(
        bind(middle_kernel),
        (lifted, nat, flags, s_turned, f_map, parts),
        (
            vm((6, cells, 48, z), F32), vm((wy - 2, wx + 1, 8, z), F32), vm((wy - 2, 16, z), F32),
            vm((384, 48), BF), vm((384, 48), BF), vm((144, wx * z), F32),
        ),
        [vm((4, cells, 48, z), BF), vm((384, 288), BF), vm((288, 256), BF)], cells * per_hex,
    )
    c3, vt, vl, v1, face, yd, yu, inner, outer = call(
        bind(turn_kernel),
        (
            visc, lifted, flags, diag, parts, my, own, c, va, vb, v1a, v1b, v3, inner, outer,
        ),
        (
            vm((2, 6, 48, z), F32), vm((2, 2, 8, z), F32), vm((2, 2, 8, z), F32), vm((wy + 2, 16, z), F32),
            vm((2, 48, z), F32), y_message, y_message, x_message, x_outer,
        ),
        [x_message, x_message], 2 * per_hex,
    )
    inner = swap(inner, "gx", "gy", 0)
    outer = swap(outer, "gx", "gy", 1)
    residual, vs, inverse, ownx = call(
        bind(assemble_kernel),
        (
            visc, lifted, flags, diag, parts, mx, my, own, c, c3, va, vb, v3, vt, vl, face, yd, yu,
        ),
        (
            vm((3, 48 * cells, z), F32), vm((wx + 1, rows, z), F32), vm((wx, rows, z), F32),
            vm((144, (wy + 2) * z), F32),
        ),
        [vm((wx - 2, 6, 48, z), F32)], 4 * per_hex,
    )
    out = call(
        bind(final_kernel),
        (
            visc, lifted, flags, parts, mx, ownx, residual, vs, inverse, v1, yd, yu, inner, outer, spread,
        ),
        jax.ShapeDtypeStruct((3, 48 * cells, z), BF),
        [vm((3, 48 * cells, z), BF), x_message, x_message, pltpu.SemaphoreType.DMA((3,))], 4 * spread.size * z,
        out_hbm=True,
    )
    return out.reshape(traces.shape)


def solution(mesh):
    in_specs = (
        P(None, None, "gx", "gy", None),
        P(None, "gx", "gy", None),
        P("gx", "gy", None),
        P(),
        P("gx", "gy", None),
        P(),
        P(),
    )
    out_specs = P(None, None, "gx", "gy", None)
    return jax.shard_map(local, mesh=mesh, in_specs=in_specs, out_specs=out_specs, check_vma=False)
```

```python
import functools
import math

import jax
import jax.numpy as jnp
import ml_dtypes
import numpy as np
from jax import lax
from jax.experimental import pallas as pl
from jax.experimental.pallas import tpu as pltpu
from jax.sharding import PartitionSpec as P

penalty = 0.5
BF = jnp.bfloat16
F32 = jnp.float32
lift = 1.3264
gain = 1.3280711361297461


def swap(value, axis, other, first):
    count, width = lax.axis_size(axis), lax.axis_size(other)
    place = (lambda i, j: i * width + j) if (axis, other) == ("gx", "gy") else (lambda i, j: j * count + i)
    lows = list(range(first, count - 1, 2))
    pairs = [(place(low, j), place(low + 1, j)) for low in lows for j in range(width)]
    alone = [i for i in range(count) if i not in lows and i - 1 not in lows]
    pairs += [(place(i, j), place(i, j + 1)) for i in alone for j in range(0, width - 1, 2)]
    return lax.ppermute(value, ("gx", "gy"), pairs + [(high, low) for low, high in pairs])


def even(axis):
    return lax.rem(lax.axis_index(axis), 2) == 0


def arrive(axis, inner_ref, outer_ref, down_ref, up_ref):
    here, last = lax.axis_index(axis), lax.axis_size(axis) - 1
    choose(even(axis), inner_ref, outer_ref, down_ref, here < last)
    choose(even(axis), outer_ref, inner_ref, up_ref, here > 0)


def depart(axis, down_ref, up_ref, inner_ref, outer_ref):
    choose(even(axis), up_ref, down_ref, inner_ref)
    choose(even(axis), down_ref, up_ref, outer_ref)


def choose(condition, yes_ref, no_ref, out_ref, present=None):
    size = min(yes_ref.shape[0], no_ref.shape[0], out_ref.shape[0])
    rows = pl.ds(0, size)
    value = jnp.where(condition, yes_ref[rows, :], no_ref[rows, :])
    out_ref[rows, :] = value if present is None else jnp.where(present, value, jnp.zeros_like(value))
    if out_ref.shape[0] > size:
        rest = pl.ds(size, out_ref.shape[0] - size)
        out_ref[rest, :] = jnp.zeros((out_ref.shape[0] - size, out_ref.shape[1]), out_ref.dtype)


def corner_table():
    gll_points = [-1.0, -math.sqrt(0.2), math.sqrt(0.2), 1.0]
    table = np.zeros((16, 4), np.float64)
    for s in range(4):
        for t in range(4):
            for p in range(2):
                for q in range(2):
                    table[4 * s + t, 2 * p + q] = (
                        (1 + (2 * p - 1) * gll_points[s]) * (1 + (2 * q - 1) * gll_points[t]) / 4
                    )
    return table


def landing(face_slot, high_s, high_t):
    direction, outward = divmod(face_slot, 2)
    if direction == 0:
        return (outward, high_s, high_t)
    if direction == 1:
        return (high_s, outward, high_t)
    return (high_s, high_t, outward)


def gather_table():
    weights = lift * corner_table()
    table = np.zeros((32, 288), np.float64)
    for slot in range(6):
        for s in range(2):
            for t in range(2):
                p, q, r = landing(slot, s, t)
                for c in range(3):
                    cols = slot * 48 + 16 * c + np.arange(16)
                    table[16 * r + 8 * p + 4 * q + c, cols] += weights[:, 2 * s + t]
    return table.astype(ml_dtypes.bfloat16)


def slot_table():
    slots = np.split(gather_table(), 6, axis=1)
    rows = [
        np.r_[0:8, 16:24], np.r_[8:16, 24:32], np.arange(32), np.arange(32), np.arange(16), np.arange(16, 32),
    ]
    return np.concatenate([slot[kept] for slot, kept in zip(slots, rows)], axis=0)


slot_rows = (0, 16, 32, 64, 96, 112, 128)


def penalty_table():
    slots = np.split(slot_table().astype(np.float64), slot_rows[1:6], axis=0)
    table = np.zeros((144, 288), np.float64)
    for s, first in enumerate((0, 16, 32, 32, 64, 80)):
        table[first : first + len(slots[s]), 48 * s : 48 * s + 48] += penalty * slots[s]
    table[96:, 144:192] = penalty * np.eye(48)
    return table.astype(ml_dtypes.bfloat16)


def spread_table(wy, rows):
    weights = lift * corner_table()
    table = np.zeros((3, 48, 2, wy, 6 * rows), np.float64)
    for d in range(3):
        for x in range(2):
            for y in range(wy):
                for s in range(2):
                    for t in range(2):
                        p, q, r = landing(2 * d, s, t)
                        for c in range(3):
                            k = (3 * r + x + p) * rows + 4 * (y + q) + c
                            table[d, 16 * c : 16 * c + 16, x, y, k] += weights[:, 2 * s + t]
    return table.reshape(-1, 6 * rows).astype(ml_dtypes.bfloat16)


def lanes(shape):
    return lax.broadcasted_iota(jnp.int32, shape, len(shape) - 1)


def z_next(value):
    last = value.shape[-1] - 1
    return jnp.where(lanes(value.shape) < last, pltpu.roll(value, last, value.ndim - 1), 0.0)


def z_prev(value):
    return jnp.where(lanes(value.shape) > 0, pltpu.roll(value, 1, value.ndim - 1), 0.0)


def dot(left, right):
    return jnp.dot(left, right, preferred_element_type=F32)


def wide(parts):
    return jnp.concatenate(parts, axis=1)


def tall(parts):
    return jnp.concatenate(parts, axis=0)


def columns(rows, count):
    z = rows.shape[1] // count
    return [rows[:, z * h : z * h + z] for h in range(count)]


def elements(slots):
    return tall([wide([hexa[s] for hexa in slots]) for s in range(6)])


def vertex_part(flux, parts_ref):
    rows = []
    for s in range(6):
        first, size = slot_rows[s], slot_rows[s + 1] - slot_rows[s]
        rows.append(dot(parts_ref[pl.ds(first, size), :], flux[48 * s : 48 * s + 48].astype(BF)))
    rows[2:4] = [rows[2] + rows[3]]
    return tall(rows)


def turned_dot(left, right):
    return lax.dot_general(left, right, (((1,), (1,)), ((), ())), preferred_element_type=F32)


def product(f_ref, st_ref, slot):
    first = 0 if slot is None else 48 * slot
    flux = turned_dot(f_ref[...], st_ref[...] if slot is None else st_ref[pl.ds(first, 48), :])
    rows = lax.broadcasted_iota(jnp.int32, flux.shape, 0)
    return flux, flux + jnp.where(rows == lax.broadcasted_iota(jnp.int32, flux.shape, 1) + first, F32(penalty), F32(0.0))


def slot_corners(traces, parts_ref, slot):
    z = traces[0].shape[1]
    first, size = slot_rows[slot], slot_rows[slot + 1] - slot_rows[slot]
    rows = dot(parts_ref[pl.ds(first, size), :], wide([trace.astype(BF) for trace in traces]))
    return [rows[:, z * h : z * h + z] for h in range(len(traces))]


def settle(rows, p):
    return rows[8 * p : 8 * p + 8] + z_prev(rows[16 + 8 * p : 24 + 8 * p])


def scaled_corners(delta, scales, offsets=(0, 1)):
    shape = (8, delta.shape[1])
    blank = jnp.zeros((1, shape[1]), F32)
    y_scale = jnp.where(
        lax.broadcasted_iota(jnp.int32, shape, 0) < 4,
        blank if scales[2] is None else scales[2], blank if scales[3] is None else scales[3],
    )
    results = []
    for p in offsets:
        parts = []
        for r in range(2):
            at = 32 + 16 * r + 8 * p
            part = delta[at : at + 8] * y_scale + delta[at + 32 : at + 40] * scales[4 + r]
            if scales[p] is not None:
                part = part + delta[16 * p + 8 * r : 16 * p + 8 * r + 8] * scales[p]
            parts.append(part)
        results.append(parts[0] + z_prev(parts[1]))
    return results


def level_visc(code, visc_ref):
    visc = jnp.zeros(code.shape, F32)
    for level in range(visc_ref.shape[0]):
        visc = visc + jnp.where(code == F32(level + 1), visc_ref[pl.ds(level, 1), :], F32(0.0))
    return visc


def merge(even, odd):
    odd = tall(odd)
    return tall(even) + pltpu.roll(odd, odd.shape[0] - 4, 0)


def first_kernel(
    wx, wy, visc_hbm, t_hbm, dir_hbm, cls_hbm, diag_hbm, st_hbm, f_hbm, parts_hbm, own_hbm,
    l_ref, nat, kp_ref, visc_ref, diag_ref, st_ref, f_ref, parts_ref, v_ref, v1_ref, v3_ref,
    inner_ref, outer_ref, down_ref, up_ref, own_ref, t_ref, dir_ref, cls_ref, levels, sems,
):
    cells = wx * wy
    pairs = [
        (f_hbm, f_ref), (parts_hbm, parts_ref), (st_hbm, st_ref), (own_hbm, own_ref), (dir_hbm, dir_ref), (t_hbm.at[0], t_ref.at[0]),
        (t_hbm.at[1], t_ref.at[1]), (t_hbm.at[2], t_ref.at[2]), (cls_hbm, cls_ref), (visc_hbm, levels),
        (diag_hbm, diag_ref),
    ]
    copies = [pltpu.make_async_copy(a, b, sems.at[i]) for i, (a, b) in enumerate(pairs)]
    for copy in copies:
        copy.start()
    copies[0].wait()
    copies[1].wait()
    left = tall([vertex_part(f_ref[...], parts_ref).astype(BF), f_ref[pl.ds(144, 48), :]])
    copies[2].wait()
    copies[3].wait()
    copies[4].wait()
    z = t_ref.shape[2]
    for d in range(3):
        keep = (1 - dir_ref[d]).astype(F32)
        kp_ref[d] = keep
        copies[5 + d].wait()
        if d == 0:
            short = (turned_dot(left, st_ref[...]) + own_ref[...].astype(F32)).astype(BF)
        masked = t_ref[d].astype(F32).reshape(48, cells, z) * keep[None]
        nat[d] = masked.reshape(48 * cells, z)
        lay_out(wx, wy, d, nat, l_ref, True)
    kp_ref[3] = z_next(kp_ref[2])
    for copy in copies[8:]:
        copy.wait()
    for level in range(visc_ref.shape[0]):
        visc_ref[pl.ds(level, 1), :] = jnp.full((1, z), levels[level], F32)
    code = cls_ref[...].astype(F32) + 1.0
    kp_ref[4] = level_visc(code, visc_ref)
    kp_ref[5] = code
    row = lambda i, col: kp_ref[i, pl.ds(col, 1), :]
    corners = []
    for side, y in enumerate((0, wy - 1)):
        where = [(x, y) for x in range(wx)]
        slots, scales, left_out = known_hexes(wx, wy, where, (l_ref, None), kp_ref)
        rows = columns(dot(short if side else short[0:96], elements(slots)), wx)
        corners += known_corners(rows, scales, left_out)
        v1_ref[side] = rows[wx - 1][16:32] * row(4, (wx - 1) * wy + y)
    place = lax.broadcasted_iota(jnp.int32, (32, z), 0)
    lone = [part * row(4, x * wy + wy - 1) for x, part in enumerate(rows)]
    for x in range(wx):
        v3_ref[x] = jnp.where(lax.rem(place, 8) < 4, 0.0, lone[x][32:64])
    sums = [line_sums(corners[:wx]), line_sums(corners[wx:])]
    for side in range(2):
        for i in range(wx + 1):
            v_ref[side, i] = sums[side][i]
    corner = (wx - 1) * wy
    top = wy - 1
    for x in range(wx):
        down_ref[pl.ds(48 * x, 48), :] = l_ref[1, x * wy]
        up_ref[pl.ds(48 * x, 48), :] = lone[x][96:144].astype(BF)
    down_ref[pl.ds(48 * wx, 48), :] = l_ref[0, 0]
    up_ref[pl.ds(48 * wx, 48), :] = l_ref[0, top]
    flags = [row(1, x * wy) for x in range(wx)] + [row(0, 0), row(5, corner), row(0, corner), row(2, corner)]
    diag = tall([diag_ref[pl.ds(x * wy, 1), :] for x in range(wx)])
    high = diag.astype(BF).astype(F32)
    rim = pack(sums[0], 0) + pack([v1_ref[0, 0:8], v1_ref[0, 8:16]], 0) + flags + [high, diag - high]
    put_tail(down_ref, 48 * wx + 48, rim)
    flags = [row(kind, x * wy + top) for kind in (5, 0, 2) for x in range(wx)]
    rim = pack(sums[1], 1) + pack([v1_ref[1, 0:8], v1_ref[1, 8:16]], 1) + flags
    put_tail(up_ref, 48 * wx + 48, rim)
    depart("gy", down_ref, up_ref, inner_ref, outer_ref)


def tail_rows(count):
    return -(-count // 16) * 16


def put_tail(ref, start, rows):
    count = sum(part.shape[0] for part in rows)
    full = ref.shape[0] - start
    if full > count:
        rows = rows + [jnp.zeros((full - count, rows[0].shape[1]), F32)]
    ref[pl.ds(start, full), :] = tall(rows).astype(BF)


def pack(parts, half):
    place = lax.broadcasted_iota(jnp.int32, parts[0].shape, 0)
    parts = parts + [jnp.zeros_like(parts[0])] * (len(parts) % 2)
    packed = []
    for low, high in zip(parts[0::2], parts[1::2]):
        if half:
            low = pltpu.roll(low, 4, 0)
        else:
            high = pltpu.roll(high, 4, 0)
        packed.append(jnp.where(place < 4, low, high))
    return packed


def unpack(packed, count, half):
    parts = []
    for n in range(count):
        part = packed[8 * (n // 2) : 8 * (n // 2) + 8]
        parts.append(part if n % 2 == half else pltpu.roll(part, 4, 0))
    return parts


def read_tail(ref, wx, half):
    start = 48 * wx + 48
    rows = ref[pl.ds(start, ref.shape[0] - start), :].astype(F32)
    size = 8 * ((wx + 2) // 2)
    return unpack(rows, wx + 1, half), unpack(rows[size : size + 8], 2, half), rows[size + 8 :]


def line_sums(corners):
    low, high = [part[0] for part in corners], [part[1] for part in corners]
    return [low[0]] + [low[x] + high[x - 1] for x in range(1, len(low))] + [high[-1]]


def early(wx, wy, d, x, y):
    return y in (0, wy - 1) or (d == 0 and x == 0) or (d == 1 and y == 1)


def lay_out(wx, wy, d, nat, l_ref, first):
    for x in range(wx):
        for y in range(wy):
            if early(wx, wy, d, x, y) == first:
                col = x * wy + y
                part = nat[d, pl.ds(col, 48, stride=wx * wy), :]
                l_ref[d, col] = part.astype(BF)
                if d == 2:
                    l_ref[3, col] = z_next(part).astype(BF)


def known_hexes(wx, wy, where, l_refs, kp_ref):
    z = l_refs[0].shape[3]
    nothing = jnp.zeros((48, z), BF)
    row = lambda i, col: kp_ref[i, pl.ds(col, 1), :]
    trace = lambda d, x, y: l_refs[0 if early(wx, wy, min(d, 2), x, y) else 1][d, x * wy + y]
    slots, scales, left_out = [], [], []
    for x, y in where:
        here = x * wy + y
        visc = row(4, here)
        last_x, last_y = x == wx - 1, y == wy - 1
        slots.append(
            [
                trace(0, x, y), nothing if last_x else trace(0, x + 1, y),
                trace(1, x, y), nothing if last_y else trace(1, x, y + 1),
                trace(2, x, y), trace(3, x, y),
            ]
        )
        scales.append(
            [
                visc * row(0, here), visc if last_x else visc * row(0, here + wy),
                visc * row(1, here), visc if last_y else visc * row(1, here + 1),
                visc * row(2, here), visc * row(3, here),
            ]
        )
        left_out.append(([1] if last_x else []) + ([3] if last_y else []))
    return slots, scales, left_out


def known_corners(vertex, scales, left_out):
    return [
        scaled_corners(part, [None if s in out else scale[s] for s in range(6)])
        for part, scale, out in zip(vertex, scales, left_out)
    ]


def middle_kernel(
    wx, wy, l_ref, nat, kp_ref, st_ref, f_ref, parts_ref,
    c_ref, v_ref, v1_ref, mx_ref, my_ref, own_ref, rest_ref, m_ref, lost_ref,
):
    for slot, ref in ((1, mx_ref), (3, my_ref)):
        bare, flux = product(f_ref, st_ref, slot)
        turned = tall([bare[0:48], bare[96:288], bare[48:96]]) if slot == 1 else bare
        ref[pl.ds(0, 288), :] = turned.astype(BF)
        ref[pl.ds(288, 96), :] = vertex_part(flux, parts_ref).astype(BF)
    flux = product(f_ref, st_ref, None)[1]
    m_ref[pl.ds(0, 288), :] = flux.astype(BF)
    m_ref[pl.ds(288, 96), :] = vertex_part(flux, parts_ref).astype(BF)
    lost_ref[...] = (flux - flux.astype(BF).astype(F32))[:, 0:256].astype(BF)
    for d in range(3):
        lay_out(wx, wy, d, nat, rest_ref, False)
    own_ref[...] = dot(
        tall([my_ref[pl.ds(144, 48), :], my_ref[pl.ds(288, 96), :]]), wide([l_ref[1, x * wy] for x in range(wx)])
    )
    for y in range(wy):
        inside = 0 < y < wy - 1
        where = [(x, y) for x in range(wx)]
        slots, scales, left_out = known_hexes(wx, wy, where, (l_ref, rest_ref), kp_ref)
        element = elements(slots)
        rows = dot(m_ref[...] if inside else m_ref[pl.ds(0, 288), :], element)
        lost = columns(dot(lost_ref[...], element[0:256]), wx)
        rows = columns(rows, wx)
        for x in range(wx):
            for s in range(6):
                part = slice(48 * s, 48 * s + 48)
                c_ref[s, x * wy + y] = (rows[x][part] + lost[x][part]) * scales[x][s]
        if inside:
            corners = known_corners([part[288:] for part in rows], scales, left_out)
            v1_ref[y - 1] = rows[wx - 1][304:320] * kp_ref[4, pl.ds((wx - 1) * wy + y, 1), :]
            for i, part in enumerate(line_sums(corners)):
                v_ref[y - 1, i] = part


def after_y(wx, wy, xs, visc_ref, l_ref, kp_ref, parts_ref, my_ref, own_ref, v3_ref, down_ref, up_ref):
    z = l_ref.shape[3]
    misc_d = read_tail(down_ref, wx, 0)[2]
    misc_u = read_tail(up_ref, wx, 1)[2]
    row = lambda i, col: kp_ref[i, pl.ds(col, 1), :]
    delta = dot(my_ref[...], wide([down_ref[pl.ds(48 * x, 48), :] for x in xs]))
    arrived = [up_ref[pl.ds(48 * x, 48), :].astype(F32) for x in xs]
    arrived_corners = slot_corners(arrived, parts_ref, 3)
    results = []
    for n, x in enumerate(xs):
        here = x * wy + wy - 1
        last = x == wx - 1
        part = delta[:, z * n : z * n + z]
        visc = row(4, here)
        scales = [
            visc * row(0, here), visc if last else visc * row(0, here + wy), visc * row(1, here),
            visc * misc_d[x : x + 1], visc * row(2, here), visc * row(3, here),
        ]
        flux = [part[48 * s : 48 * s + 48] * scales[s] for s in range(6)]
        used = [None if (s == 1 and last) else scales[s] for s in range(6)]
        known = v3_ref[x] * misc_d[x : x + 1]
        top = [rows + settle(known, p) for p, rows in enumerate(scaled_corners(part[288:384], used))]
        top_one = part[304:320] * visc
        here = x * wy
        visc = level_visc(misc_u[x : x + 1], visc_ref)
        flag = row(1, here)
        own = own_ref[:, pl.ds(z * x, z)]
        keep_z = misc_u[2 * wx + x : 2 * wx + x + 1]
        scales = [
            visc * misc_u[wx + x : wx + x + 1], None if last else visc * misc_u[wx + x + 1 : wx + x + 2],
            None, visc * flag, visc * keep_z, visc * z_next(keep_z),
        ]
        known = arrived_corners[n] * flag
        low = [rows + settle(known, p) for p, rows in enumerate(scaled_corners(own[48:144], scales))]
        low_one = own[64:80] * visc
        face = (arrived[n] + visc * (own[0:48] + penalty * l_ref[1, here].astype(F32))) * flag
        results.append((flux, top, top_one, low, low_one, face))
    return results


def turn_kernel(
    wx, wy, visc_ref, l_ref, kp_ref, diag_ref, parts_ref, my_ref, own_ref, c_ref, va_ref, vb_ref,
    v1a_ref, v1b_ref, v3_ref, inner_in, outer_in,
    c3_ref, vt_ref, vl_ref, v1_ref, face_ref, yd_ref, yu_ref, inner_ref, outer_ref, down_ref, up_ref,
):
    z = l_ref.shape[3]
    arrive("gy", inner_in, outer_in, yd_ref, yu_ref)
    xs = (0, wx - 1)
    results = after_y(wx, wy, xs, visc_ref, l_ref, kp_ref, parts_ref, my_ref, own_ref, v3_ref, yd_ref, yu_ref)
    row = lambda i, col: kp_ref[i, pl.ds(col, 1), :]
    sums_d, one_d, misc_d = read_tail(yd_ref, wx, 0)
    sums_u, one_u, misc_u = read_tail(yu_ref, wx, 1)
    edge_high, edge_low = misc_d[wx + 4 : 2 * wx + 4], misc_d[2 * wx + 4 : 3 * wx + 4]
    for n, (flux, top, top_one, low, low_one, face) in enumerate(results):
        for s in range(6):
            c3_ref[n, s] = flux[s]
        face_ref[n] = face
        for p in range(2):
            vt_ref[n, p] = top[p]
            vl_ref[n, p] = low[p]
    flux, top, top_one, low, low_one, face = results[1]
    mine = tall(one_u) + low_one
    v1_ref[0] = mine
    v1_ref[1] = v1a_ref[0]
    for y in range(wy - 2):
        v1_ref[2 + y] = v1b_ref[y]
    v1_ref[wy] = v1a_ref[1] + top_one
    v1_ref[wy + 1] = tall(one_d)

    def plane(i, n, p):
        lines = [sums_u[i] + vl_ref[n, p], va_ref[0, i]]
        lines += [vb_ref[y, i] for y in range(wy - 2)]
        lines += [va_ref[1, i] + vt_ref[n, p], sums_d[i]]
        return merge(lines[1::2], lines[0::2])

    down_ref[pl.ds(0, 48), :] = yu_ref[pl.ds(48 * wx, 48), :]
    for y in range(wy):
        down_ref[pl.ds(48 + 48 * y, 48), :] = l_ref[0, y]
    down_ref[pl.ds(48 * (wy + 1), 48), :] = yd_ref[pl.ds(48 * wx, 48), :]
    diag = diag_ref[pl.ds(0, wy), :]
    high = diag.astype(BF).astype(F32)
    rim = [plane(0, 0, 0), high, edge_high[0:1], diag - high, edge_low[0:1]]
    rim += [misc_u[wx : wx + 1], kp_ref[0, 0:wy], misc_d[wx : wx + 1]]
    put_tail(down_ref, 48 * (wy + 2), rim)
    corner = (wx - 1) * wy
    for y in range(wy):
        part = c_ref[1, corner + y]
        up_ref[pl.ds(48 * y, 48), :] = (part + flux[1] if y == wy - 1 else part).astype(BF)
    last = pl.ds(corner, wy)
    rim = [plane(wx, 1, 1), mine, *one_d]
    rim += [misc_u[wx - 1 : wx], kp_ref[5, last], misc_d[wx + 1 : wx + 2]]
    rim += [misc_u[3 * wx - 1 : 3 * wx], kp_ref[2, last], misc_d[wx + 3 : wx + 4]]
    rim += [kp_ref[1, last], misc_d[wx - 1 : wx]]
    put_tail(up_ref, 48 * wy, rim)
    depart("gx", down_ref, up_ref, inner_ref, outer_ref)


def assemble_kernel(
    wx, wy, visc_ref, l_ref, kp_ref, diag_ref, parts_ref, mx_ref, my_ref, own_ref, c_ref, c3_ref,
    va_ref, vb_ref, v3_ref, vt_ref, vl_ref, face_ref, yd_ref, yu_ref,
    r_ref, v_ref, inv_ref, ownx_ref, mid,
):
    z = l_ref.shape[3]
    cells = wx * wy
    xs = tuple(range(1, wx - 1))
    results = after_y(wx, wy, xs, visc_ref, l_ref, kp_ref, parts_ref, my_ref, own_ref, v3_ref, yd_ref, yu_ref)
    for n, part in enumerate(results):
        for s in range(6):
            mid[n, s] = part[0][s]
    traces = [yu_ref[pl.ds(48 * wx, 48), :]] + [l_ref[0, y] for y in range(wy)] + [yd_ref[pl.ds(48 * wx, 48), :]]
    ownx_ref[...] = dot(mx_ref[pl.ds(240, 144), :], wide(traces))

    def contrib(slot, x, y):
        here = c_ref[slot, x * wy + y]
        if y < wy - 1:
            return here
        return here + (mid[x - 1, slot] if 0 < x < wx - 1 else c3_ref[0 if x == 0 else 1, slot])

    for x in range(wx):
        for y in range(wy):
            col = pl.ds(x * wy + y, 48, stride=cells)
            if x:
                r_ref[0, col, :] = contrib(0, x, y) + contrib(1, x - 1, y)
            else:
                r_ref[0, col, :] = contrib(0, x, y)
            if y:
                behind = contrib(3, x, y - 1)
            elif 0 < x < wx - 1:
                behind = results[x - 1][5]
            else:
                behind = face_ref[0 if x == 0 else 1]
            r_ref[1, col, :] = contrib(2, x, y) + behind
            r_ref[2, col, :] = contrib(4, x, y) + z_prev(contrib(5, x, y))
    sums_d, one_d, misc_d = read_tail(yd_ref, wx, 0)
    sums_u, one_u, misc_u = read_tail(yu_ref, wx, 1)
    edge_diag = misc_d[wx + 4 : 2 * wx + 4] + misc_d[2 * wx + 4 : 3 * wx + 4]

    def brought(which, i):
        held = vt_ref if which == 1 else vl_ref
        terms = []
        for x, p in ((i, 0), (i - 1, 1)):
            if x in (0, wx - 1):
                terms.append(held[0 if x == 0 else 1, p])
            elif 0 < x < wx - 1:
                terms.append(results[x - 1][which][p])
        return sum(terms[1:], terms[0])

    for i in range(wx + 1):
        lines = [sums_u[i] + brought(3, i), va_ref[0, i]]
        lines += [vb_ref[y, i] for y in range(wy - 2)]
        lines += [va_ref[1, i] + brought(1, i), sums_d[i]]
        v_ref[i] = merge(lines[1::2], lines[0::2])
        if i < wx:
            parts = [jnp.broadcast_to(diag_ref[pl.ds(i * wy + y, 1), :], (4, z)) for y in range(wy)]
            parts += [jnp.broadcast_to(edge_diag[i : i + 1], (4, z)), jnp.zeros((4, z), F32)]
            inv_ref[i] = reciprocal(tall(parts))


def reciprocal(diag):
    present = diag > 0.0
    return jnp.where(present, (1.0 / (gain * gain)) / jnp.where(present, diag, 1.0), 0.0)


def final_kernel(
    wx, wy, visc_ref, l_ref, kp_ref, parts_ref, mx_ref, ownx_ref, r_ref, v_ref, inv_ref, v1_ref,
    yd_ref, yu_ref, inner_in, outer_in, p_ref, out_hbm, held, sems,
):
    here, last = lax.axis_index("gx"), lax.axis_size("gx") - 1

    def from_high(start, size):
        rows = pl.ds(start, size)
        value = jnp.where(even("gx"), inner_in[rows, :], outer_in[rows, :])
        return jnp.where(here < last, value, jnp.zeros_like(value))

    def from_low(start, size):
        rows = pl.ds(start, size)
        value = jnp.where(even("gx"), outer_in[rows, :], inner_in[rows, :])
        return jnp.where(here > 0, value, jnp.zeros_like(value))

    cells, z = wx * wy, l_ref.shape[3]
    rows = v_ref.shape[1]
    row = lambda i, col: kp_ref[i, pl.ds(col, 1), :]
    traces = [from_high(48 * j, 48) for j in range(wy + 2)]
    delta = dot(mx_ref[pl.ds(288, 96), :], wide(traces))
    rim_x = from_high(48 * (wy + 2), tail_rows(rows + 3 * wy + 4)).astype(F32)
    rim_l = from_low(48 * wy, tail_rows(rows + 32 + 3 * (wy + 2) - 1)).astype(F32)
    misc_d = read_tail(yd_ref, wx, 0)[2]
    misc_u = read_tail(yu_ref, wx, 1)[2]
    flags_high = rim_x[rows + 2 * (wy + 1) : rows + 3 * wy + 4]
    corner = (wx - 1) * wy
    arrived = [from_low(48 * y, 48) for y in range(wy)]
    arrived_corners = slot_corners(arrived, parts_ref, 1)
    codes = rim_l[rows + 32 : rows + 32 + wy + 2]
    keep_z = rim_l[rows + 32 + wy + 2 : rows + 32 + 2 * (wy + 2)]
    keep_y = rim_l[rows + 32 + 2 * (wy + 2) : rows + 32 + 3 * (wy + 2) - 1]
    low_visc = level_visc(codes, visc_ref)
    low_keep_z = z_next(keep_z)
    lines = [[], [], []]
    high_scales, faces = [], []
    for j in range(-1, wy + 1):
        n = j + 1
        part = delta[:, z * n : z * n + z]
        flag = flags_high[n : n + 1]
        if j < 0:
            visc = level_visc(misc_u[wx - 1 : wx], visc_ref)
            kz = misc_u[3 * wx - 1 : 3 * wx]
            keeps = [misc_u[2 * wx - 1 : 2 * wx], flag, None, row(1, corner), kz, z_next(kz)]
        elif j < wy:
            here = corner + j
            visc = row(4, here)
            high_y = row(1, here + 1) if j < wy - 1 else misc_d[wx - 1 : wx]
            keeps = [row(0, here), flag, row(1, here), high_y, row(2, here), row(3, here)]
        else:
            visc = level_visc(misc_d[wx + 1 : wx + 2], visc_ref)
            kz = misc_d[wx + 3 : wx + 4]
            keeps = [misc_d[wx + 2 : wx + 3], flag, misc_d[wx - 1 : wx], None, kz, z_next(kz)]
        scales = [None if keep is None else visc * keep for keep in keeps]
        corners = scaled_corners(part, scales)
        one = v1_ref[n] * flag
        lines[0].append(corners[0])
        lines[1].append(corners[1] + one[0:8] + z_prev(one[8:16]))
        high_scales.append(scales)
        own = ownx_ref[:, pl.ds(z * n, z)]
        visc = low_visc[n : n + 1]
        flag = misc_u[wx : wx + 1] if j < 0 else misc_d[wx : wx + 1] if j == wy else row(0, j)
        scales = [
            None, visc * flag, None if j < 0 else visc * keep_y[j : j + 1],
            None if j == wy else visc * keep_y[j + 1 : j + 2], visc * keep_z[n : n + 1], visc * low_keep_z[n : n + 1],
        ]
        corners = scaled_corners(own[48:144], scales, (1,))[0]
        if 0 <= j < wy:
            one = arrived_corners[j] * flag
            lines[2].append(corners + one[0:8] + z_prev(one[8:16]))
            faces.append((arrived[j].astype(F32) + visc * (own[0:48] + penalty * l_ref[0, j].astype(F32))) * flag)
        else:
            at = rows + (0 if j < 0 else 16)
            one = rim_l[at : at + 16] * flag
            lines[2].append(corners + one[0:8] + z_prev(one[8:16]))
    low, before, first = [merge(part[1::2], part[0::2]) for part in lines]
    top = v_ref[wx] + before + rim_x[0:rows]
    values = [(v_ref[0] + first + rim_l[0:rows]) * inv_ref[0]]
    values += [v_ref[i] * inv_ref[i] for i in range(1, wx - 1)]
    values += [(v_ref[wx - 1] + low) * inv_ref[wx - 1]]
    diag = rim_x[rows : rows + wy + 1] + rim_x[rows + wy + 1 : rows + 2 * (wy + 1)]
    parts = [jnp.broadcast_to(diag[j : j + 1], (4, z)) for j in range(wy + 1)]
    values += [top * reciprocal(tall(parts + [jnp.zeros((rows - 4 * (wy + 1), z), F32)]))]
    low = [tall(values[x : x + 3]) for x in range(0, wx, 2)]
    rhs = tall([wide(low), wide([z_next(part) for part in low])]).astype(BF)
    delta = columns(dot(mx_ref[pl.ds(0, 240), :], wide(traces[1 : wy + 1])), wy)
    behind = dot(mx_ref[pl.ds(96, 48), :], traces[0]) * high_scales[0][3]
    size = 96 * wy
    copies = []
    for d in range(3):
        for j in range(wy):
            scales = high_scales[j + 1]
            part = [delta[j][48 * i : 48 * i + 48] for i in range(5)]
            if d == 0:
                r_ref[0, pl.ds(j, 48, stride=cells), :] += faces[j]
                flux = part[0] * scales[0]
            elif d == 1:
                flux = part[1] * scales[2] + behind
                behind = part[2] * scales[3]
            else:
                flux = part[3] * scales[4] + z_prev(part[4] * scales[5])
            r_ref[d, pl.ds(corner + j, 48, stride=cells), :] += flux
        spread = dot(p_ref[pl.ds(size * d, size), :], rhs)
        spread = jnp.concatenate(
            [spread[:, z * g : z * g + z].reshape(48, 2 * wy, z) for g in range(wx // 2)], axis=1
        )
        total = r_ref[d].reshape(48, cells, z) + spread * kp_ref[d][None]
        held[d] = total.reshape(48 * cells, z).astype(BF)
        copies.append(pltpu.make_async_copy(held.at[d], out_hbm.at[d], sems.at[d]))
        copies[d].start()
    for copy in copies:
        copy.wait()


def call(body, args, outs, scratch, flops, hbm=False, out_hbm=False):
    if hbm:
        args = tuple(pltpu.with_memory_space_constraint(a, pltpu.HBM) for a in args)
    keywords = dict(out_specs=pl.BlockSpec(memory_space=pltpu.HBM)) if out_hbm else {}
    return pl.pallas_call(
        body,
        **keywords,
        in_specs=[pl.BlockSpec(memory_space=pltpu.HBM if hbm else pltpu.VMEM)] * len(args),
        out_shape=outs,
        scratch_shapes=scratch,
        cost_estimate=pl.CostEstimate(flops=flops, bytes_accessed=1000000, transcendentals=0),
        compiler_params=pltpu.CompilerParams(vmem_limit_bytes=16 * 1024 * 1024),
    )(*args)


def local(traces, dirichlet, visc_class, viscosity, coarse_diag, solve_map, flux_map):
    wx, wy, z = traces.shape[2:]
    cells = wx * wy
    rows = 8 * (wy // 2 + 1)
    per_hex = 2 * 384 * 288 * z
    parts = jnp.asarray(slot_table())
    own_rows = jnp.asarray(penalty_table())
    spread = jnp.asarray(spread_table(wy, rows))
    vm = pltpu.VMEM
    bind = lambda body: functools.partial(body, wx, wy)
    y_message = vm((48 * wx + 48 + tail_rows(8 * ((wx + 2) // 2) + 8 + 3 * wx + 4), z), BF)
    y_outer = vm((y_message.shape[0] + 16, z), BF)
    x_message = vm((48 * (wy + 2) + tail_rows(rows + 3 * wy + 4), z), BF)
    x_outer = vm((x_message.shape[0] + 16, z), BF)

    (lifted, nat, flags, visc, diag, s_turned, f_map, parts, va, v1a, v3, inner, outer) = call(
        bind(first_kernel),
        (
            viscosity, traces.reshape(3, 48 * cells, z), dirichlet.reshape(3, cells, z),
            visc_class.reshape(cells, z), coarse_diag.reshape(cells, z), solve_map.T, flux_map, parts, own_rows,
        ),
        (
            vm((4, cells, 48, z), BF), vm((3, 48 * cells, z), F32), vm((6, cells, z), F32), vm((viscosity.shape[0], z), F32), vm((cells, z), F32),
            vm(solve_map.shape[::-1], BF), vm(flux_map.shape, BF), vm(parts.shape, BF),
            vm((2, wx + 1, 8, z), F32), vm((2, 16, z), F32), vm((wx, 32, z), F32),
            y_message, y_outer,
        ),
        [
            y_message, y_message, vm(own_rows.shape, BF),
            vm((3, 48 * cells, z), BF), vm((3, cells, z), jnp.int32), vm((cells, z), jnp.int32),
            pltpu.SMEM(viscosity.shape, F32), pltpu.SemaphoreType.DMA((11,)),
        ],
        wx * per_hex, True,
    )
    inner = swap(inner, "gy", "gx", 0)
    outer = swap(outer, "gy", "gx", 1)
    c, vb, v1b, mx, my, own = call(
        bind(middle_kernel),
        (lifted, nat, flags, s_turned, f_map, parts),
        (
            vm((6, cells, 48, z), F32), vm((wy - 2, wx + 1, 8, z), F32), vm((wy - 2, 16, z), F32),
            vm((384, 48), BF), vm((384, 48), BF), vm((144, wx * z), F32),
        ),
        [vm((4, cells, 48, z), BF), vm((384, 288), BF), vm((288, 256), BF)], cells * per_hex,
    )
    c3, vt, vl, v1, face, yd, yu, inner, outer = call(
        bind(turn_kernel),
        (
            visc, lifted, flags, diag, parts, my, own, c, va, vb, v1a, v1b, v3, inner, outer,
        ),
        (
            vm((2, 6, 48, z), F32), vm((2, 2, 8, z), F32), vm((2, 2, 8, z), F32), vm((wy + 2, 16, z), F32),
            vm((2, 48, z), F32), y_message, y_message, x_message, x_outer,
        ),
        [x_message, x_message], 2 * per_hex,
    )
    inner = swap(inner, "gx", "gy", 0)
    outer = swap(outer, "gx", "gy", 1)
    residual, vs, inverse, ownx = call(
        bind(assemble_kernel),
        (
            visc, lifted, flags, diag, parts, mx, my, own, c, c3, va, vb, v3, vt, vl, face, yd, yu,
        ),
        (
            vm((3, 48 * cells, z), F32), vm((wx + 1, rows, z), F32), vm((wx, rows, z), F32),
            vm((144, (wy + 2) * z), F32),
        ),
        [vm((wx - 2, 6, 48, z), F32)], 4 * per_hex,
    )
    out = call(
        bind(final_kernel),
        (
            visc, lifted, flags, parts, mx, ownx, residual, vs, inverse, v1, yd, yu, inner, outer, spread,
        ),
        jax.ShapeDtypeStruct((3, 48 * cells, z), BF),
        [vm((3, 48 * cells, z), BF), pltpu.SemaphoreType.DMA((3,))], 4 * spread.size * z,
        out_hbm=True,
    )
    return out.reshape(traces.shape)


def solution(mesh):
    in_specs = (
        P(None, None, "gx", "gy", None),
        P(None, "gx", "gy", None),
        P("gx", "gy", None),
        P(),
        P("gx", "gy", None),
        P(),
        P(),
    )
    out_specs = P(None, None, "gx", "gy", None)
    return jax.shard_map(local, mesh=mesh, in_specs=in_specs, out_specs=out_specs, check_vma=False)
```

```python
import functools
import math

import jax
import jax.numpy as jnp
import ml_dtypes
import numpy as np
from jax import lax
from jax.experimental import pallas as pl
from jax.experimental.pallas import tpu as pltpu
from jax.sharding import PartitionSpec as P

penalty = 0.5
BF = jnp.bfloat16
F32 = jnp.float32
lift = 1.3264
gain = 1.3280711361297461


def swap(value, axis, other, first):
    count, width = lax.axis_size(axis), lax.axis_size(other)
    place = (lambda i, j: i * width + j) if (axis, other) == ("gx", "gy") else (lambda i, j: j * count + i)
    lows = list(range(first, count - 1, 2))
    pairs = [(place(low, j), place(low + 1, j)) for low in lows for j in range(width)]
    alone = [i for i in range(count) if i not in lows and i - 1 not in lows]
    pairs += [(place(i, j), place(i, j + 1)) for i in alone for j in range(0, width - 1, 2)]
    return lax.ppermute(value, ("gx", "gy"), pairs + [(high, low) for low, high in pairs])


def even(axis):
    return lax.rem(lax.axis_index(axis), 2) == 0


def arrive(axis, inner_ref, outer_ref, down_ref, up_ref):
    here, last = lax.axis_index(axis), lax.axis_size(axis) - 1
    choose(even(axis), inner_ref, outer_ref, down_ref, here < last)
    choose(even(axis), outer_ref, inner_ref, up_ref, here > 0)


def depart(axis, down_ref, up_ref, inner_ref, outer_ref):
    choose(even(axis), up_ref, down_ref, inner_ref)
    choose(even(axis), down_ref, up_ref, outer_ref)


def choose(condition, yes_ref, no_ref, out_ref, present=None):
    value = jnp.where(condition, yes_ref[...], no_ref[...])
    out_ref[...] = value if present is None else jnp.where(present, value, jnp.zeros_like(value))


def corner_table():
    gll_points = [-1.0, -math.sqrt(0.2), math.sqrt(0.2), 1.0]
    table = np.zeros((16, 4), np.float64)
    for s in range(4):
        for t in range(4):
            for p in range(2):
                for q in range(2):
                    table[4 * s + t, 2 * p + q] = (
                        (1 + (2 * p - 1) * gll_points[s]) * (1 + (2 * q - 1) * gll_points[t]) / 4
                    )
    return table


def landing(face_slot, high_s, high_t):
    direction, outward = divmod(face_slot, 2)
    if direction == 0:
        return (outward, high_s, high_t)
    if direction == 1:
        return (high_s, outward, high_t)
    return (high_s, high_t, outward)


def gather_table():
    weights = lift * corner_table()
    table = np.zeros((32, 288), np.float64)
    for slot in range(6):
        for s in range(2):
            for t in range(2):
                p, q, r = landing(slot, s, t)
                for c in range(3):
                    cols = slot * 48 + 16 * c + np.arange(16)
                    table[16 * r + 8 * p + 4 * q + c, cols] += weights[:, 2 * s + t]
    return table.astype(ml_dtypes.bfloat16)


def slot_table():
    slots = np.split(gather_table(), 6, axis=1)
    rows = [
        np.r_[0:8, 16:24], np.r_[8:16, 24:32], np.arange(32), np.arange(32), np.arange(16), np.arange(16, 32),
    ]
    return np.concatenate([slot[kept] for slot, kept in zip(slots, rows)], axis=0)


slot_rows = (0, 16, 32, 64, 96, 112, 128)


def spread_table(wy, rows):
    weights = lift * corner_table()
    table = np.zeros((3, 48, 2, wy, 6 * rows), np.float64)
    for d in range(3):
        for x in range(2):
            for y in range(wy):
                for s in range(2):
                    for t in range(2):
                        p, q, r = landing(2 * d, s, t)
                        for c in range(3):
                            k = (3 * r + x + p) * rows + 4 * (y + q) + c
                            table[d, 16 * c : 16 * c + 16, x, y, k] += weights[:, 2 * s + t]
    return table.reshape(-1, 6 * rows).astype(ml_dtypes.bfloat16)


def lanes(shape):
    return lax.broadcasted_iota(jnp.int32, shape, len(shape) - 1)


def z_next(value):
    last = value.shape[-1] - 1
    return jnp.where(lanes(value.shape) < last, pltpu.roll(value, last, value.ndim - 1), 0.0)


def z_prev(value):
    return jnp.where(lanes(value.shape) > 0, pltpu.roll(value, 1, value.ndim - 1), 0.0)


def dot(left, right):
    return jnp.dot(left, right, preferred_element_type=F32)


def wide(parts):
    return jnp.concatenate(parts, axis=1)


def tall(parts):
    return jnp.concatenate(parts, axis=0)


def columns(rows, count):
    z = rows.shape[1] // count
    return [rows[:, z * h : z * h + z] for h in range(count)]


def elements(slots):
    return tall([wide([hexa[s] for hexa in slots]) for s in range(6)])


def vertex_part(flux, parts_ref):
    rows = []
    for s in range(6):
        first, size = slot_rows[s], slot_rows[s + 1] - slot_rows[s]
        rows.append(dot(parts_ref[pl.ds(first, size), :], flux[48 * s : 48 * s + 48].astype(BF)))
    rows[2:4] = [rows[2] + rows[3]]
    return tall(rows)


def turned_dot(left, right):
    return lax.dot_general(left, right, (((1,), (1,)), ((), ())), preferred_element_type=F32)


def product(f_ref, st_ref, slot):
    first = 0 if slot is None else 48 * slot
    flux = turned_dot(f_ref[...], st_ref[...] if slot is None else st_ref[pl.ds(first, 48), :])
    rows = lax.broadcasted_iota(jnp.int32, flux.shape, 0)
    return flux, flux + jnp.where(rows == lax.broadcasted_iota(jnp.int32, flux.shape, 1) + first, F32(penalty), F32(0.0))


def slot_corners(traces, parts_ref, slot):
    z = traces[0].shape[1]
    first, size = slot_rows[slot], slot_rows[slot + 1] - slot_rows[slot]
    rows = dot(parts_ref[pl.ds(first, size), :], wide([trace.astype(BF) for trace in traces]))
    return [rows[:, z * h : z * h + z] for h in range(len(traces))]


def settle(rows, p):
    return rows[8 * p : 8 * p + 8] + z_prev(rows[16 + 8 * p : 24 + 8 * p])


def scaled_corners(delta, scales, offsets=(0, 1)):
    shape = (8, delta.shape[1])
    blank = jnp.zeros((1, shape[1]), F32)
    y_scale = jnp.where(
        lax.broadcasted_iota(jnp.int32, shape, 0) < 4,
        blank if scales[2] is None else scales[2], blank if scales[3] is None else scales[3],
    )
    results = []
    for p in offsets:
        parts = []
        for r in range(2):
            at = 32 + 16 * r + 8 * p
            part = delta[at : at + 8] * y_scale + delta[at + 32 : at + 40] * scales[4 + r]
            if scales[p] is not None:
                part = part + delta[16 * p + 8 * r : 16 * p + 8 * r + 8] * scales[p]
            parts.append(part)
        results.append(parts[0] + z_prev(parts[1]))
    return results


def level_visc(code, visc_ref):
    visc = jnp.zeros(code.shape, F32)
    for level in range(visc_ref.shape[0]):
        visc = visc + jnp.where(code == F32(level + 1), visc_ref[pl.ds(level, 1), :], F32(0.0))
    return visc


def merge(even, odd):
    odd = tall(odd)
    return tall(even) + pltpu.roll(odd, odd.shape[0] - 4, 0)


def first_kernel(
    wx, wy, visc_hbm, t_hbm, dir_hbm, cls_hbm, diag_hbm, st_hbm, f_hbm, parts_hbm,
    l_ref, nat, kp_ref, visc_ref, diag_ref, st_ref, f_ref, parts_ref, v_ref, v1_ref, v3_ref,
    inner_ref, outer_ref, down_ref, up_ref, t_ref, dir_ref, cls_ref, levels, sems,
):
    cells = wx * wy
    pairs = [
        (parts_hbm, parts_ref), (f_hbm, f_ref), (st_hbm, st_ref), (t_hbm, t_ref), (dir_hbm, dir_ref),
        (cls_hbm, cls_ref), (visc_hbm, levels), (diag_hbm, diag_ref),
    ]
    copies = [pltpu.make_async_copy(a, b, sems.at[i]) for i, (a, b) in enumerate(pairs)]
    for copy in copies:
        copy.start()
    diagonal = lax.broadcasted_iota(jnp.int32, (288, 288), 0) == lax.broadcasted_iota(jnp.int32, (288, 288), 1)
    diagonal = jnp.where(diagonal, F32(penalty), F32(0.0))
    copies[0].wait()
    own = tall([vertex_part(diagonal, parts_ref), diagonal[144:192]])
    copies[1].wait()
    left = tall([vertex_part(f_ref[...], parts_ref).astype(BF), f_ref[pl.ds(144, 48), :]])
    for copy in copies[2:5]:
        copy.wait()
    short = (turned_dot(left, st_ref[...]) + own).astype(BF)
    z = t_ref.shape[2]
    for d in range(3):
        keep = (1 - dir_ref[d]).astype(F32)
        kp_ref[d] = keep
        masked = t_ref[d].astype(F32).reshape(48, cells, z) * keep[None]
        nat[d] = masked.reshape(48 * cells, z)
        lay_out(wx, wy, d, nat, l_ref, True)
    kp_ref[3] = z_next(kp_ref[2])
    for copy in copies[5:]:
        copy.wait()
    for level in range(visc_ref.shape[0]):
        visc_ref[pl.ds(level, 1), :] = jnp.full((1, z), levels[level], F32)
    code = cls_ref[...].astype(F32) + 1.0
    kp_ref[4] = level_visc(code, visc_ref)
    kp_ref[5] = code
    row = lambda i, col: kp_ref[i, pl.ds(col, 1), :]
    corners = []
    for side, y in enumerate((0, wy - 1)):
        where = [(x, y) for x in range(wx)]
        slots, scales, left_out = known_hexes(wx, wy, where, (l_ref, None), kp_ref)
        rows = columns(dot(short if side else short[0:96], elements(slots)), wx)
        corners += known_corners(rows, scales, left_out)
        v1_ref[side] = rows[wx - 1][16:32] * row(4, (wx - 1) * wy + y)
    place = lax.broadcasted_iota(jnp.int32, (32, z), 0)
    lone = [part * row(4, x * wy + wy - 1) for x, part in enumerate(rows)]
    for x in range(wx):
        v3_ref[x] = jnp.where(lax.rem(place, 8) < 4, 0.0, lone[x][32:64])
    sums = [line_sums(corners[:wx]), line_sums(corners[wx:])]
    for side in range(2):
        for i in range(wx + 1):
            v_ref[side, i] = sums[side][i]
    corner = (wx - 1) * wy
    top = wy - 1
    for x in range(wx):
        down_ref[pl.ds(48 * x, 48), :] = l_ref[1, x * wy]
        up_ref[pl.ds(48 * x, 48), :] = lone[x][96:144].astype(BF)
    down_ref[pl.ds(48 * wx, 48), :] = l_ref[0, 0]
    up_ref[pl.ds(48 * wx, 48), :] = l_ref[0, top]
    flags = [row(1, x * wy) for x in range(wx)] + [row(0, 0), row(5, corner), row(0, corner), row(2, corner)]
    diag = tall([diag_ref[pl.ds(x * wy, 1), :] for x in range(wx)])
    high = diag.astype(BF).astype(F32)
    rim = pack(sums[0], 0) + pack([v1_ref[0, 0:8], v1_ref[0, 8:16]], 0) + flags + [high, diag - high]
    put_tail(down_ref, 48 * wx + 48, rim)
    flags = [row(kind, x * wy + top) for kind in (5, 0, 2) for x in range(wx)]
    rim = pack(sums[1], 1) + pack([v1_ref[1, 0:8], v1_ref[1, 8:16]], 1) + flags
    put_tail(up_ref, 48 * wx + 48, rim)
    depart("gy", down_ref, up_ref, inner_ref, outer_ref)


def tail_rows(count):
    return -(-count // 16) * 16


def put_tail(ref, start, rows):
    count = sum(part.shape[0] for part in rows)
    full = ref.shape[0] - start
    if full > count:
        rows = rows + [jnp.zeros((full - count, rows[0].shape[1]), F32)]
    ref[pl.ds(start, full), :] = tall(rows).astype(BF)


def pack(parts, half):
    place = lax.broadcasted_iota(jnp.int32, parts[0].shape, 0)
    parts = parts + [jnp.zeros_like(parts[0])] * (len(parts) % 2)
    packed = []
    for low, high in zip(parts[0::2], parts[1::2]):
        if half:
            low = pltpu.roll(low, 4, 0)
        else:
            high = pltpu.roll(high, 4, 0)
        packed.append(jnp.where(place < 4, low, high))
    return packed


def unpack(packed, count, half):
    parts = []
    for n in range(count):
        part = packed[8 * (n // 2) : 8 * (n // 2) + 8]
        parts.append(part if n % 2 == half else pltpu.roll(part, 4, 0))
    return parts


def read_tail(ref, wx, half):
    start = 48 * wx + 48
    rows = ref[pl.ds(start, ref.shape[0] - start), :].astype(F32)
    size = 8 * ((wx + 2) // 2)
    return unpack(rows, wx + 1, half), unpack(rows[size : size + 8], 2, half), rows[size + 8 :]


def line_sums(corners):
    low, high = [part[0] for part in corners], [part[1] for part in corners]
    return [low[0]] + [low[x] + high[x - 1] for x in range(1, len(low))] + [high[-1]]


def early(wx, wy, d, x, y):
    return y in (0, wy - 1) or (d == 0 and x == 0) or (d == 1 and y == 1)


def lay_out(wx, wy, d, nat, l_ref, first):
    for x in range(wx):
        for y in range(wy):
            if early(wx, wy, d, x, y) == first:
                col = x * wy + y
                part = nat[d, pl.ds(col, 48, stride=wx * wy), :]
                l_ref[d, col] = part.astype(BF)
                if d == 2:
                    l_ref[3, col] = z_next(part).astype(BF)


def known_hexes(wx, wy, where, l_refs, kp_ref):
    z = l_refs[0].shape[3]
    nothing = jnp.zeros((48, z), BF)
    row = lambda i, col: kp_ref[i, pl.ds(col, 1), :]
    trace = lambda d, x, y: l_refs[0 if early(wx, wy, min(d, 2), x, y) else 1][d, x * wy + y]
    slots, scales, left_out = [], [], []
    for x, y in where:
        here = x * wy + y
        visc = row(4, here)
        last_x, last_y = x == wx - 1, y == wy - 1
        slots.append(
            [
                trace(0, x, y), nothing if last_x else trace(0, x + 1, y),
                trace(1, x, y), nothing if last_y else trace(1, x, y + 1),
                trace(2, x, y), trace(3, x, y),
            ]
        )
        scales.append(
            [
                visc * row(0, here), visc if last_x else visc * row(0, here + wy),
                visc * row(1, here), visc if last_y else visc * row(1, here + 1),
                visc * row(2, here), visc * row(3, here),
            ]
        )
        left_out.append(([1] if last_x else []) + ([3] if last_y else []))
    return slots, scales, left_out


def known_corners(vertex, scales, left_out):
    return [
        scaled_corners(part, [None if s in out else scale[s] for s in range(6)])
        for part, scale, out in zip(vertex, scales, left_out)
    ]


def middle_kernel(
    wx, wy, l_ref, nat, kp_ref, st_ref, f_ref, parts_ref,
    c_ref, v_ref, v1_ref, mx_ref, my_ref, own_ref, rest_ref, m_ref, lost_ref,
):
    for slot, ref in ((1, mx_ref), (3, my_ref)):
        bare, flux = product(f_ref, st_ref, slot)
        turned = tall([bare[0:48], bare[96:288], bare[48:96]]) if slot == 1 else bare
        ref[pl.ds(0, 288), :] = turned.astype(BF)
        ref[pl.ds(288, 96), :] = vertex_part(flux, parts_ref).astype(BF)
    flux = product(f_ref, st_ref, None)[1]
    m_ref[pl.ds(0, 288), :] = flux.astype(BF)
    m_ref[pl.ds(288, 96), :] = vertex_part(flux, parts_ref).astype(BF)
    lost_ref[...] = (flux - flux.astype(BF).astype(F32))[:, 0:256].astype(BF)
    for d in range(3):
        lay_out(wx, wy, d, nat, rest_ref, False)
    own_ref[...] = dot(
        tall([my_ref[pl.ds(144, 48), :], my_ref[pl.ds(288, 96), :]]), wide([l_ref[1, x * wy] for x in range(wx)])
    )
    for y in range(wy):
        inside = 0 < y < wy - 1
        where = [(x, y) for x in range(wx)]
        slots, scales, left_out = known_hexes(wx, wy, where, (l_ref, rest_ref), kp_ref)
        element = elements(slots)
        rows = dot(m_ref[...] if inside else m_ref[pl.ds(0, 288), :], element)
        lost = columns(dot(lost_ref[...], element[0:256]), wx)
        rows = columns(rows, wx)
        for x in range(wx):
            for s in range(6):
                part = slice(48 * s, 48 * s + 48)
                c_ref[s, x * wy + y] = (rows[x][part] + lost[x][part]) * scales[x][s]
        if inside:
            corners = known_corners([part[288:] for part in rows], scales, left_out)
            v1_ref[y - 1] = rows[wx - 1][304:320] * kp_ref[4, pl.ds((wx - 1) * wy + y, 1), :]
            for i, part in enumerate(line_sums(corners)):
                v_ref[y - 1, i] = part


def after_y(wx, wy, xs, visc_ref, l_ref, kp_ref, parts_ref, my_ref, own_ref, v3_ref, down_ref, up_ref):
    z = l_ref.shape[3]
    misc_d = read_tail(down_ref, wx, 0)[2]
    misc_u = read_tail(up_ref, wx, 1)[2]
    row = lambda i, col: kp_ref[i, pl.ds(col, 1), :]
    delta = dot(my_ref[...], wide([down_ref[pl.ds(48 * x, 48), :] for x in xs]))
    arrived = [up_ref[pl.ds(48 * x, 48), :].astype(F32) for x in xs]
    arrived_corners = slot_corners(arrived, parts_ref, 3)
    results = []
    for n, x in enumerate(xs):
        here = x * wy + wy - 1
        last = x == wx - 1
        part = delta[:, z * n : z * n + z]
        visc = row(4, here)
        scales = [
            visc * row(0, here), visc if last else visc * row(0, here + wy), visc * row(1, here),
            visc * misc_d[x : x + 1], visc * row(2, here), visc * row(3, here),
        ]
        flux = [part[48 * s : 48 * s + 48] * scales[s] for s in range(6)]
        used = [None if (s == 1 and last) else scales[s] for s in range(6)]
        known = v3_ref[x] * misc_d[x : x + 1]
        top = [rows + settle(known, p) for p, rows in enumerate(scaled_corners(part[288:384], used))]
        top_one = part[304:320] * visc
        here = x * wy
        visc = level_visc(misc_u[x : x + 1], visc_ref)
        flag = row(1, here)
        own = own_ref[:, pl.ds(z * x, z)]
        keep_z = misc_u[2 * wx + x : 2 * wx + x + 1]
        scales = [
            visc * misc_u[wx + x : wx + x + 1], None if last else visc * misc_u[wx + x + 1 : wx + x + 2],
            None, visc * flag, visc * keep_z, visc * z_next(keep_z),
        ]
        known = arrived_corners[n] * flag
        low = [rows + settle(known, p) for p, rows in enumerate(scaled_corners(own[48:144], scales))]
        low_one = own[64:80] * visc
        face = (arrived[n] + visc * (own[0:48] + penalty * l_ref[1, here].astype(F32))) * flag
        results.append((flux, top, top_one, low, low_one, face))
    return results


def turn_kernel(
    wx, wy, visc_ref, l_ref, kp_ref, diag_ref, parts_ref, my_ref, own_ref, c_ref, va_ref, vb_ref,
    v1a_ref, v1b_ref, v3_ref, outer_in, inner_in,
    c3_ref, vt_ref, vl_ref, v1_ref, face_ref, yd_ref, yu_ref, inner_ref, outer_ref, down_ref, up_ref,
):
    z = l_ref.shape[3]
    arrive("gy", inner_in, outer_in, yd_ref, yu_ref)
    xs = (0, wx - 1)
    results = after_y(wx, wy, xs, visc_ref, l_ref, kp_ref, parts_ref, my_ref, own_ref, v3_ref, yd_ref, yu_ref)
    row = lambda i, col: kp_ref[i, pl.ds(col, 1), :]
    sums_d, one_d, misc_d = read_tail(yd_ref, wx, 0)
    sums_u, one_u, misc_u = read_tail(yu_ref, wx, 1)
    edge_high, edge_low = misc_d[wx + 4 : 2 * wx + 4], misc_d[2 * wx + 4 : 3 * wx + 4]
    for n, (flux, top, top_one, low, low_one, face) in enumerate(results):
        for s in range(6):
            c3_ref[n, s] = flux[s]
        face_ref[n] = face
        for p in range(2):
            vt_ref[n, p] = top[p]
            vl_ref[n, p] = low[p]
    flux, top, top_one, low, low_one, face = results[1]
    mine = tall(one_u) + low_one
    v1_ref[0] = mine
    v1_ref[1] = v1a_ref[0]
    for y in range(wy - 2):
        v1_ref[2 + y] = v1b_ref[y]
    v1_ref[wy] = v1a_ref[1] + top_one
    v1_ref[wy + 1] = tall(one_d)

    def plane(i, n, p):
        lines = [sums_u[i] + vl_ref[n, p], va_ref[0, i]]
        lines += [vb_ref[y, i] for y in range(wy - 2)]
        lines += [va_ref[1, i] + vt_ref[n, p], sums_d[i]]
        return merge(lines[1::2], lines[0::2])

    down_ref[pl.ds(0, 48), :] = yu_ref[pl.ds(48 * wx, 48), :]
    for y in range(wy):
        down_ref[pl.ds(48 + 48 * y, 48), :] = l_ref[0, y]
    down_ref[pl.ds(48 * (wy + 1), 48), :] = yd_ref[pl.ds(48 * wx, 48), :]
    diag = diag_ref[pl.ds(0, wy), :]
    high = diag.astype(BF).astype(F32)
    rim = [plane(0, 0, 0), high, edge_high[0:1], diag - high, edge_low[0:1]]
    rim += [misc_u[wx : wx + 1], kp_ref[0, 0:wy], misc_d[wx : wx + 1]]
    put_tail(down_ref, 48 * (wy + 2), rim)
    corner = (wx - 1) * wy
    for y in range(wy):
        part = c_ref[1, corner + y]
        up_ref[pl.ds(48 * y, 48), :] = (part + flux[1] if y == wy - 1 else part).astype(BF)
    last = pl.ds(corner, wy)
    rim = [plane(wx, 1, 1), mine, *one_d]
    rim += [misc_u[wx - 1 : wx], kp_ref[5, last], misc_d[wx + 1 : wx + 2]]
    rim += [misc_u[3 * wx - 1 : 3 * wx], kp_ref[2, last], misc_d[wx + 3 : wx + 4]]
    rim += [kp_ref[1, last], misc_d[wx - 1 : wx]]
    put_tail(up_ref, 48 * wy, rim)
    depart("gx", down_ref, up_ref, inner_ref, outer_ref)


def assemble_kernel(
    wx, wy, visc_ref, l_ref, kp_ref, diag_ref, parts_ref, mx_ref, my_ref, own_ref, c_ref, c3_ref,
    va_ref, vb_ref, v3_ref, vt_ref, vl_ref, face_ref, yd_ref, yu_ref,
    r_ref, late_ref, v_ref, inv_ref, ownx_ref, mid,
):
    z = l_ref.shape[3]
    cells = wx * wy
    xs = tuple(range(1, wx - 1))
    results = after_y(wx, wy, xs, visc_ref, l_ref, kp_ref, parts_ref, my_ref, own_ref, v3_ref, yd_ref, yu_ref)
    for n, part in enumerate(results):
        for s in range(6):
            mid[n, s] = part[0][s]
    traces = [yu_ref[pl.ds(48 * wx, 48), :]] + [l_ref[0, y] for y in range(wy)] + [yd_ref[pl.ds(48 * wx, 48), :]]
    ownx_ref[...] = dot(mx_ref[pl.ds(240, 144), :], wide(traces))

    def contrib(slot, x, y):
        here = c_ref[slot, x * wy + y]
        if y < wy - 1:
            return here
        return here + (mid[x - 1, slot] if 0 < x < wx - 1 else c3_ref[0 if x == 0 else 1, slot])

    for x in range(wx):
        for y in range(wy):
            col = pl.ds(x * wy + y, 48, stride=cells)
            if y:
                behind = contrib(3, x, y - 1)
            elif 0 < x < wx - 1:
                behind = results[x - 1][5]
            else:
                behind = face_ref[0 if x == 0 else 1]
            ahead = contrib(0, x, y) + contrib(1, x - 1, y) if x else contrib(0, x, y)
            sides = [ahead, contrib(2, x, y) + behind, contrib(4, x, y) + z_prev(contrib(5, x, y))]
            for d in range(3):
                if x == wx - 1:
                    late_ref[d, y] = sides[d]
                elif d == 0 and x == 0:
                    late_ref[3, y] = sides[d]
                else:
                    r_ref[d, col, :] = sides[d]
    sums_d, one_d, misc_d = read_tail(yd_ref, wx, 0)
    sums_u, one_u, misc_u = read_tail(yu_ref, wx, 1)
    edge_diag = misc_d[wx + 4 : 2 * wx + 4] + misc_d[2 * wx + 4 : 3 * wx + 4]

    def brought(which, i):
        held = vt_ref if which == 1 else vl_ref
        terms = []
        for x, p in ((i, 0), (i - 1, 1)):
            if x in (0, wx - 1):
                terms.append(held[0 if x == 0 else 1, p])
            elif 0 < x < wx - 1:
                terms.append(results[x - 1][which][p])
        return sum(terms[1:], terms[0])

    for i in range(wx + 1):
        lines = [sums_u[i] + brought(3, i), va_ref[0, i]]
        lines += [vb_ref[y, i] for y in range(wy - 2)]
        lines += [va_ref[1, i] + brought(1, i), sums_d[i]]
        v_ref[i] = merge(lines[1::2], lines[0::2])
        if i < wx:
            parts = [jnp.broadcast_to(diag_ref[pl.ds(i * wy + y, 1), :], (4, z)) for y in range(wy)]
            parts += [jnp.broadcast_to(edge_diag[i : i + 1], (4, z)), jnp.zeros((4, z), F32)]
            inv_ref[i] = reciprocal(tall(parts))


def reciprocal(diag):
    present = diag > 0.0
    return jnp.where(present, (1.0 / (gain * gain)) / jnp.where(present, diag, 1.0), 0.0)


def final_kernel(
    wx, wy, visc_ref, l_ref, kp_ref, parts_ref, mx_ref, ownx_ref, r_in, late_ref, v_ref, inv_ref, v1_ref,
    yd_ref, yu_ref, outer_in, inner_in, p_ref, out_hbm, r_ref, held, sems,
):
    here, last = lax.axis_index("gx"), lax.axis_size("gx") - 1

    def from_high(start, size):
        rows = pl.ds(start, size)
        value = jnp.where(even("gx"), inner_in[rows, :], outer_in[rows, :])
        return jnp.where(here < last, value, jnp.zeros_like(value))

    def from_low(start, size):
        rows = pl.ds(start, size)
        value = jnp.where(even("gx"), outer_in[rows, :], inner_in[rows, :])
        return jnp.where(here > 0, value, jnp.zeros_like(value))

    cells, z = wx * wy, l_ref.shape[3]
    rows = v_ref.shape[1]
    row = lambda i, col: kp_ref[i, pl.ds(col, 1), :]
    traces = [from_high(48 * j, 48) for j in range(wy + 2)]
    delta = dot(mx_ref[pl.ds(288, 96), :], wide(traces))
    rim_x = from_high(48 * (wy + 2), tail_rows(rows + 3 * wy + 4)).astype(F32)
    rim_l = from_low(48 * wy, tail_rows(rows + 32 + 3 * (wy + 2) - 1)).astype(F32)
    misc_d = read_tail(yd_ref, wx, 0)[2]
    misc_u = read_tail(yu_ref, wx, 1)[2]
    flags_high = rim_x[rows + 2 * (wy + 1) : rows + 3 * wy + 4]
    corner = (wx - 1) * wy
    arrived = [from_low(48 * y, 48) for y in range(wy)]
    arrived_corners = slot_corners(arrived, parts_ref, 1)
    codes = rim_l[rows + 32 : rows + 32 + wy + 2]
    keep_z = rim_l[rows + 32 + wy + 2 : rows + 32 + 2 * (wy + 2)]
    keep_y = rim_l[rows + 32 + 2 * (wy + 2) : rows + 32 + 3 * (wy + 2) - 1]
    low_visc = level_visc(codes, visc_ref)
    low_keep_z = z_next(keep_z)
    lines = [[], [], []]
    high_scales = []
    del r_in
    for j in range(-1, wy + 1):
        n = j + 1
        part = delta[:, z * n : z * n + z]
        flag = flags_high[n : n + 1]
        if j < 0:
            visc = level_visc(misc_u[wx - 1 : wx], visc_ref)
            kz = misc_u[3 * wx - 1 : 3 * wx]
            keeps = [misc_u[2 * wx - 1 : 2 * wx], flag, None, row(1, corner), kz, z_next(kz)]
        elif j < wy:
            here = corner + j
            visc = row(4, here)
            high_y = row(1, here + 1) if j < wy - 1 else misc_d[wx - 1 : wx]
            keeps = [row(0, here), flag, row(1, here), high_y, row(2, here), row(3, here)]
        else:
            visc = level_visc(misc_d[wx + 1 : wx + 2], visc_ref)
            kz = misc_d[wx + 3 : wx + 4]
            keeps = [misc_d[wx + 2 : wx + 3], flag, misc_d[wx - 1 : wx], None, kz, z_next(kz)]
        scales = [None if keep is None else visc * keep for keep in keeps]
        corners = scaled_corners(part, scales)
        one = v1_ref[n] * flag
        lines[0].append(corners[0])
        lines[1].append(corners[1] + one[0:8] + z_prev(one[8:16]))
        high_scales.append(scales)
        own = ownx_ref[:, pl.ds(z * n, z)]
        visc = low_visc[n : n + 1]
        flag = misc_u[wx : wx + 1] if j < 0 else misc_d[wx : wx + 1] if j == wy else row(0, j)
        scales = [
            None, visc * flag, None if j < 0 else visc * keep_y[j : j + 1],
            None if j == wy else visc * keep_y[j + 1 : j + 2], visc * keep_z[n : n + 1], visc * low_keep_z[n : n + 1],
        ]
        corners = scaled_corners(own[48:144], scales, (1,))[0]
        if 0 <= j < wy:
            one = arrived_corners[j] * flag
            lines[2].append(corners + one[0:8] + z_prev(one[8:16]))
            face = (arrived[j].astype(F32) + visc * (own[0:48] + penalty * l_ref[0, j].astype(F32))) * flag
            r_ref[0, pl.ds(j, 48, stride=cells), :] = late_ref[3, j] + face
        else:
            at = rows + (0 if j < 0 else 16)
            one = rim_l[at : at + 16] * flag
            lines[2].append(corners + one[0:8] + z_prev(one[8:16]))
    low, before, first = [merge(part[1::2], part[0::2]) for part in lines]
    top = v_ref[wx] + before + rim_x[0:rows]
    values = [(v_ref[0] + first + rim_l[0:rows]) * inv_ref[0]]
    values += [v_ref[i] * inv_ref[i] for i in range(1, wx - 1)]
    values += [(v_ref[wx - 1] + low) * inv_ref[wx - 1]]
    diag = rim_x[rows : rows + wy + 1] + rim_x[rows + wy + 1 : rows + 2 * (wy + 1)]
    parts = [jnp.broadcast_to(diag[j : j + 1], (4, z)) for j in range(wy + 1)]
    values += [top * reciprocal(tall(parts + [jnp.zeros((rows - 4 * (wy + 1), z), F32)]))]
    low = [tall(values[x : x + 3]) for x in range(0, wx, 2)]
    rhs = tall([wide(low), wide([z_next(part) for part in low])]).astype(BF)
    delta = columns(dot(mx_ref[pl.ds(0, 240), :], wide(traces[1 : wy + 1])), wy)
    behind = dot(mx_ref[pl.ds(96, 48), :], traces[0]) * high_scales[0][3]
    size = 96 * wy
    copies = []
    spreads = [dot(p_ref[pl.ds(size * d, size), :], rhs) for d in range(3)]
    for d in range(3):
        for j in range(wy):
            scales = high_scales[j + 1]
            part = [delta[j][48 * i : 48 * i + 48] for i in range(5)]
            if d == 0:
                flux = part[0] * scales[0]
            elif d == 1:
                flux = part[1] * scales[2] + behind
                behind = part[2] * scales[3]
            else:
                flux = part[3] * scales[4] + z_prev(part[4] * scales[5])
            r_ref[d, pl.ds(corner + j, 48, stride=cells), :] = late_ref[d, j] + flux
        spread = spreads[d]
        spread = jnp.concatenate(
            [spread[:, z * g : z * g + z].reshape(48, 2 * wy, z) for g in range(wx // 2)], axis=1
        )
        total = r_ref[d].reshape(48, cells, z) + spread * kp_ref[d][None]
        held[d] = total.reshape(48 * cells, z).astype(BF)
        copies.append(pltpu.make_async_copy(held.at[d], out_hbm.at[d], sems.at[d]))
        copies[d].start()
    for copy in copies:
        copy.wait()


def call(body, args, outs, scratch, flops, hbm=False, aliases=None):
    if hbm:
        args = tuple(pltpu.with_memory_space_constraint(a, pltpu.HBM) for a in args)
    keywords = {}
    if aliases:
        spaces = [pltpu.HBM] + [pltpu.VMEM] * (len(outs) - 1)
        keywords = dict(out_specs=tuple(pl.BlockSpec(memory_space=space) for space in spaces), input_output_aliases=aliases)
    return pl.pallas_call(
        body,
        **keywords,
        in_specs=[pl.BlockSpec(memory_space=pltpu.HBM if hbm else pltpu.VMEM)] * len(args),
        out_shape=outs,
        scratch_shapes=scratch,
        cost_estimate=pl.CostEstimate(flops=flops, bytes_accessed=1000000, transcendentals=0),
        compiler_params=pltpu.CompilerParams(vmem_limit_bytes=16 * 1024 * 1024),
    )(*args)


def local(traces, dirichlet, visc_class, viscosity, coarse_diag, solve_map, flux_map):
    wx, wy, z = traces.shape[2:]
    cells = wx * wy
    rows = 8 * (wy // 2 + 1)
    per_hex = 2 * 384 * 288 * z
    parts = jnp.asarray(slot_table())
    spread = jnp.asarray(spread_table(wy, rows))
    vm = pltpu.VMEM
    bind = lambda body: functools.partial(body, wx, wy)
    y_message = vm((48 * wx + 48 + tail_rows(8 * ((wx + 2) // 2) + 8 + 3 * wx + 4), z), BF)
    x_message = vm((48 * (wy + 2) + tail_rows(rows + 3 * wy + 4), z), BF)

    (lifted, nat, flags, visc, diag, s_turned, f_map, parts, va, v1a, v3, inner, outer) = call(
        bind(first_kernel),
        (
            viscosity, traces.reshape(3, 48 * cells, z), dirichlet.reshape(3, cells, z),
            visc_class.reshape(cells, z), coarse_diag.reshape(cells, z), solve_map.T, flux_map, parts,
        ),
        (
            vm((4, cells, 48, z), BF), vm((3, 48 * cells, z), F32), vm((6, cells, z), F32), vm((viscosity.shape[0], z), F32), vm((cells, z), F32),
            vm(solve_map.shape[::-1], BF), vm(flux_map.shape, BF), vm(parts.shape, BF),
            vm((2, wx + 1, 8, z), F32), vm((2, 16, z), F32), vm((wx, 32, z), F32),
            y_message, y_message,
        ),
        [
            y_message, y_message,
            vm((3, 48 * cells, z), BF), vm((3, cells, z), jnp.int32), vm((cells, z), jnp.int32),
            pltpu.SMEM(viscosity.shape, F32), pltpu.SemaphoreType.DMA((8,)),
        ],
        wx * per_hex, True,
    )
    inner = swap(inner, "gy", "gx", 0)
    outer = swap(outer, "gy", "gx", 1)
    c, vb, v1b, mx, my, own = call(
        bind(middle_kernel),
        (lifted, nat, flags, s_turned, f_map, parts),
        (
            vm((6, cells, 48, z), F32), vm((wy - 2, wx + 1, 8, z), F32), vm((wy - 2, 16, z), F32),
            vm((384, 48), BF), vm((384, 48), BF), vm((144, wx * z), F32),
        ),
        [vm((4, cells, 48, z), BF), vm((384, 288), BF), vm((288, 256), BF)], cells * per_hex,
    )
    c3, vt, vl, v1, face, yd, yu, inner, outer = call(
        bind(turn_kernel),
        (
            visc, lifted, flags, diag, parts, my, own, c, va, vb, v1a, v1b, v3, outer, inner,
        ),
        (
            vm((2, 6, 48, z), F32), vm((2, 2, 8, z), F32), vm((2, 2, 8, z), F32), vm((wy + 2, 16, z), F32),
            vm((2, 48, z), F32), y_message, y_message, x_message, x_message,
        ),
        [x_message, x_message], 2 * per_hex,
    )
    inner = swap(inner, "gx", "gy", 0)
    outer = swap(outer, "gx", "gy", 1)
    residual, late, vs, inverse, ownx = call(
        bind(assemble_kernel),
        (
            visc, lifted, flags, diag, parts, mx, my, own, c, c3, va, vb, v3, vt, vl, face, yd, yu,
        ),
        (
            vm((3, 48 * cells, z), F32), vm((4, wy, 48, z), F32), vm((wx + 1, rows, z), F32), vm((wx, rows, z), F32),
            vm((144, (wy + 2) * z), F32),
        ),
        [vm((wx - 2, 6, 48, z), F32)], 4 * per_hex,
    )
    out, _ = call(
        bind(final_kernel),
        (
            visc, lifted, flags, parts, mx, ownx, residual, late, vs, inverse, v1, yd, yu, outer, inner, spread,
        ),
        (jax.ShapeDtypeStruct((3, 48 * cells, z), BF), vm((3, 48 * cells, z), F32)),
        [vm((3, 48 * cells, z), BF), pltpu.SemaphoreType.DMA((3,))], 4 * spread.size * z,
        aliases={6: 1},
    )
    return out.reshape(traces.shape)


def solution(mesh):
    in_specs = (
        P(None, None, "gx", "gy", None),
        P(None, "gx", "gy", None),
        P("gx", "gy", None),
        P(),
        P("gx", "gy", None),
        P(),
        P(),
    )
    out_specs = P(None, None, "gx", "gy", None)
    return jax.shard_map(local, mesh=mesh, in_specs=in_specs, out_specs=out_specs, check_vma=False)
```

```python
import functools
import math

import jax
import jax.numpy as jnp
import ml_dtypes
import numpy as np
from jax import lax
from jax.experimental import pallas as pl
from jax.experimental.pallas import tpu as pltpu
from jax.sharding import PartitionSpec as P

penalty = 0.5
BF = jnp.bfloat16
F32 = jnp.float32
lift = 1.3264
gain = 1.3280711361297461


def swap(value, axis, other, first, step=2):
    count, width = lax.axis_size(axis), lax.axis_size(other)
    place = (lambda i, j: i * width + j) if (axis, other) == ("gx", "gy") else (lambda i, j: j * count + i)
    lows = list(range(first, count - 1, step))
    pairs = [(place(low, j), place(low + 1, j)) for low in lows for j in range(width)]
    alone = [i for i in range(count) if i not in lows and i - 1 not in lows]
    pairs += [(place(i, j), place(i, j + 1)) for i in alone for j in range(0, width - 1, 2)]
    return lax.ppermute(value, ("gx", "gy"), pairs + [(high, low) for low, high in pairs])


def even(axis):
    return lax.rem(lax.axis_index(axis), 2) == 0


def arrive(messages, down_ref, up_ref):
    here, last = lax.axis_index("gy"), lax.axis_size("gy") - 1
    values = [ref[...] for ref in messages]
    for ref, swap_of, present in ((down_ref, lax.rem(here, 3), here < last), (up_ref, lax.rem(here + 2, 3), here > 0)):
        value = jnp.where(swap_of == 0, values[0], jnp.where(swap_of == 1, values[1], values[2]))
        ref[...] = jnp.where(present, value, jnp.zeros_like(value))


def depart_three(down_ref, up_ref, messages):
    here = lax.rem(lax.axis_index("gy"), 3)
    for k, ref in enumerate(messages):
        choose(here == k, up_ref, down_ref, ref)


def depart(axis, down_ref, up_ref, inner_ref, outer_ref):
    choose(even(axis), up_ref, down_ref, inner_ref)
    choose(even(axis), down_ref, up_ref, outer_ref)


def choose(condition, yes_ref, no_ref, out_ref, present=None):
    value = jnp.where(condition, yes_ref[...], no_ref[...])
    out_ref[...] = value if present is None else jnp.where(present, value, jnp.zeros_like(value))


def corner_table():
    gll_points = [-1.0, -math.sqrt(0.2), math.sqrt(0.2), 1.0]
    table = np.zeros((16, 4), np.float64)
    for s in range(4):
        for t in range(4):
            for p in range(2):
                for q in range(2):
                    table[4 * s + t, 2 * p + q] = (
                        (1 + (2 * p - 1) * gll_points[s]) * (1 + (2 * q - 1) * gll_points[t]) / 4
                    )
    return table


def landing(face_slot, high_s, high_t):
    direction, outward = divmod(face_slot, 2)
    if direction == 0:
        return (outward, high_s, high_t)
    if direction == 1:
        return (high_s, outward, high_t)
    return (high_s, high_t, outward)


def gather_table():
    weights = lift * corner_table()
    table = np.zeros((32, 288), np.float64)
    for slot in range(6):
        for s in range(2):
            for t in range(2):
                p, q, r = landing(slot, s, t)
                for c in range(3):
                    cols = slot * 48 + 16 * c + np.arange(16)
                    table[16 * r + 8 * p + 4 * q + c, cols] += weights[:, 2 * s + t]
    return table.astype(ml_dtypes.bfloat16)


def slot_table():
    slots = np.split(gather_table(), 6, axis=1)
    rows = [
        np.r_[0:8, 16:24], np.r_[8:16, 24:32], np.arange(32), np.arange(32), np.arange(16), np.arange(16, 32),
    ]
    return np.concatenate([slot[kept] for slot, kept in zip(slots, rows)], axis=0)


slot_rows = (0, 16, 32, 64, 96, 112, 128)


def spread_table(wy, rows):
    weights = lift * corner_table()
    table = np.zeros((3, 48, 2, wy, 6 * rows), np.float64)
    for d in range(3):
        for x in range(2):
            for y in range(wy):
                for s in range(2):
                    for t in range(2):
                        p, q, r = landing(2 * d, s, t)
                        for c in range(3):
                            k = (3 * r + x + p) * rows + 4 * (y + q) + c
                            table[d, 16 * c : 16 * c + 16, x, y, k] += weights[:, 2 * s + t]
    return table.reshape(-1, 6 * rows).astype(ml_dtypes.bfloat16)


def lanes(shape):
    return lax.broadcasted_iota(jnp.int32, shape, len(shape) - 1)


def z_next(value):
    last = value.shape[-1] - 1
    return jnp.where(lanes(value.shape) < last, pltpu.roll(value, last, value.ndim - 1), 0.0)


def z_prev(value):
    return jnp.where(lanes(value.shape) > 0, pltpu.roll(value, 1, value.ndim - 1), 0.0)


def dot(left, right):
    return jnp.dot(left, right, preferred_element_type=F32)


def wide(parts):
    return jnp.concatenate(parts, axis=1)


def tall(parts):
    return jnp.concatenate(parts, axis=0)


def columns(rows, count):
    z = rows.shape[1] // count
    return [rows[:, z * h : z * h + z] for h in range(count)]


def elements(slots):
    return tall([wide([hexa[s] for hexa in slots]) for s in range(6)])


def vertex_part(flux, parts_ref):
    rows = []
    for s in range(6):
        first, size = slot_rows[s], slot_rows[s + 1] - slot_rows[s]
        rows.append(dot(parts_ref[pl.ds(first, size), :], flux[48 * s : 48 * s + 48].astype(BF)))
    rows[2:4] = [rows[2] + rows[3]]
    return tall(rows)


def turned_dot(left, right):
    return lax.dot_general(left, right, (((1,), (1,)), ((), ())), preferred_element_type=F32)


def product(f_ref, st_ref, slot):
    first = 0 if slot is None else 48 * slot
    flux = turned_dot(f_ref[...], st_ref[...] if slot is None else st_ref[pl.ds(first, 48), :])
    rows = lax.broadcasted_iota(jnp.int32, flux.shape, 0)
    return flux, flux + jnp.where(rows == lax.broadcasted_iota(jnp.int32, flux.shape, 1) + first, F32(penalty), F32(0.0))


def slot_corners(traces, parts_ref, slot):
    z = traces[0].shape[1]
    first, size = slot_rows[slot], slot_rows[slot + 1] - slot_rows[slot]
    rows = dot(parts_ref[pl.ds(first, size), :], wide([trace.astype(BF) for trace in traces]))
    return [rows[:, z * h : z * h + z] for h in range(len(traces))]


def settle(rows, p):
    return rows[8 * p : 8 * p + 8] + z_prev(rows[16 + 8 * p : 24 + 8 * p])


def scaled_corners(delta, scales, offsets=(0, 1)):
    shape = (8, delta.shape[1])
    blank = jnp.zeros((1, shape[1]), F32)
    y_scale = jnp.where(
        lax.broadcasted_iota(jnp.int32, shape, 0) < 4,
        blank if scales[2] is None else scales[2], blank if scales[3] is None else scales[3],
    )
    results = []
    for p in offsets:
        parts = []
        for r in range(2):
            at = 32 + 16 * r + 8 * p
            part = delta[at : at + 8] * y_scale + delta[at + 32 : at + 40] * scales[4 + r]
            if scales[p] is not None:
                part = part + delta[16 * p + 8 * r : 16 * p + 8 * r + 8] * scales[p]
            parts.append(part)
        results.append(parts[0] + z_prev(parts[1]))
    return results


def level_visc(code, visc_ref):
    visc = jnp.zeros(code.shape, F32)
    for level in range(visc_ref.shape[0]):
        visc = visc + jnp.where(code == F32(level + 1), visc_ref[pl.ds(level, 1), :], F32(0.0))
    return visc


def merge(even, odd):
    odd = tall(odd)
    return tall(even) + pltpu.roll(odd, odd.shape[0] - 4, 0)


def first_kernel(
    wx, wy, visc_hbm, t_hbm, dir_hbm, cls_hbm, diag_hbm, st_hbm, f_hbm, parts_hbm,
    l_ref, nat, kp_ref, visc_ref, diag_ref, st_ref, f_ref, parts_ref, v_ref, v1_ref, v3_ref,
    swap0_ref, swap1_ref, swap2_ref, down_ref, up_ref, t_ref, dir_ref, cls_ref, levels, sems,
):
    cells = wx * wy
    pairs = [
        (parts_hbm, parts_ref), (f_hbm, f_ref), (st_hbm, st_ref), (t_hbm, t_ref), (dir_hbm, dir_ref),
        (cls_hbm, cls_ref), (visc_hbm, levels), (diag_hbm, diag_ref),
    ]
    copies = [pltpu.make_async_copy(a, b, sems.at[i]) for i, (a, b) in enumerate(pairs)]
    for copy in copies:
        copy.start()
    diagonal = lax.broadcasted_iota(jnp.int32, (288, 288), 0) == lax.broadcasted_iota(jnp.int32, (288, 288), 1)
    diagonal = jnp.where(diagonal, F32(penalty), F32(0.0))
    copies[0].wait()
    own = tall([vertex_part(diagonal, parts_ref), diagonal[144:192]])
    copies[1].wait()
    left = tall([vertex_part(f_ref[...], parts_ref).astype(BF), f_ref[pl.ds(144, 48), :]])
    for copy in copies[2:5]:
        copy.wait()
    short = (turned_dot(left, st_ref[...]) + own).astype(BF)
    z = t_ref.shape[2]
    for d in range(3):
        keep = (1 - dir_ref[d]).astype(F32)
        kp_ref[d] = keep
        masked = t_ref[d].astype(F32).reshape(48, cells, z) * keep[None]
        nat[d] = masked.reshape(48 * cells, z)
        lay_out(wx, wy, d, nat, l_ref, True)
    kp_ref[3] = z_next(kp_ref[2])
    for copy in copies[5:]:
        copy.wait()
    for level in range(visc_ref.shape[0]):
        visc_ref[pl.ds(level, 1), :] = jnp.full((1, z), levels[level], F32)
    code = cls_ref[...].astype(F32) + 1.0
    kp_ref[4] = level_visc(code, visc_ref)
    kp_ref[5] = code
    row = lambda i, col: kp_ref[i, pl.ds(col, 1), :]
    corners = []
    for side, y in enumerate((0, wy - 1)):
        where = [(x, y) for x in range(wx)]
        slots, scales, left_out = known_hexes(wx, wy, where, (l_ref, None), kp_ref)
        rows = columns(dot(short if side else short[0:96], elements(slots)), wx)
        corners += known_corners(rows, scales, left_out)
        v1_ref[side] = rows[wx - 1][16:32] * row(4, (wx - 1) * wy + y)
    place = lax.broadcasted_iota(jnp.int32, (32, z), 0)
    lone = [part * row(4, x * wy + wy - 1) for x, part in enumerate(rows)]
    for x in range(wx):
        v3_ref[x] = jnp.where(lax.rem(place, 8) < 4, 0.0, lone[x][32:64])
    sums = [line_sums(corners[:wx]), line_sums(corners[wx:])]
    for side in range(2):
        for i in range(wx + 1):
            v_ref[side, i] = sums[side][i]
    corner = (wx - 1) * wy
    top = wy - 1
    for x in range(wx):
        down_ref[pl.ds(48 * x, 48), :] = l_ref[1, x * wy]
        up_ref[pl.ds(48 * x, 48), :] = lone[x][96:144].astype(BF)
    down_ref[pl.ds(48 * wx, 48), :] = l_ref[0, 0]
    up_ref[pl.ds(48 * wx, 48), :] = l_ref[0, top]
    flags = [row(1, x * wy) for x in range(wx)] + [row(0, 0), row(5, corner), row(0, corner), row(2, corner)]
    diag = tall([diag_ref[pl.ds(x * wy, 1), :] for x in range(wx)])
    high = diag.astype(BF).astype(F32)
    rim = pack(sums[0], 0) + pack([v1_ref[0, 0:8], v1_ref[0, 8:16]], 0) + flags + [high, diag - high]
    put_tail(down_ref, 48 * wx + 48, rim)
    flags = [row(kind, x * wy + top) for kind in (5, 0, 2) for x in range(wx)]
    rim = pack(sums[1], 1) + pack([v1_ref[1, 0:8], v1_ref[1, 8:16]], 1) + flags
    put_tail(up_ref, 48 * wx + 48, rim)
    depart_three(down_ref, up_ref, (swap0_ref, swap1_ref, swap2_ref))


def tail_rows(count):
    return -(-count // 16) * 16


def put_tail(ref, start, rows):
    count = sum(part.shape[0] for part in rows)
    full = ref.shape[0] - start
    if full > count:
        rows = rows + [jnp.zeros((full - count, rows[0].shape[1]), F32)]
    ref[pl.ds(start, full), :] = tall(rows).astype(BF)


def pack(parts, half):
    place = lax.broadcasted_iota(jnp.int32, parts[0].shape, 0)
    parts = parts + [jnp.zeros_like(parts[0])] * (len(parts) % 2)
    packed = []
    for low, high in zip(parts[0::2], parts[1::2]):
        if half:
            low = pltpu.roll(low, 4, 0)
        else:
            high = pltpu.roll(high, 4, 0)
        packed.append(jnp.where(place < 4, low, high))
    return packed


def unpack(packed, count, half):
    parts = []
    for n in range(count):
        part = packed[8 * (n // 2) : 8 * (n // 2) + 8]
        parts.append(part if n % 2 == half else pltpu.roll(part, 4, 0))
    return parts


def read_tail(ref, wx, half):
    start = 48 * wx + 48
    rows = ref[pl.ds(start, ref.shape[0] - start), :].astype(F32)
    size = 8 * ((wx + 2) // 2)
    return unpack(rows, wx + 1, half), unpack(rows[size : size + 8], 2, half), rows[size + 8 :]


def line_sums(corners):
    low, high = [part[0] for part in corners], [part[1] for part in corners]
    return [low[0]] + [low[x] + high[x - 1] for x in range(1, len(low))] + [high[-1]]


def early(wx, wy, d, x, y):
    return y in (0, wy - 1) or (d == 0 and x == 0) or (d == 1 and y == 1)


def lay_out(wx, wy, d, nat, l_ref, first):
    for x in range(wx):
        for y in range(wy):
            if early(wx, wy, d, x, y) == first:
                col = x * wy + y
                part = nat[d, pl.ds(col, 48, stride=wx * wy), :]
                l_ref[d, col] = part.astype(BF)
                if d == 2:
                    l_ref[3, col] = z_next(part).astype(BF)


def known_hexes(wx, wy, where, l_refs, kp_ref):
    z = l_refs[0].shape[3]
    nothing = jnp.zeros((48, z), BF)
    row = lambda i, col: kp_ref[i, pl.ds(col, 1), :]
    trace = lambda d, x, y: l_refs[0 if early(wx, wy, min(d, 2), x, y) else 1][d, x * wy + y]
    slots, scales, left_out = [], [], []
    for x, y in where:
        here = x * wy + y
        visc = row(4, here)
        last_x, last_y = x == wx - 1, y == wy - 1
        slots.append(
            [
                trace(0, x, y), nothing if last_x else trace(0, x + 1, y),
                trace(1, x, y), nothing if last_y else trace(1, x, y + 1),
                trace(2, x, y), trace(3, x, y),
            ]
        )
        scales.append(
            [
                visc * row(0, here), visc if last_x else visc * row(0, here + wy),
                visc * row(1, here), visc if last_y else visc * row(1, here + 1),
                visc * row(2, here), visc * row(3, here),
            ]
        )
        left_out.append(([1] if last_x else []) + ([3] if last_y else []))
    return slots, scales, left_out


def known_corners(vertex, scales, left_out):
    return [
        scaled_corners(part, [None if s in out else scale[s] for s in range(6)])
        for part, scale, out in zip(vertex, scales, left_out)
    ]


def middle_kernel(
    wx, wy, l_ref, nat, kp_ref, st_ref, f_ref, parts_ref,
    c_ref, v_ref, v1_ref, mx_ref, my_ref, own_ref, rest_ref, m_ref, lost_ref,
):
    for slot, ref in ((1, mx_ref), (3, my_ref)):
        bare, flux = product(f_ref, st_ref, slot)
        turned = tall([bare[0:48], bare[96:288], bare[48:96]]) if slot == 1 else bare
        ref[pl.ds(0, 288), :] = turned.astype(BF)
        ref[pl.ds(288, 96), :] = vertex_part(flux, parts_ref).astype(BF)
    flux = product(f_ref, st_ref, None)[1]
    m_ref[pl.ds(0, 288), :] = flux.astype(BF)
    m_ref[pl.ds(288, 96), :] = vertex_part(flux, parts_ref).astype(BF)
    lost_ref[...] = (flux - flux.astype(BF).astype(F32))[:, 0:256].astype(BF)
    for d in range(3):
        lay_out(wx, wy, d, nat, rest_ref, False)
    own_ref[...] = dot(
        tall([my_ref[pl.ds(144, 48), :], my_ref[pl.ds(288, 96), :]]), wide([l_ref[1, x * wy] for x in range(wx)])
    )
    for y in range(wy):
        inside = 0 < y < wy - 1
        where = [(x, y) for x in range(wx)]
        slots, scales, left_out = known_hexes(wx, wy, where, (l_ref, rest_ref), kp_ref)
        element = elements(slots)
        rows = dot(m_ref[...] if inside else m_ref[pl.ds(0, 288), :], element)
        lost = columns(dot(lost_ref[...], element[0:256]), wx)
        rows = columns(rows, wx)
        for x in range(wx):
            for s in range(6):
                part = slice(48 * s, 48 * s + 48)
                c_ref[s, x * wy + y] = (rows[x][part] + lost[x][part]) * scales[x][s]
        if inside:
            corners = known_corners([part[288:] for part in rows], scales, left_out)
            v1_ref[y - 1] = rows[wx - 1][304:320] * kp_ref[4, pl.ds((wx - 1) * wy + y, 1), :]
            for i, part in enumerate(line_sums(corners)):
                v_ref[y - 1, i] = part


def after_y(wx, wy, xs, visc_ref, l_ref, kp_ref, parts_ref, my_ref, own_ref, v3_ref, down_ref, up_ref):
    z = l_ref.shape[3]
    misc_d = read_tail(down_ref, wx, 0)[2]
    misc_u = read_tail(up_ref, wx, 1)[2]
    row = lambda i, col: kp_ref[i, pl.ds(col, 1), :]
    delta = dot(my_ref[...], wide([down_ref[pl.ds(48 * x, 48), :] for x in xs]))
    arrived = [up_ref[pl.ds(48 * x, 48), :].astype(F32) for x in xs]
    arrived_corners = slot_corners(arrived, parts_ref, 3)
    results = []
    for n, x in enumerate(xs):
        here = x * wy + wy - 1
        last = x == wx - 1
        part = delta[:, z * n : z * n + z]
        visc = row(4, here)
        scales = [
            visc * row(0, here), visc if last else visc * row(0, here + wy), visc * row(1, here),
            visc * misc_d[x : x + 1], visc * row(2, here), visc * row(3, here),
        ]
        flux = [part[48 * s : 48 * s + 48] * scales[s] for s in range(6)]
        used = [None if (s == 1 and last) else scales[s] for s in range(6)]
        known = v3_ref[x] * misc_d[x : x + 1]
        top = [rows + settle(known, p) for p, rows in enumerate(scaled_corners(part[288:384], used))]
        top_one = part[304:320] * visc
        here = x * wy
        visc = level_visc(misc_u[x : x + 1], visc_ref)
        flag = row(1, here)
        own = own_ref[:, pl.ds(z * x, z)]
        keep_z = misc_u[2 * wx + x : 2 * wx + x + 1]
        scales = [
            visc * misc_u[wx + x : wx + x + 1], None if last else visc * misc_u[wx + x + 1 : wx + x + 2],
            None, visc * flag, visc * keep_z, visc * z_next(keep_z),
        ]
        known = arrived_corners[n] * flag
        low = [rows + settle(known, p) for p, rows in enumerate(scaled_corners(own[48:144], scales))]
        low_one = own[64:80] * visc
        face = (arrived[n] + visc * (own[0:48] + penalty * l_ref[1, here].astype(F32))) * flag
        results.append((flux, top, top_one, low, low_one, face))
    return results


def turn_kernel(
    wx, wy, visc_ref, l_ref, kp_ref, diag_ref, parts_ref, my_ref, own_ref, c_ref, va_ref, vb_ref,
    v1a_ref, v1b_ref, v3_ref, swap0_in, swap1_in, swap2_in,
    c3_ref, vt_ref, vl_ref, v1_ref, face_ref, yd_ref, yu_ref, inner_ref, outer_ref, down_ref, up_ref,
):
    z = l_ref.shape[3]
    arrive((swap0_in, swap1_in, swap2_in), yd_ref, yu_ref)
    xs = (0, wx - 1)
    results = after_y(wx, wy, xs, visc_ref, l_ref, kp_ref, parts_ref, my_ref, own_ref, v3_ref, yd_ref, yu_ref)
    row = lambda i, col: kp_ref[i, pl.ds(col, 1), :]
    sums_d, one_d, misc_d = read_tail(yd_ref, wx, 0)
    sums_u, one_u, misc_u = read_tail(yu_ref, wx, 1)
    edge_high, edge_low = misc_d[wx + 4 : 2 * wx + 4], misc_d[2 * wx + 4 : 3 * wx + 4]
    for n, (flux, top, top_one, low, low_one, face) in enumerate(results):
        for s in range(6):
            c3_ref[n, s] = flux[s]
        face_ref[n] = face
        for p in range(2):
            vt_ref[n, p] = top[p]
            vl_ref[n, p] = low[p]
    flux, top, top_one, low, low_one, face = results[1]
    mine = tall(one_u) + low_one
    v1_ref[0] = mine
    v1_ref[1] = v1a_ref[0]
    for y in range(wy - 2):
        v1_ref[2 + y] = v1b_ref[y]
    v1_ref[wy] = v1a_ref[1] + top_one
    v1_ref[wy + 1] = tall(one_d)

    def plane(i, n, p):
        lines = [sums_u[i] + vl_ref[n, p], va_ref[0, i]]
        lines += [vb_ref[y, i] for y in range(wy - 2)]
        lines += [va_ref[1, i] + vt_ref[n, p], sums_d[i]]
        return merge(lines[1::2], lines[0::2])

    down_ref[pl.ds(0, 48), :] = yu_ref[pl.ds(48 * wx, 48), :]
    for y in range(wy):
        down_ref[pl.ds(48 + 48 * y, 48), :] = l_ref[0, y]
    down_ref[pl.ds(48 * (wy + 1), 48), :] = yd_ref[pl.ds(48 * wx, 48), :]
    diag = diag_ref[pl.ds(0, wy), :]
    high = diag.astype(BF).astype(F32)
    rim = [plane(0, 0, 0), high, edge_high[0:1], diag - high, edge_low[0:1]]
    rim += [misc_u[wx : wx + 1], kp_ref[0, 0:wy], misc_d[wx : wx + 1]]
    put_tail(down_ref, 48 * (wy + 2), rim)
    corner = (wx - 1) * wy
    for y in range(wy):
        part = c_ref[1, corner + y]
        up_ref[pl.ds(48 * y, 48), :] = (part + flux[1] if y == wy - 1 else part).astype(BF)
    last = pl.ds(corner, wy)
    rim = [plane(wx, 1, 1), mine, *one_d]
    rim += [misc_u[wx - 1 : wx], kp_ref[5, last], misc_d[wx + 1 : wx + 2]]
    rim += [misc_u[3 * wx - 1 : 3 * wx], kp_ref[2, last], misc_d[wx + 3 : wx + 4]]
    rim += [kp_ref[1, last], misc_d[wx - 1 : wx]]
    put_tail(up_ref, 48 * wy, rim)
    depart("gx", down_ref, up_ref, inner_ref, outer_ref)


def assemble_kernel(
    wx, wy, visc_ref, l_ref, kp_ref, diag_ref, parts_ref, mx_ref, my_ref, own_ref, c_ref, c3_ref,
    va_ref, vb_ref, v3_ref, vt_ref, vl_ref, face_ref, yd_ref, yu_ref,
    r_ref, late_ref, v_ref, inv_ref, ownx_ref, mid,
):
    z = l_ref.shape[3]
    cells = wx * wy
    xs = tuple(range(1, wx - 1))
    results = after_y(wx, wy, xs, visc_ref, l_ref, kp_ref, parts_ref, my_ref, own_ref, v3_ref, yd_ref, yu_ref)
    for n, part in enumerate(results):
        for s in range(6):
            mid[n, s] = part[0][s]
    traces = [yu_ref[pl.ds(48 * wx, 48), :]] + [l_ref[0, y] for y in range(wy)] + [yd_ref[pl.ds(48 * wx, 48), :]]
    ownx_ref[...] = dot(mx_ref[pl.ds(240, 144), :], wide(traces))

    def contrib(slot, x, y):
        here = c_ref[slot, x * wy + y]
        if y < wy - 1:
            return here
        return here + (mid[x - 1, slot] if 0 < x < wx - 1 else c3_ref[0 if x == 0 else 1, slot])

    for x in range(wx):
        for y in range(wy):
            col = pl.ds(x * wy + y, 48, stride=cells)
            if y:
                behind = contrib(3, x, y - 1)
            elif 0 < x < wx - 1:
                behind = results[x - 1][5]
            else:
                behind = face_ref[0 if x == 0 else 1]
            ahead = contrib(0, x, y) + contrib(1, x - 1, y) if x else contrib(0, x, y)
            sides = [ahead, contrib(2, x, y) + behind, contrib(4, x, y) + z_prev(contrib(5, x, y))]
            for d in range(3):
                if x == wx - 1:
                    late_ref[d, y] = sides[d]
                elif d == 0 and x == 0:
                    late_ref[3, y] = sides[d]
                else:
                    r_ref[d, col, :] = sides[d]
    sums_d, one_d, misc_d = read_tail(yd_ref, wx, 0)
    sums_u, one_u, misc_u = read_tail(yu_ref, wx, 1)
    edge_diag = misc_d[wx + 4 : 2 * wx + 4] + misc_d[2 * wx + 4 : 3 * wx + 4]

    def brought(which, i):
        held = vt_ref if which == 1 else vl_ref
        terms = []
        for x, p in ((i, 0), (i - 1, 1)):
            if x in (0, wx - 1):
                terms.append(held[0 if x == 0 else 1, p])
            elif 0 < x < wx - 1:
                terms.append(results[x - 1][which][p])
        return sum(terms[1:], terms[0])

    for i in range(wx + 1):
        lines = [sums_u[i] + brought(3, i), va_ref[0, i]]
        lines += [vb_ref[y, i] for y in range(wy - 2)]
        lines += [va_ref[1, i] + brought(1, i), sums_d[i]]
        v_ref[i] = merge(lines[1::2], lines[0::2])
        if i < wx:
            parts = [jnp.broadcast_to(diag_ref[pl.ds(i * wy + y, 1), :], (4, z)) for y in range(wy)]
            parts += [jnp.broadcast_to(edge_diag[i : i + 1], (4, z)), jnp.zeros((4, z), F32)]
            inv_ref[i] = reciprocal(tall(parts))


def reciprocal(diag):
    present = diag > 0.0
    return jnp.where(present, (1.0 / (gain * gain)) / jnp.where(present, diag, 1.0), 0.0)


def final_kernel(
    wx, wy, visc_ref, l_ref, kp_ref, parts_ref, mx_ref, ownx_ref, r_in, late_ref, v_ref, inv_ref, v1_ref,
    yd_ref, yu_ref, outer_in, inner_in, p_ref, out_hbm, r_ref, held, sems,
):
    here, last = lax.axis_index("gx"), lax.axis_size("gx") - 1

    def from_high(start, size):
        rows = pl.ds(start, size)
        value = jnp.where(even("gx"), inner_in[rows, :], outer_in[rows, :])
        return jnp.where(here < last, value, jnp.zeros_like(value))

    def from_low(start, size):
        rows = pl.ds(start, size)
        value = jnp.where(even("gx"), outer_in[rows, :], inner_in[rows, :])
        return jnp.where(here > 0, value, jnp.zeros_like(value))

    cells, z = wx * wy, l_ref.shape[3]
    rows = v_ref.shape[1]
    row = lambda i, col: kp_ref[i, pl.ds(col, 1), :]
    traces = [from_high(48 * j, 48) for j in range(wy + 2)]
    delta = dot(mx_ref[pl.ds(288, 96), :], wide(traces))
    rim_x = from_high(48 * (wy + 2), tail_rows(rows + 3 * wy + 4)).astype(F32)
    rim_l = from_low(48 * wy, tail_rows(rows + 32 + 3 * (wy + 2) - 1)).astype(F32)
    misc_d = read_tail(yd_ref, wx, 0)[2]
    misc_u = read_tail(yu_ref, wx, 1)[2]
    flags_high = rim_x[rows + 2 * (wy + 1) : rows + 3 * wy + 4]
    corner = (wx - 1) * wy
    arrived = [from_low(48 * y, 48) for y in range(wy)]
    arrived_corners = slot_corners(arrived, parts_ref, 1)
    codes = rim_l[rows + 32 : rows + 32 + wy + 2]
    keep_z = rim_l[rows + 32 + wy + 2 : rows + 32 + 2 * (wy + 2)]
    keep_y = rim_l[rows + 32 + 2 * (wy + 2) : rows + 32 + 3 * (wy + 2) - 1]
    low_visc = level_visc(codes, visc_ref)
    low_keep_z = z_next(keep_z)
    lines = [[], [], []]
    high_scales = []
    del r_in
    for j in range(-1, wy + 1):
        n = j + 1
        part = delta[:, z * n : z * n + z]
        flag = flags_high[n : n + 1]
        if j < 0:
            visc = level_visc(misc_u[wx - 1 : wx], visc_ref)
            kz = misc_u[3 * wx - 1 : 3 * wx]
            keeps = [misc_u[2 * wx - 1 : 2 * wx], flag, None, row(1, corner), kz, z_next(kz)]
        elif j < wy:
            here = corner + j
            visc = row(4, here)
            high_y = row(1, here + 1) if j < wy - 1 else misc_d[wx - 1 : wx]
            keeps = [row(0, here), flag, row(1, here), high_y, row(2, here), row(3, here)]
        else:
            visc = level_visc(misc_d[wx + 1 : wx + 2], visc_ref)
            kz = misc_d[wx + 3 : wx + 4]
            keeps = [misc_d[wx + 2 : wx + 3], flag, misc_d[wx - 1 : wx], None, kz, z_next(kz)]
        scales = [None if keep is None else visc * keep for keep in keeps]
        corners = scaled_corners(part, scales)
        one = v1_ref[n] * flag
        lines[0].append(corners[0])
        lines[1].append(corners[1] + one[0:8] + z_prev(one[8:16]))
        high_scales.append(scales)
        own = ownx_ref[:, pl.ds(z * n, z)]
        visc = low_visc[n : n + 1]
        flag = misc_u[wx : wx + 1] if j < 0 else misc_d[wx : wx + 1] if j == wy else row(0, j)
        scales = [
            None, visc * flag, None if j < 0 else visc * keep_y[j : j + 1],
            None if j == wy else visc * keep_y[j + 1 : j + 2], visc * keep_z[n : n + 1], visc * low_keep_z[n : n + 1],
        ]
        corners = scaled_corners(own[48:144], scales, (1,))[0]
        if 0 <= j < wy:
            one = arrived_corners[j] * flag
            lines[2].append(corners + one[0:8] + z_prev(one[8:16]))
            face = (arrived[j].astype(F32) + visc * (own[0:48] + penalty * l_ref[0, j].astype(F32))) * flag
            r_ref[0, pl.ds(j, 48, stride=cells), :] = late_ref[3, j] + face
        else:
            at = rows + (0 if j < 0 else 16)
            one = rim_l[at : at + 16] * flag
            lines[2].append(corners + one[0:8] + z_prev(one[8:16]))
    low, before, first = [merge(part[1::2], part[0::2]) for part in lines]
    top = v_ref[wx] + before + rim_x[0:rows]
    values = [(v_ref[0] + first + rim_l[0:rows]) * inv_ref[0]]
    values += [v_ref[i] * inv_ref[i] for i in range(1, wx - 1)]
    values += [(v_ref[wx - 1] + low) * inv_ref[wx - 1]]
    diag = rim_x[rows : rows + wy + 1] + rim_x[rows + wy + 1 : rows + 2 * (wy + 1)]
    parts = [jnp.broadcast_to(diag[j : j + 1], (4, z)) for j in range(wy + 1)]
    values += [top * reciprocal(tall(parts + [jnp.zeros((rows - 4 * (wy + 1), z), F32)]))]
    low = [tall(values[x : x + 3]) for x in range(0, wx, 2)]
    rhs = tall([wide(low), wide([z_next(part) for part in low])]).astype(BF)
    delta = columns(dot(mx_ref[pl.ds(0, 240), :], wide(traces[1 : wy + 1])), wy)
    behind = dot(mx_ref[pl.ds(96, 48), :], traces[0]) * high_scales[0][3]
    size = 96 * wy
    copies = []
    spreads = [dot(p_ref[pl.ds(size * d, size), :], rhs) for d in range(3)]
    for d in range(3):
        for j in range(wy):
            scales = high_scales[j + 1]
            part = [delta[j][48 * i : 48 * i + 48] for i in range(5)]
            if d == 0:
                flux = part[0] * scales[0]
            elif d == 1:
                flux = part[1] * scales[2] + behind
                behind = part[2] * scales[3]
            else:
                flux = part[3] * scales[4] + z_prev(part[4] * scales[5])
            r_ref[d, pl.ds(corner + j, 48, stride=cells), :] = late_ref[d, j] + flux
        spread = spreads[d]
        spread = jnp.concatenate(
            [spread[:, z * g : z * g + z].reshape(48, 2 * wy, z) for g in range(wx // 2)], axis=1
        )
        total = r_ref[d].reshape(48, cells, z) + spread * kp_ref[d][None]
        held[d] = total.reshape(48 * cells, z).astype(BF)
        copies.append(pltpu.make_async_copy(held.at[d], out_hbm.at[d], sems.at[d]))
        copies[d].start()
    for copy in copies:
        copy.wait()


def call(body, args, outs, scratch, flops, hbm=False, aliases=None):
    if hbm:
        args = tuple(pltpu.with_memory_space_constraint(a, pltpu.HBM) for a in args)
    keywords = {}
    if aliases:
        spaces = [pltpu.HBM] + [pltpu.VMEM] * (len(outs) - 1)
        keywords = dict(out_specs=tuple(pl.BlockSpec(memory_space=space) for space in spaces), input_output_aliases=aliases)
    return pl.pallas_call(
        body,
        **keywords,
        in_specs=[pl.BlockSpec(memory_space=pltpu.HBM if hbm else pltpu.VMEM)] * len(args),
        out_shape=outs,
        scratch_shapes=scratch,
        cost_estimate=pl.CostEstimate(flops=flops, bytes_accessed=1000000, transcendentals=0),
        compiler_params=pltpu.CompilerParams(vmem_limit_bytes=16 * 1024 * 1024),
    )(*args)


def local(traces, dirichlet, visc_class, viscosity, coarse_diag, solve_map, flux_map):
    wx, wy, z = traces.shape[2:]
    cells = wx * wy
    rows = 8 * (wy // 2 + 1)
    per_hex = 2 * 384 * 288 * z
    parts = jnp.asarray(slot_table())
    spread = jnp.asarray(spread_table(wy, rows))
    vm = pltpu.VMEM
    bind = lambda body: functools.partial(body, wx, wy)
    y_message = vm((48 * wx + 48 + tail_rows(8 * ((wx + 2) // 2) + 8 + 3 * wx + 4), z), BF)
    x_message = vm((48 * (wy + 2) + tail_rows(rows + 3 * wy + 4), z), BF)

    (lifted, nat, flags, visc, diag, s_turned, f_map, parts, va, v1a, v3, *swaps) = call(
        bind(first_kernel),
        (
            viscosity, traces.reshape(3, 48 * cells, z), dirichlet.reshape(3, cells, z),
            visc_class.reshape(cells, z), coarse_diag.reshape(cells, z), solve_map.T, flux_map, parts,
        ),
        (
            vm((4, cells, 48, z), BF), vm((3, 48 * cells, z), F32), vm((6, cells, z), F32), vm((viscosity.shape[0], z), F32), vm((cells, z), F32),
            vm(solve_map.shape[::-1], BF), vm(flux_map.shape, BF), vm(parts.shape, BF),
            vm((2, wx + 1, 8, z), F32), vm((2, 16, z), F32), vm((wx, 32, z), F32),
            y_message, y_message, y_message,
        ),
        [
            y_message, y_message,
            vm((3, 48 * cells, z), BF), vm((3, cells, z), jnp.int32), vm((cells, z), jnp.int32),
            pltpu.SMEM(viscosity.shape, F32), pltpu.SemaphoreType.DMA((8,)),
        ],
        wx * per_hex, True,
    )
    swaps = [swap(message, "gy", "gx", k, 3) for k, message in enumerate(swaps)]
    c, vb, v1b, mx, my, own = call(
        bind(middle_kernel),
        (lifted, nat, flags, s_turned, f_map, parts),
        (
            vm((6, cells, 48, z), F32), vm((wy - 2, wx + 1, 8, z), F32), vm((wy - 2, 16, z), F32),
            vm((384, 48), BF), vm((384, 48), BF), vm((144, wx * z), F32),
        ),
        [vm((4, cells, 48, z), BF), vm((384, 288), BF), vm((288, 256), BF)], cells * per_hex,
    )
    c3, vt, vl, v1, face, yd, yu, inner, outer = call(
        bind(turn_kernel),
        (
            visc, lifted, flags, diag, parts, my, own, c, va, vb, v1a, v1b, v3, *swaps,
        ),
        (
            vm((2, 6, 48, z), F32), vm((2, 2, 8, z), F32), vm((2, 2, 8, z), F32), vm((wy + 2, 16, z), F32),
            vm((2, 48, z), F32), y_message, y_message, x_message, x_message,
        ),
        [x_message, x_message], 2 * per_hex,
    )
    inner = swap(inner, "gx", "gy", 0)
    outer = swap(outer, "gx", "gy", 1)
    residual, late, vs, inverse, ownx = call(
        bind(assemble_kernel),
        (
            visc, lifted, flags, diag, parts, mx, my, own, c, c3, va, vb, v3, vt, vl, face, yd, yu,
        ),
        (
            vm((3, 48 * cells, z), F32), vm((4, wy, 48, z), F32), vm((wx + 1, rows, z), F32), vm((wx, rows, z), F32),
            vm((144, (wy + 2) * z), F32),
        ),
        [vm((wx - 2, 6, 48, z), F32)], 4 * per_hex,
    )
    out, _ = call(
        bind(final_kernel),
        (
            visc, lifted, flags, parts, mx, ownx, residual, late, vs, inverse, v1, yd, yu, outer, inner, spread,
        ),
        (jax.ShapeDtypeStruct((3, 48 * cells, z), BF), vm((3, 48 * cells, z), F32)),
        [vm((3, 48 * cells, z), BF), pltpu.SemaphoreType.DMA((3,))], 4 * spread.size * z,
        aliases={6: 1},
    )
    return out.reshape(traces.shape)


def solution(mesh):
    in_specs = (
        P(None, None, "gx", "gy", None),
        P(None, "gx", "gy", None),
        P("gx", "gy", None),
        P(),
        P("gx", "gy", None),
        P(),
        P(),
    )
    out_specs = P(None, None, "gx", "gy", None)
    return jax.shard_map(local, mesh=mesh, in_specs=in_specs, out_specs=out_specs, check_vma=False)
```

```python
import functools
import math

import jax
import jax.numpy as jnp
import ml_dtypes
import numpy as np
from jax import lax
from jax.experimental import pallas as pl
from jax.experimental.pallas import tpu as pltpu
from jax.sharding import PartitionSpec as P

penalty = 0.5
BF = jnp.bfloat16
F32 = jnp.float32
lift = 1.3264
gain = 1.3280711361297461


def swap(value, axis, other, first, step=2):
    count, width = lax.axis_size(axis), lax.axis_size(other)
    place = (lambda i, j: i * width + j) if (axis, other) == ("gx", "gy") else (lambda i, j: j * count + i)
    lows = list(range(first, count - 1, step))
    pairs = [(place(low, j), place(low + 1, j)) for low in lows for j in range(width)]
    alone = [i for i in range(count) if i not in lows and i - 1 not in lows]
    pairs += [(place(i, j), place(i, j + 1)) for i in alone for j in range(0, width - 1, 2)]
    return lax.ppermute(value, ("gx", "gy"), pairs + [(high, low) for low, high in pairs])


def even(axis):
    return lax.rem(lax.axis_index(axis), 2) == 0


def arrive(messages, down_ref, up_ref):
    here, last = lax.axis_index("gy"), lax.axis_size("gy") - 1
    values = [ref[...] for ref in messages]
    for ref, swap_of, present in ((down_ref, lax.rem(here, 3), here < last), (up_ref, lax.rem(here + 2, 3), here > 0)):
        value = jnp.where(swap_of == 0, values[0], jnp.where(swap_of == 1, values[1], values[2]))
        ref[...] = jnp.where(present, value, jnp.zeros_like(value))


def depart_three(down_ref, up_ref, messages):
    here = lax.rem(lax.axis_index("gy"), 3)
    for k, ref in enumerate(messages):
        choose(here == k, up_ref, down_ref, ref)


def depart(axis, down_ref, up_ref, inner_ref, outer_ref):
    choose(even(axis), up_ref, down_ref, inner_ref)
    choose(even(axis), down_ref, up_ref, outer_ref)


def choose(condition, yes_ref, no_ref, out_ref, present=None):
    value = jnp.where(condition, yes_ref[...], no_ref[...])
    out_ref[...] = value if present is None else jnp.where(present, value, jnp.zeros_like(value))


def corner_table():
    gll_points = [-1.0, -math.sqrt(0.2), math.sqrt(0.2), 1.0]
    table = np.zeros((16, 4), np.float64)
    for s in range(4):
        for t in range(4):
            for p in range(2):
                for q in range(2):
                    table[4 * s + t, 2 * p + q] = (
                        (1 + (2 * p - 1) * gll_points[s]) * (1 + (2 * q - 1) * gll_points[t]) / 4
                    )
    return table


def landing(face_slot, high_s, high_t):
    direction, outward = divmod(face_slot, 2)
    if direction == 0:
        return (outward, high_s, high_t)
    if direction == 1:
        return (high_s, outward, high_t)
    return (high_s, high_t, outward)


def gather_table():
    weights = lift * corner_table()
    table = np.zeros((32, 288), np.float64)
    for slot in range(6):
        for s in range(2):
            for t in range(2):
                p, q, r = landing(slot, s, t)
                for c in range(3):
                    cols = slot * 48 + 16 * c + np.arange(16)
                    table[16 * r + 8 * p + 4 * q + c, cols] += weights[:, 2 * s + t]
    return table.astype(ml_dtypes.bfloat16)


def slot_table():
    slots = np.split(gather_table(), 6, axis=1)
    rows = [
        np.r_[0:8, 16:24], np.r_[8:16, 24:32], np.arange(32), np.arange(32), np.arange(16), np.arange(16, 32),
    ]
    return np.concatenate([slot[kept] for slot, kept in zip(slots, rows)], axis=0)


slot_rows = (0, 16, 32, 64, 96, 112, 128)


def between(low, high):
    step = high - low
    return [low, low + (0.5 - 0.5 * math.sqrt(0.2)) * step, low + (0.5 + 0.5 * math.sqrt(0.2)) * step, high]


def lanes(shape):
    return lax.broadcasted_iota(jnp.int32, shape, len(shape) - 1)


def z_next(value):
    last = value.shape[-1] - 1
    return jnp.where(lanes(value.shape) < last, pltpu.roll(value, last, value.ndim - 1), 0.0)


def z_prev(value):
    return jnp.where(lanes(value.shape) > 0, pltpu.roll(value, 1, value.ndim - 1), 0.0)


def dot(left, right):
    return jnp.dot(left, right, preferred_element_type=F32)


def wide(parts):
    return jnp.concatenate(parts, axis=1)


def tall(parts):
    return jnp.concatenate(parts, axis=0)


def columns(rows, count):
    z = rows.shape[1] // count
    return [rows[:, z * h : z * h + z] for h in range(count)]


def elements(slots):
    return tall([wide([hexa[s] for hexa in slots]) for s in range(6)])


def vertex_part(flux, parts_ref):
    rows = []
    for s in range(6):
        first, size = slot_rows[s], slot_rows[s + 1] - slot_rows[s]
        rows.append(dot(parts_ref[pl.ds(first, size), :], flux[48 * s : 48 * s + 48].astype(BF)))
    rows[2:4] = [rows[2] + rows[3]]
    return tall(rows)


def turned_dot(left, right):
    return lax.dot_general(left, right, (((1,), (1,)), ((), ())), preferred_element_type=F32)


def product(f_ref, st_ref, slot):
    first = 0 if slot is None else 48 * slot
    flux = turned_dot(f_ref[...], st_ref[...] if slot is None else st_ref[pl.ds(first, 48), :])
    rows = lax.broadcasted_iota(jnp.int32, flux.shape, 0)
    return flux, flux + jnp.where(rows == lax.broadcasted_iota(jnp.int32, flux.shape, 1) + first, F32(penalty), F32(0.0))


def slot_corners(traces, parts_ref, slot):
    z = traces[0].shape[1]
    first, size = slot_rows[slot], slot_rows[slot + 1] - slot_rows[slot]
    rows = dot(parts_ref[pl.ds(first, size), :], wide([trace.astype(BF) for trace in traces]))
    return [rows[:, z * h : z * h + z] for h in range(len(traces))]


def settle(rows, p):
    return rows[8 * p : 8 * p + 8] + z_prev(rows[16 + 8 * p : 24 + 8 * p])


def scaled_corners(delta, scales, offsets=(0, 1)):
    shape = (8, delta.shape[1])
    blank = jnp.zeros((1, shape[1]), F32)
    y_scale = jnp.where(
        lax.broadcasted_iota(jnp.int32, shape, 0) < 4,
        blank if scales[2] is None else scales[2], blank if scales[3] is None else scales[3],
    )
    results = []
    for p in offsets:
        parts = []
        for r in range(2):
            at = 32 + 16 * r + 8 * p
            part = delta[at : at + 8] * y_scale + delta[at + 32 : at + 40] * scales[4 + r]
            if scales[p] is not None:
                part = part + delta[16 * p + 8 * r : 16 * p + 8 * r + 8] * scales[p]
            parts.append(part)
        results.append(parts[0] + z_prev(parts[1]))
    return results


def level_visc(code, visc_ref):
    visc = jnp.zeros(code.shape, F32)
    for level in range(visc_ref.shape[0]):
        visc = visc + jnp.where(code == F32(level + 1), visc_ref[pl.ds(level, 1), :], F32(0.0))
    return visc


def merge(even, odd):
    odd = tall(odd)
    return tall(even) + pltpu.roll(odd, odd.shape[0] - 4, 0)


def first_kernel(
    wx, wy, visc_hbm, t_hbm, dir_hbm, cls_hbm, diag_hbm, st_hbm, f_hbm, parts_hbm,
    l_ref, nat, kp_ref, visc_ref, diag_ref, st_ref, f_ref, parts_ref, v_ref, v1_ref, v3_ref,
    swap0_ref, swap1_ref, swap2_ref, down_ref, up_ref, t_ref, dir_ref, cls_ref, levels, sems,
):
    cells = wx * wy
    pairs = [
        (parts_hbm, parts_ref), (f_hbm, f_ref), (st_hbm, st_ref), (t_hbm, t_ref), (dir_hbm, dir_ref),
        (cls_hbm, cls_ref), (visc_hbm, levels), (diag_hbm, diag_ref),
    ]
    copies = [pltpu.make_async_copy(a, b, sems.at[i]) for i, (a, b) in enumerate(pairs)]
    for copy in copies:
        copy.start()
    diagonal = lax.broadcasted_iota(jnp.int32, (288, 288), 0) == lax.broadcasted_iota(jnp.int32, (288, 288), 1)
    diagonal = jnp.where(diagonal, F32(penalty), F32(0.0))
    copies[0].wait()
    own = tall([vertex_part(diagonal, parts_ref), diagonal[144:192]])
    copies[1].wait()
    left = tall([vertex_part(f_ref[...], parts_ref).astype(BF), f_ref[pl.ds(144, 48), :]])
    for copy in copies[2:5]:
        copy.wait()
    short = (turned_dot(left, st_ref[...]) + own).astype(BF)
    z = t_ref.shape[2]
    for d in range(3):
        keep = (1 - dir_ref[d]).astype(F32)
        kp_ref[d] = keep
        masked = t_ref[d].astype(F32).reshape(48, cells, z) * keep[None]
        nat[d] = masked.reshape(48 * cells, z)
        lay_out(wx, wy, d, nat, l_ref, True)
    kp_ref[3] = z_next(kp_ref[2])
    for copy in copies[5:]:
        copy.wait()
    for level in range(visc_ref.shape[0]):
        visc_ref[pl.ds(level, 1), :] = jnp.full((1, z), levels[level], F32)
    code = cls_ref[...].astype(F32) + 1.0
    kp_ref[4] = level_visc(code, visc_ref)
    kp_ref[5] = code
    row = lambda i, col: kp_ref[i, pl.ds(col, 1), :]
    corners = []
    for side, y in enumerate((0, wy - 1)):
        where = [(x, y) for x in range(wx)]
        slots, scales, left_out = known_hexes(wx, wy, where, (l_ref, None), kp_ref)
        rows = columns(dot(short if side else short[0:96], elements(slots)), wx)
        corners += known_corners(rows, scales, left_out)
        v1_ref[side] = rows[wx - 1][16:32] * row(4, (wx - 1) * wy + y)
    place = lax.broadcasted_iota(jnp.int32, (32, z), 0)
    lone = [part * row(4, x * wy + wy - 1) for x, part in enumerate(rows)]
    for x in range(wx):
        v3_ref[x] = jnp.where(lax.rem(place, 8) < 4, 0.0, lone[x][32:64])
    sums = [line_sums(corners[:wx]), line_sums(corners[wx:])]
    for side in range(2):
        for i in range(wx + 1):
            v_ref[side, i] = sums[side][i]
    corner = (wx - 1) * wy
    top = wy - 1
    for x in range(wx):
        down_ref[pl.ds(48 * x, 48), :] = l_ref[1, x * wy]
        up_ref[pl.ds(48 * x, 48), :] = lone[x][96:144].astype(BF)
    down_ref[pl.ds(48 * wx, 48), :] = l_ref[0, 0]
    up_ref[pl.ds(48 * wx, 48), :] = l_ref[0, top]
    flags = [row(1, x * wy) for x in range(wx)] + [row(0, 0), row(5, corner), row(0, corner), row(2, corner)]
    diag = tall([diag_ref[pl.ds(x * wy, 1), :] for x in range(wx)])
    high = diag.astype(BF).astype(F32)
    rim = pack(sums[0], 0) + pack([v1_ref[0, 0:8], v1_ref[0, 8:16]], 0) + flags + [high, diag - high]
    put_tail(down_ref, 48 * wx + 48, rim)
    flags = [row(kind, x * wy + top) for kind in (5, 0, 2) for x in range(wx)]
    rim = pack(sums[1], 1) + pack([v1_ref[1, 0:8], v1_ref[1, 8:16]], 1) + flags
    put_tail(up_ref, 48 * wx + 48, rim)
    depart_three(down_ref, up_ref, (swap0_ref, swap1_ref, swap2_ref))


def tail_rows(count):
    return -(-count // 16) * 16


def put_tail(ref, start, rows):
    count = sum(part.shape[0] for part in rows)
    full = ref.shape[0] - start
    if full > count:
        rows = rows + [jnp.zeros((full - count, rows[0].shape[1]), F32)]
    ref[pl.ds(start, full), :] = tall(rows).astype(BF)


def pack(parts, half):
    place = lax.broadcasted_iota(jnp.int32, parts[0].shape, 0)
    parts = parts + [jnp.zeros_like(parts[0])] * (len(parts) % 2)
    packed = []
    for low, high in zip(parts[0::2], parts[1::2]):
        if half:
            low = pltpu.roll(low, 4, 0)
        else:
            high = pltpu.roll(high, 4, 0)
        packed.append(jnp.where(place < 4, low, high))
    return packed


def unpack(packed, count, half):
    parts = []
    for n in range(count):
        part = packed[8 * (n // 2) : 8 * (n // 2) + 8]
        parts.append(part if n % 2 == half else pltpu.roll(part, 4, 0))
    return parts


def read_tail(ref, wx, half):
    start = 48 * wx + 48
    rows = ref[pl.ds(start, ref.shape[0] - start), :].astype(F32)
    size = 8 * ((wx + 2) // 2)
    return unpack(rows, wx + 1, half), unpack(rows[size : size + 8], 2, half), rows[size + 8 :]


def line_sums(corners):
    low, high = [part[0] for part in corners], [part[1] for part in corners]
    return [low[0]] + [low[x] + high[x - 1] for x in range(1, len(low))] + [high[-1]]


def early(wx, wy, d, x, y):
    return y in (0, wy - 1) or (d == 0 and x == 0) or (d == 1 and y == 1)


def lay_out(wx, wy, d, nat, l_ref, first):
    for x in range(wx):
        for y in range(wy):
            if early(wx, wy, d, x, y) == first:
                col = x * wy + y
                part = nat[d, pl.ds(col, 48, stride=wx * wy), :]
                l_ref[d, col] = part.astype(BF)
                if d == 2:
                    l_ref[3, col] = z_next(part).astype(BF)


def known_hexes(wx, wy, where, l_refs, kp_ref):
    z = l_refs[0].shape[3]
    nothing = jnp.zeros((48, z), BF)
    row = lambda i, col: kp_ref[i, pl.ds(col, 1), :]
    trace = lambda d, x, y: l_refs[0 if early(wx, wy, min(d, 2), x, y) else 1][d, x * wy + y]
    slots, scales, left_out = [], [], []
    for x, y in where:
        here = x * wy + y
        visc = row(4, here)
        last_x, last_y = x == wx - 1, y == wy - 1
        slots.append(
            [
                trace(0, x, y), nothing if last_x else trace(0, x + 1, y),
                trace(1, x, y), nothing if last_y else trace(1, x, y + 1),
                trace(2, x, y), trace(3, x, y),
            ]
        )
        scales.append(
            [
                visc * row(0, here), visc if last_x else visc * row(0, here + wy),
                visc * row(1, here), visc if last_y else visc * row(1, here + 1),
                visc * row(2, here), visc * row(3, here),
            ]
        )
        left_out.append(([1] if last_x else []) + ([3] if last_y else []))
    return slots, scales, left_out


def known_corners(vertex, scales, left_out):
    return [
        scaled_corners(part, [None if s in out else scale[s] for s in range(6)])
        for part, scale, out in zip(vertex, scales, left_out)
    ]


def middle_kernel(
    wx, wy, l_ref, nat, kp_ref, st_ref, f_ref, parts_ref,
    c_ref, v_ref, v1_ref, mx_ref, my_ref, own_ref, rest_ref, m_ref, lost_ref,
):
    for slot, ref in ((1, mx_ref), (3, my_ref)):
        bare, flux = product(f_ref, st_ref, slot)
        turned = tall([bare[0:48], bare[96:288], bare[48:96]]) if slot == 1 else bare
        ref[pl.ds(0, 288), :] = turned.astype(BF)
        ref[pl.ds(288, 96), :] = vertex_part(flux, parts_ref).astype(BF)
    flux = product(f_ref, st_ref, None)[1]
    m_ref[pl.ds(0, 288), :] = flux.astype(BF)
    m_ref[pl.ds(288, 96), :] = vertex_part(flux, parts_ref).astype(BF)
    lost_ref[...] = (flux - flux.astype(BF).astype(F32))[:, 0:256].astype(BF)
    for d in range(3):
        lay_out(wx, wy, d, nat, rest_ref, False)
    own_ref[...] = dot(
        tall([my_ref[pl.ds(144, 48), :], my_ref[pl.ds(288, 96), :]]), wide([l_ref[1, x * wy] for x in range(wx)])
    )
    for y in range(wy):
        inside = 0 < y < wy - 1
        where = [(x, y) for x in range(wx)]
        slots, scales, left_out = known_hexes(wx, wy, where, (l_ref, rest_ref), kp_ref)
        element = elements(slots)
        rows = dot(m_ref[...] if inside else m_ref[pl.ds(0, 288), :], element)
        lost = columns(dot(lost_ref[...], element[0:256]), wx)
        rows = columns(rows, wx)
        for x in range(wx):
            for s in range(6):
                part = slice(48 * s, 48 * s + 48)
                c_ref[s, x * wy + y] = (rows[x][part] + lost[x][part]) * scales[x][s]
        if inside:
            corners = known_corners([part[288:] for part in rows], scales, left_out)
            v1_ref[y - 1] = rows[wx - 1][304:320] * kp_ref[4, pl.ds((wx - 1) * wy + y, 1), :]
            for i, part in enumerate(line_sums(corners)):
                v_ref[y - 1, i] = part


def after_y(wx, wy, xs, visc_ref, l_ref, kp_ref, parts_ref, my_ref, own_ref, v3_ref, down_ref, up_ref):
    z = l_ref.shape[3]
    misc_d = read_tail(down_ref, wx, 0)[2]
    misc_u = read_tail(up_ref, wx, 1)[2]
    row = lambda i, col: kp_ref[i, pl.ds(col, 1), :]
    delta = dot(my_ref[...], wide([down_ref[pl.ds(48 * x, 48), :] for x in xs]))
    arrived = [up_ref[pl.ds(48 * x, 48), :].astype(F32) for x in xs]
    arrived_corners = slot_corners(arrived, parts_ref, 3)
    results = []
    for n, x in enumerate(xs):
        here = x * wy + wy - 1
        last = x == wx - 1
        part = delta[:, z * n : z * n + z]
        visc = row(4, here)
        scales = [
            visc * row(0, here), visc if last else visc * row(0, here + wy), visc * row(1, here),
            visc * misc_d[x : x + 1], visc * row(2, here), visc * row(3, here),
        ]
        flux = [part[48 * s : 48 * s + 48] * scales[s] for s in range(6)]
        used = [None if (s == 1 and last) else scales[s] for s in range(6)]
        known = v3_ref[x] * misc_d[x : x + 1]
        top = [rows + settle(known, p) for p, rows in enumerate(scaled_corners(part[288:384], used))]
        top_one = part[304:320] * visc
        here = x * wy
        visc = level_visc(misc_u[x : x + 1], visc_ref)
        flag = row(1, here)
        own = own_ref[:, pl.ds(z * x, z)]
        keep_z = misc_u[2 * wx + x : 2 * wx + x + 1]
        scales = [
            visc * misc_u[wx + x : wx + x + 1], None if last else visc * misc_u[wx + x + 1 : wx + x + 2],
            None, visc * flag, visc * keep_z, visc * z_next(keep_z),
        ]
        known = arrived_corners[n] * flag
        low = [rows + settle(known, p) for p, rows in enumerate(scaled_corners(own[48:144], scales))]
        low_one = own[64:80] * visc
        face = (arrived[n] + visc * (own[0:48] + penalty * l_ref[1, here].astype(F32))) * flag
        results.append((flux, top, top_one, low, low_one, face))
    return results


def turn_kernel(
    wx, wy, visc_ref, l_ref, kp_ref, diag_ref, parts_ref, my_ref, own_ref, c_ref, va_ref, vb_ref,
    v1a_ref, v1b_ref, v3_ref, swap0_in, swap1_in, swap2_in,
    c3_ref, vt_ref, vl_ref, v1_ref, face_ref, yd_ref, yu_ref, inner_ref, outer_ref, down_ref, up_ref,
):
    z = l_ref.shape[3]
    arrive((swap0_in, swap1_in, swap2_in), yd_ref, yu_ref)
    xs = (0, wx - 1)
    results = after_y(wx, wy, xs, visc_ref, l_ref, kp_ref, parts_ref, my_ref, own_ref, v3_ref, yd_ref, yu_ref)
    row = lambda i, col: kp_ref[i, pl.ds(col, 1), :]
    sums_d, one_d, misc_d = read_tail(yd_ref, wx, 0)
    sums_u, one_u, misc_u = read_tail(yu_ref, wx, 1)
    edge_high, edge_low = misc_d[wx + 4 : 2 * wx + 4], misc_d[2 * wx + 4 : 3 * wx + 4]
    for n, (flux, top, top_one, low, low_one, face) in enumerate(results):
        for s in range(6):
            c3_ref[n, s] = flux[s]
        face_ref[n] = face
        for p in range(2):
            vt_ref[n, p] = top[p]
            vl_ref[n, p] = low[p]
    flux, top, top_one, low, low_one, face = results[1]
    mine = tall(one_u) + low_one
    v1_ref[0] = mine
    v1_ref[1] = v1a_ref[0]
    for y in range(wy - 2):
        v1_ref[2 + y] = v1b_ref[y]
    v1_ref[wy] = v1a_ref[1] + top_one
    v1_ref[wy + 1] = tall(one_d)

    def plane(i, n, p):
        lines = [sums_u[i] + vl_ref[n, p], va_ref[0, i]]
        lines += [vb_ref[y, i] for y in range(wy - 2)]
        lines += [va_ref[1, i] + vt_ref[n, p], sums_d[i]]
        return merge(lines[1::2], lines[0::2])

    down_ref[pl.ds(0, 48), :] = yu_ref[pl.ds(48 * wx, 48), :]
    for y in range(wy):
        down_ref[pl.ds(48 + 48 * y, 48), :] = l_ref[0, y]
    down_ref[pl.ds(48 * (wy + 1), 48), :] = yd_ref[pl.ds(48 * wx, 48), :]
    diag = diag_ref[pl.ds(0, wy), :]
    high = diag.astype(BF).astype(F32)
    rim = [plane(0, 0, 0), high, edge_high[0:1], diag - high, edge_low[0:1]]
    rim += [misc_u[wx : wx + 1], kp_ref[0, 0:wy], misc_d[wx : wx + 1]]
    put_tail(down_ref, 48 * (wy + 2), rim)
    corner = (wx - 1) * wy
    for y in range(wy):
        part = c_ref[1, corner + y]
        up_ref[pl.ds(48 * y, 48), :] = (part + flux[1] if y == wy - 1 else part).astype(BF)
    last = pl.ds(corner, wy)
    rim = [plane(wx, 1, 1), mine, *one_d]
    rim += [misc_u[wx - 1 : wx], kp_ref[5, last], misc_d[wx + 1 : wx + 2]]
    rim += [misc_u[3 * wx - 1 : 3 * wx], kp_ref[2, last], misc_d[wx + 3 : wx + 4]]
    rim += [kp_ref[1, last], misc_d[wx - 1 : wx]]
    put_tail(up_ref, 48 * wy, rim)
    depart("gx", down_ref, up_ref, inner_ref, outer_ref)


def assemble_kernel(
    wx, wy, visc_ref, l_ref, kp_ref, diag_ref, parts_ref, mx_ref, my_ref, own_ref, c_ref, c3_ref,
    va_ref, vb_ref, v3_ref, vt_ref, vl_ref, face_ref, yd_ref, yu_ref,
    r_ref, late_ref, v_ref, inv_ref, ownx_ref, mid,
):
    z = l_ref.shape[3]
    cells = wx * wy
    xs = tuple(range(1, wx - 1))
    results = after_y(wx, wy, xs, visc_ref, l_ref, kp_ref, parts_ref, my_ref, own_ref, v3_ref, yd_ref, yu_ref)
    for n, part in enumerate(results):
        for s in range(6):
            mid[n, s] = part[0][s]
    traces = [yu_ref[pl.ds(48 * wx, 48), :]] + [l_ref[0, y] for y in range(wy)] + [yd_ref[pl.ds(48 * wx, 48), :]]
    ownx_ref[...] = dot(mx_ref[pl.ds(240, 144), :], wide(traces))

    def contrib(slot, x, y):
        here = c_ref[slot, x * wy + y]
        if y < wy - 1:
            return here
        return here + (mid[x - 1, slot] if 0 < x < wx - 1 else c3_ref[0 if x == 0 else 1, slot])

    for x in range(wx):
        for y in range(wy):
            col = pl.ds(x * wy + y, 48, stride=cells)
            if y:
                behind = contrib(3, x, y - 1)
            elif 0 < x < wx - 1:
                behind = results[x - 1][5]
            else:
                behind = face_ref[0 if x == 0 else 1]
            ahead = contrib(0, x, y) + contrib(1, x - 1, y) if x else contrib(0, x, y)
            sides = [ahead, contrib(2, x, y) + behind, contrib(4, x, y) + z_prev(contrib(5, x, y))]
            for d in range(3):
                if x == wx - 1:
                    late_ref[d, y] = sides[d]
                elif d == 0 and x == 0:
                    late_ref[3, y] = sides[d]
                else:
                    r_ref[d, col, :] = sides[d]
    sums_d, one_d, misc_d = read_tail(yd_ref, wx, 0)
    sums_u, one_u, misc_u = read_tail(yu_ref, wx, 1)
    edge_diag = misc_d[wx + 4 : 2 * wx + 4] + misc_d[2 * wx + 4 : 3 * wx + 4]

    def brought(which, i):
        held = vt_ref if which == 1 else vl_ref
        terms = []
        for x, p in ((i, 0), (i - 1, 1)):
            if x in (0, wx - 1):
                terms.append(held[0 if x == 0 else 1, p])
            elif 0 < x < wx - 1:
                terms.append(results[x - 1][which][p])
        return sum(terms[1:], terms[0])

    for i in range(wx + 1):
        lines = [sums_u[i] + brought(3, i), va_ref[0, i]]
        lines += [vb_ref[y, i] for y in range(wy - 2)]
        lines += [va_ref[1, i] + brought(1, i), sums_d[i]]
        v_ref[i] = merge(lines[1::2], lines[0::2])
        if i < wx:
            parts = [jnp.broadcast_to(diag_ref[pl.ds(i * wy + y, 1), :], (4, z)) for y in range(wy)]
            parts += [jnp.broadcast_to(edge_diag[i : i + 1], (4, z)), jnp.zeros((4, z), F32)]
            inv_ref[i] = reciprocal(tall(parts))


def reciprocal(diag):
    present = diag > 0.0
    return jnp.where(present, (1.0 / gain) / jnp.where(present, diag, 1.0), 0.0)


def final_kernel(
    wx, wy, visc_ref, l_ref, kp_ref, parts_ref, mx_ref, ownx_ref, r_in, late_ref, v_ref, inv_ref, v1_ref,
    yd_ref, yu_ref, outer_in, inner_in, out_hbm, r_ref, held, fix, sems,
):
    here, last = lax.axis_index("gx"), lax.axis_size("gx") - 1

    def from_high(start, size):
        rows = pl.ds(start, size)
        value = jnp.where(even("gx"), inner_in[rows, :], outer_in[rows, :])
        return jnp.where(here < last, value, jnp.zeros_like(value))

    def from_low(start, size):
        rows = pl.ds(start, size)
        value = jnp.where(even("gx"), outer_in[rows, :], inner_in[rows, :])
        return jnp.where(here > 0, value, jnp.zeros_like(value))

    cells, z = wx * wy, l_ref.shape[3]
    rows = v_ref.shape[1]
    row = lambda i, col: kp_ref[i, pl.ds(col, 1), :]
    traces = [from_high(48 * j, 48) for j in range(wy + 2)]
    delta = dot(mx_ref[pl.ds(288, 96), :], wide(traces))
    rim_x = from_high(48 * (wy + 2), tail_rows(rows + 3 * wy + 4)).astype(F32)
    rim_l = from_low(48 * wy, tail_rows(rows + 32 + 3 * (wy + 2) - 1)).astype(F32)
    misc_d = read_tail(yd_ref, wx, 0)[2]
    misc_u = read_tail(yu_ref, wx, 1)[2]
    flags_high = rim_x[rows + 2 * (wy + 1) : rows + 3 * wy + 4]
    corner = (wx - 1) * wy
    arrived = [from_low(48 * y, 48) for y in range(wy)]
    arrived_corners = slot_corners(arrived, parts_ref, 1)
    codes = rim_l[rows + 32 : rows + 32 + wy + 2]
    keep_z = rim_l[rows + 32 + wy + 2 : rows + 32 + 2 * (wy + 2)]
    keep_y = rim_l[rows + 32 + 2 * (wy + 2) : rows + 32 + 3 * (wy + 2) - 1]
    low_visc = level_visc(codes, visc_ref)
    low_keep_z = z_next(keep_z)
    lines = [[], [], []]
    high_scales = []
    del r_in
    for j in range(-1, wy + 1):
        n = j + 1
        part = delta[:, z * n : z * n + z]
        flag = flags_high[n : n + 1]
        if j < 0:
            visc = level_visc(misc_u[wx - 1 : wx], visc_ref)
            kz = misc_u[3 * wx - 1 : 3 * wx]
            keeps = [misc_u[2 * wx - 1 : 2 * wx], flag, None, row(1, corner), kz, z_next(kz)]
        elif j < wy:
            here = corner + j
            visc = row(4, here)
            high_y = row(1, here + 1) if j < wy - 1 else misc_d[wx - 1 : wx]
            keeps = [row(0, here), flag, row(1, here), high_y, row(2, here), row(3, here)]
        else:
            visc = level_visc(misc_d[wx + 1 : wx + 2], visc_ref)
            kz = misc_d[wx + 3 : wx + 4]
            keeps = [misc_d[wx + 2 : wx + 3], flag, misc_d[wx - 1 : wx], None, kz, z_next(kz)]
        scales = [None if keep is None else visc * keep for keep in keeps]
        corners = scaled_corners(part, scales)
        one = v1_ref[n] * flag
        lines[0].append(corners[0])
        lines[1].append(corners[1] + one[0:8] + z_prev(one[8:16]))
        high_scales.append(scales)
        own = ownx_ref[:, pl.ds(z * n, z)]
        visc = low_visc[n : n + 1]
        flag = misc_u[wx : wx + 1] if j < 0 else misc_d[wx : wx + 1] if j == wy else row(0, j)
        scales = [
            None, visc * flag, None if j < 0 else visc * keep_y[j : j + 1],
            None if j == wy else visc * keep_y[j + 1 : j + 2], visc * keep_z[n : n + 1], visc * low_keep_z[n : n + 1],
        ]
        corners = scaled_corners(own[48:144], scales, (1,))[0]
        if 0 <= j < wy:
            one = arrived_corners[j] * flag
            lines[2].append(corners + one[0:8] + z_prev(one[8:16]))
            face = (arrived[j].astype(F32) + visc * (own[0:48] + penalty * l_ref[0, j].astype(F32))) * flag
            r_ref[0, pl.ds(j, 48, stride=cells), :] = late_ref[3, j] + face
        else:
            at = rows + (0 if j < 0 else 16)
            one = rim_l[at : at + 16] * flag
            lines[2].append(corners + one[0:8] + z_prev(one[8:16]))
    low, before, first = [merge(part[1::2], part[0::2]) for part in lines]
    top = v_ref[wx] + before + rim_x[0:rows]
    values = [(v_ref[0] + first + rim_l[0:rows]) * inv_ref[0]]
    values += [v_ref[i] * inv_ref[i] for i in range(1, wx - 1)]
    values += [(v_ref[wx - 1] + low) * inv_ref[wx - 1]]
    diag = rim_x[rows : rows + wy + 1] + rim_x[rows + wy + 1 : rows + 2 * (wy + 1)]
    parts = [jnp.broadcast_to(diag[j : j + 1], (4, z)) for j in range(wy + 1)]
    values += [top * reciprocal(tall(parts + [jnp.zeros((rows - 4 * (wy + 1), z), F32)]))]
    high = [pltpu.roll(value, rows - 4, 0) for value in values]
    for i in range(wx + 1):
        fix[0, pl.ds(4 * wy * i, 4 * wy), :] = values[i][0 : 4 * wy]
        fix[1, pl.ds(4 * wy * i, 4 * wy), :] = high[i][0 : 4 * wy]
    vertex = lambda c, p, q: fix[q, pl.ds(4 * wy * p + c, cells, stride=4), :]
    delta = columns(dot(mx_ref[pl.ds(0, 240), :], wide(traces[1 : wy + 1])), wy)
    behind = dot(mx_ref[pl.ds(96, 48), :], traces[0]) * high_scales[0][3]
    copies = []
    for d in range(3):
        for j in range(wy):
            scales = high_scales[j + 1]
            part = [delta[j][48 * i : 48 * i + 48] for i in range(5)]
            if d == 0:
                flux = part[0] * scales[0]
            elif d == 1:
                flux = part[1] * scales[2] + behind
                behind = part[2] * scales[3]
            else:
                flux = part[3] * scales[4] + z_prev(part[4] * scales[5])
            r_ref[d, pl.ds(corner + j, 48, stride=cells), :] = late_ref[d, j] + flux
        flags = kp_ref[d]
        for c in range(3):
            if d == 0:
                near = [vertex(c, 0, q) * flags for q in range(2)]
                far = [z_next(vertex(c, 0, q)) * flags for q in range(2)]
                corner_values = [[near[0], far[0]], [near[1], far[1]]]
            elif d == 1:
                corner_values = [[vertex(c, p, 0) * flags, z_next(vertex(c, p, 0)) * flags] for p in range(2)]
            else:
                corner_values = [[vertex(c, p, q) * flags for q in range(2)] for p in range(2)]
            lines = [between(corner_values[0][t], corner_values[1][t]) for t in range(2)]
            for a in range(4):
                for b, value in enumerate(between(lines[0][a], lines[1][a])):
                    at = pl.ds(cells * (16 * c + 4 * a + b), cells)
                    held[d, at, :] = (r_ref[d, at, :] + value).astype(BF)
            part = pl.ds(16 * cells * c, 16 * cells)
            copies.append(pltpu.make_async_copy(held.at[d, part], out_hbm.at[d, part], sems.at[3 * d + c]))
            copies[-1].start()
    for copy in copies:
        copy.wait()


def call(body, args, outs, scratch, flops, hbm=False, aliases=None):
    if hbm:
        args = tuple(pltpu.with_memory_space_constraint(a, pltpu.HBM) for a in args)
    keywords = {}
    if aliases:
        spaces = [pltpu.HBM] + [pltpu.VMEM] * (len(outs) - 1)
        keywords = dict(out_specs=tuple(pl.BlockSpec(memory_space=space) for space in spaces), input_output_aliases=aliases)
    return pl.pallas_call(
        body,
        **keywords,
        in_specs=[pl.BlockSpec(memory_space=pltpu.HBM if hbm else pltpu.VMEM)] * len(args),
        out_shape=outs,
        scratch_shapes=scratch,
        cost_estimate=pl.CostEstimate(flops=flops, bytes_accessed=1000000, transcendentals=0),
        compiler_params=pltpu.CompilerParams(vmem_limit_bytes=16 * 1024 * 1024),
    )(*args)


def local(traces, dirichlet, visc_class, viscosity, coarse_diag, solve_map, flux_map):
    wx, wy, z = traces.shape[2:]
    cells = wx * wy
    rows = 8 * (wy // 2 + 1)
    per_hex = 2 * 384 * 288 * z
    parts = jnp.asarray(slot_table())
    vm = pltpu.VMEM
    bind = lambda body: functools.partial(body, wx, wy)
    y_message = vm((48 * wx + 48 + tail_rows(8 * ((wx + 2) // 2) + 8 + 3 * wx + 4), z), BF)
    x_message = vm((48 * (wy + 2) + tail_rows(rows + 3 * wy + 4), z), BF)

    (lifted, nat, flags, visc, diag, s_turned, f_map, parts, va, v1a, v3, *swaps) = call(
        bind(first_kernel),
        (
            viscosity, traces.reshape(3, 48 * cells, z), dirichlet.reshape(3, cells, z),
            visc_class.reshape(cells, z), coarse_diag.reshape(cells, z), solve_map.T, flux_map, parts,
        ),
        (
            vm((4, cells, 48, z), BF), vm((3, 48 * cells, z), F32), vm((6, cells, z), F32), vm((viscosity.shape[0], z), F32), vm((cells, z), F32),
            vm(solve_map.shape[::-1], BF), vm(flux_map.shape, BF), vm(parts.shape, BF),
            vm((2, wx + 1, 8, z), F32), vm((2, 16, z), F32), vm((wx, 32, z), F32),
            y_message, y_message, y_message,
        ),
        [
            y_message, y_message,
            vm((3, 48 * cells, z), BF), vm((3, cells, z), jnp.int32), vm((cells, z), jnp.int32),
            pltpu.SMEM(viscosity.shape, F32), pltpu.SemaphoreType.DMA((8,)),
        ],
        wx * per_hex, True,
    )
    swaps = [swap(message, "gy", "gx", k, 3) for k, message in enumerate(swaps)]
    c, vb, v1b, mx, my, own = call(
        bind(middle_kernel),
        (lifted, nat, flags, s_turned, f_map, parts),
        (
            vm((6, cells, 48, z), F32), vm((wy - 2, wx + 1, 8, z), F32), vm((wy - 2, 16, z), F32),
            vm((384, 48), BF), vm((384, 48), BF), vm((144, wx * z), F32),
        ),
        [vm((4, cells, 48, z), BF), vm((384, 288), BF), vm((288, 256), BF)], cells * per_hex,
    )
    c3, vt, vl, v1, face, yd, yu, inner, outer = call(
        bind(turn_kernel),
        (
            visc, lifted, flags, diag, parts, my, own, c, va, vb, v1a, v1b, v3, *swaps,
        ),
        (
            vm((2, 6, 48, z), F32), vm((2, 2, 8, z), F32), vm((2, 2, 8, z), F32), vm((wy + 2, 16, z), F32),
            vm((2, 48, z), F32), y_message, y_message, x_message, x_message,
        ),
        [x_message, x_message], 2 * per_hex,
    )
    inner = swap(inner, "gx", "gy", 0)
    outer = swap(outer, "gx", "gy", 1)
    residual, late, vs, inverse, ownx = call(
        bind(assemble_kernel),
        (
            visc, lifted, flags, diag, parts, mx, my, own, c, c3, va, vb, v3, vt, vl, face, yd, yu,
        ),
        (
            vm((3, 48 * cells, z), F32), vm((4, wy, 48, z), F32), vm((wx + 1, rows, z), F32), vm((wx, rows, z), F32),
            vm((144, (wy + 2) * z), F32),
        ),
        [vm((wx - 2, 6, 48, z), F32)], 4 * per_hex,
    )
    out, _ = call(
        bind(final_kernel),
        (
            visc, lifted, flags, parts, mx, ownx, residual, late, vs, inverse, v1, yd, yu, outer, inner,
        ),
        (jax.ShapeDtypeStruct((3, 48 * cells, z), BF), vm((3, 48 * cells, z), F32)),
        [vm((3, 48 * cells, z), BF), vm((2, 4 * wy * (wx + 1), z), F32), pltpu.SemaphoreType.DMA((9,))], 6 * per_hex,
        aliases={6: 1},
    )
    return out.reshape(traces.shape)


def solution(mesh):
    in_specs = (
        P(None, None, "gx", "gy", None),
        P(None, "gx", "gy", None),
        P("gx", "gy", None),
        P(),
        P("gx", "gy", None),
        P(),
        P(),
    )
    out_specs = P(None, None, "gx", "gy", None)
    return jax.shard_map(local, mesh=mesh, in_specs=in_specs, out_specs=out_specs, check_vma=False)
```

```python
import functools
import math

import jax
import jax.numpy as jnp
import ml_dtypes
import numpy as np
from jax import lax
from jax.experimental import pallas as pl
from jax.experimental.pallas import tpu as pltpu
from jax.sharding import PartitionSpec as P

penalty = 0.5
BF = jnp.bfloat16
F32 = jnp.float32
lift = 1.3264
gain = 1.3280711361297461


def swap(value, axis, other, first, step=2):
    count, width = lax.axis_size(axis), lax.axis_size(other)
    place = (lambda i, j: i * width + j) if (axis, other) == ("gx", "gy") else (lambda i, j: j * count + i)
    lows = list(range(first, count - 1, step))
    pairs = [(place(low, j), place(low + 1, j)) for low in lows for j in range(width)]
    alone = [i for i in range(count) if i not in lows and i - 1 not in lows]
    pairs += [(place(i, j), place(i, j + 1)) for i in alone for j in range(0, width - 1, 2)]
    return lax.ppermute(value, ("gx", "gy"), pairs + [(high, low) for low, high in pairs])


def even(axis):
    return lax.rem(lax.axis_index(axis), 2) == 0


def arrive(messages, down_ref, up_ref):
    here, last = lax.axis_index("gy"), lax.axis_size("gy") - 1
    values = [ref[...] for ref in messages]
    for ref, swap_of, present in ((down_ref, lax.rem(here, 3), here < last), (up_ref, lax.rem(here + 2, 3), here > 0)):
        value = jnp.where(swap_of == 0, values[0], jnp.where(swap_of == 1, values[1], values[2]))
        ref[...] = jnp.where(present, value, jnp.zeros_like(value))


def depart_three(down_ref, up_ref, messages):
    here = lax.rem(lax.axis_index("gy"), 3)
    for k, ref in enumerate(messages):
        choose(here == k, up_ref, down_ref, ref)


def depart(axis, down_ref, up_ref, inner_ref, outer_ref):
    choose(even(axis), up_ref, down_ref, inner_ref)
    choose(even(axis), down_ref, up_ref, outer_ref)


def choose(condition, yes_ref, no_ref, out_ref, present=None):
    value = jnp.where(condition, yes_ref[...], no_ref[...])
    out_ref[...] = value if present is None else jnp.where(present, value, jnp.zeros_like(value))


def corner_table():
    gll_points = [-1.0, -math.sqrt(0.2), math.sqrt(0.2), 1.0]
    table = np.zeros((16, 4), np.float64)
    for s in range(4):
        for t in range(4):
            for p in range(2):
                for q in range(2):
                    table[4 * s + t, 2 * p + q] = (
                        (1 + (2 * p - 1) * gll_points[s]) * (1 + (2 * q - 1) * gll_points[t]) / 4
                    )
    return table


def landing(face_slot, high_s, high_t):
    direction, outward = divmod(face_slot, 2)
    if direction == 0:
        return (outward, high_s, high_t)
    if direction == 1:
        return (high_s, outward, high_t)
    return (high_s, high_t, outward)


def gather_table():
    weights = lift * corner_table()
    table = np.zeros((32, 288), np.float64)
    for slot in range(6):
        for s in range(2):
            for t in range(2):
                p, q, r = landing(slot, s, t)
                for c in range(3):
                    cols = slot * 48 + 16 * c + np.arange(16)
                    table[16 * r + 8 * p + 4 * q + c, cols] += weights[:, 2 * s + t]
    return table.astype(ml_dtypes.bfloat16)


def slot_table():
    slots = np.split(gather_table(), 6, axis=1)
    rows = [
        np.r_[0:8, 16:24], np.r_[8:16, 24:32], np.arange(32), np.arange(32), np.arange(16), np.arange(16, 32),
    ]
    return np.concatenate([slot[kept] for slot, kept in zip(slots, rows)], axis=0)


slot_rows = (0, 16, 32, 64, 96, 112, 128)


def between(low, high):
    step = high - low
    return [low, low + (0.5 - 0.5 * math.sqrt(0.2)) * step, low + (0.5 + 0.5 * math.sqrt(0.2)) * step, high]


def lanes(shape):
    return lax.broadcasted_iota(jnp.int32, shape, len(shape) - 1)


def z_next(value):
    last = value.shape[-1] - 1
    return jnp.where(lanes(value.shape) < last, pltpu.roll(value, last, value.ndim - 1), 0.0)


def z_prev(value):
    return jnp.where(lanes(value.shape) > 0, pltpu.roll(value, 1, value.ndim - 1), 0.0)


def dot(left, right):
    return jnp.dot(left, right, preferred_element_type=F32)


def wide(parts):
    return jnp.concatenate(parts, axis=1)


def tall(parts):
    return jnp.concatenate(parts, axis=0)


def columns(rows, count):
    z = rows.shape[1] // count
    return [rows[:, z * h : z * h + z] for h in range(count)]


def elements(slots):
    return tall([wide([hexa[s] for hexa in slots]) for s in range(6)])


def vertex_part(flux, parts_ref):
    rows = []
    for s in range(6):
        first, size = slot_rows[s], slot_rows[s + 1] - slot_rows[s]
        rows.append(dot(parts_ref[pl.ds(first, size), :], flux[48 * s : 48 * s + 48].astype(BF)))
    rows[2:4] = [rows[2] + rows[3]]
    return tall(rows)


def turned_dot(left, right):
    return lax.dot_general(left, right, (((1,), (1,)), ((), ())), preferred_element_type=F32)


def product(f_ref, st_ref, slot):
    first = 0 if slot is None else 48 * slot
    flux = turned_dot(f_ref[...], st_ref[...] if slot is None else st_ref[pl.ds(first, 48), :])
    rows = lax.broadcasted_iota(jnp.int32, flux.shape, 0)
    return flux, flux + jnp.where(rows == lax.broadcasted_iota(jnp.int32, flux.shape, 1) + first, F32(penalty), F32(0.0))


def slot_corners(traces, parts_ref, slot):
    z = traces[0].shape[1]
    first, size = slot_rows[slot], slot_rows[slot + 1] - slot_rows[slot]
    rows = dot(parts_ref[pl.ds(first, size), :], wide([trace.astype(BF) for trace in traces]))
    return [rows[:, z * h : z * h + z] for h in range(len(traces))]


def settle(rows, p):
    return rows[8 * p : 8 * p + 8] + z_prev(rows[16 + 8 * p : 24 + 8 * p])


def scaled_corners(delta, scales, offsets=(0, 1)):
    shape = (8, delta.shape[1])
    blank = jnp.zeros((1, shape[1]), F32)
    y_scale = jnp.where(
        lax.broadcasted_iota(jnp.int32, shape, 0) < 4,
        blank if scales[2] is None else scales[2], blank if scales[3] is None else scales[3],
    )
    results = []
    for p in offsets:
        parts = []
        for r in range(2):
            at = 32 + 16 * r + 8 * p
            part = delta[at : at + 8] * y_scale + delta[at + 32 : at + 40] * scales[4 + r]
            if scales[p] is not None:
                part = part + delta[16 * p + 8 * r : 16 * p + 8 * r + 8] * scales[p]
            parts.append(part)
        results.append(parts[0] + z_prev(parts[1]))
    return results


def level_visc(code, visc_ref):
    visc = jnp.zeros(code.shape, F32)
    for level in range(visc_ref.shape[0]):
        visc = visc + jnp.where(code == F32(level + 1), visc_ref[pl.ds(level, 1), :], F32(0.0))
    return visc


def merge(even, odd):
    odd = tall(odd)
    return tall(even) + pltpu.roll(odd, odd.shape[0] - 4, 0)


def first_kernel(
    wx, wy, visc_hbm, t_hbm, dir_hbm, cls_hbm, diag_hbm, st_hbm, f_hbm, parts_hbm,
    l_ref, nat, kp_ref, visc_ref, diag_ref, st_ref, f_ref, parts_ref, v_ref, v1_ref, v3_ref,
    swap0_ref, swap1_ref, swap2_ref, down_ref, up_ref, t_ref, dir_ref, cls_ref, levels, sems,
):
    cells = wx * wy
    pairs = [
        (parts_hbm, parts_ref), (f_hbm, f_ref), (st_hbm, st_ref), (dir_hbm, dir_ref),
        (cls_hbm, cls_ref), (visc_hbm, levels), (diag_hbm, diag_ref),
    ]
    half = pl.ds(0, 24 * cells), pl.ds(24 * cells, 24 * cells)
    pairs[3:3] = [(t_hbm.at[d, part], t_ref.at[d, part]) for d in range(3) for part in half]
    copies = [pltpu.make_async_copy(a, b, sems.at[i]) for i, (a, b) in enumerate(pairs)]
    for copy in copies:
        copy.start()
    diagonal = lax.broadcasted_iota(jnp.int32, (288, 288), 0) == lax.broadcasted_iota(jnp.int32, (288, 288), 1)
    diagonal = jnp.where(diagonal, F32(penalty), F32(0.0))
    copies[0].wait()
    own = tall([vertex_part(diagonal, parts_ref), diagonal[144:192]])
    copies[1].wait()
    left = tall([vertex_part(f_ref[...], parts_ref).astype(BF), f_ref[pl.ds(144, 48), :]])
    for copy in copies[2:10]:
        copy.wait()
    short = (turned_dot(left, st_ref[...]) + own).astype(BF)
    z = t_ref.shape[2]
    for d in range(3):
        keep = (1 - dir_ref[d]).astype(F32)
        kp_ref[d] = keep
        masked = t_ref[d].astype(F32).reshape(48, cells, z) * keep[None]
        nat[d] = masked.reshape(48 * cells, z)
        lay_out(wx, wy, d, nat, l_ref, True)
    kp_ref[3] = z_next(kp_ref[2])
    for copy in copies[10:]:
        copy.wait()
    for level in range(visc_ref.shape[0]):
        visc_ref[pl.ds(level, 1), :] = jnp.full((1, z), levels[level], F32)
    code = cls_ref[...].astype(F32) + 1.0
    kp_ref[4] = level_visc(code, visc_ref)
    kp_ref[5] = code
    row = lambda i, col: kp_ref[i, pl.ds(col, 1), :]
    corners = []
    for side, y in enumerate((0, wy - 1)):
        where = [(x, y) for x in range(wx)]
        slots, scales, left_out = known_hexes(wx, wy, where, (l_ref, None), kp_ref)
        rows = columns(dot(short if side else short[0:96], elements(slots)), wx)
        corners += known_corners(rows, scales, left_out)
        v1_ref[side] = rows[wx - 1][16:32] * row(4, (wx - 1) * wy + y)
    place = lax.broadcasted_iota(jnp.int32, (32, z), 0)
    lone = [part * row(4, x * wy + wy - 1) for x, part in enumerate(rows)]
    for x in range(wx):
        v3_ref[x] = jnp.where(lax.rem(place, 8) < 4, 0.0, lone[x][32:64])
    sums = [line_sums(corners[:wx]), line_sums(corners[wx:])]
    for side in range(2):
        for i in range(wx + 1):
            v_ref[side, i] = sums[side][i]
    corner = (wx - 1) * wy
    top = wy - 1
    for x in range(wx):
        down_ref[pl.ds(48 * x, 48), :] = l_ref[1, x * wy]
        up_ref[pl.ds(48 * x, 48), :] = lone[x][96:144].astype(BF)
    down_ref[pl.ds(48 * wx, 48), :] = l_ref[0, 0]
    up_ref[pl.ds(48 * wx, 48), :] = l_ref[0, top]
    flags = [row(1, x * wy) for x in range(wx)] + [row(0, 0), row(5, corner), row(0, corner), row(2, corner)]
    diag = tall([diag_ref[pl.ds(x * wy, 1), :] for x in range(wx)])
    high = diag.astype(BF).astype(F32)
    rim = pack(sums[0], 0) + pack([v1_ref[0, 0:8], v1_ref[0, 8:16]], 0) + flags + [high, diag - high]
    put_tail(down_ref, 48 * wx + 48, rim)
    flags = [row(kind, x * wy + top) for kind in (5, 0, 2) for x in range(wx)]
    rim = pack(sums[1], 1) + pack([v1_ref[1, 0:8], v1_ref[1, 8:16]], 1) + flags
    put_tail(up_ref, 48 * wx + 48, rim)
    depart_three(down_ref, up_ref, (swap0_ref, swap1_ref, swap2_ref))


def tail_rows(count):
    return -(-count // 16) * 16


def put_tail(ref, start, rows):
    count = sum(part.shape[0] for part in rows)
    full = ref.shape[0] - start
    if full > count:
        rows = rows + [jnp.zeros((full - count, rows[0].shape[1]), F32)]
    ref[pl.ds(start, full), :] = tall(rows).astype(BF)


def pack(parts, half):
    place = lax.broadcasted_iota(jnp.int32, parts[0].shape, 0)
    parts = parts + [jnp.zeros_like(parts[0])] * (len(parts) % 2)
    packed = []
    for low, high in zip(parts[0::2], parts[1::2]):
        if half:
            low = pltpu.roll(low, 4, 0)
        else:
            high = pltpu.roll(high, 4, 0)
        packed.append(jnp.where(place < 4, low, high))
    return packed


def unpack(packed, count, half):
    parts = []
    for n in range(count):
        part = packed[8 * (n // 2) : 8 * (n // 2) + 8]
        parts.append(part if n % 2 == half else pltpu.roll(part, 4, 0))
    return parts


def read_tail(ref, wx, half):
    start = 48 * wx + 48
    rows = ref[pl.ds(start, ref.shape[0] - start), :].astype(F32)
    size = 8 * ((wx + 2) // 2)
    return unpack(rows, wx + 1, half), unpack(rows[size : size + 8], 2, half), rows[size + 8 :]


def line_sums(corners):
    low, high = [part[0] for part in corners], [part[1] for part in corners]
    return [low[0]] + [low[x] + high[x - 1] for x in range(1, len(low))] + [high[-1]]


def early(wx, wy, d, x, y):
    return y in (0, wy - 1) or (d == 0 and x == 0) or (d == 1 and y == 1)


def lay_out(wx, wy, d, nat, l_ref, first):
    for x in range(wx):
        for y in range(wy):
            if early(wx, wy, d, x, y) == first:
                col = x * wy + y
                part = nat[d, pl.ds(col, 48, stride=wx * wy), :]
                l_ref[d, col] = part.astype(BF)
                if d == 2:
                    l_ref[3, col] = z_next(part).astype(BF)


def known_hexes(wx, wy, where, l_refs, kp_ref):
    z = l_refs[0].shape[3]
    nothing = jnp.zeros((48, z), BF)
    row = lambda i, col: kp_ref[i, pl.ds(col, 1), :]
    trace = lambda d, x, y: l_refs[0 if early(wx, wy, min(d, 2), x, y) else 1][d, x * wy + y]
    slots, scales, left_out = [], [], []
    for x, y in where:
        here = x * wy + y
        visc = row(4, here)
        last_x, last_y = x == wx - 1, y == wy - 1
        slots.append(
            [
                trace(0, x, y), nothing if last_x else trace(0, x + 1, y),
                trace(1, x, y), nothing if last_y else trace(1, x, y + 1),
                trace(2, x, y), trace(3, x, y),
            ]
        )
        scales.append(
            [
                visc * row(0, here), visc if last_x else visc * row(0, here + wy),
                visc * row(1, here), visc if last_y else visc * row(1, here + 1),
                visc * row(2, here), visc * row(3, here),
            ]
        )
        left_out.append(([1] if last_x else []) + ([3] if last_y else []))
    return slots, scales, left_out


def known_corners(vertex, scales, left_out):
    return [
        scaled_corners(part, [None if s in out else scale[s] for s in range(6)])
        for part, scale, out in zip(vertex, scales, left_out)
    ]


def middle_kernel(
    wx, wy, l_ref, nat, kp_ref, st_ref, f_ref, parts_ref,
    c_ref, v_ref, v1_ref, mx_ref, my_ref, own_ref, rest_ref, m_ref, lost_ref,
):
    for slot, ref in ((1, mx_ref), (3, my_ref)):
        bare, flux = product(f_ref, st_ref, slot)
        turned = tall([bare[0:48], bare[96:288], bare[48:96]]) if slot == 1 else bare
        ref[pl.ds(0, 288), :] = turned.astype(BF)
        ref[pl.ds(288, 96), :] = vertex_part(flux, parts_ref).astype(BF)
    flux = product(f_ref, st_ref, None)[1]
    m_ref[pl.ds(0, 288), :] = flux.astype(BF)
    m_ref[pl.ds(288, 96), :] = vertex_part(flux, parts_ref).astype(BF)
    lost_ref[...] = (flux - flux.astype(BF).astype(F32))[:, 0:256].astype(BF)
    for d in range(3):
        lay_out(wx, wy, d, nat, rest_ref, False)
    own_ref[...] = dot(
        tall([my_ref[pl.ds(144, 48), :], my_ref[pl.ds(288, 96), :]]), wide([l_ref[1, x * wy] for x in range(wx)])
    )
    for y in range(wy):
        inside = 0 < y < wy - 1
        where = [(x, y) for x in range(wx)]
        slots, scales, left_out = known_hexes(wx, wy, where, (l_ref, rest_ref), kp_ref)
        element = elements(slots)
        rows = dot(m_ref[...] if inside else m_ref[pl.ds(0, 288), :], element)
        lost = columns(dot(lost_ref[...], element[0:256]), wx)
        rows = columns(rows, wx)
        for x in range(wx):
            for s in range(6):
                part = slice(48 * s, 48 * s + 48)
                c_ref[s, x * wy + y] = (rows[x][part] + lost[x][part]) * scales[x][s]
        if inside:
            corners = known_corners([part[288:] for part in rows], scales, left_out)
            v1_ref[y - 1] = rows[wx - 1][304:320] * kp_ref[4, pl.ds((wx - 1) * wy + y, 1), :]
            for i, part in enumerate(line_sums(corners)):
                v_ref[y - 1, i] = part


def after_y(wx, wy, xs, visc_ref, l_ref, kp_ref, parts_ref, my_ref, own_ref, v3_ref, down_ref, up_ref):
    z = l_ref.shape[3]
    misc_d = read_tail(down_ref, wx, 0)[2]
    misc_u = read_tail(up_ref, wx, 1)[2]
    row = lambda i, col: kp_ref[i, pl.ds(col, 1), :]
    delta = dot(my_ref[...], wide([down_ref[pl.ds(48 * x, 48), :] for x in xs]))
    arrived = [up_ref[pl.ds(48 * x, 48), :].astype(F32) for x in xs]
    arrived_corners = slot_corners(arrived, parts_ref, 3)
    results = []
    for n, x in enumerate(xs):
        here = x * wy + wy - 1
        last = x == wx - 1
        part = delta[:, z * n : z * n + z]
        visc = row(4, here)
        scales = [
            visc * row(0, here), visc if last else visc * row(0, here + wy), visc * row(1, here),
            visc * misc_d[x : x + 1], visc * row(2, here), visc * row(3, here),
        ]
        flux = [part[48 * s : 48 * s + 48] * scales[s] for s in range(6)]
        used = [None if (s == 1 and last) else scales[s] for s in range(6)]
        known = v3_ref[x] * misc_d[x : x + 1]
        top = [rows + settle(known, p) for p, rows in enumerate(scaled_corners(part[288:384], used))]
        top_one = part[304:320] * visc
        here = x * wy
        visc = level_visc(misc_u[x : x + 1], visc_ref)
        flag = row(1, here)
        own = own_ref[:, pl.ds(z * x, z)]
        keep_z = misc_u[2 * wx + x : 2 * wx + x + 1]
        scales = [
            visc * misc_u[wx + x : wx + x + 1], None if last else visc * misc_u[wx + x + 1 : wx + x + 2],
            None, visc * flag, visc * keep_z, visc * z_next(keep_z),
        ]
        known = arrived_corners[n] * flag
        low = [rows + settle(known, p) for p, rows in enumerate(scaled_corners(own[48:144], scales))]
        low_one = own[64:80] * visc
        face = (arrived[n] + visc * (own[0:48] + penalty * l_ref[1, here].astype(F32))) * flag
        results.append((flux, top, top_one, low, low_one, face))
    return results


def turn_kernel(
    wx, wy, visc_ref, l_ref, kp_ref, diag_ref, parts_ref, my_ref, own_ref, c_ref, va_ref, vb_ref,
    v1a_ref, v1b_ref, v3_ref, swap0_in, swap1_in, swap2_in,
    c3_ref, vt_ref, vl_ref, v1_ref, face_ref, yd_ref, yu_ref, inner_ref, outer_ref, down_ref, up_ref,
):
    z = l_ref.shape[3]
    arrive((swap0_in, swap1_in, swap2_in), yd_ref, yu_ref)
    xs = (0, wx - 1)
    results = after_y(wx, wy, xs, visc_ref, l_ref, kp_ref, parts_ref, my_ref, own_ref, v3_ref, yd_ref, yu_ref)
    row = lambda i, col: kp_ref[i, pl.ds(col, 1), :]
    sums_d, one_d, misc_d = read_tail(yd_ref, wx, 0)
    sums_u, one_u, misc_u = read_tail(yu_ref, wx, 1)
    edge_high, edge_low = misc_d[wx + 4 : 2 * wx + 4], misc_d[2 * wx + 4 : 3 * wx + 4]
    for n, (flux, top, top_one, low, low_one, face) in enumerate(results):
        for s in range(6):
            c3_ref[n, s] = flux[s]
        face_ref[n] = face
        for p in range(2):
            vt_ref[n, p] = top[p]
            vl_ref[n, p] = low[p]
    flux, top, top_one, low, low_one, face = results[1]
    mine = tall(one_u) + low_one
    v1_ref[0] = mine
    v1_ref[1] = v1a_ref[0]
    for y in range(wy - 2):
        v1_ref[2 + y] = v1b_ref[y]
    v1_ref[wy] = v1a_ref[1] + top_one
    v1_ref[wy + 1] = tall(one_d)

    def plane(i, n, p):
        lines = [sums_u[i] + vl_ref[n, p], va_ref[0, i]]
        lines += [vb_ref[y, i] for y in range(wy - 2)]
        lines += [va_ref[1, i] + vt_ref[n, p], sums_d[i]]
        return merge(lines[1::2], lines[0::2])

    down_ref[pl.ds(0, 48), :] = yu_ref[pl.ds(48 * wx, 48), :]
    for y in range(wy):
        down_ref[pl.ds(48 + 48 * y, 48), :] = l_ref[0, y]
    down_ref[pl.ds(48 * (wy + 1), 48), :] = yd_ref[pl.ds(48 * wx, 48), :]
    diag = diag_ref[pl.ds(0, wy), :]
    high = diag.astype(BF).astype(F32)
    rim = [plane(0, 0, 0), high, edge_high[0:1], diag - high, edge_low[0:1]]
    rim += [misc_u[wx : wx + 1], kp_ref[0, 0:wy], misc_d[wx : wx + 1]]
    put_tail(down_ref, 48 * (wy + 2), rim)
    corner = (wx - 1) * wy
    for y in range(wy):
        part = c_ref[1, corner + y]
        up_ref[pl.ds(48 * y, 48), :] = (part + flux[1] if y == wy - 1 else part).astype(BF)
    last = pl.ds(corner, wy)
    rim = [plane(wx, 1, 1), mine, *one_d]
    rim += [misc_u[wx - 1 : wx], kp_ref[5, last], misc_d[wx + 1 : wx + 2]]
    rim += [misc_u[3 * wx - 1 : 3 * wx], kp_ref[2, last], misc_d[wx + 3 : wx + 4]]
    rim += [kp_ref[1, last], misc_d[wx - 1 : wx]]
    put_tail(up_ref, 48 * wy, rim)
    depart("gx", down_ref, up_ref, inner_ref, outer_ref)


def assemble_kernel(
    wx, wy, visc_ref, l_ref, kp_ref, diag_ref, parts_ref, mx_ref, my_ref, own_ref, c_ref, c3_ref,
    va_ref, vb_ref, v3_ref, vt_ref, vl_ref, face_ref, yd_ref, yu_ref,
    r_ref, late_ref, v_ref, inv_ref, ownx_ref, mid,
):
    z = l_ref.shape[3]
    cells = wx * wy
    xs = tuple(range(1, wx - 1))
    results = after_y(wx, wy, xs, visc_ref, l_ref, kp_ref, parts_ref, my_ref, own_ref, v3_ref, yd_ref, yu_ref)
    for n, part in enumerate(results):
        for s in range(6):
            mid[n, s] = part[0][s]
    traces = [yu_ref[pl.ds(48 * wx, 48), :]] + [l_ref[0, y] for y in range(wy)] + [yd_ref[pl.ds(48 * wx, 48), :]]
    ownx_ref[...] = dot(mx_ref[pl.ds(240, 144), :], wide(traces))

    def contrib(slot, x, y):
        here = c_ref[slot, x * wy + y]
        if y < wy - 1:
            return here
        return here + (mid[x - 1, slot] if 0 < x < wx - 1 else c3_ref[0 if x == 0 else 1, slot])

    for x in range(wx):
        for y in range(wy):
            col = pl.ds(x * wy + y, 48, stride=cells)
            if y:
                behind = contrib(3, x, y - 1)
            elif 0 < x < wx - 1:
                behind = results[x - 1][5]
            else:
                behind = face_ref[0 if x == 0 else 1]
            ahead = contrib(0, x, y) + contrib(1, x - 1, y) if x else contrib(0, x, y)
            sides = [ahead, contrib(2, x, y) + behind, contrib(4, x, y) + z_prev(contrib(5, x, y))]
            for d in range(3):
                if x == wx - 1:
                    late_ref[d, y] = sides[d]
                elif d == 0 and x == 0:
                    late_ref[3, y] = sides[d]
                else:
                    r_ref[d, col, :] = sides[d]
    sums_d, one_d, misc_d = read_tail(yd_ref, wx, 0)
    sums_u, one_u, misc_u = read_tail(yu_ref, wx, 1)
    edge_diag = misc_d[wx + 4 : 2 * wx + 4] + misc_d[2 * wx + 4 : 3 * wx + 4]

    def brought(which, i):
        held = vt_ref if which == 1 else vl_ref
        terms = []
        for x, p in ((i, 0), (i - 1, 1)):
            if x in (0, wx - 1):
                terms.append(held[0 if x == 0 else 1, p])
            elif 0 < x < wx - 1:
                terms.append(results[x - 1][which][p])
        return sum(terms[1:], terms[0])

    for i in range(wx + 1):
        lines = [sums_u[i] + brought(3, i), va_ref[0, i]]
        lines += [vb_ref[y, i] for y in range(wy - 2)]
        lines += [va_ref[1, i] + brought(1, i), sums_d[i]]
        v_ref[i] = merge(lines[1::2], lines[0::2])
        if i < wx:
            parts = [jnp.broadcast_to(diag_ref[pl.ds(i * wy + y, 1), :], (4, z)) for y in range(wy)]
            parts += [jnp.broadcast_to(edge_diag[i : i + 1], (4, z)), jnp.zeros((4, z), F32)]
            inv_ref[i] = reciprocal(tall(parts))


def reciprocal(diag):
    present = diag > 0.0
    return jnp.where(present, (1.0 / gain) / jnp.where(present, diag, 1.0), 0.0)


def final_kernel(
    wx, wy, visc_ref, l_ref, kp_ref, parts_ref, mx_ref, ownx_ref, r_in, late_ref, v_ref, inv_ref, v1_ref,
    yd_ref, yu_ref, outer_in, inner_in, out_hbm, r_ref, held, fix, sems,
):
    here, last = lax.axis_index("gx"), lax.axis_size("gx") - 1

    def from_high(start, size):
        rows = pl.ds(start, size)
        value = jnp.where(even("gx"), inner_in[rows, :], outer_in[rows, :])
        return jnp.where(here < last, value, jnp.zeros_like(value))

    def from_low(start, size):
        rows = pl.ds(start, size)
        value = jnp.where(even("gx"), outer_in[rows, :], inner_in[rows, :])
        return jnp.where(here > 0, value, jnp.zeros_like(value))

    cells, z = wx * wy, l_ref.shape[3]
    rows = v_ref.shape[1]
    row = lambda i, col: kp_ref[i, pl.ds(col, 1), :]
    traces = [from_high(48 * j, 48) for j in range(wy + 2)]
    delta = dot(mx_ref[pl.ds(288, 96), :], wide(traces))
    rim_x = from_high(48 * (wy + 2), tail_rows(rows + 3 * wy + 4)).astype(F32)
    rim_l = from_low(48 * wy, tail_rows(rows + 32 + 3 * (wy + 2) - 1)).astype(F32)
    misc_d = read_tail(yd_ref, wx, 0)[2]
    misc_u = read_tail(yu_ref, wx, 1)[2]
    flags_high = rim_x[rows + 2 * (wy + 1) : rows + 3 * wy + 4]
    corner = (wx - 1) * wy
    arrived = [from_low(48 * y, 48) for y in range(wy)]
    arrived_corners = slot_corners(arrived, parts_ref, 1)
    codes = rim_l[rows + 32 : rows + 32 + wy + 2]
    keep_z = rim_l[rows + 32 + wy + 2 : rows + 32 + 2 * (wy + 2)]
    keep_y = rim_l[rows + 32 + 2 * (wy + 2) : rows + 32 + 3 * (wy + 2) - 1]
    low_visc = level_visc(codes, visc_ref)
    low_keep_z = z_next(keep_z)
    lines = [[], [], []]
    high_scales = []
    del r_in
    for j in range(-1, wy + 1):
        n = j + 1
        part = delta[:, z * n : z * n + z]
        flag = flags_high[n : n + 1]
        if j < 0:
            visc = level_visc(misc_u[wx - 1 : wx], visc_ref)
            kz = misc_u[3 * wx - 1 : 3 * wx]
            keeps = [misc_u[2 * wx - 1 : 2 * wx], flag, None, row(1, corner), kz, z_next(kz)]
        elif j < wy:
            here = corner + j
            visc = row(4, here)
            high_y = row(1, here + 1) if j < wy - 1 else misc_d[wx - 1 : wx]
            keeps = [row(0, here), flag, row(1, here), high_y, row(2, here), row(3, here)]
        else:
            visc = level_visc(misc_d[wx + 1 : wx + 2], visc_ref)
            kz = misc_d[wx + 3 : wx + 4]
            keeps = [misc_d[wx + 2 : wx + 3], flag, misc_d[wx - 1 : wx], None, kz, z_next(kz)]
        scales = [None if keep is None else visc * keep for keep in keeps]
        corners = scaled_corners(part, scales)
        one = v1_ref[n] * flag
        lines[0].append(corners[0])
        lines[1].append(corners[1] + one[0:8] + z_prev(one[8:16]))
        high_scales.append(scales)
        own = ownx_ref[:, pl.ds(z * n, z)]
        visc = low_visc[n : n + 1]
        flag = misc_u[wx : wx + 1] if j < 0 else misc_d[wx : wx + 1] if j == wy else row(0, j)
        scales = [
            None, visc * flag, None if j < 0 else visc * keep_y[j : j + 1],
            None if j == wy else visc * keep_y[j + 1 : j + 2], visc * keep_z[n : n + 1], visc * low_keep_z[n : n + 1],
        ]
        corners = scaled_corners(own[48:144], scales, (1,))[0]
        if 0 <= j < wy:
            one = arrived_corners[j] * flag
            lines[2].append(corners + one[0:8] + z_prev(one[8:16]))
            face = (arrived[j].astype(F32) + visc * (own[0:48] + penalty * l_ref[0, j].astype(F32))) * flag
            r_ref[0, pl.ds(j, 48, stride=cells), :] = late_ref[3, j] + face
        else:
            at = rows + (0 if j < 0 else 16)
            one = rim_l[at : at + 16] * flag
            lines[2].append(corners + one[0:8] + z_prev(one[8:16]))
    low, before, first = [merge(part[1::2], part[0::2]) for part in lines]
    top = v_ref[wx] + before + rim_x[0:rows]
    values = [(v_ref[0] + first + rim_l[0:rows]) * inv_ref[0]]
    values += [v_ref[i] * inv_ref[i] for i in range(1, wx - 1)]
    values += [(v_ref[wx - 1] + low) * inv_ref[wx - 1]]
    diag = rim_x[rows : rows + wy + 1] + rim_x[rows + wy + 1 : rows + 2 * (wy + 1)]
    parts = [jnp.broadcast_to(diag[j : j + 1], (4, z)) for j in range(wy + 1)]
    values += [top * reciprocal(tall(parts + [jnp.zeros((rows - 4 * (wy + 1), z), F32)]))]
    high = [pltpu.roll(value, rows - 4, 0) for value in values]
    for i in range(wx + 1):
        fix[0, pl.ds(4 * wy * i, 4 * wy), :] = values[i][0 : 4 * wy]
        fix[1, pl.ds(4 * wy * i, 4 * wy), :] = high[i][0 : 4 * wy]
    vertex = lambda c, p, q: fix[q, pl.ds(4 * wy * p + c, cells, stride=4), :]
    delta = columns(dot(mx_ref[pl.ds(0, 240), :], wide(traces[1 : wy + 1])), wy)
    behind = dot(mx_ref[pl.ds(96, 48), :], traces[0]) * high_scales[0][3]
    copies = []
    for d in range(3):
        for j in range(wy):
            scales = high_scales[j + 1]
            part = [delta[j][48 * i : 48 * i + 48] for i in range(5)]
            if d == 0:
                flux = part[0] * scales[0]
            elif d == 1:
                flux = part[1] * scales[2] + behind
                behind = part[2] * scales[3]
            else:
                flux = part[3] * scales[4] + z_prev(part[4] * scales[5])
            r_ref[d, pl.ds(corner + j, 48, stride=cells), :] = late_ref[d, j] + flux
        flags = kp_ref[d]
        for c in range(3):
            if d == 0:
                near = [vertex(c, 0, q) * flags for q in range(2)]
                far = [z_next(vertex(c, 0, q)) * flags for q in range(2)]
                corner_values = [[near[0], far[0]], [near[1], far[1]]]
            elif d == 1:
                corner_values = [[vertex(c, p, 0) * flags, z_next(vertex(c, p, 0)) * flags] for p in range(2)]
            else:
                corner_values = [[vertex(c, p, q) * flags for q in range(2)] for p in range(2)]
            lines = [between(corner_values[0][t], corner_values[1][t]) for t in range(2)]
            for a in range(4):
                for b, value in enumerate(between(lines[0][a], lines[1][a])):
                    at = pl.ds(cells * (16 * c + 4 * a + b), cells)
                    held[d, at, :] = (r_ref[d, at, :] + value).astype(BF)
        copies.append(pltpu.make_async_copy(held.at[d], out_hbm.at[d], sems.at[d]))
        copies[d].start()
    for copy in copies:
        copy.wait()


def call(body, args, outs, scratch, flops, hbm=False, aliases=None):
    if hbm:
        args = tuple(pltpu.with_memory_space_constraint(a, pltpu.HBM) for a in args)
    keywords = {}
    if aliases:
        spaces = [pltpu.HBM] + [pltpu.VMEM] * (len(outs) - 1)
        keywords = dict(out_specs=tuple(pl.BlockSpec(memory_space=space) for space in spaces), input_output_aliases=aliases)
    return pl.pallas_call(
        body,
        **keywords,
        in_specs=[pl.BlockSpec(memory_space=pltpu.HBM if hbm else pltpu.VMEM)] * len(args),
        out_shape=outs,
        scratch_shapes=scratch,
        cost_estimate=pl.CostEstimate(flops=flops, bytes_accessed=1000000, transcendentals=0),
        compiler_params=pltpu.CompilerParams(vmem_limit_bytes=16 * 1024 * 1024),
    )(*args)


def local(traces, dirichlet, visc_class, viscosity, coarse_diag, solve_map, flux_map):
    wx, wy, z = traces.shape[2:]
    cells = wx * wy
    rows = 8 * (wy // 2 + 1)
    per_hex = 2 * 384 * 288 * z
    parts = jnp.asarray(slot_table())
    vm = pltpu.VMEM
    bind = lambda body: functools.partial(body, wx, wy)
    y_message = vm((48 * wx + 48 + tail_rows(8 * ((wx + 2) // 2) + 8 + 3 * wx + 4), z), BF)
    x_message = vm((48 * (wy + 2) + tail_rows(rows + 3 * wy + 4), z), BF)

    (lifted, nat, flags, visc, diag, s_turned, f_map, parts, va, v1a, v3, *swaps) = call(
        bind(first_kernel),
        (
            viscosity, traces.reshape(3, 48 * cells, z), dirichlet.reshape(3, cells, z),
            visc_class.reshape(cells, z), coarse_diag.reshape(cells, z), solve_map.T, flux_map, parts,
        ),
        (
            vm((4, cells, 48, z), BF), vm((3, 48 * cells, z), F32), vm((6, cells, z), F32), vm((viscosity.shape[0], z), F32), vm((cells, z), F32),
            vm(solve_map.shape[::-1], BF), vm(flux_map.shape, BF), vm(parts.shape, BF),
            vm((2, wx + 1, 8, z), F32), vm((2, 16, z), F32), vm((wx, 32, z), F32),
            y_message, y_message, y_message,
        ),
        [
            y_message, y_message,
            vm((3, 48 * cells, z), BF), vm((3, cells, z), jnp.int32), vm((cells, z), jnp.int32),
            pltpu.SMEM(viscosity.shape, F32), pltpu.SemaphoreType.DMA((13,)),
        ],
        wx * per_hex, True,
    )
    swaps = [swap(message, "gy", "gx", k, 3) for k, message in enumerate(swaps)]
    c, vb, v1b, mx, my, own = call(
        bind(middle_kernel),
        (lifted, nat, flags, s_turned, f_map, parts),
        (
            vm((6, cells, 48, z), F32), vm((wy - 2, wx + 1, 8, z), F32), vm((wy - 2, 16, z), F32),
            vm((384, 48), BF), vm((384, 48), BF), vm((144, wx * z), F32),
        ),
        [vm((4, cells, 48, z), BF), vm((384, 288), BF), vm((288, 256), BF)], cells * per_hex,
    )
    c3, vt, vl, v1, face, yd, yu, inner, outer = call(
        bind(turn_kernel),
        (
            visc, lifted, flags, diag, parts, my, own, c, va, vb, v1a, v1b, v3, *swaps,
        ),
        (
            vm((2, 6, 48, z), F32), vm((2, 2, 8, z), F32), vm((2, 2, 8, z), F32), vm((wy + 2, 16, z), F32),
            vm((2, 48, z), F32), y_message, y_message, x_message, x_message,
        ),
        [x_message, x_message], 2 * per_hex,
    )
    inner = swap(inner, "gx", "gy", 0)
    outer = swap(outer, "gx", "gy", 1)
    residual, late, vs, inverse, ownx = call(
        bind(assemble_kernel),
        (
            visc, lifted, flags, diag, parts, mx, my, own, c, c3, va, vb, v3, vt, vl, face, yd, yu,
        ),
        (
            vm((3, 48 * cells, z), F32), vm((4, wy, 48, z), F32), vm((wx + 1, rows, z), F32), vm((wx, rows, z), F32),
            vm((144, (wy + 2) * z), F32),
        ),
        [vm((wx - 2, 6, 48, z), F32)], 4 * per_hex,
    )
    out, _ = call(
        bind(final_kernel),
        (
            visc, lifted, flags, parts, mx, ownx, residual, late, vs, inverse, v1, yd, yu, outer, inner,
        ),
        (jax.ShapeDtypeStruct((3, 48 * cells, z), BF), vm((3, 48 * cells, z), F32)),
        [vm((3, 48 * cells, z), BF), vm((2, 4 * wy * (wx + 1), z), F32), pltpu.SemaphoreType.DMA((3,))], 6 * per_hex,
        aliases={6: 1},
    )
    return out.reshape(traces.shape)


def solution(mesh):
    in_specs = (
        P(None, None, "gx", "gy", None),
        P(None, "gx", "gy", None),
        P("gx", "gy", None),
        P(),
        P("gx", "gy", None),
        P(),
        P(),
    )
    out_specs = P(None, None, "gx", "gy", None)
    return jax.shard_map(local, mesh=mesh, in_specs=in_specs, out_specs=out_specs, check_vma=False)
```

```python
import functools
import math

import jax
import jax.numpy as jnp
import ml_dtypes
import numpy as np
from jax import lax
from jax.experimental import pallas as pl
from jax.experimental.pallas import tpu as pltpu
from jax.sharding import PartitionSpec as P

penalty = 0.5
BF = jnp.bfloat16
F32 = jnp.float32
lift = 1.3264
gain = 1.3280711361297461


def swap(value, axis, other, first, step=2):
    count, width = lax.axis_size(axis), lax.axis_size(other)
    place = (lambda i, j: i * width + j) if (axis, other) == ("gx", "gy") else (lambda i, j: j * count + i)
    lows = list(range(first, count - 1, step))
    pairs = [(place(low, j), place(low + 1, j)) for low in lows for j in range(width)]
    alone = [i for i in range(count) if i not in lows and i - 1 not in lows]
    pairs += [(place(i, j), place(i, j + 1)) for i in alone for j in range(0, width - 1, 2)]
    return lax.ppermute(value, ("gx", "gy"), pairs + [(high, low) for low, high in pairs])


def even(axis):
    return lax.rem(lax.axis_index(axis), 2) == 0


def arrive(messages, down_ref, up_ref):
    here, last = lax.axis_index("gy"), lax.axis_size("gy") - 1
    values = [ref[...] for ref in messages]
    for ref, swap_of, present in ((down_ref, lax.rem(here, 3), here < last), (up_ref, lax.rem(here + 2, 3), here > 0)):
        value = jnp.where(swap_of == 0, values[0], jnp.where(swap_of == 1, values[1], values[2]))
        ref[...] = jnp.where(present, value, jnp.zeros_like(value))


def depart_three(down_ref, up_ref, messages):
    here = lax.rem(lax.axis_index("gy"), 3)
    for k, ref in enumerate(messages):
        choose(here == k, up_ref, down_ref, ref)


def depart(axis, down_ref, up_ref, inner_ref, outer_ref):
    choose(even(axis), up_ref, down_ref, inner_ref)
    choose(even(axis), down_ref, up_ref, outer_ref)


def choose(condition, yes_ref, no_ref, out_ref, present=None):
    value = jnp.where(condition, yes_ref[...], no_ref[...])
    out_ref[...] = value if present is None else jnp.where(present, value, jnp.zeros_like(value))


def corner_table():
    gll_points = [-1.0, -math.sqrt(0.2), math.sqrt(0.2), 1.0]
    table = np.zeros((16, 4), np.float64)
    for s in range(4):
        for t in range(4):
            for p in range(2):
                for q in range(2):
                    table[4 * s + t, 2 * p + q] = (
                        (1 + (2 * p - 1) * gll_points[s]) * (1 + (2 * q - 1) * gll_points[t]) / 4
                    )
    return table


def landing(face_slot, high_s, high_t):
    direction, outward = divmod(face_slot, 2)
    if direction == 0:
        return (outward, high_s, high_t)
    if direction == 1:
        return (high_s, outward, high_t)
    return (high_s, high_t, outward)


def gather_table():
    weights = lift * corner_table()
    table = np.zeros((32, 288), np.float64)
    for slot in range(6):
        for s in range(2):
            for t in range(2):
                p, q, r = landing(slot, s, t)
                for c in range(3):
                    cols = slot * 48 + 16 * c + np.arange(16)
                    table[16 * r + 8 * p + 4 * q + c, cols] += weights[:, 2 * s + t]
    return table.astype(ml_dtypes.bfloat16)


def slot_table():
    slots = np.split(gather_table(), 6, axis=1)
    rows = [
        np.r_[0:8, 16:24], np.r_[8:16, 24:32], np.arange(32), np.arange(32), np.arange(16), np.arange(16, 32),
    ]
    return np.concatenate([slot[kept] for slot, kept in zip(slots, rows)], axis=0)


slot_rows = (0, 16, 32, 64, 96, 112, 128)


def block_table():
    slots = np.split(slot_table().astype(np.float64), slot_rows[1:6], axis=0)
    table = np.zeros((96, 288), np.float64)
    for s, first in enumerate((0, 16, 32, 32, 64, 80)):
        table[first : first + len(slots[s]), 48 * s : 48 * s + 48] += slots[s]
    return table.astype(ml_dtypes.bfloat16)


def between(low, high):
    step = high - low
    return [low, low + (0.5 - 0.5 * math.sqrt(0.2)) * step, low + (0.5 + 0.5 * math.sqrt(0.2)) * step, high]


def lanes(shape):
    return lax.broadcasted_iota(jnp.int32, shape, len(shape) - 1)


def z_next(value):
    last = value.shape[-1] - 1
    return jnp.where(lanes(value.shape) < last, pltpu.roll(value, last, value.ndim - 1), 0.0)


def z_prev(value):
    return jnp.where(lanes(value.shape) > 0, pltpu.roll(value, 1, value.ndim - 1), 0.0)


def dot(left, right):
    return jnp.dot(left, right, preferred_element_type=F32)


def wide(parts):
    return jnp.concatenate(parts, axis=1)


def tall(parts):
    return jnp.concatenate(parts, axis=0)


def columns(rows, count):
    z = rows.shape[1] // count
    return [rows[:, z * h : z * h + z] for h in range(count)]


def elements(slots):
    return tall([wide([hexa[s] for hexa in slots]) for s in range(6)])


def vertex_part(flux, parts_ref):
    rows = []
    for s in range(6):
        first, size = slot_rows[s], slot_rows[s + 1] - slot_rows[s]
        rows.append(dot(parts_ref[pl.ds(first, size), :], flux[48 * s : 48 * s + 48].astype(BF)))
    rows[2:4] = [rows[2] + rows[3]]
    return tall(rows)


def turned_dot(left, right):
    return lax.dot_general(left, right, (((1,), (1,)), ((), ())), preferred_element_type=F32)


def product(f_ref, st_ref, slot):
    first = 0 if slot is None else 48 * slot
    flux = turned_dot(f_ref[...], st_ref[...] if slot is None else st_ref[pl.ds(first, 48), :])
    rows = lax.broadcasted_iota(jnp.int32, flux.shape, 0)
    return flux, flux + jnp.where(rows == lax.broadcasted_iota(jnp.int32, flux.shape, 1) + first, F32(penalty), F32(0.0))


def slot_corners(traces, parts_ref, slot):
    z = traces[0].shape[1]
    first, size = slot_rows[slot], slot_rows[slot + 1] - slot_rows[slot]
    rows = dot(parts_ref[pl.ds(first, size), :], wide([trace.astype(BF) for trace in traces]))
    return [rows[:, z * h : z * h + z] for h in range(len(traces))]


def settle(rows, p):
    return rows[8 * p : 8 * p + 8] + z_prev(rows[16 + 8 * p : 24 + 8 * p])


def scaled_corners(delta, scales, offsets=(0, 1)):
    shape = (8, delta.shape[1])
    blank = jnp.zeros((1, shape[1]), F32)
    y_scale = jnp.where(
        lax.broadcasted_iota(jnp.int32, shape, 0) < 4,
        blank if scales[2] is None else scales[2], blank if scales[3] is None else scales[3],
    )
    results = []
    for p in offsets:
        parts = []
        for r in range(2):
            at = 32 + 16 * r + 8 * p
            part = delta[at : at + 8] * y_scale + delta[at + 32 : at + 40] * scales[4 + r]
            if scales[p] is not None:
                part = part + delta[16 * p + 8 * r : 16 * p + 8 * r + 8] * scales[p]
            parts.append(part)
        results.append(parts[0] + z_prev(parts[1]))
    return results


def level_visc(code, visc_ref):
    visc = jnp.zeros(code.shape, F32)
    for level in range(visc_ref.shape[0]):
        visc = visc + jnp.where(code == F32(level + 1), visc_ref[pl.ds(level, 1), :], F32(0.0))
    return visc


def merge(even, odd):
    odd = tall(odd)
    return tall(even) + pltpu.roll(odd, odd.shape[0] - 4, 0)


def first_kernel(
    wx, wy, visc_hbm, t_hbm, dir_hbm, cls_hbm, diag_hbm, st_hbm, f_hbm, block_hbm,
    l_ref, nat, kp_ref, visc_ref, diag_ref, st_ref, f_ref, v_ref, v1_ref, v3_ref,
    swap0_ref, swap1_ref, swap2_ref, down_ref, up_ref, block_ref, t_ref, dir_ref, cls_ref, levels, sems,
):
    cells = wx * wy
    pairs = [
        (block_hbm, block_ref), (f_hbm, f_ref), (st_hbm, st_ref), (t_hbm, t_ref), (dir_hbm, dir_ref),
        (cls_hbm, cls_ref), (visc_hbm, levels), (diag_hbm, diag_ref),
    ]
    copies = [pltpu.make_async_copy(a, b, sems.at[i]) for i, (a, b) in enumerate(pairs)]
    for copy in copies:
        copy.start()
    copies[0].wait()
    copies[1].wait()
    left = tall([dot(block_ref[...], f_ref[...]).astype(BF), f_ref[pl.ds(144, 48), :]])
    place = lax.broadcasted_iota(jnp.int32, (48, 288), 0) + 144
    diagonal = jnp.where(place == lax.broadcasted_iota(jnp.int32, (48, 288), 1), F32(penalty), F32(0.0))
    own = tall([penalty * block_ref[...].astype(F32), diagonal])
    for copy in copies[2:5]:
        copy.wait()
    short = (turned_dot(left, st_ref[...]) + own).astype(BF)
    z = t_ref.shape[2]
    for d in range(3):
        keep = (1 - dir_ref[d]).astype(F32)
        kp_ref[d] = keep
        masked = t_ref[d].astype(F32).reshape(48, cells, z) * keep[None]
        nat[d] = masked.reshape(48 * cells, z)
        lay_out(wx, wy, d, nat, l_ref, True)
    kp_ref[3] = z_next(kp_ref[2])
    for copy in copies[5:]:
        copy.wait()
    for level in range(visc_ref.shape[0]):
        visc_ref[pl.ds(level, 1), :] = jnp.full((1, z), levels[level], F32)
    code = cls_ref[...].astype(F32) + 1.0
    kp_ref[4] = level_visc(code, visc_ref)
    kp_ref[5] = code
    row = lambda i, col: kp_ref[i, pl.ds(col, 1), :]
    corners = []
    for side, y in enumerate((0, wy - 1)):
        where = [(x, y) for x in range(wx)]
        slots, scales, left_out = known_hexes(wx, wy, where, (l_ref, None), kp_ref)
        rows = columns(dot(short if side else short[0:96], elements(slots)), wx)
        corners += known_corners(rows, scales, left_out)
        v1_ref[side] = rows[wx - 1][16:32] * row(4, (wx - 1) * wy + y)
    place = lax.broadcasted_iota(jnp.int32, (32, z), 0)
    lone = [part * row(4, x * wy + wy - 1) for x, part in enumerate(rows)]
    for x in range(wx):
        v3_ref[x] = jnp.where(lax.rem(place, 8) < 4, 0.0, lone[x][32:64])
    sums = [line_sums(corners[:wx]), line_sums(corners[wx:])]
    for side in range(2):
        for i in range(wx + 1):
            v_ref[side, i] = sums[side][i]
    corner = (wx - 1) * wy
    top = wy - 1
    for x in range(wx):
        down_ref[pl.ds(48 * x, 48), :] = l_ref[1, x * wy]
        up_ref[pl.ds(48 * x, 48), :] = lone[x][96:144].astype(BF)
    down_ref[pl.ds(48 * wx, 48), :] = l_ref[0, 0]
    up_ref[pl.ds(48 * wx, 48), :] = l_ref[0, top]
    flags = [row(1, x * wy) for x in range(wx)] + [row(0, 0), row(5, corner), row(0, corner), row(2, corner)]
    diag = tall([diag_ref[pl.ds(x * wy, 1), :] for x in range(wx)])
    high = diag.astype(BF).astype(F32)
    rim = pack(sums[0], 0) + pack([v1_ref[0, 0:8], v1_ref[0, 8:16]], 0) + flags + [high, diag - high]
    put_tail(down_ref, 48 * wx + 48, rim)
    flags = [row(kind, x * wy + top) for kind in (5, 0, 2) for x in range(wx)]
    rim = pack(sums[1], 1) + pack([v1_ref[1, 0:8], v1_ref[1, 8:16]], 1) + flags
    put_tail(up_ref, 48 * wx + 48, rim)
    depart_three(down_ref, up_ref, (swap0_ref, swap1_ref, swap2_ref))


def tail_rows(count):
    return -(-count // 16) * 16


def put_tail(ref, start, rows):
    count = sum(part.shape[0] for part in rows)
    full = ref.shape[0] - start
    if full > count:
        rows = rows + [jnp.zeros((full - count, rows[0].shape[1]), F32)]
    ref[pl.ds(start, full), :] = tall(rows).astype(BF)


def pack(parts, half):
    place = lax.broadcasted_iota(jnp.int32, parts[0].shape, 0)
    parts = parts + [jnp.zeros_like(parts[0])] * (len(parts) % 2)
    packed = []
    for low, high in zip(parts[0::2], parts[1::2]):
        if half:
            low = pltpu.roll(low, 4, 0)
        else:
            high = pltpu.roll(high, 4, 0)
        packed.append(jnp.where(place < 4, low, high))
    return packed


def unpack(packed, count, half):
    parts = []
    for n in range(count):
        part = packed[8 * (n // 2) : 8 * (n // 2) + 8]
        parts.append(part if n % 2 == half else pltpu.roll(part, 4, 0))
    return parts


def read_tail(ref, wx, half):
    start = 48 * wx + 48
    rows = ref[pl.ds(start, ref.shape[0] - start), :].astype(F32)
    size = 8 * ((wx + 2) // 2)
    return unpack(rows, wx + 1, half), unpack(rows[size : size + 8], 2, half), rows[size + 8 :]


def line_sums(corners):
    low, high = [part[0] for part in corners], [part[1] for part in corners]
    return [low[0]] + [low[x] + high[x - 1] for x in range(1, len(low))] + [high[-1]]


def early(wx, wy, d, x, y):
    return y in (0, wy - 1) or (d == 0 and x == 0) or (d == 1 and y == 1)


def lay_out(wx, wy, d, nat, l_ref, first):
    for x in range(wx):
        for y in range(wy):
            if early(wx, wy, d, x, y) == first:
                col = x * wy + y
                part = nat[d, pl.ds(col, 48, stride=wx * wy), :]
                l_ref[d, col] = part.astype(BF)
                if d == 2:
                    l_ref[3, col] = z_next(part).astype(BF)


def known_hexes(wx, wy, where, l_refs, kp_ref):
    z = l_refs[0].shape[3]
    nothing = jnp.zeros((48, z), BF)
    row = lambda i, col: kp_ref[i, pl.ds(col, 1), :]
    trace = lambda d, x, y: l_refs[0 if early(wx, wy, min(d, 2), x, y) else 1][d, x * wy + y]
    slots, scales, left_out = [], [], []
    for x, y in where:
        here = x * wy + y
        visc = row(4, here)
        last_x, last_y = x == wx - 1, y == wy - 1
        slots.append(
            [
                trace(0, x, y), nothing if last_x else trace(0, x + 1, y),
                trace(1, x, y), nothing if last_y else trace(1, x, y + 1),
                trace(2, x, y), trace(3, x, y),
            ]
        )
        scales.append(
            [
                visc * row(0, here), visc if last_x else visc * row(0, here + wy),
                visc * row(1, here), visc if last_y else visc * row(1, here + 1),
                visc * row(2, here), visc * row(3, here),
            ]
        )
        left_out.append(([1] if last_x else []) + ([3] if last_y else []))
    return slots, scales, left_out


def known_corners(vertex, scales, left_out):
    return [
        scaled_corners(part, [None if s in out else scale[s] for s in range(6)])
        for part, scale, out in zip(vertex, scales, left_out)
    ]


def middle_kernel(
    wx, wy, l_ref, nat, kp_ref, st_ref, f_ref, parts_ref,
    c_ref, v_ref, v1_ref, mx_ref, my_ref, own_ref, rest_ref, m_ref, lost_ref,
):
    for slot, ref in ((1, mx_ref), (3, my_ref)):
        bare, flux = product(f_ref, st_ref, slot)
        turned = tall([bare[0:48], bare[96:288], bare[48:96]]) if slot == 1 else bare
        ref[pl.ds(0, 288), :] = turned.astype(BF)
        ref[pl.ds(288, 96), :] = vertex_part(flux, parts_ref).astype(BF)
    flux = product(f_ref, st_ref, None)[1]
    m_ref[pl.ds(0, 288), :] = flux.astype(BF)
    m_ref[pl.ds(288, 96), :] = vertex_part(flux, parts_ref).astype(BF)
    lost_ref[...] = (flux - flux.astype(BF).astype(F32))[:, 0:256].astype(BF)
    for d in range(3):
        lay_out(wx, wy, d, nat, rest_ref, False)
    own_ref[...] = dot(
        tall([my_ref[pl.ds(144, 48), :], my_ref[pl.ds(288, 96), :]]), wide([l_ref[1, x * wy] for x in range(wx)])
    )
    for y in range(wy):
        inside = 0 < y < wy - 1
        where = [(x, y) for x in range(wx)]
        slots, scales, left_out = known_hexes(wx, wy, where, (l_ref, rest_ref), kp_ref)
        element = elements(slots)
        rows = dot(m_ref[...] if inside else m_ref[pl.ds(0, 288), :], element)
        lost = columns(dot(lost_ref[...], element[0:256]), wx)
        rows = columns(rows, wx)
        for x in range(wx):
            for s in range(6):
                part = slice(48 * s, 48 * s + 48)
                c_ref[s, x * wy + y] = (rows[x][part] + lost[x][part]) * scales[x][s]
        if inside:
            corners = known_corners([part[288:] for part in rows], scales, left_out)
            v1_ref[y - 1] = rows[wx - 1][304:320] * kp_ref[4, pl.ds((wx - 1) * wy + y, 1), :]
            for i, part in enumerate(line_sums(corners)):
                v_ref[y - 1, i] = part


def after_y(wx, wy, xs, visc_ref, l_ref, kp_ref, parts_ref, my_ref, own_ref, v3_ref, down_ref, up_ref):
    z = l_ref.shape[3]
    misc_d = read_tail(down_ref, wx, 0)[2]
    misc_u = read_tail(up_ref, wx, 1)[2]
    row = lambda i, col: kp_ref[i, pl.ds(col, 1), :]
    delta = dot(my_ref[...], wide([down_ref[pl.ds(48 * x, 48), :] for x in xs]))
    arrived = [up_ref[pl.ds(48 * x, 48), :].astype(F32) for x in xs]
    arrived_corners = slot_corners(arrived, parts_ref, 3)
    results = []
    for n, x in enumerate(xs):
        here = x * wy + wy - 1
        last = x == wx - 1
        part = delta[:, z * n : z * n + z]
        visc = row(4, here)
        scales = [
            visc * row(0, here), visc if last else visc * row(0, here + wy), visc * row(1, here),
            visc * misc_d[x : x + 1], visc * row(2, here), visc * row(3, here),
        ]
        flux = [part[48 * s : 48 * s + 48] * scales[s] for s in range(6)]
        used = [None if (s == 1 and last) else scales[s] for s in range(6)]
        known = v3_ref[x] * misc_d[x : x + 1]
        top = [rows + settle(known, p) for p, rows in enumerate(scaled_corners(part[288:384], used))]
        top_one = part[304:320] * visc
        here = x * wy
        visc = level_visc(misc_u[x : x + 1], visc_ref)
        flag = row(1, here)
        own = own_ref[:, pl.ds(z * x, z)]
        keep_z = misc_u[2 * wx + x : 2 * wx + x + 1]
        scales = [
            visc * misc_u[wx + x : wx + x + 1], None if last else visc * misc_u[wx + x + 1 : wx + x + 2],
            None, visc * flag, visc * keep_z, visc * z_next(keep_z),
        ]
        known = arrived_corners[n] * flag
        low = [rows + settle(known, p) for p, rows in enumerate(scaled_corners(own[48:144], scales))]
        low_one = own[64:80] * visc
        face = (arrived[n] + visc * (own[0:48] + penalty * l_ref[1, here].astype(F32))) * flag
        results.append((flux, top, top_one, low, low_one, face))
    return results


def turn_kernel(
    wx, wy, visc_ref, l_ref, kp_ref, diag_ref, parts_ref, my_ref, own_ref, c_ref, va_ref, vb_ref,
    v1a_ref, v1b_ref, v3_ref, swap0_in, swap1_in, swap2_in,
    c3_ref, vt_ref, vl_ref, v1_ref, face_ref, yd_ref, yu_ref, inner_ref, outer_ref, down_ref, up_ref,
):
    z = l_ref.shape[3]
    arrive((swap0_in, swap1_in, swap2_in), yd_ref, yu_ref)
    xs = (0, wx - 1)
    results = after_y(wx, wy, xs, visc_ref, l_ref, kp_ref, parts_ref, my_ref, own_ref, v3_ref, yd_ref, yu_ref)
    row = lambda i, col: kp_ref[i, pl.ds(col, 1), :]
    sums_d, one_d, misc_d = read_tail(yd_ref, wx, 0)
    sums_u, one_u, misc_u = read_tail(yu_ref, wx, 1)
    edge_high, edge_low = misc_d[wx + 4 : 2 * wx + 4], misc_d[2 * wx + 4 : 3 * wx + 4]
    for n, (flux, top, top_one, low, low_one, face) in enumerate(results):
        for s in range(6):
            c3_ref[n, s] = flux[s]
        face_ref[n] = face
        for p in range(2):
            vt_ref[n, p] = top[p]
            vl_ref[n, p] = low[p]
    flux, top, top_one, low, low_one, face = results[1]
    mine = tall(one_u) + low_one
    v1_ref[0] = mine
    v1_ref[1] = v1a_ref[0]
    for y in range(wy - 2):
        v1_ref[2 + y] = v1b_ref[y]
    v1_ref[wy] = v1a_ref[1] + top_one
    v1_ref[wy + 1] = tall(one_d)

    def plane(i, n, p):
        lines = [sums_u[i] + vl_ref[n, p], va_ref[0, i]]
        lines += [vb_ref[y, i] for y in range(wy - 2)]
        lines += [va_ref[1, i] + vt_ref[n, p], sums_d[i]]
        return merge(lines[1::2], lines[0::2])

    down_ref[pl.ds(0, 48), :] = yu_ref[pl.ds(48 * wx, 48), :]
    for y in range(wy):
        down_ref[pl.ds(48 + 48 * y, 48), :] = l_ref[0, y]
    down_ref[pl.ds(48 * (wy + 1), 48), :] = yd_ref[pl.ds(48 * wx, 48), :]
    diag = diag_ref[pl.ds(0, wy), :]
    high = diag.astype(BF).astype(F32)
    rim = [plane(0, 0, 0), high, edge_high[0:1], diag - high, edge_low[0:1]]
    rim += [misc_u[wx : wx + 1], kp_ref[0, 0:wy], misc_d[wx : wx + 1]]
    put_tail(down_ref, 48 * (wy + 2), rim)
    corner = (wx - 1) * wy
    for y in range(wy):
        part = c_ref[1, corner + y]
        up_ref[pl.ds(48 * y, 48), :] = (part + flux[1] if y == wy - 1 else part).astype(BF)
    last = pl.ds(corner, wy)
    rim = [plane(wx, 1, 1), mine, *one_d]
    rim += [misc_u[wx - 1 : wx], kp_ref[5, last], misc_d[wx + 1 : wx + 2]]
    rim += [misc_u[3 * wx - 1 : 3 * wx], kp_ref[2, last], misc_d[wx + 3 : wx + 4]]
    rim += [kp_ref[1, last], misc_d[wx - 1 : wx]]
    put_tail(up_ref, 48 * wy, rim)
    depart("gx", down_ref, up_ref, inner_ref, outer_ref)


def assemble_kernel(
    wx, wy, visc_ref, l_ref, kp_ref, diag_ref, parts_ref, mx_ref, my_ref, own_ref, c_ref, c3_ref,
    va_ref, vb_ref, v3_ref, vt_ref, vl_ref, face_ref, yd_ref, yu_ref,
    r_ref, late_ref, v_ref, inv_ref, ownx_ref, mid,
):
    z = l_ref.shape[3]
    cells = wx * wy
    xs = tuple(range(1, wx - 1))
    results = after_y(wx, wy, xs, visc_ref, l_ref, kp_ref, parts_ref, my_ref, own_ref, v3_ref, yd_ref, yu_ref)
    for n, part in enumerate(results):
        for s in range(6):
            mid[n, s] = part[0][s]
    traces = [yu_ref[pl.ds(48 * wx, 48), :]] + [l_ref[0, y] for y in range(wy)] + [yd_ref[pl.ds(48 * wx, 48), :]]
    ownx_ref[...] = dot(mx_ref[pl.ds(240, 144), :], wide(traces))

    def contrib(slot, x, y):
        here = c_ref[slot, x * wy + y]
        if y < wy - 1:
            return here
        return here + (mid[x - 1, slot] if 0 < x < wx - 1 else c3_ref[0 if x == 0 else 1, slot])

    for x in range(wx):
        for y in range(wy):
            col = pl.ds(x * wy + y, 48, stride=cells)
            if y:
                behind = contrib(3, x, y - 1)
            elif 0 < x < wx - 1:
                behind = results[x - 1][5]
            else:
                behind = face_ref[0 if x == 0 else 1]
            ahead = contrib(0, x, y) + contrib(1, x - 1, y) if x else contrib(0, x, y)
            sides = [ahead, contrib(2, x, y) + behind, contrib(4, x, y) + z_prev(contrib(5, x, y))]
            for d in range(3):
                if x == wx - 1:
                    late_ref[d, y] = sides[d]
                elif d == 0 and x == 0:
                    late_ref[3, y] = sides[d]
                else:
                    r_ref[d, col, :] = sides[d]
    sums_d, one_d, misc_d = read_tail(yd_ref, wx, 0)
    sums_u, one_u, misc_u = read_tail(yu_ref, wx, 1)
    edge_diag = misc_d[wx + 4 : 2 * wx + 4] + misc_d[2 * wx + 4 : 3 * wx + 4]

    def brought(which, i):
        held = vt_ref if which == 1 else vl_ref
        terms = []
        for x, p in ((i, 0), (i - 1, 1)):
            if x in (0, wx - 1):
                terms.append(held[0 if x == 0 else 1, p])
            elif 0 < x < wx - 1:
                terms.append(results[x - 1][which][p])
        return sum(terms[1:], terms[0])

    for i in range(wx + 1):
        lines = [sums_u[i] + brought(3, i), va_ref[0, i]]
        lines += [vb_ref[y, i] for y in range(wy - 2)]
        lines += [va_ref[1, i] + brought(1, i), sums_d[i]]
        v_ref[i] = merge(lines[1::2], lines[0::2])
        if i < wx:
            parts = [jnp.broadcast_to(diag_ref[pl.ds(i * wy + y, 1), :], (4, z)) for y in range(wy)]
            parts += [jnp.broadcast_to(edge_diag[i : i + 1], (4, z)), jnp.zeros((4, z), F32)]
            inv_ref[i] = reciprocal(tall(parts))


def reciprocal(diag):
    present = diag > 0.0
    return jnp.where(present, (1.0 / gain) / jnp.where(present, diag, 1.0), 0.0)


def final_kernel(
    wx, wy, visc_ref, l_ref, kp_ref, parts_ref, mx_ref, ownx_ref, r_in, late_ref, v_ref, inv_ref, v1_ref,
    yd_ref, yu_ref, outer_in, inner_in, out_hbm, r_ref, held, fix, sems,
):
    here, last = lax.axis_index("gx"), lax.axis_size("gx") - 1

    def from_high(start, size):
        rows = pl.ds(start, size)
        value = jnp.where(even("gx"), inner_in[rows, :], outer_in[rows, :])
        return jnp.where(here < last, value, jnp.zeros_like(value))

    def from_low(start, size):
        rows = pl.ds(start, size)
        value = jnp.where(even("gx"), outer_in[rows, :], inner_in[rows, :])
        return jnp.where(here > 0, value, jnp.zeros_like(value))

    cells, z = wx * wy, l_ref.shape[3]
    rows = v_ref.shape[1]
    row = lambda i, col: kp_ref[i, pl.ds(col, 1), :]
    traces = [from_high(48 * j, 48) for j in range(wy + 2)]
    delta = dot(mx_ref[pl.ds(288, 96), :], wide(traces))
    rim_x = from_high(48 * (wy + 2), tail_rows(rows + 3 * wy + 4)).astype(F32)
    rim_l = from_low(48 * wy, tail_rows(rows + 32 + 3 * (wy + 2) - 1)).astype(F32)
    misc_d = read_tail(yd_ref, wx, 0)[2]
    misc_u = read_tail(yu_ref, wx, 1)[2]
    flags_high = rim_x[rows + 2 * (wy + 1) : rows + 3 * wy + 4]
    corner = (wx - 1) * wy
    arrived = [from_low(48 * y, 48) for y in range(wy)]
    arrived_corners = slot_corners(arrived, parts_ref, 1)
    codes = rim_l[rows + 32 : rows + 32 + wy + 2]
    keep_z = rim_l[rows + 32 + wy + 2 : rows + 32 + 2 * (wy + 2)]
    keep_y = rim_l[rows + 32 + 2 * (wy + 2) : rows + 32 + 3 * (wy + 2) - 1]
    low_visc = level_visc(codes, visc_ref)
    low_keep_z = z_next(keep_z)
    lines = [[], [], []]
    high_scales = []
    del r_in
    for j in range(-1, wy + 1):
        n = j + 1
        part = delta[:, z * n : z * n + z]
        flag = flags_high[n : n + 1]
        if j < 0:
            visc = level_visc(misc_u[wx - 1 : wx], visc_ref)
            kz = misc_u[3 * wx - 1 : 3 * wx]
            keeps = [misc_u[2 * wx - 1 : 2 * wx], flag, None, row(1, corner), kz, z_next(kz)]
        elif j < wy:
            here = corner + j
            visc = row(4, here)
            high_y = row(1, here + 1) if j < wy - 1 else misc_d[wx - 1 : wx]
            keeps = [row(0, here), flag, row(1, here), high_y, row(2, here), row(3, here)]
        else:
            visc = level_visc(misc_d[wx + 1 : wx + 2], visc_ref)
            kz = misc_d[wx + 3 : wx + 4]
            keeps = [misc_d[wx + 2 : wx + 3], flag, misc_d[wx - 1 : wx], None, kz, z_next(kz)]
        scales = [None if keep is None else visc * keep for keep in keeps]
        corners = scaled_corners(part, scales)
        one = v1_ref[n] * flag
        lines[0].append(corners[0])
        lines[1].append(corners[1] + one[0:8] + z_prev(one[8:16]))
        high_scales.append(scales)
        own = ownx_ref[:, pl.ds(z * n, z)]
        visc = low_visc[n : n + 1]
        flag = misc_u[wx : wx + 1] if j < 0 else misc_d[wx : wx + 1] if j == wy else row(0, j)
        scales = [
            None, visc * flag, None if j < 0 else visc * keep_y[j : j + 1],
            None if j == wy else visc * keep_y[j + 1 : j + 2], visc * keep_z[n : n + 1], visc * low_keep_z[n : n + 1],
        ]
        corners = scaled_corners(own[48:144], scales, (1,))[0]
        if 0 <= j < wy:
            one = arrived_corners[j] * flag
            lines[2].append(corners + one[0:8] + z_prev(one[8:16]))
            face = (arrived[j].astype(F32) + visc * (own[0:48] + penalty * l_ref[0, j].astype(F32))) * flag
            r_ref[0, pl.ds(j, 48, stride=cells), :] = late_ref[3, j] + face
        else:
            at = rows + (0 if j < 0 else 16)
            one = rim_l[at : at + 16] * flag
            lines[2].append(corners + one[0:8] + z_prev(one[8:16]))
    low, before, first = [merge(part[1::2], part[0::2]) for part in lines]
    top = v_ref[wx] + before + rim_x[0:rows]
    values = [(v_ref[0] + first + rim_l[0:rows]) * inv_ref[0]]
    values += [v_ref[i] * inv_ref[i] for i in range(1, wx - 1)]
    values += [(v_ref[wx - 1] + low) * inv_ref[wx - 1]]
    diag = rim_x[rows : rows + wy + 1] + rim_x[rows + wy + 1 : rows + 2 * (wy + 1)]
    parts = [jnp.broadcast_to(diag[j : j + 1], (4, z)) for j in range(wy + 1)]
    values += [top * reciprocal(tall(parts + [jnp.zeros((rows - 4 * (wy + 1), z), F32)]))]
    high = [pltpu.roll(value, rows - 4, 0) for value in values]
    for i in range(wx + 1):
        fix[0, pl.ds(4 * wy * i, 4 * wy), :] = values[i][0 : 4 * wy]
        fix[1, pl.ds(4 * wy * i, 4 * wy), :] = high[i][0 : 4 * wy]
    vertex = lambda c, p, q: fix[q, pl.ds(4 * wy * p + c, cells, stride=4), :]
    delta = columns(dot(mx_ref[pl.ds(0, 240), :], wide(traces[1 : wy + 1])), wy)
    behind = dot(mx_ref[pl.ds(96, 48), :], traces[0]) * high_scales[0][3]
    copies = []
    for d in range(3):
        for j in range(wy):
            scales = high_scales[j + 1]
            part = [delta[j][48 * i : 48 * i + 48] for i in range(5)]
            if d == 0:
                flux = part[0] * scales[0]
            elif d == 1:
                flux = part[1] * scales[2] + behind
                behind = part[2] * scales[3]
            else:
                flux = part[3] * scales[4] + z_prev(part[4] * scales[5])
            r_ref[d, pl.ds(corner + j, 48, stride=cells), :] = late_ref[d, j] + flux
        flags = kp_ref[d]
        for c in range(3):
            if d == 0:
                near = [vertex(c, 0, q) * flags for q in range(2)]
                far = [z_next(vertex(c, 0, q)) * flags for q in range(2)]
                corner_values = [[near[0], far[0]], [near[1], far[1]]]
            elif d == 1:
                corner_values = [[vertex(c, p, 0) * flags, z_next(vertex(c, p, 0)) * flags] for p in range(2)]
            else:
                corner_values = [[vertex(c, p, q) * flags for q in range(2)] for p in range(2)]
            lines = [between(corner_values[0][t], corner_values[1][t]) for t in range(2)]
            for a in range(4):
                for b, value in enumerate(between(lines[0][a], lines[1][a])):
                    at = pl.ds(cells * (16 * c + 4 * a + b), cells)
                    held[d, at, :] = (r_ref[d, at, :] + value).astype(BF)
        copies.append(pltpu.make_async_copy(held.at[d], out_hbm.at[d], sems.at[d]))
        copies[d].start()
    for copy in copies:
        copy.wait()


def call(body, args, outs, scratch, flops, hbm=False, aliases=None):
    if hbm:
        args = tuple(pltpu.with_memory_space_constraint(a, pltpu.HBM) for a in args)
    keywords = {}
    if aliases:
        spaces = [pltpu.HBM] + [pltpu.VMEM] * (len(outs) - 1)
        keywords = dict(out_specs=tuple(pl.BlockSpec(memory_space=space) for space in spaces), input_output_aliases=aliases)
    return pl.pallas_call(
        body,
        **keywords,
        in_specs=[pl.BlockSpec(memory_space=pltpu.HBM if hbm else pltpu.VMEM)] * len(args),
        out_shape=outs,
        scratch_shapes=scratch,
        cost_estimate=pl.CostEstimate(flops=flops, bytes_accessed=1000000, transcendentals=0),
        compiler_params=pltpu.CompilerParams(vmem_limit_bytes=16 * 1024 * 1024),
    )(*args)


def local(traces, dirichlet, visc_class, viscosity, coarse_diag, solve_map, flux_map):
    wx, wy, z = traces.shape[2:]
    cells = wx * wy
    rows = 8 * (wy // 2 + 1)
    per_hex = 2 * 384 * 288 * z
    parts, block = jnp.asarray(slot_table()), jnp.asarray(block_table())
    vm = pltpu.VMEM
    bind = lambda body: functools.partial(body, wx, wy)
    y_message = vm((48 * wx + 48 + tail_rows(8 * ((wx + 2) // 2) + 8 + 3 * wx + 4), z), BF)
    x_message = vm((48 * (wy + 2) + tail_rows(rows + 3 * wy + 4), z), BF)

    (lifted, nat, flags, visc, diag, s_turned, f_map, va, v1a, v3, *swaps) = call(
        bind(first_kernel),
        (
            viscosity, traces.reshape(3, 48 * cells, z), dirichlet.reshape(3, cells, z),
            visc_class.reshape(cells, z), coarse_diag.reshape(cells, z), solve_map.T, flux_map, block,
        ),
        (
            vm((4, cells, 48, z), BF), vm((3, 48 * cells, z), F32), vm((6, cells, z), F32), vm((viscosity.shape[0], z), F32), vm((cells, z), F32),
            vm(solve_map.shape[::-1], BF), vm(flux_map.shape, BF),
            vm((2, wx + 1, 8, z), F32), vm((2, 16, z), F32), vm((wx, 32, z), F32),
            y_message, y_message, y_message,
        ),
        [
            y_message, y_message, vm(block.shape, BF),
            vm((3, 48 * cells, z), BF), vm((3, cells, z), jnp.int32), vm((cells, z), jnp.int32),
            pltpu.SMEM(viscosity.shape, F32), pltpu.SemaphoreType.DMA((8,)),
        ],
        wx * per_hex, True,
    )
    swaps = [swap(message, "gy", "gx", k, 3) for k, message in enumerate(swaps)]
    c, vb, v1b, mx, my, own = call(
        bind(middle_kernel),
        (lifted, nat, flags, s_turned, f_map, parts),
        (
            vm((6, cells, 48, z), F32), vm((wy - 2, wx + 1, 8, z), F32), vm((wy - 2, 16, z), F32),
            vm((384, 48), BF), vm((384, 48), BF), vm((144, wx * z), F32),
        ),
        [vm((4, cells, 48, z), BF), vm((384, 288), BF), vm((288, 256), BF)], cells * per_hex,
    )
    c3, vt, vl, v1, face, yd, yu, inner, outer = call(
        bind(turn_kernel),
        (
            visc, lifted, flags, diag, parts, my, own, c, va, vb, v1a, v1b, v3, *swaps,
        ),
        (
            vm((2, 6, 48, z), F32), vm((2, 2, 8, z), F32), vm((2, 2, 8, z), F32), vm((wy + 2, 16, z), F32),
            vm((2, 48, z), F32), y_message, y_message, x_message, x_message,
        ),
        [x_message, x_message], 2 * per_hex,
    )
    inner = swap(inner, "gx", "gy", 0)
    outer = swap(outer, "gx", "gy", 1)
    residual, late, vs, inverse, ownx = call(
        bind(assemble_kernel),
        (
            visc, lifted, flags, diag, parts, mx, my, own, c, c3, va, vb, v3, vt, vl, face, yd, yu,
        ),
        (
            vm((3, 48 * cells, z), F32), vm((4, wy, 48, z), F32), vm((wx + 1, rows, z), F32), vm((wx, rows, z), F32),
            vm((144, (wy + 2) * z), F32),
        ),
        [vm((wx - 2, 6, 48, z), F32)], 4 * per_hex,
    )
    out, _ = call(
        bind(final_kernel),
        (
            visc, lifted, flags, parts, mx, ownx, residual, late, vs, inverse, v1, yd, yu, outer, inner,
        ),
        (jax.ShapeDtypeStruct((3, 48 * cells, z), BF), vm((3, 48 * cells, z), F32)),
        [vm((3, 48 * cells, z), BF), vm((2, 4 * wy * (wx + 1), z), F32), pltpu.SemaphoreType.DMA((3,))], 6 * per_hex,
        aliases={6: 1},
    )
    return out.reshape(traces.shape)


def solution(mesh):
    in_specs = (
        P(None, None, "gx", "gy", None),
        P(None, "gx", "gy", None),
        P("gx", "gy", None),
        P(),
        P("gx", "gy", None),
        P(),
        P(),
    )
    out_specs = P(None, None, "gx", "gy", None)
    return jax.shard_map(local, mesh=mesh, in_specs=in_specs, out_specs=out_specs, check_vma=False)
```

```python
import functools
import math

import jax
import jax.numpy as jnp
import ml_dtypes
import numpy as np
from jax import lax
from jax.experimental import pallas as pl
from jax.experimental.pallas import tpu as pltpu
from jax.sharding import PartitionSpec as P

penalty = 0.5
BF = jnp.bfloat16
F32 = jnp.float32
lift = 1.3264
gain = 1.3280711361297461


def swap(value, axis, other, first, step=2):
    count, width = lax.axis_size(axis), lax.axis_size(other)
    place = (lambda i, j: i * width + j) if (axis, other) == ("gx", "gy") else (lambda i, j: j * count + i)
    lows = list(range(first, count - 1, step))
    pairs = [(place(low, j), place(low + 1, j)) for low in lows for j in range(width)]
    alone = [i for i in range(count) if i not in lows and i - 1 not in lows]
    pairs += [(place(i, j), place(i, j + 1)) for i in alone for j in range(0, width - 1, 2)]
    return lax.ppermute(value, ("gx", "gy"), pairs + [(high, low) for low, high in pairs])


def even(axis):
    return lax.rem(lax.axis_index(axis), 2) == 0


def arrive(messages, down_ref, up_ref):
    here, last = lax.axis_index("gy"), lax.axis_size("gy") - 1
    values = [ref[...] for ref in messages]
    for ref, swap_of, present in ((down_ref, lax.rem(here, 3), here < last), (up_ref, lax.rem(here + 2, 3), here > 0)):
        value = jnp.where(swap_of == 0, values[0], jnp.where(swap_of == 1, values[1], values[2]))
        ref[...] = jnp.where(present, value, jnp.zeros_like(value))


def depart_three(down_ref, up_ref, messages):
    here = lax.rem(lax.axis_index("gy"), 3)
    for k, ref in enumerate(messages):
        choose(here == k, up_ref, down_ref, ref)


def depart(axis, down_ref, up_ref, inner_ref, outer_ref):
    choose(even(axis), up_ref, down_ref, inner_ref)
    choose(even(axis), down_ref, up_ref, outer_ref)


def choose(condition, yes_ref, no_ref, out_ref, present=None):
    value = jnp.where(condition, yes_ref[...], no_ref[...])
    out_ref[...] = value if present is None else jnp.where(present, value, jnp.zeros_like(value))


def corner_table():
    gll_points = [-1.0, -math.sqrt(0.2), math.sqrt(0.2), 1.0]
    table = np.zeros((16, 4), np.float64)
    for s in range(4):
        for t in range(4):
            for p in range(2):
                for q in range(2):
                    table[4 * s + t, 2 * p + q] = (
                        (1 + (2 * p - 1) * gll_points[s]) * (1 + (2 * q - 1) * gll_points[t]) / 4
                    )
    return table


def landing(face_slot, high_s, high_t):
    direction, outward = divmod(face_slot, 2)
    if direction == 0:
        return (outward, high_s, high_t)
    if direction == 1:
        return (high_s, outward, high_t)
    return (high_s, high_t, outward)


def gather_table():
    weights = lift * corner_table()
    table = np.zeros((32, 288), np.float64)
    for slot in range(6):
        for s in range(2):
            for t in range(2):
                p, q, r = landing(slot, s, t)
                for c in range(3):
                    cols = slot * 48 + 16 * c + np.arange(16)
                    table[16 * r + 8 * p + 4 * q + c, cols] += weights[:, 2 * s + t]
    return table.astype(ml_dtypes.bfloat16)


def slot_table():
    slots = np.split(gather_table(), 6, axis=1)
    rows = [
        np.r_[0:8, 16:24], np.r_[8:16, 24:32], np.arange(32), np.arange(32), np.arange(16), np.arange(16, 32),
    ]
    return np.concatenate([slot[kept] for slot, kept in zip(slots, rows)], axis=0)


slot_rows = (0, 16, 32, 64, 96, 112, 128)


def between(low, high):
    step = high - low
    return [low, low + (0.5 - 0.5 * math.sqrt(0.2)) * step, low + (0.5 + 0.5 * math.sqrt(0.2)) * step, high]


def lanes(shape):
    return lax.broadcasted_iota(jnp.int32, shape, len(shape) - 1)


def z_next(value):
    last = value.shape[-1] - 1
    return jnp.where(lanes(value.shape) < last, pltpu.roll(value, last, value.ndim - 1), 0.0)


def z_prev(value):
    return jnp.where(lanes(value.shape) > 0, pltpu.roll(value, 1, value.ndim - 1), 0.0)


def dot(left, right):
    return jnp.dot(left, right, preferred_element_type=F32)


def wide(parts):
    return jnp.concatenate(parts, axis=1)


def tall(parts):
    return jnp.concatenate(parts, axis=0)


def columns(rows, count):
    z = rows.shape[1] // count
    return [rows[:, z * h : z * h + z] for h in range(count)]


def elements(slots):
    return tall([wide([hexa[s] for hexa in slots]) for s in range(6)])


def vertex_part(flux, parts_ref):
    rows = []
    for s in range(6):
        first, size = slot_rows[s], slot_rows[s + 1] - slot_rows[s]
        rows.append(dot(parts_ref[pl.ds(first, size), :], flux[48 * s : 48 * s + 48].astype(BF)))
    rows[2:4] = [rows[2] + rows[3]]
    return tall(rows)


def turned_dot(left, right):
    return lax.dot_general(left, right, (((1,), (1,)), ((), ())), preferred_element_type=F32)


def product(f_ref, st_ref, slot):
    first = 0 if slot is None else 48 * slot
    flux = turned_dot(f_ref[...], st_ref[...] if slot is None else st_ref[pl.ds(first, 48), :])
    rows = lax.broadcasted_iota(jnp.int32, flux.shape, 0)
    return flux, flux + jnp.where(rows == lax.broadcasted_iota(jnp.int32, flux.shape, 1) + first, F32(penalty), F32(0.0))


def slot_corners(traces, parts_ref, slot):
    z = traces[0].shape[1]
    first, size = slot_rows[slot], slot_rows[slot + 1] - slot_rows[slot]
    rows = dot(parts_ref[pl.ds(first, size), :], wide([trace.astype(BF) for trace in traces]))
    return [rows[:, z * h : z * h + z] for h in range(len(traces))]


def settle(rows, p):
    return rows[8 * p : 8 * p + 8] + z_prev(rows[16 + 8 * p : 24 + 8 * p])


def scaled_corners(delta, scales, offsets=(0, 1)):
    shape = (8, delta.shape[1])
    blank = jnp.zeros((1, shape[1]), F32)
    y_scale = jnp.where(
        lax.broadcasted_iota(jnp.int32, shape, 0) < 4,
        blank if scales[2] is None else scales[2], blank if scales[3] is None else scales[3],
    )
    results = []
    for p in offsets:
        parts = []
        for r in range(2):
            at = 32 + 16 * r + 8 * p
            part = delta[at : at + 8] * y_scale + delta[at + 32 : at + 40] * scales[4 + r]
            if scales[p] is not None:
                part = part + delta[16 * p + 8 * r : 16 * p + 8 * r + 8] * scales[p]
            parts.append(part)
        results.append(parts[0] + z_prev(parts[1]))
    return results


def level_visc(code, visc_ref):
    visc = jnp.zeros(code.shape, F32)
    for level in range(visc_ref.shape[0]):
        visc = visc + jnp.where(code == F32(level + 1), visc_ref[pl.ds(level, 1), :], F32(0.0))
    return visc


def merge(even, odd):
    odd = tall(odd)
    return tall(even) + pltpu.roll(odd, odd.shape[0] - 4, 0)


def first_kernel(
    wx, wy, visc_hbm, t_hbm, dir_hbm, cls_hbm, diag_hbm, st_hbm, f_hbm, parts_hbm,
    l_ref, nat, kp_ref, visc_ref, diag_ref, st_ref, f_ref, parts_ref, v_ref, v1_ref, v3_ref,
    swap0_ref, swap1_ref, swap2_ref, down_ref, up_ref, t_ref, dir_ref, cls_ref, levels, sems,
):
    cells = wx * wy
    pairs = [
        (parts_hbm, parts_ref), (f_hbm, f_ref), (st_hbm, st_ref), (t_hbm, t_ref), (dir_hbm, dir_ref),
        (cls_hbm, cls_ref), (visc_hbm, levels), (diag_hbm, diag_ref),
    ]
    copies = [pltpu.make_async_copy(a, b, sems.at[i]) for i, (a, b) in enumerate(pairs)]
    for copy in copies:
        copy.start()
    diagonal = lax.broadcasted_iota(jnp.int32, (288, 288), 0) == lax.broadcasted_iota(jnp.int32, (288, 288), 1)
    diagonal = jnp.where(diagonal, F32(penalty), F32(0.0))
    copies[0].wait()
    own = tall([vertex_part(diagonal, parts_ref), diagonal[144:192]])
    copies[1].wait()
    left = tall([vertex_part(f_ref[...], parts_ref).astype(BF), f_ref[pl.ds(144, 48), :]])
    for copy in copies[2:5]:
        copy.wait()
    short = (turned_dot(left, st_ref[...]) + own).astype(BF)
    z = t_ref.shape[2]
    for d in range(3):
        kp_ref[d] = (1 - dir_ref[d]).astype(F32)
        nat[d] = t_ref[d].astype(F32)
        lay_out(wx, wy, d, nat, kp_ref, l_ref, True)
    kp_ref[3] = z_next(kp_ref[2])
    for copy in copies[5:]:
        copy.wait()
    for level in range(visc_ref.shape[0]):
        visc_ref[pl.ds(level, 1), :] = jnp.full((1, z), levels[level], F32)
    code = cls_ref[...].astype(F32) + 1.0
    kp_ref[4] = level_visc(code, visc_ref)
    kp_ref[5] = code
    row = lambda i, col: kp_ref[i, pl.ds(col, 1), :]
    corners = []
    for side, y in enumerate((0, wy - 1)):
        where = [(x, y) for x in range(wx)]
        slots, scales, left_out = known_hexes(wx, wy, where, (l_ref, None), kp_ref)
        rows = columns(dot(short if side else short[0:96], elements(slots)), wx)
        corners += known_corners(rows, scales, left_out)
        v1_ref[side] = rows[wx - 1][16:32] * row(4, (wx - 1) * wy + y)
    place = lax.broadcasted_iota(jnp.int32, (32, z), 0)
    lone = [part * row(4, x * wy + wy - 1) for x, part in enumerate(rows)]
    for x in range(wx):
        v3_ref[x] = jnp.where(lax.rem(place, 8) < 4, 0.0, lone[x][32:64])
    sums = [line_sums(corners[:wx]), line_sums(corners[wx:])]
    for side in range(2):
        for i in range(wx + 1):
            v_ref[side, i] = sums[side][i]
    corner = (wx - 1) * wy
    top = wy - 1
    for x in range(wx):
        down_ref[pl.ds(48 * x, 48), :] = l_ref[1, x * wy]
        up_ref[pl.ds(48 * x, 48), :] = lone[x][96:144].astype(BF)
    down_ref[pl.ds(48 * wx, 48), :] = l_ref[0, 0]
    up_ref[pl.ds(48 * wx, 48), :] = l_ref[0, top]
    flags = [row(1, x * wy) for x in range(wx)] + [row(0, 0), row(5, corner), row(0, corner), row(2, corner)]
    diag = tall([diag_ref[pl.ds(x * wy, 1), :] for x in range(wx)])
    high = diag.astype(BF).astype(F32)
    rim = pack(sums[0], 0) + pack([v1_ref[0, 0:8], v1_ref[0, 8:16]], 0) + flags + [high, diag - high]
    put_tail(down_ref, 48 * wx + 48, rim)
    flags = [row(kind, x * wy + top) for kind in (5, 0, 2) for x in range(wx)]
    rim = pack(sums[1], 1) + pack([v1_ref[1, 0:8], v1_ref[1, 8:16]], 1) + flags
    put_tail(up_ref, 48 * wx + 48, rim)
    depart_three(down_ref, up_ref, (swap0_ref, swap1_ref, swap2_ref))


def tail_rows(count):
    return -(-count // 16) * 16


def put_tail(ref, start, rows):
    count = sum(part.shape[0] for part in rows)
    full = ref.shape[0] - start
    if full > count:
        rows = rows + [jnp.zeros((full - count, rows[0].shape[1]), F32)]
    ref[pl.ds(start, full), :] = tall(rows).astype(BF)


def pack(parts, half):
    place = lax.broadcasted_iota(jnp.int32, parts[0].shape, 0)
    parts = parts + [jnp.zeros_like(parts[0])] * (len(parts) % 2)
    packed = []
    for low, high in zip(parts[0::2], parts[1::2]):
        if half:
            low = pltpu.roll(low, 4, 0)
        else:
            high = pltpu.roll(high, 4, 0)
        packed.append(jnp.where(place < 4, low, high))
    return packed


def unpack(packed, count, half):
    parts = []
    for n in range(count):
        part = packed[8 * (n // 2) : 8 * (n // 2) + 8]
        parts.append(part if n % 2 == half else pltpu.roll(part, 4, 0))
    return parts


def read_tail(ref, wx, half):
    start = 48 * wx + 48
    rows = ref[pl.ds(start, ref.shape[0] - start), :].astype(F32)
    size = 8 * ((wx + 2) // 2)
    return unpack(rows, wx + 1, half), unpack(rows[size : size + 8], 2, half), rows[size + 8 :]


def line_sums(corners):
    low, high = [part[0] for part in corners], [part[1] for part in corners]
    return [low[0]] + [low[x] + high[x - 1] for x in range(1, len(low))] + [high[-1]]


def early(wx, wy, d, x, y):
    return y in (0, wy - 1) or (d == 0 and x == 0) or (d == 1 and y == 1)


def lay_out(wx, wy, d, nat, kp_ref, l_ref, first):
    for x in range(wx):
        for y in range(wy):
            if early(wx, wy, d, x, y) == first:
                col = x * wy + y
                part = nat[d, pl.ds(col, 48, stride=wx * wy), :] * kp_ref[d, pl.ds(col, 1), :]
                l_ref[d, col] = part.astype(BF)
                if d == 2:
                    l_ref[3, col] = z_next(part).astype(BF)


def known_hexes(wx, wy, where, l_refs, kp_ref):
    z = l_refs[0].shape[3]
    nothing = jnp.zeros((48, z), BF)
    row = lambda i, col: kp_ref[i, pl.ds(col, 1), :]
    trace = lambda d, x, y: l_refs[0 if early(wx, wy, min(d, 2), x, y) else 1][d, x * wy + y]
    slots, scales, left_out = [], [], []
    for x, y in where:
        here = x * wy + y
        visc = row(4, here)
        last_x, last_y = x == wx - 1, y == wy - 1
        slots.append(
            [
                trace(0, x, y), nothing if last_x else trace(0, x + 1, y),
                trace(1, x, y), nothing if last_y else trace(1, x, y + 1),
                trace(2, x, y), trace(3, x, y),
            ]
        )
        scales.append(
            [
                visc * row(0, here), visc if last_x else visc * row(0, here + wy),
                visc * row(1, here), visc if last_y else visc * row(1, here + 1),
                visc * row(2, here), visc * row(3, here),
            ]
        )
        left_out.append(([1] if last_x else []) + ([3] if last_y else []))
    return slots, scales, left_out


def known_corners(vertex, scales, left_out):
    return [
        scaled_corners(part, [None if s in out else scale[s] for s in range(6)])
        for part, scale, out in zip(vertex, scales, left_out)
    ]


def middle_kernel(
    wx, wy, l_ref, nat, kp_ref, st_ref, f_ref, parts_ref,
    c_ref, v_ref, v1_ref, mx_ref, my_ref, own_ref, rest_ref, m_ref, lost_ref,
):
    for slot, ref in ((1, mx_ref), (3, my_ref)):
        bare, flux = product(f_ref, st_ref, slot)
        turned = tall([bare[0:48], bare[96:288], bare[48:96]]) if slot == 1 else bare
        ref[pl.ds(0, 288), :] = turned.astype(BF)
        ref[pl.ds(288, 96), :] = vertex_part(flux, parts_ref).astype(BF)
    flux = product(f_ref, st_ref, None)[1]
    m_ref[pl.ds(0, 288), :] = flux.astype(BF)
    m_ref[pl.ds(288, 96), :] = vertex_part(flux, parts_ref).astype(BF)
    lost_ref[...] = (flux - flux.astype(BF).astype(F32))[:, 0:256].astype(BF)
    for d in range(3):
        lay_out(wx, wy, d, nat, kp_ref, rest_ref, False)
    own_ref[...] = dot(
        tall([my_ref[pl.ds(144, 48), :], my_ref[pl.ds(288, 96), :]]), wide([l_ref[1, x * wy] for x in range(wx)])
    )
    for y in range(wy):
        inside = 0 < y < wy - 1
        where = [(x, y) for x in range(wx)]
        slots, scales, left_out = known_hexes(wx, wy, where, (l_ref, rest_ref), kp_ref)
        element = elements(slots)
        rows = dot(m_ref[...] if inside else m_ref[pl.ds(0, 288), :], element)
        lost = columns(dot(lost_ref[...], element[0:256]), wx)
        rows = columns(rows, wx)
        for x in range(wx):
            for s in range(6):
                part = slice(48 * s, 48 * s + 48)
                c_ref[s, x * wy + y] = (rows[x][part] + lost[x][part]) * scales[x][s]
        if inside:
            corners = known_corners([part[288:] for part in rows], scales, left_out)
            v1_ref[y - 1] = rows[wx - 1][304:320] * kp_ref[4, pl.ds((wx - 1) * wy + y, 1), :]
            for i, part in enumerate(line_sums(corners)):
                v_ref[y - 1, i] = part


def after_y(wx, wy, xs, visc_ref, l_ref, kp_ref, parts_ref, my_ref, own_ref, v3_ref, down_ref, up_ref):
    z = l_ref.shape[3]
    misc_d = read_tail(down_ref, wx, 0)[2]
    misc_u = read_tail(up_ref, wx, 1)[2]
    row = lambda i, col: kp_ref[i, pl.ds(col, 1), :]
    delta = dot(my_ref[...], wide([down_ref[pl.ds(48 * x, 48), :] for x in xs]))
    arrived = [up_ref[pl.ds(48 * x, 48), :].astype(F32) for x in xs]
    arrived_corners = slot_corners(arrived, parts_ref, 3)
    results = []
    for n, x in enumerate(xs):
        here = x * wy + wy - 1
        last = x == wx - 1
        part = delta[:, z * n : z * n + z]
        visc = row(4, here)
        scales = [
            visc * row(0, here), visc if last else visc * row(0, here + wy), visc * row(1, here),
            visc * misc_d[x : x + 1], visc * row(2, here), visc * row(3, here),
        ]
        flux = [part[48 * s : 48 * s + 48] * scales[s] for s in range(6)]
        used = [None if (s == 1 and last) else scales[s] for s in range(6)]
        known = v3_ref[x] * misc_d[x : x + 1]
        top = [rows + settle(known, p) for p, rows in enumerate(scaled_corners(part[288:384], used))]
        top_one = part[304:320] * visc
        here = x * wy
        visc = level_visc(misc_u[x : x + 1], visc_ref)
        flag = row(1, here)
        own = own_ref[:, pl.ds(z * x, z)]
        keep_z = misc_u[2 * wx + x : 2 * wx + x + 1]
        scales = [
            visc * misc_u[wx + x : wx + x + 1], None if last else visc * misc_u[wx + x + 1 : wx + x + 2],
            None, visc * flag, visc * keep_z, visc * z_next(keep_z),
        ]
        known = arrived_corners[n] * flag
        low = [rows + settle(known, p) for p, rows in enumerate(scaled_corners(own[48:144], scales))]
        low_one = own[64:80] * visc
        face = (arrived[n] + visc * (own[0:48] + penalty * l_ref[1, here].astype(F32))) * flag
        results.append((flux, top, top_one, low, low_one, face))
    return results


def turn_kernel(
    wx, wy, visc_ref, l_ref, kp_ref, diag_ref, parts_ref, my_ref, own_ref, c_ref, va_ref, vb_ref,
    v1a_ref, v1b_ref, v3_ref, swap0_in, swap1_in, swap2_in,
    c3_ref, vt_ref, vl_ref, v1_ref, face_ref, yd_ref, yu_ref, inner_ref, outer_ref, down_ref, up_ref,
):
    z = l_ref.shape[3]
    arrive((swap0_in, swap1_in, swap2_in), yd_ref, yu_ref)
    xs = (0, wx - 1)
    results = after_y(wx, wy, xs, visc_ref, l_ref, kp_ref, parts_ref, my_ref, own_ref, v3_ref, yd_ref, yu_ref)
    row = lambda i, col: kp_ref[i, pl.ds(col, 1), :]
    sums_d, one_d, misc_d = read_tail(yd_ref, wx, 0)
    sums_u, one_u, misc_u = read_tail(yu_ref, wx, 1)
    edge_high, edge_low = misc_d[wx + 4 : 2 * wx + 4], misc_d[2 * wx + 4 : 3 * wx + 4]
    for n, (flux, top, top_one, low, low_one, face) in enumerate(results):
        for s in range(6):
            c3_ref[n, s] = flux[s]
        face_ref[n] = face
        for p in range(2):
            vt_ref[n, p] = top[p]
            vl_ref[n, p] = low[p]
    flux, top, top_one, low, low_one, face = results[1]
    mine = tall(one_u) + low_one
    v1_ref[0] = mine
    v1_ref[1] = v1a_ref[0]
    for y in range(wy - 2):
        v1_ref[2 + y] = v1b_ref[y]
    v1_ref[wy] = v1a_ref[1] + top_one
    v1_ref[wy + 1] = tall(one_d)

    def plane(i, n, p):
        lines = [sums_u[i] + vl_ref[n, p], va_ref[0, i]]
        lines += [vb_ref[y, i] for y in range(wy - 2)]
        lines += [va_ref[1, i] + vt_ref[n, p], sums_d[i]]
        return merge(lines[1::2], lines[0::2])

    down_ref[pl.ds(0, 48), :] = yu_ref[pl.ds(48 * wx, 48), :]
    for y in range(wy):
        down_ref[pl.ds(48 + 48 * y, 48), :] = l_ref[0, y]
    down_ref[pl.ds(48 * (wy + 1), 48), :] = yd_ref[pl.ds(48 * wx, 48), :]
    diag = diag_ref[pl.ds(0, wy), :]
    high = diag.astype(BF).astype(F32)
    rim = [plane(0, 0, 0), high, edge_high[0:1], diag - high, edge_low[0:1]]
    rim += [misc_u[wx : wx + 1], kp_ref[0, 0:wy], misc_d[wx : wx + 1]]
    put_tail(down_ref, 48 * (wy + 2), rim)
    corner = (wx - 1) * wy
    for y in range(wy):
        part = c_ref[1, corner + y]
        up_ref[pl.ds(48 * y, 48), :] = (part + flux[1] if y == wy - 1 else part).astype(BF)
    last = pl.ds(corner, wy)
    rim = [plane(wx, 1, 1), mine, *one_d]
    rim += [misc_u[wx - 1 : wx], kp_ref[5, last], misc_d[wx + 1 : wx + 2]]
    rim += [misc_u[3 * wx - 1 : 3 * wx], kp_ref[2, last], misc_d[wx + 3 : wx + 4]]
    rim += [kp_ref[1, last], misc_d[wx - 1 : wx]]
    put_tail(up_ref, 48 * wy, rim)
    depart("gx", down_ref, up_ref, inner_ref, outer_ref)


def assemble_kernel(
    wx, wy, visc_ref, l_ref, kp_ref, diag_ref, parts_ref, mx_ref, my_ref, own_ref, c_ref, c3_ref,
    va_ref, vb_ref, v3_ref, vt_ref, vl_ref, face_ref, yd_ref, yu_ref,
    r_ref, late_ref, v_ref, inv_ref, ownx_ref, mid,
):
    z = l_ref.shape[3]
    cells = wx * wy
    xs = tuple(range(1, wx - 1))
    results = after_y(wx, wy, xs, visc_ref, l_ref, kp_ref, parts_ref, my_ref, own_ref, v3_ref, yd_ref, yu_ref)
    for n, part in enumerate(results):
        for s in range(6):
            mid[n, s] = part[0][s]
    traces = [yu_ref[pl.ds(48 * wx, 48), :]] + [l_ref[0, y] for y in range(wy)] + [yd_ref[pl.ds(48 * wx, 48), :]]
    ownx_ref[...] = dot(mx_ref[pl.ds(240, 144), :], wide(traces))

    def contrib(slot, x, y):
        here = c_ref[slot, x * wy + y]
        if y < wy - 1:
            return here
        return here + (mid[x - 1, slot] if 0 < x < wx - 1 else c3_ref[0 if x == 0 else 1, slot])

    for x in range(wx):
        for y in range(wy):
            col = pl.ds(x * wy + y, 48, stride=cells)
            if y:
                behind = contrib(3, x, y - 1)
            elif 0 < x < wx - 1:
                behind = results[x - 1][5]
            else:
                behind = face_ref[0 if x == 0 else 1]
            ahead = contrib(0, x, y) + contrib(1, x - 1, y) if x else contrib(0, x, y)
            sides = [ahead, contrib(2, x, y) + behind, contrib(4, x, y) + z_prev(contrib(5, x, y))]
            for d in range(3):
                if x == wx - 1:
                    late_ref[d, y] = sides[d]
                elif d == 0 and x == 0:
                    late_ref[3, y] = sides[d]
                else:
                    r_ref[d, col, :] = sides[d]
    sums_d, one_d, misc_d = read_tail(yd_ref, wx, 0)
    sums_u, one_u, misc_u = read_tail(yu_ref, wx, 1)
    edge_diag = misc_d[wx + 4 : 2 * wx + 4] + misc_d[2 * wx + 4 : 3 * wx + 4]

    def brought(which, i):
        held = vt_ref if which == 1 else vl_ref
        terms = []
        for x, p in ((i, 0), (i - 1, 1)):
            if x in (0, wx - 1):
                terms.append(held[0 if x == 0 else 1, p])
            elif 0 < x < wx - 1:
                terms.append(results[x - 1][which][p])
        return sum(terms[1:], terms[0])

    for i in range(wx + 1):
        lines = [sums_u[i] + brought(3, i), va_ref[0, i]]
        lines += [vb_ref[y, i] for y in range(wy - 2)]
        lines += [va_ref[1, i] + brought(1, i), sums_d[i]]
        v_ref[i] = merge(lines[1::2], lines[0::2])
        if i < wx:
            parts = [jnp.broadcast_to(diag_ref[pl.ds(i * wy + y, 1), :], (4, z)) for y in range(wy)]
            parts += [jnp.broadcast_to(edge_diag[i : i + 1], (4, z)), jnp.zeros((4, z), F32)]
            inv_ref[i] = reciprocal(tall(parts))


def reciprocal(diag):
    present = diag > 0.0
    return jnp.where(present, (1.0 / gain) / jnp.where(present, diag, 1.0), 0.0)


def final_kernel(
    wx, wy, visc_ref, l_ref, kp_ref, parts_ref, mx_ref, ownx_ref, r_in, late_ref, v_ref, inv_ref, v1_ref,
    yd_ref, yu_ref, outer_in, inner_in, out_hbm, r_ref, held, fix, sems,
):
    here, last = lax.axis_index("gx"), lax.axis_size("gx") - 1

    def from_high(start, size):
        rows = pl.ds(start, size)
        value = jnp.where(even("gx"), inner_in[rows, :], outer_in[rows, :])
        return jnp.where(here < last, value, jnp.zeros_like(value))

    def from_low(start, size):
        rows = pl.ds(start, size)
        value = jnp.where(even("gx"), outer_in[rows, :], inner_in[rows, :])
        return jnp.where(here > 0, value, jnp.zeros_like(value))

    cells, z = wx * wy, l_ref.shape[3]
    rows = v_ref.shape[1]
    row = lambda i, col: kp_ref[i, pl.ds(col, 1), :]
    traces = [from_high(48 * j, 48) for j in range(wy + 2)]
    delta = dot(mx_ref[pl.ds(288, 96), :], wide(traces))
    rim_x = from_high(48 * (wy + 2), tail_rows(rows + 3 * wy + 4)).astype(F32)
    rim_l = from_low(48 * wy, tail_rows(rows + 32 + 3 * (wy + 2) - 1)).astype(F32)
    misc_d = read_tail(yd_ref, wx, 0)[2]
    misc_u = read_tail(yu_ref, wx, 1)[2]
    flags_high = rim_x[rows + 2 * (wy + 1) : rows + 3 * wy + 4]
    corner = (wx - 1) * wy
    arrived = [from_low(48 * y, 48) for y in range(wy)]
    arrived_corners = slot_corners(arrived, parts_ref, 1)
    codes = rim_l[rows + 32 : rows + 32 + wy + 2]
    keep_z = rim_l[rows + 32 + wy + 2 : rows + 32 + 2 * (wy + 2)]
    keep_y = rim_l[rows + 32 + 2 * (wy + 2) : rows + 32 + 3 * (wy + 2) - 1]
    low_visc = level_visc(codes, visc_ref)
    low_keep_z = z_next(keep_z)
    lines = [[], [], []]
    high_scales = []
    del r_in
    for j in range(-1, wy + 1):
        n = j + 1
        part = delta[:, z * n : z * n + z]
        flag = flags_high[n : n + 1]
        if j < 0:
            visc = level_visc(misc_u[wx - 1 : wx], visc_ref)
            kz = misc_u[3 * wx - 1 : 3 * wx]
            keeps = [misc_u[2 * wx - 1 : 2 * wx], flag, None, row(1, corner), kz, z_next(kz)]
        elif j < wy:
            here = corner + j
            visc = row(4, here)
            high_y = row(1, here + 1) if j < wy - 1 else misc_d[wx - 1 : wx]
            keeps = [row(0, here), flag, row(1, here), high_y, row(2, here), row(3, here)]
        else:
            visc = level_visc(misc_d[wx + 1 : wx + 2], visc_ref)
            kz = misc_d[wx + 3 : wx + 4]
            keeps = [misc_d[wx + 2 : wx + 3], flag, misc_d[wx - 1 : wx], None, kz, z_next(kz)]
        scales = [None if keep is None else visc * keep for keep in keeps]
        corners = scaled_corners(part, scales)
        one = v1_ref[n] * flag
        lines[0].append(corners[0])
        lines[1].append(corners[1] + one[0:8] + z_prev(one[8:16]))
        high_scales.append(scales)
        own = ownx_ref[:, pl.ds(z * n, z)]
        visc = low_visc[n : n + 1]
        flag = misc_u[wx : wx + 1] if j < 0 else misc_d[wx : wx + 1] if j == wy else row(0, j)
        scales = [
            None, visc * flag, None if j < 0 else visc * keep_y[j : j + 1],
            None if j == wy else visc * keep_y[j + 1 : j + 2], visc * keep_z[n : n + 1], visc * low_keep_z[n : n + 1],
        ]
        corners = scaled_corners(own[48:144], scales, (1,))[0]
        if 0 <= j < wy:
            one = arrived_corners[j] * flag
            lines[2].append(corners + one[0:8] + z_prev(one[8:16]))
            face = (arrived[j].astype(F32) + visc * (own[0:48] + penalty * l_ref[0, j].astype(F32))) * flag
            r_ref[0, pl.ds(j, 48, stride=cells), :] = late_ref[3, j] + face
        else:
            at = rows + (0 if j < 0 else 16)
            one = rim_l[at : at + 16] * flag
            lines[2].append(corners + one[0:8] + z_prev(one[8:16]))
    low, before, first = [merge(part[1::2], part[0::2]) for part in lines]
    top = v_ref[wx] + before + rim_x[0:rows]
    values = [(v_ref[0] + first + rim_l[0:rows]) * inv_ref[0]]
    values += [v_ref[i] * inv_ref[i] for i in range(1, wx - 1)]
    values += [(v_ref[wx - 1] + low) * inv_ref[wx - 1]]
    diag = rim_x[rows : rows + wy + 1] + rim_x[rows + wy + 1 : rows + 2 * (wy + 1)]
    parts = [jnp.broadcast_to(diag[j : j + 1], (4, z)) for j in range(wy + 1)]
    values += [top * reciprocal(tall(parts + [jnp.zeros((rows - 4 * (wy + 1), z), F32)]))]
    high = [pltpu.roll(value, rows - 4, 0) for value in values]
    for i in range(wx + 1):
        fix[0, pl.ds(4 * wy * i, 4 * wy), :] = values[i][0 : 4 * wy]
        fix[1, pl.ds(4 * wy * i, 4 * wy), :] = high[i][0 : 4 * wy]
    vertex = lambda c, p, q: fix[q, pl.ds(4 * wy * p + c, cells, stride=4), :]
    delta = columns(dot(mx_ref[pl.ds(0, 240), :], wide(traces[1 : wy + 1])), wy)
    behind = dot(mx_ref[pl.ds(96, 48), :], traces[0]) * high_scales[0][3]
    copies = []
    for d in range(3):
        for j in range(wy):
            scales = high_scales[j + 1]
            part = [delta[j][48 * i : 48 * i + 48] for i in range(5)]
            if d == 0:
                flux = part[0] * scales[0]
            elif d == 1:
                flux = part[1] * scales[2] + behind
                behind = part[2] * scales[3]
            else:
                flux = part[3] * scales[4] + z_prev(part[4] * scales[5])
            r_ref[d, pl.ds(corner + j, 48, stride=cells), :] = late_ref[d, j] + flux
        flags = kp_ref[d]
        for c in range(3):
            if d == 0:
                near = [vertex(c, 0, q) * flags for q in range(2)]
                far = [z_next(vertex(c, 0, q)) * flags for q in range(2)]
                corner_values = [[near[0], far[0]], [near[1], far[1]]]
            elif d == 1:
                corner_values = [[vertex(c, p, 0) * flags, z_next(vertex(c, p, 0)) * flags] for p in range(2)]
            else:
                corner_values = [[vertex(c, p, q) * flags for q in range(2)] for p in range(2)]
            lines = [between(corner_values[0][t], corner_values[1][t]) for t in range(2)]
            for a in range(4):
                for b, value in enumerate(between(lines[0][a], lines[1][a])):
                    at = pl.ds(cells * (16 * c + 4 * a + b), cells)
                    held[d, at, :] = (r_ref[d, at, :] + value).astype(BF)
        copies.append(pltpu.make_async_copy(held.at[d], out_hbm.at[d], sems.at[d]))
        copies[d].start()
    for copy in copies:
        copy.wait()


def call(body, args, outs, scratch, flops, hbm=False, aliases=None):
    if hbm:
        args = tuple(pltpu.with_memory_space_constraint(a, pltpu.HBM) for a in args)
    keywords = {}
    if aliases:
        spaces = [pltpu.HBM] + [pltpu.VMEM] * (len(outs) - 1)
        keywords = dict(out_specs=tuple(pl.BlockSpec(memory_space=space) for space in spaces), input_output_aliases=aliases)
    return pl.pallas_call(
        body,
        **keywords,
        in_specs=[pl.BlockSpec(memory_space=pltpu.HBM if hbm else pltpu.VMEM)] * len(args),
        out_shape=outs,
        scratch_shapes=scratch,
        cost_estimate=pl.CostEstimate(flops=flops, bytes_accessed=1000000, transcendentals=0),
        compiler_params=pltpu.CompilerParams(vmem_limit_bytes=16 * 1024 * 1024),
    )(*args)


def local(traces, dirichlet, visc_class, viscosity, coarse_diag, solve_map, flux_map):
    wx, wy, z = traces.shape[2:]
    cells = wx * wy
    rows = 8 * (wy // 2 + 1)
    per_hex = 2 * 384 * 288 * z
    parts = jnp.asarray(slot_table())
    vm = pltpu.VMEM
    bind = lambda body: functools.partial(body, wx, wy)
    y_message = vm((48 * wx + 48 + tail_rows(8 * ((wx + 2) // 2) + 8 + 3 * wx + 4), z), BF)
    x_message = vm((48 * (wy + 2) + tail_rows(rows + 3 * wy + 4), z), BF)

    (lifted, nat, flags, visc, diag, s_turned, f_map, parts, va, v1a, v3, *swaps) = call(
        bind(first_kernel),
        (
            viscosity, traces.reshape(3, 48 * cells, z), dirichlet.reshape(3, cells, z),
            visc_class.reshape(cells, z), coarse_diag.reshape(cells, z), solve_map.T, flux_map, parts,
        ),
        (
            vm((4, cells, 48, z), BF), vm((3, 48 * cells, z), F32), vm((6, cells, z), F32), vm((viscosity.shape[0], z), F32), vm((cells, z), F32),
            vm(solve_map.shape[::-1], BF), vm(flux_map.shape, BF), vm(parts.shape, BF),
            vm((2, wx + 1, 8, z), F32), vm((2, 16, z), F32), vm((wx, 32, z), F32),
            y_message, y_message, y_message,
        ),
        [
            y_message, y_message,
            vm((3, 48 * cells, z), BF), vm((3, cells, z), jnp.int32), vm((cells, z), jnp.int32),
            pltpu.SMEM(viscosity.shape, F32), pltpu.SemaphoreType.DMA((8,)),
        ],
        wx * per_hex, True,
    )
    swaps = [swap(message, "gy", "gx", k, 3) for k, message in enumerate(swaps)]
    c, vb, v1b, mx, my, own = call(
        bind(middle_kernel),
        (lifted, nat, flags, s_turned, f_map, parts),
        (
            vm((6, cells, 48, z), F32), vm((wy - 2, wx + 1, 8, z), F32), vm((wy - 2, 16, z), F32),
            vm((384, 48), BF), vm((384, 48), BF), vm((144, wx * z), F32),
        ),
        [vm((4, cells, 48, z), BF), vm((384, 288), BF), vm((288, 256), BF)], cells * per_hex,
    )
    c3, vt, vl, v1, face, yd, yu, inner, outer = call(
        bind(turn_kernel),
        (
            visc, lifted, flags, diag, parts, my, own, c, va, vb, v1a, v1b, v3, *swaps,
        ),
        (
            vm((2, 6, 48, z), F32), vm((2, 2, 8, z), F32), vm((2, 2, 8, z), F32), vm((wy + 2, 16, z), F32),
            vm((2, 48, z), F32), y_message, y_message, x_message, x_message,
        ),
        [x_message, x_message], 2 * per_hex,
    )
    inner = swap(inner, "gx", "gy", 0)
    outer = swap(outer, "gx", "gy", 1)
    residual, late, vs, inverse, ownx = call(
        bind(assemble_kernel),
        (
            visc, lifted, flags, diag, parts, mx, my, own, c, c3, va, vb, v3, vt, vl, face, yd, yu,
        ),
        (
            vm((3, 48 * cells, z), F32), vm((4, wy, 48, z), F32), vm((wx + 1, rows, z), F32), vm((wx, rows, z), F32),
            vm((144, (wy + 2) * z), F32),
        ),
        [vm((wx - 2, 6, 48, z), F32)], 4 * per_hex,
    )
    out, _ = call(
        bind(final_kernel),
        (
            visc, lifted, flags, parts, mx, ownx, residual, late, vs, inverse, v1, yd, yu, outer, inner,
        ),
        (jax.ShapeDtypeStruct((3, 48 * cells, z), BF), vm((3, 48 * cells, z), F32)),
        [vm((3, 48 * cells, z), BF), vm((2, 4 * wy * (wx + 1), z), F32), pltpu.SemaphoreType.DMA((3,))], 6 * per_hex,
        aliases={6: 1},
    )
    return out.reshape(traces.shape)


def solution(mesh):
    in_specs = (
        P(None, None, "gx", "gy", None),
        P(None, "gx", "gy", None),
        P("gx", "gy", None),
        P(),
        P("gx", "gy", None),
        P(),
        P(),
    )
    out_specs = P(None, None, "gx", "gy", None)
    return jax.shard_map(local, mesh=mesh, in_specs=in_specs, out_specs=out_specs, check_vma=False)
```

```python
import functools
import math

import jax
import jax.numpy as jnp
import ml_dtypes
import numpy as np
from jax import lax
from jax.experimental import pallas as pl
from jax.experimental.pallas import tpu as pltpu
from jax.sharding import PartitionSpec as P

penalty = 0.5
BF = jnp.bfloat16
F32 = jnp.float32
lift = 1.3264
gain = 1.3280711361297461


def swap(value, axis, other, first, step=2):
    count, width = lax.axis_size(axis), lax.axis_size(other)
    place = (lambda i, j: i * width + j) if (axis, other) == ("gx", "gy") else (lambda i, j: j * count + i)
    lows = list(range(first, count - 1, step))
    pairs = [(place(low, j), place(low + 1, j)) for low in lows for j in range(width)]
    alone = [i for i in range(count) if i not in lows and i - 1 not in lows]
    pairs += [(place(i, j), place(i, j + 1)) for i in alone for j in range(0, width - 1, 2)]
    return lax.ppermute(value, ("gx", "gy"), pairs + [(high, low) for low, high in pairs])


def even(axis):
    return lax.rem(lax.axis_index(axis), 2) == 0


def arrive(messages, down_ref, up_ref):
    here, last = lax.axis_index("gy"), lax.axis_size("gy") - 1
    values = [ref[...] for ref in messages]
    for ref, swap_of, present in ((down_ref, lax.rem(here, 3), here < last), (up_ref, lax.rem(here + 2, 3), here > 0)):
        value = jnp.where(swap_of == 0, values[0], jnp.where(swap_of == 1, values[1], values[2]))
        ref[...] = jnp.where(present, value, jnp.zeros_like(value))


def depart_three(down_ref, up_ref, messages):
    here = lax.rem(lax.axis_index("gy"), 3)
    for k, ref in enumerate(messages):
        choose(here == k, up_ref, down_ref, ref)


def depart(axis, down_ref, up_ref, inner_ref, outer_ref):
    choose(even(axis), up_ref, down_ref, inner_ref)
    choose(even(axis), down_ref, up_ref, outer_ref)


def choose(condition, yes_ref, no_ref, out_ref, present=None):
    value = jnp.where(condition, yes_ref[...], no_ref[...])
    out_ref[...] = value if present is None else jnp.where(present, value, jnp.zeros_like(value))


def corner_table():
    gll_points = [-1.0, -math.sqrt(0.2), math.sqrt(0.2), 1.0]
    table = np.zeros((16, 4), np.float64)
    for s in range(4):
        for t in range(4):
            for p in range(2):
                for q in range(2):
                    table[4 * s + t, 2 * p + q] = (
                        (1 + (2 * p - 1) * gll_points[s]) * (1 + (2 * q - 1) * gll_points[t]) / 4
                    )
    return table


def landing(face_slot, high_s, high_t):
    direction, outward = divmod(face_slot, 2)
    if direction == 0:
        return (outward, high_s, high_t)
    if direction == 1:
        return (high_s, outward, high_t)
    return (high_s, high_t, outward)


def gather_table():
    weights = lift * corner_table()
    table = np.zeros((32, 288), np.float64)
    for slot in range(6):
        for s in range(2):
            for t in range(2):
                p, q, r = landing(slot, s, t)
                for c in range(3):
                    cols = slot * 48 + 16 * c + np.arange(16)
                    table[16 * r + 8 * p + 4 * q + c, cols] += weights[:, 2 * s + t]
    return table.astype(ml_dtypes.bfloat16)


def slot_table():
    slots = np.split(gather_table(), 6, axis=1)
    rows = [
        np.r_[0:8, 16:24], np.r_[8:16, 24:32], np.arange(32), np.arange(32), np.arange(16), np.arange(16, 32),
    ]
    return np.concatenate([slot[kept] for slot, kept in zip(slots, rows)], axis=0)


slot_rows = (0, 16, 32, 64, 96, 112, 128)


def between(low, high):
    step = high - low
    return [low, low + (0.5 - 0.5 * math.sqrt(0.2)) * step, low + (0.5 + 0.5 * math.sqrt(0.2)) * step, high]


def lanes(shape):
    return lax.broadcasted_iota(jnp.int32, shape, len(shape) - 1)


def z_next(value):
    last = value.shape[-1] - 1
    return jnp.where(lanes(value.shape) < last, pltpu.roll(value, last, value.ndim - 1), 0.0)


def z_prev(value):
    return jnp.where(lanes(value.shape) > 0, pltpu.roll(value, 1, value.ndim - 1), 0.0)


def dot(left, right):
    return jnp.dot(left, right, preferred_element_type=F32)


def wide(parts):
    return jnp.concatenate(parts, axis=1)


def tall(parts):
    return jnp.concatenate(parts, axis=0)


def columns(rows, count):
    z = rows.shape[1] // count
    return [rows[:, z * h : z * h + z] for h in range(count)]


def elements(slots):
    return tall([wide([hexa[s] for hexa in slots]) for s in range(6)])


def vertex_part(flux, parts_ref):
    rows = []
    for s in range(6):
        first, size = slot_rows[s], slot_rows[s + 1] - slot_rows[s]
        rows.append(dot(parts_ref[pl.ds(first, size), :], flux[48 * s : 48 * s + 48].astype(BF)))
    rows[2:4] = [rows[2] + rows[3]]
    return tall(rows)


def turned_dot(left, right):
    return lax.dot_general(left, right, (((1,), (1,)), ((), ())), preferred_element_type=F32)


def product(f_ref, st_ref, slot):
    first = 0 if slot is None else 48 * slot
    flux = turned_dot(f_ref[...], st_ref[...] if slot is None else st_ref[pl.ds(first, 48), :])
    rows = lax.broadcasted_iota(jnp.int32, flux.shape, 0)
    return flux, flux + jnp.where(rows == lax.broadcasted_iota(jnp.int32, flux.shape, 1) + first, F32(penalty), F32(0.0))


def slot_corners(traces, parts_ref, slot):
    z = traces[0].shape[1]
    first, size = slot_rows[slot], slot_rows[slot + 1] - slot_rows[slot]
    rows = dot(parts_ref[pl.ds(first, size), :], wide([trace.astype(BF) for trace in traces]))
    return [rows[:, z * h : z * h + z] for h in range(len(traces))]


def settle(rows, p):
    return rows[8 * p : 8 * p + 8] + z_prev(rows[16 + 8 * p : 24 + 8 * p])


def scaled_corners(delta, scales, offsets=(0, 1)):
    shape = (8, delta.shape[1])
    blank = jnp.zeros((1, shape[1]), F32)
    y_scale = jnp.where(
        lax.broadcasted_iota(jnp.int32, shape, 0) < 4,
        blank if scales[2] is None else scales[2], blank if scales[3] is None else scales[3],
    )
    results = []
    for p in offsets:
        parts = []
        for r in range(2):
            at = 32 + 16 * r + 8 * p
            part = delta[at : at + 8] * y_scale + delta[at + 32 : at + 40] * scales[4 + r]
            if scales[p] is not None:
                part = part + delta[16 * p + 8 * r : 16 * p + 8 * r + 8] * scales[p]
            parts.append(part)
        results.append(parts[0] + z_prev(parts[1]))
    return results


def level_visc(code, visc_ref):
    visc = jnp.zeros(code.shape, F32)
    for level in range(visc_ref.shape[0]):
        visc = visc + jnp.where(code == F32(level + 1), visc_ref[pl.ds(level, 1), :], F32(0.0))
    return visc


def merge(even, odd):
    odd = tall(odd)
    return tall(even) + pltpu.roll(odd, odd.shape[0] - 4, 0)


def first_kernel(
    wx, wy, visc_hbm, t_hbm, dir_hbm, cls_hbm, diag_hbm, st_hbm, f_hbm, parts_hbm,
    l_ref, nat, kp_ref, visc_ref, diag_ref, st_ref, f_ref, parts_ref, v_ref, v1_ref, v3_ref,
    swap0_ref, swap1_ref, swap2_ref, down_ref, up_ref, t_ref, dir_ref, cls_ref, levels, sems,
):
    cells = wx * wy
    pairs = [
        (parts_hbm, parts_ref), (f_hbm, f_ref), (st_hbm, st_ref), (t_hbm, t_ref), (dir_hbm, dir_ref),
        (cls_hbm, cls_ref), (visc_hbm, levels), (diag_hbm, diag_ref),
    ]
    copies = [pltpu.make_async_copy(a, b, sems.at[i]) for i, (a, b) in enumerate(pairs)]
    for copy in copies:
        copy.start()
    diagonal = lax.broadcasted_iota(jnp.int32, (288, 288), 0) == lax.broadcasted_iota(jnp.int32, (288, 288), 1)
    diagonal = jnp.where(diagonal, F32(penalty), F32(0.0))
    copies[0].wait()
    own = tall([vertex_part(diagonal, parts_ref), diagonal[144:192]])
    copies[1].wait()
    left = tall([vertex_part(f_ref[...], parts_ref).astype(BF), f_ref[pl.ds(144, 48), :]])
    for copy in copies[2:5]:
        copy.wait()
    short = (turned_dot(left, st_ref[...]) + own).astype(BF)
    z = t_ref.shape[2]
    for d in range(3):
        keep = (1 - dir_ref[d]).astype(F32)
        kp_ref[d] = keep
        masked = t_ref[d].astype(F32).reshape(48, cells, z) * keep[None]
        nat[d] = masked.reshape(48 * cells, z)
    laid = lay_out(wx, wy, nat, l_ref, True)
    kp_ref[3] = z_next(kp_ref[2])
    for copy in copies[5:]:
        copy.wait()
    for level in range(visc_ref.shape[0]):
        visc_ref[pl.ds(level, 1), :] = jnp.full((1, z), levels[level], F32)
    code = cls_ref[...].astype(F32) + 1.0
    kp_ref[4] = level_visc(code, visc_ref)
    kp_ref[5] = code
    row = lambda i, col: kp_ref[i, pl.ds(col, 1), :]
    corners = []
    for side, y in enumerate((0, wy - 1)):
        where = [(x, y) for x in range(wx)]
        slots, scales, left_out = known_hexes(wx, wy, where, l_ref, laid, kp_ref)
        rows = columns(dot(short if side else short[0:96], elements(slots)), wx)
        corners += known_corners(rows, scales, left_out)
        v1_ref[side] = rows[wx - 1][16:32] * row(4, (wx - 1) * wy + y)
    place = lax.broadcasted_iota(jnp.int32, (32, z), 0)
    lone = [part * row(4, x * wy + wy - 1) for x, part in enumerate(rows)]
    for x in range(wx):
        v3_ref[x] = jnp.where(lax.rem(place, 8) < 4, 0.0, lone[x][32:64])
    sums = [line_sums(corners[:wx]), line_sums(corners[wx:])]
    for side in range(2):
        for i in range(wx + 1):
            v_ref[side, i] = sums[side][i]
    corner = (wx - 1) * wy
    top = wy - 1
    for x in range(wx):
        down_ref[pl.ds(48 * x, 48), :] = laid[1, x, 0]
        up_ref[pl.ds(48 * x, 48), :] = lone[x][96:144].astype(BF)
    down_ref[pl.ds(48 * wx, 48), :] = laid[0, 0, 0]
    up_ref[pl.ds(48 * wx, 48), :] = laid[0, 0, top]
    flags = [row(1, x * wy) for x in range(wx)] + [row(0, 0), row(5, corner), row(0, corner), row(2, corner)]
    diag = tall([diag_ref[pl.ds(x * wy, 1), :] for x in range(wx)])
    high = diag.astype(BF).astype(F32)
    rim = pack(sums[0], 0) + pack([v1_ref[0, 0:8], v1_ref[0, 8:16]], 0) + flags + [high, diag - high]
    put_tail(down_ref, 48 * wx + 48, rim)
    flags = [row(kind, x * wy + top) for kind in (5, 0, 2) for x in range(wx)]
    rim = pack(sums[1], 1) + pack([v1_ref[1, 0:8], v1_ref[1, 8:16]], 1) + flags
    put_tail(up_ref, 48 * wx + 48, rim)
    depart_three(down_ref, up_ref, (swap0_ref, swap1_ref, swap2_ref))


def tail_rows(count):
    return -(-count // 16) * 16


def put_tail(ref, start, rows):
    count = sum(part.shape[0] for part in rows)
    full = ref.shape[0] - start
    if full > count:
        rows = rows + [jnp.zeros((full - count, rows[0].shape[1]), F32)]
    ref[pl.ds(start, full), :] = tall(rows).astype(BF)


def pack(parts, half):
    place = lax.broadcasted_iota(jnp.int32, parts[0].shape, 0)
    parts = parts + [jnp.zeros_like(parts[0])] * (len(parts) % 2)
    packed = []
    for low, high in zip(parts[0::2], parts[1::2]):
        if half:
            low = pltpu.roll(low, 4, 0)
        else:
            high = pltpu.roll(high, 4, 0)
        packed.append(jnp.where(place < 4, low, high))
    return packed


def unpack(packed, count, half):
    parts = []
    for n in range(count):
        part = packed[8 * (n // 2) : 8 * (n // 2) + 8]
        parts.append(part if n % 2 == half else pltpu.roll(part, 4, 0))
    return parts


def read_tail(ref, wx, half):
    start = 48 * wx + 48
    rows = ref[pl.ds(start, ref.shape[0] - start), :].astype(F32)
    size = 8 * ((wx + 2) // 2)
    return unpack(rows, wx + 1, half), unpack(rows[size : size + 8], 2, half), rows[size + 8 :]


def line_sums(corners):
    low, high = [part[0] for part in corners], [part[1] for part in corners]
    return [low[0]] + [low[x] + high[x - 1] for x in range(1, len(low))] + [high[-1]]


def early(wx, wy, d, x, y):
    return y in (0, wy - 1) or (d == 0 and x == 0) or (d == 1 and y == 1)


def lay_out(wx, wy, nat, l_ref, first):
    laid = {}
    for d in range(3):
        for x in range(wx):
            for y in range(wy):
                if early(wx, wy, d, x, y) == first:
                    part = nat[d, pl.ds(x * wy + y, 48, stride=wx * wy), :]
                    laid[d, x, y] = part.astype(BF)
                    if d == 2:
                        laid[3, x, y] = z_next(part).astype(BF)
    for (d, x, y), part in laid.items():
        l_ref[d, x * wy + y] = part
    return laid


def known_hexes(wx, wy, where, l_ref, laid, kp_ref):
    z = l_ref.shape[3]
    nothing = jnp.zeros((48, z), BF)
    row = lambda i, col: kp_ref[i, pl.ds(col, 1), :]
    trace = lambda d, x, y: laid[d, x, y] if (d, x, y) in laid else l_ref[d, x * wy + y]
    slots, scales, left_out = [], [], []
    for x, y in where:
        here = x * wy + y
        visc = row(4, here)
        last_x, last_y = x == wx - 1, y == wy - 1
        slots.append(
            [
                trace(0, x, y), nothing if last_x else trace(0, x + 1, y),
                trace(1, x, y), nothing if last_y else trace(1, x, y + 1),
                trace(2, x, y), trace(3, x, y),
            ]
        )
        scales.append(
            [
                visc * row(0, here), visc if last_x else visc * row(0, here + wy),
                visc * row(1, here), visc if last_y else visc * row(1, here + 1),
                visc * row(2, here), visc * row(3, here),
            ]
        )
        left_out.append(([1] if last_x else []) + ([3] if last_y else []))
    return slots, scales, left_out


def known_corners(vertex, scales, left_out):
    return [
        scaled_corners(part, [None if s in out else scale[s] for s in range(6)])
        for part, scale, out in zip(vertex, scales, left_out)
    ]


def middle_kernel(
    wx, wy, l_ref, nat, kp_ref, st_ref, f_ref, parts_ref,
    c_ref, v_ref, v1_ref, mx_ref, my_ref, own_ref, rest_ref, m_ref, lost_ref,
):
    for slot, ref in ((1, mx_ref), (3, my_ref)):
        bare, flux = product(f_ref, st_ref, slot)
        turned = tall([bare[0:48], bare[96:288], bare[48:96]]) if slot == 1 else bare
        ref[pl.ds(0, 288), :] = turned.astype(BF)
        ref[pl.ds(288, 96), :] = vertex_part(flux, parts_ref).astype(BF)
    flux = product(f_ref, st_ref, None)[1]
    m_ref[pl.ds(0, 288), :] = flux.astype(BF)
    m_ref[pl.ds(288, 96), :] = vertex_part(flux, parts_ref).astype(BF)
    lost_ref[...] = (flux - flux.astype(BF).astype(F32))[:, 0:256].astype(BF)
    laid = lay_out(wx, wy, nat, rest_ref, False)
    own_ref[...] = dot(
        tall([my_ref[pl.ds(144, 48), :], my_ref[pl.ds(288, 96), :]]), wide([l_ref[1, x * wy] for x in range(wx)])
    )
    for y in range(wy):
        inside = 0 < y < wy - 1
        where = [(x, y) for x in range(wx)]
        slots, scales, left_out = known_hexes(wx, wy, where, l_ref, laid, kp_ref)
        element = elements(slots)
        rows = dot(m_ref[...] if inside else m_ref[pl.ds(0, 288), :], element)
        lost = columns(dot(lost_ref[...], element[0:256]), wx)
        rows = columns(rows, wx)
        for x in range(wx):
            for s in range(6):
                part = slice(48 * s, 48 * s + 48)
                c_ref[s, x * wy + y] = (rows[x][part] + lost[x][part]) * scales[x][s]
        if inside:
            corners = known_corners([part[288:] for part in rows], scales, left_out)
            v1_ref[y - 1] = rows[wx - 1][304:320] * kp_ref[4, pl.ds((wx - 1) * wy + y, 1), :]
            for i, part in enumerate(line_sums(corners)):
                v_ref[y - 1, i] = part


def after_y(wx, wy, xs, visc_ref, l_ref, kp_ref, parts_ref, my_ref, own_ref, v3_ref, down_ref, up_ref):
    z = l_ref.shape[3]
    misc_d = read_tail(down_ref, wx, 0)[2]
    misc_u = read_tail(up_ref, wx, 1)[2]
    row = lambda i, col: kp_ref[i, pl.ds(col, 1), :]
    delta = dot(my_ref[...], wide([down_ref[pl.ds(48 * x, 48), :] for x in xs]))
    arrived = [up_ref[pl.ds(48 * x, 48), :].astype(F32) for x in xs]
    arrived_corners = slot_corners(arrived, parts_ref, 3)
    results = []
    for n, x in enumerate(xs):
        here = x * wy + wy - 1
        last = x == wx - 1
        part = delta[:, z * n : z * n + z]
        visc = row(4, here)
        scales = [
            visc * row(0, here), visc if last else visc * row(0, here + wy), visc * row(1, here),
            visc * misc_d[x : x + 1], visc * row(2, here), visc * row(3, here),
        ]
        flux = [part[48 * s : 48 * s + 48] * scales[s] for s in range(6)]
        used = [None if (s == 1 and last) else scales[s] for s in range(6)]
        known = v3_ref[x] * misc_d[x : x + 1]
        top = [rows + settle(known, p) for p, rows in enumerate(scaled_corners(part[288:384], used))]
        top_one = part[304:320] * visc
        here = x * wy
        visc = level_visc(misc_u[x : x + 1], visc_ref)
        flag = row(1, here)
        own = own_ref[:, pl.ds(z * x, z)]
        keep_z = misc_u[2 * wx + x : 2 * wx + x + 1]
        scales = [
            visc * misc_u[wx + x : wx + x + 1], None if last else visc * misc_u[wx + x + 1 : wx + x + 2],
            None, visc * flag, visc * keep_z, visc * z_next(keep_z),
        ]
        known = arrived_corners[n] * flag
        low = [rows + settle(known, p) for p, rows in enumerate(scaled_corners(own[48:144], scales))]
        low_one = own[64:80] * visc
        face = (arrived[n] + visc * (own[0:48] + penalty * l_ref[1, here].astype(F32))) * flag
        results.append((flux, top, top_one, low, low_one, face))
    return results


def turn_kernel(
    wx, wy, visc_ref, l_ref, kp_ref, diag_ref, parts_ref, my_ref, own_ref, c_ref, va_ref, vb_ref,
    v1a_ref, v1b_ref, v3_ref, swap0_in, swap1_in, swap2_in,
    c3_ref, vt_ref, vl_ref, v1_ref, face_ref, yd_ref, yu_ref, inner_ref, outer_ref, down_ref, up_ref,
):
    z = l_ref.shape[3]
    arrive((swap0_in, swap1_in, swap2_in), yd_ref, yu_ref)
    xs = (0, wx - 1)
    results = after_y(wx, wy, xs, visc_ref, l_ref, kp_ref, parts_ref, my_ref, own_ref, v3_ref, yd_ref, yu_ref)
    row = lambda i, col: kp_ref[i, pl.ds(col, 1), :]
    sums_d, one_d, misc_d = read_tail(yd_ref, wx, 0)
    sums_u, one_u, misc_u = read_tail(yu_ref, wx, 1)
    edge_high, edge_low = misc_d[wx + 4 : 2 * wx + 4], misc_d[2 * wx + 4 : 3 * wx + 4]
    for n, (flux, top, top_one, low, low_one, face) in enumerate(results):
        for s in range(6):
            c3_ref[n, s] = flux[s]
        face_ref[n] = face
        for p in range(2):
            vt_ref[n, p] = top[p]
            vl_ref[n, p] = low[p]
    flux, top, top_one, low, low_one, face = results[1]
    mine = tall(one_u) + low_one
    v1_ref[0] = mine
    v1_ref[1] = v1a_ref[0]
    for y in range(wy - 2):
        v1_ref[2 + y] = v1b_ref[y]
    v1_ref[wy] = v1a_ref[1] + top_one
    v1_ref[wy + 1] = tall(one_d)

    def plane(i, n, p):
        lines = [sums_u[i] + vl_ref[n, p], va_ref[0, i]]
        lines += [vb_ref[y, i] for y in range(wy - 2)]
        lines += [va_ref[1, i] + vt_ref[n, p], sums_d[i]]
        return merge(lines[1::2], lines[0::2])

    down_ref[pl.ds(0, 48), :] = yu_ref[pl.ds(48 * wx, 48), :]
    for y in range(wy):
        down_ref[pl.ds(48 + 48 * y, 48), :] = l_ref[0, y]
    down_ref[pl.ds(48 * (wy + 1), 48), :] = yd_ref[pl.ds(48 * wx, 48), :]
    diag = diag_ref[pl.ds(0, wy), :]
    high = diag.astype(BF).astype(F32)
    rim = [plane(0, 0, 0), high, edge_high[0:1], diag - high, edge_low[0:1]]
    rim += [misc_u[wx : wx + 1], kp_ref[0, 0:wy], misc_d[wx : wx + 1]]
    put_tail(down_ref, 48 * (wy + 2), rim)
    corner = (wx - 1) * wy
    for y in range(wy):
        part = c_ref[1, corner + y]
        up_ref[pl.ds(48 * y, 48), :] = (part + flux[1] if y == wy - 1 else part).astype(BF)
    last = pl.ds(corner, wy)
    rim = [plane(wx, 1, 1), mine, *one_d]
    rim += [misc_u[wx - 1 : wx], kp_ref[5, last], misc_d[wx + 1 : wx + 2]]
    rim += [misc_u[3 * wx - 1 : 3 * wx], kp_ref[2, last], misc_d[wx + 3 : wx + 4]]
    rim += [kp_ref[1, last], misc_d[wx - 1 : wx]]
    put_tail(up_ref, 48 * wy, rim)
    depart("gx", down_ref, up_ref, inner_ref, outer_ref)


def assemble_kernel(
    wx, wy, visc_ref, l_ref, kp_ref, diag_ref, parts_ref, mx_ref, my_ref, own_ref, c_ref, c3_ref,
    va_ref, vb_ref, v3_ref, vt_ref, vl_ref, face_ref, yd_ref, yu_ref,
    r_ref, late_ref, v_ref, inv_ref, ownx_ref, mid,
):
    z = l_ref.shape[3]
    cells = wx * wy
    xs = tuple(range(1, wx - 1))
    results = after_y(wx, wy, xs, visc_ref, l_ref, kp_ref, parts_ref, my_ref, own_ref, v3_ref, yd_ref, yu_ref)
    for n, part in enumerate(results):
        for s in range(6):
            mid[n, s] = part[0][s]
    traces = [yu_ref[pl.ds(48 * wx, 48), :]] + [l_ref[0, y] for y in range(wy)] + [yd_ref[pl.ds(48 * wx, 48), :]]
    ownx_ref[...] = dot(mx_ref[pl.ds(240, 144), :], wide(traces))

    def contrib(slot, x, y):
        here = c_ref[slot, x * wy + y]
        if y < wy - 1:
            return here
        return here + (mid[x - 1, slot] if 0 < x < wx - 1 else c3_ref[0 if x == 0 else 1, slot])

    for x in range(wx):
        for y in range(wy):
            col = pl.ds(x * wy + y, 48, stride=cells)
            if y:
                behind = contrib(3, x, y - 1)
            elif 0 < x < wx - 1:
                behind = results[x - 1][5]
            else:
                behind = face_ref[0 if x == 0 else 1]
            ahead = contrib(0, x, y) + contrib(1, x - 1, y) if x else contrib(0, x, y)
            sides = [ahead, contrib(2, x, y) + behind, contrib(4, x, y) + z_prev(contrib(5, x, y))]
            for d in range(3):
                if x == wx - 1:
                    late_ref[d, y] = sides[d]
                elif d == 0 and x == 0:
                    late_ref[3, y] = sides[d]
                else:
                    r_ref[d, col, :] = sides[d]
    sums_d, one_d, misc_d = read_tail(yd_ref, wx, 0)
    sums_u, one_u, misc_u = read_tail(yu_ref, wx, 1)
    edge_diag = misc_d[wx + 4 : 2 * wx + 4] + misc_d[2 * wx + 4 : 3 * wx + 4]

    def brought(which, i):
        held = vt_ref if which == 1 else vl_ref
        terms = []
        for x, p in ((i, 0), (i - 1, 1)):
            if x in (0, wx - 1):
                terms.append(held[0 if x == 0 else 1, p])
            elif 0 < x < wx - 1:
                terms.append(results[x - 1][which][p])
        return sum(terms[1:], terms[0])

    for i in range(wx + 1):
        lines = [sums_u[i] + brought(3, i), va_ref[0, i]]
        lines += [vb_ref[y, i] for y in range(wy - 2)]
        lines += [va_ref[1, i] + brought(1, i), sums_d[i]]
        v_ref[i] = merge(lines[1::2], lines[0::2])
        if i < wx:
            parts = [jnp.broadcast_to(diag_ref[pl.ds(i * wy + y, 1), :], (4, z)) for y in range(wy)]
            parts += [jnp.broadcast_to(edge_diag[i : i + 1], (4, z)), jnp.zeros((4, z), F32)]
            inv_ref[i] = reciprocal(tall(parts))


def reciprocal(diag):
    present = diag > 0.0
    return jnp.where(present, (1.0 / gain) / jnp.where(present, diag, 1.0), 0.0)


def final_kernel(
    wx, wy, visc_ref, l_ref, kp_ref, parts_ref, mx_ref, ownx_ref, r_in, late_ref, v_ref, inv_ref, v1_ref,
    yd_ref, yu_ref, outer_in, inner_in, out_hbm, r_ref, held, fix, sems,
):
    here, last = lax.axis_index("gx"), lax.axis_size("gx") - 1

    def from_high(start, size):
        rows = pl.ds(start, size)
        value = jnp.where(even("gx"), inner_in[rows, :], outer_in[rows, :])
        return jnp.where(here < last, value, jnp.zeros_like(value))

    def from_low(start, size):
        rows = pl.ds(start, size)
        value = jnp.where(even("gx"), outer_in[rows, :], inner_in[rows, :])
        return jnp.where(here > 0, value, jnp.zeros_like(value))

    cells, z = wx * wy, l_ref.shape[3]
    rows = v_ref.shape[1]
    row = lambda i, col: kp_ref[i, pl.ds(col, 1), :]
    traces = [from_high(48 * j, 48) for j in range(wy + 2)]
    delta = dot(mx_ref[pl.ds(288, 96), :], wide(traces))
    rim_x = from_high(48 * (wy + 2), tail_rows(rows + 3 * wy + 4)).astype(F32)
    rim_l = from_low(48 * wy, tail_rows(rows + 32 + 3 * (wy + 2) - 1)).astype(F32)
    misc_d = read_tail(yd_ref, wx, 0)[2]
    misc_u = read_tail(yu_ref, wx, 1)[2]
    flags_high = rim_x[rows + 2 * (wy + 1) : rows + 3 * wy + 4]
    corner = (wx - 1) * wy
    arrived = [from_low(48 * y, 48) for y in range(wy)]
    arrived_corners = slot_corners(arrived, parts_ref, 1)
    codes = rim_l[rows + 32 : rows + 32 + wy + 2]
    keep_z = rim_l[rows + 32 + wy + 2 : rows + 32 + 2 * (wy + 2)]
    keep_y = rim_l[rows + 32 + 2 * (wy + 2) : rows + 32 + 3 * (wy + 2) - 1]
    low_visc = level_visc(codes, visc_ref)
    low_keep_z = z_next(keep_z)
    lines = [[], [], []]
    high_scales = []
    del r_in
    for j in range(-1, wy + 1):
        n = j + 1
        part = delta[:, z * n : z * n + z]
        flag = flags_high[n : n + 1]
        if j < 0:
            visc = level_visc(misc_u[wx - 1 : wx], visc_ref)
            kz = misc_u[3 * wx - 1 : 3 * wx]
            keeps = [misc_u[2 * wx - 1 : 2 * wx], flag, None, row(1, corner), kz, z_next(kz)]
        elif j < wy:
            here = corner + j
            visc = row(4, here)
            high_y = row(1, here + 1) if j < wy - 1 else misc_d[wx - 1 : wx]
            keeps = [row(0, here), flag, row(1, here), high_y, row(2, here), row(3, here)]
        else:
            visc = level_visc(misc_d[wx + 1 : wx + 2], visc_ref)
            kz = misc_d[wx + 3 : wx + 4]
            keeps = [misc_d[wx + 2 : wx + 3], flag, misc_d[wx - 1 : wx], None, kz, z_next(kz)]
        scales = [None if keep is None else visc * keep for keep in keeps]
        corners = scaled_corners(part, scales)
        one = v1_ref[n] * flag
        lines[0].append(corners[0])
        lines[1].append(corners[1] + one[0:8] + z_prev(one[8:16]))
        high_scales.append(scales)
        own = ownx_ref[:, pl.ds(z * n, z)]
        visc = low_visc[n : n + 1]
        flag = misc_u[wx : wx + 1] if j < 0 else misc_d[wx : wx + 1] if j == wy else row(0, j)
        scales = [
            None, visc * flag, None if j < 0 else visc * keep_y[j : j + 1],
            None if j == wy else visc * keep_y[j + 1 : j + 2], visc * keep_z[n : n + 1], visc * low_keep_z[n : n + 1],
        ]
        corners = scaled_corners(own[48:144], scales, (1,))[0]
        if 0 <= j < wy:
            one = arrived_corners[j] * flag
            lines[2].append(corners + one[0:8] + z_prev(one[8:16]))
            face = (arrived[j].astype(F32) + visc * (own[0:48] + penalty * l_ref[0, j].astype(F32))) * flag
            r_ref[0, pl.ds(j, 48, stride=cells), :] = late_ref[3, j] + face
        else:
            at = rows + (0 if j < 0 else 16)
            one = rim_l[at : at + 16] * flag
            lines[2].append(corners + one[0:8] + z_prev(one[8:16]))
    low, before, first = [merge(part[1::2], part[0::2]) for part in lines]
    top = v_ref[wx] + before + rim_x[0:rows]
    values = [(v_ref[0] + first + rim_l[0:rows]) * inv_ref[0]]
    values += [v_ref[i] * inv_ref[i] for i in range(1, wx - 1)]
    values += [(v_ref[wx - 1] + low) * inv_ref[wx - 1]]
    diag = rim_x[rows : rows + wy + 1] + rim_x[rows + wy + 1 : rows + 2 * (wy + 1)]
    parts = [jnp.broadcast_to(diag[j : j + 1], (4, z)) for j in range(wy + 1)]
    values += [top * reciprocal(tall(parts + [jnp.zeros((rows - 4 * (wy + 1), z), F32)]))]
    high = [pltpu.roll(value, rows - 4, 0) for value in values]
    for i in range(wx + 1):
        fix[0, pl.ds(4 * wy * i, 4 * wy), :] = values[i][0 : 4 * wy]
        fix[1, pl.ds(4 * wy * i, 4 * wy), :] = high[i][0 : 4 * wy]
    vertex = lambda c, p, q: fix[q, pl.ds(4 * wy * p + c, cells, stride=4), :]
    delta = columns(dot(mx_ref[pl.ds(0, 240), :], wide(traces[1 : wy + 1])), wy)
    behind = dot(mx_ref[pl.ds(96, 48), :], traces[0]) * high_scales[0][3]
    copies = []
    for d in range(3):
        for j in range(wy):
            scales = high_scales[j + 1]
            part = [delta[j][48 * i : 48 * i + 48] for i in range(5)]
            if d == 0:
                flux = part[0] * scales[0]
            elif d == 1:
                flux = part[1] * scales[2] + behind
                behind = part[2] * scales[3]
            else:
                flux = part[3] * scales[4] + z_prev(part[4] * scales[5])
            r_ref[d, pl.ds(corner + j, 48, stride=cells), :] = late_ref[d, j] + flux
        flags = kp_ref[d]
        for c in range(3):
            if d == 0:
                near = [vertex(c, 0, q) * flags for q in range(2)]
                far = [z_next(vertex(c, 0, q)) * flags for q in range(2)]
                corner_values = [[near[0], far[0]], [near[1], far[1]]]
            elif d == 1:
                corner_values = [[vertex(c, p, 0) * flags, z_next(vertex(c, p, 0)) * flags] for p in range(2)]
            else:
                corner_values = [[vertex(c, p, q) * flags for q in range(2)] for p in range(2)]
            lines = [between(corner_values[0][t], corner_values[1][t]) for t in range(2)]
            for a in range(4):
                for b, value in enumerate(between(lines[0][a], lines[1][a])):
                    at = pl.ds(cells * (16 * c + 4 * a + b), cells)
                    held[d, at, :] = (r_ref[d, at, :] + value).astype(BF)
        copies.append(pltpu.make_async_copy(held.at[d], out_hbm.at[d], sems.at[d]))
        copies[d].start()
    for copy in copies:
        copy.wait()


def call(body, args, outs, scratch, flops, hbm=False, aliases=None):
    if hbm:
        args = tuple(pltpu.with_memory_space_constraint(a, pltpu.HBM) for a in args)
    keywords = {}
    if aliases:
        spaces = [pltpu.HBM] + [pltpu.VMEM] * (len(outs) - 1)
        keywords = dict(out_specs=tuple(pl.BlockSpec(memory_space=space) for space in spaces), input_output_aliases=aliases)
    return pl.pallas_call(
        body,
        **keywords,
        in_specs=[pl.BlockSpec(memory_space=pltpu.HBM if hbm else pltpu.VMEM)] * len(args),
        out_shape=outs,
        scratch_shapes=scratch,
        cost_estimate=pl.CostEstimate(flops=flops, bytes_accessed=1000000, transcendentals=0),
        compiler_params=pltpu.CompilerParams(vmem_limit_bytes=16 * 1024 * 1024),
    )(*args)


def local(traces, dirichlet, visc_class, viscosity, coarse_diag, solve_map, flux_map):
    wx, wy, z = traces.shape[2:]
    cells = wx * wy
    rows = 8 * (wy // 2 + 1)
    per_hex = 2 * 384 * 288 * z
    parts = jnp.asarray(slot_table())
    vm = pltpu.VMEM
    bind = lambda body: functools.partial(body, wx, wy)
    y_message = vm((48 * wx + 48 + tail_rows(8 * ((wx + 2) // 2) + 8 + 3 * wx + 4), z), BF)
    x_message = vm((48 * (wy + 2) + tail_rows(rows + 3 * wy + 4), z), BF)

    (lifted, nat, flags, visc, diag, s_turned, f_map, parts, va, v1a, v3, *swaps) = call(
        bind(first_kernel),
        (
            viscosity, traces.reshape(3, 48 * cells, z), dirichlet.reshape(3, cells, z),
            visc_class.reshape(cells, z), coarse_diag.reshape(cells, z), solve_map.T, flux_map, parts,
        ),
        (
            vm((4, cells, 48, z), BF), vm((3, 48 * cells, z), F32), vm((6, cells, z), F32), vm((viscosity.shape[0], z), F32), vm((cells, z), F32),
            vm(solve_map.shape[::-1], BF), vm(flux_map.shape, BF), vm(parts.shape, BF),
            vm((2, wx + 1, 8, z), F32), vm((2, 16, z), F32), vm((wx, 32, z), F32),
            y_message, y_message, y_message,
        ),
        [
            y_message, y_message,
            vm((3, 48 * cells, z), BF), vm((3, cells, z), jnp.int32), vm((cells, z), jnp.int32),
            pltpu.SMEM(viscosity.shape, F32), pltpu.SemaphoreType.DMA((8,)),
        ],
        wx * per_hex, True,
    )
    swaps = [swap(message, "gy", "gx", k, 3) for k, message in enumerate(swaps)]
    c, vb, v1b, mx, my, own = call(
        bind(middle_kernel),
        (lifted, nat, flags, s_turned, f_map, parts),
        (
            vm((6, cells, 48, z), F32), vm((wy - 2, wx + 1, 8, z), F32), vm((wy - 2, 16, z), F32),
            vm((384, 48), BF), vm((384, 48), BF), vm((144, wx * z), F32),
        ),
        [vm((4, cells, 48, z), BF), vm((384, 288), BF), vm((288, 256), BF)], cells * per_hex,
    )
    c3, vt, vl, v1, face, yd, yu, inner, outer = call(
        bind(turn_kernel),
        (
            visc, lifted, flags, diag, parts, my, own, c, va, vb, v1a, v1b, v3, *swaps,
        ),
        (
            vm((2, 6, 48, z), F32), vm((2, 2, 8, z), F32), vm((2, 2, 8, z), F32), vm((wy + 2, 16, z), F32),
            vm((2, 48, z), F32), y_message, y_message, x_message, x_message,
        ),
        [x_message, x_message], 2 * per_hex,
    )
    inner = swap(inner, "gx", "gy", 0)
    outer = swap(outer, "gx", "gy", 1)
    residual, late, vs, inverse, ownx = call(
        bind(assemble_kernel),
        (
            visc, lifted, flags, diag, parts, mx, my, own, c, c3, va, vb, v3, vt, vl, face, yd, yu,
        ),
        (
            vm((3, 48 * cells, z), F32), vm((4, wy, 48, z), F32), vm((wx + 1, rows, z), F32), vm((wx, rows, z), F32),
            vm((144, (wy + 2) * z), F32),
        ),
        [vm((wx - 2, 6, 48, z), F32)], 4 * per_hex,
    )
    out, _ = call(
        bind(final_kernel),
        (
            visc, lifted, flags, parts, mx, ownx, residual, late, vs, inverse, v1, yd, yu, outer, inner,
        ),
        (jax.ShapeDtypeStruct((3, 48 * cells, z), BF), vm((3, 48 * cells, z), F32)),
        [vm((3, 48 * cells, z), BF), vm((2, 4 * wy * (wx + 1), z), F32), pltpu.SemaphoreType.DMA((3,))], 6 * per_hex,
        aliases={6: 1},
    )
    return out.reshape(traces.shape)


def solution(mesh):
    in_specs = (
        P(None, None, "gx", "gy", None),
        P(None, "gx", "gy", None),
        P("gx", "gy", None),
        P(),
        P("gx", "gy", None),
        P(),
        P(),
    )
    out_specs = P(None, None, "gx", "gy", None)
    return jax.shard_map(local, mesh=mesh, in_specs=in_specs, out_specs=out_specs, check_vma=False)
```

```python
import functools
import math

import jax
import jax.numpy as jnp
import ml_dtypes
import numpy as np
from jax import lax
from jax.experimental import pallas as pl
from jax.experimental.pallas import tpu as pltpu
from jax.sharding import PartitionSpec as P

penalty = 0.5
BF = jnp.bfloat16
F32 = jnp.float32
lift = 1.3264
gain = 1.3280711361297461


def swap(value, axis, other, first, step=2):
    count, width = lax.axis_size(axis), lax.axis_size(other)
    place = (lambda i, j: i * width + j) if (axis, other) == ("gx", "gy") else (lambda i, j: j * count + i)
    lows = list(range(first, count - 1, step))
    pairs = [(place(low, j), place(low + 1, j)) for low in lows for j in range(width)]
    alone = [i for i in range(count) if i not in lows and i - 1 not in lows]
    pairs += [(place(i, j), place(i, j + 1)) for i in alone for j in range(0, width - 1, 2)]
    return lax.ppermute(value, ("gx", "gy"), pairs + [(high, low) for low, high in pairs])


def even(axis):
    return lax.rem(lax.axis_index(axis), 2) == 0


def arrive(messages, down_ref, up_ref):
    here, last = lax.axis_index("gy"), lax.axis_size("gy") - 1
    values = [ref[...] for ref in messages]
    for ref, swap_of, present in ((down_ref, lax.rem(here, 3), here < last), (up_ref, lax.rem(here + 2, 3), here > 0)):
        value = jnp.where(swap_of == 0, values[0], jnp.where(swap_of == 1, values[1], values[2]))
        ref[...] = jnp.where(present, value, jnp.zeros_like(value))


def depart_three(down_ref, up_ref, messages):
    here = lax.rem(lax.axis_index("gy"), 3)
    for k, ref in enumerate(messages):
        choose(here == k, up_ref, down_ref, ref)


def depart(axis, down_ref, up_ref, inner_ref, outer_ref):
    choose(even(axis), up_ref, down_ref, inner_ref)
    choose(even(axis), down_ref, up_ref, outer_ref)


def choose(condition, yes_ref, no_ref, out_ref, present=None):
    value = jnp.where(condition, yes_ref[...], no_ref[...])
    out_ref[...] = value if present is None else jnp.where(present, value, jnp.zeros_like(value))


def corner_table():
    gll_points = [-1.0, -math.sqrt(0.2), math.sqrt(0.2), 1.0]
    table = np.zeros((16, 4), np.float64)
    for s in range(4):
        for t in range(4):
            for p in range(2):
                for q in range(2):
                    table[4 * s + t, 2 * p + q] = (
                        (1 + (2 * p - 1) * gll_points[s]) * (1 + (2 * q - 1) * gll_points[t]) / 4
                    )
    return table


def landing(face_slot, high_s, high_t):
    direction, outward = divmod(face_slot, 2)
    if direction == 0:
        return (outward, high_s, high_t)
    if direction == 1:
        return (high_s, outward, high_t)
    return (high_s, high_t, outward)


def gather_table():
    weights = lift * corner_table()
    table = np.zeros((32, 288), np.float64)
    for slot in range(6):
        for s in range(2):
            for t in range(2):
                p, q, r = landing(slot, s, t)
                for c in range(3):
                    cols = slot * 48 + 16 * c + np.arange(16)
                    table[16 * r + 8 * p + 4 * q + c, cols] += weights[:, 2 * s + t]
    return table.astype(ml_dtypes.bfloat16)


def slot_table():
    slots = np.split(gather_table(), 6, axis=1)
    rows = [
        np.r_[0:8, 16:24], np.r_[8:16, 24:32], np.arange(32), np.arange(32), np.arange(16), np.arange(16, 32),
    ]
    return np.concatenate([slot[kept] for slot, kept in zip(slots, rows)], axis=0)


slot_rows = (0, 16, 32, 64, 96, 112, 128)


def between(low, high):
    step = high - low
    return [low, low + (0.5 - 0.5 * math.sqrt(0.2)) * step, low + (0.5 + 0.5 * math.sqrt(0.2)) * step, high]


def lanes(shape):
    return lax.broadcasted_iota(jnp.int32, shape, len(shape) - 1)


def z_next(value):
    last = value.shape[-1] - 1
    return jnp.where(lanes(value.shape) < last, pltpu.roll(value, last, value.ndim - 1), 0.0)


def z_prev(value):
    return jnp.where(lanes(value.shape) > 0, pltpu.roll(value, 1, value.ndim - 1), 0.0)


def dot(left, right):
    return jnp.dot(left, right, preferred_element_type=F32)


def wide(parts):
    return jnp.concatenate(parts, axis=1)


def tall(parts):
    return jnp.concatenate(parts, axis=0)


def columns(rows, count):
    z = rows.shape[1] // count
    return [rows[:, z * h : z * h + z] for h in range(count)]


def elements(slots):
    return tall([wide([hexa[s] for hexa in slots]) for s in range(6)])


def vertex_part(flux, parts_ref):
    rows = []
    for s in range(6):
        first, size = slot_rows[s], slot_rows[s + 1] - slot_rows[s]
        rows.append(dot(parts_ref[pl.ds(first, size), :], flux[48 * s : 48 * s + 48].astype(BF)))
    rows[2:4] = [rows[2] + rows[3]]
    return tall(rows)


def turned_dot(left, right):
    return lax.dot_general(left, right, (((1,), (1,)), ((), ())), preferred_element_type=F32)


def product(f_ref, st_ref, slot):
    first = 0 if slot is None else 48 * slot
    flux = turned_dot(f_ref[...], st_ref[...] if slot is None else st_ref[pl.ds(first, 48), :])
    rows = lax.broadcasted_iota(jnp.int32, flux.shape, 0)
    return flux, flux + jnp.where(rows == lax.broadcasted_iota(jnp.int32, flux.shape, 1) + first, F32(penalty), F32(0.0))


def slot_corners(traces, parts_ref, slot):
    z = traces[0].shape[1]
    first, size = slot_rows[slot], slot_rows[slot + 1] - slot_rows[slot]
    rows = dot(parts_ref[pl.ds(first, size), :], wide([trace.astype(BF) for trace in traces]))
    return [rows[:, z * h : z * h + z] for h in range(len(traces))]


def settle(rows, p):
    return rows[8 * p : 8 * p + 8] + z_prev(rows[16 + 8 * p : 24 + 8 * p])


def scaled_corners(delta, scales, offsets=(0, 1)):
    shape = (8, delta.shape[1])
    blank = jnp.zeros((1, shape[1]), F32)
    y_scale = jnp.where(
        lax.broadcasted_iota(jnp.int32, shape, 0) < 4,
        blank if scales[2] is None else scales[2], blank if scales[3] is None else scales[3],
    )
    results = []
    for p in offsets:
        parts = []
        for r in range(2):
            at = 32 + 16 * r + 8 * p
            part = delta[at : at + 8] * y_scale + delta[at + 32 : at + 40] * scales[4 + r]
            if scales[p] is not None:
                part = part + delta[16 * p + 8 * r : 16 * p + 8 * r + 8] * scales[p]
            parts.append(part)
        results.append(parts[0] + z_prev(parts[1]))
    return results


def level_visc(code, visc_ref):
    visc = jnp.zeros(code.shape, F32)
    for level in range(visc_ref.shape[0]):
        visc = visc + jnp.where(code == F32(level + 1), visc_ref[pl.ds(level, 1), :], F32(0.0))
    return visc


def merge(even, odd):
    odd = tall(odd)
    return tall(even) + pltpu.roll(odd, odd.shape[0] - 4, 0)


def first_kernel(
    wx, wy, visc_hbm, t_hbm, dir_hbm, cls_hbm, diag_hbm, st_hbm, f_hbm, parts_hbm,
    l_ref, nat, kp_ref, visc_ref, diag_ref, st_ref, f_ref, parts_ref, v_ref, v1_ref, v3_ref,
    swap0_ref, swap1_ref, swap2_ref, down_ref, up_ref, t_ref, dir_ref, cls_ref, levels, sems,
):
    cells = wx * wy
    pairs = [
        (parts_hbm, parts_ref), (f_hbm, f_ref), (st_hbm, st_ref), (t_hbm, t_ref), (dir_hbm, dir_ref),
        (cls_hbm, cls_ref), (visc_hbm, levels), (diag_hbm, diag_ref),
    ]
    copies = [pltpu.make_async_copy(a, b, sems.at[i]) for i, (a, b) in enumerate(pairs)]
    for copy in copies:
        copy.start()
    diagonal = lax.broadcasted_iota(jnp.int32, (288, 288), 0) == lax.broadcasted_iota(jnp.int32, (288, 288), 1)
    diagonal = jnp.where(diagonal, F32(penalty), F32(0.0))
    copies[0].wait()
    own = tall([vertex_part(diagonal, parts_ref), diagonal[144:192]])
    copies[1].wait()
    left = tall([vertex_part(f_ref[...], parts_ref).astype(BF), f_ref[pl.ds(144, 48), :]])
    for copy in copies[2:5]:
        copy.wait()
    short = (turned_dot(left, st_ref[...]) + own).astype(BF)
    z = t_ref.shape[2]
    for d in range(3):
        keep = (1 - dir_ref[d]).astype(F32)
        kp_ref[d] = keep
        masked = t_ref[d].astype(F32).reshape(48, cells, z) * keep[None]
        nat[d] = masked.reshape(48 * cells, z)
        lay_out(wx, wy, d, nat, l_ref, True)
    kp_ref[3] = z_next(kp_ref[2])
    for copy in copies[5:]:
        copy.wait()
    for level in range(visc_ref.shape[0]):
        visc_ref[pl.ds(level, 1), :] = jnp.full((1, z), levels[level], F32)
    code = cls_ref[...].astype(F32) + 1.0
    kp_ref[4] = level_visc(code, visc_ref)
    kp_ref[5] = code
    row = lambda i, col: kp_ref[i, pl.ds(col, 1), :]
    corners = []
    for side, y in enumerate((0, wy - 1)):
        where = [(x, y) for x in range(wx)]
        slots, scales, left_out = known_hexes(wx, wy, where, (l_ref, None), kp_ref)
        rows = columns(dot(short if side else short[0:96], elements(slots)), wx)
        corners += known_corners(rows, scales, left_out)
        v1_ref[side] = rows[wx - 1][16:32] * row(4, (wx - 1) * wy + y)
    place = lax.broadcasted_iota(jnp.int32, (32, z), 0)
    lone = [part * row(4, x * wy + wy - 1) for x, part in enumerate(rows)]
    for x in range(wx):
        v3_ref[x] = jnp.where(lax.rem(place, 8) < 4, 0.0, lone[x][32:64])
    sums = [line_sums(corners[:wx]), line_sums(corners[wx:])]
    for side in range(2):
        for i in range(wx + 1):
            v_ref[side, i] = sums[side][i]
    corner = (wx - 1) * wy
    top = wy - 1
    for x in range(wx):
        down_ref[pl.ds(48 * x, 48), :] = l_ref[1, x * wy]
        up_ref[pl.ds(48 * x, 48), :] = lone[x][96:144].astype(BF)
    down_ref[pl.ds(48 * wx, 48), :] = l_ref[0, 0]
    up_ref[pl.ds(48 * wx, 48), :] = l_ref[0, top]
    flags = [row(1, x * wy) for x in range(wx)] + [row(0, 0), row(5, corner), row(0, corner), row(2, corner)]
    diag = tall([diag_ref[pl.ds(x * wy, 1), :] for x in range(wx)])
    high = diag.astype(BF).astype(F32)
    rim = pack(sums[0], 0) + pack([v1_ref[0, 0:8], v1_ref[0, 8:16]], 0) + flags + [high, diag - high]
    put_tail(down_ref, 48 * wx + 48, rim)
    flags = [row(kind, x * wy + top) for kind in (5, 0, 2) for x in range(wx)]
    rim = pack(sums[1], 1) + pack([v1_ref[1, 0:8], v1_ref[1, 8:16]], 1) + flags
    put_tail(up_ref, 48 * wx + 48, rim)
    depart_three(down_ref, up_ref, (swap0_ref, swap1_ref, swap2_ref))


def tail_rows(count):
    return -(-count // 16) * 16


def put_tail(ref, start, rows):
    count = sum(part.shape[0] for part in rows)
    full = ref.shape[0] - start
    if full > count:
        rows = rows + [jnp.zeros((full - count, rows[0].shape[1]), F32)]
    ref[pl.ds(start, full), :] = tall(rows).astype(BF)


def pack(parts, half):
    place = lax.broadcasted_iota(jnp.int32, parts[0].shape, 0)
    parts = parts + [jnp.zeros_like(parts[0])] * (len(parts) % 2)
    packed = []
    for low, high in zip(parts[0::2], parts[1::2]):
        if half:
            low = pltpu.roll(low, 4, 0)
        else:
            high = pltpu.roll(high, 4, 0)
        packed.append(jnp.where(place < 4, low, high))
    return packed


def unpack(packed, count, half):
    parts = []
    for n in range(count):
        part = packed[8 * (n // 2) : 8 * (n // 2) + 8]
        parts.append(part if n % 2 == half else pltpu.roll(part, 4, 0))
    return parts


def read_tail(ref, wx, half):
    start = 48 * wx + 48
    rows = ref[pl.ds(start, ref.shape[0] - start), :].astype(F32)
    size = 8 * ((wx + 2) // 2)
    return unpack(rows, wx + 1, half), unpack(rows[size : size + 8], 2, half), rows[size + 8 :]


def line_sums(corners):
    low, high = [part[0] for part in corners], [part[1] for part in corners]
    return [low[0]] + [low[x] + high[x - 1] for x in range(1, len(low))] + [high[-1]]


def early(wx, wy, d, x, y):
    return y in (0, wy - 1) or (d == 0 and x == 0) or (d == 1 and y == 1)


def lay_out(wx, wy, d, nat, l_ref, first):
    for x in range(wx):
        for y in range(wy):
            if early(wx, wy, d, x, y) == first:
                col = x * wy + y
                part = nat[d, pl.ds(col, 48, stride=wx * wy), :]
                l_ref[d, col] = part.astype(BF)
                if d == 2:
                    l_ref[3, col] = z_next(part).astype(BF)


def known_hexes(wx, wy, where, l_refs, kp_ref):
    z = l_refs[0].shape[3]
    nothing = jnp.zeros((48, z), BF)
    row = lambda i, col: kp_ref[i, pl.ds(col, 1), :]
    trace = lambda d, x, y: l_refs[0 if early(wx, wy, min(d, 2), x, y) else 1][d, x * wy + y]
    slots, scales, left_out = [], [], []
    for x, y in where:
        here = x * wy + y
        visc = row(4, here)
        last_x, last_y = x == wx - 1, y == wy - 1
        slots.append(
            [
                trace(0, x, y), nothing if last_x else trace(0, x + 1, y),
                trace(1, x, y), nothing if last_y else trace(1, x, y + 1),
                trace(2, x, y), trace(3, x, y),
            ]
        )
        scales.append(
            [
                visc * row(0, here), visc if last_x else visc * row(0, here + wy),
                visc * row(1, here), visc if last_y else visc * row(1, here + 1),
                visc * row(2, here), visc * row(3, here),
            ]
        )
        left_out.append(([1] if last_x else []) + ([3] if last_y else []))
    return slots, scales, left_out


def known_corners(vertex, scales, left_out):
    return [
        scaled_corners(part, [None if s in out else scale[s] for s in range(6)])
        for part, scale, out in zip(vertex, scales, left_out)
    ]


def middle_kernel(
    wx, wy, l_ref, nat, kp_ref, st_ref, f_ref, parts_ref,
    c_ref, v_ref, v1_ref, mx_ref, my_ref, own_ref, rest_ref, m_ref, lost_ref,
):
    for slot, ref in ((1, mx_ref), (3, my_ref)):
        bare, flux = product(f_ref, st_ref, slot)
        turned = tall([bare[0:48], bare[96:288], bare[48:96]]) if slot == 1 else bare
        ref[pl.ds(0, 288), :] = turned.astype(BF)
        ref[pl.ds(288, 96), :] = vertex_part(flux, parts_ref).astype(BF)
    flux = product(f_ref, st_ref, None)[1]
    m_ref[pl.ds(0, 288), :] = flux.astype(BF)
    m_ref[pl.ds(288, 96), :] = vertex_part(flux, parts_ref).astype(BF)
    lost_ref[...] = (flux - flux.astype(BF).astype(F32))[:, 0:256].astype(BF)
    for d in range(3):
        lay_out(wx, wy, d, nat, rest_ref, False)
    own_ref[...] = dot(
        tall([my_ref[pl.ds(144, 48), :], my_ref[pl.ds(288, 96), :]]), wide([l_ref[1, x * wy] for x in range(wx)])
    )
    for y in range(wy):
        inside = 0 < y < wy - 1
        where = [(x, y) for x in range(wx)]
        slots, scales, left_out = known_hexes(wx, wy, where, (l_ref, rest_ref), kp_ref)
        element = elements(slots)
        rows = dot(m_ref[...] if inside else m_ref[pl.ds(0, 288), :], element)
        lost = columns(dot(lost_ref[...], element[0:256]), wx)
        rows = columns(rows, wx)
        for x in range(wx):
            for s in range(6):
                part = slice(48 * s, 48 * s + 48)
                c_ref[s, x * wy + y] = (rows[x][part] + lost[x][part]) * scales[x][s]
        if inside:
            corners = known_corners([part[288:] for part in rows], scales, left_out)
            v1_ref[y - 1] = rows[wx - 1][304:320] * kp_ref[4, pl.ds((wx - 1) * wy + y, 1), :]
            for i, part in enumerate(line_sums(corners)):
                v_ref[y - 1, i] = part


def scales_top(wx, wy, x, kp_ref, misc_d):
    row = lambda i, col: kp_ref[i, pl.ds(col, 1), :]
    here = x * wy + wy - 1
    visc = row(4, here)
    scales = [
        visc * row(0, here), visc if x == wx - 1 else visc * row(0, here + wy), visc * row(1, here),
        visc * misc_d[x : x + 1], visc * row(2, here), visc * row(3, here),
    ]
    return visc, scales


def y_vertex(wx, wy, xs, visc_ref, kp_ref, parts_ref, my_ref, own_ref, v3_ref, down_ref, up_ref):
    z = kp_ref.shape[2]
    misc_d = read_tail(down_ref, wx, 0)[2]
    misc_u = read_tail(up_ref, wx, 1)[2]
    row = lambda i, col: kp_ref[i, pl.ds(col, 1), :]
    delta = dot(my_ref[pl.ds(288, 96), :], wide([down_ref[pl.ds(48 * x, 48), :] for x in xs]))
    arrived_corners = slot_corners([up_ref[pl.ds(48 * x, 48), :] for x in xs], parts_ref, 3)
    results = []
    for n, x in enumerate(xs):
        last = x == wx - 1
        part = delta[:, z * n : z * n + z]
        visc, scales = scales_top(wx, wy, x, kp_ref, misc_d)
        used = [None if (s == 1 and last) else scales[s] for s in range(6)]
        known = v3_ref[x] * misc_d[x : x + 1]
        top = [rows + settle(known, p) for p, rows in enumerate(scaled_corners(part, used))]
        top_one = part[16:32] * visc
        visc = level_visc(misc_u[x : x + 1], visc_ref)
        flag = row(1, x * wy)
        own = own_ref[:, pl.ds(z * x, z)]
        keep_z = misc_u[2 * wx + x : 2 * wx + x + 1]
        scales = [
            visc * misc_u[wx + x : wx + x + 1], None if last else visc * misc_u[wx + x + 1 : wx + x + 2],
            None, visc * flag, visc * keep_z, visc * z_next(keep_z),
        ]
        known = arrived_corners[n] * flag
        low = [rows + settle(known, p) for p, rows in enumerate(scaled_corners(own[48:144], scales))]
        results.append((top, low, top_one, own[64:80] * visc))
    return results


def y_flux(wx, wy, visc_ref, l_ref, kp_ref, my_ref, own_ref, down_ref, up_ref):
    misc_d = read_tail(down_ref, wx, 0)[2]
    misc_u = read_tail(up_ref, wx, 1)[2]
    delta = columns(dot(my_ref[pl.ds(0, 288), :], wide([down_ref[pl.ds(48 * x, 48), :] for x in range(wx)])), wx)
    own = columns(own_ref[0:48, :], wx)
    results = []
    for x in range(wx):
        scales = scales_top(wx, wy, x, kp_ref, misc_d)[1]
        flux = [delta[x][48 * s : 48 * s + 48] * scales[s] for s in range(6)]
        visc = level_visc(misc_u[x : x + 1], visc_ref)
        arrived = up_ref[pl.ds(48 * x, 48), :].astype(F32)
        face = arrived + visc * (own[x] + penalty * l_ref[1, x * wy].astype(F32))
        results.append((flux, face * kp_ref[1, pl.ds(x * wy, 1), :]))
    return results


def turn_kernel(
    wx, wy, visc_ref, l_ref, kp_ref, diag_ref, parts_ref, my_ref, own_ref, c_ref, va_ref, vb_ref,
    v1a_ref, v1b_ref, v3_ref, swap0_in, swap1_in, swap2_in,
    vt_ref, vl_ref, v1_ref, yd_ref, yu_ref, inner_ref, outer_ref, down_ref, up_ref,
):
    z = l_ref.shape[3]
    arrive((swap0_in, swap1_in, swap2_in), yd_ref, yu_ref)
    xs = (0, wx - 1)
    results = y_vertex(wx, wy, xs, visc_ref, kp_ref, parts_ref, my_ref, own_ref, v3_ref, yd_ref, yu_ref)
    sums_d, one_d, misc_d = read_tail(yd_ref, wx, 0)
    sums_u, one_u, misc_u = read_tail(yu_ref, wx, 1)
    edge_high, edge_low = misc_d[wx + 4 : 2 * wx + 4], misc_d[2 * wx + 4 : 3 * wx + 4]
    for n, (top, low, _, _) in enumerate(results):
        for p in range(2):
            vt_ref[n, p] = top[p]
            vl_ref[n, p] = low[p]
    top_one, low_one = results[1][2:]
    mine = tall(one_u) + low_one
    v1_ref[0] = mine
    v1_ref[1] = v1a_ref[0]
    for y in range(wy - 2):
        v1_ref[2 + y] = v1b_ref[y]
    v1_ref[wy] = v1a_ref[1] + top_one
    v1_ref[wy + 1] = tall(one_d)

    def plane(i, n, p):
        lines = [sums_u[i] + vl_ref[n, p], va_ref[0, i]]
        lines += [vb_ref[y, i] for y in range(wy - 2)]
        lines += [va_ref[1, i] + vt_ref[n, p], sums_d[i]]
        return merge(lines[1::2], lines[0::2])

    down_ref[pl.ds(0, 48), :] = yu_ref[pl.ds(48 * wx, 48), :]
    for y in range(wy):
        down_ref[pl.ds(48 + 48 * y, 48), :] = l_ref[0, y]
    down_ref[pl.ds(48 * (wy + 1), 48), :] = yd_ref[pl.ds(48 * wx, 48), :]
    diag = diag_ref[pl.ds(0, wy), :]
    high = diag.astype(BF).astype(F32)
    rim = [plane(0, 0, 0), high, edge_high[0:1], diag - high, edge_low[0:1]]
    rim += [misc_u[wx : wx + 1], kp_ref[0, 0:wy], misc_d[wx : wx + 1]]
    put_tail(down_ref, 48 * (wy + 2), rim)
    corner = (wx - 1) * wy
    last_trace = yd_ref[pl.ds(48 * (wx - 1), 48), :]
    flux = dot(my_ref[pl.ds(48, 48), :], last_trace) * kp_ref[4, pl.ds(corner + wy - 1, 1), :]
    for y in range(wy):
        part = c_ref[1, corner + y]
        up_ref[pl.ds(48 * y, 48), :] = (part + flux if y == wy - 1 else part).astype(BF)
    last = pl.ds(corner, wy)
    rim = [plane(wx, 1, 1), mine, *one_d]
    rim += [misc_u[wx - 1 : wx], kp_ref[5, last], misc_d[wx + 1 : wx + 2]]
    rim += [misc_u[3 * wx - 1 : 3 * wx], kp_ref[2, last], misc_d[wx + 3 : wx + 4]]
    rim += [kp_ref[1, last], misc_d[wx - 1 : wx]]
    put_tail(up_ref, 48 * wy, rim)
    depart("gx", down_ref, up_ref, inner_ref, outer_ref)


def assemble_kernel(
    wx, wy, visc_ref, l_ref, kp_ref, diag_ref, parts_ref, mx_ref, my_ref, own_ref, c_ref,
    va_ref, vb_ref, v3_ref, vt_ref, vl_ref, yd_ref, yu_ref,
    r_ref, late_ref, v_ref, inv_ref, ownx_ref, mid,
):
    z = l_ref.shape[3]
    cells = wx * wy
    xs = tuple(range(1, wx - 1))
    results = y_vertex(wx, wy, xs, visc_ref, kp_ref, parts_ref, my_ref, own_ref, v3_ref, yd_ref, yu_ref)
    faces = []
    for x, (flux, face) in enumerate(y_flux(wx, wy, visc_ref, l_ref, kp_ref, my_ref, own_ref, yd_ref, yu_ref)):
        faces.append(face)
        for s in range(6):
            mid[x, s] = flux[s]
    traces = [yu_ref[pl.ds(48 * wx, 48), :]] + [l_ref[0, y] for y in range(wy)] + [yd_ref[pl.ds(48 * wx, 48), :]]
    ownx_ref[...] = dot(mx_ref[pl.ds(240, 144), :], wide(traces))

    def contrib(slot, x, y):
        here = c_ref[slot, x * wy + y]
        if y < wy - 1:
            return here
        return here + mid[x, slot]

    for x in range(wx):
        for y in range(wy):
            col = pl.ds(x * wy + y, 48, stride=cells)
            behind = contrib(3, x, y - 1) if y else faces[x]
            ahead = contrib(0, x, y) + contrib(1, x - 1, y) if x else contrib(0, x, y)
            sides = [ahead, contrib(2, x, y) + behind, contrib(4, x, y) + z_prev(contrib(5, x, y))]
            for d in range(3):
                if x == wx - 1:
                    late_ref[d, y] = sides[d]
                elif d == 0 and x == 0:
                    late_ref[3, y] = sides[d]
                else:
                    r_ref[d, col, :] = sides[d]
    sums_d, one_d, misc_d = read_tail(yd_ref, wx, 0)
    sums_u, one_u, misc_u = read_tail(yu_ref, wx, 1)
    edge_diag = misc_d[wx + 4 : 2 * wx + 4] + misc_d[2 * wx + 4 : 3 * wx + 4]

    def brought(which, i):
        held = vl_ref if which else vt_ref
        terms = []
        for x, p in ((i, 0), (i - 1, 1)):
            if x in (0, wx - 1):
                terms.append(held[0 if x == 0 else 1, p])
            elif 0 < x < wx - 1:
                terms.append(results[x - 1][which][p])
        return sum(terms[1:], terms[0])

    for i in range(wx + 1):
        lines = [sums_u[i] + brought(1, i), va_ref[0, i]]
        lines += [vb_ref[y, i] for y in range(wy - 2)]
        lines += [va_ref[1, i] + brought(0, i), sums_d[i]]
        v_ref[i] = merge(lines[1::2], lines[0::2])
        if i < wx:
            parts = [jnp.broadcast_to(diag_ref[pl.ds(i * wy + y, 1), :], (4, z)) for y in range(wy)]
            parts += [jnp.broadcast_to(edge_diag[i : i + 1], (4, z)), jnp.zeros((4, z), F32)]
            inv_ref[i] = reciprocal(tall(parts))


def reciprocal(diag):
    present = diag > 0.0
    return jnp.where(present, (1.0 / gain) / jnp.where(present, diag, 1.0), 0.0)


def final_kernel(
    wx, wy, visc_ref, l_ref, kp_ref, parts_ref, mx_ref, ownx_ref, r_in, late_ref, v_ref, inv_ref, v1_ref,
    yd_ref, yu_ref, outer_in, inner_in, out_hbm, r_ref, held, fix, sems,
):
    here, last = lax.axis_index("gx"), lax.axis_size("gx") - 1

    def from_high(start, size):
        rows = pl.ds(start, size)
        value = jnp.where(even("gx"), inner_in[rows, :], outer_in[rows, :])
        return jnp.where(here < last, value, jnp.zeros_like(value))

    def from_low(start, size):
        rows = pl.ds(start, size)
        value = jnp.where(even("gx"), outer_in[rows, :], inner_in[rows, :])
        return jnp.where(here > 0, value, jnp.zeros_like(value))

    cells, z = wx * wy, l_ref.shape[3]
    rows = v_ref.shape[1]
    row = lambda i, col: kp_ref[i, pl.ds(col, 1), :]
    traces = [from_high(48 * j, 48) for j in range(wy + 2)]
    delta = dot(mx_ref[pl.ds(288, 96), :], wide(traces))
    rim_x = from_high(48 * (wy + 2), tail_rows(rows + 3 * wy + 4)).astype(F32)
    rim_l = from_low(48 * wy, tail_rows(rows + 32 + 3 * (wy + 2) - 1)).astype(F32)
    misc_d = read_tail(yd_ref, wx, 0)[2]
    misc_u = read_tail(yu_ref, wx, 1)[2]
    flags_high = rim_x[rows + 2 * (wy + 1) : rows + 3 * wy + 4]
    corner = (wx - 1) * wy
    arrived = [from_low(48 * y, 48) for y in range(wy)]
    arrived_corners = slot_corners(arrived, parts_ref, 1)
    codes = rim_l[rows + 32 : rows + 32 + wy + 2]
    keep_z = rim_l[rows + 32 + wy + 2 : rows + 32 + 2 * (wy + 2)]
    keep_y = rim_l[rows + 32 + 2 * (wy + 2) : rows + 32 + 3 * (wy + 2) - 1]
    low_visc = level_visc(codes, visc_ref)
    low_keep_z = z_next(keep_z)
    lines = [[], [], []]
    high_scales = []
    del r_in
    for j in range(-1, wy + 1):
        n = j + 1
        part = delta[:, z * n : z * n + z]
        flag = flags_high[n : n + 1]
        if j < 0:
            visc = level_visc(misc_u[wx - 1 : wx], visc_ref)
            kz = misc_u[3 * wx - 1 : 3 * wx]
            keeps = [misc_u[2 * wx - 1 : 2 * wx], flag, None, row(1, corner), kz, z_next(kz)]
        elif j < wy:
            here = corner + j
            visc = row(4, here)
            high_y = row(1, here + 1) if j < wy - 1 else misc_d[wx - 1 : wx]
            keeps = [row(0, here), flag, row(1, here), high_y, row(2, here), row(3, here)]
        else:
            visc = level_visc(misc_d[wx + 1 : wx + 2], visc_ref)
            kz = misc_d[wx + 3 : wx + 4]
            keeps = [misc_d[wx + 2 : wx + 3], flag, misc_d[wx - 1 : wx], None, kz, z_next(kz)]
        scales = [None if keep is None else visc * keep for keep in keeps]
        corners = scaled_corners(part, scales)
        one = v1_ref[n] * flag
        lines[0].append(corners[0])
        lines[1].append(corners[1] + one[0:8] + z_prev(one[8:16]))
        high_scales.append(scales)
        own = ownx_ref[:, pl.ds(z * n, z)]
        visc = low_visc[n : n + 1]
        flag = misc_u[wx : wx + 1] if j < 0 else misc_d[wx : wx + 1] if j == wy else row(0, j)
        scales = [
            None, visc * flag, None if j < 0 else visc * keep_y[j : j + 1],
            None if j == wy else visc * keep_y[j + 1 : j + 2], visc * keep_z[n : n + 1], visc * low_keep_z[n : n + 1],
        ]
        corners = scaled_corners(own[48:144], scales, (1,))[0]
        if 0 <= j < wy:
            one = arrived_corners[j] * flag
            lines[2].append(corners + one[0:8] + z_prev(one[8:16]))
            face = (arrived[j].astype(F32) + visc * (own[0:48] + penalty * l_ref[0, j].astype(F32))) * flag
            r_ref[0, pl.ds(j, 48, stride=cells), :] = late_ref[3, j] + face
        else:
            at = rows + (0 if j < 0 else 16)
            one = rim_l[at : at + 16] * flag
            lines[2].append(corners + one[0:8] + z_prev(one[8:16]))
    low, before, first = [merge(part[1::2], part[0::2]) for part in lines]
    top = v_ref[wx] + before + rim_x[0:rows]
    values = [(v_ref[0] + first + rim_l[0:rows]) * inv_ref[0]]
    values += [v_ref[i] * inv_ref[i] for i in range(1, wx - 1)]
    values += [(v_ref[wx - 1] + low) * inv_ref[wx - 1]]
    diag = rim_x[rows : rows + wy + 1] + rim_x[rows + wy + 1 : rows + 2 * (wy + 1)]
    parts = [jnp.broadcast_to(diag[j : j + 1], (4, z)) for j in range(wy + 1)]
    values += [top * reciprocal(tall(parts + [jnp.zeros((rows - 4 * (wy + 1), z), F32)]))]
    high = [pltpu.roll(value, rows - 4, 0) for value in values]
    for i in range(wx + 1):
        fix[0, pl.ds(4 * wy * i, 4 * wy), :] = values[i][0 : 4 * wy]
        fix[1, pl.ds(4 * wy * i, 4 * wy), :] = high[i][0 : 4 * wy]
    vertex = lambda c, p, q: fix[q, pl.ds(4 * wy * p + c, cells, stride=4), :]
    delta = columns(dot(mx_ref[pl.ds(0, 240), :], wide(traces[1 : wy + 1])), wy)
    behind = dot(mx_ref[pl.ds(96, 48), :], traces[0]) * high_scales[0][3]
    copies = []
    for d in range(3):
        for j in range(wy):
            scales = high_scales[j + 1]
            part = [delta[j][48 * i : 48 * i + 48] for i in range(5)]
            if d == 0:
                flux = part[0] * scales[0]
            elif d == 1:
                flux = part[1] * scales[2] + behind
                behind = part[2] * scales[3]
            else:
                flux = part[3] * scales[4] + z_prev(part[4] * scales[5])
            r_ref[d, pl.ds(corner + j, 48, stride=cells), :] = late_ref[d, j] + flux
        flags = kp_ref[d]
        for c in range(3):
            if d == 0:
                near = [vertex(c, 0, q) * flags for q in range(2)]
                far = [z_next(vertex(c, 0, q)) * flags for q in range(2)]
                corner_values = [[near[0], far[0]], [near[1], far[1]]]
            elif d == 1:
                corner_values = [[vertex(c, p, 0) * flags, z_next(vertex(c, p, 0)) * flags] for p in range(2)]
            else:
                corner_values = [[vertex(c, p, q) * flags for q in range(2)] for p in range(2)]
            lines = [between(corner_values[0][t], corner_values[1][t]) for t in range(2)]
            for a in range(4):
                for b, value in enumerate(between(lines[0][a], lines[1][a])):
                    at = pl.ds(cells * (16 * c + 4 * a + b), cells)
                    held[d, at, :] = (r_ref[d, at, :] + value).astype(BF)
        copies.append(pltpu.make_async_copy(held.at[d], out_hbm.at[d], sems.at[d]))
        copies[d].start()
    for copy in copies:
        copy.wait()


def call(body, args, outs, scratch, flops, hbm=False, aliases=None):
    if hbm:
        args = tuple(pltpu.with_memory_space_constraint(a, pltpu.HBM) for a in args)
    keywords = {}
    if aliases:
        spaces = [pltpu.HBM] + [pltpu.VMEM] * (len(outs) - 1)
        keywords = dict(out_specs=tuple(pl.BlockSpec(memory_space=space) for space in spaces), input_output_aliases=aliases)
    return pl.pallas_call(
        body,
        **keywords,
        in_specs=[pl.BlockSpec(memory_space=pltpu.HBM if hbm else pltpu.VMEM)] * len(args),
        out_shape=outs,
        scratch_shapes=scratch,
        cost_estimate=pl.CostEstimate(flops=flops, bytes_accessed=1000000, transcendentals=0),
        compiler_params=pltpu.CompilerParams(vmem_limit_bytes=16 * 1024 * 1024),
    )(*args)


def local(traces, dirichlet, visc_class, viscosity, coarse_diag, solve_map, flux_map):
    wx, wy, z = traces.shape[2:]
    cells = wx * wy
    rows = 8 * (wy // 2 + 1)
    per_hex = 2 * 384 * 288 * z
    parts = jnp.asarray(slot_table())
    vm = pltpu.VMEM
    bind = lambda body: functools.partial(body, wx, wy)
    y_message = vm((48 * wx + 48 + tail_rows(8 * ((wx + 2) // 2) + 8 + 3 * wx + 4), z), BF)
    x_message = vm((48 * (wy + 2) + tail_rows(rows + 3 * wy + 4), z), BF)

    (lifted, nat, flags, visc, diag, s_turned, f_map, parts, va, v1a, v3, *swaps) = call(
        bind(first_kernel),
        (
            viscosity, traces.reshape(3, 48 * cells, z), dirichlet.reshape(3, cells, z),
            visc_class.reshape(cells, z), coarse_diag.reshape(cells, z), solve_map.T, flux_map, parts,
        ),
        (
            vm((4, cells, 48, z), BF), vm((3, 48 * cells, z), F32), vm((6, cells, z), F32), vm((viscosity.shape[0], z), F32), vm((cells, z), F32),
            vm(solve_map.shape[::-1], BF), vm(flux_map.shape, BF), vm(parts.shape, BF),
            vm((2, wx + 1, 8, z), F32), vm((2, 16, z), F32), vm((wx, 32, z), F32),
            y_message, y_message, y_message,
        ),
        [
            y_message, y_message,
            vm((3, 48 * cells, z), BF), vm((3, cells, z), jnp.int32), vm((cells, z), jnp.int32),
            pltpu.SMEM(viscosity.shape, F32), pltpu.SemaphoreType.DMA((8,)),
        ],
        wx * per_hex, True,
    )
    swaps = [swap(message, "gy", "gx", k, 3) for k, message in enumerate(swaps)]
    c, vb, v1b, mx, my, own = call(
        bind(middle_kernel),
        (lifted, nat, flags, s_turned, f_map, parts),
        (
            vm((6, cells, 48, z), F32), vm((wy - 2, wx + 1, 8, z), F32), vm((wy - 2, 16, z), F32),
            vm((384, 48), BF), vm((384, 48), BF), vm((144, wx * z), F32),
        ),
        [vm((4, cells, 48, z), BF), vm((384, 288), BF), vm((288, 256), BF)], cells * per_hex,
    )
    vt, vl, v1, yd, yu, inner, outer = call(
        bind(turn_kernel),
        (
            visc, lifted, flags, diag, parts, my, own, c, va, vb, v1a, v1b, v3, *swaps,
        ),
        (
            vm((2, 2, 8, z), F32), vm((2, 2, 8, z), F32), vm((wy + 2, 16, z), F32),
            y_message, y_message, x_message, x_message,
        ),
        [x_message, x_message], 2 * per_hex,
    )
    inner = swap(inner, "gx", "gy", 0)
    outer = swap(outer, "gx", "gy", 1)
    residual, late, vs, inverse, ownx = call(
        bind(assemble_kernel),
        (
            visc, lifted, flags, diag, parts, mx, my, own, c, va, vb, v3, vt, vl, yd, yu,
        ),
        (
            vm((3, 48 * cells, z), F32), vm((4, wy, 48, z), F32), vm((wx + 1, rows, z), F32), vm((wx, rows, z), F32),
            vm((144, (wy + 2) * z), F32),
        ),
        [vm((wx, 6, 48, z), F32)], 4 * per_hex,
    )
    out, _ = call(
        bind(final_kernel),
        (
            visc, lifted, flags, parts, mx, ownx, residual, late, vs, inverse, v1, yd, yu, outer, inner,
        ),
        (jax.ShapeDtypeStruct((3, 48 * cells, z), BF), vm((3, 48 * cells, z), F32)),
        [vm((3, 48 * cells, z), BF), vm((2, 4 * wy * (wx + 1), z), F32), pltpu.SemaphoreType.DMA((3,))], 6 * per_hex,
        aliases={6: 1},
    )
    return out.reshape(traces.shape)


def solution(mesh):
    in_specs = (
        P(None, None, "gx", "gy", None),
        P(None, "gx", "gy", None),
        P("gx", "gy", None),
        P(),
        P("gx", "gy", None),
        P(),
        P(),
    )
    out_specs = P(None, None, "gx", "gy", None)
    return jax.shard_map(local, mesh=mesh, in_specs=in_specs, out_specs=out_specs, check_vma=False)
```

```python
import functools
import math

import jax
import jax.numpy as jnp
import ml_dtypes
import numpy as np
from jax import lax
from jax.experimental import pallas as pl
from jax.experimental.pallas import tpu as pltpu
from jax.sharding import PartitionSpec as P

penalty = 0.5
BF = jnp.bfloat16
F32 = jnp.float32
lift = 1.3264
gain = 1.3280711361297461


def swap(value, axis, other, first, step=2):
    count, width = lax.axis_size(axis), lax.axis_size(other)
    place = (lambda i, j: i * width + j) if (axis, other) == ("gx", "gy") else (lambda i, j: j * count + i)
    lows = list(range(first, count - 1, step))
    pairs = [(place(low, j), place(low + 1, j)) for low in lows for j in range(width)]
    alone = [i for i in range(count) if i not in lows and i - 1 not in lows]
    pairs += [(place(i, j), place(i, j + 1)) for i in alone for j in range(0, width - 1, 2)]
    return lax.ppermute(value, ("gx", "gy"), pairs + [(high, low) for low, high in pairs])


def even(axis):
    return lax.rem(lax.axis_index(axis), 2) == 0


def arrive(messages, down_ref, up_ref):
    here, last = lax.axis_index("gy"), lax.axis_size("gy") - 1
    values = [ref[...] for ref in messages]
    for ref, swap_of, present in ((down_ref, lax.rem(here, 3), here < last), (up_ref, lax.rem(here + 2, 3), here > 0)):
        value = jnp.where(swap_of == 0, values[0], jnp.where(swap_of == 1, values[1], values[2]))
        ref[...] = jnp.where(present, value, jnp.zeros_like(value))


def depart_three(down_ref, up_ref, messages):
    here = lax.rem(lax.axis_index("gy"), 3)
    for k, ref in enumerate(messages):
        choose(here == k, up_ref, down_ref, ref)


def depart(axis, down_ref, up_ref, inner_ref, outer_ref):
    choose(even(axis), up_ref, down_ref, inner_ref)
    choose(even(axis), down_ref, up_ref, outer_ref)


def choose(condition, yes_ref, no_ref, out_ref, present=None):
    value = jnp.where(condition, yes_ref[...], no_ref[...])
    out_ref[...] = value if present is None else jnp.where(present, value, jnp.zeros_like(value))


def corner_table():
    gll_points = [-1.0, -math.sqrt(0.2), math.sqrt(0.2), 1.0]
    table = np.zeros((16, 4), np.float64)
    for s in range(4):
        for t in range(4):
            for p in range(2):
                for q in range(2):
                    table[4 * s + t, 2 * p + q] = (
                        (1 + (2 * p - 1) * gll_points[s]) * (1 + (2 * q - 1) * gll_points[t]) / 4
                    )
    return table


def landing(face_slot, high_s, high_t):
    direction, outward = divmod(face_slot, 2)
    if direction == 0:
        return (outward, high_s, high_t)
    if direction == 1:
        return (high_s, outward, high_t)
    return (high_s, high_t, outward)


def gather_table():
    weights = lift * corner_table()
    table = np.zeros((32, 288), np.float64)
    for slot in range(6):
        for s in range(2):
            for t in range(2):
                p, q, r = landing(slot, s, t)
                for c in range(3):
                    cols = slot * 48 + 16 * c + np.arange(16)
                    table[16 * r + 8 * p + 4 * q + c, cols] += weights[:, 2 * s + t]
    return table.astype(ml_dtypes.bfloat16)


def slot_table():
    slots = np.split(gather_table(), 6, axis=1)
    rows = [
        np.r_[0:8, 16:24], np.r_[8:16, 24:32], np.arange(32), np.arange(32), np.arange(16), np.arange(16, 32),
    ]
    return np.concatenate([slot[kept] for slot, kept in zip(slots, rows)], axis=0)


slot_rows = (0, 16, 32, 64, 96, 112, 128)


def between(low, high):
    step = high - low
    return [low, low + (0.5 - 0.5 * math.sqrt(0.2)) * step, low + (0.5 + 0.5 * math.sqrt(0.2)) * step, high]


def lanes(shape):
    return lax.broadcasted_iota(jnp.int32, shape, len(shape) - 1)


def z_next(value):
    last = value.shape[-1] - 1
    return jnp.where(lanes(value.shape) < last, pltpu.roll(value, last, value.ndim - 1), 0.0)


def z_prev(value):
    return jnp.where(lanes(value.shape) > 0, pltpu.roll(value, 1, value.ndim - 1), 0.0)


def dot(left, right):
    return jnp.dot(left, right, preferred_element_type=F32)


def wide(parts):
    return jnp.concatenate(parts, axis=1)


def tall(parts):
    return jnp.concatenate(parts, axis=0)


def columns(rows, count):
    z = rows.shape[1] // count
    return [rows[:, z * h : z * h + z] for h in range(count)]


def elements(slots):
    return tall([wide([hexa[s] for hexa in slots]) for s in range(6)])


def vertex_part(flux, parts_ref):
    rows = []
    for s in range(6):
        first, size = slot_rows[s], slot_rows[s + 1] - slot_rows[s]
        rows.append(dot(parts_ref[pl.ds(first, size), :], flux[48 * s : 48 * s + 48].astype(BF)))
    rows[2:4] = [rows[2] + rows[3]]
    return tall(rows)


def turned_dot(left, right):
    return lax.dot_general(left, right, (((1,), (1,)), ((), ())), preferred_element_type=F32)


def product(f_ref, st_ref, slot):
    first = 0 if slot is None else 48 * slot
    flux = turned_dot(f_ref[...], st_ref[...] if slot is None else st_ref[pl.ds(first, 48), :])
    rows = lax.broadcasted_iota(jnp.int32, flux.shape, 0)
    return flux, flux + jnp.where(rows == lax.broadcasted_iota(jnp.int32, flux.shape, 1) + first, F32(penalty), F32(0.0))


def slot_corners(traces, parts_ref, slot):
    z = traces[0].shape[1]
    first, size = slot_rows[slot], slot_rows[slot + 1] - slot_rows[slot]
    rows = dot(parts_ref[pl.ds(first, size), :], wide([trace.astype(BF) for trace in traces]))
    return [rows[:, z * h : z * h + z] for h in range(len(traces))]


def settle(rows, p):
    return rows[8 * p : 8 * p + 8] + z_prev(rows[16 + 8 * p : 24 + 8 * p])


def scaled_corners(delta, scales, offsets=(0, 1)):
    shape = (8, delta.shape[1])
    blank = jnp.zeros((1, shape[1]), F32)
    y_scale = jnp.where(
        lax.broadcasted_iota(jnp.int32, shape, 0) < 4,
        blank if scales[2] is None else scales[2], blank if scales[3] is None else scales[3],
    )
    results = []
    for p in offsets:
        parts = []
        for r in range(2):
            at = 32 + 16 * r + 8 * p
            part = delta[at : at + 8] * y_scale + delta[at + 32 : at + 40] * scales[4 + r]
            if scales[p] is not None:
                part = part + delta[16 * p + 8 * r : 16 * p + 8 * r + 8] * scales[p]
            parts.append(part)
        results.append(parts[0] + z_prev(parts[1]))
    return results


def level_visc(code, visc_ref):
    visc = jnp.zeros(code.shape, F32)
    for level in range(visc_ref.shape[0]):
        visc = visc + jnp.where(code == F32(level + 1), visc_ref[pl.ds(level, 1), :], F32(0.0))
    return visc


def merge(even, odd):
    odd = tall(odd)
    return tall(even) + pltpu.roll(odd, odd.shape[0] - 4, 0)


def first_kernel(
    wx, wy, visc_hbm, t_hbm, dir_hbm, cls_hbm, diag_hbm, st_hbm, f_hbm, parts_hbm,
    l_ref, nat, kp_ref, visc_ref, diag_ref, st_ref, f_ref, parts_ref, made_ref, v_ref, v1_ref, v3_ref,
    swap0_ref, swap1_ref, swap2_ref, down_ref, up_ref, t_ref, dir_ref, cls_ref, levels, sems,
):
    cells = wx * wy
    pairs = [
        (parts_hbm, parts_ref), (f_hbm, f_ref), (st_hbm, st_ref), (t_hbm, t_ref), (dir_hbm, dir_ref),
        (cls_hbm, cls_ref), (visc_hbm, levels), (diag_hbm, diag_ref),
    ]
    copies = [pltpu.make_async_copy(a, b, sems.at[i]) for i, (a, b) in enumerate(pairs)]
    for copy in copies:
        copy.start()
    diagonal = lax.broadcasted_iota(jnp.int32, (288, 288), 0) == lax.broadcasted_iota(jnp.int32, (288, 288), 1)
    diagonal = jnp.where(diagonal, F32(penalty), F32(0.0))
    copies[0].wait()
    own = tall([vertex_part(diagonal, parts_ref), diagonal[144:192]])
    copies[1].wait()
    left = tall([vertex_part(f_ref[...], parts_ref).astype(BF), f_ref[pl.ds(144, 48), :]])
    for copy in copies[2:5]:
        copy.wait()
    short = (turned_dot(left, st_ref[...]) + own).astype(BF)
    z = t_ref.shape[2]
    for d in range(3):
        keep = (1 - dir_ref[d]).astype(F32)
        kp_ref[d] = keep
        masked = t_ref[d].astype(F32).reshape(48, cells, z) * keep[None]
        nat[d] = masked.reshape(48 * cells, z)
        lay_out(wx, wy, d, nat, l_ref, True)
    kp_ref[3] = z_next(kp_ref[2])
    for copy in copies[5:]:
        copy.wait()
    for level in range(visc_ref.shape[0]):
        visc_ref[pl.ds(level, 1), :] = jnp.full((1, z), levels[level], F32)
    code = cls_ref[...].astype(F32) + 1.0
    kp_ref[4] = level_visc(code, visc_ref)
    kp_ref[5] = code
    row = lambda i, col: kp_ref[i, pl.ds(col, 1), :]
    corners = []
    for side, y in enumerate((0, wy - 1)):
        where = [(x, y) for x in range(wx)]
        slots, scales, left_out = known_hexes(wx, wy, where, (l_ref, None), kp_ref)
        rows = columns(dot(short if side else short[0:96], elements(slots)), wx)
        corners += known_corners(rows, scales, left_out)
        v1_ref[side] = rows[wx - 1][16:32] * row(4, (wx - 1) * wy + y)
    place = lax.broadcasted_iota(jnp.int32, (32, z), 0)
    lone = [part * row(4, x * wy + wy - 1) for x, part in enumerate(rows)]
    for x in range(wx):
        v3_ref[x] = jnp.where(lax.rem(place, 8) < 4, 0.0, lone[x][32:64])
    sums = [line_sums(corners[:wx]), line_sums(corners[wx:])]
    for side in range(2):
        for i in range(wx + 1):
            v_ref[side, i] = sums[side][i]
    corner = (wx - 1) * wy
    top = wy - 1
    for x in range(wx):
        down_ref[pl.ds(48 * x, 48), :] = l_ref[1, x * wy]
        up_ref[pl.ds(48 * x, 48), :] = lone[x][96:144].astype(BF)
    down_ref[pl.ds(48 * wx, 48), :] = l_ref[0, 0]
    up_ref[pl.ds(48 * wx, 48), :] = l_ref[0, top]
    flags = [row(1, x * wy) for x in range(wx)] + [row(0, 0), row(5, corner), row(0, corner), row(2, corner)]
    diag = tall([diag_ref[pl.ds(x * wy, 1), :] for x in range(wx)])
    high = diag.astype(BF).astype(F32)
    rim = pack(sums[0], 0) + pack([v1_ref[0, 0:8], v1_ref[0, 8:16]], 0) + flags + [high, diag - high]
    put_tail(down_ref, 48 * wx + 48, rim)
    flags = [row(kind, x * wy + top) for kind in (5, 0, 2) for x in range(wx)]
    rim = pack(sums[1], 1) + pack([v1_ref[1, 0:8], v1_ref[1, 8:16]], 1) + flags
    put_tail(up_ref, 48 * wx + 48, rim)
    depart_three(down_ref, up_ref, (swap0_ref, swap1_ref, swap2_ref))

    @pl.when(jnp.logical_not(even("gx")))
    def _():
        face_matrix(1, made_ref, st_ref, f_ref, parts_ref)


def tail_rows(count):
    return -(-count // 16) * 16


def put_tail(ref, start, rows):
    count = sum(part.shape[0] for part in rows)
    full = ref.shape[0] - start
    if full > count:
        rows = rows + [jnp.zeros((full - count, rows[0].shape[1]), F32)]
    ref[pl.ds(start, full), :] = tall(rows).astype(BF)


def pack(parts, half):
    place = lax.broadcasted_iota(jnp.int32, parts[0].shape, 0)
    parts = parts + [jnp.zeros_like(parts[0])] * (len(parts) % 2)
    packed = []
    for low, high in zip(parts[0::2], parts[1::2]):
        if half:
            low = pltpu.roll(low, 4, 0)
        else:
            high = pltpu.roll(high, 4, 0)
        packed.append(jnp.where(place < 4, low, high))
    return packed


def unpack(packed, count, half):
    parts = []
    for n in range(count):
        part = packed[8 * (n // 2) : 8 * (n // 2) + 8]
        parts.append(part if n % 2 == half else pltpu.roll(part, 4, 0))
    return parts


def read_tail(ref, wx, half):
    start = 48 * wx + 48
    rows = ref[pl.ds(start, ref.shape[0] - start), :].astype(F32)
    size = 8 * ((wx + 2) // 2)
    return unpack(rows, wx + 1, half), unpack(rows[size : size + 8], 2, half), rows[size + 8 :]


def line_sums(corners):
    low, high = [part[0] for part in corners], [part[1] for part in corners]
    return [low[0]] + [low[x] + high[x - 1] for x in range(1, len(low))] + [high[-1]]


def early(wx, wy, d, x, y):
    return y in (0, wy - 1) or (d == 0 and x == 0) or (d == 1 and y == 1)


def lay_out(wx, wy, d, nat, l_ref, first):
    for x in range(wx):
        for y in range(wy):
            if early(wx, wy, d, x, y) == first:
                col = x * wy + y
                part = nat[d, pl.ds(col, 48, stride=wx * wy), :]
                l_ref[d, col] = part.astype(BF)
                if d == 2:
                    l_ref[3, col] = z_next(part).astype(BF)


def known_hexes(wx, wy, where, l_refs, kp_ref):
    z = l_refs[0].shape[3]
    nothing = jnp.zeros((48, z), BF)
    row = lambda i, col: kp_ref[i, pl.ds(col, 1), :]
    trace = lambda d, x, y: l_refs[0 if early(wx, wy, min(d, 2), x, y) else 1][d, x * wy + y]
    slots, scales, left_out = [], [], []
    for x, y in where:
        here = x * wy + y
        visc = row(4, here)
        last_x, last_y = x == wx - 1, y == wy - 1
        slots.append(
            [
                trace(0, x, y), nothing if last_x else trace(0, x + 1, y),
                trace(1, x, y), nothing if last_y else trace(1, x, y + 1),
                trace(2, x, y), trace(3, x, y),
            ]
        )
        scales.append(
            [
                visc * row(0, here), visc if last_x else visc * row(0, here + wy),
                visc * row(1, here), visc if last_y else visc * row(1, here + 1),
                visc * row(2, here), visc * row(3, here),
            ]
        )
        left_out.append(([1] if last_x else []) + ([3] if last_y else []))
    return slots, scales, left_out


def known_corners(vertex, scales, left_out):
    return [
        scaled_corners(part, [None if s in out else scale[s] for s in range(6)])
        for part, scale, out in zip(vertex, scales, left_out)
    ]


def face_matrix(slot, ref, st_ref, f_ref, parts_ref):
    bare, flux = product(f_ref, st_ref, slot)
    turned = tall([bare[0:48], bare[96:288], bare[48:96]]) if slot == 1 else bare
    ref[pl.ds(0, 288), :] = turned.astype(BF)
    ref[pl.ds(288, 96), :] = vertex_part(flux, parts_ref).astype(BF)


def middle_kernel(
    wx, wy, l_ref, nat, kp_ref, st_ref, f_ref, parts_ref, made_ref,
    c_ref, v_ref, v1_ref, mx_ref, my_ref, own_ref, rest_ref, m_ref, lost_ref,
):
    face_matrix(3, my_ref, st_ref, f_ref, parts_ref)

    @pl.when(even("gx"))
    def _():
        face_matrix(1, mx_ref, st_ref, f_ref, parts_ref)

    @pl.when(jnp.logical_not(even("gx")))
    def _():
        mx_ref[...] = made_ref[...]

    flux = product(f_ref, st_ref, None)[1]
    m_ref[pl.ds(0, 288), :] = flux.astype(BF)
    m_ref[pl.ds(288, 96), :] = vertex_part(flux, parts_ref).astype(BF)
    lost_ref[...] = (flux - flux.astype(BF).astype(F32))[:, 0:256].astype(BF)
    for d in range(3):
        lay_out(wx, wy, d, nat, rest_ref, False)
    own_ref[...] = dot(
        tall([my_ref[pl.ds(144, 48), :], my_ref[pl.ds(288, 96), :]]), wide([l_ref[1, x * wy] for x in range(wx)])
    )
    for y in range(wy):
        inside = 0 < y < wy - 1
        where = [(x, y) for x in range(wx)]
        slots, scales, left_out = known_hexes(wx, wy, where, (l_ref, rest_ref), kp_ref)
        element = elements(slots)
        rows = dot(m_ref[...] if inside else m_ref[pl.ds(0, 288), :], element)
        lost = columns(dot(lost_ref[...], element[0:256]), wx)
        rows = columns(rows, wx)
        for x in range(wx):
            for s in range(6):
                part = slice(48 * s, 48 * s + 48)
                c_ref[s, x * wy + y] = (rows[x][part] + lost[x][part]) * scales[x][s]
        if inside:
            corners = known_corners([part[288:] for part in rows], scales, left_out)
            v1_ref[y - 1] = rows[wx - 1][304:320] * kp_ref[4, pl.ds((wx - 1) * wy + y, 1), :]
            for i, part in enumerate(line_sums(corners)):
                v_ref[y - 1, i] = part


def scales_top(wx, wy, x, kp_ref, misc_d):
    row = lambda i, col: kp_ref[i, pl.ds(col, 1), :]
    here = x * wy + wy - 1
    visc = row(4, here)
    scales = [
        visc * row(0, here), visc if x == wx - 1 else visc * row(0, here + wy), visc * row(1, here),
        visc * misc_d[x : x + 1], visc * row(2, here), visc * row(3, here),
    ]
    return visc, scales


def y_vertex(wx, wy, xs, visc_ref, kp_ref, parts_ref, my_ref, own_ref, v3_ref, down_ref, up_ref):
    z = kp_ref.shape[2]
    misc_d = read_tail(down_ref, wx, 0)[2]
    misc_u = read_tail(up_ref, wx, 1)[2]
    row = lambda i, col: kp_ref[i, pl.ds(col, 1), :]
    delta = dot(my_ref[pl.ds(288, 96), :], wide([down_ref[pl.ds(48 * x, 48), :] for x in xs]))
    arrived_corners = slot_corners([up_ref[pl.ds(48 * x, 48), :] for x in xs], parts_ref, 3)
    results = []
    for n, x in enumerate(xs):
        last = x == wx - 1
        part = delta[:, z * n : z * n + z]
        visc, scales = scales_top(wx, wy, x, kp_ref, misc_d)
        used = [None if (s == 1 and last) else scales[s] for s in range(6)]
        known = v3_ref[x] * misc_d[x : x + 1]
        top = [rows + settle(known, p) for p, rows in enumerate(scaled_corners(part, used))]
        top_one = part[16:32] * visc
        visc = level_visc(misc_u[x : x + 1], visc_ref)
        flag = row(1, x * wy)
        own = own_ref[:, pl.ds(z * x, z)]
        keep_z = misc_u[2 * wx + x : 2 * wx + x + 1]
        scales = [
            visc * misc_u[wx + x : wx + x + 1], None if last else visc * misc_u[wx + x + 1 : wx + x + 2],
            None, visc * flag, visc * keep_z, visc * z_next(keep_z),
        ]
        known = arrived_corners[n] * flag
        low = [rows + settle(known, p) for p, rows in enumerate(scaled_corners(own[48:144], scales))]
        results.append((top, low, top_one, own[64:80] * visc))
    return results


def y_flux(wx, wy, visc_ref, l_ref, kp_ref, my_ref, own_ref, down_ref, up_ref):
    misc_d = read_tail(down_ref, wx, 0)[2]
    misc_u = read_tail(up_ref, wx, 1)[2]
    delta = columns(dot(my_ref[pl.ds(0, 288), :], wide([down_ref[pl.ds(48 * x, 48), :] for x in range(wx)])), wx)
    own = columns(own_ref[0:48, :], wx)
    results = []
    for x in range(wx):
        scales = scales_top(wx, wy, x, kp_ref, misc_d)[1]
        flux = [delta[x][48 * s : 48 * s + 48] * scales[s] for s in range(6)]
        visc = level_visc(misc_u[x : x + 1], visc_ref)
        arrived = up_ref[pl.ds(48 * x, 48), :].astype(F32)
        face = arrived + visc * (own[x] + penalty * l_ref[1, x * wy].astype(F32))
        results.append((flux, face * kp_ref[1, pl.ds(x * wy, 1), :]))
    return results


def turn_kernel(
    wx, wy, visc_ref, l_ref, kp_ref, diag_ref, parts_ref, my_ref, own_ref, c_ref, va_ref, vb_ref,
    v1a_ref, v1b_ref, v3_ref, swap0_in, swap1_in, swap2_in,
    vt_ref, vl_ref, v1_ref, yd_ref, yu_ref, inner_ref, outer_ref, down_ref, up_ref,
):
    z = l_ref.shape[3]
    arrive((swap0_in, swap1_in, swap2_in), yd_ref, yu_ref)
    xs = (0, wx - 1)
    results = y_vertex(wx, wy, xs, visc_ref, kp_ref, parts_ref, my_ref, own_ref, v3_ref, yd_ref, yu_ref)
    sums_d, one_d, misc_d = read_tail(yd_ref, wx, 0)
    sums_u, one_u, misc_u = read_tail(yu_ref, wx, 1)
    edge_high, edge_low = misc_d[wx + 4 : 2 * wx + 4], misc_d[2 * wx + 4 : 3 * wx + 4]
    for n, (top, low, _, _) in enumerate(results):
        for p in range(2):
            vt_ref[n, p] = top[p]
            vl_ref[n, p] = low[p]
    top_one, low_one = results[1][2:]
    mine = tall(one_u) + low_one
    v1_ref[0] = mine
    v1_ref[1] = v1a_ref[0]
    for y in range(wy - 2):
        v1_ref[2 + y] = v1b_ref[y]
    v1_ref[wy] = v1a_ref[1] + top_one
    v1_ref[wy + 1] = tall(one_d)

    def plane(i, n, p):
        lines = [sums_u[i] + vl_ref[n, p], va_ref[0, i]]
        lines += [vb_ref[y, i] for y in range(wy - 2)]
        lines += [va_ref[1, i] + vt_ref[n, p], sums_d[i]]
        return merge(lines[1::2], lines[0::2])

    down_ref[pl.ds(0, 48), :] = yu_ref[pl.ds(48 * wx, 48), :]
    for y in range(wy):
        down_ref[pl.ds(48 + 48 * y, 48), :] = l_ref[0, y]
    down_ref[pl.ds(48 * (wy + 1), 48), :] = yd_ref[pl.ds(48 * wx, 48), :]
    diag = diag_ref[pl.ds(0, wy), :]
    high = diag.astype(BF).astype(F32)
    rim = [plane(0, 0, 0), high, edge_high[0:1], diag - high, edge_low[0:1]]
    rim += [misc_u[wx : wx + 1], kp_ref[0, 0:wy], misc_d[wx : wx + 1]]
    put_tail(down_ref, 48 * (wy + 2), rim)
    corner = (wx - 1) * wy
    last_trace = yd_ref[pl.ds(48 * (wx - 1), 48), :]
    flux = dot(my_ref[pl.ds(48, 48), :], last_trace) * kp_ref[4, pl.ds(corner + wy - 1, 1), :]
    for y in range(wy):
        part = c_ref[1, corner + y]
        up_ref[pl.ds(48 * y, 48), :] = (part + flux if y == wy - 1 else part).astype(BF)
    last = pl.ds(corner, wy)
    rim = [plane(wx, 1, 1), mine, *one_d]
    rim += [misc_u[wx - 1 : wx], kp_ref[5, last], misc_d[wx + 1 : wx + 2]]
    rim += [misc_u[3 * wx - 1 : 3 * wx], kp_ref[2, last], misc_d[wx + 3 : wx + 4]]
    rim += [kp_ref[1, last], misc_d[wx - 1 : wx]]
    put_tail(up_ref, 48 * wy, rim)
    depart("gx", down_ref, up_ref, inner_ref, outer_ref)


def assemble_kernel(
    wx, wy, visc_ref, l_ref, kp_ref, diag_ref, parts_ref, mx_ref, my_ref, own_ref, c_ref,
    va_ref, vb_ref, v3_ref, vt_ref, vl_ref, yd_ref, yu_ref,
    r_ref, late_ref, v_ref, inv_ref, ownx_ref, mid,
):
    z = l_ref.shape[3]
    cells = wx * wy
    xs = tuple(range(1, wx - 1))
    results = y_vertex(wx, wy, xs, visc_ref, kp_ref, parts_ref, my_ref, own_ref, v3_ref, yd_ref, yu_ref)
    faces = []
    for x, (flux, face) in enumerate(y_flux(wx, wy, visc_ref, l_ref, kp_ref, my_ref, own_ref, yd_ref, yu_ref)):
        faces.append(face)
        for s in range(6):
            mid[x, s] = flux[s]
    traces = [yu_ref[pl.ds(48 * wx, 48), :]] + [l_ref[0, y] for y in range(wy)] + [yd_ref[pl.ds(48 * wx, 48), :]]
    ownx_ref[...] = dot(mx_ref[pl.ds(240, 144), :], wide(traces))

    def contrib(slot, x, y):
        here = c_ref[slot, x * wy + y]
        if y < wy - 1:
            return here
        return here + mid[x, slot]

    for x in range(wx):
        for y in range(wy):
            col = pl.ds(x * wy + y, 48, stride=cells)
            behind = contrib(3, x, y - 1) if y else faces[x]
            ahead = contrib(0, x, y) + contrib(1, x - 1, y) if x else contrib(0, x, y)
            sides = [ahead, contrib(2, x, y) + behind, contrib(4, x, y) + z_prev(contrib(5, x, y))]
            for d in range(3):
                if x == wx - 1:
                    late_ref[d, y] = sides[d]
                elif d == 0 and x == 0:
                    late_ref[3, y] = sides[d]
                else:
                    r_ref[d, col, :] = sides[d]
    sums_d, one_d, misc_d = read_tail(yd_ref, wx, 0)
    sums_u, one_u, misc_u = read_tail(yu_ref, wx, 1)
    edge_diag = misc_d[wx + 4 : 2 * wx + 4] + misc_d[2 * wx + 4 : 3 * wx + 4]

    def brought(which, i):
        held = vl_ref if which else vt_ref
        terms = []
        for x, p in ((i, 0), (i - 1, 1)):
            if x in (0, wx - 1):
                terms.append(held[0 if x == 0 else 1, p])
            elif 0 < x < wx - 1:
                terms.append(results[x - 1][which][p])
        return sum(terms[1:], terms[0])

    for i in range(wx + 1):
        lines = [sums_u[i] + brought(1, i), va_ref[0, i]]
        lines += [vb_ref[y, i] for y in range(wy - 2)]
        lines += [va_ref[1, i] + brought(0, i), sums_d[i]]
        v_ref[i] = merge(lines[1::2], lines[0::2])
        if i < wx:
            parts = [jnp.broadcast_to(diag_ref[pl.ds(i * wy + y, 1), :], (4, z)) for y in range(wy)]
            parts += [jnp.broadcast_to(edge_diag[i : i + 1], (4, z)), jnp.zeros((4, z), F32)]
            inv_ref[i] = reciprocal(tall(parts))


def reciprocal(diag):
    present = diag > 0.0
    return jnp.where(present, (1.0 / gain) / jnp.where(present, diag, 1.0), 0.0)


def final_kernel(
    wx, wy, visc_ref, l_ref, kp_ref, parts_ref, mx_ref, ownx_ref, r_in, late_ref, v_ref, inv_ref, v1_ref,
    yd_ref, yu_ref, outer_in, inner_in, out_hbm, r_ref, held, fix, sems,
):
    here, last = lax.axis_index("gx"), lax.axis_size("gx") - 1

    def from_high(start, size):
        rows = pl.ds(start, size)
        value = jnp.where(even("gx"), inner_in[rows, :], outer_in[rows, :])
        return jnp.where(here < last, value, jnp.zeros_like(value))

    def from_low(start, size):
        rows = pl.ds(start, size)
        value = jnp.where(even("gx"), outer_in[rows, :], inner_in[rows, :])
        return jnp.where(here > 0, value, jnp.zeros_like(value))

    cells, z = wx * wy, l_ref.shape[3]
    rows = v_ref.shape[1]
    row = lambda i, col: kp_ref[i, pl.ds(col, 1), :]
    traces = [from_high(48 * j, 48) for j in range(wy + 2)]
    delta = dot(mx_ref[pl.ds(288, 96), :], wide(traces))
    rim_x = from_high(48 * (wy + 2), tail_rows(rows + 3 * wy + 4)).astype(F32)
    rim_l = from_low(48 * wy, tail_rows(rows + 32 + 3 * (wy + 2) - 1)).astype(F32)
    misc_d = read_tail(yd_ref, wx, 0)[2]
    misc_u = read_tail(yu_ref, wx, 1)[2]
    flags_high = rim_x[rows + 2 * (wy + 1) : rows + 3 * wy + 4]
    corner = (wx - 1) * wy
    arrived = [from_low(48 * y, 48) for y in range(wy)]
    arrived_corners = slot_corners(arrived, parts_ref, 1)
    codes = rim_l[rows + 32 : rows + 32 + wy + 2]
    keep_z = rim_l[rows + 32 + wy + 2 : rows + 32 + 2 * (wy + 2)]
    keep_y = rim_l[rows + 32 + 2 * (wy + 2) : rows + 32 + 3 * (wy + 2) - 1]
    low_visc = level_visc(codes, visc_ref)
    low_keep_z = z_next(keep_z)
    lines = [[], [], []]
    high_scales = []
    del r_in
    for j in range(-1, wy + 1):
        n = j + 1
        part = delta[:, z * n : z * n + z]
        flag = flags_high[n : n + 1]
        if j < 0:
            visc = level_visc(misc_u[wx - 1 : wx], visc_ref)
            kz = misc_u[3 * wx - 1 : 3 * wx]
            keeps = [misc_u[2 * wx - 1 : 2 * wx], flag, None, row(1, corner), kz, z_next(kz)]
        elif j < wy:
            here = corner + j
            visc = row(4, here)
            high_y = row(1, here + 1) if j < wy - 1 else misc_d[wx - 1 : wx]
            keeps = [row(0, here), flag, row(1, here), high_y, row(2, here), row(3, here)]
        else:
            visc = level_visc(misc_d[wx + 1 : wx + 2], visc_ref)
            kz = misc_d[wx + 3 : wx + 4]
            keeps = [misc_d[wx + 2 : wx + 3], flag, misc_d[wx - 1 : wx], None, kz, z_next(kz)]
        scales = [None if keep is None else visc * keep for keep in keeps]
        corners = scaled_corners(part, scales)
        one = v1_ref[n] * flag
        lines[0].append(corners[0])
        lines[1].append(corners[1] + one[0:8] + z_prev(one[8:16]))
        high_scales.append(scales)
        own = ownx_ref[:, pl.ds(z * n, z)]
        visc = low_visc[n : n + 1]
        flag = misc_u[wx : wx + 1] if j < 0 else misc_d[wx : wx + 1] if j == wy else row(0, j)
        scales = [
            None, visc * flag, None if j < 0 else visc * keep_y[j : j + 1],
            None if j == wy else visc * keep_y[j + 1 : j + 2], visc * keep_z[n : n + 1], visc * low_keep_z[n : n + 1],
        ]
        corners = scaled_corners(own[48:144], scales, (1,))[0]
        if 0 <= j < wy:
            one = arrived_corners[j] * flag
            lines[2].append(corners + one[0:8] + z_prev(one[8:16]))
            face = (arrived[j].astype(F32) + visc * (own[0:48] + penalty * l_ref[0, j].astype(F32))) * flag
            r_ref[0, pl.ds(j, 48, stride=cells), :] = late_ref[3, j] + face
        else:
            at = rows + (0 if j < 0 else 16)
            one = rim_l[at : at + 16] * flag
            lines[2].append(corners + one[0:8] + z_prev(one[8:16]))
    low, before, first = [merge(part[1::2], part[0::2]) for part in lines]
    top = v_ref[wx] + before + rim_x[0:rows]
    values = [(v_ref[0] + first + rim_l[0:rows]) * inv_ref[0]]
    values += [v_ref[i] * inv_ref[i] for i in range(1, wx - 1)]
    values += [(v_ref[wx - 1] + low) * inv_ref[wx - 1]]
    diag = rim_x[rows : rows + wy + 1] + rim_x[rows + wy + 1 : rows + 2 * (wy + 1)]
    parts = [jnp.broadcast_to(diag[j : j + 1], (4, z)) for j in range(wy + 1)]
    values += [top * reciprocal(tall(parts + [jnp.zeros((rows - 4 * (wy + 1), z), F32)]))]
    high = [pltpu.roll(value, rows - 4, 0) for value in values]
    for i in range(wx + 1):
        fix[0, pl.ds(4 * wy * i, 4 * wy), :] = values[i][0 : 4 * wy]
        fix[1, pl.ds(4 * wy * i, 4 * wy), :] = high[i][0 : 4 * wy]
    vertex = lambda c, p, q: fix[q, pl.ds(4 * wy * p + c, cells, stride=4), :]
    delta = columns(dot(mx_ref[pl.ds(0, 240), :], wide(traces[1 : wy + 1])), wy)
    behind = dot(mx_ref[pl.ds(96, 48), :], traces[0]) * high_scales[0][3]
    copies = []
    for d in range(3):
        for j in range(wy):
            scales = high_scales[j + 1]
            part = [delta[j][48 * i : 48 * i + 48] for i in range(5)]
            if d == 0:
                flux = part[0] * scales[0]
            elif d == 1:
                flux = part[1] * scales[2] + behind
                behind = part[2] * scales[3]
            else:
                flux = part[3] * scales[4] + z_prev(part[4] * scales[5])
            r_ref[d, pl.ds(corner + j, 48, stride=cells), :] = late_ref[d, j] + flux
        flags = kp_ref[d]
        for c in range(3):
            if d == 0:
                near = [vertex(c, 0, q) * flags for q in range(2)]
                far = [z_next(vertex(c, 0, q)) * flags for q in range(2)]
                corner_values = [[near[0], far[0]], [near[1], far[1]]]
            elif d == 1:
                corner_values = [[vertex(c, p, 0) * flags, z_next(vertex(c, p, 0)) * flags] for p in range(2)]
            else:
                corner_values = [[vertex(c, p, q) * flags for q in range(2)] for p in range(2)]
            lines = [between(corner_values[0][t], corner_values[1][t]) for t in range(2)]
            for a in range(4):
                for b, value in enumerate(between(lines[0][a], lines[1][a])):
                    at = pl.ds(cells * (16 * c + 4 * a + b), cells)
                    held[d, at, :] = (r_ref[d, at, :] + value).astype(BF)
        copies.append(pltpu.make_async_copy(held.at[d], out_hbm.at[d], sems.at[d]))
        copies[d].start()
    for copy in copies:
        copy.wait()


def call(body, args, outs, scratch, flops, hbm=False, aliases=None):
    if hbm:
        args = tuple(pltpu.with_memory_space_constraint(a, pltpu.HBM) for a in args)
    keywords = {}
    if aliases:
        spaces = [pltpu.HBM] + [pltpu.VMEM] * (len(outs) - 1)
        keywords = dict(out_specs=tuple(pl.BlockSpec(memory_space=space) for space in spaces), input_output_aliases=aliases)
    return pl.pallas_call(
        body,
        **keywords,
        in_specs=[pl.BlockSpec(memory_space=pltpu.HBM if hbm else pltpu.VMEM)] * len(args),
        out_shape=outs,
        scratch_shapes=scratch,
        cost_estimate=pl.CostEstimate(flops=flops, bytes_accessed=1000000, transcendentals=0),
        compiler_params=pltpu.CompilerParams(vmem_limit_bytes=16 * 1024 * 1024),
    )(*args)


def local(traces, dirichlet, visc_class, viscosity, coarse_diag, solve_map, flux_map):
    wx, wy, z = traces.shape[2:]
    cells = wx * wy
    rows = 8 * (wy // 2 + 1)
    per_hex = 2 * 384 * 288 * z
    parts = jnp.asarray(slot_table())
    vm = pltpu.VMEM
    bind = lambda body: functools.partial(body, wx, wy)
    y_message = vm((48 * wx + 48 + tail_rows(8 * ((wx + 2) // 2) + 8 + 3 * wx + 4), z), BF)
    x_message = vm((48 * (wy + 2) + tail_rows(rows + 3 * wy + 4), z), BF)

    (lifted, nat, flags, visc, diag, s_turned, f_map, parts, made, va, v1a, v3, *swaps) = call(
        bind(first_kernel),
        (
            viscosity, traces.reshape(3, 48 * cells, z), dirichlet.reshape(3, cells, z),
            visc_class.reshape(cells, z), coarse_diag.reshape(cells, z), solve_map.T, flux_map, parts,
        ),
        (
            vm((4, cells, 48, z), BF), vm((3, 48 * cells, z), F32), vm((6, cells, z), F32), vm((viscosity.shape[0], z), F32), vm((cells, z), F32),
            vm(solve_map.shape[::-1], BF), vm(flux_map.shape, BF), vm(parts.shape, BF), vm((384, 48), BF),
            vm((2, wx + 1, 8, z), F32), vm((2, 16, z), F32), vm((wx, 32, z), F32),
            y_message, y_message, y_message,
        ),
        [
            y_message, y_message,
            vm((3, 48 * cells, z), BF), vm((3, cells, z), jnp.int32), vm((cells, z), jnp.int32),
            pltpu.SMEM(viscosity.shape, F32), pltpu.SemaphoreType.DMA((8,)),
        ],
        wx * per_hex, True,
    )
    swaps = [swap(message, "gy", "gx", k, 3) for k, message in enumerate(swaps)]
    c, vb, v1b, mx, my, own = call(
        bind(middle_kernel),
        (lifted, nat, flags, s_turned, f_map, parts, made),
        (
            vm((6, cells, 48, z), F32), vm((wy - 2, wx + 1, 8, z), F32), vm((wy - 2, 16, z), F32),
            vm((384, 48), BF), vm((384, 48), BF), vm((144, wx * z), F32),
        ),
        [vm((4, cells, 48, z), BF), vm((384, 288), BF), vm((288, 256), BF)], cells * per_hex,
    )
    vt, vl, v1, yd, yu, inner, outer = call(
        bind(turn_kernel),
        (
            visc, lifted, flags, diag, parts, my, own, c, va, vb, v1a, v1b, v3, *swaps,
        ),
        (
            vm((2, 2, 8, z), F32), vm((2, 2, 8, z), F32), vm((wy + 2, 16, z), F32),
            y_message, y_message, x_message, x_message,
        ),
        [x_message, x_message], 2 * per_hex,
    )
    inner = swap(inner, "gx", "gy", 0)
    outer = swap(outer, "gx", "gy", 1)
    residual, late, vs, inverse, ownx = call(
        bind(assemble_kernel),
        (
            visc, lifted, flags, diag, parts, mx, my, own, c, va, vb, v3, vt, vl, yd, yu,
        ),
        (
            vm((3, 48 * cells, z), F32), vm((4, wy, 48, z), F32), vm((wx + 1, rows, z), F32), vm((wx, rows, z), F32),
            vm((144, (wy + 2) * z), F32),
        ),
        [vm((wx, 6, 48, z), F32)], 4 * per_hex,
    )
    out, _ = call(
        bind(final_kernel),
        (
            visc, lifted, flags, parts, mx, ownx, residual, late, vs, inverse, v1, yd, yu, outer, inner,
        ),
        (jax.ShapeDtypeStruct((3, 48 * cells, z), BF), vm((3, 48 * cells, z), F32)),
        [vm((3, 48 * cells, z), BF), vm((2, 4 * wy * (wx + 1), z), F32), pltpu.SemaphoreType.DMA((3,))], 6 * per_hex,
        aliases={6: 1},
    )
    return out.reshape(traces.shape)


def solution(mesh):
    in_specs = (
        P(None, None, "gx", "gy", None),
        P(None, "gx", "gy", None),
        P("gx", "gy", None),
        P(),
        P("gx", "gy", None),
        P(),
        P(),
    )
    out_specs = P(None, None, "gx", "gy", None)
    return jax.shard_map(local, mesh=mesh, in_specs=in_specs, out_specs=out_specs, check_vma=False)
```

```python
import functools
import math

import jax
import jax.numpy as jnp
import ml_dtypes
import numpy as np
from jax import lax
from jax.experimental import pallas as pl
from jax.experimental.pallas import tpu as pltpu
from jax.sharding import PartitionSpec as P

penalty = 0.5
BF = jnp.bfloat16
F32 = jnp.float32
lift = 1.3264
gain = 1.3280711361297461


def swap(value, axis, other, first, step=2):
    count, width = lax.axis_size(axis), lax.axis_size(other)
    place = (lambda i, j: i * width + j) if (axis, other) == ("gx", "gy") else (lambda i, j: j * count + i)
    lows = list(range(first, count - 1, step))
    pairs = [(place(low, j), place(low + 1, j)) for low in lows for j in range(width)]
    alone = [i for i in range(count) if i not in lows and i - 1 not in lows]
    pairs += [(place(i, j), place(i, j + 1)) for i in alone for j in range(0, width - 1, 2)]
    return lax.ppermute(value, ("gx", "gy"), pairs + [(high, low) for low, high in pairs])


def even(axis):
    return lax.rem(lax.axis_index(axis), 2) == 0


def arrive(messages, down_ref, up_ref):
    here, last = lax.axis_index("gy"), lax.axis_size("gy") - 1
    values = [ref[...] for ref in messages]
    for ref, swap_of, present in ((down_ref, lax.rem(here, 3), here < last), (up_ref, lax.rem(here + 2, 3), here > 0)):
        value = jnp.where(swap_of == 0, values[0], jnp.where(swap_of == 1, values[1], values[2]))
        ref[...] = jnp.where(present, value, jnp.zeros_like(value))


def depart_three(down_ref, up_ref, messages):
    here = lax.rem(lax.axis_index("gy"), 3)
    for k, ref in enumerate(messages):
        choose(here == k, up_ref, down_ref, ref)


def depart(axis, down_ref, up_ref, inner_ref, outer_ref):
    choose(even(axis), up_ref, down_ref, inner_ref)
    choose(even(axis), down_ref, up_ref, outer_ref)


def choose(condition, yes_ref, no_ref, out_ref, present=None):
    value = jnp.where(condition, yes_ref[...], no_ref[...])
    out_ref[...] = value if present is None else jnp.where(present, value, jnp.zeros_like(value))


def corner_table():
    gll_points = [-1.0, -math.sqrt(0.2), math.sqrt(0.2), 1.0]
    table = np.zeros((16, 4), np.float64)
    for s in range(4):
        for t in range(4):
            for p in range(2):
                for q in range(2):
                    table[4 * s + t, 2 * p + q] = (
                        (1 + (2 * p - 1) * gll_points[s]) * (1 + (2 * q - 1) * gll_points[t]) / 4
                    )
    return table


def landing(face_slot, high_s, high_t):
    direction, outward = divmod(face_slot, 2)
    if direction == 0:
        return (outward, high_s, high_t)
    if direction == 1:
        return (high_s, outward, high_t)
    return (high_s, high_t, outward)


def gather_table():
    weights = lift * corner_table()
    table = np.zeros((32, 288), np.float64)
    for slot in range(6):
        for s in range(2):
            for t in range(2):
                p, q, r = landing(slot, s, t)
                for c in range(3):
                    cols = slot * 48 + 16 * c + np.arange(16)
                    table[16 * r + 8 * p + 4 * q + c, cols] += weights[:, 2 * s + t]
    return table.astype(ml_dtypes.bfloat16)


def slot_table():
    slots = np.split(gather_table(), 6, axis=1)
    rows = [
        np.r_[0:8, 16:24], np.r_[8:16, 24:32], np.arange(32), np.arange(32), np.arange(16), np.arange(16, 32),
    ]
    return np.concatenate([slot[kept] for slot, kept in zip(slots, rows)], axis=0)


slot_rows = (0, 16, 32, 64, 96, 112, 128)


def between(low, high):
    step = high - low
    return [low, low + (0.5 - 0.5 * math.sqrt(0.2)) * step, low + (0.5 + 0.5 * math.sqrt(0.2)) * step, high]


def lanes(shape):
    return lax.broadcasted_iota(jnp.int32, shape, len(shape) - 1)


def z_next(value):
    last = value.shape[-1] - 1
    return jnp.where(lanes(value.shape) < last, pltpu.roll(value, last, value.ndim - 1), 0.0)


def z_prev(value):
    return jnp.where(lanes(value.shape) > 0, pltpu.roll(value, 1, value.ndim - 1), 0.0)


def dot(left, right):
    return jnp.dot(left, right, preferred_element_type=F32)


def wide(parts):
    return jnp.concatenate(parts, axis=1)


def tall(parts):
    return jnp.concatenate(parts, axis=0)


def columns(rows, count):
    z = rows.shape[1] // count
    return [rows[:, z * h : z * h + z] for h in range(count)]


def elements(slots):
    return tall([wide([hexa[s] for hexa in slots]) for s in range(6)])


def vertex_part(flux, parts_ref):
    rows = []
    for s in range(6):
        first, size = slot_rows[s], slot_rows[s + 1] - slot_rows[s]
        rows.append(dot(parts_ref[pl.ds(first, size), :], flux[48 * s : 48 * s + 48].astype(BF)))
    rows[2:4] = [rows[2] + rows[3]]
    return tall(rows)


def turned_dot(left, right):
    return lax.dot_general(left, right, (((1,), (1,)), ((), ())), preferred_element_type=F32)


def product(f_ref, st_ref, slot):
    first = 0 if slot is None else 48 * slot
    flux = turned_dot(f_ref[...], st_ref[...] if slot is None else st_ref[pl.ds(first, 48), :])
    rows = lax.broadcasted_iota(jnp.int32, flux.shape, 0)
    return flux, flux + jnp.where(rows == lax.broadcasted_iota(jnp.int32, flux.shape, 1) + first, F32(penalty), F32(0.0))


def slot_corners(traces, parts_ref, slot):
    z = traces[0].shape[1]
    first, size = slot_rows[slot], slot_rows[slot + 1] - slot_rows[slot]
    rows = dot(parts_ref[pl.ds(first, size), :], wide([trace.astype(BF) for trace in traces]))
    return [rows[:, z * h : z * h + z] for h in range(len(traces))]


def settle(rows, p):
    return rows[8 * p : 8 * p + 8] + z_prev(rows[16 + 8 * p : 24 + 8 * p])


def scaled_corners(delta, scales, offsets=(0, 1)):
    shape = (8, delta.shape[1])
    blank = jnp.zeros((1, shape[1]), F32)
    y_scale = jnp.where(
        lax.broadcasted_iota(jnp.int32, shape, 0) < 4,
        blank if scales[2] is None else scales[2], blank if scales[3] is None else scales[3],
    )
    results = []
    for p in offsets:
        parts = []
        for r in range(2):
            at = 32 + 16 * r + 8 * p
            part = delta[at : at + 8] * y_scale + delta[at + 32 : at + 40] * scales[4 + r]
            if scales[p] is not None:
                part = part + delta[16 * p + 8 * r : 16 * p + 8 * r + 8] * scales[p]
            parts.append(part)
        results.append(parts[0] + z_prev(parts[1]))
    return results


def level_visc(code, visc_ref):
    visc = jnp.zeros(code.shape, F32)
    for level in range(visc_ref.shape[0]):
        visc = visc + jnp.where(code == F32(level + 1), visc_ref[pl.ds(level, 1), :], F32(0.0))
    return visc


def merge(even, odd):
    odd = tall(odd)
    return tall(even) + pltpu.roll(odd, odd.shape[0] - 4, 0)


def first_kernel(
    wx, wy, visc_hbm, t_hbm, dir_hbm, cls_hbm, diag_hbm, st_hbm, f_hbm, parts_hbm,
    l_ref, nat, kp_ref, visc_ref, diag_ref, st_ref, f_ref, parts_ref, v_ref, v1_ref, v3_ref,
    swap0_ref, swap1_ref, swap2_ref, down_ref, up_ref, t_ref, dir_ref, cls_ref, levels, sems,
):
    cells = wx * wy
    pairs = [
        (t_hbm, t_ref), (parts_hbm, parts_ref), (f_hbm, f_ref), (st_hbm, st_ref), (dir_hbm, dir_ref),
        (cls_hbm, cls_ref), (visc_hbm, levels), (diag_hbm, diag_ref),
    ]
    copies = [pltpu.make_async_copy(a, b, sems.at[i]) for i, (a, b) in enumerate(pairs)]
    for copy in copies:
        copy.start()
    diagonal = lax.broadcasted_iota(jnp.int32, (288, 288), 0) == lax.broadcasted_iota(jnp.int32, (288, 288), 1)
    diagonal = jnp.where(diagonal, F32(penalty), F32(0.0))
    copies[1].wait()
    own = tall([vertex_part(diagonal, parts_ref), diagonal[144:192]])
    copies[2].wait()
    left = tall([vertex_part(f_ref[...], parts_ref).astype(BF), f_ref[pl.ds(144, 48), :]])
    for copy in (copies[3], copies[4], copies[0]):
        copy.wait()
    short = (turned_dot(left, st_ref[...]) + own).astype(BF)
    z = t_ref.shape[2]
    for d in range(3):
        keep = (1 - dir_ref[d]).astype(F32)
        kp_ref[d] = keep
        masked = t_ref[d].astype(F32).reshape(48, cells, z) * keep[None]
        nat[d] = masked.reshape(48 * cells, z)
        lay_out(wx, wy, d, nat, l_ref, True)
    kp_ref[3] = z_next(kp_ref[2])
    for copy in copies[5:]:
        copy.wait()
    for level in range(visc_ref.shape[0]):
        visc_ref[pl.ds(level, 1), :] = jnp.full((1, z), levels[level], F32)
    code = cls_ref[...].astype(F32) + 1.0
    kp_ref[4] = level_visc(code, visc_ref)
    kp_ref[5] = code
    row = lambda i, col: kp_ref[i, pl.ds(col, 1), :]
    corners = []
    for side, y in enumerate((0, wy - 1)):
        where = [(x, y) for x in range(wx)]
        slots, scales, left_out = known_hexes(wx, wy, where, (l_ref, None), kp_ref)
        rows = columns(dot(short if side else short[0:96], elements(slots)), wx)
        corners += known_corners(rows, scales, left_out)
        v1_ref[side] = rows[wx - 1][16:32] * row(4, (wx - 1) * wy + y)
    place = lax.broadcasted_iota(jnp.int32, (32, z), 0)
    lone = [part * row(4, x * wy + wy - 1) for x, part in enumerate(rows)]
    for x in range(wx):
        v3_ref[x] = jnp.where(lax.rem(place, 8) < 4, 0.0, lone[x][32:64])
    sums = [line_sums(corners[:wx]), line_sums(corners[wx:])]
    for side in range(2):
        for i in range(wx + 1):
            v_ref[side, i] = sums[side][i]
    corner = (wx - 1) * wy
    top = wy - 1
    for x in range(wx):
        down_ref[pl.ds(48 * x, 48), :] = l_ref[1, x * wy]
        up_ref[pl.ds(48 * x, 48), :] = lone[x][96:144].astype(BF)
    down_ref[pl.ds(48 * wx, 48), :] = l_ref[0, 0]
    up_ref[pl.ds(48 * wx, 48), :] = l_ref[0, top]
    flags = [row(1, x * wy) for x in range(wx)] + [row(0, 0), row(5, corner), row(0, corner), row(2, corner)]
    diag = tall([diag_ref[pl.ds(x * wy, 1), :] for x in range(wx)])
    high = diag.astype(BF).astype(F32)
    rim = pack(sums[0], 0) + pack([v1_ref[0, 0:8], v1_ref[0, 8:16]], 0) + flags + [high, diag - high]
    put_tail(down_ref, 48 * wx + 48, rim)
    flags = [row(kind, x * wy + top) for kind in (5, 0, 2) for x in range(wx)]
    rim = pack(sums[1], 1) + pack([v1_ref[1, 0:8], v1_ref[1, 8:16]], 1) + flags
    put_tail(up_ref, 48 * wx + 48, rim)
    depart_three(down_ref, up_ref, (swap0_ref, swap1_ref, swap2_ref))


def tail_rows(count):
    return -(-count // 16) * 16


def put_tail(ref, start, rows):
    count = sum(part.shape[0] for part in rows)
    full = ref.shape[0] - start
    if full > count:
        rows = rows + [jnp.zeros((full - count, rows[0].shape[1]), F32)]
    ref[pl.ds(start, full), :] = tall(rows).astype(BF)


def pack(parts, half):
    place = lax.broadcasted_iota(jnp.int32, parts[0].shape, 0)
    parts = parts + [jnp.zeros_like(parts[0])] * (len(parts) % 2)
    packed = []
    for low, high in zip(parts[0::2], parts[1::2]):
        if half:
            low = pltpu.roll(low, 4, 0)
        else:
            high = pltpu.roll(high, 4, 0)
        packed.append(jnp.where(place < 4, low, high))
    return packed


def unpack(packed, count, half):
    parts = []
    for n in range(count):
        part = packed[8 * (n // 2) : 8 * (n // 2) + 8]
        parts.append(part if n % 2 == half else pltpu.roll(part, 4, 0))
    return parts


def read_tail(ref, wx, half):
    start = 48 * wx + 48
    rows = ref[pl.ds(start, ref.shape[0] - start), :].astype(F32)
    size = 8 * ((wx + 2) // 2)
    return unpack(rows, wx + 1, half), unpack(rows[size : size + 8], 2, half), rows[size + 8 :]


def line_sums(corners):
    low, high = [part[0] for part in corners], [part[1] for part in corners]
    return [low[0]] + [low[x] + high[x - 1] for x in range(1, len(low))] + [high[-1]]


def early(wx, wy, d, x, y):
    return y in (0, wy - 1) or (d == 0 and x == 0) or (d == 1 and y == 1)


def lay_out(wx, wy, d, nat, l_ref, first):
    for x in range(wx):
        for y in range(wy):
            if early(wx, wy, d, x, y) == first:
                col = x * wy + y
                part = nat[d, pl.ds(col, 48, stride=wx * wy), :]
                l_ref[d, col] = part.astype(BF)
                if d == 2:
                    l_ref[3, col] = z_next(part).astype(BF)


def known_hexes(wx, wy, where, l_refs, kp_ref):
    z = l_refs[0].shape[3]
    nothing = jnp.zeros((48, z), BF)
    row = lambda i, col: kp_ref[i, pl.ds(col, 1), :]
    trace = lambda d, x, y: l_refs[0 if early(wx, wy, min(d, 2), x, y) else 1][d, x * wy + y]
    slots, scales, left_out = [], [], []
    for x, y in where:
        here = x * wy + y
        visc = row(4, here)
        last_x, last_y = x == wx - 1, y == wy - 1
        slots.append(
            [
                trace(0, x, y), nothing if last_x else trace(0, x + 1, y),
                trace(1, x, y), nothing if last_y else trace(1, x, y + 1),
                trace(2, x, y), trace(3, x, y),
            ]
        )
        scales.append(
            [
                visc * row(0, here), visc if last_x else visc * row(0, here + wy),
                visc * row(1, here), visc if last_y else visc * row(1, here + 1),
                visc * row(2, here), visc * row(3, here),
            ]
        )
        left_out.append(([1] if last_x else []) + ([3] if last_y else []))
    return slots, scales, left_out


def known_corners(vertex, scales, left_out):
    return [
        scaled_corners(part, [None if s in out else scale[s] for s in range(6)])
        for part, scale, out in zip(vertex, scales, left_out)
    ]


def middle_kernel(
    wx, wy, l_ref, nat, kp_ref, st_ref, f_ref, parts_ref,
    c_ref, v_ref, v1_ref, mx_ref, my_ref, own_ref, rest_ref, m_ref, lost_ref,
):
    for slot, ref in ((1, mx_ref), (3, my_ref)):
        bare, flux = product(f_ref, st_ref, slot)
        turned = tall([bare[0:48], bare[96:288], bare[48:96]]) if slot == 1 else bare
        ref[pl.ds(0, 288), :] = turned.astype(BF)
        ref[pl.ds(288, 96), :] = vertex_part(flux, parts_ref).astype(BF)
    flux = product(f_ref, st_ref, None)[1]
    m_ref[pl.ds(0, 288), :] = flux.astype(BF)
    m_ref[pl.ds(288, 96), :] = vertex_part(flux, parts_ref).astype(BF)
    lost_ref[...] = (flux - flux.astype(BF).astype(F32))[:, 0:256].astype(BF)
    for d in range(3):
        lay_out(wx, wy, d, nat, rest_ref, False)
    own_ref[...] = dot(
        tall([my_ref[pl.ds(144, 48), :], my_ref[pl.ds(288, 96), :]]), wide([l_ref[1, x * wy] for x in range(wx)])
    )
    for y in range(wy):
        inside = 0 < y < wy - 1
        where = [(x, y) for x in range(wx)]
        slots, scales, left_out = known_hexes(wx, wy, where, (l_ref, rest_ref), kp_ref)
        element = elements(slots)
        rows = dot(m_ref[...] if inside else m_ref[pl.ds(0, 288), :], element)
        lost = columns(dot(lost_ref[...], element[0:256]), wx)
        rows = columns(rows, wx)
        for x in range(wx):
            for s in range(6):
                part = slice(48 * s, 48 * s + 48)
                c_ref[s, x * wy + y] = (rows[x][part] + lost[x][part]) * scales[x][s]
        if inside:
            corners = known_corners([part[288:] for part in rows], scales, left_out)
            v1_ref[y - 1] = rows[wx - 1][304:320] * kp_ref[4, pl.ds((wx - 1) * wy + y, 1), :]
            for i, part in enumerate(line_sums(corners)):
                v_ref[y - 1, i] = part


def scales_top(wx, wy, x, kp_ref, misc_d):
    row = lambda i, col: kp_ref[i, pl.ds(col, 1), :]
    here = x * wy + wy - 1
    visc = row(4, here)
    scales = [
        visc * row(0, here), visc if x == wx - 1 else visc * row(0, here + wy), visc * row(1, here),
        visc * misc_d[x : x + 1], visc * row(2, here), visc * row(3, here),
    ]
    return visc, scales


def y_vertex(wx, wy, xs, visc_ref, kp_ref, parts_ref, my_ref, own_ref, v3_ref, down_ref, up_ref):
    z = kp_ref.shape[2]
    misc_d = read_tail(down_ref, wx, 0)[2]
    misc_u = read_tail(up_ref, wx, 1)[2]
    row = lambda i, col: kp_ref[i, pl.ds(col, 1), :]
    delta = dot(my_ref[pl.ds(288, 96), :], wide([down_ref[pl.ds(48 * x, 48), :] for x in xs]))
    arrived_corners = slot_corners([up_ref[pl.ds(48 * x, 48), :] for x in xs], parts_ref, 3)
    results = []
    for n, x in enumerate(xs):
        last = x == wx - 1
        part = delta[:, z * n : z * n + z]
        visc, scales = scales_top(wx, wy, x, kp_ref, misc_d)
        used = [None if (s == 1 and last) else scales[s] for s in range(6)]
        known = v3_ref[x] * misc_d[x : x + 1]
        top = [rows + settle(known, p) for p, rows in enumerate(scaled_corners(part, used))]
        top_one = part[16:32] * visc
        visc = level_visc(misc_u[x : x + 1], visc_ref)
        flag = row(1, x * wy)
        own = own_ref[:, pl.ds(z * x, z)]
        keep_z = misc_u[2 * wx + x : 2 * wx + x + 1]
        scales = [
            visc * misc_u[wx + x : wx + x + 1], None if last else visc * misc_u[wx + x + 1 : wx + x + 2],
            None, visc * flag, visc * keep_z, visc * z_next(keep_z),
        ]
        known = arrived_corners[n] * flag
        low = [rows + settle(known, p) for p, rows in enumerate(scaled_corners(own[48:144], scales))]
        results.append((top, low, top_one, own[64:80] * visc))
    return results


def y_flux(wx, wy, visc_ref, l_ref, kp_ref, my_ref, own_ref, down_ref, up_ref):
    misc_d = read_tail(down_ref, wx, 0)[2]
    misc_u = read_tail(up_ref, wx, 1)[2]
    delta = columns(dot(my_ref[pl.ds(0, 288), :], wide([down_ref[pl.ds(48 * x, 48), :] for x in range(wx)])), wx)
    own = columns(own_ref[0:48, :], wx)
    results = []
    for x in range(wx):
        scales = scales_top(wx, wy, x, kp_ref, misc_d)[1]
        flux = [delta[x][48 * s : 48 * s + 48] * scales[s] for s in range(6)]
        visc = level_visc(misc_u[x : x + 1], visc_ref)
        arrived = up_ref[pl.ds(48 * x, 48), :].astype(F32)
        face = arrived + visc * (own[x] + penalty * l_ref[1, x * wy].astype(F32))
        results.append((flux, face * kp_ref[1, pl.ds(x * wy, 1), :]))
    return results


def turn_kernel(
    wx, wy, visc_ref, l_ref, kp_ref, diag_ref, parts_ref, my_ref, own_ref, c_ref, va_ref, vb_ref,
    v1a_ref, v1b_ref, v3_ref, swap0_in, swap1_in, swap2_in,
    vt_ref, vl_ref, v1_ref, yd_ref, yu_ref, inner_ref, outer_ref, down_ref, up_ref,
):
    z = l_ref.shape[3]
    arrive((swap0_in, swap1_in, swap2_in), yd_ref, yu_ref)
    xs = (0, wx - 1)
    results = y_vertex(wx, wy, xs, visc_ref, kp_ref, parts_ref, my_ref, own_ref, v3_ref, yd_ref, yu_ref)
    sums_d, one_d, misc_d = read_tail(yd_ref, wx, 0)
    sums_u, one_u, misc_u = read_tail(yu_ref, wx, 1)
    edge_high, edge_low = misc_d[wx + 4 : 2 * wx + 4], misc_d[2 * wx + 4 : 3 * wx + 4]
    for n, (top, low, _, _) in enumerate(results):
        for p in range(2):
            vt_ref[n, p] = top[p]
            vl_ref[n, p] = low[p]
    top_one, low_one = results[1][2:]
    mine = tall(one_u) + low_one
    v1_ref[0] = mine
    v1_ref[1] = v1a_ref[0]
    for y in range(wy - 2):
        v1_ref[2 + y] = v1b_ref[y]
    v1_ref[wy] = v1a_ref[1] + top_one
    v1_ref[wy + 1] = tall(one_d)

    def plane(i, n, p):
        lines = [sums_u[i] + vl_ref[n, p], va_ref[0, i]]
        lines += [vb_ref[y, i] for y in range(wy - 2)]
        lines += [va_ref[1, i] + vt_ref[n, p], sums_d[i]]
        return merge(lines[1::2], lines[0::2])

    down_ref[pl.ds(0, 48), :] = yu_ref[pl.ds(48 * wx, 48), :]
    for y in range(wy):
        down_ref[pl.ds(48 + 48 * y, 48), :] = l_ref[0, y]
    down_ref[pl.ds(48 * (wy + 1), 48), :] = yd_ref[pl.ds(48 * wx, 48), :]
    diag = diag_ref[pl.ds(0, wy), :]
    high = diag.astype(BF).astype(F32)
    rim = [plane(0, 0, 0), high, edge_high[0:1], diag - high, edge_low[0:1]]
    rim += [misc_u[wx : wx + 1], kp_ref[0, 0:wy], misc_d[wx : wx + 1]]
    put_tail(down_ref, 48 * (wy + 2), rim)
    corner = (wx - 1) * wy
    last_trace = yd_ref[pl.ds(48 * (wx - 1), 48), :]
    flux = dot(my_ref[pl.ds(48, 48), :], last_trace) * kp_ref[4, pl.ds(corner + wy - 1, 1), :]
    for y in range(wy):
        part = c_ref[1, corner + y]
        up_ref[pl.ds(48 * y, 48), :] = (part + flux if y == wy - 1 else part).astype(BF)
    last = pl.ds(corner, wy)
    rim = [plane(wx, 1, 1), mine, *one_d]
    rim += [misc_u[wx - 1 : wx], kp_ref[5, last], misc_d[wx + 1 : wx + 2]]
    rim += [misc_u[3 * wx - 1 : 3 * wx], kp_ref[2, last], misc_d[wx + 3 : wx + 4]]
    rim += [kp_ref[1, last], misc_d[wx - 1 : wx]]
    put_tail(up_ref, 48 * wy, rim)
    depart("gx", down_ref, up_ref, inner_ref, outer_ref)


def assemble_kernel(
    wx, wy, visc_ref, l_ref, kp_ref, diag_ref, parts_ref, mx_ref, my_ref, own_ref, c_ref,
    va_ref, vb_ref, v3_ref, vt_ref, vl_ref, yd_ref, yu_ref,
    r_ref, late_ref, v_ref, inv_ref, ownx_ref, mid,
):
    z = l_ref.shape[3]
    cells = wx * wy
    xs = tuple(range(1, wx - 1))
    results = y_vertex(wx, wy, xs, visc_ref, kp_ref, parts_ref, my_ref, own_ref, v3_ref, yd_ref, yu_ref)
    faces = []
    for x, (flux, face) in enumerate(y_flux(wx, wy, visc_ref, l_ref, kp_ref, my_ref, own_ref, yd_ref, yu_ref)):
        faces.append(face)
        for s in range(6):
            mid[x, s] = flux[s]
    traces = [yu_ref[pl.ds(48 * wx, 48), :]] + [l_ref[0, y] for y in range(wy)] + [yd_ref[pl.ds(48 * wx, 48), :]]
    ownx_ref[...] = dot(mx_ref[pl.ds(240, 144), :], wide(traces))

    def contrib(slot, x, y):
        here = c_ref[slot, x * wy + y]
        if y < wy - 1:
            return here
        return here + mid[x, slot]

    for x in range(wx):
        for y in range(wy):
            col = pl.ds(x * wy + y, 48, stride=cells)
            behind = contrib(3, x, y - 1) if y else faces[x]
            ahead = contrib(0, x, y) + contrib(1, x - 1, y) if x else contrib(0, x, y)
            sides = [ahead, contrib(2, x, y) + behind, contrib(4, x, y) + z_prev(contrib(5, x, y))]
            for d in range(3):
                if x == wx - 1:
                    late_ref[d, y] = sides[d]
                elif d == 0 and x == 0:
                    late_ref[3, y] = sides[d]
                else:
                    r_ref[d, col, :] = sides[d]
    sums_d, one_d, misc_d = read_tail(yd_ref, wx, 0)
    sums_u, one_u, misc_u = read_tail(yu_ref, wx, 1)
    edge_diag = misc_d[wx + 4 : 2 * wx + 4] + misc_d[2 * wx + 4 : 3 * wx + 4]

    def brought(which, i):
        held = vl_ref if which else vt_ref
        terms = []
        for x, p in ((i, 0), (i - 1, 1)):
            if x in (0, wx - 1):
                terms.append(held[0 if x == 0 else 1, p])
            elif 0 < x < wx - 1:
                terms.append(results[x - 1][which][p])
        return sum(terms[1:], terms[0])

    for i in range(wx + 1):
        lines = [sums_u[i] + brought(1, i), va_ref[0, i]]
        lines += [vb_ref[y, i] for y in range(wy - 2)]
        lines += [va_ref[1, i] + brought(0, i), sums_d[i]]
        v_ref[i] = merge(lines[1::2], lines[0::2])
        if i < wx:
            parts = [jnp.broadcast_to(diag_ref[pl.ds(i * wy + y, 1), :], (4, z)) for y in range(wy)]
            parts += [jnp.broadcast_to(edge_diag[i : i + 1], (4, z)), jnp.zeros((4, z), F32)]
            inv_ref[i] = reciprocal(tall(parts))


def reciprocal(diag):
    present = diag > 0.0
    return jnp.where(present, (1.0 / gain) / jnp.where(present, diag, 1.0), 0.0)


def final_kernel(
    wx, wy, visc_ref, l_ref, kp_ref, parts_ref, mx_ref, ownx_ref, r_in, late_ref, v_ref, inv_ref, v1_ref,
    yd_ref, yu_ref, outer_in, inner_in, out_hbm, r_ref, held, fix, sems,
):
    here, last = lax.axis_index("gx"), lax.axis_size("gx") - 1

    def from_high(start, size):
        rows = pl.ds(start, size)
        value = jnp.where(even("gx"), inner_in[rows, :], outer_in[rows, :])
        return jnp.where(here < last, value, jnp.zeros_like(value))

    def from_low(start, size):
        rows = pl.ds(start, size)
        value = jnp.where(even("gx"), outer_in[rows, :], inner_in[rows, :])
        return jnp.where(here > 0, value, jnp.zeros_like(value))

    cells, z = wx * wy, l_ref.shape[3]
    rows = v_ref.shape[1]
    row = lambda i, col: kp_ref[i, pl.ds(col, 1), :]
    traces = [from_high(48 * j, 48) for j in range(wy + 2)]
    delta = dot(mx_ref[pl.ds(288, 96), :], wide(traces))
    rim_x = from_high(48 * (wy + 2), tail_rows(rows + 3 * wy + 4)).astype(F32)
    rim_l = from_low(48 * wy, tail_rows(rows + 32 + 3 * (wy + 2) - 1)).astype(F32)
    misc_d = read_tail(yd_ref, wx, 0)[2]
    misc_u = read_tail(yu_ref, wx, 1)[2]
    flags_high = rim_x[rows + 2 * (wy + 1) : rows + 3 * wy + 4]
    corner = (wx - 1) * wy
    arrived = [from_low(48 * y, 48) for y in range(wy)]
    arrived_corners = slot_corners(arrived, parts_ref, 1)
    codes = rim_l[rows + 32 : rows + 32 + wy + 2]
    keep_z = rim_l[rows + 32 + wy + 2 : rows + 32 + 2 * (wy + 2)]
    keep_y = rim_l[rows + 32 + 2 * (wy + 2) : rows + 32 + 3 * (wy + 2) - 1]
    low_visc = level_visc(codes, visc_ref)
    low_keep_z = z_next(keep_z)
    lines = [[], [], []]
    high_scales = []
    del r_in
    for j in range(-1, wy + 1):
        n = j + 1
        part = delta[:, z * n : z * n + z]
        flag = flags_high[n : n + 1]
        if j < 0:
            visc = level_visc(misc_u[wx - 1 : wx], visc_ref)
            kz = misc_u[3 * wx - 1 : 3 * wx]
            keeps = [misc_u[2 * wx - 1 : 2 * wx], flag, None, row(1, corner), kz, z_next(kz)]
        elif j < wy:
            here = corner + j
            visc = row(4, here)
            high_y = row(1, here + 1) if j < wy - 1 else misc_d[wx - 1 : wx]
            keeps = [row(0, here), flag, row(1, here), high_y, row(2, here), row(3, here)]
        else:
            visc = level_visc(misc_d[wx + 1 : wx + 2], visc_ref)
            kz = misc_d[wx + 3 : wx + 4]
            keeps = [misc_d[wx + 2 : wx + 3], flag, misc_d[wx - 1 : wx], None, kz, z_next(kz)]
        scales = [None if keep is None else visc * keep for keep in keeps]
        corners = scaled_corners(part, scales)
        one = v1_ref[n] * flag
        lines[0].append(corners[0])
        lines[1].append(corners[1] + one[0:8] + z_prev(one[8:16]))
        high_scales.append(scales)
        own = ownx_ref[:, pl.ds(z * n, z)]
        visc = low_visc[n : n + 1]
        flag = misc_u[wx : wx + 1] if j < 0 else misc_d[wx : wx + 1] if j == wy else row(0, j)
        scales = [
            None, visc * flag, None if j < 0 else visc * keep_y[j : j + 1],
            None if j == wy else visc * keep_y[j + 1 : j + 2], visc * keep_z[n : n + 1], visc * low_keep_z[n : n + 1],
        ]
        corners = scaled_corners(own[48:144], scales, (1,))[0]
        if 0 <= j < wy:
            one = arrived_corners[j] * flag
            lines[2].append(corners + one[0:8] + z_prev(one[8:16]))
            face = (arrived[j].astype(F32) + visc * (own[0:48] + penalty * l_ref[0, j].astype(F32))) * flag
            r_ref[0, pl.ds(j, 48, stride=cells), :] = late_ref[3, j] + face
        else:
            at = rows + (0 if j < 0 else 16)
            one = rim_l[at : at + 16] * flag
            lines[2].append(corners + one[0:8] + z_prev(one[8:16]))
    low, before, first = [merge(part[1::2], part[0::2]) for part in lines]
    top = v_ref[wx] + before + rim_x[0:rows]
    values = [(v_ref[0] + first + rim_l[0:rows]) * inv_ref[0]]
    values += [v_ref[i] * inv_ref[i] for i in range(1, wx - 1)]
    values += [(v_ref[wx - 1] + low) * inv_ref[wx - 1]]
    diag = rim_x[rows : rows + wy + 1] + rim_x[rows + wy + 1 : rows + 2 * (wy + 1)]
    parts = [jnp.broadcast_to(diag[j : j + 1], (4, z)) for j in range(wy + 1)]
    values += [top * reciprocal(tall(parts + [jnp.zeros((rows - 4 * (wy + 1), z), F32)]))]
    high = [pltpu.roll(value, rows - 4, 0) for value in values]
    for i in range(wx + 1):
        fix[0, pl.ds(4 * wy * i, 4 * wy), :] = values[i][0 : 4 * wy]
        fix[1, pl.ds(4 * wy * i, 4 * wy), :] = high[i][0 : 4 * wy]
    vertex = lambda c, p, q: fix[q, pl.ds(4 * wy * p + c, cells, stride=4), :]
    delta = columns(dot(mx_ref[pl.ds(0, 240), :], wide(traces[1 : wy + 1])), wy)
    behind = dot(mx_ref[pl.ds(96, 48), :], traces[0]) * high_scales[0][3]
    copies = []
    for d in range(3):
        for j in range(wy):
            scales = high_scales[j + 1]
            part = [delta[j][48 * i : 48 * i + 48] for i in range(5)]
            if d == 0:
                flux = part[0] * scales[0]
            elif d == 1:
                flux = part[1] * scales[2] + behind
                behind = part[2] * scales[3]
            else:
                flux = part[3] * scales[4] + z_prev(part[4] * scales[5])
            r_ref[d, pl.ds(corner + j, 48, stride=cells), :] = late_ref[d, j] + flux
        flags = kp_ref[d]
        for c in range(3):
            if d == 0:
                near = [vertex(c, 0, q) * flags for q in range(2)]
                far = [z_next(vertex(c, 0, q)) * flags for q in range(2)]
                corner_values = [[near[0], far[0]], [near[1], far[1]]]
            elif d == 1:
                corner_values = [[vertex(c, p, 0) * flags, z_next(vertex(c, p, 0)) * flags] for p in range(2)]
            else:
                corner_values = [[vertex(c, p, q) * flags for q in range(2)] for p in range(2)]
            lines = [between(corner_values[0][t], corner_values[1][t]) for t in range(2)]
            for a in range(4):
                for b, value in enumerate(between(lines[0][a], lines[1][a])):
                    at = pl.ds(cells * (16 * c + 4 * a + b), cells)
                    held[d, at, :] = (r_ref[d, at, :] + value).astype(BF)
        copies.append(pltpu.make_async_copy(held.at[d], out_hbm.at[d], sems.at[d]))
        copies[d].start()
    for copy in copies:
        copy.wait()


def call(body, args, outs, scratch, flops, hbm=False, aliases=None):
    if hbm:
        args = tuple(pltpu.with_memory_space_constraint(a, pltpu.HBM) for a in args)
    keywords = {}
    if aliases:
        spaces = [pltpu.HBM] + [pltpu.VMEM] * (len(outs) - 1)
        keywords = dict(out_specs=tuple(pl.BlockSpec(memory_space=space) for space in spaces), input_output_aliases=aliases)
    return pl.pallas_call(
        body,
        **keywords,
        in_specs=[pl.BlockSpec(memory_space=pltpu.HBM if hbm else pltpu.VMEM)] * len(args),
        out_shape=outs,
        scratch_shapes=scratch,
        cost_estimate=pl.CostEstimate(flops=flops, bytes_accessed=1000000, transcendentals=0),
        compiler_params=pltpu.CompilerParams(vmem_limit_bytes=16 * 1024 * 1024),
    )(*args)


def local(traces, dirichlet, visc_class, viscosity, coarse_diag, solve_map, flux_map):
    wx, wy, z = traces.shape[2:]
    cells = wx * wy
    rows = 8 * (wy // 2 + 1)
    per_hex = 2 * 384 * 288 * z
    parts = jnp.asarray(slot_table())
    vm = pltpu.VMEM
    bind = lambda body: functools.partial(body, wx, wy)
    y_message = vm((48 * wx + 48 + tail_rows(8 * ((wx + 2) // 2) + 8 + 3 * wx + 4), z), BF)
    x_message = vm((48 * (wy + 2) + tail_rows(rows + 3 * wy + 4), z), BF)

    (lifted, nat, flags, visc, diag, s_turned, f_map, parts, va, v1a, v3, *swaps) = call(
        bind(first_kernel),
        (
            viscosity, traces.reshape(3, 48 * cells, z), dirichlet.reshape(3, cells, z),
            visc_class.reshape(cells, z), coarse_diag.reshape(cells, z), solve_map.T, flux_map, parts,
        ),
        (
            vm((4, cells, 48, z), BF), vm((3, 48 * cells, z), F32), vm((6, cells, z), F32), vm((viscosity.shape[0], z), F32), vm((cells, z), F32),
            vm(solve_map.shape[::-1], BF), vm(flux_map.shape, BF), vm(parts.shape, BF),
            vm((2, wx + 1, 8, z), F32), vm((2, 16, z), F32), vm((wx, 32, z), F32),
            y_message, y_message, y_message,
        ),
        [
            y_message, y_message,
            vm((3, 48 * cells, z), BF), vm((3, cells, z), jnp.int32), vm((cells, z), jnp.int32),
            pltpu.SMEM(viscosity.shape, F32), pltpu.SemaphoreType.DMA((8,)),
        ],
        wx * per_hex, True,
    )
    swaps = [swap(message, "gy", "gx", k, 3) for k, message in enumerate(swaps)]
    c, vb, v1b, mx, my, own = call(
        bind(middle_kernel),
        (lifted, nat, flags, s_turned, f_map, parts),
        (
            vm((6, cells, 48, z), F32), vm((wy - 2, wx + 1, 8, z), F32), vm((wy - 2, 16, z), F32),
            vm((384, 48), BF), vm((384, 48), BF), vm((144, wx * z), F32),
        ),
        [vm((4, cells, 48, z), BF), vm((384, 288), BF), vm((288, 256), BF)], cells * per_hex,
    )
    vt, vl, v1, yd, yu, inner, outer = call(
        bind(turn_kernel),
        (
            visc, lifted, flags, diag, parts, my, own, c, va, vb, v1a, v1b, v3, *swaps,
        ),
        (
            vm((2, 2, 8, z), F32), vm((2, 2, 8, z), F32), vm((wy + 2, 16, z), F32),
            y_message, y_message, x_message, x_message,
        ),
        [x_message, x_message], 2 * per_hex,
    )
    inner = swap(inner, "gx", "gy", 0)
    outer = swap(outer, "gx", "gy", 1)
    residual, late, vs, inverse, ownx = call(
        bind(assemble_kernel),
        (
            visc, lifted, flags, diag, parts, mx, my, own, c, va, vb, v3, vt, vl, yd, yu,
        ),
        (
            vm((3, 48 * cells, z), F32), vm((4, wy, 48, z), F32), vm((wx + 1, rows, z), F32), vm((wx, rows, z), F32),
            vm((144, (wy + 2) * z), F32),
        ),
        [vm((wx, 6, 48, z), F32)], 4 * per_hex,
    )
    out, _ = call(
        bind(final_kernel),
        (
            visc, lifted, flags, parts, mx, ownx, residual, late, vs, inverse, v1, yd, yu, outer, inner,
        ),
        (jax.ShapeDtypeStruct((3, 48 * cells, z), BF), vm((3, 48 * cells, z), F32)),
        [vm((3, 48 * cells, z), BF), vm((2, 4 * wy * (wx + 1), z), F32), pltpu.SemaphoreType.DMA((3,))], 6 * per_hex,
        aliases={6: 1},
    )
    return out.reshape(traces.shape)


def solution(mesh):
    in_specs = (
        P(None, None, "gx", "gy", None),
        P(None, "gx", "gy", None),
        P("gx", "gy", None),
        P(),
        P("gx", "gy", None),
        P(),
        P(),
    )
    out_specs = P(None, None, "gx", "gy", None)
    return jax.shard_map(local, mesh=mesh, in_specs=in_specs, out_specs=out_specs, check_vma=False)
```

```python
import functools
import math

import jax
import jax.numpy as jnp
import ml_dtypes
import numpy as np
from jax import lax
from jax.experimental import pallas as pl
from jax.experimental.pallas import tpu as pltpu
from jax.sharding import PartitionSpec as P

penalty = 0.5
BF = jnp.bfloat16
F32 = jnp.float32
lift = 1.3264
gain = 1.3280711361297461


def swap(value, axis, other, first, step=2):
    count, width = lax.axis_size(axis), lax.axis_size(other)
    place = (lambda i, j: i * width + j) if (axis, other) == ("gx", "gy") else (lambda i, j: j * count + i)
    lows = list(range(first, count - 1, step))
    pairs = [(place(low, j), place(low + 1, j)) for low in lows for j in range(width)]
    alone = [i for i in range(count) if i not in lows and i - 1 not in lows]
    pairs += [(place(i, j), place(i, j + 1)) for i in alone for j in range(0, width - 1, 2)]
    return lax.ppermute(value, ("gx", "gy"), pairs + [(high, low) for low, high in pairs])


def even(axis):
    return lax.rem(lax.axis_index(axis), 2) == 0


def arrive(messages, down_ref, up_ref):
    here, last = lax.axis_index("gy"), lax.axis_size("gy") - 1
    values = [ref[...] for ref in messages]
    for ref, swap_of, present in ((down_ref, lax.rem(here, 3), here < last), (up_ref, lax.rem(here + 2, 3), here > 0)):
        value = jnp.where(swap_of == 0, values[0], jnp.where(swap_of == 1, values[1], values[2]))
        ref[...] = jnp.where(present, value, jnp.zeros_like(value))


def depart_three(down_ref, up_ref, messages):
    here = lax.rem(lax.axis_index("gy"), 3)
    for k, ref in enumerate(messages):
        choose(here == k, up_ref, down_ref, ref)


def depart(axis, down_ref, up_ref, inner_ref, outer_ref):
    choose(even(axis), up_ref, down_ref, inner_ref)
    choose(even(axis), down_ref, up_ref, outer_ref)


def choose(condition, yes_ref, no_ref, out_ref, present=None):
    value = jnp.where(condition, yes_ref[...], no_ref[...])
    out_ref[...] = value if present is None else jnp.where(present, value, jnp.zeros_like(value))


def corner_table():
    gll_points = [-1.0, -math.sqrt(0.2), math.sqrt(0.2), 1.0]
    table = np.zeros((16, 4), np.float64)
    for s in range(4):
        for t in range(4):
            for p in range(2):
                for q in range(2):
                    table[4 * s + t, 2 * p + q] = (
                        (1 + (2 * p - 1) * gll_points[s]) * (1 + (2 * q - 1) * gll_points[t]) / 4
                    )
    return table


def landing(face_slot, high_s, high_t):
    direction, outward = divmod(face_slot, 2)
    if direction == 0:
        return (outward, high_s, high_t)
    if direction == 1:
        return (high_s, outward, high_t)
    return (high_s, high_t, outward)


def gather_table():
    weights = lift * corner_table()
    table = np.zeros((32, 288), np.float64)
    for slot in range(6):
        for s in range(2):
            for t in range(2):
                p, q, r = landing(slot, s, t)
                for c in range(3):
                    cols = slot * 48 + 16 * c + np.arange(16)
                    table[16 * r + 8 * p + 4 * q + c, cols] += weights[:, 2 * s + t]
    return table.astype(ml_dtypes.bfloat16)


def slot_table():
    slots = np.split(gather_table(), 6, axis=1)
    rows = [
        np.r_[0:8, 16:24], np.r_[8:16, 24:32], np.arange(32), np.arange(32), np.arange(16), np.arange(16, 32),
    ]
    return np.concatenate([slot[kept] for slot, kept in zip(slots, rows)], axis=0)


slot_rows = (0, 16, 32, 64, 96, 112, 128)


def between(low, high):
    step = high - low
    return [low, low + (0.5 - 0.5 * math.sqrt(0.2)) * step, low + (0.5 + 0.5 * math.sqrt(0.2)) * step, high]


def lanes(shape):
    return lax.broadcasted_iota(jnp.int32, shape, len(shape) - 1)


def z_next(value):
    last = value.shape[-1] - 1
    return jnp.where(lanes(value.shape) < last, pltpu.roll(value, last, value.ndim - 1), 0.0)


def z_prev(value):
    return jnp.where(lanes(value.shape) > 0, pltpu.roll(value, 1, value.ndim - 1), 0.0)


def dot(left, right):
    return jnp.dot(left, right, preferred_element_type=F32)


def wide(parts):
    return jnp.concatenate(parts, axis=1)


def tall(parts):
    return jnp.concatenate(parts, axis=0)


def columns(rows, count):
    z = rows.shape[1] // count
    return [rows[:, z * h : z * h + z] for h in range(count)]


def elements(slots):
    return tall([wide([hexa[s] for hexa in slots]) for s in range(6)])


def vertex_part(flux, parts_ref):
    rows = []
    for s in range(6):
        first, size = slot_rows[s], slot_rows[s + 1] - slot_rows[s]
        rows.append(dot(parts_ref[pl.ds(first, size), :], flux[48 * s : 48 * s + 48].astype(BF)))
    rows[2:4] = [rows[2] + rows[3]]
    return tall(rows)


def turned_dot(left, right):
    return lax.dot_general(left, right, (((1,), (1,)), ((), ())), preferred_element_type=F32)


def product(f_ref, st_ref, slot):
    first = 0 if slot is None else 48 * slot
    flux = turned_dot(f_ref[...], st_ref[...] if slot is None else st_ref[pl.ds(first, 48), :])
    rows = lax.broadcasted_iota(jnp.int32, flux.shape, 0)
    return flux, flux + jnp.where(rows == lax.broadcasted_iota(jnp.int32, flux.shape, 1) + first, F32(penalty), F32(0.0))


def slot_corners(traces, parts_ref, slot):
    z = traces[0].shape[1]
    first, size = slot_rows[slot], slot_rows[slot + 1] - slot_rows[slot]
    rows = dot(parts_ref[pl.ds(first, size), :], wide([trace.astype(BF) for trace in traces]))
    return [rows[:, z * h : z * h + z] for h in range(len(traces))]


def settle(rows, p):
    return rows[8 * p : 8 * p + 8] + z_prev(rows[16 + 8 * p : 24 + 8 * p])


def scaled_corners(delta, scales, offsets=(0, 1)):
    shape = (8, delta.shape[1])
    blank = jnp.zeros((1, shape[1]), F32)
    y_scale = jnp.where(
        lax.broadcasted_iota(jnp.int32, shape, 0) < 4,
        blank if scales[2] is None else scales[2], blank if scales[3] is None else scales[3],
    )
    results = []
    for p in offsets:
        parts = []
        for r in range(2):
            at = 32 + 16 * r + 8 * p
            part = delta[at : at + 8] * y_scale + delta[at + 32 : at + 40] * scales[4 + r]
            if scales[p] is not None:
                part = part + delta[16 * p + 8 * r : 16 * p + 8 * r + 8] * scales[p]
            parts.append(part)
        results.append(parts[0] + z_prev(parts[1]))
    return results


def level_visc(code, visc_ref):
    visc = jnp.zeros(code.shape, F32)
    for level in range(visc_ref.shape[0]):
        visc = visc + jnp.where(code == F32(level + 1), visc_ref[pl.ds(level, 1), :], F32(0.0))
    return visc


def merge(even, odd):
    odd = tall(odd)
    return tall(even) + pltpu.roll(odd, odd.shape[0] - 4, 0)


def first_kernel(
    wx, wy, visc_hbm, t_hbm, dir_hbm, cls_hbm, diag_hbm, st_hbm, f_hbm, parts_hbm,
    l_ref, nat, kp_ref, visc_ref, diag_ref, st_ref, f_ref, parts_ref, v_ref, v1_ref, v3_ref,
    swap0_ref, swap1_ref, swap2_ref, down_ref, up_ref, t_ref, dir_ref, cls_ref, levels, sems,
):
    cells = wx * wy
    pairs = [
        (parts_hbm, parts_ref), (f_hbm, f_ref), (st_hbm, st_ref), (t_hbm, t_ref), (dir_hbm, dir_ref),
        (cls_hbm, cls_ref), (visc_hbm, levels), (diag_hbm, diag_ref),
    ]
    copies = [pltpu.make_async_copy(a, b, sems.at[i]) for i, (a, b) in enumerate(pairs)]
    for copy in copies:
        copy.start()
    diagonal = lax.broadcasted_iota(jnp.int32, (288, 288), 0) == lax.broadcasted_iota(jnp.int32, (288, 288), 1)
    diagonal = jnp.where(diagonal, F32(penalty), F32(0.0))
    copies[0].wait()
    own = tall([vertex_part(diagonal, parts_ref), diagonal[144:192]])
    copies[1].wait()
    left = tall([vertex_part(f_ref[...], parts_ref).astype(BF), f_ref[pl.ds(144, 48), :]])
    for copy in copies[2:5]:
        copy.wait()
    short = (turned_dot(left, st_ref[...]) + own).astype(BF)
    z = t_ref.shape[2]
    for d in range(3):
        keep = (1 - dir_ref[d]).astype(F32)
        kp_ref[d] = keep
        masked = t_ref[d].astype(F32).reshape(48, cells, z) * keep[None]
        nat[d] = masked.reshape(48 * cells, z)
        lay_out(wx, wy, d, nat, l_ref, True)
    kp_ref[3] = z_next(kp_ref[2])
    for copy in copies[5:]:
        copy.wait()
    for level in range(visc_ref.shape[0]):
        visc_ref[pl.ds(level, 1), :] = jnp.full((1, z), levels[level], F32)
    code = cls_ref[...].astype(F32) + 1.0
    kp_ref[4] = level_visc(code, visc_ref)
    kp_ref[5] = code
    row = lambda i, col: kp_ref[i, pl.ds(col, 1), :]
    corners = []
    for side, y in enumerate((0, wy - 1)):
        where = [(x, y) for x in range(wx)]
        slots, scales, left_out = known_hexes(wx, wy, where, (l_ref, None), kp_ref)
        rows = columns(dot(short if side else short[0:96], elements(slots)), wx)
        corners += known_corners(rows, scales, left_out)
        v1_ref[side] = rows[wx - 1][16:32] * row(4, (wx - 1) * wy + y)
    place = lax.broadcasted_iota(jnp.int32, (32, z), 0)
    lone = [part * row(4, x * wy + wy - 1) for x, part in enumerate(rows)]
    for x in range(wx):
        v3_ref[x] = jnp.where(lax.rem(place, 8) < 4, 0.0, lone[x][32:64])
    sums = [line_sums(corners[:wx]), line_sums(corners[wx:])]
    for side in range(2):
        for i in range(wx + 1):
            v_ref[side, i] = sums[side][i]
    corner = (wx - 1) * wy
    top = wy - 1
    for x in range(wx):
        down_ref[pl.ds(48 * x, 48), :] = l_ref[1, x * wy]
        up_ref[pl.ds(48 * x, 48), :] = lone[x][96:144].astype(BF)
    down_ref[pl.ds(48 * wx, 48), :] = l_ref[0, 0]
    up_ref[pl.ds(48 * wx, 48), :] = l_ref[0, top]
    flags = [row(1, x * wy) for x in range(wx)] + [row(0, 0), row(5, corner), row(0, corner), row(2, corner)]
    diag = tall([diag_ref[pl.ds(x * wy, 1), :] for x in range(wx)])
    high = diag.astype(BF).astype(F32)
    rim = pack(sums[0], 0) + pack([v1_ref[0, 0:8], v1_ref[0, 8:16]], 0) + flags + [high, diag - high]
    put_tail(down_ref, 48 * wx + 48, rim)
    flags = [row(kind, x * wy + top) for kind in (5, 0, 2) for x in range(wx)]
    rim = pack(sums[1], 1) + pack([v1_ref[1, 0:8], v1_ref[1, 8:16]], 1) + flags
    put_tail(up_ref, 48 * wx + 48, rim)
    depart_three(down_ref, up_ref, (swap0_ref, swap1_ref, swap2_ref))


def tail_rows(count):
    return -(-count // 16) * 16


def put_tail(ref, start, rows):
    count = sum(part.shape[0] for part in rows)
    full = ref.shape[0] - start
    if full > count:
        rows = rows + [jnp.zeros((full - count, rows[0].shape[1]), F32)]
    ref[pl.ds(start, full), :] = tall(rows).astype(BF)


def pack(parts, half):
    place = lax.broadcasted_iota(jnp.int32, parts[0].shape, 0)
    parts = parts + [jnp.zeros_like(parts[0])] * (len(parts) % 2)
    packed = []
    for low, high in zip(parts[0::2], parts[1::2]):
        if half:
            low = pltpu.roll(low, 4, 0)
        else:
            high = pltpu.roll(high, 4, 0)
        packed.append(jnp.where(place < 4, low, high))
    return packed


def unpack(packed, count, half):
    parts = []
    for n in range(count):
        part = packed[8 * (n // 2) : 8 * (n // 2) + 8]
        parts.append(part if n % 2 == half else pltpu.roll(part, 4, 0))
    return parts


def read_tail(ref, wx, half):
    start = 48 * wx + 48
    rows = ref[pl.ds(start, ref.shape[0] - start), :].astype(F32)
    size = 8 * ((wx + 2) // 2)
    return unpack(rows, wx + 1, half), unpack(rows[size : size + 8], 2, half), rows[size + 8 :]


def line_sums(corners):
    low, high = [part[0] for part in corners], [part[1] for part in corners]
    return [low[0]] + [low[x] + high[x - 1] for x in range(1, len(low))] + [high[-1]]


def early(wx, wy, d, x, y):
    return y in (0, wy - 1) or (d == 0 and x == 0) or (d == 1 and y == 1)


def lay_out(wx, wy, d, nat, l_ref, first):
    for x in range(wx):
        for y in range(wy):
            if early(wx, wy, d, x, y) == first:
                col = x * wy + y
                part = nat[d, pl.ds(col, 48, stride=wx * wy), :]
                l_ref[d, col] = part.astype(BF)
                if d == 2:
                    l_ref[3, col] = z_next(part).astype(BF)


def known_hexes(wx, wy, where, l_refs, kp_ref):
    z = l_refs[0].shape[3]
    nothing = jnp.zeros((48, z), BF)
    row = lambda i, col: kp_ref[i, pl.ds(col, 1), :]
    trace = lambda d, x, y: l_refs[0 if early(wx, wy, min(d, 2), x, y) else 1][d, x * wy + y]
    slots, scales, left_out = [], [], []
    for x, y in where:
        here = x * wy + y
        visc = row(4, here)
        last_x, last_y = x == wx - 1, y == wy - 1
        slots.append(
            [
                trace(0, x, y), nothing if last_x else trace(0, x + 1, y),
                trace(1, x, y), nothing if last_y else trace(1, x, y + 1),
                trace(2, x, y), trace(3, x, y),
            ]
        )
        scales.append(
            [
                visc * row(0, here), visc if last_x else visc * row(0, here + wy),
                visc * row(1, here), visc if last_y else visc * row(1, here + 1),
                visc * row(2, here), visc * row(3, here),
            ]
        )
        left_out.append(([1] if last_x else []) + ([3] if last_y else []))
    return slots, scales, left_out


def known_corners(vertex, scales, left_out):
    return [
        scaled_corners(part, [None if s in out else scale[s] for s in range(6)])
        for part, scale, out in zip(vertex, scales, left_out)
    ]


def middle_kernel(
    wx, wy, l_ref, nat, kp_ref, st_ref, f_ref, parts_ref,
    c_ref, v_ref, v1_ref, mx_ref, my_ref, own_ref, rest_ref, m_ref, lost_ref,
):
    for slot, ref in ((1, mx_ref), (3, my_ref)):
        bare, flux = product(f_ref, st_ref, slot)
        turned = tall([bare[0:48], bare[96:288], bare[48:96]]) if slot == 1 else bare
        ref[pl.ds(0, 288), :] = turned.astype(BF)
        ref[pl.ds(288, 96), :] = vertex_part(flux, parts_ref).astype(BF)
    flux = product(f_ref, st_ref, None)[1]
    m_ref[pl.ds(0, 288), :] = flux.astype(BF)
    m_ref[pl.ds(288, 96), :] = vertex_part(flux, parts_ref).astype(BF)
    lost_ref[...] = (flux - flux.astype(BF).astype(F32))[:, 0:256].astype(BF)
    for d in range(3):
        lay_out(wx, wy, d, nat, rest_ref, False)
    own_ref[...] = dot(
        tall([my_ref[pl.ds(144, 48), :], my_ref[pl.ds(288, 96), :]]), wide([l_ref[1, x * wy] for x in range(wx)])
    )
    for y in range(wy):
        inside = 0 < y < wy - 1
        where = [(x, y) for x in range(wx)]
        slots, scales, left_out = known_hexes(wx, wy, where, (l_ref, rest_ref), kp_ref)
        element = elements(slots)
        rows = dot(m_ref[...] if inside else m_ref[pl.ds(0, 288), :], element)
        lost = columns(dot(lost_ref[...], element[0:256]), wx)
        rows = columns(rows, wx)
        for x in range(wx):
            for s in range(6):
                part = slice(48 * s, 48 * s + 48)
                c_ref[s, x * wy + y] = (rows[x][part] + lost[x][part]) * scales[x][s]
        if inside:
            corners = known_corners([part[288:] for part in rows], scales, left_out)
            v1_ref[y - 1] = rows[wx - 1][304:320] * kp_ref[4, pl.ds((wx - 1) * wy + y, 1), :]
            for i, part in enumerate(line_sums(corners)):
                v_ref[y - 1, i] = part


def scales_top(wx, wy, x, kp_ref, misc_d):
    row = lambda i, col: kp_ref[i, pl.ds(col, 1), :]
    here = x * wy + wy - 1
    visc = row(4, here)
    scales = [
        visc * row(0, here), visc if x == wx - 1 else visc * row(0, here + wy), visc * row(1, here),
        visc * misc_d[x : x + 1], visc * row(2, here), visc * row(3, here),
    ]
    return visc, scales


def y_vertex(wx, wy, xs, visc_ref, kp_ref, parts_ref, my_ref, own_ref, v3_ref, down_ref, up_ref):
    z = kp_ref.shape[2]
    misc_d = read_tail(down_ref, wx, 0)[2]
    misc_u = read_tail(up_ref, wx, 1)[2]
    row = lambda i, col: kp_ref[i, pl.ds(col, 1), :]
    delta = dot(my_ref[pl.ds(288, 96), :], wide([down_ref[pl.ds(48 * x, 48), :] for x in xs]))
    arrived_corners = slot_corners([up_ref[pl.ds(48 * x, 48), :] for x in xs], parts_ref, 3)
    results = []
    for n, x in enumerate(xs):
        last = x == wx - 1
        part = delta[:, z * n : z * n + z]
        visc, scales = scales_top(wx, wy, x, kp_ref, misc_d)
        used = [None if (s == 1 and last) else scales[s] for s in range(6)]
        known = v3_ref[x] * misc_d[x : x + 1]
        top = [rows + settle(known, p) for p, rows in enumerate(scaled_corners(part, used))]
        top_one = part[16:32] * visc
        visc = level_visc(misc_u[x : x + 1], visc_ref)
        flag = row(1, x * wy)
        own = own_ref[:, pl.ds(z * x, z)]
        keep_z = misc_u[2 * wx + x : 2 * wx + x + 1]
        scales = [
            visc * misc_u[wx + x : wx + x + 1], None if last else visc * misc_u[wx + x + 1 : wx + x + 2],
            None, visc * flag, visc * keep_z, visc * z_next(keep_z),
        ]
        known = arrived_corners[n] * flag
        low = [rows + settle(known, p) for p, rows in enumerate(scaled_corners(own[48:144], scales))]
        results.append((top, low, top_one, own[64:80] * visc))
    return results


def y_flux(wx, wy, visc_ref, l_ref, kp_ref, my_ref, own_ref, down_ref, up_ref):
    misc_d = read_tail(down_ref, wx, 0)[2]
    misc_u = read_tail(up_ref, wx, 1)[2]
    delta = columns(dot(my_ref[pl.ds(0, 288), :], wide([down_ref[pl.ds(48 * x, 48), :] for x in range(wx)])), wx)
    own = columns(own_ref[0:48, :], wx)
    results = []
    for x in range(wx):
        scales = scales_top(wx, wy, x, kp_ref, misc_d)[1]
        flux = [delta[x][48 * s : 48 * s + 48] * scales[s] for s in range(6)]
        visc = level_visc(misc_u[x : x + 1], visc_ref)
        arrived = up_ref[pl.ds(48 * x, 48), :].astype(F32)
        face = arrived + visc * (own[x] + penalty * l_ref[1, x * wy].astype(F32))
        results.append((flux, face * kp_ref[1, pl.ds(x * wy, 1), :]))
    return results


def turn_kernel(
    wx, wy, visc_ref, l_ref, kp_ref, diag_ref, parts_ref, my_ref, own_ref, c_ref, va_ref, vb_ref,
    v1a_ref, v1b_ref, v3_ref, swap0_in, swap1_in, swap2_in,
    vt_ref, vl_ref, v1_ref, yd_ref, yu_ref, inner_ref, outer_ref, down_ref, up_ref,
):
    z = l_ref.shape[3]
    arrive((swap0_in, swap1_in, swap2_in), yd_ref, yu_ref)
    xs = (0, wx - 1)
    results = y_vertex(wx, wy, xs, visc_ref, kp_ref, parts_ref, my_ref, own_ref, v3_ref, yd_ref, yu_ref)
    sums_d, one_d, misc_d = read_tail(yd_ref, wx, 0)
    sums_u, one_u, misc_u = read_tail(yu_ref, wx, 1)
    edge_high, edge_low = misc_d[wx + 4 : 2 * wx + 4], misc_d[2 * wx + 4 : 3 * wx + 4]
    for n, (top, low, _, _) in enumerate(results):
        for p in range(2):
            vt_ref[n, p] = top[p]
            vl_ref[n, p] = low[p]
    top_one, low_one = results[1][2:]
    mine = tall(one_u) + low_one
    v1_ref[0] = mine
    v1_ref[1] = v1a_ref[0]
    for y in range(wy - 2):
        v1_ref[2 + y] = v1b_ref[y]
    v1_ref[wy] = v1a_ref[1] + top_one
    v1_ref[wy + 1] = tall(one_d)

    def plane(i, n, p):
        lines = [sums_u[i] + vl_ref[n, p], va_ref[0, i]]
        lines += [vb_ref[y, i] for y in range(wy - 2)]
        lines += [va_ref[1, i] + vt_ref[n, p], sums_d[i]]
        return merge(lines[1::2], lines[0::2])

    down_ref[pl.ds(0, 48), :] = yu_ref[pl.ds(48 * wx, 48), :]
    for y in range(wy):
        down_ref[pl.ds(48 + 48 * y, 48), :] = l_ref[0, y]
    down_ref[pl.ds(48 * (wy + 1), 48), :] = yd_ref[pl.ds(48 * wx, 48), :]
    diag = diag_ref[pl.ds(0, wy), :]
    high = diag.astype(BF).astype(F32)
    first = plane(0, 0, 0)
    rim = [first[4 * y : 4 * y + 3] for y in range(wy + 1)]
    rim += [high, edge_high[0:1], diag - high, edge_low[0:1]]
    rim += [misc_u[wx : wx + 1], kp_ref[0, 0:wy], misc_d[wx : wx + 1]]
    put_tail(down_ref, 48 * (wy + 2), rim)
    corner = (wx - 1) * wy
    last_trace = yd_ref[pl.ds(48 * (wx - 1), 48), :]
    flux = dot(my_ref[pl.ds(48, 48), :], last_trace) * kp_ref[4, pl.ds(corner + wy - 1, 1), :]
    for y in range(wy):
        part = c_ref[1, corner + y]
        up_ref[pl.ds(48 * y, 48), :] = (part + flux if y == wy - 1 else part).astype(BF)
    last = pl.ds(corner, wy)
    rim = [plane(wx, 1, 1), mine, *one_d]
    rim += [misc_u[wx - 1 : wx], kp_ref[5, last], misc_d[wx + 1 : wx + 2]]
    rim += [misc_u[3 * wx - 1 : 3 * wx], kp_ref[2, last], misc_d[wx + 3 : wx + 4]]
    rim += [kp_ref[1, last], misc_d[wx - 1 : wx]]
    put_tail(up_ref, 48 * wy, rim)
    depart("gx", down_ref, up_ref, inner_ref, outer_ref)


def assemble_kernel(
    wx, wy, visc_ref, l_ref, kp_ref, diag_ref, parts_ref, mx_ref, my_ref, own_ref, c_ref,
    va_ref, vb_ref, v3_ref, vt_ref, vl_ref, yd_ref, yu_ref,
    r_ref, late_ref, v_ref, inv_ref, ownx_ref, mid,
):
    z = l_ref.shape[3]
    cells = wx * wy
    xs = tuple(range(1, wx - 1))
    results = y_vertex(wx, wy, xs, visc_ref, kp_ref, parts_ref, my_ref, own_ref, v3_ref, yd_ref, yu_ref)
    faces = []
    for x, (flux, face) in enumerate(y_flux(wx, wy, visc_ref, l_ref, kp_ref, my_ref, own_ref, yd_ref, yu_ref)):
        faces.append(face)
        for s in range(6):
            mid[x, s] = flux[s]
    traces = [yu_ref[pl.ds(48 * wx, 48), :]] + [l_ref[0, y] for y in range(wy)] + [yd_ref[pl.ds(48 * wx, 48), :]]
    ownx_ref[...] = dot(mx_ref[pl.ds(240, 144), :], wide(traces))

    def contrib(slot, x, y):
        here = c_ref[slot, x * wy + y]
        if y < wy - 1:
            return here
        return here + mid[x, slot]

    for x in range(wx):
        for y in range(wy):
            col = pl.ds(x * wy + y, 48, stride=cells)
            behind = contrib(3, x, y - 1) if y else faces[x]
            ahead = contrib(0, x, y) + contrib(1, x - 1, y) if x else contrib(0, x, y)
            sides = [ahead, contrib(2, x, y) + behind, contrib(4, x, y) + z_prev(contrib(5, x, y))]
            for d in range(3):
                if x == wx - 1:
                    late_ref[d, y] = sides[d]
                elif d == 0 and x == 0:
                    late_ref[3, y] = sides[d]
                else:
                    r_ref[d, col, :] = sides[d]
    sums_d, one_d, misc_d = read_tail(yd_ref, wx, 0)
    sums_u, one_u, misc_u = read_tail(yu_ref, wx, 1)
    edge_diag = misc_d[wx + 4 : 2 * wx + 4] + misc_d[2 * wx + 4 : 3 * wx + 4]

    def brought(which, i):
        held = vl_ref if which else vt_ref
        terms = []
        for x, p in ((i, 0), (i - 1, 1)):
            if x in (0, wx - 1):
                terms.append(held[0 if x == 0 else 1, p])
            elif 0 < x < wx - 1:
                terms.append(results[x - 1][which][p])
        return sum(terms[1:], terms[0])

    for i in range(wx + 1):
        lines = [sums_u[i] + brought(1, i), va_ref[0, i]]
        lines += [vb_ref[y, i] for y in range(wy - 2)]
        lines += [va_ref[1, i] + brought(0, i), sums_d[i]]
        v_ref[i] = merge(lines[1::2], lines[0::2])
        if i < wx:
            parts = [jnp.broadcast_to(diag_ref[pl.ds(i * wy + y, 1), :], (4, z)) for y in range(wy)]
            parts += [jnp.broadcast_to(edge_diag[i : i + 1], (4, z)), jnp.zeros((4, z), F32)]
            inv_ref[i] = reciprocal(tall(parts))


def reciprocal(diag):
    present = diag > 0.0
    return jnp.where(present, (1.0 / gain) / jnp.where(present, diag, 1.0), 0.0)


def final_kernel(
    wx, wy, visc_ref, l_ref, kp_ref, parts_ref, mx_ref, ownx_ref, r_in, late_ref, v_ref, inv_ref, v1_ref,
    yd_ref, yu_ref, outer_in, inner_in, out_hbm, r_ref, held, fix, sems,
):
    here, last = lax.axis_index("gx"), lax.axis_size("gx") - 1

    def from_high(start, size):
        rows = pl.ds(start, size)
        value = jnp.where(even("gx"), inner_in[rows, :], outer_in[rows, :])
        return jnp.where(here < last, value, jnp.zeros_like(value))

    def from_low(start, size):
        rows = pl.ds(start, size)
        value = jnp.where(even("gx"), outer_in[rows, :], inner_in[rows, :])
        return jnp.where(here > 0, value, jnp.zeros_like(value))

    cells, z = wx * wy, l_ref.shape[3]
    rows = v_ref.shape[1]
    row = lambda i, col: kp_ref[i, pl.ds(col, 1), :]
    traces = [from_high(48 * j, 48) for j in range(wy + 2)]
    delta = dot(mx_ref[pl.ds(288, 96), :], wide(traces))
    rim_x = from_high(48 * (wy + 2), tail_rows(6 * wy + 7)).astype(F32)
    gap = jnp.zeros((1, z), F32)
    ahead = [part for j in range(wy + 1) for part in (rim_x[3 * j : 3 * j + 3], gap)]
    ahead = tall(ahead + [jnp.zeros((rows - 4 * (wy + 1), z), F32)])
    rim_x = rim_x[3 * (wy + 1) :]
    rim_l = from_low(48 * wy, tail_rows(rows + 32 + 3 * (wy + 2) - 1)).astype(F32)
    misc_d = read_tail(yd_ref, wx, 0)[2]
    misc_u = read_tail(yu_ref, wx, 1)[2]
    flags_high = rim_x[2 * (wy + 1) : 3 * wy + 4]
    corner = (wx - 1) * wy
    arrived = [from_low(48 * y, 48) for y in range(wy)]
    arrived_corners = slot_corners(arrived, parts_ref, 1)
    codes = rim_l[rows + 32 : rows + 32 + wy + 2]
    keep_z = rim_l[rows + 32 + wy + 2 : rows + 32 + 2 * (wy + 2)]
    keep_y = rim_l[rows + 32 + 2 * (wy + 2) : rows + 32 + 3 * (wy + 2) - 1]
    low_visc = level_visc(codes, visc_ref)
    low_keep_z = z_next(keep_z)
    lines = [[], [], []]
    high_scales = []
    del r_in
    for j in range(-1, wy + 1):
        n = j + 1
        part = delta[:, z * n : z * n + z]
        flag = flags_high[n : n + 1]
        if j < 0:
            visc = level_visc(misc_u[wx - 1 : wx], visc_ref)
            kz = misc_u[3 * wx - 1 : 3 * wx]
            keeps = [misc_u[2 * wx - 1 : 2 * wx], flag, None, row(1, corner), kz, z_next(kz)]
        elif j < wy:
            here = corner + j
            visc = row(4, here)
            high_y = row(1, here + 1) if j < wy - 1 else misc_d[wx - 1 : wx]
            keeps = [row(0, here), flag, row(1, here), high_y, row(2, here), row(3, here)]
        else:
            visc = level_visc(misc_d[wx + 1 : wx + 2], visc_ref)
            kz = misc_d[wx + 3 : wx + 4]
            keeps = [misc_d[wx + 2 : wx + 3], flag, misc_d[wx - 1 : wx], None, kz, z_next(kz)]
        scales = [None if keep is None else visc * keep for keep in keeps]
        corners = scaled_corners(part, scales)
        one = v1_ref[n] * flag
        lines[0].append(corners[0])
        lines[1].append(corners[1] + one[0:8] + z_prev(one[8:16]))
        high_scales.append(scales)
        own = ownx_ref[:, pl.ds(z * n, z)]
        visc = low_visc[n : n + 1]
        flag = misc_u[wx : wx + 1] if j < 0 else misc_d[wx : wx + 1] if j == wy else row(0, j)
        scales = [
            None, visc * flag, None if j < 0 else visc * keep_y[j : j + 1],
            None if j == wy else visc * keep_y[j + 1 : j + 2], visc * keep_z[n : n + 1], visc * low_keep_z[n : n + 1],
        ]
        corners = scaled_corners(own[48:144], scales, (1,))[0]
        if 0 <= j < wy:
            one = arrived_corners[j] * flag
            lines[2].append(corners + one[0:8] + z_prev(one[8:16]))
            face = (arrived[j].astype(F32) + visc * (own[0:48] + penalty * l_ref[0, j].astype(F32))) * flag
            r_ref[0, pl.ds(j, 48, stride=cells), :] = late_ref[3, j] + face
        else:
            at = rows + (0 if j < 0 else 16)
            one = rim_l[at : at + 16] * flag
            lines[2].append(corners + one[0:8] + z_prev(one[8:16]))
    low, before, first = [merge(part[1::2], part[0::2]) for part in lines]
    top = v_ref[wx] + before + ahead
    values = [(v_ref[0] + first + rim_l[0:rows]) * inv_ref[0]]
    values += [v_ref[i] * inv_ref[i] for i in range(1, wx - 1)]
    values += [(v_ref[wx - 1] + low) * inv_ref[wx - 1]]
    diag = rim_x[0 : wy + 1] + rim_x[wy + 1 : 2 * (wy + 1)]
    parts = [jnp.broadcast_to(diag[j : j + 1], (4, z)) for j in range(wy + 1)]
    values += [top * reciprocal(tall(parts + [jnp.zeros((rows - 4 * (wy + 1), z), F32)]))]
    high = [pltpu.roll(value, rows - 4, 0) for value in values]
    for i in range(wx + 1):
        fix[0, pl.ds(4 * wy * i, 4 * wy), :] = values[i][0 : 4 * wy]
        fix[1, pl.ds(4 * wy * i, 4 * wy), :] = high[i][0 : 4 * wy]
    vertex = lambda c, p, q: fix[q, pl.ds(4 * wy * p + c, cells, stride=4), :]
    delta = columns(dot(mx_ref[pl.ds(0, 240), :], wide(traces[1 : wy + 1])), wy)
    behind = dot(mx_ref[pl.ds(96, 48), :], traces[0]) * high_scales[0][3]
    copies = []
    for d in range(3):
        for j in range(wy):
            scales = high_scales[j + 1]
            part = [delta[j][48 * i : 48 * i + 48] for i in range(5)]
            if d == 0:
                flux = part[0] * scales[0]
            elif d == 1:
                flux = part[1] * scales[2] + behind
                behind = part[2] * scales[3]
            else:
                flux = part[3] * scales[4] + z_prev(part[4] * scales[5])
            r_ref[d, pl.ds(corner + j, 48, stride=cells), :] = late_ref[d, j] + flux
        flags = kp_ref[d]
        for c in range(3):
            if d == 0:
                near = [vertex(c, 0, q) * flags for q in range(2)]
                far = [z_next(vertex(c, 0, q)) * flags for q in range(2)]
                corner_values = [[near[0], far[0]], [near[1], far[1]]]
            elif d == 1:
                corner_values = [[vertex(c, p, 0) * flags, z_next(vertex(c, p, 0)) * flags] for p in range(2)]
            else:
                corner_values = [[vertex(c, p, q) * flags for q in range(2)] for p in range(2)]
            lines = [between(corner_values[0][t], corner_values[1][t]) for t in range(2)]
            for a in range(4):
                for b, value in enumerate(between(lines[0][a], lines[1][a])):
                    at = pl.ds(cells * (16 * c + 4 * a + b), cells)
                    held[d, at, :] = (r_ref[d, at, :] + value).astype(BF)
        copies.append(pltpu.make_async_copy(held.at[d], out_hbm.at[d], sems.at[d]))
        copies[d].start()
    for copy in copies:
        copy.wait()


def call(body, args, outs, scratch, flops, hbm=False, aliases=None):
    if hbm:
        args = tuple(pltpu.with_memory_space_constraint(a, pltpu.HBM) for a in args)
    keywords = {}
    if aliases:
        spaces = [pltpu.HBM] + [pltpu.VMEM] * (len(outs) - 1)
        keywords = dict(out_specs=tuple(pl.BlockSpec(memory_space=space) for space in spaces), input_output_aliases=aliases)
    return pl.pallas_call(
        body,
        **keywords,
        in_specs=[pl.BlockSpec(memory_space=pltpu.HBM if hbm else pltpu.VMEM)] * len(args),
        out_shape=outs,
        scratch_shapes=scratch,
        cost_estimate=pl.CostEstimate(flops=flops, bytes_accessed=1000000, transcendentals=0),
        compiler_params=pltpu.CompilerParams(vmem_limit_bytes=16 * 1024 * 1024),
    )(*args)


def local(traces, dirichlet, visc_class, viscosity, coarse_diag, solve_map, flux_map):
    wx, wy, z = traces.shape[2:]
    cells = wx * wy
    rows = 8 * (wy // 2 + 1)
    per_hex = 2 * 384 * 288 * z
    parts = jnp.asarray(slot_table())
    vm = pltpu.VMEM
    bind = lambda body: functools.partial(body, wx, wy)
    y_message = vm((48 * wx + 48 + tail_rows(8 * ((wx + 2) // 2) + 8 + 3 * wx + 4), z), BF)
    x_message = vm((48 * (wy + 2) + tail_rows(6 * wy + 7), z), BF)

    (lifted, nat, flags, visc, diag, s_turned, f_map, parts, va, v1a, v3, *swaps) = call(
        bind(first_kernel),
        (
            viscosity, traces.reshape(3, 48 * cells, z), dirichlet.reshape(3, cells, z),
            visc_class.reshape(cells, z), coarse_diag.reshape(cells, z), solve_map.T, flux_map, parts,
        ),
        (
            vm((4, cells, 48, z), BF), vm((3, 48 * cells, z), F32), vm((6, cells, z), F32), vm((viscosity.shape[0], z), F32), vm((cells, z), F32),
            vm(solve_map.shape[::-1], BF), vm(flux_map.shape, BF), vm(parts.shape, BF),
            vm((2, wx + 1, 8, z), F32), vm((2, 16, z), F32), vm((wx, 32, z), F32),
            y_message, y_message, y_message,
        ),
        [
            y_message, y_message,
            vm((3, 48 * cells, z), BF), vm((3, cells, z), jnp.int32), vm((cells, z), jnp.int32),
            pltpu.SMEM(viscosity.shape, F32), pltpu.SemaphoreType.DMA((8,)),
        ],
        wx * per_hex, True,
    )
    swaps = [swap(message, "gy", "gx", k, 3) for k, message in enumerate(swaps)]
    c, vb, v1b, mx, my, own = call(
        bind(middle_kernel),
        (lifted, nat, flags, s_turned, f_map, parts),
        (
            vm((6, cells, 48, z), F32), vm((wy - 2, wx + 1, 8, z), F32), vm((wy - 2, 16, z), F32),
            vm((384, 48), BF), vm((384, 48), BF), vm((144, wx * z), F32),
        ),
        [vm((4, cells, 48, z), BF), vm((384, 288), BF), vm((288, 256), BF)], cells * per_hex,
    )
    vt, vl, v1, yd, yu, inner, outer = call(
        bind(turn_kernel),
        (
            visc, lifted, flags, diag, parts, my, own, c, va, vb, v1a, v1b, v3, *swaps,
        ),
        (
            vm((2, 2, 8, z), F32), vm((2, 2, 8, z), F32), vm((wy + 2, 16, z), F32),
            y_message, y_message, x_message, x_message,
        ),
        [x_message, x_message], 2 * per_hex,
    )
    inner = swap(inner, "gx", "gy", 0)
    outer = swap(outer, "gx", "gy", 1)
    residual, late, vs, inverse, ownx = call(
        bind(assemble_kernel),
        (
            visc, lifted, flags, diag, parts, mx, my, own, c, va, vb, v3, vt, vl, yd, yu,
        ),
        (
            vm((3, 48 * cells, z), F32), vm((4, wy, 48, z), F32), vm((wx + 1, rows, z), F32), vm((wx, rows, z), F32),
            vm((144, (wy + 2) * z), F32),
        ),
        [vm((wx, 6, 48, z), F32)], 4 * per_hex,
    )
    out, _ = call(
        bind(final_kernel),
        (
            visc, lifted, flags, parts, mx, ownx, residual, late, vs, inverse, v1, yd, yu, outer, inner,
        ),
        (jax.ShapeDtypeStruct((3, 48 * cells, z), BF), vm((3, 48 * cells, z), F32)),
        [vm((3, 48 * cells, z), BF), vm((2, 4 * wy * (wx + 1), z), F32), pltpu.SemaphoreType.DMA((3,))], 6 * per_hex,
        aliases={6: 1},
    )
    return out.reshape(traces.shape)


def solution(mesh):
    in_specs = (
        P(None, None, "gx", "gy", None),
        P(None, "gx", "gy", None),
        P("gx", "gy", None),
        P(),
        P("gx", "gy", None),
        P(),
        P(),
    )
    out_specs = P(None, None, "gx", "gy", None)
    return jax.shard_map(local, mesh=mesh, in_specs=in_specs, out_specs=out_specs, check_vma=False)
```

```python
import functools
import math

import jax
import jax.numpy as jnp
import ml_dtypes
import numpy as np
from jax import lax
from jax.experimental import pallas as pl
from jax.experimental.pallas import tpu as pltpu
from jax.sharding import PartitionSpec as P

penalty = 0.5
BF = jnp.bfloat16
F32 = jnp.float32
lift = 1.3264
gain = 1.3280711361297461


def swap(value, axis, other, first, step=2):
    count, width = lax.axis_size(axis), lax.axis_size(other)
    place = (lambda i, j: i * width + j) if (axis, other) == ("gx", "gy") else (lambda i, j: j * count + i)
    lows = list(range(first, count - 1, step))
    pairs = [(place(low, j), place(low + 1, j)) for low in lows for j in range(width)]
    alone = [i for i in range(count) if i not in lows and i - 1 not in lows]
    pairs += [(place(i, j), place(i, j + 1)) for i in alone for j in range(0, width - 1, 2)]
    return lax.ppermute(value, ("gx", "gy"), pairs + [(high, low) for low, high in pairs])


def even(axis):
    return lax.rem(lax.axis_index(axis), 2) == 0


def arrive(messages, down_ref, up_ref):
    here, last = lax.axis_index("gy"), lax.axis_size("gy") - 1
    values = [ref[...] for ref in messages]
    for ref, swap_of, present in ((down_ref, lax.rem(here, 3), here < last), (up_ref, lax.rem(here + 2, 3), here > 0)):
        value = jnp.where(swap_of == 0, values[0], jnp.where(swap_of == 1, values[1], values[2]))
        ref[...] = jnp.where(present, value, jnp.zeros_like(value))


def depart_three(down_ref, up_ref, messages):
    here = lax.rem(lax.axis_index("gy"), 3)
    for k, ref in enumerate(messages):
        choose(here == k, up_ref, down_ref, ref)


def depart(axis, down_ref, up_ref, inner_ref, outer_ref):
    choose(even(axis), up_ref, down_ref, inner_ref)
    choose(even(axis), down_ref, up_ref, outer_ref)


def choose(condition, yes_ref, no_ref, out_ref, present=None):
    value = jnp.where(condition, yes_ref[...], no_ref[...])
    out_ref[...] = value if present is None else jnp.where(present, value, jnp.zeros_like(value))


def corner_table():
    gll_points = [-1.0, -math.sqrt(0.2), math.sqrt(0.2), 1.0]
    table = np.zeros((16, 4), np.float64)
    for s in range(4):
        for t in range(4):
            for p in range(2):
                for q in range(2):
                    table[4 * s + t, 2 * p + q] = (
                        (1 + (2 * p - 1) * gll_points[s]) * (1 + (2 * q - 1) * gll_points[t]) / 4
                    )
    return table


def landing(face_slot, high_s, high_t):
    direction, outward = divmod(face_slot, 2)
    if direction == 0:
        return (outward, high_s, high_t)
    if direction == 1:
        return (high_s, outward, high_t)
    return (high_s, high_t, outward)


def gather_table():
    weights = lift * corner_table()
    table = np.zeros((32, 288), np.float64)
    for slot in range(6):
        for s in range(2):
            for t in range(2):
                p, q, r = landing(slot, s, t)
                for c in range(3):
                    cols = slot * 48 + 16 * c + np.arange(16)
                    table[16 * r + 8 * p + 4 * q + c, cols] += weights[:, 2 * s + t]
    return table.astype(ml_dtypes.bfloat16)


def slot_table():
    slots = np.split(gather_table(), 6, axis=1)
    rows = [
        np.r_[0:8, 16:24], np.r_[8:16, 24:32], np.arange(32), np.arange(32), np.arange(16), np.arange(16, 32),
    ]
    return np.concatenate([slot[kept] for slot, kept in zip(slots, rows)], axis=0)


slot_rows = (0, 16, 32, 64, 96, 112, 128)


def between(low, high):
    step = high - low
    return [low, low + (0.5 - 0.5 * math.sqrt(0.2)) * step, low + (0.5 + 0.5 * math.sqrt(0.2)) * step, high]


def lanes(shape):
    return lax.broadcasted_iota(jnp.int32, shape, len(shape) - 1)


def z_next(value):
    last = value.shape[-1] - 1
    return jnp.where(lanes(value.shape) < last, pltpu.roll(value, last, value.ndim - 1), 0.0)


def z_prev(value):
    return jnp.where(lanes(value.shape) > 0, pltpu.roll(value, 1, value.ndim - 1), 0.0)


def dot(left, right):
    return jnp.dot(left, right, preferred_element_type=F32)


def wide(parts):
    return jnp.concatenate(parts, axis=1)


def tall(parts):
    return jnp.concatenate(parts, axis=0)


def columns(rows, count):
    z = rows.shape[1] // count
    return [rows[:, z * h : z * h + z] for h in range(count)]


def elements(slots):
    return tall([wide([hexa[s] for hexa in slots]) for s in range(6)])


def vertex_part(flux, parts_ref):
    rows = []
    for s in range(6):
        first, size = slot_rows[s], slot_rows[s + 1] - slot_rows[s]
        rows.append(dot(parts_ref[pl.ds(first, size), :], flux[48 * s : 48 * s + 48].astype(BF)))
    rows[2:4] = [rows[2] + rows[3]]
    return tall(rows)


def turned_dot(left, right):
    return lax.dot_general(left, right, (((1,), (1,)), ((), ())), preferred_element_type=F32)


def product(f_ref, st_ref, slot):
    first = 0 if slot is None else 48 * slot
    flux = turned_dot(f_ref[...], st_ref[...] if slot is None else st_ref[pl.ds(first, 48), :])
    rows = lax.broadcasted_iota(jnp.int32, flux.shape, 0)
    return flux, flux + jnp.where(rows == lax.broadcasted_iota(jnp.int32, flux.shape, 1) + first, F32(penalty), F32(0.0))


def slot_corners(traces, parts_ref, slot):
    z = traces[0].shape[1]
    first, size = slot_rows[slot], slot_rows[slot + 1] - slot_rows[slot]
    rows = dot(parts_ref[pl.ds(first, size), :], wide([trace.astype(BF) for trace in traces]))
    return [rows[:, z * h : z * h + z] for h in range(len(traces))]


def settle(rows, p):
    return rows[8 * p : 8 * p + 8] + z_prev(rows[16 + 8 * p : 24 + 8 * p])


def scaled_corners(delta, scales, offsets=(0, 1)):
    shape = (8, delta.shape[1])
    blank = jnp.zeros((1, shape[1]), F32)
    y_scale = jnp.where(
        lax.broadcasted_iota(jnp.int32, shape, 0) < 4,
        blank if scales[2] is None else scales[2], blank if scales[3] is None else scales[3],
    )
    results = []
    for p in offsets:
        parts = []
        for r in range(2):
            at = 32 + 16 * r + 8 * p
            part = delta[at : at + 8] * y_scale + delta[at + 32 : at + 40] * scales[4 + r]
            if scales[p] is not None:
                part = part + delta[16 * p + 8 * r : 16 * p + 8 * r + 8] * scales[p]
            parts.append(part)
        results.append(parts[0] + z_prev(parts[1]))
    return results


def level_visc(code, visc_ref):
    visc = jnp.zeros(code.shape, F32)
    for level in range(visc_ref.shape[0]):
        visc = visc + jnp.where(code == F32(level + 1), visc_ref[pl.ds(level, 1), :], F32(0.0))
    return visc


def merge(even, odd):
    odd = tall(odd)
    return tall(even) + pltpu.roll(odd, odd.shape[0] - 4, 0)


def first_kernel(
    wx, wy, visc_hbm, t_hbm, dir_hbm, cls_hbm, diag_hbm, st_hbm, f_hbm, parts_hbm,
    l_ref, nat, kp_ref, visc_ref, diag_ref, st_ref, f_ref, parts_ref, v_ref, v1_ref, v3_ref,
    swap0_ref, swap1_ref, swap2_ref, down_ref, up_ref, t_ref, dir_ref, cls_ref, levels, sems,
):
    cells = wx * wy
    pairs = [
        (parts_hbm, parts_ref), (f_hbm, f_ref), (st_hbm, st_ref), (t_hbm, t_ref), (dir_hbm, dir_ref),
        (cls_hbm, cls_ref), (visc_hbm, levels), (diag_hbm, diag_ref),
    ]
    copies = [pltpu.make_async_copy(a, b, sems.at[i]) for i, (a, b) in enumerate(pairs)]
    for copy in copies:
        copy.start()
    diagonal = lax.broadcasted_iota(jnp.int32, (288, 288), 0) == lax.broadcasted_iota(jnp.int32, (288, 288), 1)
    diagonal = jnp.where(diagonal, F32(penalty), F32(0.0))
    copies[0].wait()
    own = tall([vertex_part(diagonal, parts_ref), diagonal[144:192]])
    copies[1].wait()
    left = tall([vertex_part(f_ref[...], parts_ref).astype(BF), f_ref[pl.ds(144, 48), :]])
    for copy in copies[2:5]:
        copy.wait()
    short = (turned_dot(left, st_ref[...]) + own).astype(BF)
    z = t_ref.shape[2]
    for d in range(3):
        keep = (1 - dir_ref[d]).astype(F32)
        kp_ref[d] = keep
        masked = t_ref[d].astype(F32).reshape(48, cells, z) * keep[None]
        nat[d] = masked.reshape(48 * cells, z)
        lay_out(wx, wy, d, nat, l_ref, True)
    kp_ref[3] = z_next(kp_ref[2])
    for copy in copies[5:]:
        copy.wait()
    for level in range(visc_ref.shape[0]):
        visc_ref[pl.ds(level, 1), :] = jnp.full((1, z), levels[level], F32)
    code = cls_ref[...].astype(F32) + 1.0
    kp_ref[4] = level_visc(code, visc_ref)
    kp_ref[5] = code
    row = lambda i, col: kp_ref[i, pl.ds(col, 1), :]
    corners = []
    for side, y in enumerate((0, wy - 1)):
        where = [(x, y) for x in range(wx)]
        slots, scales, left_out = known_hexes(wx, wy, where, (l_ref, None), kp_ref)
        rows = columns(dot(short if side else short[0:96], elements(slots)), wx)
        corners += known_corners(rows, scales, left_out)
        v1_ref[side] = rows[wx - 1][16:32] * row(4, (wx - 1) * wy + y)
    place = lax.broadcasted_iota(jnp.int32, (32, z), 0)
    lone = [part * row(4, x * wy + wy - 1) for x, part in enumerate(rows)]
    for x in range(wx):
        v3_ref[x] = jnp.where(lax.rem(place, 8) < 4, 0.0, lone[x][32:64])
    sums = [line_sums(corners[:wx]), line_sums(corners[wx:])]
    for side in range(2):
        for i in range(wx + 1):
            v_ref[side, i] = sums[side][i]
    corner = (wx - 1) * wy
    top = wy - 1
    for x in range(wx):
        down_ref[pl.ds(48 * x, 48), :] = l_ref[1, x * wy]
        up_ref[pl.ds(48 * x, 48), :] = lone[x][96:144].astype(BF)
    down_ref[pl.ds(48 * wx, 48), :] = l_ref[0, 0]
    up_ref[pl.ds(48 * wx, 48), :] = l_ref[0, top]
    flags = [row(1, x * wy) for x in range(wx)] + [row(0, 0), row(5, corner), row(0, corner), row(2, corner)]
    diag = tall([diag_ref[pl.ds(x * wy, 1), :] for x in range(wx)])
    high = diag.astype(BF).astype(F32)
    rim = pack(sums[0], 0) + pack([v1_ref[0, 0:8], v1_ref[0, 8:16]], 0) + flags + [high, diag - high]
    put_tail(down_ref, 48 * wx + 48, rim)
    flags = [row(kind, x * wy + top) for kind in (5, 0, 2) for x in range(wx)]
    rim = pack(sums[1], 1) + pack([v1_ref[1, 0:8], v1_ref[1, 8:16]], 1) + flags
    put_tail(up_ref, 48 * wx + 48, rim)
    depart_three(down_ref, up_ref, (swap0_ref, swap1_ref, swap2_ref))


def tail_rows(count):
    return -(-count // 16) * 16


def put_tail(ref, start, rows):
    count = sum(part.shape[0] for part in rows)
    full = ref.shape[0] - start
    if full > count:
        rows = rows + [jnp.zeros((full - count, rows[0].shape[1]), F32)]
    ref[pl.ds(start, full), :] = tall(rows).astype(BF)


def pack(parts, half):
    place = lax.broadcasted_iota(jnp.int32, parts[0].shape, 0)
    parts = parts + [jnp.zeros_like(parts[0])] * (len(parts) % 2)
    packed = []
    for low, high in zip(parts[0::2], parts[1::2]):
        if half:
            low = pltpu.roll(low, 4, 0)
        else:
            high = pltpu.roll(high, 4, 0)
        packed.append(jnp.where(place < 4, low, high))
    return packed


def unpack(packed, count, half):
    parts = []
    for n in range(count):
        part = packed[8 * (n // 2) : 8 * (n // 2) + 8]
        parts.append(part if n % 2 == half else pltpu.roll(part, 4, 0))
    return parts


def read_tail(ref, wx, half):
    start = 48 * wx + 48
    rows = ref[pl.ds(start, ref.shape[0] - start), :].astype(F32)
    size = 8 * ((wx + 2) // 2)
    return unpack(rows, wx + 1, half), unpack(rows[size : size + 8], 2, half), rows[size + 8 :]


def line_sums(corners):
    low, high = [part[0] for part in corners], [part[1] for part in corners]
    return [low[0]] + [low[x] + high[x - 1] for x in range(1, len(low))] + [high[-1]]


def early(wx, wy, d, x, y):
    return y in (0, wy - 1) or (d == 0 and x == 0) or (d == 1 and y == 1)


def lay_out(wx, wy, d, nat, l_ref, first):
    for x in range(wx):
        for y in range(wy):
            if early(wx, wy, d, x, y) == first:
                col = x * wy + y
                part = nat[d, pl.ds(col, 48, stride=wx * wy), :]
                l_ref[d, col] = part.astype(BF)
                if d == 2:
                    l_ref[3, col] = z_next(part).astype(BF)


def known_hexes(wx, wy, where, l_refs, kp_ref):
    z = l_refs[0].shape[3]
    nothing = jnp.zeros((48, z), BF)
    row = lambda i, col: kp_ref[i, pl.ds(col, 1), :]
    trace = lambda d, x, y: l_refs[0 if early(wx, wy, min(d, 2), x, y) else 1][d, x * wy + y]
    slots, scales, left_out = [], [], []
    for x, y in where:
        here = x * wy + y
        visc = row(4, here)
        last_x, last_y = x == wx - 1, y == wy - 1
        slots.append(
            [
                trace(0, x, y), nothing if last_x else trace(0, x + 1, y),
                trace(1, x, y), nothing if last_y else trace(1, x, y + 1),
                trace(2, x, y), trace(3, x, y),
            ]
        )
        scales.append(
            [
                visc * row(0, here), visc if last_x else visc * row(0, here + wy),
                visc * row(1, here), visc if last_y else visc * row(1, here + 1),
                visc * row(2, here), visc * row(3, here),
            ]
        )
        left_out.append(([1] if last_x else []) + ([3] if last_y else []))
    return slots, scales, left_out


def known_corners(vertex, scales, left_out):
    return [
        scaled_corners(part, [None if s in out else scale[s] for s in range(6)])
        for part, scale, out in zip(vertex, scales, left_out)
    ]


def middle_kernel(
    wx, wy, l_ref, nat, kp_ref, st_ref, f_ref, parts_ref,
    c_ref, v_ref, v1_ref, mx_ref, my_ref, own_ref, rest_ref, m_ref, lost_ref,
):
    for slot, ref in ((1, mx_ref), (3, my_ref)):
        bare, flux = product(f_ref, st_ref, slot)
        turned = tall([bare[0:48], bare[96:288], bare[48:96]]) if slot == 1 else bare
        ref[pl.ds(0, 288), :] = turned.astype(BF)
        ref[pl.ds(288, 96), :] = vertex_part(flux, parts_ref).astype(BF)
    flux = product(f_ref, st_ref, None)[1]
    m_ref[pl.ds(0, 288), :] = flux.astype(BF)
    m_ref[pl.ds(288, 96), :] = vertex_part(flux, parts_ref).astype(BF)
    lost_ref[...] = (flux - flux.astype(BF).astype(F32))[:, 0:256].astype(BF)
    for d in range(3):
        lay_out(wx, wy, d, nat, rest_ref, False)
    own_ref[...] = dot(
        tall([my_ref[pl.ds(144, 48), :], my_ref[pl.ds(288, 96), :]]), wide([l_ref[1, x * wy] for x in range(wx)])
    )
    for y in range(wy):
        inside = 0 < y < wy - 1
        where = [(x, y) for x in range(wx)]
        slots, scales, left_out = known_hexes(wx, wy, where, (l_ref, rest_ref), kp_ref)
        element = elements(slots)
        rows = dot(m_ref[...] if inside else m_ref[pl.ds(0, 288), :], element)
        lost = columns(dot(lost_ref[...], element[0:256]), wx)
        rows = columns(rows, wx)
        for x in range(wx):
            for s in range(6):
                part = slice(48 * s, 48 * s + 48)
                c_ref[s, x * wy + y] = (rows[x][part] + lost[x][part]) * scales[x][s]
        if inside:
            corners = known_corners([part[288:] for part in rows], scales, left_out)
            v1_ref[y - 1] = rows[wx - 1][304:320] * kp_ref[4, pl.ds((wx - 1) * wy + y, 1), :]
            for i, part in enumerate(line_sums(corners)):
                v_ref[y - 1, i] = part


def scales_top(wx, wy, x, kp_ref, misc_d):
    row = lambda i, col: kp_ref[i, pl.ds(col, 1), :]
    here = x * wy + wy - 1
    visc = row(4, here)
    scales = [
        visc * row(0, here), visc if x == wx - 1 else visc * row(0, here + wy), visc * row(1, here),
        visc * misc_d[x : x + 1], visc * row(2, here), visc * row(3, here),
    ]
    return visc, scales


def y_vertex(wx, wy, xs, visc_ref, kp_ref, parts_ref, my_ref, own_ref, v3_ref, down_ref, up_ref):
    z = kp_ref.shape[2]
    misc_d = read_tail(down_ref, wx, 0)[2]
    misc_u = read_tail(up_ref, wx, 1)[2]
    row = lambda i, col: kp_ref[i, pl.ds(col, 1), :]
    delta = dot(my_ref[pl.ds(288, 96), :], wide([down_ref[pl.ds(48 * x, 48), :] for x in xs]))
    arrived_corners = slot_corners([up_ref[pl.ds(48 * x, 48), :] for x in xs], parts_ref, 3)
    results = []
    for n, x in enumerate(xs):
        last = x == wx - 1
        part = delta[:, z * n : z * n + z]
        visc, scales = scales_top(wx, wy, x, kp_ref, misc_d)
        used = [None if (s == 1 and last) else scales[s] for s in range(6)]
        known = v3_ref[x] * misc_d[x : x + 1]
        top = [rows + settle(known, p) for p, rows in enumerate(scaled_corners(part, used))]
        top_one = part[16:32] * visc
        visc = level_visc(misc_u[x : x + 1], visc_ref)
        flag = row(1, x * wy)
        own = own_ref[:, pl.ds(z * x, z)]
        keep_z = misc_u[2 * wx + x : 2 * wx + x + 1]
        scales = [
            visc * misc_u[wx + x : wx + x + 1], None if last else visc * misc_u[wx + x + 1 : wx + x + 2],
            None, visc * flag, visc * keep_z, visc * z_next(keep_z),
        ]
        known = arrived_corners[n] * flag
        low = [rows + settle(known, p) for p, rows in enumerate(scaled_corners(own[48:144], scales))]
        results.append((top, low, top_one, own[64:80] * visc))
    return results


def y_flux(wx, wy, visc_ref, l_ref, kp_ref, my_ref, own_ref, down_ref, up_ref):
    misc_d = read_tail(down_ref, wx, 0)[2]
    misc_u = read_tail(up_ref, wx, 1)[2]
    delta = columns(dot(my_ref[pl.ds(0, 288), :], wide([down_ref[pl.ds(48 * x, 48), :] for x in range(wx)])), wx)
    own = columns(own_ref[0:48, :], wx)
    results = []
    for x in range(wx):
        scales = scales_top(wx, wy, x, kp_ref, misc_d)[1]
        flux = [delta[x][48 * s : 48 * s + 48] * scales[s] for s in range(6)]
        visc = level_visc(misc_u[x : x + 1], visc_ref)
        arrived = up_ref[pl.ds(48 * x, 48), :].astype(F32)
        face = arrived + visc * (own[x] + penalty * l_ref[1, x * wy].astype(F32))
        results.append((flux, face * kp_ref[1, pl.ds(x * wy, 1), :]))
    return results


def turn_kernel(
    wx, wy, visc_ref, l_ref, kp_ref, diag_ref, parts_ref, my_ref, own_ref, c_ref, va_ref, vb_ref,
    v1a_ref, v1b_ref, v3_ref, swap0_in, swap1_in, swap2_in,
    vt_ref, vl_ref, v1_ref, yd_ref, yu_ref, inner_ref, outer_ref, down_ref, up_ref,
):
    z = l_ref.shape[3]
    arrive((swap0_in, swap1_in, swap2_in), yd_ref, yu_ref)
    xs = (0, wx - 1)
    results = y_vertex(wx, wy, xs, visc_ref, kp_ref, parts_ref, my_ref, own_ref, v3_ref, yd_ref, yu_ref)
    sums_d, one_d, misc_d = read_tail(yd_ref, wx, 0)
    sums_u, one_u, misc_u = read_tail(yu_ref, wx, 1)
    edge_high, edge_low = misc_d[wx + 4 : 2 * wx + 4], misc_d[2 * wx + 4 : 3 * wx + 4]
    for n, (top, low, _, _) in enumerate(results):
        for p in range(2):
            vt_ref[n, p] = top[p]
            vl_ref[n, p] = low[p]
    top_one, low_one = results[1][2:]
    mine = tall(one_u) + low_one
    v1_ref[0] = mine
    v1_ref[1] = v1a_ref[0]
    for y in range(wy - 2):
        v1_ref[2 + y] = v1b_ref[y]
    v1_ref[wy] = v1a_ref[1] + top_one
    v1_ref[wy + 1] = tall(one_d)

    def plane(i, n, p):
        lines = [sums_u[i] + vl_ref[n, p], va_ref[0, i]]
        lines += [vb_ref[y, i] for y in range(wy - 2)]
        lines += [va_ref[1, i] + vt_ref[n, p], sums_d[i]]
        return merge(lines[1::2], lines[0::2])

    down_ref[pl.ds(0, 48), :] = yu_ref[pl.ds(48 * wx, 48), :]
    for y in range(wy):
        down_ref[pl.ds(48 + 48 * y, 48), :] = l_ref[0, y]
    down_ref[pl.ds(48 * (wy + 1), 48), :] = yd_ref[pl.ds(48 * wx, 48), :]
    diag = diag_ref[pl.ds(0, wy), :]
    high = diag.astype(BF).astype(F32)
    first = plane(0, 0, 0)
    rim = [first[4 * y : 4 * y + 3] for y in range(wy + 1)]
    rim += [high, edge_high[0:1], diag - high, edge_low[0:1]]
    rim += [misc_u[wx : wx + 1], kp_ref[0, 0:wy], misc_d[wx : wx + 1]]
    put_tail(down_ref, 48 * (wy + 2), rim)
    corner = (wx - 1) * wy
    last_trace = yd_ref[pl.ds(48 * (wx - 1), 48), :]
    flux = dot(my_ref[pl.ds(48, 48), :], last_trace) * kp_ref[4, pl.ds(corner + wy - 1, 1), :]
    for y in range(wy):
        part = c_ref[1, corner + y]
        up_ref[pl.ds(48 * y, 48), :] = (part + flux if y == wy - 1 else part).astype(BF)
    last = pl.ds(corner, wy)
    rim = [plane(wx, 1, 1), mine, *one_d]
    rim += [misc_u[wx - 1 : wx], kp_ref[5, last], misc_d[wx + 1 : wx + 2]]
    rim += [misc_u[3 * wx - 1 : 3 * wx], kp_ref[2, last], misc_d[wx + 3 : wx + 4]]
    rim += [kp_ref[1, last], misc_d[wx - 1 : wx]]
    put_tail(up_ref, 48 * wy, rim)
    depart("gx", down_ref, up_ref, inner_ref, outer_ref)


def assemble_kernel(
    wx, wy, visc_ref, l_ref, kp_ref, diag_ref, parts_ref, mx_ref, my_ref, own_ref, c_ref,
    va_ref, vb_ref, v3_ref, vt_ref, vl_ref, yd_ref, yu_ref,
    r_ref, late_ref, v_ref, inv_ref, ownx_ref, mid,
):
    z = l_ref.shape[3]
    cells = wx * wy
    xs = tuple(range(1, wx - 1))
    results = y_vertex(wx, wy, xs, visc_ref, kp_ref, parts_ref, my_ref, own_ref, v3_ref, yd_ref, yu_ref)
    faces = []
    for x, (flux, face) in enumerate(y_flux(wx, wy, visc_ref, l_ref, kp_ref, my_ref, own_ref, yd_ref, yu_ref)):
        faces.append(face)
        for s in range(6):
            mid[x, s] = flux[s]
    traces = [yu_ref[pl.ds(48 * wx, 48), :]] + [l_ref[0, y] for y in range(wy)] + [yd_ref[pl.ds(48 * wx, 48), :]]
    ownx_ref[...] = dot(mx_ref[pl.ds(240, 144), :], wide(traces))

    def contrib(slot, x, y):
        here = c_ref[slot, x * wy + y]
        if y < wy - 1:
            return here
        return here + mid[x, slot]

    for x in range(wx):
        for y in range(wy):
            col = pl.ds(x * wy + y, 48, stride=cells)
            behind = contrib(3, x, y - 1) if y else faces[x]
            ahead = contrib(0, x, y) + contrib(1, x - 1, y) if x else contrib(0, x, y)
            sides = [ahead, contrib(2, x, y) + behind, contrib(4, x, y) + z_prev(contrib(5, x, y))]
            for d in range(3):
                if x == wx - 1:
                    late_ref[d, y] = sides[d]
                elif d == 0 and x == 0:
                    late_ref[3, y] = sides[d]
                else:
                    r_ref[d, col, :] = sides[d]
    sums_d, one_d, misc_d = read_tail(yd_ref, wx, 0)
    sums_u, one_u, misc_u = read_tail(yu_ref, wx, 1)
    edge_diag = misc_d[wx + 4 : 2 * wx + 4] + misc_d[2 * wx + 4 : 3 * wx + 4]

    def brought(which, i):
        held = vl_ref if which else vt_ref
        terms = []
        for x, p in ((i, 0), (i - 1, 1)):
            if x in (0, wx - 1):
                terms.append(held[0 if x == 0 else 1, p])
            elif 0 < x < wx - 1:
                terms.append(results[x - 1][which][p])
        return sum(terms[1:], terms[0])

    for i in range(wx + 1):
        lines = [sums_u[i] + brought(1, i), va_ref[0, i]]
        lines += [vb_ref[y, i] for y in range(wy - 2)]
        lines += [va_ref[1, i] + brought(0, i), sums_d[i]]
        v_ref[i] = merge(lines[1::2], lines[0::2])
        if i < wx:
            parts = [jnp.broadcast_to(diag_ref[pl.ds(i * wy + y, 1), :], (4, z)) for y in range(wy)]
            parts += [jnp.broadcast_to(edge_diag[i : i + 1], (4, z)), jnp.zeros((4, z), F32)]
            inv_ref[i] = reciprocal(tall(parts))


def reciprocal(diag):
    present = diag > 0.0
    return jnp.where(present, (1.0 / gain) / jnp.where(present, diag, 1.0), 0.0)


def final_kernel(
    wx, wy, visc_ref, l_ref, kp_ref, parts_ref, mx_ref, ownx_ref, r_in, late_ref, v_ref, inv_ref, v1_ref,
    yd_ref, yu_ref, outer_in, inner_in, out_hbm, r_ref, held, fix, sems,
):
    here, last = lax.axis_index("gx"), lax.axis_size("gx") - 1

    def from_high(start, size):
        rows = pl.ds(start, size)
        value = jnp.where(even("gx"), inner_in[rows, :], outer_in[rows, :])
        return jnp.where(here < last, value, jnp.zeros_like(value))

    def from_low(start, size):
        rows = pl.ds(start, size)
        value = jnp.where(even("gx"), outer_in[rows, :], inner_in[rows, :])
        return jnp.where(here > 0, value, jnp.zeros_like(value))

    cells, z = wx * wy, l_ref.shape[3]
    rows = v_ref.shape[1]
    row = lambda i, col: kp_ref[i, pl.ds(col, 1), :]
    traces = [from_high(48 * j, 48) for j in range(wy + 2)]
    delta = dot(mx_ref[pl.ds(288, 96), :], wide(traces))
    rim_x = from_high(48 * (wy + 2), tail_rows(6 * wy + 7)).astype(F32)
    gap = jnp.zeros((1, z), F32)
    ahead = [part for j in range(wy + 1) for part in (rim_x[3 * j : 3 * j + 3], gap)]
    ahead = tall(ahead + [jnp.zeros((rows - 4 * (wy + 1), z), F32)])
    rim_x = rim_x[3 * (wy + 1) :]
    rim_l = from_low(48 * wy, tail_rows(rows + 32 + 3 * (wy + 2) - 1)).astype(F32)
    misc_d = read_tail(yd_ref, wx, 0)[2]
    misc_u = read_tail(yu_ref, wx, 1)[2]
    flags_high = rim_x[2 * (wy + 1) : 3 * wy + 4]
    corner = (wx - 1) * wy
    arrived = [from_low(48 * y, 48) for y in range(wy)]
    arrived_corners = slot_corners(arrived, parts_ref, 1)
    codes = rim_l[rows + 32 : rows + 32 + wy + 2]
    keep_z = rim_l[rows + 32 + wy + 2 : rows + 32 + 2 * (wy + 2)]
    keep_y = rim_l[rows + 32 + 2 * (wy + 2) : rows + 32 + 3 * (wy + 2) - 1]
    low_visc = level_visc(codes, visc_ref)
    low_keep_z = z_next(keep_z)
    lines = [[], [], []]
    high_scales = []
    del r_in
    for j in range(-1, wy + 1):
        n = j + 1
        part = delta[:, z * n : z * n + z]
        flag = flags_high[n : n + 1]
        if j < 0:
            visc = level_visc(misc_u[wx - 1 : wx], visc_ref)
            kz = misc_u[3 * wx - 1 : 3 * wx]
            keeps = [misc_u[2 * wx - 1 : 2 * wx], flag, None, row(1, corner), kz, z_next(kz)]
        elif j < wy:
            here = corner + j
            visc = row(4, here)
            high_y = row(1, here + 1) if j < wy - 1 else misc_d[wx - 1 : wx]
            keeps = [row(0, here), flag, row(1, here), high_y, row(2, here), row(3, here)]
        else:
            visc = level_visc(misc_d[wx + 1 : wx + 2], visc_ref)
            kz = misc_d[wx + 3 : wx + 4]
            keeps = [misc_d[wx + 2 : wx + 3], flag, misc_d[wx - 1 : wx], None, kz, z_next(kz)]
        scales = [None if keep is None else visc * keep for keep in keeps]
        corners = scaled_corners(part, scales)
        one = v1_ref[n] * flag
        lines[0].append(corners[0])
        lines[1].append(corners[1] + one[0:8] + z_prev(one[8:16]))
        high_scales.append(scales)
        own = ownx_ref[:, pl.ds(z * n, z)]
        visc = low_visc[n : n + 1]
        flag = misc_u[wx : wx + 1] if j < 0 else misc_d[wx : wx + 1] if j == wy else row(0, j)
        scales = [
            None, visc * flag, None if j < 0 else visc * keep_y[j : j + 1],
            None if j == wy else visc * keep_y[j + 1 : j + 2], visc * keep_z[n : n + 1], visc * low_keep_z[n : n + 1],
        ]
        corners = scaled_corners(own[48:144], scales, (1,))[0]
        if 0 <= j < wy:
            one = arrived_corners[j] * flag
            lines[2].append(corners + one[0:8] + z_prev(one[8:16]))
            face = (arrived[j].astype(F32) + visc * (own[0:48] + penalty * l_ref[0, j].astype(F32))) * flag
            r_ref[0, pl.ds(j, 48, stride=cells), :] = late_ref[3, j] + face
        else:
            at = rows + (0 if j < 0 else 16)
            one = rim_l[at : at + 16] * flag
            lines[2].append(corners + one[0:8] + z_prev(one[8:16]))
    low, before, first = [merge(part[1::2], part[0::2]) for part in lines]
    top = v_ref[wx] + before + ahead
    values = [(v_ref[0] + first + rim_l[0:rows]) * inv_ref[0]]
    values += [v_ref[i] * inv_ref[i] for i in range(1, wx - 1)]
    values += [(v_ref[wx - 1] + low) * inv_ref[wx - 1]]
    diag = rim_x[0 : wy + 1] + rim_x[wy + 1 : 2 * (wy + 1)]
    parts = [jnp.broadcast_to(diag[j : j + 1], (4, z)) for j in range(wy + 1)]
    values += [top * reciprocal(tall(parts + [jnp.zeros((rows - 4 * (wy + 1), z), F32)]))]
    high = [pltpu.roll(value, rows - 4, 0) for value in values]
    for i in range(wx + 1):
        fix[0, pl.ds(4 * wy * i, 4 * wy), :] = values[i][0 : 4 * wy]
        fix[1, pl.ds(4 * wy * i, 4 * wy), :] = high[i][0 : 4 * wy]
    vertex = lambda c, p, q: fix[q, pl.ds(4 * wy * p + c, cells, stride=4), :]
    delta = columns(dot(mx_ref[pl.ds(0, 240), :], wide(traces[1 : wy + 1])), wy)
    behind = dot(mx_ref[pl.ds(96, 48), :], traces[0]) * high_scales[0][3]
    copies = []
    for d in range(3):
        for j in range(wy):
            scales = high_scales[j + 1]
            part = [delta[j][48 * i : 48 * i + 48] for i in range(5)]
            if d == 0:
                flux = part[0] * scales[0]
            elif d == 1:
                flux = part[1] * scales[2] + behind
                behind = part[2] * scales[3]
            else:
                flux = part[3] * scales[4] + z_prev(part[4] * scales[5])
            r_ref[d, pl.ds(corner + j, 48, stride=cells), :] = late_ref[d, j] + flux
        flags = kp_ref[d]
        for c in range(3):
            if d == 0:
                near = [vertex(c, 0, q) * flags for q in range(2)]
                far = [z_next(vertex(c, 0, q)) * flags for q in range(2)]
                corner_values = [[near[0], far[0]], [near[1], far[1]]]
            elif d == 1:
                corner_values = [[vertex(c, p, 0) * flags, z_next(vertex(c, p, 0)) * flags] for p in range(2)]
            else:
                corner_values = [[vertex(c, p, q) * flags for q in range(2)] for p in range(2)]
            lines = [between(corner_values[0][t], corner_values[1][t]) for t in range(2)]
            for a in range(4):
                for b, value in enumerate(between(lines[0][a], lines[1][a])):
                    at = pl.ds(cells * (16 * c + 4 * a + b), cells)
                    held[d, at, :] = (r_ref[d, at, :] + value).astype(BF)
        if d:
            part = pl.ds(0, 2) if d == 1 else pl.ds(2, 1)
            copies.append(pltpu.make_async_copy(held.at[part], out_hbm.at[part], sems.at[d - 1]))
            copies[-1].start()
    for copy in copies:
        copy.wait()


def call(body, args, outs, scratch, flops, hbm=False, aliases=None):
    if hbm:
        args = tuple(pltpu.with_memory_space_constraint(a, pltpu.HBM) for a in args)
    keywords = {}
    if aliases:
        spaces = [pltpu.HBM] + [pltpu.VMEM] * (len(outs) - 1)
        keywords = dict(out_specs=tuple(pl.BlockSpec(memory_space=space) for space in spaces), input_output_aliases=aliases)
    return pl.pallas_call(
        body,
        **keywords,
        in_specs=[pl.BlockSpec(memory_space=pltpu.HBM if hbm else pltpu.VMEM)] * len(args),
        out_shape=outs,
        scratch_shapes=scratch,
        cost_estimate=pl.CostEstimate(flops=flops, bytes_accessed=1000000, transcendentals=0),
        compiler_params=pltpu.CompilerParams(vmem_limit_bytes=16 * 1024 * 1024),
    )(*args)


def local(traces, dirichlet, visc_class, viscosity, coarse_diag, solve_map, flux_map):
    wx, wy, z = traces.shape[2:]
    cells = wx * wy
    rows = 8 * (wy // 2 + 1)
    per_hex = 2 * 384 * 288 * z
    parts = jnp.asarray(slot_table())
    vm = pltpu.VMEM
    bind = lambda body: functools.partial(body, wx, wy)
    y_message = vm((48 * wx + 48 + tail_rows(8 * ((wx + 2) // 2) + 8 + 3 * wx + 4), z), BF)
    x_message = vm((48 * (wy + 2) + tail_rows(6 * wy + 7), z), BF)

    (lifted, nat, flags, visc, diag, s_turned, f_map, parts, va, v1a, v3, *swaps) = call(
        bind(first_kernel),
        (
            viscosity, traces.reshape(3, 48 * cells, z), dirichlet.reshape(3, cells, z),
            visc_class.reshape(cells, z), coarse_diag.reshape(cells, z), solve_map.T, flux_map, parts,
        ),
        (
            vm((4, cells, 48, z), BF), vm((3, 48 * cells, z), F32), vm((6, cells, z), F32), vm((viscosity.shape[0], z), F32), vm((cells, z), F32),
            vm(solve_map.shape[::-1], BF), vm(flux_map.shape, BF), vm(parts.shape, BF),
            vm((2, wx + 1, 8, z), F32), vm((2, 16, z), F32), vm((wx, 32, z), F32),
            y_message, y_message, y_message,
        ),
        [
            y_message, y_message,
            vm((3, 48 * cells, z), BF), vm((3, cells, z), jnp.int32), vm((cells, z), jnp.int32),
            pltpu.SMEM(viscosity.shape, F32), pltpu.SemaphoreType.DMA((8,)),
        ],
        wx * per_hex, True,
    )
    swaps = [swap(message, "gy", "gx", k, 3) for k, message in enumerate(swaps)]
    c, vb, v1b, mx, my, own = call(
        bind(middle_kernel),
        (lifted, nat, flags, s_turned, f_map, parts),
        (
            vm((6, cells, 48, z), F32), vm((wy - 2, wx + 1, 8, z), F32), vm((wy - 2, 16, z), F32),
            vm((384, 48), BF), vm((384, 48), BF), vm((144, wx * z), F32),
        ),
        [vm((4, cells, 48, z), BF), vm((384, 288), BF), vm((288, 256), BF)], cells * per_hex,
    )
    vt, vl, v1, yd, yu, inner, outer = call(
        bind(turn_kernel),
        (
            visc, lifted, flags, diag, parts, my, own, c, va, vb, v1a, v1b, v3, *swaps,
        ),
        (
            vm((2, 2, 8, z), F32), vm((2, 2, 8, z), F32), vm((wy + 2, 16, z), F32),
            y_message, y_message, x_message, x_message,
        ),
        [x_message, x_message], 2 * per_hex,
    )
    inner = swap(inner, "gx", "gy", 0)
    outer = swap(outer, "gx", "gy", 1)
    residual, late, vs, inverse, ownx = call(
        bind(assemble_kernel),
        (
            visc, lifted, flags, diag, parts, mx, my, own, c, va, vb, v3, vt, vl, yd, yu,
        ),
        (
            vm((3, 48 * cells, z), F32), vm((4, wy, 48, z), F32), vm((wx + 1, rows, z), F32), vm((wx, rows, z), F32),
            vm((144, (wy + 2) * z), F32),
        ),
        [vm((wx, 6, 48, z), F32)], 4 * per_hex,
    )
    out, _ = call(
        bind(final_kernel),
        (
            visc, lifted, flags, parts, mx, ownx, residual, late, vs, inverse, v1, yd, yu, outer, inner,
        ),
        (jax.ShapeDtypeStruct((3, 48 * cells, z), BF), vm((3, 48 * cells, z), F32)),
        [vm((3, 48 * cells, z), BF), vm((2, 4 * wy * (wx + 1), z), F32), pltpu.SemaphoreType.DMA((2,))], 6 * per_hex,
        aliases={6: 1},
    )
    return out.reshape(traces.shape)


def solution(mesh):
    in_specs = (
        P(None, None, "gx", "gy", None),
        P(None, "gx", "gy", None),
        P("gx", "gy", None),
        P(),
        P("gx", "gy", None),
        P(),
        P(),
    )
    out_specs = P(None, None, "gx", "gy", None)
    return jax.shard_map(local, mesh=mesh, in_specs=in_specs, out_specs=out_specs, check_vma=False)
```
